32 devices in a mesh: section: 2 (over core), batch: 16 (over z, y, x).
Axes of the slice: x: 2, y: 2, z: 4, core: 2. Of those that a mesh axis runs over, the one named last changes fastest.
Arguments:
- frames: bfloat16 [2, 24, 384, 2000], P(None, None, 'batch', 'section'), may hold values from -6 to 6
- grad_out: bfloat16 [2, 24, 384, 2000], P(None, None, 'batch', 'section'), may hold values from -6 to 6
- weights: bfloat16 [2, 2000, 2000], P('section'), may hold values from -0.125 to 0.125
- gains: float32 [2, 2000], P('section'), may hold values from 0.5 to 1.5
- shifts: float32 [2, 2000], P('section'), may hold values from -1 to 1
- recurs: float32 [2, 2000], P('section'), may hold values from 0.05 to 0.95
- lengths: int32 [2, 128], P(None, 'batch'), may hold values from 1 to 24, 1920 in all within a row
- masks: int32 [2, 24, 384], P(None, None, 'batch'), may hold values 0 or 1
Outputs:
- grad_frames: bfloat16 [2, 24, 384, 2000], P(None, None, 'batch', 'section')
- grad_weights: float32 [2, 2000, 2000], P('section')
- grad_gains: float32 [2, 2000], P('section')
- grad_shifts: float32 [2, 2000], P('section')
- grad_recurs: float32 [2, 2000], P('section')
- rms_table: float32 [2, 2], P('section')
The draws below stay inside these ranges and needn't reach their ends.
Inputs may be any that keep to these rules, and one draw needn't show every extreme that they name: `lengths`: each micro-batch has a group of 24 frames.
All inputs are finite; a program needn't handle non-finite values. No bound on the sum of `masks` on one device may be relied on, other than what follows from the above.
Results may differ from the reference program's by a relative error of at most 0.007.
Values may be sent and summed in bfloat16 or wider, within the bound.
A program may use at most 256 MiB of HBM per device.

```python
import math
from functools import partial
import jax
import jax.numpy as jnp
import numpy as np
from jax import lax

H = 2000
VIEWS = 3
MICRO = 2
TSTEPS = 24
SEQS = 384
GROUPS = 128
N_SECTION = 2


def with_ends(values, stream_key, least, top_value):
    index_at = [jax.random.randint(jax.random.fold_in(stream_key, axis), (), 0, length) for axis, length in enumerate(values.shape)]
    main_axis = values.shape.index(max(values.shape))
    next_to = index_at[:main_axis] + [(index_at[main_axis] + 1) % values.shape[main_axis]] + index_at[main_axis + 1:]
    return values.at[tuple(index_at)].set(least).at[tuple(next_to)].set(top_value)


def block_scale(key, extent, shards, low, largest):
    level, own = 1.0, jax.random.fold_in(key, 6)
    for position, blocks in shards:
        steps = jnp.exp(jax.random.uniform(jax.random.fold_in(own, position), (blocks,), jnp.float32, low / len(shards), largest / len(shards)))
        level = level * jnp.repeat(steps, extent[position] // blocks).reshape([-1 if axis == position else 1 for axis in range(len(extent))])
    return level


def length_profile(amount, total, limit, skew):
    weights = [(1 << 20) // math.isqrt(standing ** skew) + 1 for standing in range(2, amount + 1)]
    rest, given = total - limit - (amount - 1), [1] * (amount - 1)
    while rest > 0:
        free = [i for i in range(amount - 1) if given[i] < limit]
        pool, left = sum([weights[i] for i in free]), rest
        for i in free:
            more = min(limit - given[i], max(1, left * weights[i] // pool), rest)
            given[i] = given[i] + more
            rest = rest - more
    return np.array([limit] + given)


def ragged_sizes(rng, number_of, total, most, slope):
    if number_of == 2:
        one = jax.random.randint(rng, (), max(1, total - most), min(most, total - 1) + 1)
        return jnp.stack([one, total - one])
    tallies = jnp.asarray(length_profile(number_of, total, most, slope), jnp.int32)
    twos = (number_of - 1) // 2
    giver, sink = tallies[1:1 + 2 * twos:2], tallies[2:2 + 2 * twos:2]
    room = jnp.minimum(giver - 1, most - sink)
    moved = jax.random.randint(jax.random.fold_in(rng, 1), (twos,), 0, 1 << 20) % (room + 1)
    tallies = tallies.at[1:1 + 2 * twos:2].set(giver - moved).at[2:2 + 2 * twos:2].set(sink + moved)
    return tallies[jax.random.permutation(jax.random.fold_in(rng, 2), number_of)]


def scatter_about(stream_key, shape, scale, bound, shards=(), held_as=jnp.bfloat16):
    loudness = block_scale(stream_key, shape, shards, -0.22, 0.18) if shards else 1.0
    values = jax.random.normal(stream_key, shape, jnp.float32) * scale * loudness
    return jnp.minimum(jnp.maximum(values, -bound), bound).astype(held_as)


def setup_inputs(seed: int = 0) -> dict:
    key_of = jax.random.split(jax.random.key(seed), 9)
    frames = scatter_about(key_of[0], (MICRO, TSTEPS, SEQS, H), 1.0, 6.0, ((2, 16), (3, 2)))
    grad_out = scatter_about(key_of[1], (MICRO, TSTEPS, SEQS, H), 1.0, 6.0, ((2, 16), (3, 2)))
    weights = scatter_about(key_of[2], (N_SECTION, H, H), H ** -0.5, 0.125, ((0, 2),))
    gains = jnp.clip(1.0 + 0.1 * jax.random.normal(key_of[3], (N_SECTION, H), jnp.float32), 0.5, 1.5)
    shifts = jnp.clip(jax.random.uniform(key_of[4], (N_SECTION, H), jnp.float32, -1.0, 1.0) * block_scale(key_of[4], (N_SECTION, H), ((0, 2),), -0.4, 0.0), -1.0, 1.0)
    recurs = jnp.clip(0.05 + 0.9 * jax.random.uniform(key_of[5], (N_SECTION, H), jnp.float32) ** block_scale(key_of[5], (N_SECTION, H), ((0, 2),), -0.2, 0.2), 0.05, 0.95)
    lengths = jax.vmap(lambda own: ragged_sizes(own, GROUPS, GROUPS * TSTEPS * 5 // 8, TSTEPS, 2))(jax.random.split(key_of[6], MICRO)).reshape((MICRO, GROUPS)).astype(jnp.int32)
    masks = with_ends((jax.random.randint(key_of[7], (MICRO, TSTEPS, SEQS), 0, 8) < 7).astype(jnp.int32), jax.random.fold_in(key_of[7], 1), 0, 1)
    return dict(frames=frames, grad_out=grad_out, weights=weights, gains=gains, shifts=shifts, recurs=recurs, lengths=lengths, masks=masks)


@jax.custom_vjp
def low(v):
    return lax.optimization_barrier(v.astype(jnp.bfloat16)).astype(jnp.float32)

@jax.custom_vjp
def low_back(v):
    return v

def low_keep(v):
    return (low(v), None)

def low_pass(kept, grad):
    return (grad,)

def back_keep(v):
    return (v, None)

def back_low(kept, grad):
    return (low(grad),)
low.defvjp(low_keep, low_pass)
low_back.defvjp(back_keep, back_low)
HIGH = lax.Precision.HIGHEST
EPS = 1e-05

def validity(lengths, masks):
    seq_len = jnp.repeat(lengths, VIEWS, axis=1)
    positions = jnp.arange(TSTEPS, dtype=jnp.int32)[None, :, None]
    live = (positions < seq_len[:, None, :]) & ((masks > 0) | (positions == 0))
    return live.astype(jnp.float32)

def recur_step(recur, state, item):
    value, keep = item
    keep = keep[:, None]
    fresh = keep * jax.nn.softplus(value + recur * state) + (1.0 - keep) * state
    return (fresh, fresh)

def layer(source, weight, gain, shift, recur, live):
    steps, seqs, width = source.shape
    rows = jnp.dot(source.reshape(steps * seqs, width), weight, precision=HIGH).reshape(steps, seqs, width)
    rows = low_back(rows)
    cells = live[:, :, None]
    count = jnp.sum(live)
    mean = lax.optimization_barrier(jnp.sum(cells * rows, axis=(0, 1))) / count
    spread = lax.optimization_barrier(jnp.sum(cells * jnp.square(rows - mean), axis=(0, 1))) / count
    normed = (rows - mean) * lax.rsqrt(spread + EPS)
    drive = gain * normed + shift
    advance = jax.checkpoint(partial(recur_step, recur))
    start = jnp.zeros((seqs, width), jnp.float32)
    _, hidden = lax.scan(advance, start, (drive, live))
    return hidden

def reference(frames, grad_out, weights, gains, shifts, recurs, lengths, masks):
    live = validity(lengths, masks)

    def forward(inputs, weight_all, gain_all, shift_all, recur_all):
        inputs = low_back(inputs)
        results, first_list, second_list = ([], [], [])
        for micro_index in range(MICRO):
            hidden_one = layer(inputs[micro_index], weight_all[0], gain_all[0], shift_all[0], recur_all[0], live[micro_index])
            passed = low(low_back(hidden_one))
            hidden_two = layer(passed, weight_all[1], gain_all[1], shift_all[1], recur_all[1], live[micro_index])
            results.append(inputs[micro_index] + hidden_two)
            first_list.append(hidden_one)
            second_list.append(hidden_two)
        return (jnp.stack(results), (jnp.stack(first_list), jnp.stack(second_list)))
    result, pullback, hiddens = jax.vjp(forward, frames.astype(jnp.float32), weights.astype(jnp.float32), gains, shifts, recurs, has_aux=True)
    grad_frames, grad_weights, grad_gains, grad_shifts, grad_recurs = pullback(grad_out.astype(jnp.float32))
    cells = live[..., None]
    total = jnp.sum(live) * H

    def masked_rms(values):
        return jnp.sqrt(jnp.sum(cells * jnp.square(values)) / total)
    base = frames.astype(jnp.float32)
    table = jnp.stack([jnp.stack([masked_rms(hiddens[0]), masked_rms(base)]), jnp.stack([masked_rms(hiddens[1]), masked_rms(result)])])
    return (grad_frames.astype(jnp.bfloat16), grad_weights, grad_gains, grad_shifts, grad_recurs, table)
```

```python
import functools

import jax
import jax.numpy as jnp
from jax import lax
from jax.experimental import pallas as pl
from jax.experimental.pallas import tpu as pltpu
from jax.sharding import PartitionSpec as P

EPS = 1e-05
W = 1024
HALF = W // 2
QUART = W // 4
MESH = pl.DeviceIdType.MESH
F32 = jnp.float32
BF16 = jnp.bfloat16


def grid_of(size):
    if size == 16:
        return (4, 2, 2)
    if size == 128:
        return (8, 4, 4)
    return (size, 1, 1)


def aligned(x, k):
    return pl.multiple_of(x, k)


def wide(x, reps):
    return jnp.concatenate([x] * reps, axis=1)


def fold(x):
    rows = x.shape[0]
    total = x[0:8]
    for k in range(8, rows, 8):
        total = total + x[k : k + 8]
    return total


def dot(a, b, dims):
    return lax.dot_general(a, b, (dims, ((), ())), preferred_element_type=F32)


class Reduction:
    def __init__(self, env, layer, part, block, first, second, third, lanes):
        self.env, self.layer, self.part, self.block = env, layer, part, block
        self.axes = (first, second, third)
        self.lanes = lanes
        n1, n2, n3 = (a[0] for a in self.axes)
        self.r1, self.r2, self.c3 = W // n1, W // n1 // n2, W // n3
        self.base1 = aligned(first[1] * self.r1, 16)
        self.base2 = aligned(first[1] * self.r1 + second[1] * self.r2, 16)
        self.lane3 = aligned(third[1] * self.c3, 128)
        self.own2 = aligned(second[1] * self.r2, 16)
        self.space12 = env["r12"].at[layer, part]
        self.space3 = env["r3"].at[layer, part]
        self.send = env["ar_send"].at[layer, part]
        self.recv = env["ar_recv"].at[layer, part]
        self.count = 0
        self.pending = []
        self.step = 0
        self.steps = (
            self.scatter1, self.scatter2, self.scatter3, self.gather3, self.gather2, self.gather1, self.finish,
        )

    def advance(self):
        if self.step < len(self.steps):
            self.steps[self.step]()
            self.step += 1

    def copy(self, src, dst, slot, axis, k):
        size, mine, to_device = axis
        where = to_device(lax.rem(mine + k, size))
        return pltpu.make_async_remote_copy(
            src_ref=src, dst_ref=dst, send_sem=self.send.at[slot], recv_sem=self.recv.at[slot],
            device_id=where, device_id_type=MESH,
        )

    def exchange(self, axis, source, target, incoming):
        size, mine, _ = axis
        self.pending = []
        for k in range(1, size):
            made = self.copy(source(lax.rem(mine + k, size)), target(k), self.count, axis, k)
            made.start()
            came = incoming(lax.rem(mine + size - k, size), k)
            self.pending.append((made, self.copy(came, came, self.count, axis, k)))
            self.count += 1

    def wait(self):
        for made, came in self.pending:
            made.wait_send()
            came.wait_recv()
        self.pending = []

    def scatter1(self):
        r1 = self.r1
        self.exchange(
            self.axes[0],
            lambda other: self.block.at[pl.ds(aligned(other * r1, 16), r1), :],
            lambda k: self.space12.at[pl.ds((k - 1) * r1, r1), :],
            lambda frm, k: self.space12.at[pl.ds((k - 1) * r1, r1), :],
        )

    def scatter2(self):
        self.wait()
        r1, r2 = self.r1, self.r2
        n1 = self.axes[0][0]

        def body(i, _):
            here = pl.ds(aligned(self.base1 + i * 16, 16), 16)
            total = self.block[here, :].astype(F32)
            for k in range(n1 - 1):
                total = total + self.space12[pl.ds(aligned(k * r1 + i * 16, 16), 16), :].astype(F32)
            self.block[here, :] = total.astype(BF16)
            return 0

        if n1 > 1:
            lax.fori_loop(0, r1 // 16, body, 0)
        self.start2 = (n1 - 1) * r1
        self.exchange(
            self.axes[1],
            lambda other: self.block.at[pl.ds(aligned(self.base1 + other * r2, 16), r2), :],
            lambda k: self.space12.at[pl.ds(self.start2 + (k - 1) * r2, r2), :],
            lambda frm, k: self.space12.at[pl.ds(self.start2 + (k - 1) * r2, r2), :],
        )

    def scatter3(self):
        self.wait()
        r2, c3 = self.r2, self.c3
        n2 = self.axes[1][0]

        def body(i, _):
            here = pl.ds(aligned(self.base2 + i * 16, 16), 16)
            total = self.block[here, :].astype(F32)
            for k in range(n2 - 1):
                total = total + self.space12[pl.ds(aligned(self.start2 + k * r2 + i * 16, 16), 16), :].astype(F32)
            self.block[here, :] = total.astype(BF16)
            return 0

        if n2 > 1:
            lax.fori_loop(0, r2 // 16, body, 0)
        self.exchange(
            self.axes[2],
            lambda other: self.block.at[pl.ds(self.base2, r2), pl.ds(aligned(other * c3, 128), c3)],
            lambda k: self.space3.at[k - 1],
            lambda frm, k: self.space3.at[k - 1],
        )

    def gather3(self):
        self.wait()
        r2, c3 = self.r2, self.c3
        n3 = self.axes[2][0]
        cols = pl.ds(self.lane3, c3)
        sums = self.env["vtot"][self.layer, self.part : self.part + 1, cols]
        column = self.env["column"].at[self.layer]

        def body(i, _):
            here = pl.ds(aligned(self.base2 + i * 16, 16), 16)
            total = self.block[here, cols].astype(F32)
            for k in range(n3 - 1):
                total = total + self.space3[k, pl.ds(aligned(i * 16, 16), 16), :].astype(F32)
            total = total + wide(column[here, :].astype(F32), c3 // 128) * sums
            self.space12[pl.ds(aligned(self.own2 + i * 16, 16), 16), cols] = total.astype(BF16)
            return 0

        lax.fori_loop(0, r2 // 16, body, 0)
        mine = self.space12.at[pl.ds(self.own2, r2), cols]
        self.exchange(
            self.axes[2], lambda other: mine, lambda k: mine,
            lambda frm, k: self.space12.at[pl.ds(self.own2, r2), pl.ds(aligned(frm * c3, 128), c3)],
        )

    def gather2(self):
        self.wait()
        mine = self.space12.at[pl.ds(self.own2, self.r2), :]
        self.exchange(
            self.axes[1], lambda other: mine, lambda k: mine,
            lambda frm, k: self.space12.at[pl.ds(aligned(frm * self.r2, 16), self.r2), :],
        )

    def result(self, index, section):
        return self.env["o"].at[section, pl.ds(aligned(index * self.r1, 16), self.r1), pl.ds(self.lanes(section), W)]

    def deliver(self, k, straight):
        source = self.space12.at[pl.ds(0, self.r1), :]
        size, mine, to_device = self.axes[0]
        recv = self.recv.at[self.count + k] if straight else self.env["ar_other"].at[self.layer, self.part, k]
        return pltpu.make_async_remote_copy(
            src_ref=source, dst_ref=self.result(mine, self.env["section"]), send_sem=self.send.at[self.count + k],
            recv_sem=recv, device_id=dict(to_device(lax.rem(mine + k, size)), section=self.layer), device_id_type=MESH,
        )

    def arrival(self, k, straight):
        section = self.env["section"]
        size, mine, to_device = self.axes[0]
        source = self.space12.at[pl.ds(0, self.r1), :]
        frm = lax.rem(mine + size - k, size)
        recv = self.recv.at[self.count + k] if straight else self.env["ar_other"].at[self.layer, self.part, k]
        return pltpu.make_async_remote_copy(
            src_ref=source, dst_ref=self.result(frm, section if straight else 1 - section),
            send_sem=self.send.at[self.count + k], recv_sem=recv,
            device_id=dict(to_device(frm), section=self.layer), device_id_type=MESH,
        )

    def kept(self):
        source = self.space12.at[pl.ds(0, self.r1), :]
        return pltpu.make_async_copy(
            source, self.result(self.axes[0][1], self.env["section"]), self.recv.at[self.count]
        )

    def gather1(self):
        self.wait()

        @pl.when(self.env["section"] == self.layer)
        def _():
            self.kept().start()
            for k in range(1, self.axes[0][0]):
                self.deliver(k, True).start()

        @pl.when(self.env["section"] != self.layer)
        def _():
            for k in range(self.axes[0][0]):
                self.deliver(k, False).start()

    def finish(self):
        size = self.axes[0][0]

        @pl.when(self.env["section"] == self.layer)
        def _():
            self.kept().wait()
            for k in range(1, size):
                self.deliver(k, True).wait_send()
                self.arrival(k, True).wait_recv()
            for k in range(size):
                self.arrival(k, False).wait_recv()

        @pl.when(self.env["section"] != self.layer)
        def _():
            for k in range(size):
                self.deliver(k, False).wait_send()


def kernel(dims, steps, seqs, fu, gu, wp, vec, live_in, o, v, gs, f_own, f_far, p_own, p_far, g3, wc, wr1, src_t, live,
           vecs, rows, hid, coef, tot, vtot, column, st_plane, st_z, r12, r3, sems, v_sems, pl_send, pl_recv, z_send, z_recv,
           ar_send, ar_recv, ar_other):
    nz, ny, nx = dims
    np_ = ny * nx
    span = steps * seqs
    total_rows = 2 * span
    sent_rows = total_rows + 16
    pairs = steps // 2
    section = lax.axis_index("section")
    other = 1 - section
    b = lax.axis_index("batch")
    mx = lax.rem(b, nx)
    my = lax.rem(b // nx, ny)
    mz = b // np_
    mp = lax.rem(b, np_)

    def at_x(i):
        return {"batch": b - mx + i}

    def at_y(i):
        return {"batch": b + (i - my) * nx}

    def at_z(i):
        return {"batch": b + (i - mz) * np_}

    def at_plane(i):
        return {"batch": b - mp + i}

    axis_x, axis_y, axis_z = (nx, mx, at_x), (ny, my, at_y), (nz, mz, at_z)
    sibling = {"section": other}

    def local(src, dst, slot):
        return pltpu.make_async_copy(src, dst, sems.at[0, slot])

    def across(src, dst, slot):
        return pltpu.make_async_remote_copy(
            src_ref=src, dst_ref=dst, send_sem=sems.at[1, slot], recv_sem=sems.at[2, slot],
            device_id=sibling, device_id_type=MESH,
        )

    own = [
        local(fu, f_own.at[pl.ds(0, total_rows), :], 0),
        local(live_in, live, 1),
        local(vec, vecs.at[section], 3),
    ]
    for made in own:
        made.start()

    w_hbm = wp

    def w_block(row, lane):
        return w_hbm.at[pl.ds(row, W), pl.ds(lane, W)]

    def w_plan(layer):
        mine, far = W * layer, W * (1 - layer)
        plan = [
            (w_block(mine, mine), w_block(far, far), wc.at[layer, 0]),
            (w_block(far, mine), w_block(mine, far), wc.at[layer, 1]),
        ]
        if layer == 1:
            plan.append((w_block(mine, far), w_block(far, mine), wr1))
        return plan

    late_plan = [
        (w_block(0, 0), w_block(W - 32, W), wc.at[0, 0]),
        (w_block(0, W), w_block(W - 32, 0), wc.at[0, 1]),
    ]
    slot_of = {0: 4, 1: 6, 2: 9}

    def local_w(plan, base):
        return [local(a, t, base + i) for i, (a, _, t) in enumerate(plan)]

    def across_w(plan, base):
        return [across(c, t, base + i) for i, (_, c, t) in enumerate(plan)]

    for layer in range(2):

        @pl.when(section == layer)
        def _(layer=layer):
            for made in local_w(w_plan(layer), slot_of[layer]):
                made.start()

    barrier = pltpu.get_barrier_semaphore()
    greeted = [dict(sibling)]
    greeted += [at_plane(lax.rem(mp + k, np_)) for k in range(1, np_)]
    greeted += [at_z(lax.rem(mz + k, nz)) for k in range(1, nz)]
    greeted += [dict(at_x(lax.rem(mx + k, nx)), section=other) for k in range(1, nx)]
    greeted += [dict(at_y(lax.rem(my + k, ny)), section=other) for k in range(1, ny)]
    for where in greeted:
        pl.semaphore_signal(barrier, inc=1, device_id=where, device_id_type=MESH)
    pl.semaphore_wait(barrier, len(greeted))

    send_f = across(fu, f_far, 0)
    send_vec = across(vec, vecs.at[section], 3)
    send_f.start()
    for layer in range(2):

        @pl.when(section == layer)
        def _(layer=layer):
            for made in across_w(w_plan(layer), slot_of[layer]):
                made.start()

    send_vec.start()

    def wait_w(layer, plan, base, which):
        @pl.when(section == layer)
        def _():
            local_w(plan, base)[which].wait()

        @pl.when(section != layer)
        def _():
            across_w(plan, base)[which].wait_recv()

    def done_w(layer, plan, base):
        @pl.when(section == layer)
        def _():
            for made in across_w(plan, base):
                made.wait_send()

    def matmul_to(out, a, w, first):
        def body(i, _):
            r = pl.ds(aligned((i // 2) * span, 16), span)
            c = pl.ds(aligned((i % 2) * HALF, HALF), HALF)
            y = dot(a[r, :], w[:, c], ((1,), (0,)))
            out[r, c] = y if first else out[r, c] + y
            return 0

        lax.fori_loop(0, 4, body, 0)

    def vec_of(layer, k):
        return vecs[layer, k : k + 1, pl.ds(aligned(section * W, W), W)]

    def stage_copy(where, rnd, slot, k, back):
        buf, size, me, at, send, recv = where
        there = at(lax.rem(me + (size - k if back else k), size))
        ref = buf.at[rnd % 2, slot]
        return pltpu.make_async_remote_copy(
            src_ref=ref, dst_ref=ref, send_sem=send.at[rnd, k], recv_sem=recv.at[rnd, k],
            device_id=there, device_id_type=MESH,
        )

    in_plane = (st_plane, np_, mp, at_plane, pl_send, pl_recv)
    in_line = (st_z, nz, mz, at_z, z_send, z_recv)

    def stage_start(where, rnd, value):
        buf, size, me = where[:3]
        buf[rnd % 2, me] = value
        for k in range(1, size):
            stage_copy(where, rnd, me, k, False).start()

    def stage_wait(where, rnd):
        size, me = where[1:3]
        for k in range(1, size):
            stage_copy(where, rnd, me, k, False).wait_send()
            stage_copy(where, rnd, lax.rem(me + size - k, size), k, True).wait_recv()

    def add_slots(where, rnd):
        buf, size, idx = where[0], where[1], rnd % 2
        total = buf[idx, 0]
        for k in range(1, size):
            total = total + buf[idx, k]
        return total

    def merge_slots(where, rnd):
        buf, size, idx = where[0], where[1], rnd % 2
        out = []
        for m in range(2):
            s = [buf[idx, k, 3 * m : 3 * m + 1, :] for k in range(size)]
            q = [buf[idx, k, 3 * m + 1 : 3 * m + 2, :] for k in range(size)]
            n = [buf[idx, k, 3 * m + 2 : 3 * m + 3, :] for k in range(size)]
            total, squares, count = sum(s[1:], s[0]), sum(q[1:], q[0]), sum(n[1:], n[0])
            mean = total / count
            for k in range(size):
                d = s[k] / n[k] - mean
                squares = squares + n[k] * d * d
            out += [total, squares, count]
        both = [buf[idx, k, 6:8, :] for k in range(size)]
        return jnp.concatenate(out + [sum(both[1:], both[0])], axis=0)

    def forward_stats(layer):
        out = []
        source = f_own if layer == 0 else p_own
        level = jnp.zeros((8, W), F32)
        for m in range(2):

            def sums(i, carry):
                acc, cnt, lev = carry
                r = pl.ds(aligned(m * span + i * (2 * seqs), 16), 2 * seqs)
                lv = live[r, :]
                keep = wide(lv, 8)
                acc = acc + fold(keep * rows[layer, r, :])
                return acc, cnt + fold(lv), lev + fold(keep * source[r, :].astype(F32))

            acc, cnt, level = lax.fori_loop(
                0, pairs, sums, (jnp.zeros((8, W), F32), jnp.zeros((8, 128), F32), level)
            )
            total = jnp.sum(acc, axis=0, keepdims=True)
            count = wide(jnp.sum(cnt, axis=0, keepdims=True), 8)
            mean = total / count

            def squares(i, acc):
                r = pl.ds(aligned(m * span + i * (2 * seqs), 16), 2 * seqs)
                d = rows[layer, r, :] - mean
                return acc + fold(wide(live[r, :], 8) * (d * d))

            sq = lax.fori_loop(0, pairs, squares, jnp.zeros((8, W), F32))
            out += [total, jnp.sum(sq, axis=0, keepdims=True), count]
        level = jnp.sum(level, axis=0, keepdims=True)
        value = jnp.concatenate(out + [level, jnp.zeros_like(level)], axis=0)
        stage_start(in_plane, layer, value)
        stage_wait(in_plane, layer)
        stage_start(in_line, layer, merge_slots(in_plane, layer))
        stage_wait(in_line, layer)
        value = merge_slots(in_line, layer)
        for m in range(2):
            count = value[3 * m + 2 : 3 * m + 3]
            mean = value[3 * m : 3 * m + 1] / count
            spread = value[3 * m + 1 : 3 * m + 2] / count
            coef[layer, 3 * m : 3 * m + 1, :] = mean
            coef[layer, 3 * m + 1 : 3 * m + 2, :] = lax.rsqrt(spread + EPS)
            coef[layer, 3 * m + 2 : 3 * m + 3, :] = count
        level = value[6:7] / (value[2:3] + value[5:6])
        top = lax.broadcasted_iota(jnp.int32, (16, W), 0) == 0
        source[total_rows:sent_rows, :] = jnp.where(top, level, 0.0).astype(BF16)

    def forward_scan(layer, keep_passed):
        gain, shift, recur = vec_of(layer, 0), vec_of(layer, 1), vec_of(layer, 2)
        sends = []
        for lh in range(2):
            lanes = slice(lh * HALF, (lh + 1) * HALF)
            a, c = [], []
            for m in range(2):
                mean = coef[layer, 3 * m : 3 * m + 1, lanes]
                scale = coef[layer, 3 * m + 1 : 3 * m + 2, lanes]
                a.append(gain[:, lanes] * scale)
                c.append((shift[:, lanes], mean))
            rec = recur[:, lanes]

            def body(i, carry):
                out = []
                for m in range(2):
                    r = pl.ds(aligned(m * span + i * (2 * seqs), 16), 2 * seqs)
                    x = (rows[layer, r, lanes] - c[m][1]) * a[m] + c[m][0]
                    alive = wide(live[r, :], 4) > 0.0
                    h = carry[m]
                    both = []
                    for k in range(2):
                        part = slice(k * seqs, (k + 1) * seqs)
                        z = x[part] + rec * h
                        soft = jnp.maximum(z, 0.0) + jnp.log(1.0 + jnp.exp(-jnp.abs(z)))
                        h = jnp.where(alive[part], soft, h)
                        both.append(h)
                    two = jnp.concatenate(both, axis=0)
                    hid[layer, r, lanes] = two
                    if keep_passed:
                        p_own[r, lanes] = two.astype(BF16)
                    out.append(h)
                return tuple(out)

            zero = jnp.zeros((seqs, HALF), F32)
            lax.fori_loop(0, pairs, body, (zero, zero))
            if keep_passed:
                made = across(p_own.at[pl.ds(0, total_rows), lanes], p_far.at[:, lanes], 12 + lh)
                made.start()
                sends.append(made)
        return sends

    def backward_scan(layer, above):
        gain, shift, recur = vec_of(layer, 0), vec_of(layer, 1), vec_of(layer, 2)
        for lq in range(4):
            lanes = slice(lq * QUART, (lq + 1) * QUART)
            gq, sq, rec = gain[:, lanes], shift[:, lanes], recur[:, lanes]
            mean = [coef[layer, 3 * m : 3 * m + 1, lanes] for m in range(2)]
            scale = [coef[layer, 3 * m + 1 : 3 * m + 2, lanes] for m in range(2)]

            def body(i, carry):
                down, s1, s2, rsum, sqh, sqa = carry
                down, s1, s2 = list(down), list(s1), list(s2)
                i = pairs - 1 - i
                for m in range(2):
                    start = m * span + i * (2 * seqs)
                    r = pl.ds(aligned(start, 16), 2 * seqs)
                    before = pl.ds(aligned(jnp.maximum(start - seqs, 0), 8), seqs)
                    normed = (rows[layer, r, lanes] - mean[m]) * scale[m]
                    drive = gq * normed + sq
                    h2 = hid[layer, r, lanes]
                    hb = jnp.where(i > 0, hid[layer, before, lanes], 0.0)
                    lv = wide(live[r, :], 2)
                    up = above[r, lanes].astype(F32)
                    res = f_own[r, lanes].astype(F32)
                    aux = res + h2 if layer == 1 else res
                    sqh = sqh + fold(lv * (h2 * h2))
                    sqa = sqa + fold(lv * (aux * aux))
                    grads = [None, None]
                    for k in (1, 0):
                        part = slice(k * seqs, (k + 1) * seqs)
                        prior = h2[0:seqs] if k == 1 else hb
                        slope = 0.5 + 0.5 * jnp.tanh(0.5 * (drive[part] + rec * prior))
                        total = up[part] + down[m]
                        gd = lv[part] * slope * total
                        down[m] = (1.0 - lv[part]) * total + rec * gd
                        grads[k] = gd
                        rsum = rsum + fold(gd * prior)
                    gd2 = jnp.concatenate(grads, axis=0)
                    hid[layer, r, lanes] = gd2
                    s1[m] = s1[m] + fold(gd2)
                    s2[m] = s2[m] + fold(gd2 * normed)
                return tuple(down), tuple(s1), tuple(s2), rsum, sqh, sqa

            zero = jnp.zeros((seqs, QUART), F32)
            z8 = jnp.zeros((8, QUART), F32)
            _, s1, s2, rsum, sqh, sqa = lax.fori_loop(
                0, pairs, body, ((zero, zero), (z8, z8), (z8, z8), z8, z8, z8)
            )
            for k, x in enumerate((s1[0], s1[1], s2[0], s2[1], rsum, sqh, sqa)):
                tot[layer, k : k + 1, lanes] = jnp.sum(x, axis=0, keepdims=True)
        tot[layer, 7:8, :] = jnp.zeros((1, W), F32)

    def backward_stats(layer, between):
        rnd = 2 if layer == 1 else 4
        stage_start(in_plane, rnd, tot[layer])
        between()
        stage_wait(in_plane, rnd)
        stage_start(in_line, rnd, add_slots(in_plane, rnd))
        stage_wait(in_line, rnd)
        tot[layer] = add_slots(in_line, rnd)
        tot[layer, 7:8, :] = coef[layer, 2:3, :] + coef[layer, 5:6, :]

        @pl.when(section == layer)
        def _():
            pltpu.make_async_copy(tot.at[layer], v.at[section], v_sems.at[0]).start()

        @pl.when(section != layer)
        def _():
            v_across(layer).start()

    def v_across(layer):
        return pltpu.make_async_remote_copy(
            src_ref=tot.at[layer], dst_ref=v.at[section], send_sem=v_sems.at[1], recv_sem=v_sems.at[2],
            device_id=sibling, device_id_type=MESH,
        )

    def grad_rows(layer, slot):
        gain = vec_of(layer, 0)
        sends = []
        for lh in range(2):
            lanes = slice(lh * HALF, (lh + 1) * HALF)
            acc = jnp.zeros((8, HALF), F32)
            for m in range(2):
                mean = coef[layer, 3 * m : 3 * m + 1, lanes]
                scale = coef[layer, 3 * m + 1 : 3 * m + 2, lanes]
                count = coef[layer, 3 * m + 2 : 3 * m + 3, lanes]
                first = tot[layer, m : m + 1, lanes] / count
                second = tot[layer, 2 + m : 3 + m, lanes] / count * scale
                k = scale * gain[:, lanes]

                def body(i, acc):
                    r = pl.ds(aligned(m * span + i * (2 * seqs), 16), 2 * seqs)
                    y = hid[layer, r, lanes] - first - (rows[layer, r, lanes] - mean) * second
                    y = wide(live[r, :], 4) * (k * y)
                    g3[0, r, lanes] = y.astype(BF16)
                    return acc + fold(y)

                acc = lax.fori_loop(0, pairs, body, acc)
            top = lax.broadcasted_iota(jnp.int32, (16, HALF), 0) == 0
            minus = jnp.where(top, -jnp.sum(acc, axis=0, keepdims=True), 0.0)
            g3[0, total_rows:sent_rows, lanes] = minus.astype(BF16)
            made = across(g3.at[0, pl.ds(0, sent_rows), lanes], g3.at[1 + layer, pl.ds(0, sent_rows), lanes], slot + lh)
            made.start()
            sends.append(made)
        return sends

    def sums_start(layer):
        own_sum = -g3[0, total_rows:sent_rows, :].astype(F32)[0:1]
        far_sum = -g3[1 + layer, total_rows:sent_rows, :].astype(F32)[0:1]
        value = jnp.concatenate([own_sum, far_sum, jnp.zeros((6, W), F32)], axis=0)
        stage_start(in_plane, 3 if layer == 1 else 5, value)

    def sums_middle(layer):
        rnd = 3 if layer == 1 else 5
        stage_wait(in_plane, rnd)
        stage_start(in_line, rnd, add_slots(in_plane, rnd))

    def sums_end(layer):
        rnd = 3 if layer == 1 else 5
        stage_wait(in_line, rnd)
        vtot[layer] = add_slots(in_line, rnd)

    def transpose(src, layer):
        def body(j, _):
            c = pl.ds(aligned(j * 128, 128), 128)
            src_t[c, :] = src[:, c].T
            level = src[total_rows:sent_rows, c].astype(F32)[0:1]
            column[layer, c, :] = jnp.broadcast_to(level, (128, 128)).T.astype(BF16)
            return 0

        lax.fori_loop(0, W // 128, body, 0)

    def weight_grad(block, grads):
        def body(j, _):
            r = pl.ds(aligned(j * 256, 256), 256)
            block[r, :] = dot(src_t[r, :], grads[...], ((1,), (0,))).astype(BF16)
            return 0

        lax.fori_loop(0, W // 256, body, 0)

    def source_grad(store, w_own, w_far, far):
        def body(i, _):
            r = pl.ds(aligned((i // 2) * span, 16), span)
            c = pl.ds(aligned((i % 2) * HALF, HALF), HALF)
            y = dot(g3[0, r, :], w_own[c, :], ((1,), (1,))) + dot(g3[far, r, :], w_far[c, :], ((1,), (1,)))
            store(r, c, y)
            return 0

        lax.fori_loop(0, 4, body, 0)

    env = dict(vtot=vtot, column=column, r12=r12, r3=r3, ar_send=ar_send, ar_recv=ar_recv, ar_other=ar_other, o=o, section=section)

    def lanes_own(sec):
        return aligned(sec * W, W)

    def lanes_far(sec):
        return aligned((1 - sec) * W, W)

    blocks = {
        (1, 0): f_far.at[pl.ds(0, W), :],
        (1, 1): p_far.at[pl.ds(0, W), :],
        (0, 0): wc.at[1, 1],
        (0, 1): wr1,
    }
    parts = {}
    for layer in (1, 0):
        parts[layer, 0] = Reduction(env, layer, 0, blocks[layer, 0], axis_x, axis_y, axis_z, lanes_own)
        parts[layer, 1] = Reduction(env, layer, 1, blocks[layer, 1], axis_y, axis_x, axis_z, lanes_far)

    for spare in (f_own, p_own, g3.at[0], g3.at[1], g3.at[2]):
        spare[sent_rows:, :] = jnp.zeros((spare.shape[0] - sent_rows, W), BF16)

    own[0].wait()
    wait_w(0, w_plan(0), slot_of[0], 0)
    matmul_to(rows.at[0], f_own, wc.at[0, 0], True)
    wait_w(0, w_plan(0), slot_of[0], 1)
    send_f.wait()
    matmul_to(rows.at[0], f_far, wc.at[0, 1], False)
    own_g = local(gu, f_far, 2)
    own_g.start()
    own[1].wait()
    own[2].wait()
    send_vec.wait_send()
    across(vec, vecs.at[other], 3).wait_recv()
    forward_stats(0)
    sends = forward_scan(0, True)
    wait_w(1, w_plan(1), slot_of[1], 0)
    matmul_to(rows.at[1], p_own, wc.at[1, 0], True)
    wait_w(1, w_plan(1), slot_of[1], 1)
    for made in sends:
        made.wait()
    done_w(0, w_plan(0), slot_of[0])

    @pl.when(section == 0)
    def _():
        for made in local_w(late_plan, slot_of[2]):
            made.start()
        for made in across_w(late_plan, slot_of[2]):
            made.start()

    matmul_to(rows.at[1], p_far, wc.at[1, 1], False)
    forward_stats(1)
    forward_scan(1, False)
    own_g.wait()
    backward_scan(1, f_far)
    backward_stats(1, lambda: transpose(p_own, 1))
    sends = grad_rows(1, 14)
    weight_grad(blocks[1, 0], g3.at[0])
    parts[1, 0].advance()
    for made in sends:
        made.wait()
    sums_start(1)
    weight_grad(blocks[1, 1], g3.at[2])
    parts[1, 1].advance()
    wait_w(1, w_plan(1), slot_of[1], 2)
    done_w(1, w_plan(1), slot_of[1])

    def keep_down(r, c, y):
        p_own[r, c] = y.astype(BF16)

    source_grad(keep_down, wc.at[1, 0], wr1, 2)
    sums_middle(1)
    backward_scan(0, p_own)
    sums_end(1)
    backward_stats(0, lambda: transpose(f_own, 0))
    sends = grad_rows(0, 16)
    parts[1, 0].advance()
    parts[1, 1].advance()
    weight_grad(blocks[0, 0], g3.at[0])
    parts[0, 0].advance()
    for made in sends:
        made.wait()
    sums_start(0)
    weight_grad(blocks[0, 1], g3.at[1])
    parts[0, 1].advance()
    parts[1, 0].advance()
    parts[1, 1].advance()
    sums_middle(0)
    wait_w(0, late_plan, slot_of[2], 0)
    wait_w(0, late_plan, slot_of[2], 1)
    done_w(0, late_plan, slot_of[2])

    def keep_source(r, c, y):
        rows[0, r, c] = y

    source_grad(keep_source, wc.at[0, 0], wc.at[0, 1], 1)
    result = local(rows.at[0], gs, 18)
    result.start()
    sums_end(0)
    for _ in range(7):
        for layer in (1, 0):
            parts[layer, 0].advance()
            parts[layer, 1].advance()
    result.wait()

    for layer in range(2):

        @pl.when(section == layer)
        def _(layer=layer):
            pltpu.make_async_copy(tot.at[layer], v.at[section], v_sems.at[0]).wait()
            pltpu.make_async_remote_copy(
                src_ref=tot.at[layer], dst_ref=v.at[other], send_sem=v_sems.at[1], recv_sem=v_sems.at[2],
                device_id=sibling, device_id_type=MESH,
            ).wait_recv()

        @pl.when(section != layer)
        def _(layer=layer):
            v_across(layer).wait_send()


def whole_step(dims, steps, seqs, fu, gu, wp, vec, live):
    nz, ny, nx = dims
    rows = 2 * steps * seqs
    np_ = ny * nx
    n1 = min(nx, ny)
    wide_rows = (rows + 16 + 127) // 128 * 128
    r12_rows = max((a - 1) * (W // a) + (c - 1) * (W // a // c) for a, c in ((nx, ny), (ny, nx)))
    r2 = W // nx // ny
    ar_count = (nx - 1) + (ny - 1) + 2 * (nz - 1) + max(nx, ny) - 1 + max(nx, ny)
    any_ = pl.BlockSpec(memory_space=pl.ANY)
    dma = pltpu.SemaphoreType.DMA
    return pl.pallas_call(
        functools.partial(kernel, dims, steps, seqs),
        out_shape=(
            jax.ShapeDtypeStruct((2, W, 2 * W), BF16),
            jax.ShapeDtypeStruct((2, 8, W), F32),
            jax.ShapeDtypeStruct((rows, W), F32),
        ),
        in_specs=[any_] * 5,
        out_specs=(any_, any_, any_),
        scratch_shapes=[
            pltpu.VMEM((wide_rows, W), BF16),
            pltpu.VMEM((rows, W), BF16),
            pltpu.VMEM((wide_rows, W), BF16),
            pltpu.VMEM((rows, W), BF16),
            pltpu.VMEM((3, wide_rows, W), BF16),
            pltpu.VMEM((2, 2, W, W), BF16),
            pltpu.VMEM((W, W), BF16),
            pltpu.VMEM((W, wide_rows), BF16),
            pltpu.VMEM((rows, 128), F32),
            pltpu.VMEM((2, 8, 2 * W), F32),
            pltpu.VMEM((2, rows, W), F32),
            pltpu.VMEM((2, rows, W), F32),
            pltpu.VMEM((2, 8, W), F32),
            pltpu.VMEM((2, 8, W), F32),
            pltpu.VMEM((2, 8, W), F32),
            pltpu.VMEM((2, W, 128), BF16),
            pltpu.VMEM((2, np_, 8, W), F32),
            pltpu.VMEM((2, nz, 8, W), F32),
            pltpu.VMEM((2, 2, max(r12_rows, W // n1), W), BF16),
            pltpu.VMEM((2, 2, max(nz - 1, 1), r2, W // nz), BF16),
            dma((3, 19)),
            dma((3,)),
            dma((6, max(np_, 2))),
            dma((6, max(np_, 2))),
            dma((6, max(nz, 2))),
            dma((6, max(nz, 2))),
            dma((2, 2, ar_count)),
            dma((2, 2, ar_count)),
            dma((2, 2, max(nx, ny))),
        ],
        compiler_params=pltpu.CompilerParams(
            collective_id=0, has_side_effects=True, vmem_limit_bytes=64 * 1024 * 1024
        ),
    )(fu, gu, wp, vec, live)


def by_units(x, section):
    half = x.shape[1]
    lead = W - half
    head = lax.ppermute(x[:, :lead], "section", [(1, 0)])
    first = jnp.concatenate([x, head], axis=1)
    second = jnp.pad(x[:, lead:], ((0, 0), (0, 2 * lead)))
    return jnp.where(section == 0, first, second)


def shards(dims, frames, grad_out, weights, gains, shifts, recurs, lengths, masks):
    section = lax.axis_index("section")
    micro, steps, seqs, half = frames.shape
    width = 2 * half
    views = seqs // lengths.shape[1]
    seq_len = jnp.repeat(lengths, views, axis=1)
    positions = jnp.arange(steps, dtype=jnp.int32)[None, :, None]
    alive = (positions < seq_len[:, None, :]) & ((masks > 0) | (positions == 0))
    live = jnp.broadcast_to(alive.astype(F32).reshape(-1, 1), (micro * steps * seqs, 128))
    fu = by_units(frames.reshape(-1, half), section)
    gu = by_units(grad_out.reshape(-1, half), section)
    spare = 2 * W - width
    wp = jnp.pad(weights[0], ((0, spare), (0, spare)))
    vec = jnp.concatenate(
        [
            jnp.pad(gains, ((0, 0), (0, spare))),
            jnp.pad(shifts, ((0, 0), (0, spare)), constant_values=-1e30),
            jnp.pad(recurs, ((0, 0), (0, spare))),
            jnp.zeros((5, 2 * W), F32),
        ],
        axis=0,
    )
    o, v, gs = whole_step(dims, steps, seqs, fu, gu, wp, vec, live)
    grad_weight = o.reshape(2 * W, 2 * W)[:width, :width].astype(F32)
    shifted = jnp.where(section == 0, gs[:, :half], gs[:, W - half - 16 : W - 16])
    grad_frames = (shifted.reshape(frames.shape) + grad_out.astype(F32)).astype(BF16)
    sums = jnp.concatenate([v[0], v[1]], axis=1)[:, :width]
    cells = v[0, 7, 0] * width
    table = jnp.sqrt(jnp.sum(sums[5:7], axis=1) / cells)[None]
    return (
        grad_frames,
        grad_weight[None],
        (sums[2] + sums[3])[None],
        (sums[0] + sums[1])[None],
        sums[4][None],
        table,
    )


def solution(mesh):
    in_specs = (
        P(None, None, "batch", "section"),
        P(None, None, "batch", "section"),
        P("section", None, None),
        P("section", None),
        P("section", None),
        P("section", None),
        P(None, "batch"),
        P(None, None, "batch"),
    )
    out_specs = (
        P(None, None, "batch", "section"),
        P("section", None, None),
        P("section", None),
        P("section", None),
        P("section", None),
        P("section", None),
    )
    body = functools.partial(shards, grid_of(mesh.shape["batch"]))
    return jax.shard_map(body, mesh=mesh, in_specs=in_specs, out_specs=out_specs, check_vma=False)
```

```python
import functools

import jax
import jax.numpy as jnp
from jax import lax
from jax.experimental import pallas as pl
from jax.experimental.pallas import tpu as pltpu
from jax.sharding import PartitionSpec as P

EPS = 1e-05
W = 1024
HALF = W // 2
QUART = W // 4
MESH = pl.DeviceIdType.MESH
F32 = jnp.float32
BF16 = jnp.bfloat16


def grid_of(size):
    if size == 16:
        return (4, 2, 2)
    if size == 128:
        return (8, 4, 4)
    return (size, 1, 1)


def aligned(x, k):
    return pl.multiple_of(x, k)


def wide(x, reps):
    return jnp.concatenate([x] * reps, axis=1)


def fold(x):
    rows = x.shape[0]
    total = x[0:8]
    for k in range(8, rows, 8):
        total = total + x[k : k + 8]
    return total


def dot(a, b, dims):
    return lax.dot_general(a, b, (dims, ((), ())), preferred_element_type=F32)


class Reduction:
    def __init__(self, env, layer, part, block, first, second, third, lanes):
        self.env, self.layer, self.part, self.block = env, layer, part, block
        self.axes = (first, second, third)
        self.lanes = lanes
        n1, n2, n3 = (a[0] for a in self.axes)
        self.r1, self.r2, self.c3 = W // n1, W // n1 // n2, W // n3
        self.base1 = aligned(first[1] * self.r1, 16)
        self.base2 = aligned(first[1] * self.r1 + second[1] * self.r2, 16)
        self.lane3 = aligned(third[1] * self.c3, 128)
        self.own2 = aligned(second[1] * self.r2, 16)
        self.space12 = env["r12"].at[layer, part]
        self.space3 = env["r3"].at[layer, part]
        self.send = env["ar_send"].at[layer, part]
        self.recv = env["ar_recv"].at[layer, part]
        self.count = 0
        self.pending = []
        self.step = 0
        self.steps = (
            self.scatter1, self.scatter2, self.scatter3, self.gather3, self.gather2, self.gather1, self.finish,
        )

    def advance(self):
        if self.step < len(self.steps):
            self.steps[self.step]()
            self.step += 1

    def copy(self, src, dst, slot, axis, k):
        size, mine, to_device = axis
        where = to_device(lax.rem(mine + k, size))
        return pltpu.make_async_remote_copy(
            src_ref=src, dst_ref=dst, send_sem=self.send.at[slot], recv_sem=self.recv.at[slot],
            device_id=where, device_id_type=MESH,
        )

    def exchange(self, axis, source, target, incoming):
        size, mine, _ = axis
        self.pending = []
        for k in range(1, size):
            made = self.copy(source(lax.rem(mine + k, size)), target(k), self.count, axis, k)
            made.start()
            came = incoming(lax.rem(mine + size - k, size), k)
            self.pending.append((made, self.copy(came, came, self.count, axis, k)))
            self.count += 1

    def wait(self):
        for made, came in self.pending:
            made.wait_send()
            came.wait_recv()
        self.pending = []

    def scatter1(self):
        r1 = self.r1
        self.exchange(
            self.axes[0],
            lambda other: self.block.at[pl.ds(aligned(other * r1, 16), r1), :],
            lambda k: self.space12.at[pl.ds((k - 1) * r1, r1), :],
            lambda frm, k: self.space12.at[pl.ds((k - 1) * r1, r1), :],
        )

    def scatter2(self):
        self.wait()
        r1, r2 = self.r1, self.r2
        n1 = self.axes[0][0]

        def body(i, _):
            here = pl.ds(aligned(self.base1 + i * 16, 16), 16)
            total = self.block[here, :].astype(F32)
            for k in range(n1 - 1):
                total = total + self.space12[pl.ds(aligned(k * r1 + i * 16, 16), 16), :].astype(F32)
            self.block[here, :] = total.astype(BF16)
            return 0

        if n1 > 1:
            lax.fori_loop(0, r1 // 16, body, 0)
        self.start2 = (n1 - 1) * r1
        self.exchange(
            self.axes[1],
            lambda other: self.block.at[pl.ds(aligned(self.base1 + other * r2, 16), r2), :],
            lambda k: self.space12.at[pl.ds(self.start2 + (k - 1) * r2, r2), :],
            lambda frm, k: self.space12.at[pl.ds(self.start2 + (k - 1) * r2, r2), :],
        )

    def scatter3(self):
        self.wait()
        r2, c3 = self.r2, self.c3
        n2 = self.axes[1][0]

        def body(i, _):
            here = pl.ds(aligned(self.base2 + i * 16, 16), 16)
            total = self.block[here, :].astype(F32)
            for k in range(n2 - 1):
                total = total + self.space12[pl.ds(aligned(self.start2 + k * r2 + i * 16, 16), 16), :].astype(F32)
            self.block[here, :] = total.astype(BF16)
            return 0

        if n2 > 1:
            lax.fori_loop(0, r2 // 16, body, 0)
        self.exchange(
            self.axes[2],
            lambda other: self.block.at[pl.ds(self.base2, r2), pl.ds(aligned(other * c3, 128), c3)],
            lambda k: self.space3.at[k - 1],
            lambda frm, k: self.space3.at[k - 1],
        )

    def gather3(self):
        self.wait()
        r2, c3 = self.r2, self.c3
        n3 = self.axes[2][0]
        cols = pl.ds(self.lane3, c3)
        sums = self.env["vtot"][self.layer, self.part : self.part + 1, cols]
        column = self.env["column"].at[self.layer]

        def body(i, _):
            here = pl.ds(aligned(self.base2 + i * 16, 16), 16)
            total = self.block[here, cols].astype(F32)
            for k in range(n3 - 1):
                total = total + self.space3[k, pl.ds(aligned(i * 16, 16), 16), :].astype(F32)
            total = total + wide(column[here, :].astype(F32), c3 // 128) * sums
            self.space12[pl.ds(aligned(self.own2 + i * 16, 16), 16), cols] = total.astype(BF16)
            return 0

        lax.fori_loop(0, r2 // 16, body, 0)
        mine = self.space12.at[pl.ds(self.own2, r2), cols]
        self.exchange(
            self.axes[2], lambda other: mine, lambda k: mine,
            lambda frm, k: self.space12.at[pl.ds(self.own2, r2), pl.ds(aligned(frm * c3, 128), c3)],
        )

    def gather2(self):
        self.wait()
        mine = self.space12.at[pl.ds(self.own2, self.r2), :]
        self.exchange(
            self.axes[1], lambda other: mine, lambda k: mine,
            lambda frm, k: self.space12.at[pl.ds(aligned(frm * self.r2, 16), self.r2), :],
        )

    def result(self, index, section):
        return self.env["o"].at[section, pl.ds(aligned(index * self.r1, 16), self.r1), pl.ds(self.lanes(section), W)]

    def deliver(self, k, straight):
        source = self.space12.at[pl.ds(0, self.r1), :]
        size, mine, to_device = self.axes[0]
        recv = self.recv.at[self.count + k] if straight else self.env["ar_other"].at[self.layer, self.part, k]
        return pltpu.make_async_remote_copy(
            src_ref=source, dst_ref=self.result(mine, self.env["section"]), send_sem=self.send.at[self.count + k],
            recv_sem=recv, device_id=dict(to_device(lax.rem(mine + k, size)), section=self.layer), device_id_type=MESH,
        )

    def arrival(self, k, straight):
        section = self.env["section"]
        size, mine, to_device = self.axes[0]
        source = self.space12.at[pl.ds(0, self.r1), :]
        frm = lax.rem(mine + size - k, size)
        recv = self.recv.at[self.count + k] if straight else self.env["ar_other"].at[self.layer, self.part, k]
        return pltpu.make_async_remote_copy(
            src_ref=source, dst_ref=self.result(frm, section if straight else 1 - section),
            send_sem=self.send.at[self.count + k], recv_sem=recv,
            device_id=dict(to_device(frm), section=self.layer), device_id_type=MESH,
        )

    def kept(self):
        source = self.space12.at[pl.ds(0, self.r1), :]
        return pltpu.make_async_copy(
            source, self.result(self.axes[0][1], self.env["section"]), self.recv.at[self.count]
        )

    def gather1(self):
        self.wait()

        @pl.when(self.env["section"] == self.layer)
        def _():
            self.kept().start()
            for k in range(1, self.axes[0][0]):
                self.deliver(k, True).start()

        @pl.when(self.env["section"] != self.layer)
        def _():
            for k in range(self.axes[0][0]):
                self.deliver(k, False).start()

    def finish(self):
        size = self.axes[0][0]

        @pl.when(self.env["section"] == self.layer)
        def _():
            self.kept().wait()
            for k in range(1, size):
                self.deliver(k, True).wait_send()
                self.arrival(k, True).wait_recv()
            for k in range(size):
                self.arrival(k, False).wait_recv()

        @pl.when(self.env["section"] != self.layer)
        def _():
            for k in range(size):
                self.deliver(k, False).wait_send()


def kernel(dims, steps, seqs, views, frames, grad_out, weights, tail, gains, shifts, recurs, lengths, masks, o, gf,
           out_gains, out_shifts, out_recurs, out_table, f_own, f_far, p_own, p_far, g3, wc, wr1, src_t, live, turn,
           stage_in, heads, v, vecs, rows, hid, coef, tot, vtot, column, st_plane, st_z, r12, r3, sems, v_sems, stage_sem, pl_send, pl_recv, z_send, z_recv,
           ar_send, ar_recv, ar_other):
    nz, ny, nx = dims
    np_ = ny * nx
    span = steps * seqs
    total_rows = 2 * span
    sent_rows = total_rows + 16
    pairs = steps // 2
    section = lax.axis_index("section")
    other = 1 - section
    b = lax.axis_index("batch")
    mx = lax.rem(b, nx)
    my = lax.rem(b // nx, ny)
    mz = b // np_
    mp = lax.rem(b, np_)

    def at_x(i):
        return {"batch": b - mx + i}

    def at_y(i):
        return {"batch": b + (i - my) * nx}

    def at_z(i):
        return {"batch": b + (i - mz) * np_}

    def at_plane(i):
        return {"batch": b - mp + i}

    axis_x, axis_y, axis_z = (nx, mx, at_x), (ny, my, at_y), (nz, mz, at_z)
    sibling = {"section": other}

    def local(src, dst, slot):
        return pltpu.make_async_copy(src, dst, sems.at[0, slot])

    def across(src, dst, slot):
        return pltpu.make_async_remote_copy(
            src_ref=src, dst_ref=dst, send_sem=sems.at[1, slot], recv_sem=sems.at[2, slot],
            device_id=sibling, device_id_type=MESH,
        )

    half = frames.shape[3]
    width = 2 * half
    lead = W - half
    rest = width - W
    full = rest // 128 * 128
    chunk = stage_in.shape[1]
    chunks = 2 * steps // chunk

    def fetch(source, c):
        piece = source.at[c * chunk // steps, pl.ds(c * chunk % steps, chunk)]
        return pltpu.make_async_copy(piece, stage_in.at[c % 2], stage_sem.at[c % 2])

    def by_units(source, target, ready):
        for c in range(chunks):
            fetch(source, c).wait()
            if c == 0:
                ready()

            def place(i, _, c=c):
                x = stage_in[c % 2, pl.ds(2 * i, 2)].astype(F32).reshape(2 * seqs, half)
                to = pl.ds(aligned((c * chunk + 2 * i) * seqs, 16), 2 * seqs)

                @pl.when(section == 0)
                def _():
                    t = c * chunk % steps + 2 * i
                    head = heads[c * chunk // steps, pl.ds(t, 2)].astype(F32).reshape(2 * seqs, 128)
                    target[to, :] = jnp.concatenate([x, head[:, :lead]], axis=1).astype(BF16)

                @pl.when(section == 1)
                def _():
                    pad = jnp.zeros((2 * seqs, 2 * lead), F32)
                    target[to, :] = jnp.concatenate([x[:, lead:], pad], axis=1).astype(BF16)

                return 0

            lax.fori_loop(0, chunk // 2, place, 0)
            if c + 2 < chunks:
                fetch(source, c + 2).start()

    def pieces(row, count, u, block):
        r = pl.ds(row, count)
        to = pl.ds(0, count)
        if u == 0:
            return [(weights.at[0, r, pl.ds(0, W)], block.at[to, :])]
        return [
            (weights.at[0, r, pl.ds(W, full)], block.at[to, pl.ds(0, full)]),
            (tail.at[r, :], block.at[to, pl.ds(full, 128)]),
        ]

    rows_of = {0: (0, W), 1: (W, rest)}

    def w_plan(layer):
        mine, far = rows_of[layer], rows_of[1 - layer]
        plan = [
            (mine, layer, far, 1 - layer, wc.at[layer, 0]),
            (far, layer, mine, 1 - layer, wc.at[layer, 1]),
        ]
        if layer == 1:
            plan.append((mine, 0, far, 1, wr1))
        return plan

    late_row = (width - half) // 16 * 16
    late_shift = half - late_row
    late_plan = [
        ((0, W), 0, (late_row, width - late_row), 1, wc.at[0, 0]),
        ((0, W), 1, (late_row, width - late_row), 0, wc.at[0, 1]),
    ]
    slot_of = {0: 4, 1: 8, 2: 14}

    def local_w(plan, base, which):
        r, u, _, _, block = plan[which]
        return [local(a, t, base + 2 * which + i) for i, (a, t) in enumerate(pieces(*r, u, block))]

    def across_w(plan, base, which):
        _, _, r, u, block = plan[which]
        return [across(a, t, base + 2 * which + i) for i, (a, t) in enumerate(pieces(*r, u, block))]

    def start_local_w(layer, plan, base):
        @pl.when(section == layer)
        def _():
            for which in range(len(plan)):
                for made in local_w(plan, base, which):
                    made.start()

    def start_across_w(layer, plan, base):
        @pl.when(section == layer)
        def _():
            for which in range(len(plan)):
                for made in across_w(plan, base, which):
                    made.start()

    fetch(frames, 0).start()
    fetch(frames, 1).start()
    for layer in range(2):
        start_local_w(layer, w_plan(layer), slot_of[layer])

    barrier = pltpu.get_barrier_semaphore()
    greeted = [dict(sibling)]
    greeted += [at_plane(lax.rem(mp + k, np_)) for k in range(1, np_)]
    greeted += [at_z(lax.rem(mz + k, nz)) for k in range(1, nz)]
    greeted += [dict(at_x(lax.rem(mx + k, nx)), section=other) for k in range(1, nx)]
    greeted += [dict(at_y(lax.rem(my + k, ny)), section=other) for k in range(1, ny)]
    for where in greeted:
        pl.semaphore_signal(barrier, inc=1, device_id=where, device_id_type=MESH)
    pl.semaphore_wait(barrier, len(greeted))

    def heads_copy(source, slot):
        return across(source.at[:, :, :, pl.ds(0, 128)], heads, slot)

    @pl.when(section == 1)
    def _():
        heads_copy(frames, 1).start()

    for layer in range(2):
        start_across_w(layer, w_plan(layer), slot_of[layer])

    def wait_w(layer, plan, base, which):
        @pl.when(section == layer)
        def _():
            for made in local_w(plan, base, which):
                made.wait()

        @pl.when(section != layer)
        def _():
            for made in across_w(plan, base, which):
                made.wait_recv()

    def done_w(layer, plan, base):
        @pl.when(section == layer)
        def _():
            for which in range(len(plan)):
                for made in across_w(plan, base, which):
                    made.wait_send()

    def wait_heads(source, slot):
        @pl.when(section == 0)
        def _():
            heads_copy(source, slot).wait_recv()

        @pl.when(section == 1)
        def _():
            heads_copy(source, slot).wait_send()

    for k, (x, fill) in enumerate(((gains, 0.0), (shifts, -1e30), (recurs, 0.0))):
        vecs[section, k : k + 1, 0:width] = x[...]
        vecs[section, k : k + 1, width:] = jnp.full((1, 2 * W - width), fill, F32)
    vecs[section, 3:8, :] = jnp.zeros((5, 2 * W), F32)
    send_vec = across(vecs.at[section], vecs.at[section], 3)
    send_vec.start()

    gap = jnp.zeros((W - rest, W), BF16)

    @pl.when(section == 0)
    def _():
        wc[0, 1, rest:, :] = gap
        wc[1, 1, rest:, :] = gap

    @pl.when(section == 1)
    def _():
        wc[0, 0, rest:, :] = gap
        wc[1, 0, rest:, :] = gap
        wr1[rest:, :] = gap

    for m in range(2):
        turn[...] = jnp.zeros_like(turn)
        turn[0:steps, 0:seqs] = masks[m].astype(F32)
        mask = turn[...].T[0:seqs]
        groups = lengths.shape[1]
        s_at = lax.broadcasted_iota(jnp.int32, (seqs, groups), 0)
        g_at = lax.broadcasted_iota(jnp.int32, (seqs, groups), 1) * views
        there = (s_at >= g_at) & (s_at < g_at + views)
        length = jnp.broadcast_to(lengths[m : m + 1, :], (seqs, groups)).astype(F32)
        limit = jnp.sum(jnp.where(there, length, 0.0), axis=1, keepdims=True)
        position = lax.broadcasted_iota(jnp.int32, (seqs, 128), 1)
        alive = (position.astype(F32) < limit) & ((mask > 0.0) | (position == 0))
        alive = alive.astype(F32)
        for t in range(steps):
            at = m * span + t * seqs
            live[at : at + seqs, :] = jnp.broadcast_to(alive[:, t : t + 1], (seqs, 128))

    def matmul_to(out, a, w, first):
        def body(i, _):
            r = pl.ds(aligned((i // 2) * span, 16), span)
            c = pl.ds(aligned((i % 2) * HALF, HALF), HALF)
            y = dot(a[r, :], w[:, c], ((1,), (0,)))
            out[r, c] = y if first else out[r, c] + y
            return 0

        lax.fori_loop(0, 4, body, 0)

    def vec_of(layer, k):
        return vecs[layer, k : k + 1, pl.ds(aligned(section * W, W), W)]

    def stage_copy(where, rnd, slot, k, back):
        buf, size, me, at, send, recv = where
        there = at(lax.rem(me + (size - k if back else k), size))
        ref = buf.at[rnd % 2, slot]
        return pltpu.make_async_remote_copy(
            src_ref=ref, dst_ref=ref, send_sem=send.at[rnd, k], recv_sem=recv.at[rnd, k],
            device_id=there, device_id_type=MESH,
        )

    in_plane = (st_plane, np_, mp, at_plane, pl_send, pl_recv)
    in_line = (st_z, nz, mz, at_z, z_send, z_recv)

    def stage_start(where, rnd, value):
        buf, size, me = where[:3]
        buf[rnd % 2, me] = value
        for k in range(1, size):
            stage_copy(where, rnd, me, k, False).start()

    def stage_wait(where, rnd):
        size, me = where[1:3]
        for k in range(1, size):
            stage_copy(where, rnd, me, k, False).wait_send()
            stage_copy(where, rnd, lax.rem(me + size - k, size), k, True).wait_recv()

    def add_slots(where, rnd):
        buf, size, idx = where[0], where[1], rnd % 2
        total = buf[idx, 0]
        for k in range(1, size):
            total = total + buf[idx, k]
        return total

    def merge_slots(where, rnd):
        buf, size, idx = where[0], where[1], rnd % 2
        out = []
        for m in range(2):
            s = [buf[idx, k, 3 * m : 3 * m + 1, :] for k in range(size)]
            q = [buf[idx, k, 3 * m + 1 : 3 * m + 2, :] for k in range(size)]
            n = [buf[idx, k, 3 * m + 2 : 3 * m + 3, :] for k in range(size)]
            total, squares, count = sum(s[1:], s[0]), sum(q[1:], q[0]), sum(n[1:], n[0])
            mean = total / count
            for k in range(size):
                d = s[k] / n[k] - mean
                squares = squares + n[k] * d * d
            out += [total, squares, count]
        both = [buf[idx, k, 6:8, :] for k in range(size)]
        return jnp.concatenate(out + [sum(both[1:], both[0])], axis=0)

    def forward_stats(layer, between=None):
        out = []
        source = f_own if layer == 0 else p_own
        level = jnp.zeros((8, W), F32)
        for m in range(2):

            def sums(i, carry):
                acc, cnt, lev = carry
                r = pl.ds(aligned(m * span + i * (2 * seqs), 16), 2 * seqs)
                lv = live[r, :]
                keep = wide(lv, 8)
                acc = acc + fold(keep * rows[layer, r, :])
                return acc, cnt + fold(lv), lev + fold(keep * source[r, :].astype(F32))

            acc, cnt, level = lax.fori_loop(
                0, pairs, sums, (jnp.zeros((8, W), F32), jnp.zeros((8, 128), F32), level)
            )
            total = jnp.sum(acc, axis=0, keepdims=True)
            count = wide(jnp.sum(cnt, axis=0, keepdims=True), 8)
            mean = total / count

            def squares(i, acc):
                r = pl.ds(aligned(m * span + i * (2 * seqs), 16), 2 * seqs)
                d = rows[layer, r, :] - mean
                return acc + fold(wide(live[r, :], 8) * (d * d))

            sq = lax.fori_loop(0, pairs, squares, jnp.zeros((8, W), F32))
            out += [total, jnp.sum(sq, axis=0, keepdims=True), count]
        level = jnp.sum(level, axis=0, keepdims=True)
        value = jnp.concatenate(out + [level, jnp.zeros_like(level)], axis=0)
        stage_start(in_plane, layer, value)
        if between is not None:
            between()
        stage_wait(in_plane, layer)
        stage_start(in_line, layer, merge_slots(in_plane, layer))
        stage_wait(in_line, layer)
        value = merge_slots(in_line, layer)
        for m in range(2):
            count = value[3 * m + 2 : 3 * m + 3]
            mean = value[3 * m : 3 * m + 1] / count
            spread = value[3 * m + 1 : 3 * m + 2] / count
            coef[layer, 3 * m : 3 * m + 1, :] = mean
            coef[layer, 3 * m + 1 : 3 * m + 2, :] = lax.rsqrt(spread + EPS)
            coef[layer, 3 * m + 2 : 3 * m + 3, :] = count
        level = value[6:7] / (value[2:3] + value[5:6])
        top = lax.broadcasted_iota(jnp.int32, (16, W), 0) == 0
        source[total_rows:sent_rows, :] = jnp.where(top, level, 0.0).astype(BF16)

    def forward_scan(layer, keep_passed):
        gain, shift, recur = vec_of(layer, 0), vec_of(layer, 1), vec_of(layer, 2)
        sends = []
        for lh in range(2):
            lanes = slice(lh * HALF, (lh + 1) * HALF)
            a, c = [], []
            for m in range(2):
                mean = coef[layer, 3 * m : 3 * m + 1, lanes]
                scale = coef[layer, 3 * m + 1 : 3 * m + 2, lanes]
                a.append(gain[:, lanes] * scale)
                c.append((shift[:, lanes], mean))
            rec = recur[:, lanes]

            def body(i, carry):
                out = []
                for m in range(2):
                    r = pl.ds(aligned(m * span + i * (2 * seqs), 16), 2 * seqs)
                    x = (rows[layer, r, lanes] - c[m][1]) * a[m] + c[m][0]
                    alive = wide(live[r, :], 4) > 0.0
                    h = carry[m]
                    both = []
                    for k in range(2):
                        part = slice(k * seqs, (k + 1) * seqs)
                        z = x[part] + rec * h
                        soft = jnp.maximum(z, 0.0) + jnp.log(1.0 + jnp.exp(-jnp.abs(z)))
                        h = jnp.where(alive[part], soft, h)
                        both.append(h)
                    two = jnp.concatenate(both, axis=0)
                    hid[layer, r, lanes] = two
                    if keep_passed:
                        p_own[r, lanes] = two.astype(BF16)
                    out.append(h)
                return tuple(out)

            zero = jnp.zeros((seqs, HALF), F32)
            lax.fori_loop(0, pairs, body, (zero, zero))
            if keep_passed:
                made = across(p_own.at[pl.ds(0, total_rows), lanes], p_far.at[:, lanes], 18 + lh)
                made.start()
                sends.append(made)
        return sends

    def backward_scan(layer, above):
        gain, shift, recur = vec_of(layer, 0), vec_of(layer, 1), vec_of(layer, 2)
        for lq in range(4):
            lanes = slice(lq * QUART, (lq + 1) * QUART)
            gq, sq, rec = gain[:, lanes], shift[:, lanes], recur[:, lanes]
            mean = [coef[layer, 3 * m : 3 * m + 1, lanes] for m in range(2)]
            scale = [coef[layer, 3 * m + 1 : 3 * m + 2, lanes] for m in range(2)]

            def body(i, carry):
                down, s1, s2, rsum, sqh, sqa = carry
                down, s1, s2 = list(down), list(s1), list(s2)
                i = pairs - 1 - i
                for m in range(2):
                    start = m * span + i * (2 * seqs)
                    r = pl.ds(aligned(start, 16), 2 * seqs)
                    before = pl.ds(aligned(jnp.maximum(start - seqs, 0), 8), seqs)
                    normed = (rows[layer, r, lanes] - mean[m]) * scale[m]
                    drive = gq * normed + sq
                    h2 = hid[layer, r, lanes]
                    hb = jnp.where(i > 0, hid[layer, before, lanes], 0.0)
                    lv = wide(live[r, :], 2)
                    up = above[r, lanes].astype(F32)
                    res = f_own[r, lanes].astype(F32)
                    aux = res + h2 if layer == 1 else res
                    sqh = sqh + fold(lv * (h2 * h2))
                    sqa = sqa + fold(lv * (aux * aux))
                    grads = [None, None]
                    for k in (1, 0):
                        part = slice(k * seqs, (k + 1) * seqs)
                        prior = h2[0:seqs] if k == 1 else hb
                        slope = 0.5 + 0.5 * jnp.tanh(0.5 * (drive[part] + rec * prior))
                        total = up[part] + down[m]
                        gd = lv[part] * slope * total
                        down[m] = (1.0 - lv[part]) * total + rec * gd
                        grads[k] = gd
                        rsum = rsum + fold(gd * prior)
                    gd2 = jnp.concatenate(grads, axis=0)
                    hid[layer, r, lanes] = gd2
                    s1[m] = s1[m] + fold(gd2)
                    s2[m] = s2[m] + fold(gd2 * normed)
                return tuple(down), tuple(s1), tuple(s2), rsum, sqh, sqa

            zero = jnp.zeros((seqs, QUART), F32)
            z8 = jnp.zeros((8, QUART), F32)
            _, s1, s2, rsum, sqh, sqa = lax.fori_loop(
                0, pairs, body, ((zero, zero), (z8, z8), (z8, z8), z8, z8, z8)
            )
            for k, x in enumerate((s1[0], s1[1], s2[0], s2[1], rsum, sqh, sqa)):
                tot[layer, k : k + 1, lanes] = jnp.sum(x, axis=0, keepdims=True)
        tot[layer, 7:8, :] = jnp.zeros((1, W), F32)

    def backward_stats(layer, between):
        rnd = 2 if layer == 1 else 4
        stage_start(in_plane, rnd, tot[layer])
        between()
        stage_wait(in_plane, rnd)
        stage_start(in_line, rnd, add_slots(in_plane, rnd))
        stage_wait(in_line, rnd)
        tot[layer] = add_slots(in_line, rnd)
        tot[layer, 7:8, :] = coef[layer, 2:3, :] + coef[layer, 5:6, :]

        @pl.when(section == layer)
        def _():
            pltpu.make_async_copy(tot.at[layer], v.at[section], v_sems.at[0]).start()

        @pl.when(section != layer)
        def _():
            v_across(layer).start()

    def v_across(layer):
        return pltpu.make_async_remote_copy(
            src_ref=tot.at[layer], dst_ref=v.at[section], send_sem=v_sems.at[1], recv_sem=v_sems.at[2],
            device_id=sibling, device_id_type=MESH,
        )

    def grad_rows(layer, slot):
        gain = vec_of(layer, 0)
        sends = []
        for lh in range(2):
            lanes = slice(lh * HALF, (lh + 1) * HALF)
            acc = jnp.zeros((8, HALF), F32)
            for m in range(2):
                mean = coef[layer, 3 * m : 3 * m + 1, lanes]
                scale = coef[layer, 3 * m + 1 : 3 * m + 2, lanes]
                count = coef[layer, 3 * m + 2 : 3 * m + 3, lanes]
                first = tot[layer, m : m + 1, lanes] / count
                second = tot[layer, 2 + m : 3 + m, lanes] / count * scale
                k = scale * gain[:, lanes]

                def body(i, acc):
                    r = pl.ds(aligned(m * span + i * (2 * seqs), 16), 2 * seqs)
                    y = hid[layer, r, lanes] - first - (rows[layer, r, lanes] - mean) * second
                    y = wide(live[r, :], 4) * (k * y)
                    g3[0, r, lanes] = y.astype(BF16)
                    return acc + fold(y)

                acc = lax.fori_loop(0, pairs, body, acc)
            top = lax.broadcasted_iota(jnp.int32, (16, HALF), 0) == 0
            minus = jnp.where(top, -jnp.sum(acc, axis=0, keepdims=True), 0.0)
            g3[0, total_rows:sent_rows, lanes] = minus.astype(BF16)
            made = across(g3.at[0, pl.ds(0, sent_rows), lanes], g3.at[1 + layer, pl.ds(0, sent_rows), lanes], slot + lh)
            made.start()
            sends.append(made)
        return sends

    def sums_start(layer):
        own_sum = -g3[0, total_rows:sent_rows, :].astype(F32)[0:1]
        far_sum = -g3[1 + layer, total_rows:sent_rows, :].astype(F32)[0:1]
        value = jnp.concatenate([own_sum, far_sum, jnp.zeros((6, W), F32)], axis=0)
        stage_start(in_plane, 3 if layer == 1 else 5, value)

    def sums_middle(layer):
        rnd = 3 if layer == 1 else 5
        stage_wait(in_plane, rnd)
        stage_start(in_line, rnd, add_slots(in_plane, rnd))

    def sums_end(layer):
        rnd = 3 if layer == 1 else 5
        stage_wait(in_line, rnd)
        vtot[layer] = add_slots(in_line, rnd)

    def transpose(src, layer):
        def body(j, _):
            c = pl.ds(aligned(j * 128, 128), 128)
            src_t[c, :] = src[:, c].T
            level = src[total_rows:sent_rows, c].astype(F32)[0:1]
            column[layer, c, :] = jnp.broadcast_to(level, (128, 128)).T.astype(BF16)
            return 0

        lax.fori_loop(0, W // 128, body, 0)

    def weight_grad(block, grads):
        def body(j, _):
            r = pl.ds(aligned(j * 256, 256), 256)
            block[r, :] = dot(src_t[r, :], grads[...], ((1,), (0,))).astype(BF16)
            return 0

        lax.fori_loop(0, W // 256, body, 0)

    def source_grad(store, w_own, w_far, far):
        def body(i, _):
            r = pl.ds(aligned((i // 2) * span, 16), span)
            c = pl.ds(aligned((i % 2) * HALF, HALF), HALF)
            y = dot(g3[0, r, :], w_own[c, :], ((1,), (1,))) + dot(g3[far, r, :], w_far[c, :], ((1,), (1,)))
            store(r, c, y)
            return 0

        lax.fori_loop(0, 4, body, 0)

    env = dict(vtot=vtot, column=column, r12=r12, r3=r3, ar_send=ar_send, ar_recv=ar_recv, ar_other=ar_other, o=o, section=section)

    def lanes_own(sec):
        return aligned(sec * W, W)

    def lanes_far(sec):
        return aligned((1 - sec) * W, W)

    blocks = {
        (1, 0): f_far.at[pl.ds(0, W), :],
        (1, 1): p_far.at[pl.ds(0, W), :],
        (0, 0): wc.at[1, 1],
        (0, 1): wr1,
    }
    parts = {}
    for layer in (1, 0):
        parts[layer, 0] = Reduction(env, layer, 0, blocks[layer, 0], axis_x, axis_y, axis_z, lanes_own)
        parts[layer, 1] = Reduction(env, layer, 1, blocks[layer, 1], axis_y, axis_x, axis_z, lanes_far)

    for spare in (f_own, p_own, g3.at[0], g3.at[1], g3.at[2]):
        spare[sent_rows:, :] = jnp.zeros((spare.shape[0] - sent_rows, W), BF16)

    by_units(frames, f_own, lambda: wait_heads(frames, 1))
    send_f = across(f_own.at[pl.ds(0, total_rows), :], f_far, 0)
    send_f.start()
    wait_w(0, w_plan(0), slot_of[0], 0)
    matmul_to(rows.at[0], f_own, wc.at[0, 0], True)
    wait_w(0, w_plan(0), slot_of[0], 1)
    send_f.wait()
    matmul_to(rows.at[0], f_far, wc.at[0, 1], False)
    send_vec.wait_send()
    across(vecs.at[other], vecs.at[other], 3).wait_recv()
    fetch(grad_out, 0).start()
    fetch(grad_out, 1).start()
    forward_stats(0)
    sends = forward_scan(0, True)
    wait_w(1, w_plan(1), slot_of[1], 0)
    matmul_to(rows.at[1], p_own, wc.at[1, 0], True)
    wait_w(1, w_plan(1), slot_of[1], 1)
    for made in sends:
        made.wait()
    done_w(0, w_plan(0), slot_of[0])

    start_local_w(0, late_plan, slot_of[2])
    start_across_w(0, late_plan, slot_of[2])

    @pl.when(section == 1)
    def _():
        wc[0, 1, width - late_row :, :] = jnp.zeros((W - width + late_row, W), BF16)
        heads_copy(grad_out, 2).start()

    matmul_to(rows.at[1], p_far, wc.at[1, 1], False)
    forward_stats(1, lambda: by_units(grad_out, f_far, lambda: wait_heads(grad_out, 2)))
    forward_scan(1, False)
    backward_scan(1, f_far)
    backward_stats(1, lambda: transpose(p_own, 1))
    sends = grad_rows(1, 20)
    weight_grad(blocks[1, 0], g3.at[0])
    parts[1, 0].advance()
    for made in sends:
        made.wait()
    sums_start(1)
    weight_grad(blocks[1, 1], g3.at[2])
    parts[1, 1].advance()
    wait_w(1, w_plan(1), slot_of[1], 2)
    done_w(1, w_plan(1), slot_of[1])

    def keep_down(r, c, y):
        p_own[r, c] = y.astype(BF16)

    source_grad(keep_down, wc.at[1, 0], wr1, 2)
    sums_middle(1)
    backward_scan(0, p_own)
    sums_end(1)
    backward_stats(0, lambda: transpose(f_own, 0))
    sends = grad_rows(0, 22)
    parts[1, 0].advance()
    parts[1, 1].advance()
    weight_grad(blocks[0, 0], g3.at[0])
    parts[0, 0].advance()
    for made in sends:
        made.wait()
    sums_start(0)
    weight_grad(blocks[0, 1], g3.at[1])
    parts[0, 1].advance()
    parts[1, 0].advance()
    parts[1, 1].advance()
    sums_middle(0)
    wait_w(0, late_plan, slot_of[2], 0)
    wait_w(0, late_plan, slot_of[2], 1)
    done_w(0, late_plan, slot_of[2])

    def keep_source(r, c, y):
        rows[0, r, c] = y

    fetch(grad_out, 0).start()
    fetch(grad_out, 1).start()
    source_grad(keep_source, wc.at[0, 0], wc.at[0, 1], 1)

    def give(c):
        piece = gf.at[c * chunk // steps, pl.ds(c * chunk % steps, chunk)]
        return pltpu.make_async_copy(stage_in.at[c % 2], piece, stage_sem.at[c % 2])

    for c in range(chunks):
        fetch(grad_out, c).wait()

        def finish_frames(i, _, c=c):
            straight = stage_in[c % 2, pl.ds(2 * i, 2)].astype(F32).reshape(2 * seqs, half)
            y = rows[0, pl.ds(aligned((c * chunk + 2 * i) * seqs, 8), 2 * seqs), :]
            y = jnp.where(section == 0, y[:, :half], y[:, late_shift : late_shift + half])
            stage_in[c % 2, pl.ds(2 * i, 2)] = (y + straight).reshape(2, seqs, half).astype(BF16)
            return 0

        lax.fori_loop(0, chunk // 2, finish_frames, 0)
        give(c).start()
        if c >= 1:
            give(c - 1).wait()
            if c + 1 < chunks:
                fetch(grad_out, c + 1).start()
    give(chunks - 1).wait()
    sums_end(0)
    for _ in range(7):
        for layer in (1, 0):
            parts[layer, 0].advance()
            parts[layer, 1].advance()

    for layer in range(2):

        @pl.when(section == layer)
        def _(layer=layer):
            pltpu.make_async_copy(tot.at[layer], v.at[section], v_sems.at[0]).wait()
            pltpu.make_async_remote_copy(
                src_ref=tot.at[layer], dst_ref=v.at[other], send_sem=v_sems.at[1], recv_sem=v_sems.at[2],
                device_id=sibling, device_id_type=MESH,
            ).wait_recv()

        @pl.when(section != layer)
        def _(layer=layer):
            v_across(layer).wait_send()

    own_part, far_part = v[section], v[other]
    first = jnp.where(section == 0, own_part, far_part)
    second = jnp.where(section == 0, far_part, own_part)
    for out, terms in ((out_gains, (2, 3)), (out_shifts, (0, 1)), (out_recurs, (4,))):
        out[0:1, 0:W] = sum(first[k : k + 1, :] for k in terms[1:]) + first[terms[0] : terms[0] + 1, :]
        out[0:1, W:width] = (
            sum(second[k : k + 1, :rest] for k in terms[1:]) + second[terms[0] : terms[0] + 1, :rest]
        )
    squares = jnp.sum(first[5:7, :] + second[5:7, :], axis=1, keepdims=True)
    root = jnp.sqrt(squares / (first[7:8, 0:1] * width))
    out_table[...] = jnp.concatenate([root[0:1], root[1:2]], axis=1)


def whole_step(dims, frames, grad_out, weights, tail, gains, shifts, recurs, lengths, masks):
    nz, ny, nx = dims
    micro, steps, seqs, half = frames.shape
    width = 2 * half
    views = seqs // lengths.shape[1]
    rows = micro * steps * seqs
    np_ = ny * nx
    wide_rows = (rows + 16 + 127) // 128 * 128
    r12_rows = max((a - 1) * (W // a) + (c - 1) * (W // a // c) for a, c in ((nx, ny), (ny, nx)))
    n1 = min(nx, ny)
    r2 = W // nx // ny
    ar_count = (nx - 1) + (ny - 1) + 2 * (nz - 1) + max(nx, ny) - 1 + max(nx, ny)
    any_ = pl.BlockSpec(memory_space=pl.ANY)
    held = pl.BlockSpec(memory_space=pltpu.VMEM)
    dma = pltpu.SemaphoreType.DMA
    return pl.pallas_call(
        functools.partial(kernel, dims, steps, seqs, views),
        out_shape=(
            jax.ShapeDtypeStruct((2, W, 2 * W), BF16),
            jax.ShapeDtypeStruct(frames.shape, BF16),
            jax.ShapeDtypeStruct((1, width), F32),
            jax.ShapeDtypeStruct((1, width), F32),
            jax.ShapeDtypeStruct((1, width), F32),
            jax.ShapeDtypeStruct((1, 2), F32),
        ),
        in_specs=[any_] * 4 + [held] * 5,
        out_specs=(any_, any_, held, held, held, held),
        scratch_shapes=[
            pltpu.VMEM((wide_rows, W), BF16),
            pltpu.VMEM((rows, W), BF16),
            pltpu.VMEM((wide_rows, W), BF16),
            pltpu.VMEM((rows, W), BF16),
            pltpu.VMEM((3, wide_rows, W), BF16),
            pltpu.VMEM((2, 2, W, W), BF16),
            pltpu.VMEM((W, W), BF16),
            pltpu.VMEM((W, wide_rows), BF16),
            pltpu.VMEM((rows, 128), F32),
            pltpu.VMEM((128, 128), F32),
            pltpu.VMEM((2, steps // 4, seqs, half), BF16),
            pltpu.VMEM((micro, steps, seqs, 128), BF16),
            pltpu.VMEM((2, 8, W), F32),
            pltpu.VMEM((2, 8, 2 * W), F32),
            pltpu.VMEM((2, rows, W), F32),
            pltpu.VMEM((2, rows, W), F32),
            pltpu.VMEM((2, 8, W), F32),
            pltpu.VMEM((2, 8, W), F32),
            pltpu.VMEM((2, 8, W), F32),
            pltpu.VMEM((2, W, 128), BF16),
            pltpu.VMEM((2, np_, 8, W), F32),
            pltpu.VMEM((2, nz, 8, W), F32),
            pltpu.VMEM((2, 2, max(r12_rows, W // n1), W), BF16),
            pltpu.VMEM((2, 2, max(nz - 1, 1), r2, W // nz), BF16),
            dma((3, 24)),
            dma((3,)),
            dma((2,)),
            dma((6, max(np_, 2))),
            dma((6, max(np_, 2))),
            dma((6, max(nz, 2))),
            dma((6, max(nz, 2))),
            dma((2, 2, ar_count)),
            dma((2, 2, ar_count)),
            dma((2, 2, max(nx, ny))),
        ],
        compiler_params=pltpu.CompilerParams(
            collective_id=0, has_side_effects=True, vmem_limit_bytes=64 * 1024 * 1024
        ),
    )(frames, grad_out, weights, tail, gains, shifts, recurs, lengths, masks)


def shards(dims, frames, grad_out, weights, gains, shifts, recurs, lengths, masks):
    width = 2 * frames.shape[3]
    last = W + (width - W) // 128 * 128
    tail = jnp.pad(weights[0, :, last:], ((0, 0), (0, 128 - (width - last))))
    o, grad_frames, grad_gains, grad_shifts, grad_recurs, table = whole_step(
        dims, frames, grad_out, weights, tail, gains, shifts, recurs, lengths, masks
    )
    grad_weight = o.reshape(2 * W, 2 * W)[:width, :width].astype(F32)
    return grad_frames, grad_weight[None], grad_gains, grad_shifts, grad_recurs, table


def solution(mesh):
    in_specs = (
        P(None, None, "batch", "section"),
        P(None, None, "batch", "section"),
        P("section", None, None),
        P("section", None),
        P("section", None),
        P("section", None),
        P(None, "batch"),
        P(None, None, "batch"),
    )
    out_specs = (
        P(None, None, "batch", "section"),
        P("section", None, None),
        P("section", None),
        P("section", None),
        P("section", None),
        P("section", None),
    )
    body = functools.partial(shards, grid_of(mesh.shape["batch"]))
    return jax.shard_map(body, mesh=mesh, in_specs=in_specs, out_specs=out_specs, check_vma=False)
```

```python
import functools

import jax
import jax.numpy as jnp
from jax import lax
from jax.experimental import pallas as pl
from jax.experimental.pallas import tpu as pltpu
from jax.sharding import PartitionSpec as P

EPS = 1e-05
W = 1024
HALF = W // 2
QUART = W // 4
MESH = pl.DeviceIdType.MESH
F32 = jnp.float32
BF16 = jnp.bfloat16


def grid_of(size):
    if size == 16:
        return (4, 2, 2)
    if size == 128:
        return (8, 4, 4)
    return (size, 1, 1)


def aligned(x, k):
    return pl.multiple_of(x, k)


def wide(x, reps):
    return jnp.concatenate([x] * reps, axis=1)


def fold(x):
    rows = x.shape[0]
    total = x[0:8]
    for k in range(8, rows, 8):
        total = total + x[k : k + 8]
    return total


def dot(a, b, dims):
    return lax.dot_general(a, b, (dims, ((), ())), preferred_element_type=F32)


class Reduction:
    def __init__(self, env, layer, index, block, orders, lane_of):
        self.env, self.layer, self.index, self.block, self.orders = env, layer, index, block, orders
        self.lane_of = lane_of
        self.space = env["space"].at[layer, index]
        self.depth = len(orders[0])
        self.regions = [self.halves(i, order) for i, order in enumerate(orders)]
        self.step = 0
        self.waits = []
        depth = self.depth
        self.steps = [functools.partial(self.scatter, 0)]
        self.steps += [functools.partial(self.scatter, k) for k in range(1, depth)]
        self.steps += [functools.partial(self.gather, k) for k in range(depth - 1, 0, -1)]
        self.steps += [self.give, self.finish]

    def halves(self, i, order):
        row, rows, lane, lanes = 0, W, i * QUART, QUART
        out = [(row, rows, lane, lanes)]
        for axis in order:
            if rows > 16:
                rows //= 2
                row = row + axis["bit"] * rows
            else:
                lanes //= 2
                lane = lane + axis["bit"] * lanes
            out.append((row, rows, lane, lanes))
        return out

    @property
    def free_to_go(self):
        return self.step != self.depth or self.layer in self.env["summed"]

    @property
    def done(self):
        return self.step >= len(self.steps)

    def advance(self):
        self.sent = []
        self.steps[self.step]()
        self.step += 1
        return self.sent

    def remote(self, i, src, dst, slot, where, recv=None):
        sems = (self.layer, self.index, i, slot)
        return pltpu.make_async_remote_copy(
            src_ref=src, dst_ref=dst, send_sem=self.env["ar_send"].at[sems],
            recv_sem=self.env["ar_recv"].at[sems] if recv is None else recv, device_id=where, device_id_type=MESH,
        )

    def wait(self):
        for made, came in self.waits:
            made.wait_send()
            came.wait_recv()
        self.waits = []

    def came_at(self, i, k):
        row = sum(r[1] for r in self.regions[i][1 : k + 1])
        _, rows, _, lanes = self.regions[i][k + 1]
        return row, rows, i * QUART, lanes

    def scatter(self, k):
        if k > 0:
            self.wait()
            self.add(k - 1)
        for i, order in enumerate(self.orders):
            self.scatter_part(i, k, order[k])

    def start_part(self, i):
        self.sent = []
        self.scatter_part(i, 0, self.orders[i][0])
        if i == 1:
            self.step = 1
        return self.sent

    def scatter_part(self, i, k, axis):
        row, rows, lane, lanes = self.regions[i][k]
        _, rows2, _, lanes2 = self.regions[i][k + 1]
        give_row = row + (1 - axis["bit"]) * rows2 if rows2 < rows else row
        give_lane = lane if rows2 < rows else lane + (1 - axis["bit"]) * lanes2
        src = self.block.at[pl.ds(aligned(give_row, 16), rows2), pl.ds(aligned(give_lane, 128), lanes2)]
        at, n, at_lane, n_lanes = self.came_at(i, k)
        dst = self.space.at[pl.ds(at, n), pl.ds(at_lane, n_lanes)]
        made = self.remote(i, src, dst, k, axis["partner"])
        made.start()
        self.waits.append((made, made))
        self.sent.append((axis["link"], rows2 * lanes2 * 2))

    def add(self, k, last=False):
        rows = self.regions[0][k + 1][1]
        size = min(rows, 32)
        out = []
        for i in range(2):
            row, _, lane, lanes = self.regions[i][k + 1]
            at, _, at_lane, _ = self.came_at(i, k)
            lane = aligned(lane, 128)
            extra = None
            if last:
                part = self.index // 2
                first = aligned((self.index % 2) * HALF + lane, 128)
                extra = self.env["vtot"][self.layer, part : part + 1, pl.ds(first, lanes)]
            out.append((row, lane, lanes, at, at_lane, self.local(i, k + 1)[0], extra))

        def body(j, _):
            for row, lane, lanes, at, at_lane, home, extra in out:
                here = pl.ds(aligned(row + j * size, 16), size)
                total = self.block[here, pl.ds(lane, lanes)].astype(F32)
                total = total + self.space[pl.ds(aligned(at + j * size, 16), size), pl.ds(at_lane, lanes)].astype(F32)
                if last:
                    column = self.env["column"][self.layer, here, :].astype(F32)
                    total = total + wide(column, lanes // 128) * extra
                    to = pl.ds(aligned(home + j * size, 16), size)
                    self.space[to, pl.ds(lane, lanes)] = total.astype(BF16)
                else:
                    self.block[here, pl.ds(lane, lanes)] = total.astype(BF16)
            return 0

        lax.fori_loop(0, rows // size, body, 0)

    def local(self, i, k):
        row, rows, lane, lanes = self.regions[i][k]
        return row - self.regions[i][1][0], rows, lane, lanes

    def gather(self, k):
        self.wait()
        if k == self.depth - 1:
            self.add(k, last=True)
        for i, order in enumerate(self.orders):
            axis = order[k]
            row, rows, lane, lanes = self.local(i, k + 1)
            row0, rows0, lane0, lanes0 = self.local(i, k)
            if rows0 > rows:
                far = (row0 + (1 - axis["bit"]) * rows, rows, lane, lanes)
            else:
                far = (row, rows, lane0 + (1 - axis["bit"]) * lanes, lanes)
            refs = [
                self.space.at[pl.ds(aligned(r, 16), n), pl.ds(aligned(c, 128), w)]
                for r, n, c, w in ((row, rows, lane, lanes), far)
            ]
            made = self.remote(i, refs[0], refs[0], self.depth + k, axis["partner"])
            made.start()
            self.waits.append((made, self.remote(i, refs[1], refs[1], self.depth + k, axis["partner"])))
            self.sent.append((axis["link"], rows * lanes * 2))

    def result(self, i, bit, section):
        rows = self.regions[i][1][1]
        lane = aligned(self.lane_of(section) + i * QUART, QUART)
        return self.env["o"].at[section, pl.ds(aligned(bit * rows, 16), rows), pl.ds(lane, QUART)]

    def gathered(self, i):
        return self.space.at[pl.ds(0, self.regions[i][1][1]), pl.ds(i * QUART, QUART)]

    def deliver(self, i, near, straight):
        axis, section = self.orders[i][0], self.env["section"]
        slot = 2 * self.depth + (0 if near else 1)
        recv = None if straight else self.env["ar_other"].at[self.layer, self.index, i, 0 if near else 1]
        where = dict(self.env["here"] if near else axis["partner"], section=self.layer)
        return self.remote(i, self.gathered(i), self.result(i, axis["bit"], section), slot, where, recv)

    def arrival(self, i, near, straight):
        axis, section = self.orders[i][0], self.env["section"]
        slot = 2 * self.depth + (0 if near else 1)
        recv = None if straight else self.env["ar_other"].at[self.layer, self.index, i, 0 if near else 1]
        bit = axis["bit"] if near else 1 - axis["bit"]
        frm = section if straight else 1 - section
        where = dict(self.env["here"] if near else axis["partner"], section=frm)
        return self.remote(i, self.gathered(i), self.result(i, bit, frm), slot, where, recv)

    def kept(self, i):
        sem = self.env["ar_recv"].at[self.layer, self.index, i, 2 * self.depth]
        return pltpu.make_async_copy(
            self.gathered(i), self.result(i, self.orders[i][0]["bit"], self.env["section"]), sem
        )

    def give(self):
        self.wait()

        @pl.when(self.env["section"] == self.layer)
        def _():
            for i in range(2):
                self.deliver(i, False, True).start()
                self.kept(i).start()

        @pl.when(self.env["section"] != self.layer)
        def _():
            for i in range(2):
                self.deliver(i, False, False).start()
                self.deliver(i, True, False).start()

        for i, order in enumerate(self.orders):
            self.sent.append((order[0]["link"], self.regions[i][1][1] * QUART * 2))

    def finish(self):
        @pl.when(self.env["section"] == self.layer)
        def _():
            for i in range(2):
                self.kept(i).wait()
                self.deliver(i, False, True).wait_send()
                self.arrival(i, False, True).wait_recv()
                self.arrival(i, True, False).wait_recv()
                self.arrival(i, False, False).wait_recv()

        @pl.when(self.env["section"] != self.layer)
        def _():
            for i in range(2):
                self.deliver(i, False, False).wait_send()
                self.deliver(i, True, False).wait_send()


class Order:
    RATE, HOP = 45e3, 2.0

    def __init__(self):
        self.now = 0.0
        self.free = {}
        self.going = []

    def sent(self, copies):
        end = self.now
        for link, size in copies:
            self.free[link] = max(self.now, self.free.get(link, 0.0)) + size / self.RATE
            end = max(end, self.free[link])
        return end + self.HOP

    def begin(self, one, i):
        end = self.sent(one.start_part(i))
        if i == 0:
            one.due = end
        else:
            one.due = max(one.due, end)
            self.going.append(one)

    def advance(self, one):
        self.now = max(self.now, one.due) + 0.4
        one.due = self.sent(one.advance())
        if one.done:
            self.going.remove(one)

    def work(self, cost):
        self.now += cost
        while True:
            due = [x for x in self.going if x.due <= self.now and x.free_to_go]
            if not due:
                return
            self.advance(min(due, key=lambda x: x.due))

    def drain(self):
        while self.going:
            self.advance(min(self.going, key=lambda x: x.due))


def kernel(dims, steps, seqs, views, frames, grad_out, weights, tail, gains, shifts, recurs, lengths, masks, o, gf,
           out_gains, out_shifts, out_recurs, out_table, f_own, f_far, p_own, p_far, g3, wc, wr1, src_t, live, turn,
           stage_in, heads, v, vecs, rows, hid, coef, tot, vtot, column, st_plane, st_z, space, sems, v_sems, stage_sem, pl_send, pl_recv, z_send, z_recv,
           ar_send, ar_recv, ar_other):
    nz, ny, nx = dims
    np_ = ny * nx
    span = steps * seqs
    total_rows = 2 * span
    sent_rows = total_rows + 16
    pairs = steps // 2
    section = lax.axis_index("section")
    other = 1 - section
    b = lax.axis_index("batch")
    mx = lax.rem(b, nx)
    my = lax.rem(b // nx, ny)
    mz = b // np_
    mp = lax.rem(b, np_)

    def at_x(i):
        return {"batch": b - mx + i}

    def at_y(i):
        return {"batch": b + (i - my) * nx}

    def at_z(i):
        return {"batch": b + (i - mz) * np_}

    def at_plane(i):
        return {"batch": b - mp + i}

    bits = []
    for link, count, stride in (("x", nx, 1), ("y", ny, nx), ("z", nz, np_)):
        while count > 1:
            bit = lax.rem(b // stride, 2)
            bits.append(dict(bit=bit, partner={"batch": b + (1 - 2 * bit) * stride}, link=link))
            count //= 2
            stride *= 2
    sibling = {"section": other}

    def local(src, dst, slot):
        return pltpu.make_async_copy(src, dst, sems.at[0, slot])

    def across(src, dst, slot):
        return pltpu.make_async_remote_copy(
            src_ref=src, dst_ref=dst, send_sem=sems.at[1, slot], recv_sem=sems.at[2, slot],
            device_id=sibling, device_id_type=MESH,
        )

    half = frames.shape[3]
    width = 2 * half
    lead = W - half
    rest = width - W
    full = rest // 128 * 128
    chunk = stage_in.shape[1]
    chunks = 2 * steps // chunk

    def fetch(source, c):
        piece = source.at[c * chunk // steps, pl.ds(c * chunk % steps, chunk)]
        return pltpu.make_async_copy(piece, stage_in.at[c % 2], stage_sem.at[c % 2])

    def by_units(source, target, ready):
        for c in range(chunks):
            fetch(source, c).wait()
            if c == 0:
                ready()

            def place(i, _, c=c):
                x = stage_in[c % 2, pl.ds(2 * i, 2)].astype(F32).reshape(2 * seqs, half)
                to = pl.ds(aligned((c * chunk + 2 * i) * seqs, 16), 2 * seqs)

                @pl.when(section == 0)
                def _():
                    t = c * chunk % steps + 2 * i
                    head = heads[c * chunk // steps, pl.ds(t, 2)].astype(F32).reshape(2 * seqs, 128)
                    target[to, :] = jnp.concatenate([x, head[:, :lead]], axis=1).astype(BF16)

                @pl.when(section == 1)
                def _():
                    pad = jnp.zeros((2 * seqs, 2 * lead), F32)
                    target[to, :] = jnp.concatenate([x[:, lead:], pad], axis=1).astype(BF16)

                return 0

            lax.fori_loop(0, chunk // 2, place, 0)
            if c + 2 < chunks:
                fetch(source, c + 2).start()

    def pieces(row, count, u, block):
        r = pl.ds(row, count)
        to = pl.ds(0, count)
        if u == 0:
            return [(weights.at[0, r, pl.ds(0, W)], block.at[to, :])]
        return [
            (weights.at[0, r, pl.ds(W, full)], block.at[to, pl.ds(0, full)]),
            (tail.at[r, :], block.at[to, pl.ds(full, 128)]),
        ]

    rows_of = {0: (0, W), 1: (W, rest)}

    def w_plan(layer):
        mine, far = rows_of[layer], rows_of[1 - layer]
        plan = [
            (mine, layer, far, 1 - layer, wc.at[layer, 0]),
            (far, layer, mine, 1 - layer, wc.at[layer, 1]),
        ]
        if layer == 1:
            plan.append((mine, 0, far, 1, wr1))
        return plan

    late_row = (width - half) // 16 * 16
    late_shift = half - late_row
    late_plan = [
        ((0, W), 0, (late_row, width - late_row), 1, wc.at[0, 0]),
        ((0, W), 1, (late_row, width - late_row), 0, wc.at[0, 1]),
    ]
    slot_of = {0: 4, 1: 8, 2: 14}

    def local_w(plan, base, which):
        r, u, _, _, block = plan[which]
        return [local(a, t, base + 2 * which + i) for i, (a, t) in enumerate(pieces(*r, u, block))]

    def across_w(plan, base, which):
        _, _, r, u, block = plan[which]
        return [across(a, t, base + 2 * which + i) for i, (a, t) in enumerate(pieces(*r, u, block))]

    def start_local_w(layer, plan, base):
        @pl.when(section == layer)
        def _():
            for which in range(len(plan)):
                for made in local_w(plan, base, which):
                    made.start()

    def start_across_w(layer, plan, base):
        @pl.when(section == layer)
        def _():
            for which in range(len(plan)):
                for made in across_w(plan, base, which):
                    made.start()

    fetch(frames, 0).start()
    fetch(frames, 1).start()
    for layer in range(2):
        start_local_w(layer, w_plan(layer), slot_of[layer])

    barrier = pltpu.get_barrier_semaphore()
    greeted = [dict(sibling)]
    greeted += [at_plane(lax.rem(mp + k, np_)) for k in range(1, np_)]
    greeted += [at_z(lax.rem(mz + k, nz)) for k in range(1, nz)]
    greeted += [dict(axis["partner"], section=other) for axis in bits]
    for where in greeted:
        pl.semaphore_signal(barrier, inc=1, device_id=where, device_id_type=MESH)
    pl.semaphore_wait(barrier, len(greeted))

    def heads_copy(source, slot):
        return across(source.at[:, :, :, pl.ds(0, 128)], heads, slot)

    @pl.when(section == 1)
    def _():
        heads_copy(frames, 1).start()

    for layer in range(2):
        start_across_w(layer, w_plan(layer), slot_of[layer])

    def wait_w(layer, plan, base, which):
        @pl.when(section == layer)
        def _():
            for made in local_w(plan, base, which):
                made.wait()

        @pl.when(section != layer)
        def _():
            for made in across_w(plan, base, which):
                made.wait_recv()

    def done_w(layer, plan, base):
        @pl.when(section == layer)
        def _():
            for which in range(len(plan)):
                for made in across_w(plan, base, which):
                    made.wait_send()

    def wait_heads(source, slot):
        @pl.when(section == 0)
        def _():
            heads_copy(source, slot).wait_recv()

        @pl.when(section == 1)
        def _():
            heads_copy(source, slot).wait_send()

    for k, (x, fill) in enumerate(((gains, 0.0), (shifts, -1e30), (recurs, 0.0))):
        vecs[section, k : k + 1, 0:width] = x[...]
        vecs[section, k : k + 1, width:] = jnp.full((1, 2 * W - width), fill, F32)
    vecs[section, 3:8, :] = jnp.zeros((5, 2 * W), F32)
    send_vec = across(vecs.at[section], vecs.at[section], 3)
    send_vec.start()

    gap = jnp.zeros((W - rest, W), BF16)

    @pl.when(section == 0)
    def _():
        wc[0, 1, rest:, :] = gap
        wc[1, 1, rest:, :] = gap

    @pl.when(section == 1)
    def _():
        wc[0, 0, rest:, :] = gap
        wc[1, 0, rest:, :] = gap
        wr1[rest:, :] = gap

    for m in range(2):
        turn[...] = jnp.zeros_like(turn)
        turn[0:steps, 0:seqs] = masks[m].astype(F32)
        mask = turn[...].T[0:seqs]
        groups = lengths.shape[1]
        s_at = lax.broadcasted_iota(jnp.int32, (seqs, groups), 0)
        g_at = lax.broadcasted_iota(jnp.int32, (seqs, groups), 1) * views
        there = (s_at >= g_at) & (s_at < g_at + views)
        length = jnp.broadcast_to(lengths[m : m + 1, :], (seqs, groups)).astype(F32)
        limit = jnp.sum(jnp.where(there, length, 0.0), axis=1, keepdims=True)
        position = lax.broadcasted_iota(jnp.int32, (seqs, 128), 1)
        alive = (position.astype(F32) < limit) & ((mask > 0.0) | (position == 0))
        alive = alive.astype(F32)
        for t in range(steps):
            at = m * span + t * seqs
            live[at : at + seqs, :] = jnp.broadcast_to(alive[:, t : t + 1], (seqs, 128))

    def matmul_to(out, a, w, first):
        def body(i, _):
            r = pl.ds(aligned((i // 2) * span, 16), span)
            c = pl.ds(aligned((i % 2) * HALF, HALF), HALF)
            y = dot(a[r, :], w[:, c], ((1,), (0,)))
            out[r, c] = y if first else out[r, c] + y
            return 0

        lax.fori_loop(0, 4, body, 0)

    def vec_of(layer, k):
        return vecs[layer, k : k + 1, pl.ds(aligned(section * W, W), W)]

    def stage_copy(where, rnd, slot, k, back):
        buf, size, me, at, send, recv = where
        there = at(lax.rem(me + (size - k if back else k), size))
        ref = buf.at[rnd % 2, slot]
        return pltpu.make_async_remote_copy(
            src_ref=ref, dst_ref=ref, send_sem=send.at[rnd, k], recv_sem=recv.at[rnd, k],
            device_id=there, device_id_type=MESH,
        )

    in_plane = (st_plane, np_, mp, at_plane, pl_send, pl_recv)
    in_line = (st_z, nz, mz, at_z, z_send, z_recv)

    def stage_start(where, rnd, value):
        buf, size, me = where[:3]
        buf[rnd % 2, me] = value
        for k in range(1, size):
            stage_copy(where, rnd, me, k, False).start()

    def stage_wait(where, rnd):
        size, me = where[1:3]
        for k in range(1, size):
            stage_copy(where, rnd, me, k, False).wait_send()
            stage_copy(where, rnd, lax.rem(me + size - k, size), k, True).wait_recv()

    def add_slots(where, rnd):
        buf, size, idx = where[0], where[1], rnd % 2
        total = buf[idx, 0]
        for k in range(1, size):
            total = total + buf[idx, k]
        return total

    def merge_slots(where, rnd):
        buf, size, idx = where[0], where[1], rnd % 2
        out = []
        for m in range(2):
            s = [buf[idx, k, 3 * m : 3 * m + 1, :] for k in range(size)]
            q = [buf[idx, k, 3 * m + 1 : 3 * m + 2, :] for k in range(size)]
            n = [buf[idx, k, 3 * m + 2 : 3 * m + 3, :] for k in range(size)]
            total, squares, count = sum(s[1:], s[0]), sum(q[1:], q[0]), sum(n[1:], n[0])
            mean = total / count
            for k in range(size):
                d = s[k] / n[k] - mean
                squares = squares + n[k] * d * d
            out += [total, squares, count]
        both = [buf[idx, k, 6:8, :] for k in range(size)]
        return jnp.concatenate(out + [sum(both[1:], both[0])], axis=0)

    def forward_stats(layer, between=None):
        out = []
        source = f_own if layer == 0 else p_own
        level = jnp.zeros((8, W), F32)
        for m in range(2):

            def sums(i, carry):
                acc, cnt, lev = carry
                r = pl.ds(aligned(m * span + i * (2 * seqs), 16), 2 * seqs)
                lv = live[r, :]
                keep = wide(lv, 8)
                acc = acc + fold(keep * rows[layer, r, :])
                return acc, cnt + fold(lv), lev + fold(keep * source[r, :].astype(F32))

            acc, cnt, level = lax.fori_loop(
                0, pairs, sums, (jnp.zeros((8, W), F32), jnp.zeros((8, 128), F32), level)
            )
            total = jnp.sum(acc, axis=0, keepdims=True)
            count = wide(jnp.sum(cnt, axis=0, keepdims=True), 8)
            mean = total / count

            def squares(i, acc):
                r = pl.ds(aligned(m * span + i * (2 * seqs), 16), 2 * seqs)
                d = rows[layer, r, :] - mean
                return acc + fold(wide(live[r, :], 8) * (d * d))

            sq = lax.fori_loop(0, pairs, squares, jnp.zeros((8, W), F32))
            out += [total, jnp.sum(sq, axis=0, keepdims=True), count]
        level = jnp.sum(level, axis=0, keepdims=True)
        value = jnp.concatenate(out + [level, jnp.zeros_like(level)], axis=0)
        stage_start(in_plane, layer, value)
        if between is not None:
            between()
        stage_wait(in_plane, layer)
        stage_start(in_line, layer, merge_slots(in_plane, layer))
        stage_wait(in_line, layer)
        value = merge_slots(in_line, layer)
        for m in range(2):
            count = value[3 * m + 2 : 3 * m + 3]
            mean = value[3 * m : 3 * m + 1] / count
            spread = value[3 * m + 1 : 3 * m + 2] / count
            coef[layer, 3 * m : 3 * m + 1, :] = mean
            coef[layer, 3 * m + 1 : 3 * m + 2, :] = lax.rsqrt(spread + EPS)
            coef[layer, 3 * m + 2 : 3 * m + 3, :] = count
        level = value[6:7] / (value[2:3] + value[5:6])
        top = lax.broadcasted_iota(jnp.int32, (16, W), 0) == 0
        source[total_rows:sent_rows, :] = jnp.where(top, level, 0.0).astype(BF16)

    def forward_scan(layer, keep_passed):
        gain, shift, recur = vec_of(layer, 0), vec_of(layer, 1), vec_of(layer, 2)
        sends = []
        for lh in range(2):
            lanes = slice(lh * HALF, (lh + 1) * HALF)
            a, c = [], []
            for m in range(2):
                mean = coef[layer, 3 * m : 3 * m + 1, lanes]
                scale = coef[layer, 3 * m + 1 : 3 * m + 2, lanes]
                a.append(gain[:, lanes] * scale)
                c.append((shift[:, lanes], mean))
            rec = recur[:, lanes]

            def body(i, carry):
                out = []
                for m in range(2):
                    r = pl.ds(aligned(m * span + i * (2 * seqs), 16), 2 * seqs)
                    x = (rows[layer, r, lanes] - c[m][1]) * a[m] + c[m][0]
                    alive = wide(live[r, :], 4) > 0.0
                    h = carry[m]
                    both = []
                    for k in range(2):
                        part = slice(k * seqs, (k + 1) * seqs)
                        z = x[part] + rec * h
                        soft = jnp.maximum(z, 0.0) + jnp.log(1.0 + jnp.exp(-jnp.abs(z)))
                        h = jnp.where(alive[part], soft, h)
                        both.append(h)
                    two = jnp.concatenate(both, axis=0)
                    hid[layer, r, lanes] = two
                    if keep_passed:
                        p_own[r, lanes] = two.astype(BF16)
                    out.append(h)
                return tuple(out)

            zero = jnp.zeros((seqs, HALF), F32)
            lax.fori_loop(0, pairs, body, (zero, zero))
            if keep_passed:
                made = across(p_own.at[pl.ds(0, total_rows), lanes], p_far.at[:, lanes], 18 + lh)
                made.start()
                sends.append(made)
        return sends

    def backward_scan(layer, above, between=lambda: None):
        gain, shift, recur = vec_of(layer, 0), vec_of(layer, 1), vec_of(layer, 2)
        for lq in range(4):
            lanes = slice(lq * QUART, (lq + 1) * QUART)
            gq, sq, rec = gain[:, lanes], shift[:, lanes], recur[:, lanes]
            mean = [coef[layer, 3 * m : 3 * m + 1, lanes] for m in range(2)]
            scale = [coef[layer, 3 * m + 1 : 3 * m + 2, lanes] for m in range(2)]

            def body(i, carry):
                down, s1, s2, rsum, sqh, sqa = carry
                down, s1, s2 = list(down), list(s1), list(s2)
                i = pairs - 1 - i
                for m in range(2):
                    start = m * span + i * (2 * seqs)
                    r = pl.ds(aligned(start, 16), 2 * seqs)
                    before = pl.ds(aligned(jnp.maximum(start - seqs, 0), 8), seqs)
                    normed = (rows[layer, r, lanes] - mean[m]) * scale[m]
                    drive = gq * normed + sq
                    h2 = hid[layer, r, lanes]
                    hb = jnp.where(i > 0, hid[layer, before, lanes], 0.0)
                    lv = wide(live[r, :], 2)
                    up = above[r, lanes].astype(F32)
                    res = f_own[r, lanes].astype(F32)
                    aux = res + h2 if layer == 1 else res
                    sqh = sqh + fold(lv * (h2 * h2))
                    sqa = sqa + fold(lv * (aux * aux))
                    grads = [None, None]
                    for k in (1, 0):
                        part = slice(k * seqs, (k + 1) * seqs)
                        prior = h2[0:seqs] if k == 1 else hb
                        slope = 0.5 + 0.5 * jnp.tanh(0.5 * (drive[part] + rec * prior))
                        total = up[part] + down[m]
                        gd = lv[part] * slope * total
                        down[m] = (1.0 - lv[part]) * total + rec * gd
                        grads[k] = gd
                        rsum = rsum + fold(gd * prior)
                    gd2 = jnp.concatenate(grads, axis=0)
                    hid[layer, r, lanes] = gd2
                    s1[m] = s1[m] + fold(gd2)
                    s2[m] = s2[m] + fold(gd2 * normed)
                return tuple(down), tuple(s1), tuple(s2), rsum, sqh, sqa

            zero = jnp.zeros((seqs, QUART), F32)
            z8 = jnp.zeros((8, QUART), F32)
            _, s1, s2, rsum, sqh, sqa = lax.fori_loop(
                0, pairs, body, ((zero, zero), (z8, z8), (z8, z8), z8, z8, z8)
            )
            for k, x in enumerate((s1[0], s1[1], s2[0], s2[1], rsum, sqh, sqa)):
                tot[layer, k : k + 1, lanes] = jnp.sum(x, axis=0, keepdims=True)
            between()
        tot[layer, 7:8, :] = jnp.zeros((1, W), F32)

    def backward_stats(layer, between, after=lambda: None):
        rnd = 2 if layer == 1 else 4
        stage_start(in_plane, rnd, tot[layer])
        between()
        after()
        stage_wait(in_plane, rnd)
        stage_start(in_line, rnd, add_slots(in_plane, rnd))
        after()
        stage_wait(in_line, rnd)
        tot[layer] = add_slots(in_line, rnd)
        tot[layer, 7:8, :] = coef[layer, 2:3, :] + coef[layer, 5:6, :]

        @pl.when(section == layer)
        def _():
            pltpu.make_async_copy(tot.at[layer], v.at[section], v_sems.at[0]).start()

        @pl.when(section != layer)
        def _():
            v_across(layer).start()

    def v_across(layer):
        return pltpu.make_async_remote_copy(
            src_ref=tot.at[layer], dst_ref=v.at[section], send_sem=v_sems.at[1], recv_sem=v_sems.at[2],
            device_id=sibling, device_id_type=MESH,
        )

    def grad_rows(layer, slot):
        gain = vec_of(layer, 0)
        sends = []
        for lh in range(2):
            lanes = slice(lh * HALF, (lh + 1) * HALF)
            acc = jnp.zeros((8, HALF), F32)
            for m in range(2):
                mean = coef[layer, 3 * m : 3 * m + 1, lanes]
                scale = coef[layer, 3 * m + 1 : 3 * m + 2, lanes]
                count = coef[layer, 3 * m + 2 : 3 * m + 3, lanes]
                first = tot[layer, m : m + 1, lanes] / count
                second = tot[layer, 2 + m : 3 + m, lanes] / count * scale
                k = scale * gain[:, lanes]

                def body(i, acc):
                    r = pl.ds(aligned(m * span + i * (2 * seqs), 16), 2 * seqs)
                    y = hid[layer, r, lanes] - first - (rows[layer, r, lanes] - mean) * second
                    y = wide(live[r, :], 4) * (k * y)
                    g3[0, r, lanes] = y.astype(BF16)
                    return acc + fold(y)

                acc = lax.fori_loop(0, pairs, body, acc)
            top = lax.broadcasted_iota(jnp.int32, (16, HALF), 0) == 0
            minus = jnp.where(top, -jnp.sum(acc, axis=0, keepdims=True), 0.0)
            g3[0, total_rows:sent_rows, lanes] = minus.astype(BF16)
            made = across(g3.at[0, pl.ds(0, sent_rows), lanes], g3.at[1 + layer, pl.ds(0, sent_rows), lanes], slot + lh)
            made.start()
            sends.append(made)
        return sends

    def sums_start(layer):
        own_sum = -g3[0, total_rows:sent_rows, :].astype(F32)[0:1]
        far_sum = -g3[1 + layer, total_rows:sent_rows, :].astype(F32)[0:1]
        value = jnp.concatenate([own_sum, far_sum, jnp.zeros((6, W), F32)], axis=0)
        stage_start(in_plane, 3 if layer == 1 else 5, value)

    def sums_middle(layer):
        rnd = 3 if layer == 1 else 5
        stage_wait(in_plane, rnd)
        stage_start(in_line, rnd, add_slots(in_plane, rnd))

    def sums_end(layer):
        rnd = 3 if layer == 1 else 5
        stage_wait(in_line, rnd)
        vtot[layer] = add_slots(in_line, rnd)
        env["summed"].add(layer)

    def transpose(src, layer):
        def body(j, _):
            c = pl.ds(aligned(j * 128, 128), 128)
            src_t[c, :] = src[:, c].T
            level = src[total_rows:sent_rows, c].astype(F32)[0:1]
            column[layer, c, :] = jnp.broadcast_to(level, (128, 128)).T.astype(BF16)
            return 0

        lax.fori_loop(0, W // 128, body, 0)

    def weight_part(block, grads, c):
        lanes = pl.ds(c * QUART, QUART)

        def body(j, _):
            r = pl.ds(aligned(j * HALF, HALF), HALF)
            block[r, lanes] = dot(src_t[r, :], grads[:, lanes], ((1,), (0,))).astype(BF16)
            return 0

        lax.fori_loop(0, W // HALF, body, 0)

    def source_grad(store, w_own, w_far, far, between):
        for m in range(2):
            r = pl.ds(m * span, span)

            def body(i, _):
                c = pl.ds(aligned(i * HALF, HALF), HALF)
                y = dot(g3[0, r, :], w_own[c, :], ((1,), (1,))) + dot(g3[far, r, :], w_far[c, :], ((1,), (1,)))
                store(r, c, y)
                return 0

            lax.fori_loop(0, 2, body, 0)
            between()

    env = dict(summed=set(), vtot=vtot, column=column, space=space, ar_send=ar_send, ar_recv=ar_recv, ar_other=ar_other, o=o,
               section=section, here={"batch": b})
    xs = [a for a in bits if a["link"] == "x"]
    ys = [a for a in bits if a["link"] == "y"]
    zs = [a for a in bits if a["link"] == "z"]
    flat = (xs + ys + zs, ys + xs + zs)
    tall = (zs + xs + ys, zs + ys + xs)
    blocks = {
        (1, 0): f_far.at[pl.ds(0, W), :],
        (1, 1): p_far.at[pl.ds(0, W), :],
        (0, 0): wc.at[1, 1],
        (0, 1): wr1,
    }
    parts = {}
    for layer in (1, 0):
        for index, orders in enumerate((flat, tall, flat, flat)):
            part, side = index // 2, index % 2

            def lane_of(sec, part=part, side=side):
                return (sec if part == 0 else 1 - sec) * W + side * HALF

            block = blocks[layer, part].at[:, pl.ds(side * HALF, HALF)]
            parts[layer, index] = Reduction(env, layer, index, block, orders, lane_of)
    order = Order()

    def weight_grads(layer, far, between):
        for part, grads in enumerate((g3.at[0], g3.at[far])):
            if part == 1:
                between()
            for c in range(4):
                weight_part(blocks[layer, part], grads, c)
                order.work(0.9)
                order.begin(parts[layer, 2 * part + c // 2], c % 2)

    for spare in (f_own, p_own, g3.at[0], g3.at[1], g3.at[2]):
        spare[sent_rows:, :] = jnp.zeros((spare.shape[0] - sent_rows, W), BF16)

    by_units(frames, f_own, lambda: wait_heads(frames, 1))
    send_f = across(f_own.at[pl.ds(0, total_rows), :], f_far, 0)
    send_f.start()
    wait_w(0, w_plan(0), slot_of[0], 0)
    matmul_to(rows.at[0], f_own, wc.at[0, 0], True)
    wait_w(0, w_plan(0), slot_of[0], 1)
    send_f.wait()
    matmul_to(rows.at[0], f_far, wc.at[0, 1], False)
    send_vec.wait_send()
    across(vecs.at[other], vecs.at[other], 3).wait_recv()
    fetch(grad_out, 0).start()
    fetch(grad_out, 1).start()
    forward_stats(0)
    sends = forward_scan(0, True)
    wait_w(1, w_plan(1), slot_of[1], 0)
    matmul_to(rows.at[1], p_own, wc.at[1, 0], True)
    wait_w(1, w_plan(1), slot_of[1], 1)
    for made in sends:
        made.wait()
    done_w(0, w_plan(0), slot_of[0])

    start_local_w(0, late_plan, slot_of[2])
    start_across_w(0, late_plan, slot_of[2])

    @pl.when(section == 1)
    def _():
        wc[0, 1, width - late_row :, :] = jnp.zeros((W - width + late_row, W), BF16)
        heads_copy(grad_out, 2).start()

    matmul_to(rows.at[1], p_far, wc.at[1, 1], False)
    forward_stats(1, lambda: by_units(grad_out, f_far, lambda: wait_heads(grad_out, 2)))
    forward_scan(1, False)
    backward_scan(1, f_far)
    backward_stats(1, lambda: transpose(p_own, 1))
    sends = grad_rows(1, 20)

    def arrived(layer, sends):
        for made in sends:
            made.wait()
        sums_start(layer)

    weight_grads(1, 2, lambda: arrived(1, sends))
    wait_w(1, w_plan(1), slot_of[1], 2)
    done_w(1, w_plan(1), slot_of[1])

    def keep_down(r, c, y):
        p_own[r, c] = y.astype(BF16)

    source_grad(keep_down, wc.at[1, 0], wr1, 2, lambda: order.work(3.0))
    sums_middle(1)
    backward_scan(0, p_own, lambda: order.work(1.2))
    sums_end(1)
    backward_stats(0, lambda: transpose(f_own, 0), lambda: order.work(3.0))
    sends = grad_rows(0, 22)
    order.work(2.0)
    weight_grads(0, 1, lambda: arrived(0, sends))
    sums_middle(0)
    wait_w(0, late_plan, slot_of[2], 0)
    wait_w(0, late_plan, slot_of[2], 1)
    done_w(0, late_plan, slot_of[2])

    def keep_source(r, c, y):
        rows[0, r, c] = y

    fetch(grad_out, 0).start()
    fetch(grad_out, 1).start()
    source_grad(keep_source, wc.at[0, 0], wc.at[0, 1], 1, lambda: order.work(3.0))
    sums_end(0)

    def give(c):
        piece = gf.at[c * chunk // steps, pl.ds(c * chunk % steps, chunk)]
        return pltpu.make_async_copy(stage_in.at[c % 2], piece, stage_sem.at[c % 2])

    for c in range(chunks):
        fetch(grad_out, c).wait()

        def finish_frames(i, _, c=c):
            straight = stage_in[c % 2, pl.ds(2 * i, 2)].astype(F32).reshape(2 * seqs, half)
            y = rows[0, pl.ds(aligned((c * chunk + 2 * i) * seqs, 8), 2 * seqs), :]
            y = jnp.where(section == 0, y[:, :half], y[:, late_shift : late_shift + half])
            stage_in[c % 2, pl.ds(2 * i, 2)] = (y + straight).reshape(2, seqs, half).astype(BF16)
            return 0

        lax.fori_loop(0, chunk // 2, finish_frames, 0)
        order.work(0.5)
        give(c).start()
        if c >= 1:
            give(c - 1).wait()
            if c + 1 < chunks:
                fetch(grad_out, c + 1).start()
    give(chunks - 1).wait()
    order.drain()

    for layer in range(2):

        @pl.when(section == layer)
        def _(layer=layer):
            pltpu.make_async_copy(tot.at[layer], v.at[section], v_sems.at[0]).wait()
            pltpu.make_async_remote_copy(
                src_ref=tot.at[layer], dst_ref=v.at[other], send_sem=v_sems.at[1], recv_sem=v_sems.at[2],
                device_id=sibling, device_id_type=MESH,
            ).wait_recv()

        @pl.when(section != layer)
        def _(layer=layer):
            v_across(layer).wait_send()

    own_part, far_part = v[section], v[other]
    first = jnp.where(section == 0, own_part, far_part)
    second = jnp.where(section == 0, far_part, own_part)
    for out, terms in ((out_gains, (2, 3)), (out_shifts, (0, 1)), (out_recurs, (4,))):
        out[0:1, 0:W] = sum(first[k : k + 1, :] for k in terms[1:]) + first[terms[0] : terms[0] + 1, :]
        out[0:1, W:width] = (
            sum(second[k : k + 1, :rest] for k in terms[1:]) + second[terms[0] : terms[0] + 1, :rest]
        )
    squares = jnp.sum(first[5:7, :] + second[5:7, :], axis=1, keepdims=True)
    root = jnp.sqrt(squares / (first[7:8, 0:1] * width))
    out_table[...] = jnp.concatenate([root[0:1], root[1:2]], axis=1)


def whole_step(dims, frames, grad_out, weights, tail, gains, shifts, recurs, lengths, masks):
    nz, ny, nx = dims
    micro, steps, seqs, half = frames.shape
    width = 2 * half
    views = seqs // lengths.shape[1]
    rows = micro * steps * seqs
    np_ = ny * nx
    wide_rows = (rows + 16 + 127) // 128 * 128
    depth = (nx * ny * nz - 1).bit_length()
    any_ = pl.BlockSpec(memory_space=pl.ANY)
    held = pl.BlockSpec(memory_space=pltpu.VMEM)
    dma = pltpu.SemaphoreType.DMA
    return pl.pallas_call(
        functools.partial(kernel, dims, steps, seqs, views),
        out_shape=(
            jax.ShapeDtypeStruct((2, W, 2 * W), BF16),
            jax.ShapeDtypeStruct(frames.shape, BF16),
            jax.ShapeDtypeStruct((1, width), F32),
            jax.ShapeDtypeStruct((1, width), F32),
            jax.ShapeDtypeStruct((1, width), F32),
            jax.ShapeDtypeStruct((1, 2), F32),
        ),
        in_specs=[any_] * 4 + [held] * 5,
        out_specs=(any_, any_, held, held, held, held),
        scratch_shapes=[
            pltpu.VMEM((wide_rows, W), BF16),
            pltpu.VMEM((rows, W), BF16),
            pltpu.VMEM((wide_rows, W), BF16),
            pltpu.VMEM((rows, W), BF16),
            pltpu.VMEM((3, wide_rows, W), BF16),
            pltpu.VMEM((2, 2, W, W), BF16),
            pltpu.VMEM((W, W), BF16),
            pltpu.VMEM((W, wide_rows), BF16),
            pltpu.VMEM((rows, 128), F32),
            pltpu.VMEM((128, 128), F32),
            pltpu.VMEM((2, steps // 4, seqs, half), BF16),
            pltpu.VMEM((micro, steps, seqs, 128), BF16),
            pltpu.VMEM((2, 8, W), F32),
            pltpu.VMEM((2, 8, 2 * W), F32),
            pltpu.VMEM((2, rows, W), F32),
            pltpu.VMEM((2, rows, W), F32),
            pltpu.VMEM((2, 8, W), F32),
            pltpu.VMEM((2, 8, W), F32),
            pltpu.VMEM((2, 8, W), F32),
            pltpu.VMEM((2, W, 128), BF16),
            pltpu.VMEM((2, np_, 8, W), F32),
            pltpu.VMEM((2, nz, 8, W), F32),
            pltpu.VMEM((2, 4, W, HALF), BF16),
            dma((3, 24)),
            dma((3,)),
            dma((2,)),
            dma((6, max(np_, 2))),
            dma((6, max(np_, 2))),
            dma((6, max(nz, 2))),
            dma((6, max(nz, 2))),
            dma((2, 4, 2, 2 * depth + 2)),
            dma((2, 4, 2, 2 * depth + 2)),
            dma((2, 4, 2, 2)),
        ],
        compiler_params=pltpu.CompilerParams(
            collective_id=0, has_side_effects=True, vmem_limit_bytes=64 * 1024 * 1024
        ),
    )(frames, grad_out, weights, tail, gains, shifts, recurs, lengths, masks)


def shards(dims, frames, grad_out, weights, gains, shifts, recurs, lengths, masks):
    width = 2 * frames.shape[3]
    last = W + (width - W) // 128 * 128
    tail = jnp.pad(weights[0, :, last:], ((0, 0), (0, 128 - (width - last))))
    o, grad_frames, grad_gains, grad_shifts, grad_recurs, table = whole_step(
        dims, frames, grad_out, weights, tail, gains, shifts, recurs, lengths, masks
    )
    grad_weight = o.reshape(2 * W, 2 * W)[:width, :width].astype(F32)
    return grad_frames, grad_weight[None], grad_gains, grad_shifts, grad_recurs, table


def solution(mesh):
    in_specs = (
        P(None, None, "batch", "section"),
        P(None, None, "batch", "section"),
        P("section", None, None),
        P("section", None),
        P("section", None),
        P("section", None),
        P(None, "batch"),
        P(None, None, "batch"),
    )
    out_specs = (
        P(None, None, "batch", "section"),
        P("section", None, None),
        P("section", None),
        P("section", None),
        P("section", None),
        P("section", None),
    )
    body = functools.partial(shards, grid_of(mesh.shape["batch"]))
    return jax.shard_map(body, mesh=mesh, in_specs=in_specs, out_specs=out_specs, check_vma=False)
```

```python
import functools

import jax
import jax.numpy as jnp
from jax import lax
from jax.experimental import pallas as pl
from jax.experimental.pallas import tpu as pltpu
from jax.sharding import PartitionSpec as P

EPS = 1e-05
W = 1024
HALF = W // 2
QUART = W // 4
MESH = pl.DeviceIdType.MESH
F32 = jnp.float32
BF16 = jnp.bfloat16


def grid_of(size):
    if size == 16:
        return (4, 2, 2)
    if size == 128:
        return (8, 4, 4)
    return (size, 1, 1)


def aligned(x, k):
    return pl.multiple_of(x, k)


def wide(x, reps):
    return jnp.concatenate([x] * reps, axis=1)


def fold(x):
    rows = x.shape[0]
    total = x[0:8]
    for k in range(8, rows, 8):
        total = total + x[k : k + 8]
    return total


def dot(a, b, dims):
    return lax.dot_general(a, b, (dims, ((), ())), preferred_element_type=F32)


class Reduction:
    def __init__(self, env, layer, index, block, orders, lane_of):
        self.env, self.layer, self.index, self.block, self.orders = env, layer, index, block, orders
        self.lane_of = lane_of
        self.space = env["space"].at[layer, index]
        self.depth = len(orders[0])
        self.regions = [self.halves(i, order) for i, order in enumerate(orders)]
        self.step = 0
        self.waits = []
        depth = self.depth
        self.steps = [functools.partial(self.scatter, 0)]
        self.steps += [functools.partial(self.scatter, k) for k in range(1, depth)]
        self.steps += [functools.partial(self.gather, k) for k in range(depth - 1, 0, -1)]
        self.steps += [self.give, self.finish]

    def halves(self, i, order):
        row, rows, lane, lanes = 0, W, i * QUART, QUART
        out = [(row, rows, lane, lanes)]
        for axis in order:
            if rows > 16:
                rows //= 2
                row = row + axis["bit"] * rows
            else:
                lanes //= 2
                lane = lane + axis["bit"] * lanes
            out.append((row, rows, lane, lanes))
        return out

    @property
    def free_to_go(self):
        return self.step != self.depth or self.layer in self.env["summed"]

    @property
    def done(self):
        return self.step >= len(self.steps)

    def advance(self):
        self.sent = []
        self.steps[self.step]()
        self.step += 1
        return self.sent

    def remote(self, i, src, dst, slot, where, recv=None):
        sems = (self.layer, self.index, i, slot)
        return pltpu.make_async_remote_copy(
            src_ref=src, dst_ref=dst, send_sem=self.env["ar_send"].at[sems],
            recv_sem=self.env["ar_recv"].at[sems] if recv is None else recv, device_id=where, device_id_type=MESH,
        )

    def wait(self):
        for made, came in self.waits:
            made.wait_send()
            came.wait_recv()
        self.waits = []

    def came_at(self, i, k):
        row = sum(r[1] for r in self.regions[i][1 : k + 1])
        _, rows, _, lanes = self.regions[i][k + 1]
        return row, rows, i * QUART, lanes

    def scatter(self, k):
        if k > 0:
            self.wait()
            self.add(k - 1)
        for i, order in enumerate(self.orders):
            self.scatter_part(i, k, order[k])

    def start_part(self, i):
        self.sent = []
        self.scatter_part(i, 0, self.orders[i][0])
        if i == 1:
            self.step = 1
        return self.sent

    def scatter_part(self, i, k, axis):
        row, rows, lane, lanes = self.regions[i][k]
        _, rows2, _, lanes2 = self.regions[i][k + 1]
        give_row = row + (1 - axis["bit"]) * rows2 if rows2 < rows else row
        give_lane = lane if rows2 < rows else lane + (1 - axis["bit"]) * lanes2
        src = self.block.at[pl.ds(aligned(give_row, 16), rows2), pl.ds(aligned(give_lane, 128), lanes2)]
        at, n, at_lane, n_lanes = self.came_at(i, k)
        dst = self.space.at[pl.ds(at, n), pl.ds(at_lane, n_lanes)]
        made = self.remote(i, src, dst, k, axis["partner"])
        made.start()
        self.waits.append((made, made))
        self.sent.append((axis["link"], rows2 * lanes2 * 2))

    def add(self, k, last=False):
        rows = self.regions[0][k + 1][1]
        size = min(rows, 32)
        out = []
        for i in range(2):
            row, _, lane, lanes = self.regions[i][k + 1]
            at, _, at_lane, _ = self.came_at(i, k)
            lane = aligned(lane, 128)
            extra = None
            if last:
                part = self.index // 2
                first = aligned((self.index % 2) * HALF + lane, 128)
                extra = self.env["vtot"][self.layer, part : part + 1, pl.ds(first, lanes)]
            out.append((row, lane, lanes, at, at_lane, self.local(i, k + 1)[0], extra))

        def body(j, _):
            for row, lane, lanes, at, at_lane, home, extra in out:
                here = pl.ds(aligned(row + j * size, 16), size)
                total = self.block[here, pl.ds(lane, lanes)].astype(F32)
                total = total + self.space[pl.ds(aligned(at + j * size, 16), size), pl.ds(at_lane, lanes)].astype(F32)
                if last:
                    column = self.env["column"][self.layer, here, :].astype(F32)
                    total = total + wide(column, lanes // 128) * extra
                    to = pl.ds(aligned(home + j * size, 16), size)
                    self.space[to, pl.ds(lane, lanes)] = total.astype(BF16)
                else:
                    self.block[here, pl.ds(lane, lanes)] = total.astype(BF16)
            return 0

        lax.fori_loop(0, rows // size, body, 0)

    def local(self, i, k):
        row, rows, lane, lanes = self.regions[i][k]
        return row - self.regions[i][1][0], rows, lane, lanes

    def gather(self, k):
        self.wait()
        if k == self.depth - 1:
            self.add(k, last=True)
        for i, order in enumerate(self.orders):
            axis = order[k]
            row, rows, lane, lanes = self.local(i, k + 1)
            row0, rows0, lane0, lanes0 = self.local(i, k)
            if rows0 > rows:
                far = (row0 + (1 - axis["bit"]) * rows, rows, lane, lanes)
            else:
                far = (row, rows, lane0 + (1 - axis["bit"]) * lanes, lanes)
            refs = [
                self.space.at[pl.ds(aligned(r, 16), n), pl.ds(aligned(c, 128), w)]
                for r, n, c, w in ((row, rows, lane, lanes), far)
            ]
            made = self.remote(i, refs[0], refs[0], self.depth + k, axis["partner"])
            made.start()
            self.waits.append((made, self.remote(i, refs[1], refs[1], self.depth + k, axis["partner"])))
            self.sent.append((axis["link"], rows * lanes * 2))

    def result(self, i, bit, section):
        rows = self.regions[i][1][1]
        lane = aligned(self.lane_of(section) + i * QUART, QUART)
        return self.env["o"].at[section, pl.ds(aligned(bit * rows, 16), rows), pl.ds(lane, QUART)]

    def gathered(self, i):
        return self.space.at[pl.ds(0, self.regions[i][1][1]), pl.ds(i * QUART, QUART)]

    def deliver(self, i, near, straight):
        axis, section = self.orders[i][0], self.env["section"]
        slot = 2 * self.depth + (0 if near else 1)
        recv = None if straight else self.env["ar_other"].at[self.layer, self.index, i, 0 if near else 1]
        where = dict(self.env["here"] if near else axis["partner"], section=self.layer)
        return self.remote(i, self.gathered(i), self.result(i, axis["bit"], section), slot, where, recv)

    def arrival(self, i, near, straight):
        axis, section = self.orders[i][0], self.env["section"]
        slot = 2 * self.depth + (0 if near else 1)
        recv = None if straight else self.env["ar_other"].at[self.layer, self.index, i, 0 if near else 1]
        bit = axis["bit"] if near else 1 - axis["bit"]
        frm = section if straight else 1 - section
        where = dict(self.env["here"] if near else axis["partner"], section=frm)
        return self.remote(i, self.gathered(i), self.result(i, bit, frm), slot, where, recv)

    def kept(self, i):
        sem = self.env["ar_recv"].at[self.layer, self.index, i, 2 * self.depth]
        return pltpu.make_async_copy(
            self.gathered(i), self.result(i, self.orders[i][0]["bit"], self.env["section"]), sem
        )

    def give(self):
        self.wait()

        @pl.when(self.env["section"] == self.layer)
        def _():
            for i in range(2):
                self.deliver(i, False, True).start()
                self.kept(i).start()

        @pl.when(self.env["section"] != self.layer)
        def _():
            for i in range(2):
                self.deliver(i, False, False).start()
                self.deliver(i, True, False).start()

        for i, order in enumerate(self.orders):
            self.sent.append((order[0]["link"], self.regions[i][1][1] * QUART * 2))

    def finish(self):
        @pl.when(self.env["section"] == self.layer)
        def _():
            for i in range(2):
                self.kept(i).wait()
                self.deliver(i, False, True).wait_send()
                self.arrival(i, False, True).wait_recv()
                self.arrival(i, True, False).wait_recv()
                self.arrival(i, False, False).wait_recv()

        @pl.when(self.env["section"] != self.layer)
        def _():
            for i in range(2):
                self.deliver(i, False, False).wait_send()
                self.deliver(i, True, False).wait_send()


class Order:
    RATE, HOP = 50e3, 1.8

    def __init__(self):
        self.now = 0.0
        self.free = {}
        self.going = []

    def sent(self, copies):
        end = self.now
        for link, size in copies:
            self.free[link] = max(self.now, self.free.get(link, 0.0)) + size / self.RATE
            end = max(end, self.free[link])
        return end + self.HOP

    def begin(self, one, i):
        end = self.sent(one.start_part(i))
        if i == 0:
            one.due = end
        else:
            one.due = max(one.due, end)
            self.going.append(one)

    def advance(self, one):
        self.now = max(self.now, one.due) + 0.4
        one.due = self.sent(one.advance())
        if one.done:
            self.going.remove(one)

    def work(self, cost):
        self.now += cost
        while True:
            due = [x for x in self.going if x.due <= self.now and x.free_to_go]
            if not due:
                return
            self.advance(min(due, key=lambda x: x.due))

    def drain(self):
        while self.going:
            self.advance(min(self.going, key=lambda x: x.due))


def kernel(dims, steps, seqs, views, frames, grad_out, weights, tail, gains, shifts, recurs, lengths, masks, o, gf,
           out_gains, out_shifts, out_recurs, out_table, f_own, f_far, p_own, p_far, g3, wc, wr1, src_t, live, turn,
           stage_in, heads, v, vecs, rows, hid, coef, tot, vtot, column, st_plane, st_z, space, sems, v_sems, stage_sem, pl_send, pl_recv, z_send, z_recv,
           ar_send, ar_recv, ar_other):
    nz, ny, nx = dims
    np_ = ny * nx
    span = steps * seqs
    total_rows = 2 * span
    sent_rows = total_rows + 16
    pairs = steps // 2
    section = lax.axis_index("section")
    other = 1 - section
    b = lax.axis_index("batch")
    mx = lax.rem(b, nx)
    my = lax.rem(b // nx, ny)
    mz = b // np_
    mp = lax.rem(b, np_)

    def at_x(i):
        return {"batch": b - mx + i}

    def at_y(i):
        return {"batch": b + (i - my) * nx}

    def at_z(i):
        return {"batch": b + (i - mz) * np_}

    def at_plane(i):
        return {"batch": b - mp + i}

    bits = []
    for link, count, stride in (("x", nx, 1), ("y", ny, nx), ("z", nz, np_)):
        while count > 1:
            bit = lax.rem(b // stride, 2)
            bits.append(dict(bit=bit, partner={"batch": b + (1 - 2 * bit) * stride}, link=link))
            count //= 2
            stride *= 2
    sibling = {"section": other}

    def local(src, dst, slot):
        return pltpu.make_async_copy(src, dst, sems.at[0, slot])

    def across(src, dst, slot):
        return pltpu.make_async_remote_copy(
            src_ref=src, dst_ref=dst, send_sem=sems.at[1, slot], recv_sem=sems.at[2, slot],
            device_id=sibling, device_id_type=MESH,
        )

    half = frames.shape[3]
    width = 2 * half
    lead = W - half
    rest = width - W
    full = rest // 128 * 128
    chunk = stage_in.shape[1]
    chunks = 2 * steps // chunk

    def fetch(source, c):
        piece = source.at[c * chunk // steps, pl.ds(c * chunk % steps, chunk)]
        return pltpu.make_async_copy(piece, stage_in.at[c % 2], stage_sem.at[c % 2])

    def by_units(source, target, ready):
        for c in range(chunks):
            fetch(source, c).wait()
            if c == 0:
                ready()

            def place(i, _, c=c):
                x = stage_in[c % 2, pl.ds(2 * i, 2)].astype(F32).reshape(2 * seqs, half)
                to = pl.ds(aligned((c * chunk + 2 * i) * seqs, 16), 2 * seqs)

                @pl.when(section == 0)
                def _():
                    t = c * chunk % steps + 2 * i
                    head = heads[c * chunk // steps, pl.ds(t, 2)].astype(F32).reshape(2 * seqs, 128)
                    target[to, :] = jnp.concatenate([x, head[:, :lead]], axis=1).astype(BF16)

                @pl.when(section == 1)
                def _():
                    pad = jnp.zeros((2 * seqs, 2 * lead), F32)
                    target[to, :] = jnp.concatenate([x[:, lead:], pad], axis=1).astype(BF16)

                return 0

            lax.fori_loop(0, chunk // 2, place, 0)
            if c + 2 < chunks:
                fetch(source, c + 2).start()

    def pieces(row, count, u, block):
        r = pl.ds(row, count)
        to = pl.ds(0, count)
        if u == 0:
            return [(weights.at[0, r, pl.ds(0, W)], block.at[to, :])]
        return [
            (weights.at[0, r, pl.ds(W, full)], block.at[to, pl.ds(0, full)]),
            (tail.at[r, :], block.at[to, pl.ds(full, 128)]),
        ]

    rows_of = {0: (0, W), 1: (W, rest)}

    def w_plan(layer):
        mine, far = rows_of[layer], rows_of[1 - layer]
        plan = [
            (mine, layer, far, 1 - layer, wc.at[layer, 0]),
            (far, layer, mine, 1 - layer, wc.at[layer, 1]),
        ]
        if layer == 1:
            plan.append((mine, 0, far, 1, wr1))
        return plan

    late_row = (width - half) // 16 * 16
    late_shift = half - late_row
    late_plan = [
        ((0, W), 0, (late_row, width - late_row), 1, wc.at[0, 0]),
        ((0, W), 1, (late_row, width - late_row), 0, wc.at[0, 1]),
    ]
    slot_of = {0: 4, 1: 8, 2: 14}

    def local_w(plan, base, which):
        r, u, _, _, block = plan[which]
        return [local(a, t, base + 2 * which + i) for i, (a, t) in enumerate(pieces(*r, u, block))]

    def across_w(plan, base, which):
        _, _, r, u, block = plan[which]
        return [across(a, t, base + 2 * which + i) for i, (a, t) in enumerate(pieces(*r, u, block))]

    def start_local_w(layer, plan, base):
        @pl.when(section == layer)
        def _():
            for which in range(len(plan)):
                for made in local_w(plan, base, which):
                    made.start()

    def start_across_w(layer, plan, base):
        @pl.when(section == layer)
        def _():
            for which in range(len(plan)):
                for made in across_w(plan, base, which):
                    made.start()

    fetch(frames, 0).start()
    fetch(frames, 1).start()
    for layer in range(2):
        start_local_w(layer, w_plan(layer), slot_of[layer])

    barrier = pltpu.get_barrier_semaphore()
    greeted = [dict(sibling)]
    greeted += [at_plane(lax.rem(mp + k, np_)) for k in range(1, np_)]
    greeted += [at_z(lax.rem(mz + k, nz)) for k in range(1, nz)]
    greeted += [dict(axis["partner"], section=other) for axis in bits]
    for where in greeted:
        pl.semaphore_signal(barrier, inc=1, device_id=where, device_id_type=MESH)
    pl.semaphore_wait(barrier, len(greeted))

    def heads_copy(source, slot):
        return across(source.at[:, :, :, pl.ds(0, 128)], heads, slot)

    @pl.when(section == 1)
    def _():
        heads_copy(frames, 1).start()

    for layer in range(2):
        start_across_w(layer, w_plan(layer), slot_of[layer])

    def wait_w(layer, plan, base, which):
        @pl.when(section == layer)
        def _():
            for made in local_w(plan, base, which):
                made.wait()

        @pl.when(section != layer)
        def _():
            for made in across_w(plan, base, which):
                made.wait_recv()

    def done_w(layer, plan, base):
        @pl.when(section == layer)
        def _():
            for which in range(len(plan)):
                for made in across_w(plan, base, which):
                    made.wait_send()

    def wait_heads(source, slot):
        @pl.when(section == 0)
        def _():
            heads_copy(source, slot).wait_recv()

        @pl.when(section == 1)
        def _():
            heads_copy(source, slot).wait_send()

    for k, (x, fill) in enumerate(((gains, 0.0), (shifts, -1e30), (recurs, 0.0))):
        vecs[section, k : k + 1, 0:width] = x[...]
        vecs[section, k : k + 1, width:] = jnp.full((1, 2 * W - width), fill, F32)
    vecs[section, 3:8, :] = jnp.zeros((5, 2 * W), F32)
    send_vec = across(vecs.at[section], vecs.at[section], 3)
    send_vec.start()

    gap = jnp.zeros((W - rest, W), BF16)

    @pl.when(section == 0)
    def _():
        wc[0, 1, rest:, :] = gap
        wc[1, 1, rest:, :] = gap

    @pl.when(section == 1)
    def _():
        wc[0, 0, rest:, :] = gap
        wc[1, 0, rest:, :] = gap
        wr1[rest:, :] = gap

    for m in range(2):
        turn[...] = jnp.zeros_like(turn)
        turn[0:steps, 0:seqs] = masks[m].astype(F32)
        mask = turn[...].T[0:seqs]
        groups = lengths.shape[1]
        s_at = lax.broadcasted_iota(jnp.int32, (seqs, groups), 0)
        g_at = lax.broadcasted_iota(jnp.int32, (seqs, groups), 1) * views
        there = (s_at >= g_at) & (s_at < g_at + views)
        length = jnp.broadcast_to(lengths[m : m + 1, :], (seqs, groups)).astype(F32)
        limit = jnp.sum(jnp.where(there, length, 0.0), axis=1, keepdims=True)
        position = lax.broadcasted_iota(jnp.int32, (seqs, 128), 1)
        alive = (position.astype(F32) < limit) & ((mask > 0.0) | (position == 0))
        alive = alive.astype(F32)
        for t in range(steps):
            at = m * span + t * seqs
            live[at : at + seqs, :] = jnp.broadcast_to(alive[:, t : t + 1], (seqs, 128))

    def matmul_to(out, a, w, first):
        def body(i, _):
            r = pl.ds(aligned((i // 2) * span, 16), span)
            c = pl.ds(aligned((i % 2) * HALF, HALF), HALF)
            y = dot(a[r, :], w[:, c], ((1,), (0,)))
            out[r, c] = y if first else out[r, c] + y
            return 0

        lax.fori_loop(0, 4, body, 0)

    def vec_of(layer, k):
        return vecs[layer, k : k + 1, pl.ds(aligned(section * W, W), W)]

    def stage_copy(where, rnd, slot, k, back):
        buf, size, me, at, send, recv = where
        there = at(lax.rem(me + (size - k if back else k), size))
        ref = buf.at[rnd % 2, slot]
        return pltpu.make_async_remote_copy(
            src_ref=ref, dst_ref=ref, send_sem=send.at[rnd, k], recv_sem=recv.at[rnd, k],
            device_id=there, device_id_type=MESH,
        )

    in_plane = (st_plane, np_, mp, at_plane, pl_send, pl_recv)
    in_line = (st_z, nz, mz, at_z, z_send, z_recv)

    def stage_start(where, rnd, value):
        buf, size, me = where[:3]
        buf[rnd % 2, me] = value
        for k in range(1, size):
            stage_copy(where, rnd, me, k, False).start()

    def stage_wait(where, rnd):
        size, me = where[1:3]
        for k in range(1, size):
            stage_copy(where, rnd, me, k, False).wait_send()
            stage_copy(where, rnd, lax.rem(me + size - k, size), k, True).wait_recv()

    def add_slots(where, rnd):
        buf, size, idx = where[0], where[1], rnd % 2
        total = buf[idx, 0]
        for k in range(1, size):
            total = total + buf[idx, k]
        return total

    def merge_slots(where, rnd):
        buf, size, idx = where[0], where[1], rnd % 2
        out = []
        for m in range(2):
            s = [buf[idx, k, 3 * m : 3 * m + 1, :] for k in range(size)]
            q = [buf[idx, k, 3 * m + 1 : 3 * m + 2, :] for k in range(size)]
            n = [buf[idx, k, 3 * m + 2 : 3 * m + 3, :] for k in range(size)]
            total, squares, count = sum(s[1:], s[0]), sum(q[1:], q[0]), sum(n[1:], n[0])
            mean = total / count
            for k in range(size):
                d = s[k] / n[k] - mean
                squares = squares + n[k] * d * d
            out += [total, squares, count]
        both = [buf[idx, k, 6:8, :] for k in range(size)]
        return jnp.concatenate(out + [sum(both[1:], both[0])], axis=0)

    def forward_stats(layer, between=None):
        out = []
        source = f_own if layer == 0 else p_own
        level = jnp.zeros((8, W), F32)
        for m in range(2):

            def sums(i, carry):
                acc, cnt, lev = carry
                r = pl.ds(aligned(m * span + i * (2 * seqs), 16), 2 * seqs)
                lv = live[r, :]
                keep = wide(lv, 8)
                acc = acc + fold(keep * rows[layer, r, :])
                return acc, cnt + fold(lv), lev + fold(keep * source[r, :].astype(F32))

            acc, cnt, level = lax.fori_loop(
                0, pairs, sums, (jnp.zeros((8, W), F32), jnp.zeros((8, 128), F32), level)
            )
            total = jnp.sum(acc, axis=0, keepdims=True)
            count = wide(jnp.sum(cnt, axis=0, keepdims=True), 8)
            mean = total / count

            def squares(i, acc):
                r = pl.ds(aligned(m * span + i * (2 * seqs), 16), 2 * seqs)
                d = rows[layer, r, :] - mean
                return acc + fold(wide(live[r, :], 8) * (d * d))

            sq = lax.fori_loop(0, pairs, squares, jnp.zeros((8, W), F32))
            out += [total, jnp.sum(sq, axis=0, keepdims=True), count]
        level = jnp.sum(level, axis=0, keepdims=True)
        value = jnp.concatenate(out + [level, jnp.zeros_like(level)], axis=0)
        stage_start(in_plane, layer, value)
        if between is not None:
            between()
        stage_wait(in_plane, layer)
        stage_start(in_line, layer, merge_slots(in_plane, layer))
        stage_wait(in_line, layer)
        value = merge_slots(in_line, layer)
        for m in range(2):
            count = value[3 * m + 2 : 3 * m + 3]
            mean = value[3 * m : 3 * m + 1] / count
            spread = value[3 * m + 1 : 3 * m + 2] / count
            coef[layer, 3 * m : 3 * m + 1, :] = mean
            coef[layer, 3 * m + 1 : 3 * m + 2, :] = lax.rsqrt(spread + EPS)
            coef[layer, 3 * m + 2 : 3 * m + 3, :] = count
        level = value[6:7] / (value[2:3] + value[5:6])
        top = lax.broadcasted_iota(jnp.int32, (16, W), 0) == 0
        source[total_rows:sent_rows, :] = jnp.where(top, level, 0.0).astype(BF16)

    def forward_scan(layer, keep_passed):
        gain, shift, recur = vec_of(layer, 0), vec_of(layer, 1), vec_of(layer, 2)
        sends = []
        for lh in range(2):
            lanes = slice(lh * HALF, (lh + 1) * HALF)
            a, c = [], []
            for m in range(2):
                mean = coef[layer, 3 * m : 3 * m + 1, lanes]
                scale = coef[layer, 3 * m + 1 : 3 * m + 2, lanes]
                a.append(gain[:, lanes] * scale)
                c.append((shift[:, lanes], mean))
            rec = recur[:, lanes]

            def body(i, carry):
                out = []
                for m in range(2):
                    r = pl.ds(aligned(m * span + i * (2 * seqs), 16), 2 * seqs)
                    x = (rows[layer, r, lanes] - c[m][1]) * a[m] + c[m][0]
                    alive = wide(live[r, :], 4) > 0.0
                    h = carry[m]
                    both = []
                    for k in range(2):
                        part = slice(k * seqs, (k + 1) * seqs)
                        z = x[part] + rec * h
                        soft = jnp.maximum(z, 0.0) + jnp.log(1.0 + jnp.exp(-jnp.abs(z)))
                        h = jnp.where(alive[part], soft, h)
                        both.append(h)
                    two = jnp.concatenate(both, axis=0)
                    hid[layer, r, lanes] = two
                    if keep_passed:
                        p_own[r, lanes] = two.astype(BF16)
                    out.append(h)
                return tuple(out)

            zero = jnp.zeros((seqs, HALF), F32)
            lax.fori_loop(0, pairs, body, (zero, zero))
            if keep_passed:
                made = across(p_own.at[pl.ds(0, total_rows), lanes], p_far.at[:, lanes], 18 + lh)
                made.start()
                sends.append(made)
        return sends

    def backward_scan(layer, above, between=lambda: None):
        gain, shift, recur = vec_of(layer, 0), vec_of(layer, 1), vec_of(layer, 2)
        for lq in range(4):
            lanes = slice(lq * QUART, (lq + 1) * QUART)
            gq, sq, rec = gain[:, lanes], shift[:, lanes], recur[:, lanes]
            mean = [coef[layer, 3 * m : 3 * m + 1, lanes] for m in range(2)]
            scale = [coef[layer, 3 * m + 1 : 3 * m + 2, lanes] for m in range(2)]

            def body(i, carry):
                down, s1, s2, rsum, sqh, sqa = carry
                down, s1, s2 = list(down), list(s1), list(s2)
                i = pairs - 1 - i
                for m in range(2):
                    start = m * span + i * (2 * seqs)
                    r = pl.ds(aligned(start, 16), 2 * seqs)
                    before = pl.ds(aligned(jnp.maximum(start - seqs, 0), 8), seqs)
                    normed = (rows[layer, r, lanes] - mean[m]) * scale[m]
                    drive = gq * normed + sq
                    h2 = hid[layer, r, lanes]
                    hb = jnp.where(i > 0, hid[layer, before, lanes], 0.0)
                    lv = wide(live[r, :], 2)
                    up = above[r, lanes].astype(F32)
                    res = f_own[r, lanes].astype(F32)
                    aux = res + h2 if layer == 1 else res
                    sqh = sqh + fold(lv * (h2 * h2))
                    sqa = sqa + fold(lv * (aux * aux))
                    grads = [None, None]
                    for k in (1, 0):
                        part = slice(k * seqs, (k + 1) * seqs)
                        prior = h2[0:seqs] if k == 1 else hb
                        slope = 0.5 + 0.5 * jnp.tanh(0.5 * (drive[part] + rec * prior))
                        total = up[part] + down[m]
                        gd = lv[part] * slope * total
                        down[m] = (1.0 - lv[part]) * total + rec * gd
                        grads[k] = gd
                        rsum = rsum + fold(gd * prior)
                    gd2 = jnp.concatenate(grads, axis=0)
                    hid[layer, r, lanes] = gd2
                    s1[m] = s1[m] + fold(gd2)
                    s2[m] = s2[m] + fold(gd2 * normed)
                return tuple(down), tuple(s1), tuple(s2), rsum, sqh, sqa

            zero = jnp.zeros((seqs, QUART), F32)
            z8 = jnp.zeros((8, QUART), F32)
            _, s1, s2, rsum, sqh, sqa = lax.fori_loop(
                0, pairs, body, ((zero, zero), (z8, z8), (z8, z8), z8, z8, z8)
            )
            for k, x in enumerate((s1[0], s1[1], s2[0], s2[1], rsum, sqh, sqa)):
                tot[layer, k : k + 1, lanes] = jnp.sum(x, axis=0, keepdims=True)
            between()
        tot[layer, 7:8, :] = jnp.zeros((1, W), F32)

    def backward_stats(layer, between, after=lambda: None):
        rnd = 2 if layer == 1 else 4
        stage_start(in_plane, rnd, tot[layer])
        between()
        after()
        stage_wait(in_plane, rnd)
        stage_start(in_line, rnd, add_slots(in_plane, rnd))
        after()
        stage_wait(in_line, rnd)
        tot[layer] = add_slots(in_line, rnd)
        tot[layer, 7:8, :] = coef[layer, 2:3, :] + coef[layer, 5:6, :]

        @pl.when(section == layer)
        def _():
            pltpu.make_async_copy(tot.at[layer], v.at[section], v_sems.at[0]).start()

        @pl.when(section != layer)
        def _():
            v_across(layer).start()

    def v_across(layer):
        return pltpu.make_async_remote_copy(
            src_ref=tot.at[layer], dst_ref=v.at[section], send_sem=v_sems.at[1], recv_sem=v_sems.at[2],
            device_id=sibling, device_id_type=MESH,
        )

    def grad_rows(layer, slot):
        gain = vec_of(layer, 0)
        sends = []
        for lh in range(2):
            lanes = slice(lh * HALF, (lh + 1) * HALF)
            acc = jnp.zeros((8, HALF), F32)
            for m in range(2):
                mean = coef[layer, 3 * m : 3 * m + 1, lanes]
                scale = coef[layer, 3 * m + 1 : 3 * m + 2, lanes]
                count = coef[layer, 3 * m + 2 : 3 * m + 3, lanes]
                first = tot[layer, m : m + 1, lanes] / count
                second = tot[layer, 2 + m : 3 + m, lanes] / count * scale
                k = scale * gain[:, lanes]

                def body(i, acc):
                    r = pl.ds(aligned(m * span + i * (2 * seqs), 16), 2 * seqs)
                    y = hid[layer, r, lanes] - first - (rows[layer, r, lanes] - mean) * second
                    y = wide(live[r, :], 4) * (k * y)
                    g3[0, r, lanes] = y.astype(BF16)
                    return acc + fold(y)

                acc = lax.fori_loop(0, pairs, body, acc)
            top = lax.broadcasted_iota(jnp.int32, (16, HALF), 0) == 0
            minus = jnp.where(top, -jnp.sum(acc, axis=0, keepdims=True), 0.0)
            g3[0, total_rows:sent_rows, lanes] = minus.astype(BF16)
            made = across(g3.at[0, pl.ds(0, sent_rows), lanes], g3.at[1 + layer, pl.ds(0, sent_rows), lanes], slot + lh)
            made.start()
            sends.append(made)
        return sends

    def sums_start(layer):
        own_sum = -g3[0, total_rows:sent_rows, :].astype(F32)[0:1]
        far_sum = -g3[1 + layer, total_rows:sent_rows, :].astype(F32)[0:1]
        value = jnp.concatenate([own_sum, far_sum, jnp.zeros((6, W), F32)], axis=0)
        stage_start(in_plane, 3 if layer == 1 else 5, value)

    def sums_middle(layer):
        rnd = 3 if layer == 1 else 5
        stage_wait(in_plane, rnd)
        stage_start(in_line, rnd, add_slots(in_plane, rnd))

    def sums_end(layer):
        rnd = 3 if layer == 1 else 5
        stage_wait(in_line, rnd)
        vtot[layer] = add_slots(in_line, rnd)
        env["summed"].add(layer)

    def transpose(src, layer):
        def body(j, _):
            c = pl.ds(aligned(j * 128, 128), 128)
            src_t[c, :] = src[:, c].T
            level = src[total_rows:sent_rows, c].astype(F32)[0:1]
            column[layer, c, :] = jnp.broadcast_to(level, (128, 128)).T.astype(BF16)
            return 0

        lax.fori_loop(0, W // 128, body, 0)

    def weight_part(block, grads, c):
        lanes = pl.ds(c * QUART, QUART)

        def body(j, _):
            r = pl.ds(aligned(j * HALF, HALF), HALF)
            block[r, lanes] = dot(src_t[r, :], grads[:, lanes], ((1,), (0,))).astype(BF16)
            return 0

        lax.fori_loop(0, W // HALF, body, 0)

    def source_grad(store, w_own, w_far, far, between):
        for m in range(2):
            r = pl.ds(m * span, span)

            def body(i, _):
                c = pl.ds(aligned(i * HALF, HALF), HALF)
                y = dot(g3[0, r, :], w_own[c, :], ((1,), (1,))) + dot(g3[far, r, :], w_far[c, :], ((1,), (1,)))
                store(r, c, y)
                return 0

            lax.fori_loop(0, 2, body, 0)
            between()

    env = dict(summed=set(), vtot=vtot, column=column, space=space, ar_send=ar_send, ar_recv=ar_recv, ar_other=ar_other, o=o,
               section=section, here={"batch": b})
    xs = [a for a in bits if a["link"] == "x"]
    ys = [a for a in bits if a["link"] == "y"]
    zs = [a for a in bits if a["link"] == "z"]
    flat = (xs + ys + zs, ys + xs + zs)
    blocks = {
        (1, 0): f_far.at[pl.ds(0, W), :],
        (1, 1): p_far.at[pl.ds(0, W), :],
        (0, 0): wc.at[1, 1],
        (0, 1): wr1,
    }
    parts = {}
    for layer in (1, 0):
        for index, orders in enumerate((flat, flat, flat, flat)):
            part, side = index // 2, index % 2

            def lane_of(sec, part=part, side=side):
                return (sec if part == 0 else 1 - sec) * W + side * HALF

            block = blocks[layer, part].at[:, pl.ds(side * HALF, HALF)]
            parts[layer, index] = Reduction(env, layer, index, block, orders, lane_of)
    order = Order()

    def weight_grads(layer, far, between):
        for part, grads in enumerate((g3.at[0], g3.at[far])):
            if part == 1:
                between()
            for c in range(4):
                weight_part(blocks[layer, part], grads, c)
                order.work(0.9)
                order.begin(parts[layer, 2 * part + c // 2], c % 2)

    for spare in (f_own, p_own, g3.at[0], g3.at[1], g3.at[2]):
        spare[sent_rows:, :] = jnp.zeros((spare.shape[0] - sent_rows, W), BF16)

    by_units(frames, f_own, lambda: wait_heads(frames, 1))
    send_f = across(f_own.at[pl.ds(0, total_rows), :], f_far, 0)
    send_f.start()
    wait_w(0, w_plan(0), slot_of[0], 0)
    matmul_to(rows.at[0], f_own, wc.at[0, 0], True)
    wait_w(0, w_plan(0), slot_of[0], 1)
    send_f.wait()
    matmul_to(rows.at[0], f_far, wc.at[0, 1], False)
    send_vec.wait_send()
    across(vecs.at[other], vecs.at[other], 3).wait_recv()
    fetch(grad_out, 0).start()
    fetch(grad_out, 1).start()
    forward_stats(0)
    sends = forward_scan(0, True)
    wait_w(1, w_plan(1), slot_of[1], 0)
    matmul_to(rows.at[1], p_own, wc.at[1, 0], True)
    wait_w(1, w_plan(1), slot_of[1], 1)
    for made in sends:
        made.wait()
    done_w(0, w_plan(0), slot_of[0])

    start_local_w(0, late_plan, slot_of[2])
    start_across_w(0, late_plan, slot_of[2])

    @pl.when(section == 1)
    def _():
        wc[0, 1, width - late_row :, :] = jnp.zeros((W - width + late_row, W), BF16)
        heads_copy(grad_out, 2).start()

    matmul_to(rows.at[1], p_far, wc.at[1, 1], False)
    forward_stats(1, lambda: by_units(grad_out, f_far, lambda: wait_heads(grad_out, 2)))
    forward_scan(1, False)
    backward_scan(1, f_far)
    backward_stats(1, lambda: transpose(p_own, 1))
    sends = grad_rows(1, 20)

    def arrived(layer, sends):
        for made in sends:
            made.wait()
        sums_start(layer)

    weight_grads(1, 2, lambda: arrived(1, sends))
    wait_w(1, w_plan(1), slot_of[1], 2)
    done_w(1, w_plan(1), slot_of[1])

    def keep_down(r, c, y):
        p_own[r, c] = y.astype(BF16)

    source_grad(keep_down, wc.at[1, 0], wr1, 2, lambda: order.work(3.0))
    sums_middle(1)
    backward_scan(0, p_own, lambda: order.work(1.2))
    sums_end(1)
    backward_stats(0, lambda: transpose(f_own, 0), lambda: order.work(3.0))
    sends = grad_rows(0, 22)
    order.work(2.0)
    weight_grads(0, 1, lambda: arrived(0, sends))
    sums_middle(0)
    wait_w(0, late_plan, slot_of[2], 0)
    wait_w(0, late_plan, slot_of[2], 1)
    done_w(0, late_plan, slot_of[2])

    def keep_source(r, c, y):
        rows[0, r, c] = y

    fetch(grad_out, 0).start()
    fetch(grad_out, 1).start()
    source_grad(keep_source, wc.at[0, 0], wc.at[0, 1], 1, lambda: order.work(3.0))
    sums_end(0)

    def give(c):
        piece = gf.at[c * chunk // steps, pl.ds(c * chunk % steps, chunk)]
        return pltpu.make_async_copy(stage_in.at[c % 2], piece, stage_sem.at[c % 2])

    for c in range(chunks):
        fetch(grad_out, c).wait()

        def finish_frames(i, _, c=c):
            straight = stage_in[c % 2, pl.ds(2 * i, 2)].astype(F32).reshape(2 * seqs, half)
            y = rows[0, pl.ds(aligned((c * chunk + 2 * i) * seqs, 8), 2 * seqs), :]
            y = jnp.where(section == 0, y[:, :half], y[:, late_shift : late_shift + half])
            stage_in[c % 2, pl.ds(2 * i, 2)] = (y + straight).reshape(2, seqs, half).astype(BF16)
            return 0

        lax.fori_loop(0, chunk // 2, finish_frames, 0)
        order.work(0.5)
        give(c).start()
        if c >= 1:
            give(c - 1).wait()
            if c + 1 < chunks:
                fetch(grad_out, c + 1).start()
    give(chunks - 1).wait()
    order.drain()

    for layer in range(2):

        @pl.when(section == layer)
        def _(layer=layer):
            pltpu.make_async_copy(tot.at[layer], v.at[section], v_sems.at[0]).wait()
            pltpu.make_async_remote_copy(
                src_ref=tot.at[layer], dst_ref=v.at[other], send_sem=v_sems.at[1], recv_sem=v_sems.at[2],
                device_id=sibling, device_id_type=MESH,
            ).wait_recv()

        @pl.when(section != layer)
        def _(layer=layer):
            v_across(layer).wait_send()

    own_part, far_part = v[section], v[other]
    first = jnp.where(section == 0, own_part, far_part)
    second = jnp.where(section == 0, far_part, own_part)
    for out, terms in ((out_gains, (2, 3)), (out_shifts, (0, 1)), (out_recurs, (4,))):
        out[0:1, 0:W] = sum(first[k : k + 1, :] for k in terms[1:]) + first[terms[0] : terms[0] + 1, :]
        out[0:1, W:width] = (
            sum(second[k : k + 1, :rest] for k in terms[1:]) + second[terms[0] : terms[0] + 1, :rest]
        )
    squares = jnp.sum(first[5:7, :] + second[5:7, :], axis=1, keepdims=True)
    root = jnp.sqrt(squares / (first[7:8, 0:1] * width))
    out_table[...] = jnp.concatenate([root[0:1], root[1:2]], axis=1)


def whole_step(dims, frames, grad_out, weights, tail, gains, shifts, recurs, lengths, masks):
    nz, ny, nx = dims
    micro, steps, seqs, half = frames.shape
    width = 2 * half
    views = seqs // lengths.shape[1]
    rows = micro * steps * seqs
    np_ = ny * nx
    wide_rows = (rows + 16 + 127) // 128 * 128
    depth = (nx * ny * nz - 1).bit_length()
    any_ = pl.BlockSpec(memory_space=pl.ANY)
    held = pl.BlockSpec(memory_space=pltpu.VMEM)
    dma = pltpu.SemaphoreType.DMA
    return pl.pallas_call(
        functools.partial(kernel, dims, steps, seqs, views),
        out_shape=(
            jax.ShapeDtypeStruct((2, W, 2 * W), BF16),
            jax.ShapeDtypeStruct(frames.shape, BF16),
            jax.ShapeDtypeStruct((1, width), F32),
            jax.ShapeDtypeStruct((1, width), F32),
            jax.ShapeDtypeStruct((1, width), F32),
            jax.ShapeDtypeStruct((1, 2), F32),
        ),
        in_specs=[any_] * 4 + [held] * 5,
        out_specs=(any_, any_, held, held, held, held),
        scratch_shapes=[
            pltpu.VMEM((wide_rows, W), BF16),
            pltpu.VMEM((rows, W), BF16),
            pltpu.VMEM((wide_rows, W), BF16),
            pltpu.VMEM((rows, W), BF16),
            pltpu.VMEM((3, wide_rows, W), BF16),
            pltpu.VMEM((2, 2, W, W), BF16),
            pltpu.VMEM((W, W), BF16),
            pltpu.VMEM((W, wide_rows), BF16),
            pltpu.VMEM((rows, 128), F32),
            pltpu.VMEM((128, 128), F32),
            pltpu.VMEM((2, steps // 4, seqs, half), BF16),
            pltpu.VMEM((micro, steps, seqs, 128), BF16),
            pltpu.VMEM((2, 8, W), F32),
            pltpu.VMEM((2, 8, 2 * W), F32),
            pltpu.VMEM((2, rows, W), F32),
            pltpu.VMEM((2, rows, W), F32),
            pltpu.VMEM((2, 8, W), F32),
            pltpu.VMEM((2, 8, W), F32),
            pltpu.VMEM((2, 8, W), F32),
            pltpu.VMEM((2, W, 128), BF16),
            pltpu.VMEM((2, np_, 8, W), F32),
            pltpu.VMEM((2, nz, 8, W), F32),
            pltpu.VMEM((2, 4, W, HALF), BF16),
            dma((3, 24)),
            dma((3,)),
            dma((2,)),
            dma((6, max(np_, 2))),
            dma((6, max(np_, 2))),
            dma((6, max(nz, 2))),
            dma((6, max(nz, 2))),
            dma((2, 4, 2, 2 * depth + 2)),
            dma((2, 4, 2, 2 * depth + 2)),
            dma((2, 4, 2, 2)),
        ],
        compiler_params=pltpu.CompilerParams(
            collective_id=0, has_side_effects=True, vmem_limit_bytes=64 * 1024 * 1024
        ),
    )(frames, grad_out, weights, tail, gains, shifts, recurs, lengths, masks)


def shards(dims, frames, grad_out, weights, gains, shifts, recurs, lengths, masks):
    width = 2 * frames.shape[3]
    last = W + (width - W) // 128 * 128
    tail = jnp.pad(weights[0, :, last:], ((0, 0), (0, 128 - (width - last))))
    o, grad_frames, grad_gains, grad_shifts, grad_recurs, table = whole_step(
        dims, frames, grad_out, weights, tail, gains, shifts, recurs, lengths, masks
    )
    grad_weight = o.reshape(2 * W, 2 * W)[:width, :width].astype(F32)
    return grad_frames, grad_weight[None], grad_gains, grad_shifts, grad_recurs, table


def solution(mesh):
    in_specs = (
        P(None, None, "batch", "section"),
        P(None, None, "batch", "section"),
        P("section", None, None),
        P("section", None),
        P("section", None),
        P("section", None),
        P(None, "batch"),
        P(None, None, "batch"),
    )
    out_specs = (
        P(None, None, "batch", "section"),
        P("section", None, None),
        P("section", None),
        P("section", None),
        P("section", None),
        P("section", None),
    )
    body = functools.partial(shards, grid_of(mesh.shape["batch"]))
    return jax.shard_map(body, mesh=mesh, in_specs=in_specs, out_specs=out_specs, check_vma=False)
```

```python
import functools

import jax
import jax.numpy as jnp
from jax import lax
from jax.experimental import pallas as pl
from jax.experimental.pallas import tpu as pltpu
from jax.sharding import PartitionSpec as P

EPS = 1e-05
W = 1024
HALF = W // 2
QUART = W // 4
MESH = pl.DeviceIdType.MESH
F32 = jnp.float32
BF16 = jnp.bfloat16


def grid_of(size):
    if size == 16:
        return (4, 2, 2)
    if size == 128:
        return (8, 4, 4)
    return (size, 1, 1)


def aligned(x, k):
    return pl.multiple_of(x, k)


def wide(x, reps):
    return jnp.concatenate([x] * reps, axis=1)


def fold(x):
    rows = x.shape[0]
    total = x[0:8]
    for k in range(8, rows, 8):
        total = total + x[k : k + 8]
    return total


def dot(a, b, dims):
    return lax.dot_general(a, b, (dims, ((), ())), preferred_element_type=F32)


class Reduction:
    def __init__(self, env, layer, index, block, orders, lane_of):
        self.env, self.layer, self.index, self.block, self.orders = env, layer, index, block, orders
        self.lane_of = lane_of
        self.space = env["space"].at[layer, index]
        self.depth = len(orders[0])
        self.regions = [self.halves(i, order) for i, order in enumerate(orders)]
        self.step = 0
        self.waits = []
        depth = self.depth
        self.steps = [functools.partial(self.scatter, 0)]
        self.steps += [functools.partial(self.scatter, k) for k in range(1, depth)]
        self.steps += [functools.partial(self.gather, k) for k in range(depth - 1, 0, -1)]
        self.steps += [self.give, self.finish]

    def halves(self, i, order):
        row, rows, lane, lanes = 0, W, i * QUART, QUART
        out = [(row, rows, lane, lanes)]
        for axis in order:
            if rows > 16:
                rows //= 2
                row = row + axis["bit"] * rows
            else:
                lanes //= 2
                lane = lane + axis["bit"] * lanes
            out.append((row, rows, lane, lanes))
        return out

    @property
    def free_to_go(self):
        return self.step != self.depth or self.layer in self.env["summed"]

    @property
    def done(self):
        return self.step >= len(self.steps)

    def advance(self):
        self.sent = []
        self.steps[self.step]()
        self.step += 1
        return self.sent

    def remote(self, i, src, dst, slot, where, recv=None):
        sems = (self.layer, self.index, i, slot)
        return pltpu.make_async_remote_copy(
            src_ref=src, dst_ref=dst, send_sem=self.env["ar_send"].at[sems],
            recv_sem=self.env["ar_recv"].at[sems] if recv is None else recv, device_id=where, device_id_type=MESH,
        )

    def wait(self):
        for made, came in self.waits:
            made.wait_send()
            came.wait_recv()
        self.waits = []

    def came_at(self, i, k):
        row = sum(r[1] for r in self.regions[i][1 : k + 1])
        _, rows, _, lanes = self.regions[i][k + 1]
        return row, rows, i * QUART, lanes

    def scatter(self, k):
        if k > 0:
            self.wait()
            self.add(k - 1)
        for i, order in enumerate(self.orders):
            self.scatter_part(i, k, order[k])

    def start_part(self, i):
        self.sent = []
        self.scatter_part(i, 0, self.orders[i][0])
        if i == 1:
            self.step = 1
        return self.sent

    def scatter_part(self, i, k, axis):
        row, rows, lane, lanes = self.regions[i][k]
        _, rows2, _, lanes2 = self.regions[i][k + 1]
        give_row = row + (1 - axis["bit"]) * rows2 if rows2 < rows else row
        give_lane = lane if rows2 < rows else lane + (1 - axis["bit"]) * lanes2
        src = self.block.at[pl.ds(aligned(give_row, 16), rows2), pl.ds(aligned(give_lane, 128), lanes2)]
        at, n, at_lane, n_lanes = self.came_at(i, k)
        dst = self.space.at[pl.ds(at, n), pl.ds(at_lane, n_lanes)]
        made = self.remote(i, src, dst, k, axis["partner"])
        made.start()
        self.waits.append((made, made))
        self.sent.append((axis["link"], rows2 * lanes2 * 2))

    def add(self, k, last=False):
        rows = self.regions[0][k + 1][1]
        size = min(rows, 32)
        out = []
        for i in range(2):
            row, _, lane, lanes = self.regions[i][k + 1]
            at, _, at_lane, _ = self.came_at(i, k)
            lane = aligned(lane, 128)
            extra = None
            if last:
                part = self.index // 2
                first = aligned((self.index % 2) * HALF + lane, 128)
                extra = self.env["vtot"][self.layer, part : part + 1, pl.ds(first, lanes)]
            out.append((row, lane, lanes, at, at_lane, self.local(i, k + 1)[0], extra))

        def body(j, _):
            for row, lane, lanes, at, at_lane, home, extra in out:
                here = pl.ds(aligned(row + j * size, 16), size)
                total = self.block[here, pl.ds(lane, lanes)].astype(F32)
                total = total + self.space[pl.ds(aligned(at + j * size, 16), size), pl.ds(at_lane, lanes)].astype(F32)
                if last:
                    column = self.env["column"][self.layer, here, :].astype(F32)
                    total = total + wide(column, lanes // 128) * extra
                    to = pl.ds(aligned(home + j * size, 16), size)
                    self.space[to, pl.ds(lane, lanes)] = total.astype(BF16)
                else:
                    self.block[here, pl.ds(lane, lanes)] = total.astype(BF16)
            return 0

        lax.fori_loop(0, rows // size, body, 0)

    def local(self, i, k):
        row, rows, lane, lanes = self.regions[i][k]
        return row - self.regions[i][1][0], rows, lane, lanes

    def gather(self, k):
        self.wait()
        if k == self.depth - 1:
            self.add(k, last=True)
        for i, order in enumerate(self.orders):
            axis = order[k]
            row, rows, lane, lanes = self.local(i, k + 1)
            row0, rows0, lane0, lanes0 = self.local(i, k)
            if rows0 > rows:
                far = (row0 + (1 - axis["bit"]) * rows, rows, lane, lanes)
            else:
                far = (row, rows, lane0 + (1 - axis["bit"]) * lanes, lanes)
            refs = [
                self.space.at[pl.ds(aligned(r, 16), n), pl.ds(aligned(c, 128), w)]
                for r, n, c, w in ((row, rows, lane, lanes), far)
            ]
            made = self.remote(i, refs[0], refs[0], self.depth + k, axis["partner"])
            made.start()
            self.waits.append((made, self.remote(i, refs[1], refs[1], self.depth + k, axis["partner"])))
            self.sent.append((axis["link"], rows * lanes * 2))

    def result(self, i, bit, section):
        rows = self.regions[i][1][1]
        lane = aligned(self.lane_of(section) + i * QUART, QUART)
        return self.env["o"].at[section, pl.ds(aligned(bit * rows, 16), rows), pl.ds(lane, QUART)]

    def gathered(self, i):
        return self.space.at[pl.ds(0, self.regions[i][1][1]), pl.ds(i * QUART, QUART)]

    def deliver(self, i, near, straight):
        axis, section = self.orders[i][0], self.env["section"]
        slot = 2 * self.depth + (0 if near else 1)
        recv = None if straight else self.env["ar_other"].at[self.layer, self.index, i, 0 if near else 1]
        where = dict(self.env["here"] if near else axis["partner"], section=self.layer)
        return self.remote(i, self.gathered(i), self.result(i, axis["bit"], section), slot, where, recv)

    def arrival(self, i, near, straight):
        axis, section = self.orders[i][0], self.env["section"]
        slot = 2 * self.depth + (0 if near else 1)
        recv = None if straight else self.env["ar_other"].at[self.layer, self.index, i, 0 if near else 1]
        bit = axis["bit"] if near else 1 - axis["bit"]
        frm = section if straight else 1 - section
        where = dict(self.env["here"] if near else axis["partner"], section=frm)
        return self.remote(i, self.gathered(i), self.result(i, bit, frm), slot, where, recv)

    def kept(self, i):
        sem = self.env["ar_recv"].at[self.layer, self.index, i, 2 * self.depth]
        return pltpu.make_async_copy(
            self.gathered(i), self.result(i, self.orders[i][0]["bit"], self.env["section"]), sem
        )

    def give(self):
        self.wait()

        @pl.when(self.env["section"] == self.layer)
        def _():
            for i in range(2):
                self.deliver(i, False, True).start()
                self.kept(i).start()

        @pl.when(self.env["section"] != self.layer)
        def _():
            for i in range(2):
                self.deliver(i, False, False).start()
                self.deliver(i, True, False).start()

        for i, order in enumerate(self.orders):
            self.sent.append((order[0]["link"], self.regions[i][1][1] * QUART * 2))

    def finish(self):
        @pl.when(self.env["section"] == self.layer)
        def _():
            for i in range(2):
                self.kept(i).wait()
                self.deliver(i, False, True).wait_send()
                self.arrival(i, False, True).wait_recv()
                self.arrival(i, True, False).wait_recv()
                self.arrival(i, False, False).wait_recv()

        @pl.when(self.env["section"] != self.layer)
        def _():
            for i in range(2):
                self.deliver(i, False, False).wait_send()
                self.deliver(i, True, False).wait_send()


class Order:
    RATE, HOP = 50e3, 1.8

    def __init__(self):
        self.now = 0.0
        self.free = {}
        self.going = []

    def sent(self, copies):
        end = self.now
        for link, size in copies:
            self.free[link] = max(self.now, self.free.get(link, 0.0)) + size / self.RATE
            end = max(end, self.free[link])
        return end + self.HOP

    def begin(self, one, i):
        end = self.sent(one.start_part(i))
        if i == 0:
            one.due = end
        else:
            one.due = max(one.due, end)
            self.going.append(one)

    def advance(self, one):
        self.now = max(self.now, one.due) + 0.4
        one.due = self.sent(one.advance())
        if one.done:
            self.going.remove(one)

    def work(self, cost):
        self.now += cost
        while True:
            due = [x for x in self.going if x.due <= self.now and x.free_to_go]
            if not due:
                return
            self.advance(min(due, key=lambda x: x.due))

    def drain(self):
        while self.going:
            self.advance(min(self.going, key=lambda x: x.due))


def kernel(dims, steps, seqs, views, frames, grad_out, weights, tail, gains, shifts, recurs, lengths, masks, o, gf,
           out_gains, out_shifts, out_recurs, out_table, f_own, f_far, p_own, p_far, g3, wc, wr1, src_t, live, turn,
           staged, heads, v, vecs, rows, hid, coef, tot, vtot, levels, column, counts, cnt_p, cnt_z, slim_p, slim_z,
           wide_p, wide_z, space, sems, v_sems, stage_sem, credit, pl_send, pl_recv, z_send, z_recv, ar_send, ar_recv,
           ar_other):
    nz, ny, nx = dims
    np_ = ny * nx
    span = steps * seqs
    total_rows = 2 * span
    sent_rows = total_rows + 16
    pairs = steps // 2
    section = lax.axis_index("section")
    other = 1 - section
    b = lax.axis_index("batch")
    mp = lax.rem(b, np_)
    mz = b // np_

    def at_plane(i):
        return {"batch": b - mp + i}

    def at_z(i):
        return {"batch": b + (i - mz) * np_}

    bits = []
    for link, count, stride in (("x", nx, 1), ("y", ny, nx), ("z", nz, np_)):
        while count > 1:
            bit = lax.rem(b // stride, 2)
            bits.append(dict(bit=bit, partner={"batch": b + (1 - 2 * bit) * stride}, link=link))
            count //= 2
            stride *= 2
    sibling = {"section": other}

    def local(src, dst, slot):
        return pltpu.make_async_copy(src, dst, sems.at[0, slot])

    def across(src, dst, slot):
        return pltpu.make_async_remote_copy(
            src_ref=src, dst_ref=dst, send_sem=sems.at[1, slot], recv_sem=sems.at[2, slot],
            device_id=sibling, device_id_type=MESH,
        )

    half = frames.shape[3]
    width = 2 * half
    lead = W - half
    rest = width - W
    full = rest // 128 * 128

    def fetch(source, m):
        return pltpu.make_async_copy(source.at[m], staged.at[m], stage_sem.at[m])

    def by_units(source, target, m):
        fetch(source, m).wait()

        @pl.when(section == 0)
        def _():
            def place(i, _):
                x = staged[m, pl.ds(2 * i, 2)].astype(F32).reshape(2 * seqs, half)
                head = heads[m, pl.ds(2 * i, 2)].astype(F32).reshape(2 * seqs, 128)
                to = pl.ds(aligned(m * span + 2 * i * seqs, 16), 2 * seqs)
                target[to, :] = jnp.concatenate([x, head[:, :lead]], axis=1).astype(BF16)
                return 0

            lax.fori_loop(0, pairs, place, 0)

        @pl.when(section == 1)
        def _():
            pad = jnp.zeros((2 * seqs, 2 * lead), F32)

            def place(i, _):
                x = staged[m, pl.ds(2 * i, 2)].astype(F32).reshape(2 * seqs, half)
                to = pl.ds(aligned(m * span + 2 * i * seqs, 16), 2 * seqs)
                target[to, :] = jnp.concatenate([x[:, lead:], pad], axis=1).astype(BF16)
                return 0

            lax.fori_loop(0, pairs, place, 0)

    def pieces(row, count, u, block):
        r = pl.ds(row, count)
        to = pl.ds(0, count)
        if u == 0:
            return [(weights.at[0, r, pl.ds(0, W)], block.at[to, :])]
        return [
            (weights.at[0, r, pl.ds(W, full)], block.at[to, pl.ds(0, full)]),
            (tail.at[r, :], block.at[to, pl.ds(full, 128)]),
        ]

    rows_of = {0: (0, W), 1: (W, rest)}

    def w_plan(layer):
        mine, far = rows_of[layer], rows_of[1 - layer]
        plan = [
            (mine, layer, far, 1 - layer, wc.at[layer, 0]),
            (far, layer, mine, 1 - layer, wc.at[layer, 1]),
        ]
        if layer == 1:
            plan.append((mine, 0, far, 1, wr1))
        return plan

    late_row = (width - half) // 16 * 16
    late_shift = half - late_row
    late_plan = [
        ((0, W), 0, (late_row, width - late_row), 1, wc.at[0, 0]),
        ((0, W), 1, (late_row, width - late_row), 0, wc.at[0, 1]),
    ]
    slot_of = {0: 4, 1: 8, 2: 14}

    def local_w(plan, base, which):
        r, u, _, _, block = plan[which]
        return [local(a, t, base + 2 * which + i) for i, (a, t) in enumerate(pieces(*r, u, block))]

    def across_w(plan, base, which):
        _, _, r, u, block = plan[which]
        return [across(a, t, base + 2 * which + i) for i, (a, t) in enumerate(pieces(*r, u, block))]

    def start_local_w(layer, plan, base):
        @pl.when(section == layer)
        def _():
            for which in range(len(plan)):
                for made in local_w(plan, base, which):
                    made.start()

    def start_across_w(layer, plan, base):
        @pl.when(section == layer)
        def _():
            for which in range(len(plan)):
                for made in across_w(plan, base, which):
                    made.start()

    def wait_w(layer, plan, base, which):
        @pl.when(section == layer)
        def _():
            for made in local_w(plan, base, which):
                made.wait()

        @pl.when(section != layer)
        def _():
            for made in across_w(plan, base, which):
                made.wait_recv()

    def done_w(layer, plan, base):
        @pl.when(section == layer)
        def _():
            for which in range(len(plan)):
                for made in across_w(plan, base, which):
                    made.wait_send()

    def heads_copy(source, slot):
        return across(source.at[:, :, :, pl.ds(0, 128)], heads, slot)

    def wait_heads(source, slot):
        @pl.when(section == 0)
        def _():
            heads_copy(source, slot).wait_recv()

        @pl.when(section == 1)
        def _():
            heads_copy(source, slot).wait_send()

    fetch(frames, 0).start()
    fetch(frames, 1).start()
    for layer in range(2):
        start_local_w(layer, w_plan(layer), slot_of[layer])

    barrier = pltpu.get_barrier_semaphore()
    greeted = [dict(sibling)]
    greeted += [at_plane(lax.rem(mp + k, np_)) for k in range(1, np_)]
    greeted += [at_z(lax.rem(mz + k, nz)) for k in range(1, nz)]
    greeted += [dict(axis["partner"], section=other) for axis in bits]
    for where in greeted:
        pl.semaphore_signal(barrier, inc=1, device_id=where, device_id_type=MESH)

    for k, (x, fill) in enumerate(((gains, 0.0), (shifts, -1e30), (recurs, 0.0))):
        vecs[section, k : k + 1, 0:width] = x[...]
        vecs[section, k : k + 1, width:] = jnp.full((1, 2 * W - width), fill, F32)
    vecs[section, 3:8, :] = jnp.zeros((5, 2 * W), F32)

    gap = jnp.zeros((W - rest, W), BF16)

    @pl.when(section == 0)
    def _():
        wc[0, 1, rest:, :] = gap
        wc[1, 1, rest:, :] = gap

    @pl.when(section == 1)
    def _():
        wc[0, 0, rest:, :] = gap
        wc[1, 0, rest:, :] = gap
        wr1[rest:, :] = gap

    for spare in (f_own, p_own, g3.at[0], g3.at[1]):
        spare[sent_rows:, :] = jnp.zeros((spare.shape[0] - sent_rows, W), BF16)

    pl.semaphore_wait(barrier, len(greeted))

    @pl.when(section == 1)
    def _():
        heads_copy(frames, 1).start()

    for layer in range(2):
        start_across_w(layer, w_plan(layer), slot_of[layer])
    send_vec = across(vecs.at[section], vecs.at[section], 3)
    send_vec.start()

    def stage_copy(where, rnd, slot, k, back):
        buf, parity, size, me, at, send, recv = where
        there = at(lax.rem(me + (size - k if back else k), size))
        ref = buf.at[parity, slot]
        return pltpu.make_async_remote_copy(
            src_ref=ref, dst_ref=ref, send_sem=send.at[rnd, k], recv_sem=recv.at[rnd, k],
            device_id=there, device_id_type=MESH,
        )

    def in_plane(buf, parity):
        return (buf, parity, np_, mp, at_plane, pl_send, pl_recv)

    def in_line(buf, parity):
        return (buf, parity, nz, mz, at_z, z_send, z_recv)

    def stage_start(where, rnd, value):
        buf, parity, size, me = where[:4]
        buf[parity, me] = value
        for k in range(1, size):
            stage_copy(where, rnd, me, k, False).start()

    def stage_wait(where, rnd):
        size, me = where[2:4]
        for k in range(1, size):
            stage_copy(where, rnd, me, k, False).wait_send()
            stage_copy(where, rnd, lax.rem(me + size - k, size), k, True).wait_recv()

    def add_slots(where):
        buf, parity, size = where[:3]
        total = buf[parity, 0]
        for k in range(1, size):
            total = total + buf[parity, k]
        return total

    groups = lengths.shape[1]
    s_at = lax.broadcasted_iota(jnp.int32, (seqs, groups), 0)
    g_at = lax.broadcasted_iota(jnp.int32, (seqs, groups), 1) * views
    there = (s_at >= g_at) & (s_at < g_at + views)
    position = lax.broadcasted_iota(jnp.int32, (seqs, 128), 1)
    local_counts = []
    for m in range(2):
        turn[...] = jnp.zeros_like(turn)
        turn[0:steps, 0:seqs] = masks[m].astype(F32)
        mask = turn[...].T[0:seqs]
        length = jnp.broadcast_to(lengths[m : m + 1, :], (seqs, groups)).astype(F32)
        limit = jnp.sum(jnp.where(there, length, 0.0), axis=1, keepdims=True)
        alive = (position.astype(F32) < limit) & ((mask > 0.0) | (position == 0))
        alive = jnp.where(position < steps, alive.astype(F32), 0.0)
        total = jnp.zeros((seqs, 128), F32)
        for t in range(steps):
            at = m * span + t * seqs
            cells = jnp.broadcast_to(alive[:, t : t + 1], (seqs, 128))
            live[at : at + seqs, :] = cells
            total = total + cells
        local_counts.append(jnp.sum(total, axis=0, keepdims=True))
    n_own = jnp.concatenate(local_counts * 4, axis=0)

    cnt_plane, cnt_line = in_plane(cnt_p, 0), in_line(cnt_z, 0)
    stage_start(cnt_plane, 0, n_own)

    def vec_of(layer, k):
        return vecs[layer, k : k + 1, pl.ds(aligned(section * W, W), W)]

    def matmul_to(out, a, w, first, m):
        r = pl.ds(m * span, span)

        def body(i, _):
            c = pl.ds(aligned(i * HALF, HALF), HALF)
            y = dot(a[r, :], w[:, c], ((1,), (0,)))
            out[r, c] = y if first else out[r, c] + y
            return 0

        lax.fori_loop(0, 2, body, 0)

    def packed(pair_a, pair_b):
        a = jnp.concatenate(pair_a, axis=0)
        c = jnp.concatenate(pair_b, axis=0)
        return jnp.concatenate([a[:, :HALF], a[:, HALF:], c[:, :HALF], c[:, HALF:]], axis=0)

    def unpacked(x):
        return jnp.concatenate([x[0:2], x[2:4]], axis=1)

    def merge_slots(where, counts_of):
        buf, parity, size = where[:3]
        s = [buf[parity, k, 0:4, :] for k in range(size)]
        q = [buf[parity, k, 4:8, :] for k in range(size)]
        n = [wide(counts_of(k)[0:4], 4) for k in range(size)]
        total, squares, count = sum(s[1:], s[0]), sum(q[1:], q[0]), sum(n[1:], n[0])
        mean = total / count
        for k in range(size):
            d = s[k] / n[k] - mean
            squares = squares + n[k] * d * d
        return jnp.concatenate([total, squares], axis=0)

    def forward_stats(layer, fill_plane, fill_line):
        sums, squares = [], []
        for m in range(2):
            start = jnp.sum(rows[layer, m * span : m * span + seqs, :], axis=0, keepdims=True) * (1.0 / seqs)

            def body(i, carry):
                s, q = carry
                r = pl.ds(aligned(m * span + i * (2 * seqs), 16), 2 * seqs)
                d = rows[layer, r, :] - start
                kept = wide(live[r, :], 8) * d
                return s + fold(kept), q + fold(kept * d)

            zero = jnp.zeros((8, W), F32)
            s, q = lax.fori_loop(0, pairs, body, (zero, zero))
            s, q = jnp.sum(s, axis=0, keepdims=True), jnp.sum(q, axis=0, keepdims=True)
            n = wide(local_counts[m], 8)
            sums.append(s + n * start)
            squares.append(jnp.maximum(q - s * s / n, 0.0))
        plane, line = in_plane(slim_p, layer), in_line(slim_z, layer)
        stage_start(plane, 1 + layer, packed(sums, squares))
        fill_plane()
        stage_wait(plane, 1 + layer)
        stage_start(line, 1 + layer, merge_slots(plane, lambda k: cnt_p[0, k]))
        fill_line()
        stage_wait(line, 1 + layer)
        value = merge_slots(line, lambda k: cnt_z[0, k])
        total, squares = unpacked(value[0:4]), unpacked(value[4:8])
        for m in range(2):
            count = wide(counts[m : m + 1, :], 8)
            coef[layer, 2 * m : 2 * m + 1, :] = total[m : m + 1] / count
            coef[layer, 2 * m + 1 : 2 * m + 2, :] = lax.rsqrt(squares[m : m + 1] / count + EPS)

    def forward_scan(layer, passes):
        gain, shift, recur = vec_of(layer, 0), vec_of(layer, 1), vec_of(layer, 2)
        sends = []
        for lh in range(2):
            lanes = slice(lh * HALF, (lh + 1) * HALF)
            a, c = [], []
            for m in range(2):
                mean = coef[layer, 2 * m : 2 * m + 1, lanes]
                a.append(gain[:, lanes] * coef[layer, 2 * m + 1 : 2 * m + 2, lanes])
                c.append((shift[:, lanes], mean))
            rec = recur[:, lanes]

            def body(i, carry):
                states, level = carry
                out = []
                for m in range(2):
                    r = pl.ds(aligned(m * span + i * (2 * seqs), 16), 2 * seqs)
                    x = (rows[layer, r, lanes] - c[m][1]) * a[m] + c[m][0]
                    lv = wide(live[r, :], 4)
                    alive = lv > 0.0
                    h = states[m]
                    both = []
                    for k in range(2):
                        part = slice(k * seqs, (k + 1) * seqs)
                        z = x[part] + rec * h
                        soft = jnp.maximum(z, 0.0) + jnp.log(1.0 + jnp.exp(-jnp.abs(z)))
                        h = jnp.where(alive[part], soft, h)
                        both.append(h)
                    two = jnp.concatenate(both, axis=0)
                    hid[layer, r, lanes] = two
                    if passes:
                        p_own[r, lanes] = two.astype(BF16)
                        level = level + fold(lv * two)
                    out.append(h)
                return tuple(out), level

            zero = jnp.zeros((seqs, HALF), F32)
            _, level = lax.fori_loop(0, pairs, body, ((zero, zero), jnp.zeros((8, HALF), F32)))
            if passes:
                levels[1:2, lanes] = jnp.sum(level, axis=0, keepdims=True)
                made = across(p_own.at[pl.ds(0, total_rows), lanes], p_far.at[:, lanes], 18 + lh)
                made.start()
                sends.append(made)
        return sends

    def backward_scan(layer, above, between=lambda: None):
        gain, shift, recur = vec_of(layer, 0), vec_of(layer, 1), vec_of(layer, 2)
        for lq in range(4):
            lanes = slice(lq * QUART, (lq + 1) * QUART)
            gq, sq, rec = gain[:, lanes], shift[:, lanes], recur[:, lanes]
            mean = [coef[layer, 2 * m : 2 * m + 1, lanes] for m in range(2)]
            scale = [coef[layer, 2 * m + 1 : 2 * m + 2, lanes] for m in range(2)]

            def body(i, carry):
                down, s1, s2, rsum, sqh, sqa = carry
                down, s1, s2 = list(down), list(s1), list(s2)
                i = pairs - 1 - i
                for m in range(2):
                    start = m * span + i * (2 * seqs)
                    r = pl.ds(aligned(start, 16), 2 * seqs)
                    before = pl.ds(aligned(jnp.maximum(start - seqs, 0), 8), seqs)
                    normed = (rows[layer, r, lanes] - mean[m]) * scale[m]
                    drive = gq * normed + sq
                    h2 = hid[layer, r, lanes]
                    hb = jnp.where(i > 0, hid[layer, before, lanes], 0.0)
                    lv = wide(live[r, :], 2)
                    up = above[r, lanes].astype(F32)
                    res = f_own[r, lanes].astype(F32)
                    aux = res + h2 if layer == 1 else res
                    sqh = sqh + fold(lv * (h2 * h2))
                    sqa = sqa + fold(lv * (aux * aux))
                    grads = [None, None]
                    for k in (1, 0):
                        part = slice(k * seqs, (k + 1) * seqs)
                        prior = h2[0:seqs] if k == 1 else hb
                        slope = 0.5 + 0.5 * jnp.tanh(0.5 * (drive[part] + rec * prior))
                        total = up[part] + down[m]
                        gd = lv[part] * slope * total
                        down[m] = (1.0 - lv[part]) * total + rec * gd
                        grads[k] = gd
                        rsum = rsum + fold(gd * prior)
                    gd2 = jnp.concatenate(grads, axis=0)
                    hid[layer, r, lanes] = gd2
                    s1[m] = s1[m] + fold(gd2)
                    s2[m] = s2[m] + fold(gd2 * normed)
                return tuple(down), tuple(s1), tuple(s2), rsum, sqh, sqa

            zero = jnp.zeros((seqs, QUART), F32)
            z8 = jnp.zeros((8, QUART), F32)
            _, s1, s2, rsum, sqh, sqa = lax.fori_loop(
                0, pairs, body, ((zero, zero), (z8, z8), (z8, z8), z8, z8, z8)
            )
            for k, x in enumerate((s1[0], s1[1], s2[0], s2[1], rsum, sqh, sqa)):
                tot[layer, k : k + 1, lanes] = jnp.sum(x, axis=0, keepdims=True)
            between()

    def backward_stats(layer, fill_plane, fill_line):
        rnd = 4 if layer == 1 else 3
        plane, line = in_plane(slim_p, 1 - layer), in_line(slim_z, 1 - layer)
        t = tot[layer]
        stage_start(plane, rnd, packed([t[0:1], t[1:2]], [t[2:3], t[3:4]]))
        fill_plane()
        stage_wait(plane, rnd)
        stage_start(line, rnd, add_slots(plane))
        fill_line()
        stage_wait(line, rnd)
        value = add_slots(line)
        tot[layer, 0:2, :] = unpacked(value[0:4])
        tot[layer, 2:4, :] = unpacked(value[4:8])

    def grad_rows(layer, slot):
        gain = vec_of(layer, 0)
        sends = []
        for lh in range(2):
            lanes = slice(lh * HALF, (lh + 1) * HALF)
            acc = jnp.zeros((8, HALF), F32)
            for m in range(2):
                mean = coef[layer, 2 * m : 2 * m + 1, lanes]
                scale = coef[layer, 2 * m + 1 : 2 * m + 2, lanes]
                count = wide(counts[m : m + 1, :], 4)
                first = tot[layer, m : m + 1, lanes] / count
                second = tot[layer, 2 + m : 3 + m, lanes] / count * scale
                k = scale * gain[:, lanes]

                def body(i, acc):
                    r = pl.ds(aligned(m * span + i * (2 * seqs), 16), 2 * seqs)
                    y = hid[layer, r, lanes] - first - (rows[layer, r, lanes] - mean) * second
                    y = wide(live[r, :], 4) * (k * y)
                    g3[0, r, lanes] = y.astype(BF16)
                    return acc + fold(y)

                acc = lax.fori_loop(0, pairs, body, acc)
            top = lax.broadcasted_iota(jnp.int32, (16, HALF), 0) == 0
            minus = jnp.where(top, -jnp.sum(acc, axis=0, keepdims=True), 0.0)
            g3[0, total_rows:sent_rows, lanes] = minus.astype(BF16)
            made = across(g3.at[0, pl.ds(0, sent_rows), lanes], g3.at[1, pl.ds(0, sent_rows), lanes], slot + lh)
            made.start()
            sends.append(made)
        return sends

    sums_round = {1: (1, 6), 0: (0, 7)}

    def sums_start(layer):
        parity, rnd = sums_round[layer]
        own_sum = -g3[0, total_rows:sent_rows, :].astype(F32)[0:1]
        far_sum = -g3[1, total_rows:sent_rows, :].astype(F32)[0:1]
        value = jnp.concatenate([own_sum, far_sum, tot[layer, 4:7, :], jnp.zeros((3, W), F32)], axis=0)
        stage_start(in_plane(wide_p, parity), rnd, value)

    def sums_middle(layer):
        parity, rnd = sums_round[layer]
        stage_wait(in_plane(wide_p, parity), rnd)
        stage_start(in_line(wide_z, parity), rnd, add_slots(in_plane(wide_p, parity)))

    def sums_end(layer):
        parity, rnd = sums_round[layer]
        stage_wait(in_line(wide_z, parity), rnd)
        vtot[layer] = add_slots(in_line(wide_z, parity))
        tot[layer, 4:7, :] = vtot[layer, 2:5, :]
        tot[layer, 7:8, :] = wide(counts[0:1, :] + counts[1:2, :], 8)
        env["summed"].add(layer)

        @pl.when(section == layer)
        def _():
            pltpu.make_async_copy(tot.at[layer], v.at[section], v_sems.at[0]).start()

        @pl.when(section != layer)
        def _():
            v_across(layer).start()

    def v_across(layer):
        return pltpu.make_async_remote_copy(
            src_ref=tot.at[layer], dst_ref=v.at[section], send_sem=v_sems.at[1], recv_sem=v_sems.at[2],
            device_id=sibling, device_id_type=MESH,
        )

    def transpose(src):
        def body(j, _):
            c = pl.ds(aligned(j * 128, 128), 128)
            src_t[c, 0:total_rows] = src[0:total_rows, c].T
            return 0

        lax.fori_loop(0, W // 128, body, 0)

    def transpose_level(src, layer):
        top = lax.broadcasted_iota(jnp.int32, (16, W), 0) == 0
        src[total_rows:sent_rows, :] = jnp.where(top, levels[2 + layer : 3 + layer, :], 0.0).astype(BF16)

        def body(j, _):
            c = pl.ds(aligned(j * 128, 128), 128)
            src_t[c, total_rows:] = src[total_rows:, c].T
            level = src[total_rows:sent_rows, c].astype(F32)[0:1]
            column[layer, c, :] = jnp.broadcast_to(level, (128, 128)).T.astype(BF16)
            return 0

        lax.fori_loop(0, W // 128, body, 0)

    def weight_part(block, grads, c):
        lanes = pl.ds(c * QUART, QUART)

        def body(j, _):
            r = pl.ds(aligned(j * HALF, HALF), HALF)
            block[r, lanes] = dot(src_t[r, :], grads[:, lanes], ((1,), (0,))).astype(BF16)
            return 0

        lax.fori_loop(0, W // HALF, body, 0)

    def source_grad(store, w_own, w_far, between):
        for m in range(2):
            r = pl.ds(m * span, span)

            def body(i, _):
                c = pl.ds(aligned(i * HALF, HALF), HALF)
                y = dot(g3[0, r, :], w_own[c, :], ((1,), (1,))) + dot(g3[1, r, :], w_far[c, :], ((1,), (1,)))
                store(r, c, y)
                return 0

            lax.fori_loop(0, 2, body, 0)
            between()

    env = dict(summed=set(), vtot=vtot, column=column, space=space, ar_send=ar_send, ar_recv=ar_recv,
               ar_other=ar_other, o=o, section=section, here={"batch": b})
    xs = [a for a in bits if a["link"] == "x"]
    ys = [a for a in bits if a["link"] == "y"]
    zs = [a for a in bits if a["link"] == "z"]
    orders = (xs + ys + zs, ys + xs + zs)
    blocks = {
        (1, 0): f_far.at[pl.ds(0, W), :],
        (1, 1): p_far.at[pl.ds(0, W), :],
        (0, 0): wc.at[1, 1],
        (0, 1): wr1,
    }
    parts = {}
    for layer in (1, 0):
        for index in range(4):
            part, side = index // 2, index % 2

            def lane_of(sec, part=part, side=side):
                return (sec if part == 0 else 1 - sec) * W + side * HALF

            block = blocks[layer, part].at[:, pl.ds(side * HALF, HALF)]
            parts[layer, index] = Reduction(env, layer, index, block, orders, lane_of)
    order = Order()

    def weight_grads(layer, between):
        for part in range(2):
            if part == 1:
                between()
            for c in range(4):
                weight_part(blocks[layer, part], g3.at[part], c)
                order.work(0.9)
                order.begin(parts[layer, 2 * part + c // 2], c % 2)

    def arrived(layer, sends):
        for made in sends:
            made.wait()
        sums_start(layer)

    nothing = lambda: None

    wait_heads(frames, 1)
    send_f = []
    for m in range(2):
        by_units(frames, f_own, m)
        here = pl.ds(m * span, span)
        made = across(f_own.at[here, :], f_far.at[here, :], (0, 24)[m])
        made.start()
        send_f.append(made)
    wait_w(0, w_plan(0), slot_of[0], 0)
    for m in range(2):
        matmul_to(rows.at[0], f_own, wc.at[0, 0], True, m)
    wait_w(0, w_plan(0), slot_of[0], 1)
    for m in range(2):
        send_f[m].wait()
        matmul_to(rows.at[0], f_far, wc.at[0, 1], False, m)
    fetch(grad_out, 0).start()
    fetch(grad_out, 1).start()
    stage_wait(cnt_plane, 0)
    stage_start(cnt_line, 0, add_slots(cnt_plane))
    send_vec.wait_send()
    across(vecs.at[other], vecs.at[other], 3).wait_recv()

    def source_level():
        def body(i, acc):
            r = pl.ds(aligned(i * (2 * seqs), 16), 2 * seqs)
            return acc + fold(wide(live[r, :], 8) * f_own[r, :].astype(F32))

        acc = lax.fori_loop(0, 2 * pairs, body, jnp.zeros((8, W), F32))
        levels[0:1, :] = jnp.sum(acc, axis=0, keepdims=True)

    def counted():
        source_level()
        stage_wait(cnt_line, 0)
        counts[...] = add_slots(cnt_line)

    forward_stats(0, nothing, counted)
    sends = forward_scan(0, True)
    level_plane, level_line = in_plane(wide_p, 0), in_line(wide_z, 0)
    stage_start(level_plane, 5, jnp.concatenate([levels[0:2, :], jnp.zeros((6, W), F32)], axis=0))
    wait_w(1, w_plan(1), slot_of[1], 0)
    for m in range(2):
        matmul_to(rows.at[1], p_own, wc.at[1, 0], True, m)
    wait_w(1, w_plan(1), slot_of[1], 1)
    for made in sends:
        made.wait()
    done_w(0, w_plan(0), slot_of[0])

    start_local_w(0, late_plan, slot_of[2])
    start_across_w(0, late_plan, slot_of[2])

    @pl.when(section == 1)
    def _():
        wc[0, 1, width - late_row :, :] = jnp.zeros((W - width + late_row, W), BF16)
        heads_copy(grad_out, 2).start()

    for m in range(2):
        matmul_to(rows.at[1], p_far, wc.at[1, 1], False, m)
    stage_wait(level_plane, 5)
    stage_start(level_line, 5, add_slots(level_plane))

    def cotangent():
        wait_heads(grad_out, 2)
        for m in range(2):
            by_units(grad_out, f_far, m)

    def levelled():
        stage_wait(level_line, 5)
        value = add_slots(level_line) / wide(counts[0:1, :] + counts[1:2, :], 8)
        levels[2:4, :] = value[0:2]

    forward_stats(1, lambda: transpose(p_own), cotangent)
    forward_scan(1, False)
    levelled()
    backward_scan(1, f_far)
    backward_stats(1, lambda: transpose_level(p_own, 1), nothing)
    sends = grad_rows(1, 20)
    weight_grads(1, lambda: arrived(1, sends))
    wait_w(1, w_plan(1), slot_of[1], 2)
    done_w(1, w_plan(1), slot_of[1])

    def keep_down(r, c, y):
        p_own[r, c] = y.astype(BF16)

    source_grad(keep_down, wc.at[1, 0], wr1, lambda: order.work(3.0))
    pl.semaphore_signal(credit, inc=1, device_id=sibling, device_id_type=MESH)
    sums_middle(1)
    backward_scan(0, p_own, lambda: order.work(1.2))
    sums_end(1)

    def turn_frames():
        transpose(f_own)
        transpose_level(f_own, 0)
        order.work(3.0)

    backward_stats(0, turn_frames, lambda: order.work(3.0))
    pl.semaphore_wait(credit, 1)
    sends = grad_rows(0, 22)
    order.work(2.0)
    weight_grads(0, lambda: arrived(0, sends))
    wait_w(0, late_plan, slot_of[2], 0)
    wait_w(0, late_plan, slot_of[2], 1)
    done_w(0, late_plan, slot_of[2])

    def keep_source(r, c, y):
        rows[0, r, c] = y

    fetch(grad_out, 0).start()
    fetch(grad_out, 1).start()
    sums_middle(0)
    source_grad(keep_source, wc.at[0, 0], wc.at[0, 1], lambda: order.work(3.0))
    sums_end(0)

    def give(m):
        return pltpu.make_async_copy(staged.at[m], gf.at[m], stage_sem.at[m])

    for m in range(2):
        fetch(grad_out, m).wait()

        def finish_frames(i, _, m=m):
            straight = staged[m, pl.ds(2 * i, 2)].astype(F32).reshape(2 * seqs, half)
            y = rows[0, pl.ds(aligned(m * span + 2 * i * seqs, 8), 2 * seqs), :]
            y = jnp.where(section == 0, y[:, :half], y[:, late_shift : late_shift + half])
            staged[m, pl.ds(2 * i, 2)] = (y + straight).reshape(2, seqs, half).astype(BF16)
            return 0

        lax.fori_loop(0, pairs, finish_frames, 0)
        give(m).start()
        order.work(2.0)
    order.drain()
    for m in range(2):
        give(m).wait()

    for layer in range(2):

        @pl.when(section == layer)
        def _(layer=layer):
            pltpu.make_async_copy(tot.at[layer], v.at[section], v_sems.at[0]).wait()
            pltpu.make_async_remote_copy(
                src_ref=tot.at[layer], dst_ref=v.at[other], send_sem=v_sems.at[1], recv_sem=v_sems.at[2],
                device_id=sibling, device_id_type=MESH,
            ).wait_recv()

        @pl.when(section != layer)
        def _(layer=layer):
            v_across(layer).wait_send()

    own_part, far_part = v[section], v[other]
    first = jnp.where(section == 0, own_part, far_part)
    second = jnp.where(section == 0, far_part, own_part)
    for out, terms in ((out_gains, (2, 3)), (out_shifts, (0, 1)), (out_recurs, (4,))):
        out[0:1, 0:W] = sum(first[k : k + 1, :] for k in terms[1:]) + first[terms[0] : terms[0] + 1, :]
        out[0:1, W:width] = (
            sum(second[k : k + 1, :rest] for k in terms[1:]) + second[terms[0] : terms[0] + 1, :rest]
        )
    squares = jnp.sum(first[5:7, :] + second[5:7, :], axis=1, keepdims=True)
    root = jnp.sqrt(squares / (first[7:8, 0:1] * width))
    out_table[...] = jnp.concatenate([root[0:1], root[1:2]], axis=1)


def whole_step(dims, frames, grad_out, weights, tail, gains, shifts, recurs, lengths, masks):
    nz, ny, nx = dims
    micro, steps, seqs, half = frames.shape
    width = 2 * half
    views = seqs // lengths.shape[1]
    rows = micro * steps * seqs
    np_ = ny * nx
    wide_rows = (rows + 16 + 127) // 128 * 128
    depth = (nx * ny * nz - 1).bit_length()
    any_ = pl.BlockSpec(memory_space=pl.ANY)
    held = pl.BlockSpec(memory_space=pltpu.VMEM)
    dma = pltpu.SemaphoreType.DMA
    return pl.pallas_call(
        functools.partial(kernel, dims, steps, seqs, views),
        out_shape=(
            jax.ShapeDtypeStruct((2, W, 2 * W), BF16),
            jax.ShapeDtypeStruct(frames.shape, BF16),
            jax.ShapeDtypeStruct((1, width), F32),
            jax.ShapeDtypeStruct((1, width), F32),
            jax.ShapeDtypeStruct((1, width), F32),
            jax.ShapeDtypeStruct((1, 2), F32),
        ),
        in_specs=[any_] * 4 + [held] * 5,
        out_specs=(any_, any_, held, held, held, held),
        scratch_shapes=[
            pltpu.VMEM((wide_rows, W), BF16),
            pltpu.VMEM((rows, W), BF16),
            pltpu.VMEM((wide_rows, W), BF16),
            pltpu.VMEM((rows, W), BF16),
            pltpu.VMEM((2, wide_rows, W), BF16),
            pltpu.VMEM((2, 2, W, W), BF16),
            pltpu.VMEM((W, W), BF16),
            pltpu.VMEM((W, wide_rows), BF16),
            pltpu.VMEM((rows, 128), F32),
            pltpu.VMEM((128, 128), F32),
            pltpu.VMEM(frames.shape, BF16),
            pltpu.VMEM((micro, steps, seqs, 128), BF16),
            pltpu.VMEM((2, 8, W), F32),
            pltpu.VMEM((2, 8, 2 * W), F32),
            pltpu.VMEM((2, rows, W), F32),
            pltpu.VMEM((2, rows, W), F32),
            pltpu.VMEM((2, 8, W), F32),
            pltpu.VMEM((2, 8, W), F32),
            pltpu.VMEM((2, 8, W), F32),
            pltpu.VMEM((8, W), F32),
            pltpu.VMEM((2, W, 128), BF16),
            pltpu.VMEM((8, 128), F32),
            pltpu.VMEM((1, np_, 8, 128), F32),
            pltpu.VMEM((1, nz, 8, 128), F32),
            pltpu.VMEM((2, np_, 8, HALF), F32),
            pltpu.VMEM((2, nz, 8, HALF), F32),
            pltpu.VMEM((2, np_, 8, W), F32),
            pltpu.VMEM((2, nz, 8, W), F32),
            pltpu.VMEM((2, 4, W, HALF), BF16),
            dma((3, 25)),
            dma((3,)),
            dma((2,)),
            pltpu.SemaphoreType.REGULAR,
            dma((8, max(np_, 2))),
            dma((8, max(np_, 2))),
            dma((8, max(nz, 2))),
            dma((8, max(nz, 2))),
            dma((2, 4, 2, 2 * depth + 2)),
            dma((2, 4, 2, 2 * depth + 2)),
            dma((2, 4, 2, 2)),
        ],
        compiler_params=pltpu.CompilerParams(
            collective_id=0, has_side_effects=True, vmem_limit_bytes=64 * 1024 * 1024
        ),
    )(frames, grad_out, weights, tail, gains, shifts, recurs, lengths, masks)


def shards(dims, frames, grad_out, weights, gains, shifts, recurs, lengths, masks):
    width = 2 * frames.shape[3]
    last = W + (width - W) // 128 * 128
    tail = jnp.pad(weights[0, :, last:], ((0, 0), (0, 128 - (width - last))))
    o, grad_frames, grad_gains, grad_shifts, grad_recurs, table = whole_step(
        dims, frames, grad_out, weights, tail, gains, shifts, recurs, lengths, masks
    )
    grad_weight = o.reshape(2 * W, 2 * W)[:width, :width].astype(F32)
    return grad_frames, grad_weight[None], grad_gains, grad_shifts, grad_recurs, table


def solution(mesh):
    in_specs = (
        P(None, None, "batch", "section"),
        P(None, None, "batch", "section"),
        P("section", None, None),
        P("section", None),
        P("section", None),
        P("section", None),
        P(None, "batch"),
        P(None, None, "batch"),
    )
    out_specs = (
        P(None, None, "batch", "section"),
        P("section", None, None),
        P("section", None),
        P("section", None),
        P("section", None),
        P("section", None),
    )
    body = functools.partial(shards, grid_of(mesh.shape["batch"]))
    return jax.shard_map(body, mesh=mesh, in_specs=in_specs, out_specs=out_specs, check_vma=False)
```

```python
import functools

import jax
import jax.numpy as jnp
from jax import lax
from jax.experimental import pallas as pl
from jax.experimental.pallas import tpu as pltpu
from jax.sharding import PartitionSpec as P

EPS = 1e-05
W = 1024
HALF = W // 2
QUART = W // 4
MESH = pl.DeviceIdType.MESH
F32 = jnp.float32
BF16 = jnp.bfloat16


def grid_of(size):
    if size == 16:
        return (4, 2, 2)
    if size == 128:
        return (8, 4, 4)
    return (size, 1, 1)


def aligned(x, k):
    return pl.multiple_of(x, k)


def wide(x, reps):
    return jnp.concatenate([x] * reps, axis=1)


def fold(x):
    rows = x.shape[0]
    total = x[0:8]
    for k in range(8, rows, 8):
        total = total + x[k : k + 8]
    return total


def dot(a, b, dims):
    return lax.dot_general(a, b, (dims, ((), ())), preferred_element_type=F32)


class Reduction:
    def __init__(self, env, layer, index, block, orders, lane_of):
        self.env, self.layer, self.index, self.block, self.orders = env, layer, index, block, orders
        self.lane_of = lane_of
        self.space = env["space"].at[layer, index]
        self.depth = len(orders[0])
        self.regions = [self.halves(i, order) for i, order in enumerate(orders)]
        self.step = 0
        self.waits = []
        depth = self.depth
        self.steps = [functools.partial(self.scatter, 0)]
        self.steps += [functools.partial(self.scatter, k) for k in range(1, depth)]
        self.steps += [functools.partial(self.gather, k) for k in range(depth - 1, 0, -1)]
        self.steps += [self.give, self.finish]

    def halves(self, i, order):
        row, rows, lane, lanes = 0, W, i * QUART, QUART
        out = [(row, rows, lane, lanes)]
        for axis in order:
            if rows > 16:
                rows //= 2
                row = row + axis["bit"] * rows
            else:
                lanes //= 2
                lane = lane + axis["bit"] * lanes
            out.append((row, rows, lane, lanes))
        return out

    @property
    def free_to_go(self):
        return self.step != self.depth or self.layer in self.env["summed"]

    @property
    def done(self):
        return self.step >= len(self.steps)

    def advance(self):
        self.sent = []
        self.steps[self.step]()
        self.step += 1
        return self.sent

    def remote(self, i, src, dst, slot, where, recv=None):
        sems = (self.layer, self.index, i, slot)
        return pltpu.make_async_remote_copy(
            src_ref=src, dst_ref=dst, send_sem=self.env["ar_send"].at[sems],
            recv_sem=self.env["ar_recv"].at[sems] if recv is None else recv, device_id=where, device_id_type=MESH,
        )

    def wait(self):
        for made, came in self.waits:
            made.wait_send()
            came.wait_recv()
        self.waits = []

    def came_at(self, i, k):
        row = sum(r[1] for r in self.regions[i][1 : k + 1])
        _, rows, _, lanes = self.regions[i][k + 1]
        return row, rows, i * QUART, lanes

    def scatter(self, k):
        if k > 0:
            self.wait()
            self.add(k - 1)
        for i, order in enumerate(self.orders):
            self.scatter_part(i, k, order[k])

    def start_part(self, i):
        self.sent = []
        self.scatter_part(i, 0, self.orders[i][0])
        if i == 1:
            self.step = 1
        return self.sent

    def scatter_part(self, i, k, axis):
        row, rows, lane, lanes = self.regions[i][k]
        _, rows2, _, lanes2 = self.regions[i][k + 1]
        give_row = row + (1 - axis["bit"]) * rows2 if rows2 < rows else row
        give_lane = lane if rows2 < rows else lane + (1 - axis["bit"]) * lanes2
        src = self.block.at[pl.ds(aligned(give_row, 16), rows2), pl.ds(aligned(give_lane, 128), lanes2)]
        at, n, at_lane, n_lanes = self.came_at(i, k)
        dst = self.space.at[pl.ds(at, n), pl.ds(at_lane, n_lanes)]
        made = self.remote(i, src, dst, k, axis["partner"])
        made.start()
        self.waits.append((made, made))
        self.sent.append((axis["link"], rows2 * lanes2 * 2))

    def add(self, k, last=False):
        rows = self.regions[0][k + 1][1]
        size = min(rows, 32)
        out = []
        for i in range(2):
            row, _, lane, lanes = self.regions[i][k + 1]
            at, _, at_lane, _ = self.came_at(i, k)
            lane = aligned(lane, 128)
            extra = None
            if last:
                part = self.index // 2
                first = aligned((self.index % 2) * HALF + lane, 128)
                extra = self.env["vtot"][self.layer, part : part + 1, pl.ds(first, lanes)]
            out.append((row, lane, lanes, at, at_lane, self.local(i, k + 1)[0], extra))

        def body(j, _):
            for row, lane, lanes, at, at_lane, home, extra in out:
                here = pl.ds(aligned(row + j * size, 16), size)
                total = self.block[here, pl.ds(lane, lanes)].astype(F32)
                total = total + self.space[pl.ds(aligned(at + j * size, 16), size), pl.ds(at_lane, lanes)].astype(F32)
                if last:
                    column = self.env["column"][self.layer, here, :].astype(F32)
                    total = total + wide(column, lanes // 128) * extra
                    to = pl.ds(aligned(home + j * size, 16), size)
                    self.space[to, pl.ds(lane, lanes)] = total.astype(BF16)
                else:
                    self.block[here, pl.ds(lane, lanes)] = total.astype(BF16)
            return 0

        lax.fori_loop(0, rows // size, body, 0)

    def local(self, i, k):
        row, rows, lane, lanes = self.regions[i][k]
        return row - self.regions[i][1][0], rows, lane, lanes

    def gather(self, k):
        self.wait()
        if k == self.depth - 1:
            self.add(k, last=True)
        for i, order in enumerate(self.orders):
            axis = order[k]
            row, rows, lane, lanes = self.local(i, k + 1)
            row0, rows0, lane0, lanes0 = self.local(i, k)
            if rows0 > rows:
                far = (row0 + (1 - axis["bit"]) * rows, rows, lane, lanes)
            else:
                far = (row, rows, lane0 + (1 - axis["bit"]) * lanes, lanes)
            refs = [
                self.space.at[pl.ds(aligned(r, 16), n), pl.ds(aligned(c, 128), w)]
                for r, n, c, w in ((row, rows, lane, lanes), far)
            ]
            made = self.remote(i, refs[0], refs[0], self.depth + k, axis["partner"])
            made.start()
            self.waits.append((made, self.remote(i, refs[1], refs[1], self.depth + k, axis["partner"])))
            self.sent.append((axis["link"], rows * lanes * 2))

    def result(self, i, bit, section):
        rows = self.regions[i][1][1]
        lane = aligned(self.lane_of(section) + i * QUART, QUART)
        return self.env["o"].at[section, pl.ds(aligned(bit * rows, 16), rows), pl.ds(lane, QUART)]

    def gathered(self, i):
        return self.space.at[pl.ds(0, self.regions[i][1][1]), pl.ds(i * QUART, QUART)]

    def deliver(self, i, near, straight):
        axis, section = self.orders[i][0], self.env["section"]
        slot = 2 * self.depth + (0 if near else 1)
        recv = None if straight else self.env["ar_other"].at[self.layer, self.index, i, 0 if near else 1]
        where = dict(self.env["here"] if near else axis["partner"], section=self.layer)
        return self.remote(i, self.gathered(i), self.result(i, axis["bit"], section), slot, where, recv)

    def arrival(self, i, near, straight):
        axis, section = self.orders[i][0], self.env["section"]
        slot = 2 * self.depth + (0 if near else 1)
        recv = None if straight else self.env["ar_other"].at[self.layer, self.index, i, 0 if near else 1]
        bit = axis["bit"] if near else 1 - axis["bit"]
        frm = section if straight else 1 - section
        where = dict(self.env["here"] if near else axis["partner"], section=frm)
        return self.remote(i, self.gathered(i), self.result(i, bit, frm), slot, where, recv)

    def kept(self, i):
        sem = self.env["ar_recv"].at[self.layer, self.index, i, 2 * self.depth]
        return pltpu.make_async_copy(
            self.gathered(i), self.result(i, self.orders[i][0]["bit"], self.env["section"]), sem
        )

    def give(self):
        self.wait()

        @pl.when(self.env["section"] == self.layer)
        def _():
            for i in range(2):
                self.deliver(i, False, True).start()
                self.kept(i).start()

        @pl.when(self.env["section"] != self.layer)
        def _():
            for i in range(2):
                self.deliver(i, False, False).start()
                self.deliver(i, True, False).start()

        for i, order in enumerate(self.orders):
            self.sent.append((order[0]["link"], self.regions[i][1][1] * QUART * 2))

    def finish(self):
        @pl.when(self.env["section"] == self.layer)
        def _():
            for i in range(2):
                self.kept(i).wait()
                self.deliver(i, False, True).wait_send()
                self.arrival(i, False, True).wait_recv()
                self.arrival(i, True, False).wait_recv()
                self.arrival(i, False, False).wait_recv()

        @pl.when(self.env["section"] != self.layer)
        def _():
            for i in range(2):
                self.deliver(i, False, False).wait_send()
                self.deliver(i, True, False).wait_send()


class Order:
    RATE, HOP = 50e3, 1.8

    def __init__(self):
        self.now = 0.0
        self.free = {}
        self.going = []

    def sent(self, copies):
        end = self.now
        for link, size in copies:
            self.free[link] = max(self.now, self.free.get(link, 0.0)) + size / self.RATE
            end = max(end, self.free[link])
        return end + self.HOP

    def begin(self, one, i):
        end = self.sent(one.start_part(i))
        if i == 0:
            one.due = end
        else:
            one.due = max(one.due, end)
            self.going.append(one)

    def advance(self, one):
        self.now = max(self.now, one.due) + 0.4
        one.due = self.sent(one.advance())
        if one.done:
            self.going.remove(one)

    def work(self, cost):
        self.now += cost
        while True:
            due = [x for x in self.going if x.due <= self.now and x.free_to_go]
            if not due:
                return
            self.advance(min(due, key=lambda x: x.due))

    def drain(self):
        while self.going:
            self.advance(min(self.going, key=lambda x: x.due))


def kernel(dims, steps, seqs, views, frames, grad_out, weights, gains, shifts, recurs, lengths, masks, o, gf, vectors, f_own, f_far, p_own, p_far, g3, wc, wr1, src_t, live, turn,
           staged, heads, tails, v, vecs, rows, hid, coef, tot, vtot, levels, column, counts, cnt_p, cnt_z, slim_p, slim_z,
           wide_p, wide_z, space, sems, v_sems, stage_sem, credit, pl_send, pl_recv, z_send, z_recv, ar_send, ar_recv,
           ar_other):
    nz, ny, nx = dims
    np_ = ny * nx
    span = steps * seqs
    total_rows = 2 * span
    sent_rows = total_rows + 16
    pairs = steps // 2
    section = lax.axis_index("section")
    other = 1 - section
    b = lax.axis_index("batch")
    mp = lax.rem(b, np_)
    mz = b // np_

    def at_plane(i):
        return {"batch": b - mp + i}

    def at_z(i):
        return {"batch": b + (i - mz) * np_}

    bits = []
    for link, count, stride in (("x", nx, 1), ("y", ny, nx), ("z", nz, np_)):
        while count > 1:
            bit = lax.rem(b // stride, 2)
            bits.append(dict(bit=bit, partner={"batch": b + (1 - 2 * bit) * stride}, link=link))
            count //= 2
            stride *= 2
    sibling = {"section": other}

    def local(src, dst, slot):
        return pltpu.make_async_copy(src, dst, sems.at[0, slot])

    def across(src, dst, slot):
        return pltpu.make_async_remote_copy(
            src_ref=src, dst_ref=dst, send_sem=sems.at[1, slot], recv_sem=sems.at[2, slot],
            device_id=sibling, device_id_type=MESH,
        )

    half = frames.shape[3]
    width = 2 * half
    lead = W - half
    rest = width - W
    full = rest // 128 * 128

    def fetch(source, m):
        return pltpu.make_async_copy(source.at[m], staged.at[m], stage_sem.at[m])

    def by_units(source, target, m):
        fetch(source, m).wait()

        @pl.when(section == 0)
        def _():
            def place(i, _):
                x = staged[m, pl.ds(2 * i, 2)].astype(F32).reshape(2 * seqs, half)
                head = heads[m, pl.ds(2 * i, 2)].astype(F32).reshape(2 * seqs, 128)
                to = pl.ds(aligned(m * span + 2 * i * seqs, 16), 2 * seqs)
                target[to, :] = jnp.concatenate([x, head[:, :lead]], axis=1).astype(BF16)
                return 0

            lax.fori_loop(0, pairs, place, 0)

        @pl.when(section == 1)
        def _():
            pad = jnp.zeros((2 * seqs, 2 * lead), F32)

            def place(i, _):
                x = staged[m, pl.ds(2 * i, 2)].astype(F32).reshape(2 * seqs, half)
                to = pl.ds(aligned(m * span + 2 * i * seqs, 16), 2 * seqs)
                target[to, :] = jnp.concatenate([x[:, lead:], pad], axis=1).astype(BF16)
                return 0

            lax.fori_loop(0, pairs, place, 0)

    def pieces(row, count, u, block, spot):
        r = pl.ds(row, count)
        to = pl.ds(0, count)
        if u == 0:
            return [(weights.at[0, r, pl.ds(0, W)], block.at[to, :])]
        return [
            (weights.at[0, r, pl.ds(W, full)], block.at[to, pl.ds(0, full)]),
            (weights.at[0, r, pl.ds(W + full, rest - full)], tails.at[spot, to, :]),
        ]

    rows_of = {0: (0, W), 1: (W, rest)}

    def w_plan(layer):
        mine, far = rows_of[layer], rows_of[1 - layer]
        plan = [
            (mine, layer, far, 1 - layer, wc.at[layer, 0], 2 * layer),
            (far, layer, mine, 1 - layer, wc.at[layer, 1], 2 * layer + 1),
        ]
        if layer == 1:
            plan.append((mine, 0, far, 1, wr1, 4))
        return plan

    late_row = (width - half) // 16 * 16
    late_shift = half - late_row
    late_plan = [
        ((0, W), 0, (late_row, width - late_row), 1, wc.at[0, 0], 0),
        ((0, W), 1, (late_row, width - late_row), 0, wc.at[0, 1], 1),
    ]
    slot_of = {0: 4, 1: 8, 2: 14}

    def local_w(plan, base, which):
        r, u, _, _, block, spot = plan[which]
        return [local(a, t, base + 2 * which + i) for i, (a, t) in enumerate(pieces(*r, u, block, spot))]

    def across_w(plan, base, which):
        _, _, r, u, block, spot = plan[which]
        return [across(a, t, base + 2 * which + i) for i, (a, t) in enumerate(pieces(*r, u, block, spot))]

    def start_local_w(layer, plan, base):
        @pl.when(section == layer)
        def _():
            for which in range(len(plan)):
                for made in local_w(plan, base, which):
                    made.start()

    def start_across_w(layer, plan, base):
        @pl.when(section == layer)
        def _():
            for which in range(len(plan)):
                for made in across_w(plan, base, which):
                    made.start()

    def last_units(block, spot):
        def body(i, _):
            r = pl.ds(aligned(i * 128, 128), 128)
            x = tails[spot, r, :].astype(F32)
            x = jnp.concatenate([x, jnp.zeros((128, 128 - x.shape[1]), F32)], axis=1)
            block[r, full:] = x.astype(BF16)
            return 0

        lax.fori_loop(0, W // 128, body, 0)

    def wait_w(layer, plan, base, which):
        _, own_u, _, far_u, block, spot = plan[which]

        @pl.when(section == layer)
        def _():
            for made in local_w(plan, base, which):
                made.wait()
            if own_u == 1:
                last_units(block, spot)

        @pl.when(section != layer)
        def _():
            for made in across_w(plan, base, which):
                made.wait_recv()
            if far_u == 1:
                last_units(block, spot)

    def done_w(layer, plan, base):
        @pl.when(section == layer)
        def _():
            for which in range(len(plan)):
                for made in across_w(plan, base, which):
                    made.wait_send()

    def heads_copy(source, slot):
        return across(source.at[:, :, :, pl.ds(0, 128)], heads, slot)

    def wait_heads(source, slot):
        @pl.when(section == 0)
        def _():
            heads_copy(source, slot).wait_recv()

        @pl.when(section == 1)
        def _():
            heads_copy(source, slot).wait_send()

    fetch(frames, 0).start()
    fetch(frames, 1).start()
    for layer in range(2):
        start_local_w(layer, w_plan(layer), slot_of[layer])

    barrier = pltpu.get_barrier_semaphore()
    greeted = [dict(sibling)]
    greeted += [at_plane(lax.rem(mp + k, np_)) for k in range(1, np_)]
    greeted += [at_z(lax.rem(mz + k, nz)) for k in range(1, nz)]
    greeted += [dict(axis["partner"], section=other) for axis in bits]
    for where in greeted:
        pl.semaphore_signal(barrier, inc=1, device_id=where, device_id_type=MESH)

    for k, (x, fill) in enumerate(((gains, 0.0), (shifts, -1e30), (recurs, 0.0))):
        vecs[section, k : k + 1, 0:width] = x[...]
        vecs[section, k : k + 1, width:] = jnp.full((1, 2 * W - width), fill, F32)
    vecs[section, 3:8, :] = jnp.zeros((5, 2 * W), F32)

    gap = jnp.zeros((W - rest, W), BF16)

    @pl.when(section == 0)
    def _():
        wc[0, 1, rest:, :] = gap
        wc[1, 1, rest:, :] = gap

    @pl.when(section == 1)
    def _():
        wc[0, 0, rest:, :] = gap
        wc[1, 0, rest:, :] = gap
        wr1[rest:, :] = gap

    for spot in (0, 2):
        tails[spot, rest:, :] = jnp.zeros((W - rest, rest - full), BF16)
    for spare in (f_own, p_own, g3.at[0], g3.at[1]):
        spare[sent_rows:, :] = jnp.zeros((spare.shape[0] - sent_rows, W), BF16)

    pl.semaphore_wait(barrier, len(greeted))

    @pl.when(section == 1)
    def _():
        heads_copy(frames, 1).start()

    for layer in range(2):
        start_across_w(layer, w_plan(layer), slot_of[layer])
    send_vec = across(vecs.at[section], vecs.at[section], 3)
    send_vec.start()

    def stage_copy(where, rnd, slot, k, back):
        buf, parity, size, me, at, send, recv = where
        there = at(lax.rem(me + (size - k if back else k), size))
        ref = buf.at[parity, slot]
        return pltpu.make_async_remote_copy(
            src_ref=ref, dst_ref=ref, send_sem=send.at[rnd, k], recv_sem=recv.at[rnd, k],
            device_id=there, device_id_type=MESH,
        )

    def in_plane(buf, parity):
        return (buf, parity, np_, mp, at_plane, pl_send, pl_recv)

    def in_line(buf, parity):
        return (buf, parity, nz, mz, at_z, z_send, z_recv)

    def stage_start(where, rnd, value):
        buf, parity, size, me = where[:4]
        buf[parity, me] = value
        for k in range(1, size):
            stage_copy(where, rnd, me, k, False).start()

    def stage_wait(where, rnd):
        size, me = where[2:4]
        for k in range(1, size):
            stage_copy(where, rnd, me, k, False).wait_send()
            stage_copy(where, rnd, lax.rem(me + size - k, size), k, True).wait_recv()

    def add_slots(where):
        buf, parity, size = where[:3]
        total = buf[parity, 0]
        for k in range(1, size):
            total = total + buf[parity, k]
        return total

    groups = lengths.shape[1]
    s_at = lax.broadcasted_iota(jnp.int32, (seqs, groups), 0)
    g_at = lax.broadcasted_iota(jnp.int32, (seqs, groups), 1) * views
    there = (s_at >= g_at) & (s_at < g_at + views)
    position = lax.broadcasted_iota(jnp.int32, (seqs, 128), 1)
    local_counts = []
    for m in range(2):
        turn[...] = jnp.zeros_like(turn)
        turn[0:steps, 0:seqs] = masks[m].astype(F32)
        mask = turn[...].T[0:seqs]
        length = jnp.broadcast_to(lengths[m : m + 1, :], (seqs, groups)).astype(F32)
        limit = jnp.sum(jnp.where(there, length, 0.0), axis=1, keepdims=True)
        alive = (position.astype(F32) < limit) & ((mask > 0.0) | (position == 0))
        alive = jnp.where(position < steps, alive.astype(F32), 0.0)
        total = jnp.zeros((seqs, 128), F32)
        for t in range(steps):
            at = m * span + t * seqs
            cells = jnp.broadcast_to(alive[:, t : t + 1], (seqs, 128))
            live[at : at + seqs, :] = cells
            total = total + cells
        local_counts.append(jnp.sum(total, axis=0, keepdims=True))
    n_own = jnp.concatenate(local_counts * 4, axis=0)

    cnt_plane, cnt_line = in_plane(cnt_p, 0), in_line(cnt_z, 0)
    stage_start(cnt_plane, 0, n_own)

    def vec_of(layer, k):
        return vecs[layer, k : k + 1, pl.ds(aligned(section * W, W), W)]

    def matmul_to(out, a, w, first, m):
        r = pl.ds(m * span, span)

        def body(i, _):
            c = pl.ds(aligned(i * HALF, HALF), HALF)
            y = dot(a[r, :], w[:, c], ((1,), (0,)))
            out[r, c] = y if first else out[r, c] + y
            return 0

        lax.fori_loop(0, 2, body, 0)

    def packed(pair_a, pair_b):
        a = jnp.concatenate(pair_a, axis=0)
        c = jnp.concatenate(pair_b, axis=0)
        return jnp.concatenate([a[:, :HALF], a[:, HALF:], c[:, :HALF], c[:, HALF:]], axis=0)

    def unpacked(x):
        return jnp.concatenate([x[0:2], x[2:4]], axis=1)

    def merge_slots(where, counts_of):
        buf, parity, size = where[:3]
        s = [buf[parity, k, 0:4, :] for k in range(size)]
        q = [buf[parity, k, 4:8, :] for k in range(size)]
        n = [wide(counts_of(k)[0:4], 4) for k in range(size)]
        total, squares, count = sum(s[1:], s[0]), sum(q[1:], q[0]), sum(n[1:], n[0])
        mean = total / count
        for k in range(size):
            d = s[k] / n[k] - mean
            squares = squares + n[k] * d * d
        return jnp.concatenate([total, squares], axis=0)

    def forward_stats(layer, fill_plane, fill_line):
        sums, squares = [], []
        for m in range(2):
            start = jnp.sum(rows[layer, m * span : m * span + seqs, :], axis=0, keepdims=True) * (1.0 / seqs)

            def body(i, carry):
                s, q = carry
                r = pl.ds(aligned(m * span + i * (2 * seqs), 16), 2 * seqs)
                d = rows[layer, r, :] - start
                kept = wide(live[r, :], 8) * d
                return s + fold(kept), q + fold(kept * d)

            zero = jnp.zeros((8, W), F32)
            s, q = lax.fori_loop(0, pairs, body, (zero, zero))
            s, q = jnp.sum(s, axis=0, keepdims=True), jnp.sum(q, axis=0, keepdims=True)
            n = wide(local_counts[m], 8)
            sums.append(s + n * start)
            squares.append(jnp.maximum(q - s * s / n, 0.0))
        plane, line = in_plane(slim_p, layer), in_line(slim_z, layer)
        stage_start(plane, 1 + layer, packed(sums, squares))
        fill_plane()
        stage_wait(plane, 1 + layer)
        stage_start(line, 1 + layer, merge_slots(plane, lambda k: cnt_p[0, k]))
        fill_line()
        stage_wait(line, 1 + layer)
        value = merge_slots(line, lambda k: cnt_z[0, k])
        total, squares = unpacked(value[0:4]), unpacked(value[4:8])
        for m in range(2):
            count = wide(counts[m : m + 1, :], 8)
            coef[layer, 2 * m : 2 * m + 1, :] = total[m : m + 1] / count
            coef[layer, 2 * m + 1 : 2 * m + 2, :] = lax.rsqrt(squares[m : m + 1] / count + EPS)

    def forward_scan(layer, passes):
        gain, shift, recur = vec_of(layer, 0), vec_of(layer, 1), vec_of(layer, 2)
        sends = []
        for lh in range(2):
            lanes = slice(lh * HALF, (lh + 1) * HALF)
            a, c = [], []
            for m in range(2):
                mean = coef[layer, 2 * m : 2 * m + 1, lanes]
                a.append(gain[:, lanes] * coef[layer, 2 * m + 1 : 2 * m + 2, lanes])
                c.append((shift[:, lanes], mean))
            rec = recur[:, lanes]

            def body(i, carry):
                states, level = carry
                out = []
                for m in range(2):
                    r = pl.ds(aligned(m * span + i * (2 * seqs), 16), 2 * seqs)
                    x = (rows[layer, r, lanes] - c[m][1]) * a[m] + c[m][0]
                    lv = wide(live[r, :], 4)
                    alive = lv > 0.0
                    h = states[m]
                    both = []
                    for k in range(2):
                        part = slice(k * seqs, (k + 1) * seqs)
                        z = x[part] + rec * h
                        soft = jnp.maximum(z, 0.0) + jnp.log(1.0 + jnp.exp(-jnp.abs(z)))
                        h = jnp.where(alive[part], soft, h)
                        both.append(h)
                    two = jnp.concatenate(both, axis=0)
                    hid[layer, r, lanes] = two
                    if passes:
                        p_own[r, lanes] = two.astype(BF16)
                        level = level + fold(lv * two)
                    out.append(h)
                return tuple(out), level

            zero = jnp.zeros((seqs, HALF), F32)
            _, level = lax.fori_loop(0, pairs, body, ((zero, zero), jnp.zeros((8, HALF), F32)))
            if passes:
                levels[1:2, lanes] = jnp.sum(level, axis=0, keepdims=True)
                made = across(p_own.at[pl.ds(0, total_rows), lanes], p_far.at[:, lanes], 18 + lh)
                made.start()
                sends.append(made)
        return sends

    def backward_scan(layer, above, between=lambda: None):
        gain, shift, recur = vec_of(layer, 0), vec_of(layer, 1), vec_of(layer, 2)
        for lq in range(4):
            lanes = slice(lq * QUART, (lq + 1) * QUART)
            gq, sq, rec = gain[:, lanes], shift[:, lanes], recur[:, lanes]
            mean = [coef[layer, 2 * m : 2 * m + 1, lanes] for m in range(2)]
            scale = [coef[layer, 2 * m + 1 : 2 * m + 2, lanes] for m in range(2)]

            def body(i, carry):
                down, s1, s2, rsum, sqh, sqa = carry
                down, s1, s2 = list(down), list(s1), list(s2)
                i = pairs - 1 - i
                for m in range(2):
                    start = m * span + i * (2 * seqs)
                    r = pl.ds(aligned(start, 16), 2 * seqs)
                    before = pl.ds(aligned(jnp.maximum(start - seqs, 0), 8), seqs)
                    normed = (rows[layer, r, lanes] - mean[m]) * scale[m]
                    drive = gq * normed + sq
                    h2 = hid[layer, r, lanes]
                    hb = jnp.where(i > 0, hid[layer, before, lanes], 0.0)
                    lv = wide(live[r, :], 2)
                    up = above[r, lanes].astype(F32)
                    res = f_own[r, lanes].astype(F32)
                    aux = res + h2 if layer == 1 else res
                    sqh = sqh + fold(lv * (h2 * h2))
                    sqa = sqa + fold(lv * (aux * aux))
                    grads = [None, None]
                    for k in (1, 0):
                        part = slice(k * seqs, (k + 1) * seqs)
                        prior = h2[0:seqs] if k == 1 else hb
                        slope = 0.5 + 0.5 * jnp.tanh(0.5 * (drive[part] + rec * prior))
                        total = up[part] + down[m]
                        gd = lv[part] * slope * total
                        down[m] = (1.0 - lv[part]) * total + rec * gd
                        grads[k] = gd
                        rsum = rsum + fold(gd * prior)
                    gd2 = jnp.concatenate(grads, axis=0)
                    hid[layer, r, lanes] = gd2
                    s1[m] = s1[m] + fold(gd2)
                    s2[m] = s2[m] + fold(gd2 * normed)
                return tuple(down), tuple(s1), tuple(s2), rsum, sqh, sqa

            zero = jnp.zeros((seqs, QUART), F32)
            z8 = jnp.zeros((8, QUART), F32)
            _, s1, s2, rsum, sqh, sqa = lax.fori_loop(
                0, pairs, body, ((zero, zero), (z8, z8), (z8, z8), z8, z8, z8)
            )
            for k, x in enumerate((s1[0], s1[1], s2[0], s2[1], rsum, sqh, sqa)):
                tot[layer, k : k + 1, lanes] = jnp.sum(x, axis=0, keepdims=True)
            between()

    def backward_stats(layer, fill_plane, fill_line):
        rnd = 4 if layer == 1 else 3
        plane, line = in_plane(slim_p, 1 - layer), in_line(slim_z, 1 - layer)
        t = tot[layer]
        stage_start(plane, rnd, packed([t[0:1], t[1:2]], [t[2:3], t[3:4]]))
        fill_plane()
        stage_wait(plane, rnd)
        stage_start(line, rnd, add_slots(plane))
        fill_line()
        stage_wait(line, rnd)
        value = add_slots(line)
        tot[layer, 0:2, :] = unpacked(value[0:4])
        tot[layer, 2:4, :] = unpacked(value[4:8])

    def grad_rows(layer, slot):
        gain = vec_of(layer, 0)
        sends = []
        for lh in range(2):
            lanes = slice(lh * HALF, (lh + 1) * HALF)
            acc = jnp.zeros((8, HALF), F32)
            for m in range(2):
                mean = coef[layer, 2 * m : 2 * m + 1, lanes]
                scale = coef[layer, 2 * m + 1 : 2 * m + 2, lanes]
                count = wide(counts[m : m + 1, :], 4)
                first = tot[layer, m : m + 1, lanes] / count
                second = tot[layer, 2 + m : 3 + m, lanes] / count * scale
                k = scale * gain[:, lanes]

                def body(i, acc):
                    r = pl.ds(aligned(m * span + i * (2 * seqs), 16), 2 * seqs)
                    y = hid[layer, r, lanes] - first - (rows[layer, r, lanes] - mean) * second
                    y = wide(live[r, :], 4) * (k * y)
                    g3[0, r, lanes] = y.astype(BF16)
                    return acc + fold(y)

                acc = lax.fori_loop(0, pairs, body, acc)
            top = lax.broadcasted_iota(jnp.int32, (16, HALF), 0) == 0
            minus = jnp.where(top, -jnp.sum(acc, axis=0, keepdims=True), 0.0)
            g3[0, total_rows:sent_rows, lanes] = minus.astype(BF16)
            made = across(g3.at[0, pl.ds(0, sent_rows), lanes], g3.at[1, pl.ds(0, sent_rows), lanes], slot + lh)
            made.start()
            sends.append(made)
        return sends

    sums_round = {1: (1, 6), 0: (0, 7)}

    def sums_start(layer):
        parity, rnd = sums_round[layer]
        own_sum = -g3[0, total_rows:sent_rows, :].astype(F32)[0:1]
        far_sum = -g3[1, total_rows:sent_rows, :].astype(F32)[0:1]
        value = jnp.concatenate([own_sum, far_sum, tot[layer, 4:7, :], jnp.zeros((3, W), F32)], axis=0)
        stage_start(in_plane(wide_p, parity), rnd, value)

    def sums_middle(layer):
        parity, rnd = sums_round[layer]
        stage_wait(in_plane(wide_p, parity), rnd)
        stage_start(in_line(wide_z, parity), rnd, add_slots(in_plane(wide_p, parity)))

    def sums_end(layer):
        parity, rnd = sums_round[layer]
        stage_wait(in_line(wide_z, parity), rnd)
        vtot[layer] = add_slots(in_line(wide_z, parity))
        tot[layer, 4:7, :] = vtot[layer, 2:5, :]
        tot[layer, 7:8, :] = wide(counts[0:1, :] + counts[1:2, :], 8)
        env["summed"].add(layer)

        @pl.when(section == layer)
        def _():
            pltpu.make_async_copy(tot.at[layer], v.at[section], v_sems.at[0]).start()

        @pl.when(section != layer)
        def _():
            v_across(layer).start()

    def v_across(layer):
        return pltpu.make_async_remote_copy(
            src_ref=tot.at[layer], dst_ref=v.at[section], send_sem=v_sems.at[1], recv_sem=v_sems.at[2],
            device_id=sibling, device_id_type=MESH,
        )

    def transpose(src):
        def body(j, _):
            c = pl.ds(aligned(j * 128, 128), 128)
            src_t[c, 0:total_rows] = src[0:total_rows, c].T
            return 0

        lax.fori_loop(0, W // 128, body, 0)

    def transpose_level(src, layer):
        top = lax.broadcasted_iota(jnp.int32, (16, W), 0) == 0
        src[total_rows:sent_rows, :] = jnp.where(top, levels[2 + layer : 3 + layer, :], 0.0).astype(BF16)

        def body(j, _):
            c = pl.ds(aligned(j * 128, 128), 128)
            src_t[c, total_rows:] = src[total_rows:, c].T
            level = src[total_rows:sent_rows, c].astype(F32)[0:1]
            column[layer, c, :] = jnp.broadcast_to(level, (128, 128)).T.astype(BF16)
            return 0

        lax.fori_loop(0, W // 128, body, 0)

    def weight_part(block, grads, c):
        lanes = pl.ds(c * QUART, QUART)

        def body(j, _):
            r = pl.ds(aligned(j * HALF, HALF), HALF)
            block[r, lanes] = dot(src_t[r, :], grads[:, lanes], ((1,), (0,))).astype(BF16)
            return 0

        lax.fori_loop(0, W // HALF, body, 0)

    def source_grad(store, w_own, w_far, between):
        for m in range(2):
            r = pl.ds(m * span, span)

            def body(i, _):
                c = pl.ds(aligned(i * HALF, HALF), HALF)
                y = dot(g3[0, r, :], w_own[c, :], ((1,), (1,))) + dot(g3[1, r, :], w_far[c, :], ((1,), (1,)))
                store(r, c, y)
                return 0

            lax.fori_loop(0, 2, body, 0)
            between()

    env = dict(summed=set(), vtot=vtot, column=column, space=space, ar_send=ar_send, ar_recv=ar_recv,
               ar_other=ar_other, o=o, section=section, here={"batch": b})
    xs = [a for a in bits if a["link"] == "x"]
    ys = [a for a in bits if a["link"] == "y"]
    zs = [a for a in bits if a["link"] == "z"]
    orders = (xs + ys + zs, ys + xs + zs)
    blocks = {
        (1, 0): f_far.at[pl.ds(0, W), :],
        (1, 1): p_far.at[pl.ds(0, W), :],
        (0, 0): wc.at[1, 1],
        (0, 1): wr1,
    }
    parts = {}
    for layer in (1, 0):
        for index in range(4):
            part, side = index // 2, index % 2

            def lane_of(sec, part=part, side=side):
                return (sec if part == 0 else 1 - sec) * W + side * HALF

            block = blocks[layer, part].at[:, pl.ds(side * HALF, HALF)]
            parts[layer, index] = Reduction(env, layer, index, block, orders, lane_of)
    order = Order()

    def weight_grads(layer, between):
        for part in range(2):
            if part == 1:
                between()
            for c in range(4):
                weight_part(blocks[layer, part], g3.at[part], c)
                order.work(0.9)
                order.begin(parts[layer, 2 * part + c // 2], c % 2)

    def arrived(layer, sends):
        for made in sends:
            made.wait()
        sums_start(layer)

    nothing = lambda: None

    wait_heads(frames, 1)
    send_f = []
    for m in range(2):
        by_units(frames, f_own, m)
        here = pl.ds(m * span, span)
        made = across(f_own.at[here, :], f_far.at[here, :], (0, 24)[m])
        made.start()
        send_f.append(made)
    wait_w(0, w_plan(0), slot_of[0], 0)
    for m in range(2):
        matmul_to(rows.at[0], f_own, wc.at[0, 0], True, m)
    wait_w(0, w_plan(0), slot_of[0], 1)
    for m in range(2):
        send_f[m].wait()
        matmul_to(rows.at[0], f_far, wc.at[0, 1], False, m)
    fetch(grad_out, 0).start()
    fetch(grad_out, 1).start()
    stage_wait(cnt_plane, 0)
    stage_start(cnt_line, 0, add_slots(cnt_plane))
    send_vec.wait_send()
    across(vecs.at[other], vecs.at[other], 3).wait_recv()

    def source_level():
        def body(i, acc):
            r = pl.ds(aligned(i * (2 * seqs), 16), 2 * seqs)
            return acc + fold(wide(live[r, :], 8) * f_own[r, :].astype(F32))

        acc = lax.fori_loop(0, 2 * pairs, body, jnp.zeros((8, W), F32))
        levels[0:1, :] = jnp.sum(acc, axis=0, keepdims=True)

    def counted():
        source_level()
        stage_wait(cnt_line, 0)
        counts[...] = add_slots(cnt_line)

    forward_stats(0, nothing, counted)
    sends = forward_scan(0, True)
    level_plane, level_line = in_plane(wide_p, 0), in_line(wide_z, 0)
    stage_start(level_plane, 5, jnp.concatenate([levels[0:2, :], jnp.zeros((6, W), F32)], axis=0))
    wait_w(1, w_plan(1), slot_of[1], 0)
    for m in range(2):
        matmul_to(rows.at[1], p_own, wc.at[1, 0], True, m)
    wait_w(1, w_plan(1), slot_of[1], 1)
    for made in sends:
        made.wait()
    done_w(0, w_plan(0), slot_of[0])

    start_local_w(0, late_plan, slot_of[2])
    start_across_w(0, late_plan, slot_of[2])

    @pl.when(section == 1)
    def _():
        wc[0, 1, width - late_row :, :] = jnp.zeros((W - width + late_row, W), BF16)
        heads_copy(grad_out, 2).start()

    for m in range(2):
        matmul_to(rows.at[1], p_far, wc.at[1, 1], False, m)
    stage_wait(level_plane, 5)
    stage_start(level_line, 5, add_slots(level_plane))

    def cotangent():
        wait_heads(grad_out, 2)
        for m in range(2):
            by_units(grad_out, f_far, m)

    def levelled():
        stage_wait(level_line, 5)
        value = add_slots(level_line) / wide(counts[0:1, :] + counts[1:2, :], 8)
        levels[2:4, :] = value[0:2]

    forward_stats(1, lambda: transpose(p_own), cotangent)
    forward_scan(1, False)
    levelled()
    backward_scan(1, f_far)
    backward_stats(1, lambda: transpose_level(p_own, 1), nothing)
    sends = grad_rows(1, 20)
    weight_grads(1, lambda: arrived(1, sends))
    wait_w(1, w_plan(1), slot_of[1], 2)
    done_w(1, w_plan(1), slot_of[1])

    def keep_down(r, c, y):
        p_own[r, c] = y.astype(BF16)

    source_grad(keep_down, wc.at[1, 0], wr1, lambda: order.work(3.0))
    pl.semaphore_signal(credit, inc=1, device_id=sibling, device_id_type=MESH)
    sums_middle(1)
    backward_scan(0, p_own, lambda: order.work(1.2))
    sums_end(1)

    def turn_frames():
        transpose(f_own)
        transpose_level(f_own, 0)
        order.work(3.0)

    backward_stats(0, turn_frames, lambda: order.work(3.0))
    pl.semaphore_wait(credit, 1)
    sends = grad_rows(0, 22)
    order.work(2.0)
    weight_grads(0, lambda: arrived(0, sends))
    wait_w(0, late_plan, slot_of[2], 0)
    wait_w(0, late_plan, slot_of[2], 1)
    done_w(0, late_plan, slot_of[2])

    def keep_source(r, c, y):
        rows[0, r, c] = y

    fetch(grad_out, 0).start()
    fetch(grad_out, 1).start()
    sums_middle(0)
    source_grad(keep_source, wc.at[0, 0], wc.at[0, 1], lambda: order.work(3.0))
    sums_end(0)

    def give(m):
        return pltpu.make_async_copy(staged.at[m], gf.at[m], stage_sem.at[m])

    for m in range(2):
        fetch(grad_out, m).wait()

        def finish_frames(i, _, m=m):
            straight = staged[m, pl.ds(2 * i, 2)].astype(F32).reshape(2 * seqs, half)
            y = rows[0, pl.ds(aligned(m * span + 2 * i * seqs, 8), 2 * seqs), :]
            y = jnp.where(section == 0, y[:, :half], y[:, late_shift : late_shift + half])
            staged[m, pl.ds(2 * i, 2)] = (y + straight).reshape(2, seqs, half).astype(BF16)
            return 0

        lax.fori_loop(0, pairs, finish_frames, 0)
        give(m).start()
        order.work(2.0)
    order.drain()
    for m in range(2):
        give(m).wait()

    for layer in range(2):

        @pl.when(section == layer)
        def _(layer=layer):
            pltpu.make_async_copy(tot.at[layer], v.at[section], v_sems.at[0]).wait()
            pltpu.make_async_remote_copy(
                src_ref=tot.at[layer], dst_ref=v.at[other], send_sem=v_sems.at[1], recv_sem=v_sems.at[2],
                device_id=sibling, device_id_type=MESH,
            ).wait_recv()

        @pl.when(section != layer)
        def _(layer=layer):
            v_across(layer).wait_send()

    own_part, far_part = v[section], v[other]
    first = jnp.where(section == 0, own_part, far_part)
    second = jnp.where(section == 0, far_part, own_part)
    for row, terms in ((0, (2, 3)), (1, (0, 1)), (2, (4,))):
        for lane, x in ((0, first), (W, second)):
            total = x[terms[0] : terms[0] + 1, :]
            for k in terms[1:]:
                total = total + x[k : k + 1, :]
            vectors[row : row + 1, lane : lane + W] = total
    squares = jnp.sum(first[5:7, :] + second[5:7, :], axis=1, keepdims=True)
    root = jnp.sqrt(squares / (first[7:8, 0:1] * width))
    for k in range(2):
        vectors[3 + k : 4 + k, :] = jnp.broadcast_to(root[k : k + 1], (1, 2 * W))
    vectors[5:8, :] = jnp.zeros((3, 2 * W), F32)


def write_results(o, gf, vectors, grad_weight, grad_frames, grad_gains, grad_shifts, grad_recurs, table):
    width = grad_weight.shape[2]
    grad_weight[0] = o[...][:, :width].astype(F32)
    grad_frames[...] = gf[...]

    @pl.when(pl.program_id(0) == 0)
    def _():
        for k, out in enumerate((grad_gains, grad_shifts, grad_recurs)):
            out[...] = vectors[k : k + 1, 0:width]
        table[...] = jnp.concatenate([vectors[3:4, 0:1], vectors[4:5, 0:1]], axis=1)


def results(o, gf, vectors):
    micro, steps, seqs, half = gf.shape
    width = 2 * half
    count = W * 2 // 128
    frames = micro * steps // count
    whole = lambda shape: pl.BlockSpec(shape, lambda i: (0, 0))
    out = pl.pallas_call(
        write_results,
        grid=(count,),
        in_specs=[
            pl.BlockSpec((128, 2 * W), lambda i: (i, 0)),
            pl.BlockSpec((frames, seqs, half), lambda i: (i, 0, 0)),
            whole((8, 2 * W)),
        ],
        out_specs=(
            pl.BlockSpec((1, 128, width), lambda i: (0, i, 0)),
            pl.BlockSpec((frames, seqs, half), lambda i: (i, 0, 0)),
            whole((1, width)),
            whole((1, width)),
            whole((1, width)),
            whole((1, 2)),
        ),
        out_shape=(
            jax.ShapeDtypeStruct((1, width, width), F32),
            jax.ShapeDtypeStruct((micro * steps, seqs, half), BF16),
            jax.ShapeDtypeStruct((1, width), F32),
            jax.ShapeDtypeStruct((1, width), F32),
            jax.ShapeDtypeStruct((1, width), F32),
            jax.ShapeDtypeStruct((1, 2), F32),
        ),
        compiler_params=pltpu.CompilerParams(vmem_limit_bytes=32 * 1024 * 1024),
    )(o.reshape(2 * W, 2 * W), gf.reshape(micro * steps, seqs, half), vectors)
    return out[1].reshape(gf.shape), out[0], *out[2:]


def whole_step(dims, frames, grad_out, weights, gains, shifts, recurs, lengths, masks):
    nz, ny, nx = dims
    micro, steps, seqs, half = frames.shape
    width = 2 * half
    views = seqs // lengths.shape[1]
    rows = micro * steps * seqs
    np_ = ny * nx
    wide_rows = (rows + 16 + 127) // 128 * 128
    depth = (nx * ny * nz - 1).bit_length()
    any_ = pl.BlockSpec(memory_space=pl.ANY)
    held = pl.BlockSpec(memory_space=pltpu.VMEM)
    dma = pltpu.SemaphoreType.DMA
    return pl.pallas_call(
        functools.partial(kernel, dims, steps, seqs, views),
        out_shape=(
            jax.ShapeDtypeStruct((2, W, 2 * W), BF16),
            jax.ShapeDtypeStruct(frames.shape, BF16),
            jax.ShapeDtypeStruct((8, 2 * W), F32),
        ),
        in_specs=[any_] * 3 + [held] * 5,
        out_specs=(any_, any_, held),
        scratch_shapes=[
            pltpu.VMEM((wide_rows, W), BF16),
            pltpu.VMEM((rows, W), BF16),
            pltpu.VMEM((wide_rows, W), BF16),
            pltpu.VMEM((rows, W), BF16),
            pltpu.VMEM((2, wide_rows, W), BF16),
            pltpu.VMEM((2, 2, W, W), BF16),
            pltpu.VMEM((W, W), BF16),
            pltpu.VMEM((W, wide_rows), BF16),
            pltpu.VMEM((rows, 128), F32),
            pltpu.VMEM((128, 128), F32),
            pltpu.VMEM(frames.shape, BF16),
            pltpu.VMEM((micro, steps, seqs, 128), BF16),
            pltpu.VMEM((5, W, (width - W) % 128), BF16),
            pltpu.VMEM((2, 8, W), F32),
            pltpu.VMEM((2, 8, 2 * W), F32),
            pltpu.VMEM((2, rows, W), F32),
            pltpu.VMEM((2, rows, W), F32),
            pltpu.VMEM((2, 8, W), F32),
            pltpu.VMEM((2, 8, W), F32),
            pltpu.VMEM((2, 8, W), F32),
            pltpu.VMEM((8, W), F32),
            pltpu.VMEM((2, W, 128), BF16),
            pltpu.VMEM((8, 128), F32),
            pltpu.VMEM((1, np_, 8, 128), F32),
            pltpu.VMEM((1, nz, 8, 128), F32),
            pltpu.VMEM((2, np_, 8, HALF), F32),
            pltpu.VMEM((2, nz, 8, HALF), F32),
            pltpu.VMEM((2, np_, 8, W), F32),
            pltpu.VMEM((2, nz, 8, W), F32),
            pltpu.VMEM((2, 4, W, HALF), BF16),
            dma((3, 25)),
            dma((3,)),
            dma((2,)),
            pltpu.SemaphoreType.REGULAR,
            dma((8, max(np_, 2))),
            dma((8, max(np_, 2))),
            dma((8, max(nz, 2))),
            dma((8, max(nz, 2))),
            dma((2, 4, 2, 2 * depth + 2)),
            dma((2, 4, 2, 2 * depth + 2)),
            dma((2, 4, 2, 2)),
        ],
        compiler_params=pltpu.CompilerParams(
            collective_id=0, has_side_effects=True, vmem_limit_bytes=64 * 1024 * 1024
        ),
    )(frames, grad_out, weights, gains, shifts, recurs, lengths, masks)


def shards(dims, frames, grad_out, weights, gains, shifts, recurs, lengths, masks):
    return results(*whole_step(dims, frames, grad_out, weights, gains, shifts, recurs, lengths, masks))


def solution(mesh):
    in_specs = (
        P(None, None, "batch", "section"),
        P(None, None, "batch", "section"),
        P("section", None, None),
        P("section", None),
        P("section", None),
        P("section", None),
        P(None, "batch"),
        P(None, None, "batch"),
    )
    out_specs = (
        P(None, None, "batch", "section"),
        P("section", None, None),
        P("section", None),
        P("section", None),
        P("section", None),
        P("section", None),
    )
    body = functools.partial(shards, grid_of(mesh.shape["batch"]))
    return jax.shard_map(body, mesh=mesh, in_specs=in_specs, out_specs=out_specs, check_vma=False)
```

```python
import functools

import jax
import jax.numpy as jnp
from jax import lax
from jax.experimental import pallas as pl
from jax.experimental.pallas import tpu as pltpu
from jax.sharding import PartitionSpec as P

EPS = 1e-05
W = 1024
HALF = W // 2
QUART = W // 4
MESH = pl.DeviceIdType.MESH
F32 = jnp.float32
BF16 = jnp.bfloat16


def grid_of(size):
    if size == 16:
        return (4, 2, 2)
    if size == 128:
        return (8, 4, 4)
    return (size, 1, 1)


def aligned(x, k):
    return pl.multiple_of(x, k)


def wide(x, reps):
    return jnp.concatenate([x] * reps, axis=1)


def fold(x):
    rows = x.shape[0]
    total = x[0:8]
    for k in range(8, rows, 8):
        total = total + x[k : k + 8]
    return total


def dot(a, b, dims):
    return lax.dot_general(a, b, (dims, ((), ())), preferred_element_type=F32)


class Reduction:
    def __init__(self, env, layer, index, block, orders, lane_of):
        self.env, self.layer, self.index, self.block, self.orders = env, layer, index, block, orders
        self.lane_of = lane_of
        self.space = env["space"].at[layer, index]
        self.depth = len(orders[0])
        self.regions = [self.halves(i, order) for i, order in enumerate(orders)]
        self.step = 0
        self.waits = []
        depth = self.depth
        self.steps = [functools.partial(self.scatter, 0)]
        self.steps += [functools.partial(self.scatter, k) for k in range(1, depth)]
        self.steps += [functools.partial(self.gather, k) for k in range(depth - 1, 0, -1)]
        self.steps += [self.give, self.finish]

    def halves(self, i, order):
        row, rows, lane, lanes = 0, W, i * QUART, QUART
        out = [(row, rows, lane, lanes)]
        for axis in order:
            if rows > 16:
                rows //= 2
                row = row + axis["bit"] * rows
            else:
                lanes //= 2
                lane = lane + axis["bit"] * lanes
            out.append((row, rows, lane, lanes))
        return out

    @property
    def free_to_go(self):
        return self.step != self.depth or self.layer in self.env["summed"]

    @property
    def done(self):
        return self.step >= len(self.steps)

    def advance(self):
        self.sent = []
        self.steps[self.step]()
        self.step += 1
        return self.sent

    def remote(self, i, src, dst, slot, where, recv=None):
        sems = (self.layer, self.index, i, slot)
        return pltpu.make_async_remote_copy(
            src_ref=src, dst_ref=dst, send_sem=self.env["ar_send"].at[sems],
            recv_sem=self.env["ar_recv"].at[sems] if recv is None else recv, device_id=where, device_id_type=MESH,
        )

    def wait(self):
        for made, came in self.waits:
            made.wait_send()
            came.wait_recv()
        self.waits = []

    def came_at(self, i, k):
        row = sum(r[1] for r in self.regions[i][1 : k + 1])
        _, rows, _, lanes = self.regions[i][k + 1]
        return row, rows, i * QUART, lanes

    def scatter(self, k):
        if k > 0:
            self.wait()
            self.add(k - 1)
        for i, order in enumerate(self.orders):
            self.scatter_part(i, k, order[k])

    def start_part(self, i):
        self.sent = []
        self.scatter_part(i, 0, self.orders[i][0])
        if i == 1:
            self.step = 1
        return self.sent

    def scatter_part(self, i, k, axis):
        row, rows, lane, lanes = self.regions[i][k]
        _, rows2, _, lanes2 = self.regions[i][k + 1]
        give_row = row + (1 - axis["bit"]) * rows2 if rows2 < rows else row
        give_lane = lane if rows2 < rows else lane + (1 - axis["bit"]) * lanes2
        src = self.block.at[pl.ds(aligned(give_row, 16), rows2), pl.ds(aligned(give_lane, 128), lanes2)]
        at, n, at_lane, n_lanes = self.came_at(i, k)
        dst = self.space.at[pl.ds(at, n), pl.ds(at_lane, n_lanes)]
        made = self.remote(i, src, dst, k, axis["partner"])
        made.start()
        self.waits.append((made, made))
        self.sent.append((axis["link"], rows2 * lanes2 * 2))

    def add(self, k, last=False):
        rows = self.regions[0][k + 1][1]
        size = min(rows, 32)
        out = []
        for i in range(2):
            row, _, lane, lanes = self.regions[i][k + 1]
            at, _, at_lane, _ = self.came_at(i, k)
            lane = aligned(lane, 128)
            extra = None
            if last:
                part = self.index // 2
                first = aligned((self.index % 2) * HALF + lane, 128)
                extra = self.env["vtot"][self.layer, part : part + 1, pl.ds(first, lanes)]
            out.append((row, lane, lanes, at, at_lane, self.local(i, k + 1)[0], extra))

        def body(j, _):
            for row, lane, lanes, at, at_lane, home, extra in out:
                here = pl.ds(aligned(row + j * size, 16), size)
                total = self.block[here, pl.ds(lane, lanes)].astype(F32)
                total = total + self.space[pl.ds(aligned(at + j * size, 16), size), pl.ds(at_lane, lanes)].astype(F32)
                if last:
                    column = self.env["column"][self.layer, here, :].astype(F32)
                    total = total + wide(column, lanes // 128) * extra
                    to = pl.ds(aligned(home + j * size, 16), size)
                    self.space[to, pl.ds(lane, lanes)] = total.astype(BF16)
                else:
                    self.block[here, pl.ds(lane, lanes)] = total.astype(BF16)
            return 0

        lax.fori_loop(0, rows // size, body, 0)

    def local(self, i, k):
        row, rows, lane, lanes = self.regions[i][k]
        return row - self.regions[i][1][0], rows, lane, lanes

    def gather(self, k):
        self.wait()
        if k == self.depth - 1:
            self.add(k, last=True)
        for i, order in enumerate(self.orders):
            axis = order[k]
            row, rows, lane, lanes = self.local(i, k + 1)
            row0, rows0, lane0, lanes0 = self.local(i, k)
            if rows0 > rows:
                far = (row0 + (1 - axis["bit"]) * rows, rows, lane, lanes)
            else:
                far = (row, rows, lane0 + (1 - axis["bit"]) * lanes, lanes)
            refs = [
                self.space.at[pl.ds(aligned(r, 16), n), pl.ds(aligned(c, 128), w)]
                for r, n, c, w in ((row, rows, lane, lanes), far)
            ]
            made = self.remote(i, refs[0], refs[0], self.depth + k, axis["partner"])
            made.start()
            self.waits.append((made, self.remote(i, refs[1], refs[1], self.depth + k, axis["partner"])))
            self.sent.append((axis["link"], rows * lanes * 2))

    def result(self, i, bit, section):
        rows = self.regions[i][1][1]
        lane = aligned(self.lane_of(section) + i * QUART, QUART)
        return self.env["o"].at[section, pl.ds(aligned(bit * rows, 16), rows), pl.ds(lane, QUART)]

    def gathered(self, i):
        return self.space.at[pl.ds(0, self.regions[i][1][1]), pl.ds(i * QUART, QUART)]

    def deliver(self, i, near, straight):
        axis, section = self.orders[i][0], self.env["section"]
        slot = 2 * self.depth + (0 if near else 1)
        recv = None if straight else self.env["ar_other"].at[self.layer, self.index, i, 0 if near else 1]
        where = dict(self.env["here"] if near else axis["partner"], section=self.layer)
        return self.remote(i, self.gathered(i), self.result(i, axis["bit"], section), slot, where, recv)

    def arrival(self, i, near, straight):
        axis, section = self.orders[i][0], self.env["section"]
        slot = 2 * self.depth + (0 if near else 1)
        recv = None if straight else self.env["ar_other"].at[self.layer, self.index, i, 0 if near else 1]
        bit = axis["bit"] if near else 1 - axis["bit"]
        frm = section if straight else 1 - section
        where = dict(self.env["here"] if near else axis["partner"], section=frm)
        return self.remote(i, self.gathered(i), self.result(i, bit, frm), slot, where, recv)

    def kept(self, i):
        sem = self.env["ar_recv"].at[self.layer, self.index, i, 2 * self.depth]
        return pltpu.make_async_copy(
            self.gathered(i), self.result(i, self.orders[i][0]["bit"], self.env["section"]), sem
        )

    def give(self):
        self.wait()

        @pl.when(self.env["section"] == self.layer)
        def _():
            for i in range(2):
                self.deliver(i, False, True).start()
                self.kept(i).start()

        @pl.when(self.env["section"] != self.layer)
        def _():
            for i in range(2):
                self.deliver(i, False, False).start()
                self.deliver(i, True, False).start()

        for i, order in enumerate(self.orders):
            self.sent.append((order[0]["link"], self.regions[i][1][1] * QUART * 2))

    def finish(self):
        @pl.when(self.env["section"] == self.layer)
        def _():
            for i in range(2):
                self.kept(i).wait()
                self.deliver(i, False, True).wait_send()
                self.arrival(i, False, True).wait_recv()
                self.arrival(i, True, False).wait_recv()
                self.arrival(i, False, False).wait_recv()

        @pl.when(self.env["section"] != self.layer)
        def _():
            for i in range(2):
                self.deliver(i, False, False).wait_send()
                self.deliver(i, True, False).wait_send()


class Order:
    RATE, HOP = 50e3, 1.8

    def __init__(self):
        self.now = 0.0
        self.free = {}
        self.going = []

    def sent(self, copies):
        end = self.now
        for link, size in copies:
            self.free[link] = max(self.now, self.free.get(link, 0.0)) + size / self.RATE
            end = max(end, self.free[link])
        return end + self.HOP

    def begin(self, one, i):
        end = self.sent(one.start_part(i))
        if i == 0:
            one.due = end
        else:
            one.due = max(one.due, end)
            self.going.append(one)

    def advance(self, one):
        self.now = max(self.now, one.due) + 0.4
        one.due = self.sent(one.advance())
        if one.done:
            self.going.remove(one)

    def work(self, cost):
        self.now += cost
        while True:
            due = [x for x in self.going if x.due <= self.now and x.free_to_go]
            if not due:
                return
            self.advance(min(due, key=lambda x: x.due))

    def drain(self):
        while self.going:
            self.advance(min(self.going, key=lambda x: x.due))


def kernel(dims, steps, seqs, views, frames, grad_out, weights, gains, shifts, recurs, lengths, masks, o, gf, vectors, f_own, f_far, p_own, p_far, g3, wc, wr1, src_t, live, turn,
           staged, heads, tails, v, vecs, rows, hid, coef, tot, vtot, levels, column, counts, cnt_p, cnt_z, slim_p, slim_z,
           wide_p, wide_z, space, sems, v_sems, stage_sem, credit, pl_send, pl_recv, z_send, z_recv, ar_send, ar_recv,
           ar_other):
    nz, ny, nx = dims
    np_ = ny * nx
    span = steps * seqs
    total_rows = 2 * span
    sent_rows = total_rows + 16
    pairs = steps // 2
    section = lax.axis_index("section")
    other = 1 - section
    b = lax.axis_index("batch")
    mp = lax.rem(b, np_)
    mz = b // np_

    def at_plane(i):
        return {"batch": b - mp + i}

    def at_z(i):
        return {"batch": b + (i - mz) * np_}

    bits = []
    for link, count, stride in (("x", nx, 1), ("y", ny, nx), ("z", nz, np_)):
        while count > 1:
            bit = lax.rem(b // stride, 2)
            bits.append(dict(bit=bit, partner={"batch": b + (1 - 2 * bit) * stride}, link=link))
            count //= 2
            stride *= 2
    sibling = {"section": other}

    def local(src, dst, slot):
        return pltpu.make_async_copy(src, dst, sems.at[0, slot])

    def across(src, dst, slot):
        return pltpu.make_async_remote_copy(
            src_ref=src, dst_ref=dst, send_sem=sems.at[1, slot], recv_sem=sems.at[2, slot],
            device_id=sibling, device_id_type=MESH,
        )

    half = frames.shape[3]
    width = 2 * half
    lead = W - half
    rest = width - W
    full = rest // 128 * 128

    def fetch(source, m):
        return pltpu.make_async_copy(source.at[m], staged.at[m], stage_sem.at[m])

    def by_units(source, target, m):
        fetch(source, m).wait()

        @pl.when(section == 0)
        def _():
            def place(i, _):
                x = staged[m, pl.ds(2 * i, 2)].astype(F32).reshape(2 * seqs, half)
                head = heads[m, pl.ds(2 * i, 2)].astype(F32).reshape(2 * seqs, 128)
                to = pl.ds(aligned(m * span + 2 * i * seqs, 16), 2 * seqs)
                target[to, :] = jnp.concatenate([x, head[:, :lead]], axis=1).astype(BF16)
                return 0

            lax.fori_loop(0, pairs, place, 0)

        @pl.when(section == 1)
        def _():
            pad = jnp.zeros((2 * seqs, 2 * lead), F32)

            def place(i, _):
                x = staged[m, pl.ds(2 * i, 2)].astype(F32).reshape(2 * seqs, half)
                to = pl.ds(aligned(m * span + 2 * i * seqs, 16), 2 * seqs)
                target[to, :] = jnp.concatenate([x[:, lead:], pad], axis=1).astype(BF16)
                return 0

            lax.fori_loop(0, pairs, place, 0)

    def pieces(row, count, u, block, spot):
        r = pl.ds(row, count)
        to = pl.ds(0, count)
        if u == 0:
            return [(weights.at[0, r, pl.ds(0, W)], block.at[to, :])]
        return [
            (weights.at[0, r, pl.ds(W, full)], block.at[to, pl.ds(0, full)]),
            (weights.at[0, r, pl.ds(W + full, rest - full)], tails.at[spot, to, :]),
        ]

    rows_of = {0: (0, W), 1: (W, rest)}

    def w_plan(layer):
        mine, far = rows_of[layer], rows_of[1 - layer]
        plan = [
            (mine, layer, far, 1 - layer, wc.at[layer, 0], 2 * layer),
            (far, layer, mine, 1 - layer, wc.at[layer, 1], 2 * layer + 1),
        ]
        if layer == 1:
            plan.append((mine, 0, far, 1, wr1, 4))
        return plan

    late_row = (width - half) // 16 * 16
    late_shift = half - late_row
    late_plan = [
        ((0, W), 0, (late_row, width - late_row), 1, wc.at[0, 0], 0),
        ((0, W), 1, (late_row, width - late_row), 0, wc.at[0, 1], 1),
    ]
    slot_of = {0: 4, 1: 8, 2: 14}

    def local_w(plan, base, which):
        r, u, _, _, block, spot = plan[which]
        return [local(a, t, base + 2 * which + i) for i, (a, t) in enumerate(pieces(*r, u, block, spot))]

    def across_w(plan, base, which):
        _, _, r, u, block, spot = plan[which]
        return [across(a, t, base + 2 * which + i) for i, (a, t) in enumerate(pieces(*r, u, block, spot))]

    def start_local_w(layer, plan, base):
        @pl.when(section == layer)
        def _():
            for which in range(len(plan)):
                for made in local_w(plan, base, which):
                    made.start()

    def start_across_w(layer, plan, base):
        @pl.when(section == layer)
        def _():
            for which in range(len(plan)):
                for made in across_w(plan, base, which):
                    made.start()

    def last_units(block, spot):
        def body(i, _):
            r = pl.ds(aligned(i * 128, 128), 128)
            x = tails[spot, r, :].astype(F32)
            x = jnp.concatenate([x, jnp.zeros((128, 128 - x.shape[1]), F32)], axis=1)
            block[r, full:] = x.astype(BF16)
            return 0

        lax.fori_loop(0, W // 128, body, 0)

    def wait_w(layer, plan, base, which):
        _, own_u, _, far_u, block, spot = plan[which]

        @pl.when(section == layer)
        def _():
            for made in local_w(plan, base, which):
                made.wait()
            if own_u == 1:
                last_units(block, spot)

        @pl.when(section != layer)
        def _():
            for made in across_w(plan, base, which):
                made.wait_recv()
            if far_u == 1:
                last_units(block, spot)

    def done_w(layer, plan, base):
        @pl.when(section == layer)
        def _():
            for which in range(len(plan)):
                for made in across_w(plan, base, which):
                    made.wait_send()

    def heads_copy(source, slot):
        return across(source.at[:, :, :, pl.ds(0, 128)], heads, slot)

    def wait_heads(source, slot):
        @pl.when(section == 0)
        def _():
            heads_copy(source, slot).wait_recv()

        @pl.when(section == 1)
        def _():
            heads_copy(source, slot).wait_send()

    fetch(frames, 0).start()
    fetch(frames, 1).start()
    for layer in range(2):
        start_local_w(layer, w_plan(layer), slot_of[layer])

    barrier = pltpu.get_barrier_semaphore()
    greeted = [dict(sibling)]
    greeted += [at_plane(lax.rem(mp + k, np_)) for k in range(1, np_)]
    greeted += [at_z(lax.rem(mz + k, nz)) for k in range(1, nz)]
    greeted += [dict(axis["partner"], section=other) for axis in bits]
    for where in greeted:
        pl.semaphore_signal(barrier, inc=1, device_id=where, device_id_type=MESH)

    for k, (x, fill) in enumerate(((gains, 0.0), (shifts, -1e30), (recurs, 0.0))):
        vecs[section, k : k + 1, 0:width] = x[...]
        vecs[section, k : k + 1, width:] = jnp.full((1, 2 * W - width), fill, F32)
    vecs[section, 3:8, :] = jnp.zeros((5, 2 * W), F32)

    gap = jnp.zeros((W - rest, W), BF16)

    @pl.when(section == 0)
    def _():
        wc[0, 1, rest:, :] = gap
        wc[1, 1, rest:, :] = gap

    @pl.when(section == 1)
    def _():
        wc[0, 0, rest:, :] = gap
        wc[1, 0, rest:, :] = gap
        wr1[rest:, :] = gap

    for spot in (0, 2):
        tails[spot, rest:, :] = jnp.zeros((W - rest, rest - full), BF16)
    for spare in (f_own, p_own, g3.at[0], g3.at[1]):
        spare[sent_rows:, :] = jnp.zeros((spare.shape[0] - sent_rows, W), BF16)

    pl.semaphore_wait(barrier, len(greeted))

    @pl.when(section == 1)
    def _():
        heads_copy(frames, 1).start()

    for layer in range(2):
        start_across_w(layer, w_plan(layer), slot_of[layer])
    send_vec = across(vecs.at[section], vecs.at[section], 3)
    send_vec.start()

    def stage_copy(where, rnd, slot, k, back):
        buf, parity, size, me, at, send, recv = where
        there = at(lax.rem(me + (size - k if back else k), size))
        ref = buf.at[parity, slot]
        return pltpu.make_async_remote_copy(
            src_ref=ref, dst_ref=ref, send_sem=send.at[rnd, k], recv_sem=recv.at[rnd, k],
            device_id=there, device_id_type=MESH,
        )

    def in_plane(buf, parity):
        return (buf, parity, np_, mp, at_plane, pl_send, pl_recv)

    def in_line(buf, parity):
        return (buf, parity, nz, mz, at_z, z_send, z_recv)

    def stage_start(where, rnd, value):
        buf, parity, size, me = where[:4]
        buf[parity, me] = value
        for k in range(1, size):
            stage_copy(where, rnd, me, k, False).start()

    def stage_wait(where, rnd):
        size, me = where[2:4]
        for k in range(1, size):
            stage_copy(where, rnd, me, k, False).wait_send()
            stage_copy(where, rnd, lax.rem(me + size - k, size), k, True).wait_recv()

    def add_slots(where):
        buf, parity, size = where[:3]
        total = buf[parity, 0]
        for k in range(1, size):
            total = total + buf[parity, k]
        return total

    groups = lengths.shape[1]
    s_at = lax.broadcasted_iota(jnp.int32, (seqs, groups), 0)
    g_at = lax.broadcasted_iota(jnp.int32, (seqs, groups), 1) * views
    there = (s_at >= g_at) & (s_at < g_at + views)
    position = lax.broadcasted_iota(jnp.int32, (seqs, 128), 1)
    local_counts = []
    for m in range(2):
        turn[...] = jnp.zeros_like(turn)
        turn[0:steps, 0:seqs] = masks[m].astype(F32)
        mask = turn[...].T[0:seqs]
        length = jnp.broadcast_to(lengths[m : m + 1, :], (seqs, groups)).astype(F32)
        limit = jnp.sum(jnp.where(there, length, 0.0), axis=1, keepdims=True)
        alive = (position.astype(F32) < limit) & ((mask > 0.0) | (position == 0))
        alive = jnp.where(position < steps, alive.astype(F32), 0.0)
        total = jnp.zeros((seqs, 128), F32)
        for t in range(steps):
            at = m * span + t * seqs
            cells = jnp.broadcast_to(alive[:, t : t + 1], (seqs, 128))
            live[at : at + seqs, :] = cells
            total = total + cells
        local_counts.append(jnp.sum(total, axis=0, keepdims=True))
    n_own = jnp.concatenate(local_counts * 4, axis=0)

    cnt_plane, cnt_line = in_plane(cnt_p, 0), in_line(cnt_z, 0)
    stage_start(cnt_plane, 0, n_own)

    def vec_of(layer, k):
        return vecs[layer, k : k + 1, pl.ds(aligned(section * W, W), W)]

    def matmul_to(out, a, w, first, m):
        r = pl.ds(m * span, span)

        def body(i, _):
            c = pl.ds(aligned(i * HALF, HALF), HALF)
            y = dot(a[r, :], w[:, c], ((1,), (0,)))
            out[r, c] = y if first else out[r, c] + y
            return 0

        lax.fori_loop(0, 2, body, 0)

    def packed(pair_a, pair_b):
        a = jnp.concatenate(pair_a, axis=0)
        c = jnp.concatenate(pair_b, axis=0)
        return jnp.concatenate([a[:, :HALF], a[:, HALF:], c[:, :HALF], c[:, HALF:]], axis=0)

    def unpacked(x):
        return jnp.concatenate([x[0:2], x[2:4]], axis=1)

    def merge_slots(where, counts_of):
        buf, parity, size = where[:3]
        s = [buf[parity, k, 0:4, :] for k in range(size)]
        q = [buf[parity, k, 4:8, :] for k in range(size)]
        n = [wide(counts_of(k)[0:4], 4) for k in range(size)]
        total, squares, count = sum(s[1:], s[0]), sum(q[1:], q[0]), sum(n[1:], n[0])
        mean = total / count
        for k in range(size):
            d = s[k] / n[k] - mean
            squares = squares + n[k] * d * d
        return jnp.concatenate([total, squares], axis=0)

    def forward_stats(layer, fill_plane, fill_line):
        sums, squares = [], []
        for m in range(2):
            start = jnp.sum(rows[layer, m * span : m * span + seqs, :], axis=0, keepdims=True) * (1.0 / seqs)

            def body(i, carry):
                s, q = carry
                r = pl.ds(aligned(m * span + i * (2 * seqs), 16), 2 * seqs)
                d = rows[layer, r, :] - start
                kept = wide(live[r, :], 8) * d
                return s + fold(kept), q + fold(kept * d)

            zero = jnp.zeros((8, W), F32)
            s, q = lax.fori_loop(0, pairs, body, (zero, zero))
            s, q = jnp.sum(s, axis=0, keepdims=True), jnp.sum(q, axis=0, keepdims=True)
            n = wide(local_counts[m], 8)
            sums.append(s + n * start)
            squares.append(jnp.maximum(q - s * s / n, 0.0))
        plane, line = in_plane(slim_p, layer), in_line(slim_z, layer)
        stage_start(plane, 1 + layer, packed(sums, squares))
        fill_plane()
        stage_wait(plane, 1 + layer)
        stage_start(line, 1 + layer, merge_slots(plane, lambda k: cnt_p[0, k]))
        fill_line()
        stage_wait(line, 1 + layer)
        value = merge_slots(line, lambda k: cnt_z[0, k])
        total, squares = unpacked(value[0:4]), unpacked(value[4:8])
        for m in range(2):
            count = wide(counts[m : m + 1, :], 8)
            coef[layer, 2 * m : 2 * m + 1, :] = total[m : m + 1] / count
            coef[layer, 2 * m + 1 : 2 * m + 2, :] = lax.rsqrt(squares[m : m + 1] / count + EPS)

    def forward_scan(layer, passes):
        gain, shift, recur = vec_of(layer, 0), vec_of(layer, 1), vec_of(layer, 2)
        sends = []
        for lh in range(2):
            lanes = slice(lh * HALF, (lh + 1) * HALF)
            a, c = [], []
            for m in range(2):
                mean = coef[layer, 2 * m : 2 * m + 1, lanes]
                a.append(gain[:, lanes] * coef[layer, 2 * m + 1 : 2 * m + 2, lanes])
                c.append((shift[:, lanes], mean))
            rec = recur[:, lanes]

            def body(i, carry):
                states, level = carry
                out = []
                for m in range(2):
                    r = pl.ds(aligned(m * span + i * (2 * seqs), 16), 2 * seqs)
                    x = (rows[layer, r, lanes] - c[m][1]) * a[m] + c[m][0]
                    lv = wide(live[r, :], 4)
                    alive = lv > 0.0
                    h = states[m]
                    both = []
                    for k in range(2):
                        part = slice(k * seqs, (k + 1) * seqs)
                        z = x[part] + rec * h
                        soft = jnp.maximum(z, 0.0) + jnp.log(1.0 + jnp.exp(-jnp.abs(z)))
                        h = jnp.where(alive[part], soft, h)
                        both.append(h)
                    two = jnp.concatenate(both, axis=0)
                    hid[layer, r, lanes] = two
                    if passes:
                        p_own[r, lanes] = two.astype(BF16)
                        level = level + fold(lv * two)
                    out.append(h)
                return tuple(out), level

            zero = jnp.zeros((seqs, HALF), F32)
            _, level = lax.fori_loop(0, pairs, body, ((zero, zero), jnp.zeros((8, HALF), F32)))
            if passes:
                levels[1:2, lanes] = jnp.sum(level, axis=0, keepdims=True)
                made = across(p_own.at[pl.ds(0, total_rows), lanes], p_far.at[:, lanes], 18 + lh)
                made.start()
                sends.append(made)
        return sends

    def backward_scan(layer, above, between=lambda: None):
        gain, shift, recur = vec_of(layer, 0), vec_of(layer, 1), vec_of(layer, 2)
        for lq in range(4):
            lanes = slice(lq * QUART, (lq + 1) * QUART)
            gq, sq, rec = gain[:, lanes], shift[:, lanes], recur[:, lanes]
            mean = [coef[layer, 2 * m : 2 * m + 1, lanes] for m in range(2)]
            scale = [coef[layer, 2 * m + 1 : 2 * m + 2, lanes] for m in range(2)]

            def body(i, carry):
                down, s1, s2, rsum, sqh, sqa = carry
                down, s1, s2 = list(down), list(s1), list(s2)
                i = pairs - 1 - i
                for m in range(2):
                    start = m * span + i * (2 * seqs)
                    r = pl.ds(aligned(start, 16), 2 * seqs)
                    before = pl.ds(aligned(jnp.maximum(start - seqs, 0), 8), seqs)
                    normed = (rows[layer, r, lanes] - mean[m]) * scale[m]
                    drive = gq * normed + sq
                    h2 = hid[layer, r, lanes]
                    hb = jnp.where(i > 0, hid[layer, before, lanes], 0.0)
                    lv = wide(live[r, :], 2)
                    up = above[r, lanes].astype(F32)
                    res = f_own[r, lanes].astype(F32)
                    aux = res + h2 if layer == 1 else res
                    sqh = sqh + fold(lv * (h2 * h2))
                    sqa = sqa + fold(lv * (aux * aux))
                    grads = [None, None]
                    for k in (1, 0):
                        part = slice(k * seqs, (k + 1) * seqs)
                        prior = h2[0:seqs] if k == 1 else hb
                        slope = 0.5 + 0.5 * jnp.tanh(0.5 * (drive[part] + rec * prior))
                        total = up[part] + down[m]
                        gd = lv[part] * slope * total
                        down[m] = (1.0 - lv[part]) * total + rec * gd
                        grads[k] = gd
                        rsum = rsum + fold(gd * prior)
                    gd2 = jnp.concatenate(grads, axis=0)
                    hid[layer, r, lanes] = gd2
                    s1[m] = s1[m] + fold(gd2)
                    s2[m] = s2[m] + fold(gd2 * normed)
                return tuple(down), tuple(s1), tuple(s2), rsum, sqh, sqa

            zero = jnp.zeros((seqs, QUART), F32)
            z8 = jnp.zeros((8, QUART), F32)
            _, s1, s2, rsum, sqh, sqa = lax.fori_loop(
                0, pairs, body, ((zero, zero), (z8, z8), (z8, z8), z8, z8, z8)
            )
            for k, x in enumerate((s1[0], s1[1], s2[0], s2[1], rsum, sqh, sqa)):
                tot[layer, k : k + 1, lanes] = jnp.sum(x, axis=0, keepdims=True)
            between()

    def backward_stats(layer, fill_plane, fill_line):
        rnd = 4 if layer == 1 else 3
        plane, line = in_plane(slim_p, 1 - layer), in_line(slim_z, 1 - layer)
        t = tot[layer]
        stage_start(plane, rnd, packed([t[0:1], t[1:2]], [t[2:3], t[3:4]]))
        fill_plane()
        stage_wait(plane, rnd)
        stage_start(line, rnd, add_slots(plane))
        fill_line()
        stage_wait(line, rnd)
        value = add_slots(line)
        tot[layer, 0:2, :] = unpacked(value[0:4])
        tot[layer, 2:4, :] = unpacked(value[4:8])

    def grad_rows(layer, slot):
        gain = vec_of(layer, 0)
        sends = []
        for lh in range(2):
            lanes = slice(lh * HALF, (lh + 1) * HALF)
            acc = jnp.zeros((8, HALF), F32)
            for m in range(2):
                mean = coef[layer, 2 * m : 2 * m + 1, lanes]
                scale = coef[layer, 2 * m + 1 : 2 * m + 2, lanes]
                count = wide(counts[m : m + 1, :], 4)
                first = tot[layer, m : m + 1, lanes] / count
                second = tot[layer, 2 + m : 3 + m, lanes] / count * scale
                k = scale * gain[:, lanes]

                def body(i, acc):
                    r = pl.ds(aligned(m * span + i * (2 * seqs), 16), 2 * seqs)
                    y = hid[layer, r, lanes] - first - (rows[layer, r, lanes] - mean) * second
                    y = wide(live[r, :], 4) * (k * y)
                    g3[0, r, lanes] = y.astype(BF16)
                    return acc + fold(y)

                acc = lax.fori_loop(0, pairs, body, acc)
            top = lax.broadcasted_iota(jnp.int32, (16, HALF), 0) == 0
            minus = jnp.where(top, -jnp.sum(acc, axis=0, keepdims=True), 0.0)
            g3[0, total_rows:sent_rows, lanes] = minus.astype(BF16)
            made = across(g3.at[0, pl.ds(0, sent_rows), lanes], g3.at[1, pl.ds(0, sent_rows), lanes], slot + lh)
            made.start()
            sends.append(made)
        return sends

    sums_round = {1: (1, 6), 0: (0, 7)}

    def sums_start(layer):
        parity, rnd = sums_round[layer]
        own_sum = -g3[0, total_rows:sent_rows, :].astype(F32)[0:1]
        far_sum = -g3[1, total_rows:sent_rows, :].astype(F32)[0:1]
        value = jnp.concatenate([own_sum, far_sum, tot[layer, 4:7, :], jnp.zeros((3, W), F32)], axis=0)
        stage_start(in_plane(wide_p, parity), rnd, value)

    def sums_middle(layer):
        parity, rnd = sums_round[layer]
        stage_wait(in_plane(wide_p, parity), rnd)
        stage_start(in_line(wide_z, parity), rnd, add_slots(in_plane(wide_p, parity)))

    def sums_end(layer):
        parity, rnd = sums_round[layer]
        stage_wait(in_line(wide_z, parity), rnd)
        vtot[layer] = add_slots(in_line(wide_z, parity))
        tot[layer, 4:7, :] = vtot[layer, 2:5, :]
        tot[layer, 7:8, :] = wide(counts[0:1, :] + counts[1:2, :], 8)
        env["summed"].add(layer)

        @pl.when(section == layer)
        def _():
            pltpu.make_async_copy(tot.at[layer], v.at[section], v_sems.at[0]).start()

        @pl.when(section != layer)
        def _():
            v_across(layer).start()

    def v_across(layer):
        return pltpu.make_async_remote_copy(
            src_ref=tot.at[layer], dst_ref=v.at[section], send_sem=v_sems.at[1], recv_sem=v_sems.at[2],
            device_id=sibling, device_id_type=MESH,
        )

    def transpose(src):
        def body(j, _):
            c = pl.ds(aligned(j * 128, 128), 128)
            src_t[c, 0:total_rows] = src[0:total_rows, c].T
            return 0

        lax.fori_loop(0, W // 128, body, 0)

    def transpose_level(src, layer):
        top = lax.broadcasted_iota(jnp.int32, (16, W), 0) == 0
        src[total_rows:sent_rows, :] = jnp.where(top, levels[2 + layer : 3 + layer, :], 0.0).astype(BF16)

        def body(j, _):
            c = pl.ds(aligned(j * 128, 128), 128)
            src_t[c, total_rows:] = src[total_rows:, c].T
            level = src[total_rows:sent_rows, c].astype(F32)[0:1]
            column[layer, c, :] = jnp.broadcast_to(level, (128, 128)).T.astype(BF16)
            return 0

        lax.fori_loop(0, W // 128, body, 0)

    def weight_part(block, grads, c):
        lanes = pl.ds(c * QUART, QUART)

        def body(j, _):
            r = pl.ds(aligned(j * HALF, HALF), HALF)
            block[r, lanes] = dot(src_t[r, :], grads[:, lanes], ((1,), (0,))).astype(BF16)
            return 0

        lax.fori_loop(0, W // HALF, body, 0)

    def source_grad(store, w_own, w_far, between):
        for m in range(2):
            r = pl.ds(m * span, span)

            def body(i, _):
                c = pl.ds(aligned(i * HALF, HALF), HALF)
                y = dot(g3[0, r, :], w_own[c, :], ((1,), (1,))) + dot(g3[1, r, :], w_far[c, :], ((1,), (1,)))
                store(r, c, y)
                return 0

            lax.fori_loop(0, 2, body, 0)
            between()

    env = dict(summed=set(), vtot=vtot, column=column, space=space, ar_send=ar_send, ar_recv=ar_recv,
               ar_other=ar_other, o=o, section=section, here={"batch": b})
    xs = [a for a in bits if a["link"] == "x"]
    ys = [a for a in bits if a["link"] == "y"]
    zs = [a for a in bits if a["link"] == "z"]
    orders = (xs + ys + zs, ys + xs + zs)
    blocks = {
        (1, 0): f_far.at[pl.ds(0, W), :],
        (1, 1): p_far.at[pl.ds(0, W), :],
        (0, 0): wc.at[1, 1],
        (0, 1): wr1,
    }
    parts = {}
    for layer in (1, 0):
        for index in range(4):
            part, side = index // 2, index % 2

            def lane_of(sec, part=part, side=side):
                return (sec if part == 0 else 1 - sec) * W + side * HALF

            block = blocks[layer, part].at[:, pl.ds(side * HALF, HALF)]
            parts[layer, index] = Reduction(env, layer, index, block, orders, lane_of)
    order = Order()

    def weight_grads(layer, between):
        for part in range(2):
            if part == 1:
                between()
            for c in range(4):
                weight_part(blocks[layer, part], g3.at[part], c)
                order.work(0.9)
                order.begin(parts[layer, 2 * part + c // 2], c % 2)

    def arrived(layer, sends):
        for made in sends:
            made.wait()
        sums_start(layer)

    nothing = lambda: None

    wait_heads(frames, 1)
    send_f = []
    for m in range(2):
        by_units(frames, f_own, m)
        here = pl.ds(m * span, span)
        made = across(f_own.at[here, :], f_far.at[here, :], (0, 24)[m])
        made.start()
        send_f.append(made)
    wait_w(0, w_plan(0), slot_of[0], 0)
    for m in range(2):
        matmul_to(rows.at[0], f_own, wc.at[0, 0], True, m)
    wait_w(0, w_plan(0), slot_of[0], 1)
    for m in range(2):
        send_f[m].wait()
        matmul_to(rows.at[0], f_far, wc.at[0, 1], False, m)
    fetch(grad_out, 0).start()
    fetch(grad_out, 1).start()
    stage_wait(cnt_plane, 0)
    stage_start(cnt_line, 0, add_slots(cnt_plane))
    send_vec.wait_send()
    across(vecs.at[other], vecs.at[other], 3).wait_recv()

    def source_level():
        def body(i, acc):
            r = pl.ds(aligned(i * (2 * seqs), 16), 2 * seqs)
            return acc + fold(wide(live[r, :], 8) * f_own[r, :].astype(F32))

        acc = lax.fori_loop(0, 2 * pairs, body, jnp.zeros((8, W), F32))
        levels[0:1, :] = jnp.sum(acc, axis=0, keepdims=True)

    def counted():
        source_level()
        stage_wait(cnt_line, 0)
        counts[...] = add_slots(cnt_line)

    forward_stats(0, nothing, counted)
    sends = forward_scan(0, True)
    level_plane, level_line = in_plane(wide_p, 0), in_line(wide_z, 0)
    stage_start(level_plane, 5, jnp.concatenate([levels[0:2, :], jnp.zeros((6, W), F32)], axis=0))
    wait_w(1, w_plan(1), slot_of[1], 0)
    for m in range(2):
        matmul_to(rows.at[1], p_own, wc.at[1, 0], True, m)
    wait_w(1, w_plan(1), slot_of[1], 1)
    for made in sends:
        made.wait()
    done_w(0, w_plan(0), slot_of[0])

    start_local_w(0, late_plan, slot_of[2])
    start_across_w(0, late_plan, slot_of[2])

    @pl.when(section == 1)
    def _():
        wc[0, 1, width - late_row :, :] = jnp.zeros((W - width + late_row, W), BF16)
        heads_copy(grad_out, 2).start()

    for m in range(2):
        matmul_to(rows.at[1], p_far, wc.at[1, 1], False, m)
    stage_wait(level_plane, 5)
    stage_start(level_line, 5, add_slots(level_plane))

    def cotangent():
        wait_heads(grad_out, 2)
        for m in range(2):
            by_units(grad_out, f_far, m)

    def levelled():
        stage_wait(level_line, 5)
        value = add_slots(level_line) / wide(counts[0:1, :] + counts[1:2, :], 8)
        levels[2:4, :] = value[0:2]

    forward_stats(1, lambda: transpose(p_own), cotangent)
    forward_scan(1, False)
    levelled()
    backward_scan(1, f_far)
    backward_stats(1, lambda: transpose_level(p_own, 1), nothing)
    sends = grad_rows(1, 20)
    weight_grads(1, lambda: arrived(1, sends))
    wait_w(1, w_plan(1), slot_of[1], 2)
    done_w(1, w_plan(1), slot_of[1])

    def keep_down(r, c, y):
        p_own[r, c] = y.astype(BF16)

    source_grad(keep_down, wc.at[1, 0], wr1, lambda: order.work(3.0))
    pl.semaphore_signal(credit, inc=1, device_id=sibling, device_id_type=MESH)
    sums_middle(1)
    backward_scan(0, p_own, lambda: order.work(1.2))
    sums_end(1)

    def turn_frames():
        transpose(f_own)
        transpose_level(f_own, 0)
        order.work(3.0)

    backward_stats(0, turn_frames, lambda: order.work(3.0))
    pl.semaphore_wait(credit, 1)
    sends = grad_rows(0, 22)
    order.work(2.0)
    weight_grads(0, lambda: arrived(0, sends))
    wait_w(0, late_plan, slot_of[2], 0)
    wait_w(0, late_plan, slot_of[2], 1)
    done_w(0, late_plan, slot_of[2])

    def keep_source(r, c, y):
        rows[0, r, c] = y

    fetch(grad_out, 0).start()
    fetch(grad_out, 1).start()
    sums_middle(0)
    source_grad(keep_source, wc.at[0, 0], wc.at[0, 1], lambda: order.work(3.0))
    sums_end(0)

    def give(m):
        return pltpu.make_async_copy(staged.at[m], gf.at[m], stage_sem.at[m])

    for m in range(2):
        fetch(grad_out, m).wait()

        def finish_frames(i, _, m=m):
            straight = staged[m, pl.ds(2 * i, 2)].astype(F32).reshape(2 * seqs, half)
            y = rows[0, pl.ds(aligned(m * span + 2 * i * seqs, 8), 2 * seqs), :]
            y = jnp.where(section == 0, y[:, :half], y[:, late_shift : late_shift + half])
            staged[m, pl.ds(2 * i, 2)] = (y + straight).reshape(2, seqs, half).astype(BF16)
            return 0

        lax.fori_loop(0, pairs, finish_frames, 0)
        give(m).start()
        order.work(2.0)
    order.drain()
    for m in range(2):
        give(m).wait()

    for layer in range(2):

        @pl.when(section == layer)
        def _(layer=layer):
            pltpu.make_async_copy(tot.at[layer], v.at[section], v_sems.at[0]).wait()
            pltpu.make_async_remote_copy(
                src_ref=tot.at[layer], dst_ref=v.at[other], send_sem=v_sems.at[1], recv_sem=v_sems.at[2],
                device_id=sibling, device_id_type=MESH,
            ).wait_recv()

        @pl.when(section != layer)
        def _(layer=layer):
            v_across(layer).wait_send()

    own_part, far_part = v[section], v[other]
    first = jnp.where(section == 0, own_part, far_part)
    second = jnp.where(section == 0, far_part, own_part)
    for row, terms in ((0, (2, 3)), (1, (0, 1)), (2, (4,))):
        for lane, x in ((0, first), (W, second)):
            total = x[terms[0] : terms[0] + 1, :]
            for k in terms[1:]:
                total = total + x[k : k + 1, :]
            vectors[row : row + 1, lane : lane + W] = total
    squares = jnp.sum(first[5:7, :] + second[5:7, :], axis=1, keepdims=True)
    root = jnp.sqrt(squares / (first[7:8, 0:1] * width))
    for k in range(2):
        vectors[3 + k : 4 + k, :] = jnp.broadcast_to(root[k : k + 1], (1, 2 * W))
    vectors[5:8, :] = jnp.zeros((3, 2 * W), F32)


def write_results(o, gf, vectors, grad_weight, grad_frames, grad_gains, grad_shifts, grad_recurs, table):
    width = grad_weight.shape[2]
    grad_weight[0] = o[...][:, :width].astype(F32)
    grad_frames[...] = gf[...]

    @pl.when(pl.program_id(0) == 0)
    def _():
        for k, out in enumerate((grad_gains, grad_shifts, grad_recurs)):
            out[...] = vectors[k : k + 1, 0:width]
        table[...] = jnp.concatenate([vectors[3:4, 0:1], vectors[4:5, 0:1]], axis=1)


def results(o, gf, vectors):
    micro, steps, seqs, half = gf.shape
    width = 2 * half
    count = W * 2 // 128
    frames = micro * steps // count
    whole = lambda shape: pl.BlockSpec(shape, lambda i: (0, 0))
    out = pl.pallas_call(
        write_results,
        grid=(count,),
        in_specs=[
            pl.BlockSpec((128, 2 * W), lambda i: (i, 0)),
            pl.BlockSpec((frames, seqs, half), lambda i: (i, 0, 0)),
            whole((8, 2 * W)),
        ],
        out_specs=(
            pl.BlockSpec((1, 128, width), lambda i: (0, i, 0)),
            pl.BlockSpec((frames, seqs, half), lambda i: (i, 0, 0)),
            whole((1, width)),
            whole((1, width)),
            whole((1, width)),
            whole((1, 2)),
        ),
        out_shape=(
            jax.ShapeDtypeStruct((1, width, width), F32),
            jax.ShapeDtypeStruct((micro * steps, seqs, half), BF16),
            jax.ShapeDtypeStruct((1, width), F32),
            jax.ShapeDtypeStruct((1, width), F32),
            jax.ShapeDtypeStruct((1, width), F32),
            jax.ShapeDtypeStruct((1, 2), F32),
        ),
        compiler_params=pltpu.CompilerParams(vmem_limit_bytes=64 * 1024 * 1024),
    )(o.reshape(2 * W, 2 * W), gf.reshape(micro * steps, seqs, half), vectors)
    return out[1].reshape(gf.shape), out[0], *out[2:]


def whole_step(dims, frames, grad_out, weights, gains, shifts, recurs, lengths, masks):
    nz, ny, nx = dims
    micro, steps, seqs, half = frames.shape
    width = 2 * half
    views = seqs // lengths.shape[1]
    rows = micro * steps * seqs
    np_ = ny * nx
    wide_rows = (rows + 16 + 127) // 128 * 128
    depth = (nx * ny * nz - 1).bit_length()
    any_ = pl.BlockSpec(memory_space=pl.ANY)
    held = pl.BlockSpec(memory_space=pltpu.VMEM)
    dma = pltpu.SemaphoreType.DMA
    return pl.pallas_call(
        functools.partial(kernel, dims, steps, seqs, views),
        out_shape=(
            jax.ShapeDtypeStruct((2, W, 2 * W), BF16),
            jax.ShapeDtypeStruct(frames.shape, BF16),
            jax.ShapeDtypeStruct((8, 2 * W), F32),
        ),
        in_specs=[any_] * 3 + [held] * 5,
        out_specs=(any_, any_, held),
        scratch_shapes=[
            pltpu.VMEM((wide_rows, W), BF16),
            pltpu.VMEM((rows, W), BF16),
            pltpu.VMEM((wide_rows, W), BF16),
            pltpu.VMEM((rows, W), BF16),
            pltpu.VMEM((2, wide_rows, W), BF16),
            pltpu.VMEM((2, 2, W, W), BF16),
            pltpu.VMEM((W, W), BF16),
            pltpu.VMEM((W, wide_rows), BF16),
            pltpu.VMEM((rows, 128), F32),
            pltpu.VMEM((128, 128), F32),
            pltpu.VMEM(frames.shape, BF16),
            pltpu.VMEM((micro, steps, seqs, 128), BF16),
            pltpu.VMEM((5, W, (width - W) % 128), BF16),
            pltpu.VMEM((2, 8, W), F32),
            pltpu.VMEM((2, 8, 2 * W), F32),
            pltpu.VMEM((2, rows, W), F32),
            pltpu.VMEM((2, rows, W), F32),
            pltpu.VMEM((2, 8, W), F32),
            pltpu.VMEM((2, 8, W), F32),
            pltpu.VMEM((2, 8, W), F32),
            pltpu.VMEM((8, W), F32),
            pltpu.VMEM((2, W, 128), BF16),
            pltpu.VMEM((8, 128), F32),
            pltpu.VMEM((1, np_, 8, 128), F32),
            pltpu.VMEM((1, nz, 8, 128), F32),
            pltpu.VMEM((2, np_, 8, HALF), F32),
            pltpu.VMEM((2, nz, 8, HALF), F32),
            pltpu.VMEM((2, np_, 8, W), F32),
            pltpu.VMEM((2, nz, 8, W), F32),
            pltpu.VMEM((2, 4, W, HALF), BF16),
            dma((3, 25)),
            dma((3,)),
            dma((2,)),
            pltpu.SemaphoreType.REGULAR,
            dma((8, max(np_, 2))),
            dma((8, max(np_, 2))),
            dma((8, max(nz, 2))),
            dma((8, max(nz, 2))),
            dma((2, 4, 2, 2 * depth + 2)),
            dma((2, 4, 2, 2 * depth + 2)),
            dma((2, 4, 2, 2)),
        ],
        compiler_params=pltpu.CompilerParams(
            collective_id=0, has_side_effects=True, vmem_limit_bytes=64 * 1024 * 1024
        ),
    )(frames, grad_out, weights, gains, shifts, recurs, lengths, masks)


def shards(dims, frames, grad_out, weights, gains, shifts, recurs, lengths, masks):
    return results(*whole_step(dims, frames, grad_out, weights, gains, shifts, recurs, lengths, masks))


def solution(mesh):
    in_specs = (
        P(None, None, "batch", "section"),
        P(None, None, "batch", "section"),
        P("section", None, None),
        P("section", None),
        P("section", None),
        P("section", None),
        P(None, "batch"),
        P(None, None, "batch"),
    )
    out_specs = (
        P(None, None, "batch", "section"),
        P("section", None, None),
        P("section", None),
        P("section", None),
        P("section", None),
        P("section", None),
    )
    body = functools.partial(shards, grid_of(mesh.shape["batch"]))
    return jax.shard_map(body, mesh=mesh, in_specs=in_specs, out_specs=out_specs, check_vma=False)
```

```python
import functools

import jax
import jax.numpy as jnp
from jax import lax
from jax.experimental import pallas as pl
from jax.experimental.pallas import tpu as pltpu
from jax.sharding import PartitionSpec as P

EPS = 1e-05
W = 1024
HALF = W // 2
QUART = W // 4
MESH = pl.DeviceIdType.MESH
F32 = jnp.float32
BF16 = jnp.bfloat16


def grid_of(size):
    if size == 16:
        return (4, 2, 2)
    if size == 128:
        return (8, 4, 4)
    return (size, 1, 1)


def aligned(x, k):
    return pl.multiple_of(x, k)


def wide(x, reps):
    return jnp.concatenate([x] * reps, axis=1)


def fold(x):
    rows = x.shape[0]
    total = x[0:8]
    for k in range(8, rows, 8):
        total = total + x[k : k + 8]
    return total


def dot(a, b, dims):
    return lax.dot_general(a, b, (dims, ((), ())), preferred_element_type=F32)


class Reduction:
    def __init__(self, env, layer, index, block, orders, lane_of):
        self.env, self.layer, self.index, self.block, self.orders = env, layer, index, block, orders
        self.lane_of = lane_of
        self.space = env["space"].at[layer, index]
        self.depth = len(orders[0])
        self.regions = [self.halves(i, order) for i, order in enumerate(orders)]
        self.step = 0
        self.waits = []
        depth = self.depth
        self.steps = [functools.partial(self.scatter, 0)]
        self.steps += [functools.partial(self.scatter, k) for k in range(1, depth)]
        self.steps += [functools.partial(self.gather, k) for k in range(depth - 1, 0, -1)]
        self.steps += [self.give, self.finish]

    def halves(self, i, order):
        row, rows, lane, lanes = 0, W, i * QUART, QUART
        out = [(row, rows, lane, lanes)]
        for axis in order:
            if rows > 16:
                rows //= 2
                row = row + axis["bit"] * rows
            else:
                lanes //= 2
                lane = lane + axis["bit"] * lanes
            out.append((row, rows, lane, lanes))
        return out

    @property
    def free_to_go(self):
        return self.step != self.depth or self.layer in self.env["summed"]

    @property
    def done(self):
        return self.step >= len(self.steps)

    def advance(self):
        self.sent = []
        self.steps[self.step]()
        self.step += 1
        return self.sent

    def remote(self, i, src, dst, slot, where, recv=None):
        sems = (self.layer, self.index, i, slot)
        return pltpu.make_async_remote_copy(
            src_ref=src, dst_ref=dst, send_sem=self.env["ar_send"].at[sems],
            recv_sem=self.env["ar_recv"].at[sems] if recv is None else recv, device_id=where, device_id_type=MESH,
        )

    def wait(self):
        for made, came in self.waits:
            made.wait_send()
            came.wait_recv()
        self.waits = []

    def came_at(self, i, k):
        row = sum(r[1] for r in self.regions[i][1 : k + 1])
        _, rows, _, lanes = self.regions[i][k + 1]
        return row, rows, i * QUART, lanes

    def scatter(self, k):
        if k > 0:
            self.wait()
            self.add(k - 1)
        for i, order in enumerate(self.orders):
            self.scatter_part(i, k, order[k])

    def start_part(self, i):
        self.sent = []
        self.scatter_part(i, 0, self.orders[i][0])
        if i == 1:
            self.step = 1
        return self.sent

    def scatter_part(self, i, k, axis):
        row, rows, lane, lanes = self.regions[i][k]
        _, rows2, _, lanes2 = self.regions[i][k + 1]
        give_row = row + (1 - axis["bit"]) * rows2 if rows2 < rows else row
        give_lane = lane if rows2 < rows else lane + (1 - axis["bit"]) * lanes2
        src = self.block.at[pl.ds(aligned(give_row, 16), rows2), pl.ds(aligned(give_lane, 128), lanes2)]
        at, n, at_lane, n_lanes = self.came_at(i, k)
        dst = self.space.at[pl.ds(at, n), pl.ds(at_lane, n_lanes)]
        made = self.remote(i, src, dst, k, axis["partner"])
        made.start()
        self.waits.append((made, made))
        self.sent.append((axis["link"], rows2 * lanes2 * 2))

    def add(self, k, last=False):
        rows = self.regions[0][k + 1][1]
        size = min(rows, 32)
        out = []
        for i in range(2):
            row, _, lane, lanes = self.regions[i][k + 1]
            at, _, at_lane, _ = self.came_at(i, k)
            lane = aligned(lane, 128)
            extra = None
            if last:
                part = self.index // 2
                first = aligned((self.index % 2) * HALF + lane, 128)
                extra = self.env["vtot"][self.layer, part : part + 1, pl.ds(first, lanes)]
            out.append((row, lane, lanes, at, at_lane, self.local(i, k + 1)[0], extra))

        def body(j, _):
            for row, lane, lanes, at, at_lane, home, extra in out:
                here = pl.ds(aligned(row + j * size, 16), size)
                total = self.block[here, pl.ds(lane, lanes)].astype(F32)
                total = total + self.space[pl.ds(aligned(at + j * size, 16), size), pl.ds(at_lane, lanes)].astype(F32)
                if last:
                    column = self.env["column"][self.layer, here, :].astype(F32)
                    total = total + wide(column, lanes // 128) * extra
                    to = pl.ds(aligned(home + j * size, 16), size)
                    self.space[to, pl.ds(lane, lanes)] = total.astype(BF16)
                else:
                    self.block[here, pl.ds(lane, lanes)] = total.astype(BF16)
            return 0

        lax.fori_loop(0, rows // size, body, 0)

    def local(self, i, k):
        row, rows, lane, lanes = self.regions[i][k]
        return row - self.regions[i][1][0], rows, lane, lanes

    def gather(self, k):
        self.wait()
        if k == self.depth - 1:
            self.add(k, last=True)
        for i, order in enumerate(self.orders):
            axis = order[k]
            row, rows, lane, lanes = self.local(i, k + 1)
            row0, rows0, lane0, lanes0 = self.local(i, k)
            if rows0 > rows:
                far = (row0 + (1 - axis["bit"]) * rows, rows, lane, lanes)
            else:
                far = (row, rows, lane0 + (1 - axis["bit"]) * lanes, lanes)
            refs = [
                self.space.at[pl.ds(aligned(r, 16), n), pl.ds(aligned(c, 128), w)]
                for r, n, c, w in ((row, rows, lane, lanes), far)
            ]
            made = self.remote(i, refs[0], refs[0], self.depth + k, axis["partner"])
            made.start()
            self.waits.append((made, self.remote(i, refs[1], refs[1], self.depth + k, axis["partner"])))
            self.sent.append((axis["link"], rows * lanes * 2))

    def result(self, i, bit, section):
        rows = self.regions[i][1][1]
        lane = aligned(self.lane_of(section) + i * QUART, QUART)
        return self.env["o"].at[section, pl.ds(aligned(bit * rows, 16), rows), pl.ds(lane, QUART)]

    def gathered(self, i):
        return self.space.at[pl.ds(0, self.regions[i][1][1]), pl.ds(i * QUART, QUART)]

    def deliver(self, i, near, straight):
        axis, section = self.orders[i][0], self.env["section"]
        slot = 2 * self.depth + (0 if near else 1)
        recv = None if straight else self.env["ar_other"].at[self.layer, self.index, i, 0 if near else 1]
        where = dict(self.env["here"] if near else axis["partner"], section=self.layer)
        return self.remote(i, self.gathered(i), self.result(i, axis["bit"], section), slot, where, recv)

    def arrival(self, i, near, straight):
        axis, section = self.orders[i][0], self.env["section"]
        slot = 2 * self.depth + (0 if near else 1)
        recv = None if straight else self.env["ar_other"].at[self.layer, self.index, i, 0 if near else 1]
        bit = axis["bit"] if near else 1 - axis["bit"]
        frm = section if straight else 1 - section
        where = dict(self.env["here"] if near else axis["partner"], section=frm)
        return self.remote(i, self.gathered(i), self.result(i, bit, frm), slot, where, recv)

    def kept(self, i):
        sem = self.env["ar_recv"].at[self.layer, self.index, i, 2 * self.depth]
        return pltpu.make_async_copy(
            self.gathered(i), self.result(i, self.orders[i][0]["bit"], self.env["section"]), sem
        )

    def give(self):
        self.wait()

        @pl.when(self.env["section"] == self.layer)
        def _():
            for i in range(2):
                self.deliver(i, False, True).start()
                self.kept(i).start()

        @pl.when(self.env["section"] != self.layer)
        def _():
            for i in range(2):
                self.deliver(i, False, False).start()
                self.deliver(i, True, False).start()

        for i, order in enumerate(self.orders):
            self.sent.append((order[0]["link"], self.regions[i][1][1] * QUART * 2))

    def finish(self):
        @pl.when(self.env["section"] == self.layer)
        def _():
            for i in range(2):
                self.kept(i).wait()
                self.deliver(i, False, True).wait_send()
                self.arrival(i, False, True).wait_recv()
                self.arrival(i, True, False).wait_recv()
                self.arrival(i, False, False).wait_recv()

        @pl.when(self.env["section"] != self.layer)
        def _():
            for i in range(2):
                self.deliver(i, False, False).wait_send()
                self.deliver(i, True, False).wait_send()


class Order:
    RATE, HOP = 50e3, 1.8

    def __init__(self):
        self.now = 0.0
        self.free = {}
        self.going = []

    def sent(self, copies):
        end = self.now
        for link, size in copies:
            self.free[link] = max(self.now, self.free.get(link, 0.0)) + size / self.RATE
            end = max(end, self.free[link])
        return end + self.HOP

    def begin(self, one, i):
        end = self.sent(one.start_part(i))
        if i == 0:
            one.due = end
        else:
            one.due = max(one.due, end)
            self.going.append(one)

    def advance(self, one):
        self.now = max(self.now, one.due) + 0.4
        one.due = self.sent(one.advance())
        if one.done:
            self.going.remove(one)

    def work(self, cost):
        self.now += cost
        while True:
            due = [x for x in self.going if x.due <= self.now and x.free_to_go]
            if not due:
                return
            self.advance(min(due, key=lambda x: x.due))

    def drain(self):
        while self.going:
            self.advance(min(self.going, key=lambda x: x.due))


def kernel(dims, steps, seqs, views, frames, grad_out, weights, gains, shifts, recurs, lengths, masks, o, gf, vectors, f_own, f_far, p_own, p_far, g3, wc, wr1, src_t, live, turn,
           staged, heads, tails, v, vecs, rows, hid, coef, tot, vtot, levels, column, counts, cnt_p, cnt_z, slim_p, slim_z,
           wide_p, wide_z, space, sems, v_sems, stage_sem, credit, pl_send, pl_recv, z_send, z_recv, ar_send, ar_recv,
           ar_other):
    nz, ny, nx = dims
    np_ = ny * nx
    span = steps * seqs
    total_rows = 2 * span
    sent_rows = total_rows + 16
    pairs = steps // 2
    section = lax.axis_index("section")
    other = 1 - section
    b = lax.axis_index("batch")
    mp = lax.rem(b, np_)
    mz = b // np_

    def at_plane(i):
        return {"batch": b - mp + i}

    def at_z(i):
        return {"batch": b + (i - mz) * np_}

    bits = []
    for link, count, stride in (("x", nx, 1), ("y", ny, nx), ("z", nz, np_)):
        while count > 1:
            bit = lax.rem(b // stride, 2)
            bits.append(dict(bit=bit, partner={"batch": b + (1 - 2 * bit) * stride}, link=link))
            count //= 2
            stride *= 2
    sibling = {"section": other}

    def local(src, dst, slot):
        return pltpu.make_async_copy(src, dst, sems.at[0, slot])

    def across(src, dst, slot):
        return pltpu.make_async_remote_copy(
            src_ref=src, dst_ref=dst, send_sem=sems.at[1, slot], recv_sem=sems.at[2, slot],
            device_id=sibling, device_id_type=MESH,
        )

    half = frames.shape[3]
    width = 2 * half
    lead = W - half
    rest = width - W
    full = rest // 128 * 128

    def fetch(source, m):
        return pltpu.make_async_copy(source.at[m], staged.at[m], stage_sem.at[m])

    def by_units(source, target, m):
        fetch(source, m).wait()

        @pl.when(section == 0)
        def _():
            def place(i, _):
                x = staged[m, pl.ds(2 * i, 2)].astype(F32).reshape(2 * seqs, half)
                head = heads[m, pl.ds(2 * i, 2)].astype(F32).reshape(2 * seqs, 128)
                to = pl.ds(aligned(m * span + 2 * i * seqs, 16), 2 * seqs)
                target[to, :] = jnp.concatenate([x, head[:, :lead]], axis=1).astype(BF16)
                return 0

            lax.fori_loop(0, pairs, place, 0)

        @pl.when(section == 1)
        def _():
            pad = jnp.zeros((2 * seqs, 2 * lead), F32)

            def place(i, _):
                x = staged[m, pl.ds(2 * i, 2)].astype(F32).reshape(2 * seqs, half)
                to = pl.ds(aligned(m * span + 2 * i * seqs, 16), 2 * seqs)
                target[to, :] = jnp.concatenate([x[:, lead:], pad], axis=1).astype(BF16)
                return 0

            lax.fori_loop(0, pairs, place, 0)

    def pieces(row, count, u, block, spot):
        r = pl.ds(row, count)
        to = pl.ds(0, count)
        if u == 0:
            return [(weights.at[0, r, pl.ds(0, W)], block.at[to, :])]
        return [
            (weights.at[0, r, pl.ds(W, full)], block.at[to, pl.ds(0, full)]),
            (weights.at[0, r, pl.ds(W + full, rest - full)], tails.at[spot, to, :]),
        ]

    rows_of = {0: (0, W), 1: (W, rest)}

    def w_plan(layer):
        mine, far = rows_of[layer], rows_of[1 - layer]
        plan = [
            (mine, layer, far, 1 - layer, wc.at[layer, 0], 2 * layer),
            (far, layer, mine, 1 - layer, wc.at[layer, 1], 2 * layer + 1),
        ]
        if layer == 1:
            plan.append((mine, 0, far, 1, wr1, 4))
        return plan

    late_row = (width - half) // 16 * 16
    late_shift = half - late_row
    late_plan = [
        ((0, W), 0, (late_row, width - late_row), 1, wc.at[0, 0], 0),
        ((0, W), 1, (late_row, width - late_row), 0, wc.at[0, 1], 1),
    ]
    slot_of = {0: 4, 1: 8, 2: 14}

    def local_w(plan, base, which):
        r, u, _, _, block, spot = plan[which]
        return [local(a, t, base + 2 * which + i) for i, (a, t) in enumerate(pieces(*r, u, block, spot))]

    def across_w(plan, base, which):
        _, _, r, u, block, spot = plan[which]
        return [across(a, t, base + 2 * which + i) for i, (a, t) in enumerate(pieces(*r, u, block, spot))]

    def start_local_w(layer, plan, base):
        @pl.when(section == layer)
        def _():
            for which in range(len(plan)):
                for made in local_w(plan, base, which):
                    made.start()

    def start_across_w(layer, plan, base):
        @pl.when(section == layer)
        def _():
            for which in range(len(plan)):
                for made in across_w(plan, base, which):
                    made.start()

    def last_units(block, spot):
        def body(i, _):
            r = pl.ds(aligned(i * 128, 128), 128)
            x = tails[spot, r, :].astype(F32)
            x = jnp.concatenate([x, jnp.zeros((128, 128 - x.shape[1]), F32)], axis=1)
            block[r, full:] = x.astype(BF16)
            return 0

        lax.fori_loop(0, W // 128, body, 0)

    def wait_w(layer, plan, base, which):
        _, own_u, _, far_u, block, spot = plan[which]

        @pl.when(section == layer)
        def _():
            for made in local_w(plan, base, which):
                made.wait()
            if own_u == 1:
                last_units(block, spot)

        @pl.when(section != layer)
        def _():
            for made in across_w(plan, base, which):
                made.wait_recv()
            if far_u == 1:
                last_units(block, spot)

    def done_w(layer, plan, base):
        @pl.when(section == layer)
        def _():
            for which in range(len(plan)):
                for made in across_w(plan, base, which):
                    made.wait_send()

    def heads_copy(source, slot):
        return across(source.at[:, :, :, pl.ds(0, 128)], heads, slot)

    def wait_heads(source, slot):
        @pl.when(section == 0)
        def _():
            heads_copy(source, slot).wait_recv()

        @pl.when(section == 1)
        def _():
            heads_copy(source, slot).wait_send()

    fetch(frames, 0).start()
    fetch(frames, 1).start()
    for layer in range(2):
        start_local_w(layer, w_plan(layer), slot_of[layer])

    barrier = pltpu.get_barrier_semaphore()
    greeted = [dict(sibling)]
    greeted += [at_plane(lax.rem(mp + k, np_)) for k in range(1, np_)]
    greeted += [at_z(lax.rem(mz + k, nz)) for k in range(1, nz)]
    greeted += [dict(axis["partner"], section=other) for axis in bits]
    for where in greeted:
        pl.semaphore_signal(barrier, inc=1, device_id=where, device_id_type=MESH)

    for k, (x, fill) in enumerate(((gains, 0.0), (shifts, -1e30), (recurs, 0.0))):
        vecs[section, k : k + 1, 0:width] = x[...]
        vecs[section, k : k + 1, width:] = jnp.full((1, 2 * W - width), fill, F32)
    vecs[section, 3:8, :] = jnp.zeros((5, 2 * W), F32)

    gap = jnp.zeros((W - rest, W), BF16)

    @pl.when(section == 0)
    def _():
        wc[0, 1, rest:, :] = gap
        wc[1, 1, rest:, :] = gap

    @pl.when(section == 1)
    def _():
        wc[0, 0, rest:, :] = gap
        wc[1, 0, rest:, :] = gap
        wr1[rest:, :] = gap

    for spot in (0, 2):
        tails[spot, rest:, :] = jnp.zeros((W - rest, rest - full), BF16)
    for spare in (f_own, p_own, g3.at[0], g3.at[1]):
        spare[sent_rows:, :] = jnp.zeros((spare.shape[0] - sent_rows, W), BF16)

    pl.semaphore_wait(barrier, len(greeted))

    @pl.when(section == 1)
    def _():
        heads_copy(frames, 1).start()

    for layer in range(2):
        start_across_w(layer, w_plan(layer), slot_of[layer])
    send_vec = across(vecs.at[section], vecs.at[section], 3)
    send_vec.start()

    def stage_copy(where, rnd, slot, k, back):
        buf, parity, size, me, at, send, recv = where
        there = at(lax.rem(me + (size - k if back else k), size))
        ref = buf.at[parity, slot]
        return pltpu.make_async_remote_copy(
            src_ref=ref, dst_ref=ref, send_sem=send.at[rnd, k], recv_sem=recv.at[rnd, k],
            device_id=there, device_id_type=MESH,
        )

    def in_plane(buf, parity):
        return (buf, parity, np_, mp, at_plane, pl_send, pl_recv)

    def in_line(buf, parity):
        return (buf, parity, nz, mz, at_z, z_send, z_recv)

    def stage_start(where, rnd, value):
        buf, parity, size, me = where[:4]
        buf[parity, me] = value
        for k in range(1, size):
            stage_copy(where, rnd, me, k, False).start()

    def stage_wait(where, rnd):
        size, me = where[2:4]
        for k in range(1, size):
            stage_copy(where, rnd, me, k, False).wait_send()
            stage_copy(where, rnd, lax.rem(me + size - k, size), k, True).wait_recv()

    def add_slots(where):
        buf, parity, size = where[:3]
        total = buf[parity, 0]
        for k in range(1, size):
            total = total + buf[parity, k]
        return total

    groups = lengths.shape[1]
    s_at = lax.broadcasted_iota(jnp.int32, (seqs, groups), 0)
    g_at = lax.broadcasted_iota(jnp.int32, (seqs, groups), 1) * views
    there = (s_at >= g_at) & (s_at < g_at + views)
    position = lax.broadcasted_iota(jnp.int32, (seqs, 128), 1)
    local_counts = []
    for m in range(2):
        turn[...] = jnp.zeros_like(turn)
        turn[0:steps, 0:seqs] = masks[m].astype(F32)
        mask = turn[...].T[0:seqs]
        length = jnp.broadcast_to(lengths[m : m + 1, :], (seqs, groups)).astype(F32)
        limit = jnp.sum(jnp.where(there, length, 0.0), axis=1, keepdims=True)
        alive = (position.astype(F32) < limit) & ((mask > 0.0) | (position == 0))
        alive = jnp.where(position < steps, alive.astype(F32), 0.0)
        total = jnp.zeros((seqs, 128), F32)
        for t in range(steps):
            at = m * span + t * seqs
            cells = jnp.broadcast_to(alive[:, t : t + 1], (seqs, 128))
            live[at : at + seqs, :] = cells
            total = total + cells
        local_counts.append(jnp.sum(total, axis=0, keepdims=True))
    n_own = jnp.concatenate(local_counts * 4, axis=0)

    cnt_plane, cnt_line = in_plane(cnt_p, 0), in_line(cnt_z, 0)
    stage_start(cnt_plane, 0, n_own)

    def vec_of(layer, k):
        return vecs[layer, k : k + 1, pl.ds(aligned(section * W, W), W)]

    def matmul_to(out, a, w, first, m):
        r = pl.ds(m * span, span)

        def body(i, _):
            c = pl.ds(aligned(i * HALF, HALF), HALF)
            y = dot(a[r, :], w[:, c], ((1,), (0,)))
            out[r, c] = y if first else out[r, c] + y
            return 0

        lax.fori_loop(0, 2, body, 0)

    def packed(x, y):
        return jnp.concatenate([z[:, k * QUART : (k + 1) * QUART] for z in (x, y) for k in range(4)], axis=0)

    def unpacked(x):
        return jnp.concatenate([x[k : k + 1] for k in range(4)], axis=1)

    def merge_slots(where, counts_of):
        buf, parity, size = where[:3]
        s = [buf[parity, k, 0:4, :] for k in range(size)]
        q = [buf[parity, k, 4:8, :] for k in range(size)]
        n = [wide(counts_of(k), 2) for k in range(size)]
        total, squares, count = sum(s[1:], s[0]), sum(q[1:], q[0]), sum(n[1:], n[0])
        mean = total / count
        for k in range(size):
            d = s[k] / n[k] - mean
            squares = squares + n[k] * d * d
        return jnp.concatenate([total, squares], axis=0)

    def slim_round(which, m):
        return 1 + 2 * which + m, in_plane(slim_p, 2 * m + which % 2), in_line(slim_z, 2 * m + which % 2)

    def forward_stats(layer, m):
        start = jnp.sum(rows[layer, m * span : m * span + seqs, :], axis=0, keepdims=True) * (1.0 / seqs)

        def body(i, carry):
            s, q = carry
            r = pl.ds(aligned(m * span + i * (2 * seqs), 16), 2 * seqs)
            d = rows[layer, r, :] - start
            kept = wide(live[r, :], 8) * d
            return s + fold(kept), q + fold(kept * d)

        zero = jnp.zeros((8, W), F32)
        s, q = lax.fori_loop(0, pairs, body, (zero, zero))
        s, q = jnp.sum(s, axis=0, keepdims=True), jnp.sum(q, axis=0, keepdims=True)
        n = wide(local_counts[m], 8)
        rnd, plane, _ = slim_round(layer, m)
        stage_start(plane, rnd, packed(s + n * start, jnp.maximum(q - s * s / n, 0.0)))

    def forward_middle(layer, m):
        rnd, plane, line = slim_round(layer, m)
        stage_wait(plane, rnd)
        stage_start(line, rnd, merge_slots(plane, lambda k: cnt_p[0, k, m : m + 1, :]))

    def forward_end(layer, m):
        rnd, _, line = slim_round(layer, m)
        stage_wait(line, rnd)
        value = merge_slots(line, lambda k: cnt_z[0, k, m : m + 1, :])
        count = wide(counts[m : m + 1, :], 8)
        mean = unpacked(value[0:4]) / count
        scale = lax.rsqrt(unpacked(value[4:8]) / count + EPS)
        coef[layer, 2 * m : 2 * m + 1, :] = mean
        coef[layer, 2 * m + 1 : 2 * m + 2, :] = scale
        slope = vec_of(layer, 0) * scale
        coef[layer, 4 + 2 * m : 5 + 2 * m, :] = slope
        coef[layer, 5 + 2 * m : 6 + 2 * m, :] = vec_of(layer, 1) - mean * slope

    def forward_scan(layer, m, passes):
        rec = vec_of(layer, 2)
        slope = coef[layer, 4 + 2 * m : 5 + 2 * m, :]
        shift = coef[layer, 5 + 2 * m : 6 + 2 * m, :]

        def body(i, carry):
            h, level = carry
            r = pl.ds(aligned(m * span + i * (2 * seqs), 16), 2 * seqs)
            x = rows[layer, r, :] * slope + shift
            lv = wide(live[r, :], 8)
            alive = lv > 0.0
            both = []
            for k in range(2):
                part = slice(k * seqs, (k + 1) * seqs)
                z = x[part] + rec * h
                soft = jnp.maximum(z, 0.0) + jnp.log(1.0 + jnp.exp(-jnp.abs(z)))
                h = jnp.where(alive[part], soft, h)
                both.append(h)
            two = jnp.concatenate(both, axis=0)
            hid[layer, r, :] = two
            if passes:
                p_own[r, :] = two.astype(BF16)
                level = level + fold(lv * two)
            return h, level

        _, level = lax.fori_loop(0, pairs, body, (jnp.zeros((seqs, W), F32), jnp.zeros((8, W), F32)))
        if not passes:
            return None
        level = jnp.sum(level, axis=0, keepdims=True)
        levels[1:2, :] = level if m == 0 else levels[1:2, :] + level
        here = pl.ds(m * span, span)
        made = across(p_own.at[here, :], p_far.at[here, :], 18 + m)
        made.start()
        return made

    def backward_scan(layer, m, above, between=lambda: None):
        gain, shift, recur = vec_of(layer, 0), vec_of(layer, 1), vec_of(layer, 2)
        for lq in range(4):
            lanes = slice(lq * QUART, (lq + 1) * QUART)
            gq, sq, rec = gain[:, lanes], shift[:, lanes], recur[:, lanes]
            mean = coef[layer, 2 * m : 2 * m + 1, lanes]
            scale = coef[layer, 2 * m + 1 : 2 * m + 2, lanes]

            def body(i, carry):
                down, s1, s2, rsum, sqh, sqa = carry
                i = pairs - 1 - i
                start = m * span + i * (2 * seqs)
                r = pl.ds(aligned(start, 16), 2 * seqs)
                before = pl.ds(aligned(jnp.maximum(start - seqs, 0), 8), seqs)
                normed = (rows[layer, r, lanes] - mean) * scale
                drive = gq * normed + sq
                h2 = hid[layer, r, lanes]
                hb = jnp.where(i > 0, hid[layer, before, lanes], 0.0)
                lv = wide(live[r, :], 2)
                up = above[r, lanes].astype(F32)
                res = f_own[r, lanes].astype(F32)
                aux = res + h2 if layer == 1 else res
                sqh = sqh + fold(lv * (h2 * h2))
                sqa = sqa + fold(lv * (aux * aux))
                grads = [None, None]
                for k in (1, 0):
                    part = slice(k * seqs, (k + 1) * seqs)
                    prior = h2[0:seqs] if k == 1 else hb
                    slope = 0.5 + 0.5 * jnp.tanh(0.5 * (drive[part] + rec * prior))
                    total = up[part] + down
                    gd = lv[part] * slope * total
                    down = (1.0 - lv[part]) * total + rec * gd
                    grads[k] = gd
                    rsum = rsum + fold(gd * prior)
                gd2 = jnp.concatenate(grads, axis=0)
                hid[layer, r, lanes] = gd2
                return down, s1 + fold(gd2), s2 + fold(gd2 * normed), rsum, sqh, sqa

            z8 = jnp.zeros((8, QUART), F32)
            _, s1, s2, rsum, sqh, sqa = lax.fori_loop(
                0, pairs, body, (jnp.zeros((seqs, QUART), F32), z8, z8, z8, z8, z8)
            )
            for k, x in ((m, s1), (2 + m, s2)):
                tot[layer, k : k + 1, lanes] = jnp.sum(x, axis=0, keepdims=True)
            for k, x in ((4, rsum), (5, sqh), (6, sqa)):
                x = jnp.sum(x, axis=0, keepdims=True)
                tot[layer, k : k + 1, lanes] = x if m == 0 else tot[layer, k : k + 1, lanes] + x
            between()

    def backward_stats(layer, m):
        rnd, plane, _ = slim_round(3 - layer, m)
        stage_start(plane, rnd, packed(tot[layer, m : m + 1, :], tot[layer, 2 + m : 3 + m, :]))

    def backward_middle(layer, m):
        rnd, plane, line = slim_round(3 - layer, m)
        stage_wait(plane, rnd)
        stage_start(line, rnd, add_slots(plane))

    def backward_end(layer, m):
        rnd, _, line = slim_round(3 - layer, m)
        stage_wait(line, rnd)
        value = add_slots(line)
        tot[layer, m : m + 1, :] = unpacked(value[0:4])
        tot[layer, 2 + m : 3 + m, :] = unpacked(value[4:8])

    def grad_rows(layer, m, slot):
        gain = vec_of(layer, 0)
        for lh in range(2):
            lanes = slice(lh * HALF, (lh + 1) * HALF)
            mean = coef[layer, 2 * m : 2 * m + 1, lanes]
            scale = coef[layer, 2 * m + 1 : 2 * m + 2, lanes]
            count = wide(counts[m : m + 1, :], 4)
            first = tot[layer, m : m + 1, lanes] / count
            second = tot[layer, 2 + m : 3 + m, lanes] / count * scale
            k = scale * gain[:, lanes]

            def body(i, acc):
                r = pl.ds(aligned(m * span + i * (2 * seqs), 16), 2 * seqs)
                y = hid[layer, r, lanes] - first - (rows[layer, r, lanes] - mean) * second
                y = wide(live[r, :], 4) * (k * y)
                g3[0, r, lanes] = y.astype(BF16)
                return acc + fold(y)

            acc = lax.fori_loop(0, pairs, body, jnp.zeros((8, HALF), F32))
            acc = jnp.sum(acc, axis=0, keepdims=True)
            if m == 0:
                levels[4:5, lanes] = acc
            else:
                top = lax.broadcasted_iota(jnp.int32, (16, HALF), 0) == 0
                minus = jnp.where(top, -(levels[4:5, lanes] + acc), 0.0)
                g3[0, total_rows:sent_rows, lanes] = minus.astype(BF16)
        here = pl.ds(0, span) if m == 0 else pl.ds(span, span + 16)
        made = across(g3.at[0, here, :], g3.at[1, here, :], slot + m)
        made.start()
        return made

    sums_round = {1: (1, 10), 0: (0, 11)}

    def sums_start(layer):
        parity, rnd = sums_round[layer]
        own_sum = -g3[0, total_rows:sent_rows, :].astype(F32)[0:1]
        far_sum = -g3[1, total_rows:sent_rows, :].astype(F32)[0:1]
        value = jnp.concatenate([own_sum, far_sum, tot[layer, 4:7, :], jnp.zeros((3, W), F32)], axis=0)
        stage_start(in_plane(wide_p, parity), rnd, value)

    def sums_middle(layer):
        parity, rnd = sums_round[layer]
        stage_wait(in_plane(wide_p, parity), rnd)
        stage_start(in_line(wide_z, parity), rnd, add_slots(in_plane(wide_p, parity)))

    def sums_end(layer):
        parity, rnd = sums_round[layer]
        stage_wait(in_line(wide_z, parity), rnd)
        vtot[layer] = add_slots(in_line(wide_z, parity))
        tot[layer, 4:7, :] = vtot[layer, 2:5, :]
        tot[layer, 7:8, :] = wide(counts[0:1, :] + counts[1:2, :], 8)
        env["summed"].add(layer)

        @pl.when(section == layer)
        def _():
            pltpu.make_async_copy(tot.at[layer], v.at[section], v_sems.at[0]).start()

        @pl.when(section != layer)
        def _():
            v_across(layer).start()

    def v_across(layer):
        return pltpu.make_async_remote_copy(
            src_ref=tot.at[layer], dst_ref=v.at[section], send_sem=v_sems.at[1], recv_sem=v_sems.at[2],
            device_id=sibling, device_id_type=MESH,
        )

    def transpose(src, begin=0, end=W // 128):
        def body(j, _):
            c = pl.ds(aligned(j * 128, 128), 128)
            src_t[c, 0:total_rows] = src[0:total_rows, c].T
            return 0

        lax.fori_loop(begin, end, body, 0)

    def transpose_level(src, layer):
        top = lax.broadcasted_iota(jnp.int32, (16, W), 0) == 0
        src[total_rows:sent_rows, :] = jnp.where(top, levels[2 + layer : 3 + layer, :], 0.0).astype(BF16)

        def body(j, _):
            c = pl.ds(aligned(j * 128, 128), 128)
            src_t[c, total_rows:] = src[total_rows:, c].T
            level = src[total_rows:sent_rows, c].astype(F32)[0:1]
            column[layer, c, :] = jnp.broadcast_to(level, (128, 128)).T.astype(BF16)
            return 0

        lax.fori_loop(0, W // 128, body, 0)

    def weight_part(block, grads, c):
        lanes = pl.ds(c * QUART, QUART)

        def body(j, _):
            r = pl.ds(aligned(j * HALF, HALF), HALF)
            block[r, lanes] = dot(src_t[r, :], grads[:, lanes], ((1,), (0,))).astype(BF16)
            return 0

        lax.fori_loop(0, W // HALF, body, 0)

    def source_grad(store, w_own, w_far, between):
        for m in range(2):
            r = pl.ds(m * span, span)

            def body(i, _):
                c = pl.ds(aligned(i * HALF, HALF), HALF)
                y = dot(g3[0, r, :], w_own[c, :], ((1,), (1,))) + dot(g3[1, r, :], w_far[c, :], ((1,), (1,)))
                store(r, c, y)
                return 0

            lax.fori_loop(0, 2, body, 0)
            between()

    env = dict(summed=set(), vtot=vtot, column=column, space=space, ar_send=ar_send, ar_recv=ar_recv,
               ar_other=ar_other, o=o, section=section, here={"batch": b})
    xs = [a for a in bits if a["link"] == "x"]
    ys = [a for a in bits if a["link"] == "y"]
    zs = [a for a in bits if a["link"] == "z"]
    orders = (xs + ys + zs, ys + xs + zs)
    blocks = {
        (1, 0): f_far.at[pl.ds(0, W), :],
        (1, 1): p_far.at[pl.ds(0, W), :],
        (0, 0): wc.at[1, 1],
        (0, 1): wr1,
    }
    parts = {}
    for layer in (1, 0):
        for index in range(4):
            part, side = index // 2, index % 2

            def lane_of(sec, part=part, side=side):
                return (sec if part == 0 else 1 - sec) * W + side * HALF

            block = blocks[layer, part].at[:, pl.ds(side * HALF, HALF)]
            parts[layer, index] = Reduction(env, layer, index, block, orders, lane_of)
    order = Order()

    def weight_grads(layer, between):
        for part in range(2):
            if part == 1:
                between()
            for c in range(4):
                weight_part(blocks[layer, part], g3.at[part], c)
                order.work(0.9)
                order.begin(parts[layer, 2 * part + c // 2], c % 2)

    def arrived(layer, sends):
        for made in sends:
            made.wait()
        sums_start(layer)

    wait_heads(frames, 1)
    send_f = []
    for m in range(2):
        by_units(frames, f_own, m)
        fetch(grad_out, m).start()
        here = pl.ds(m * span, span)
        made = across(f_own.at[here, :], f_far.at[here, :], (0, 24)[m])
        made.start()
        send_f.append(made)

    stage_wait(cnt_plane, 0)
    stage_start(cnt_line, 0, add_slots(cnt_plane))
    wait_w(0, w_plan(0), slot_of[0], 0)
    matmul_to(rows.at[0], f_own, wc.at[0, 0], True, 0)
    wait_w(0, w_plan(0), slot_of[0], 1)
    send_f[0].wait()
    matmul_to(rows.at[0], f_far, wc.at[0, 1], False, 0)
    forward_stats(0, 0)
    matmul_to(rows.at[0], f_own, wc.at[0, 0], True, 1)
    forward_middle(0, 0)
    send_f[1].wait()

    @pl.when(section == 1)
    def _():
        heads_copy(grad_out, 2).start()

    matmul_to(rows.at[0], f_far, wc.at[0, 1], False, 1)
    forward_stats(0, 1)
    send_vec.wait_send()
    across(vecs.at[other], vecs.at[other], 3).wait_recv()
    stage_wait(cnt_line, 0)
    counts[...] = add_slots(cnt_line)
    forward_end(0, 0)
    sends = [forward_scan(0, 0, True)]
    forward_middle(0, 1)
    wait_heads(grad_out, 2)
    by_units(grad_out, g3.at[1], 0)
    forward_end(0, 1)
    sends.append(forward_scan(0, 1, True))
    wait_w(1, w_plan(1), slot_of[1], 0)
    matmul_to(rows.at[1], p_own, wc.at[1, 0], True, 0)
    wait_w(1, w_plan(1), slot_of[1], 1)
    sends[0].wait()
    matmul_to(rows.at[1], p_far, wc.at[1, 1], False, 0)
    forward_stats(1, 0)
    matmul_to(rows.at[1], p_own, wc.at[1, 0], True, 1)
    forward_middle(1, 0)
    sends[1].wait()
    matmul_to(rows.at[1], p_far, wc.at[1, 1], False, 1)
    forward_stats(1, 1)
    done_w(0, w_plan(0), slot_of[0])

    start_local_w(0, late_plan, slot_of[2])
    start_across_w(0, late_plan, slot_of[2])

    @pl.when(section == 1)
    def _():
        wc[0, 1, width - late_row :, :] = jnp.zeros((W - width + late_row, W), BF16)

    def source_level():
        def body(i, acc):
            r = pl.ds(aligned(i * (2 * seqs), 16), 2 * seqs)
            return acc + fold(wide(live[r, :], 8) * f_own[r, :].astype(F32))

        acc = lax.fori_loop(0, 2 * pairs, body, jnp.zeros((8, W), F32))
        levels[0:1, :] = jnp.sum(acc, axis=0, keepdims=True)

    forward_end(1, 0)
    forward_scan(1, 0, False)
    forward_middle(1, 1)
    by_units(grad_out, g3.at[1], 1)
    source_level()
    forward_end(1, 1)
    level_plane, level_line = in_plane(wide_p, 0), in_line(wide_z, 0)
    stage_start(level_plane, 9, jnp.concatenate([levels[0:2, :], jnp.zeros((6, W), F32)], axis=0))
    forward_scan(1, 1, False)
    backward_scan(1, 0, g3.at[1])
    backward_stats(1, 0)
    stage_wait(level_plane, 9)
    stage_start(level_line, 9, add_slots(level_plane))
    backward_scan(1, 1, g3.at[1])
    backward_stats(1, 1)
    backward_middle(1, 0)
    pl.semaphore_signal(credit.at[0], inc=1, device_id=sibling, device_id_type=MESH)
    transpose(p_own, 0, W // 256)
    backward_middle(1, 1)
    backward_end(1, 0)
    pl.semaphore_wait(credit.at[0], 1)
    sends = [grad_rows(1, 0, 20)]
    transpose(p_own, W // 256)
    stage_wait(level_line, 9)
    levels[2:4, :] = (add_slots(level_line) / wide(counts[0:1, :] + counts[1:2, :], 8))[0:2]
    transpose_level(p_own, 1)
    backward_end(1, 1)
    sends.append(grad_rows(1, 1, 20))
    weight_grads(1, lambda: arrived(1, sends))
    wait_w(1, w_plan(1), slot_of[1], 2)
    done_w(1, w_plan(1), slot_of[1])

    def keep_down(r, c, y):
        p_own[r, c] = y.astype(BF16)

    source_grad(keep_down, wc.at[1, 0], wr1, lambda: order.work(3.0))
    pl.semaphore_signal(credit.at[1], inc=1, device_id=sibling, device_id_type=MESH)
    sums_middle(1)
    backward_scan(0, 0, p_own, lambda: order.work(0.6))
    backward_stats(0, 0)
    backward_scan(0, 1, p_own, lambda: order.work(0.6))
    backward_stats(0, 1)
    backward_middle(0, 0)
    sums_end(1)
    transpose(f_own)
    transpose_level(f_own, 0)
    backward_middle(0, 1)
    order.work(3.0)
    backward_end(0, 0)
    pl.semaphore_wait(credit.at[1], 1)
    sends = [grad_rows(0, 0, 22)]
    backward_end(0, 1)
    sends.append(grad_rows(0, 1, 22))
    order.work(2.0)
    weight_grads(0, lambda: arrived(0, sends))
    wait_w(0, late_plan, slot_of[2], 0)
    wait_w(0, late_plan, slot_of[2], 1)
    done_w(0, late_plan, slot_of[2])

    def keep_source(r, c, y):
        rows[0, r, c] = y

    fetch(grad_out, 0).start()
    fetch(grad_out, 1).start()
    sums_middle(0)
    source_grad(keep_source, wc.at[0, 0], wc.at[0, 1], lambda: order.work(3.0))
    sums_end(0)

    def give(m):
        return pltpu.make_async_copy(staged.at[m], gf.at[m], stage_sem.at[m])

    for m in range(2):
        fetch(grad_out, m).wait()

        def finish_frames(i, _, m=m):
            straight = staged[m, pl.ds(2 * i, 2)].astype(F32).reshape(2 * seqs, half)
            y = rows[0, pl.ds(aligned(m * span + 2 * i * seqs, 8), 2 * seqs), :]
            y = jnp.where(section == 0, y[:, :half], y[:, late_shift : late_shift + half])
            staged[m, pl.ds(2 * i, 2)] = (y + straight).reshape(2, seqs, half).astype(BF16)
            return 0

        lax.fori_loop(0, pairs, finish_frames, 0)
        give(m).start()
        order.work(2.0)
    order.drain()
    for m in range(2):
        give(m).wait()

    for layer in range(2):

        @pl.when(section == layer)
        def _(layer=layer):
            pltpu.make_async_copy(tot.at[layer], v.at[section], v_sems.at[0]).wait()
            pltpu.make_async_remote_copy(
                src_ref=tot.at[layer], dst_ref=v.at[other], send_sem=v_sems.at[1], recv_sem=v_sems.at[2],
                device_id=sibling, device_id_type=MESH,
            ).wait_recv()

        @pl.when(section != layer)
        def _(layer=layer):
            v_across(layer).wait_send()

    own_part, far_part = v[section], v[other]
    first = jnp.where(section == 0, own_part, far_part)
    second = jnp.where(section == 0, far_part, own_part)
    for row, terms in ((0, (2, 3)), (1, (0, 1)), (2, (4,))):
        for lane, x in ((0, first), (W, second)):
            total = x[terms[0] : terms[0] + 1, :]
            for k in terms[1:]:
                total = total + x[k : k + 1, :]
            vectors[row : row + 1, lane : lane + W] = total
    squares = jnp.sum(first[5:7, :] + second[5:7, :], axis=1, keepdims=True)
    root = jnp.sqrt(squares / (first[7:8, 0:1] * width))
    for k in range(2):
        vectors[3 + k : 4 + k, :] = jnp.broadcast_to(root[k : k + 1], (1, 2 * W))
    vectors[5:8, :] = jnp.zeros((3, 2 * W), F32)


def write_results(o, gf, vectors, grad_weight, grad_frames, grad_gains, grad_shifts, grad_recurs, table):
    width = grad_weight.shape[2]
    grad_weight[0] = o[...][:, :width].astype(F32)
    grad_frames[...] = gf[...]

    @pl.when(pl.program_id(0) == 0)
    def _():
        for k, out in enumerate((grad_gains, grad_shifts, grad_recurs)):
            out[...] = vectors[k : k + 1, 0:width]
        table[...] = jnp.concatenate([vectors[3:4, 0:1], vectors[4:5, 0:1]], axis=1)


def results(o, gf, vectors):
    micro, steps, seqs, half = gf.shape
    width = 2 * half
    count = W * 2 // 256
    frames = micro * steps // count
    whole = lambda shape: pl.BlockSpec(shape, lambda i: (0, 0))
    out = pl.pallas_call(
        write_results,
        grid=(count,),
        in_specs=[
            pl.BlockSpec((256, 2 * W), lambda i: (i, 0)),
            pl.BlockSpec((frames, seqs, half), lambda i: (i, 0, 0)),
            whole((8, 2 * W)),
        ],
        out_specs=(
            pl.BlockSpec((1, 256, width), lambda i: (0, i, 0)),
            pl.BlockSpec((frames, seqs, half), lambda i: (i, 0, 0)),
            whole((1, width)),
            whole((1, width)),
            whole((1, width)),
            whole((1, 2)),
        ),
        out_shape=(
            jax.ShapeDtypeStruct((1, width, width), F32),
            jax.ShapeDtypeStruct((micro * steps, seqs, half), BF16),
            jax.ShapeDtypeStruct((1, width), F32),
            jax.ShapeDtypeStruct((1, width), F32),
            jax.ShapeDtypeStruct((1, width), F32),
            jax.ShapeDtypeStruct((1, 2), F32),
        ),
        compiler_params=pltpu.CompilerParams(vmem_limit_bytes=64 * 1024 * 1024),
    )(o.reshape(2 * W, 2 * W), gf.reshape(micro * steps, seqs, half), vectors)
    return out[1].reshape(gf.shape), out[0], *out[2:]


def whole_step(dims, frames, grad_out, weights, gains, shifts, recurs, lengths, masks):
    nz, ny, nx = dims
    micro, steps, seqs, half = frames.shape
    width = 2 * half
    views = seqs // lengths.shape[1]
    rows = micro * steps * seqs
    np_ = ny * nx
    wide_rows = (rows + 16 + 127) // 128 * 128
    depth = (nx * ny * nz - 1).bit_length()
    any_ = pl.BlockSpec(memory_space=pl.ANY)
    held = pl.BlockSpec(memory_space=pltpu.VMEM)
    dma = pltpu.SemaphoreType.DMA
    return pl.pallas_call(
        functools.partial(kernel, dims, steps, seqs, views),
        out_shape=(
            jax.ShapeDtypeStruct((2, W, 2 * W), BF16),
            jax.ShapeDtypeStruct(frames.shape, BF16),
            jax.ShapeDtypeStruct((8, 2 * W), F32),
        ),
        in_specs=[any_] * 3 + [held] * 5,
        out_specs=(any_, any_, held),
        scratch_shapes=[
            pltpu.VMEM((wide_rows, W), BF16),
            pltpu.VMEM((rows, W), BF16),
            pltpu.VMEM((wide_rows, W), BF16),
            pltpu.VMEM((rows, W), BF16),
            pltpu.VMEM((2, wide_rows, W), BF16),
            pltpu.VMEM((2, 2, W, W), BF16),
            pltpu.VMEM((W, W), BF16),
            pltpu.VMEM((W, wide_rows), BF16),
            pltpu.VMEM((rows, 128), F32),
            pltpu.VMEM((128, 128), F32),
            pltpu.VMEM(frames.shape, BF16),
            pltpu.VMEM((micro, steps, seqs, 128), BF16),
            pltpu.VMEM((5, W, (width - W) % 128), BF16),
            pltpu.VMEM((2, 8, W), F32),
            pltpu.VMEM((2, 8, 2 * W), F32),
            pltpu.VMEM((2, rows, W), F32),
            pltpu.VMEM((2, rows, W), F32),
            pltpu.VMEM((2, 8, W), F32),
            pltpu.VMEM((2, 8, W), F32),
            pltpu.VMEM((2, 8, W), F32),
            pltpu.VMEM((8, W), F32),
            pltpu.VMEM((2, W, 128), BF16),
            pltpu.VMEM((8, 128), F32),
            pltpu.VMEM((1, np_, 8, 128), F32),
            pltpu.VMEM((1, nz, 8, 128), F32),
            pltpu.VMEM((4, np_, 8, QUART), F32),
            pltpu.VMEM((4, nz, 8, QUART), F32),
            pltpu.VMEM((2, np_, 8, W), F32),
            pltpu.VMEM((2, nz, 8, W), F32),
            pltpu.VMEM((2, 4, W, HALF), BF16),
            dma((3, 25)),
            dma((3,)),
            dma((2,)),
            pltpu.SemaphoreType.REGULAR((2,)),
            dma((12, max(np_, 2))),
            dma((12, max(np_, 2))),
            dma((12, max(nz, 2))),
            dma((12, max(nz, 2))),
            dma((2, 4, 2, 2 * depth + 2)),
            dma((2, 4, 2, 2 * depth + 2)),
            dma((2, 4, 2, 2)),
        ],
        compiler_params=pltpu.CompilerParams(
            collective_id=0, has_side_effects=True, vmem_limit_bytes=64 * 1024 * 1024
        ),
    )(frames, grad_out, weights, gains, shifts, recurs, lengths, masks)


def shards(dims, frames, grad_out, weights, gains, shifts, recurs, lengths, masks):
    return results(*whole_step(dims, frames, grad_out, weights, gains, shifts, recurs, lengths, masks))


def solution(mesh):
    in_specs = (
        P(None, None, "batch", "section"),
        P(None, None, "batch", "section"),
        P("section", None, None),
        P("section", None),
        P("section", None),
        P("section", None),
        P(None, "batch"),
        P(None, None, "batch"),
    )
    out_specs = (
        P(None, None, "batch", "section"),
        P("section", None, None),
        P("section", None),
        P("section", None),
        P("section", None),
        P("section", None),
    )
    body = functools.partial(shards, grid_of(mesh.shape["batch"]))
    return jax.shard_map(body, mesh=mesh, in_specs=in_specs, out_specs=out_specs, check_vma=False)
```

```python
import functools

import jax
import jax.numpy as jnp
from jax import lax
from jax.experimental import pallas as pl
from jax.experimental.pallas import tpu as pltpu
from jax.sharding import PartitionSpec as P

EPS = 1e-05
W = 1024
HALF = W // 2
QUART = W // 4
MESH = pl.DeviceIdType.MESH
F32 = jnp.float32
BF16 = jnp.bfloat16


def grid_of(size):
    if size == 16:
        return (4, 2, 2)
    if size == 128:
        return (8, 4, 4)
    return (size, 1, 1)


def aligned(x, k):
    return pl.multiple_of(x, k)


def wide(x, reps):
    return jnp.concatenate([x] * reps, axis=1)


def fold(x):
    rows = x.shape[0]
    total = x[0:8]
    for k in range(8, rows, 8):
        total = total + x[k : k + 8]
    return total


def dot(a, b, dims):
    return lax.dot_general(a, b, (dims, ((), ())), preferred_element_type=F32)


class Reduction:
    def __init__(self, env, layer, index, block, orders, lane_of):
        self.env, self.layer, self.index, self.block, self.orders = env, layer, index, block, orders
        self.lane_of = lane_of
        self.space = env["space"].at[layer, index]
        self.depth = len(orders[0])
        self.regions = [self.halves(i, order) for i, order in enumerate(orders)]
        self.step = 0
        self.waits = []
        depth = self.depth
        self.steps = [functools.partial(self.scatter, 0)]
        self.steps += [functools.partial(self.scatter, k) for k in range(1, depth)]
        self.steps += [functools.partial(self.gather, k) for k in range(depth - 1, 0, -1)]
        self.steps += [self.give, self.finish]

    def halves(self, i, order):
        row, rows, lane, lanes = 0, W, i * QUART, QUART
        out = [(row, rows, lane, lanes)]
        for axis in order:
            if rows > 16:
                rows //= 2
                row = row + axis["bit"] * rows
            else:
                lanes //= 2
                lane = lane + axis["bit"] * lanes
            out.append((row, rows, lane, lanes))
        return out

    @property
    def free_to_go(self):
        return self.step != self.depth or self.layer in self.env["summed"]

    @property
    def done(self):
        return self.step >= len(self.steps)

    def advance(self):
        self.sent = []
        self.steps[self.step]()
        self.step += 1
        return self.sent

    def remote(self, i, src, dst, slot, where, recv=None):
        sems = (self.layer, self.index, i, slot)
        return pltpu.make_async_remote_copy(
            src_ref=src, dst_ref=dst, send_sem=self.env["ar_send"].at[sems],
            recv_sem=self.env["ar_recv"].at[sems] if recv is None else recv, device_id=where, device_id_type=MESH,
        )

    def wait(self):
        for made, came in self.waits:
            made.wait_send()
            came.wait_recv()
        self.waits = []

    def came_at(self, i, k):
        row = sum(r[1] for r in self.regions[i][1 : k + 1])
        _, rows, _, lanes = self.regions[i][k + 1]
        return row, rows, i * QUART, lanes

    def scatter(self, k):
        if k > 0:
            self.wait()
            self.add(k - 1)
        for i, order in enumerate(self.orders):
            self.scatter_part(i, k, order[k])

    def start_part(self, i):
        self.sent = []
        self.scatter_part(i, 0, self.orders[i][0])
        if i == 1:
            self.step = 1
        return self.sent

    def scatter_part(self, i, k, axis):
        row, rows, lane, lanes = self.regions[i][k]
        _, rows2, _, lanes2 = self.regions[i][k + 1]
        give_row = row + (1 - axis["bit"]) * rows2 if rows2 < rows else row
        give_lane = lane if rows2 < rows else lane + (1 - axis["bit"]) * lanes2
        src = self.block.at[pl.ds(aligned(give_row, 16), rows2), pl.ds(aligned(give_lane, 128), lanes2)]
        at, n, at_lane, n_lanes = self.came_at(i, k)
        dst = self.space.at[pl.ds(at, n), pl.ds(at_lane, n_lanes)]
        made = self.remote(i, src, dst, k, axis["partner"])
        made.start()
        self.waits.append((made, made))
        self.sent.append((axis["link"], rows2 * lanes2 * 2))

    def add(self, k, last=False):
        rows = self.regions[0][k + 1][1]
        size = min(rows, 32)
        out = []
        for i in range(2):
            row, _, lane, lanes = self.regions[i][k + 1]
            at, _, at_lane, _ = self.came_at(i, k)
            lane = aligned(lane, 128)
            extra = None
            if last:
                part = self.index // 2
                first = aligned((self.index % 2) * HALF + lane, 128)
                extra = self.env["vtot"][self.layer, part : part + 1, pl.ds(first, lanes)]
            out.append((row, lane, lanes, at, at_lane, self.local(i, k + 1)[0], extra))

        def body(j, _):
            for row, lane, lanes, at, at_lane, home, extra in out:
                here = pl.ds(aligned(row + j * size, 16), size)
                total = self.block[here, pl.ds(lane, lanes)].astype(F32)
                total = total + self.space[pl.ds(aligned(at + j * size, 16), size), pl.ds(at_lane, lanes)].astype(F32)
                if last:
                    column = self.env["column"][self.layer, here, :].astype(F32)
                    total = total + wide(column, lanes // 128) * extra
                    to = pl.ds(aligned(home + j * size, 16), size)
                    self.space[to, pl.ds(lane, lanes)] = total.astype(BF16)
                else:
                    self.block[here, pl.ds(lane, lanes)] = total.astype(BF16)
            return 0

        lax.fori_loop(0, rows // size, body, 0)

    def local(self, i, k):
        row, rows, lane, lanes = self.regions[i][k]
        return row - self.regions[i][1][0], rows, lane, lanes

    def gather(self, k):
        self.wait()
        if k == self.depth - 1:
            self.add(k, last=True)
        for i, order in enumerate(self.orders):
            axis = order[k]
            row, rows, lane, lanes = self.local(i, k + 1)
            row0, rows0, lane0, lanes0 = self.local(i, k)
            if rows0 > rows:
                far = (row0 + (1 - axis["bit"]) * rows, rows, lane, lanes)
            else:
                far = (row, rows, lane0 + (1 - axis["bit"]) * lanes, lanes)
            refs = [
                self.space.at[pl.ds(aligned(r, 16), n), pl.ds(aligned(c, 128), w)]
                for r, n, c, w in ((row, rows, lane, lanes), far)
            ]
            made = self.remote(i, refs[0], refs[0], self.depth + k, axis["partner"])
            made.start()
            self.waits.append((made, self.remote(i, refs[1], refs[1], self.depth + k, axis["partner"])))
            self.sent.append((axis["link"], rows * lanes * 2))

    def result(self, i, bit, section):
        rows = self.regions[i][1][1]
        lane = aligned(self.lane_of(section) + i * QUART, QUART)
        return self.env["o"].at[section, pl.ds(aligned(bit * rows, 16), rows), pl.ds(lane, QUART)]

    def gathered(self, i):
        return self.space.at[pl.ds(0, self.regions[i][1][1]), pl.ds(i * QUART, QUART)]

    def deliver(self, i, near, straight):
        axis, section = self.orders[i][0], self.env["section"]
        slot = 2 * self.depth + (0 if near else 1)
        recv = None if straight else self.env["ar_other"].at[self.layer, self.index, i, 0 if near else 1]
        where = dict(self.env["here"] if near else axis["partner"], section=self.layer)
        return self.remote(i, self.gathered(i), self.result(i, axis["bit"], section), slot, where, recv)

    def arrival(self, i, near, straight):
        axis, section = self.orders[i][0], self.env["section"]
        slot = 2 * self.depth + (0 if near else 1)
        recv = None if straight else self.env["ar_other"].at[self.layer, self.index, i, 0 if near else 1]
        bit = axis["bit"] if near else 1 - axis["bit"]
        frm = section if straight else 1 - section
        where = dict(self.env["here"] if near else axis["partner"], section=frm)
        return self.remote(i, self.gathered(i), self.result(i, bit, frm), slot, where, recv)

    def kept(self, i):
        sem = self.env["ar_recv"].at[self.layer, self.index, i, 2 * self.depth]
        return pltpu.make_async_copy(
            self.gathered(i), self.result(i, self.orders[i][0]["bit"], self.env["section"]), sem
        )

    def give(self):
        self.wait()

        @pl.when(self.env["section"] == self.layer)
        def _():
            for i in range(2):
                self.deliver(i, False, True).start()
                self.kept(i).start()

        @pl.when(self.env["section"] != self.layer)
        def _():
            for i in range(2):
                self.deliver(i, False, False).start()
                self.deliver(i, True, False).start()

        for i, order in enumerate(self.orders):
            self.sent.append((order[0]["link"], self.regions[i][1][1] * QUART * 2))

    def finish(self):
        @pl.when(self.env["section"] == self.layer)
        def _():
            for i in range(2):
                self.kept(i).wait()
                self.deliver(i, False, True).wait_send()
                self.arrival(i, False, True).wait_recv()
                self.arrival(i, True, False).wait_recv()
                self.arrival(i, False, False).wait_recv()

        @pl.when(self.env["section"] != self.layer)
        def _():
            for i in range(2):
                self.deliver(i, False, False).wait_send()
                self.deliver(i, True, False).wait_send()


class Order:
    RATE, HOP = 70e3, 1.8

    def __init__(self):
        self.now = 0.0
        self.free = {}
        self.going = []

    def sent(self, copies):
        end = self.now
        for link, size in copies:
            self.free[link] = max(self.now, self.free.get(link, 0.0)) + size / self.RATE
            end = max(end, self.free[link])
        return end + self.HOP

    def begin(self, one, i):
        end = self.sent(one.start_part(i))
        if i == 0:
            one.due = end
        else:
            one.due = max(one.due, end)
            self.going.append(one)

    def advance(self, one):
        self.now = max(self.now, one.due) + 0.4
        one.due = self.sent(one.advance())
        if one.done:
            self.going.remove(one)

    def work(self, cost):
        self.now += cost
        while True:
            due = [x for x in self.going if x.due <= self.now and x.free_to_go]
            if not due:
                return
            self.advance(min(due, key=lambda x: x.due))

    def drain(self):
        while self.going:
            self.advance(min(self.going, key=lambda x: x.due))


def kernel(dims, steps, seqs, views, frames, grad_out, weights, gains, shifts, recurs, lengths, masks, o, gf, vectors, f_own, f_far, p_own, p_far, g3, wc, wr1, src_t, live, turn,
           staged, heads, tails, v, vecs, rows, hid, coef, tot, vtot, levels, column, counts, cnt_p, cnt_z, slim_p, slim_z,
           wide_p, wide_z, space, sems, v_sems, stage_sem, credit, pl_send, pl_recv, z_send, z_recv, ar_send, ar_recv,
           ar_other):
    nz, ny, nx = dims
    np_ = ny * nx
    span = steps * seqs
    total_rows = 2 * span
    sent_rows = total_rows + 16
    pairs = steps // 2
    section = lax.axis_index("section")
    other = 1 - section
    b = lax.axis_index("batch")
    mp = lax.rem(b, np_)
    mz = b // np_

    def at_plane(i):
        return {"batch": b - mp + i}

    def at_z(i):
        return {"batch": b + (i - mz) * np_}

    bits = []
    for link, count, stride in (("x", nx, 1), ("y", ny, nx), ("z", nz, np_)):
        while count > 1:
            bit = lax.rem(b // stride, 2)
            bits.append(dict(bit=bit, partner={"batch": b + (1 - 2 * bit) * stride}, link=link))
            count //= 2
            stride *= 2
    sibling = {"section": other}

    def local(src, dst, slot):
        return pltpu.make_async_copy(src, dst, sems.at[0, slot])

    def across(src, dst, slot):
        return pltpu.make_async_remote_copy(
            src_ref=src, dst_ref=dst, send_sem=sems.at[1, slot], recv_sem=sems.at[2, slot],
            device_id=sibling, device_id_type=MESH,
        )

    half = frames.shape[3]
    width = 2 * half
    lead = W - half
    rest = width - W
    full = rest // 128 * 128

    def fetch(source, m):
        return pltpu.make_async_copy(source.at[m], staged.at[m], stage_sem.at[m])

    def by_units(source, target, m):
        fetch(source, m).wait()

        @pl.when(section == 0)
        def _():
            pad = jnp.zeros((2 * seqs, lead), F32)

            def place(i, _):
                x = staged[m, pl.ds(2 * i, 2)].astype(F32).reshape(2 * seqs, half)
                to = pl.ds(aligned(m * span + 2 * i * seqs, 16), 2 * seqs)
                target[to, :] = jnp.concatenate([x, pad], axis=1).astype(BF16)
                return 0

            lax.fori_loop(0, pairs, place, 0)

        @pl.when(section == 1)
        def _():
            pad = jnp.zeros((2 * seqs, 2 * lead), F32)

            def place(i, _):
                x = staged[m, pl.ds(2 * i, 2)].astype(F32).reshape(2 * seqs, half)
                to = pl.ds(aligned(m * span + 2 * i * seqs, 16), 2 * seqs)
                target[to, :] = jnp.concatenate([x[:, lead:], pad], axis=1).astype(BF16)
                return 0

            lax.fori_loop(0, pairs, place, 0)

    def patch_heads(target, m):
        @pl.when(section == 0)
        def _():
            lane = lax.broadcasted_iota(jnp.int32, (2 * seqs, 128), 1)

            def place(i, _):
                to = pl.ds(aligned(m * span + 2 * i * seqs, 16), 2 * seqs)
                head = heads[m, pl.ds(2 * i, 2)].astype(F32).reshape(2 * seqs, 128)
                head = pltpu.roll(head, 128 - lead, 1)
                old = target[to, W - 128 :].astype(F32)
                target[to, W - 128 :] = jnp.where(lane < 128 - lead, old, head).astype(BF16)
                return 0

            lax.fori_loop(0, pairs, place, 0)

    def pieces(row, count, u, block, spot):
        r = pl.ds(row, count)
        to = pl.ds(0, count)
        if u == 0:
            return [(weights.at[0, r, pl.ds(0, W)], block.at[to, :])]
        return [
            (weights.at[0, r, pl.ds(W, full)], block.at[to, pl.ds(0, full)]),
            (weights.at[0, r, pl.ds(W + full, rest - full)], tails.at[spot, to, :]),
        ]

    rows_of = {0: (0, W), 1: (W, rest)}

    def w_plan(layer):
        mine, far = rows_of[layer], rows_of[1 - layer]
        plan = [
            (mine, layer, far, 1 - layer, wc.at[layer, 0], 2 * layer),
            (far, layer, mine, 1 - layer, wc.at[layer, 1], 2 * layer + 1),
        ]
        if layer == 1:
            plan.append((mine, 0, far, 1, wr1, 4))
        return plan

    late_row = (width - half) // 16 * 16
    late_shift = half - late_row
    late_plan = [
        ((0, W), 0, (late_row, width - late_row), 1, wc.at[0, 0], 0),
        ((0, W), 1, (late_row, width - late_row), 0, wc.at[0, 1], 1),
    ]
    slot_of = {0: 4, 1: 8, 2: 14}

    def local_w(plan, base, which):
        r, u, _, _, block, spot = plan[which]
        return [local(a, t, base + 2 * which + i) for i, (a, t) in enumerate(pieces(*r, u, block, spot))]

    def across_w(plan, base, which):
        _, _, r, u, block, spot = plan[which]
        return [across(a, t, base + 2 * which + i) for i, (a, t) in enumerate(pieces(*r, u, block, spot))]

    def start_local_w(layer, plan, base):
        @pl.when(section == layer)
        def _():
            for which in range(len(plan)):
                for made in local_w(plan, base, which):
                    made.start()

    def start_across_w(layer, plan, base):
        @pl.when(section == layer)
        def _():
            for which in range(len(plan)):
                for made in across_w(plan, base, which):
                    made.start()

    def last_units(block, spot):
        def body(i, _):
            r = pl.ds(aligned(i * 128, 128), 128)
            x = tails[spot, r, :].astype(F32)
            x = jnp.concatenate([x, jnp.zeros((128, 128 - x.shape[1]), F32)], axis=1)
            block[r, full:] = x.astype(BF16)
            return 0

        lax.fori_loop(0, W // 128, body, 0)

    def wait_w(layer, plan, base, which):
        _, own_u, _, far_u, block, spot = plan[which]

        @pl.when(section == layer)
        def _():
            for made in local_w(plan, base, which):
                made.wait()
            if own_u == 1:
                last_units(block, spot)

        @pl.when(section != layer)
        def _():
            for made in across_w(plan, base, which):
                made.wait_recv()
            if far_u == 1:
                last_units(block, spot)

    def done_w(layer, plan, base):
        @pl.when(section == layer)
        def _():
            for which in range(len(plan)):
                for made in across_w(plan, base, which):
                    made.wait_send()

    def heads_copy(source, slot):
        return across(source.at[:, :, :, pl.ds(0, 128)], heads, slot)

    def wait_heads(source, slot):
        @pl.when(section == 0)
        def _():
            heads_copy(source, slot).wait_recv()

        @pl.when(section == 1)
        def _():
            heads_copy(source, slot).wait_send()

    fetch(frames, 0).start()
    fetch(frames, 1).start()
    for layer in range(2):
        start_local_w(layer, w_plan(layer), slot_of[layer])

    barrier = pltpu.get_barrier_semaphore()
    greeted = [dict(sibling)]
    greeted += [at_plane(lax.rem(mp + k, np_)) for k in range(1, np_)]
    greeted += [at_z(lax.rem(mz + k, nz)) for k in range(1, nz)]
    greeted += [dict(axis["partner"], section=other) for axis in bits]
    for where in greeted:
        pl.semaphore_signal(barrier, inc=1, device_id=where, device_id_type=MESH)

    for k, (x, fill) in enumerate(((gains, 0.0), (shifts, -1e30), (recurs, 0.0))):
        vecs[section, k : k + 1, 0:width] = x[...]
        vecs[section, k : k + 1, width:] = jnp.full((1, 2 * W - width), fill, F32)
    vecs[section, 3:8, :] = jnp.zeros((5, 2 * W), F32)

    gap = jnp.zeros((W - rest, W), BF16)

    @pl.when(section == 0)
    def _():
        wc[0, 1, rest:, :] = gap
        wc[1, 1, rest:, :] = gap

    @pl.when(section == 1)
    def _():
        wc[0, 0, rest:, :] = gap
        wc[1, 0, rest:, :] = gap
        wr1[rest:, :] = gap

    for spot in (0, 2):
        tails[spot, rest:, :] = jnp.zeros((W - rest, rest - full), BF16)
    for spare in (f_own, p_own, g3.at[0], g3.at[1]):
        spare[sent_rows:, :] = jnp.zeros((spare.shape[0] - sent_rows, W), BF16)

    pl.semaphore_wait(barrier, len(greeted))

    @pl.when(section == 1)
    def _():
        heads_copy(frames, 1).start()

    start_across_w(0, w_plan(0), slot_of[0])
    send_vec = across(vecs.at[section], vecs.at[section], 3)
    send_vec.start()

    def stage_copy(where, rnd, slot, k, back):
        buf, parity, size, me, at, send, recv = where
        there = at(lax.rem(me + (size - k if back else k), size))
        ref = buf.at[parity, slot]
        return pltpu.make_async_remote_copy(
            src_ref=ref, dst_ref=ref, send_sem=send.at[rnd, k], recv_sem=recv.at[rnd, k],
            device_id=there, device_id_type=MESH,
        )

    def in_plane(buf, parity):
        return (buf, parity, np_, mp, at_plane, pl_send, pl_recv)

    def in_line(buf, parity):
        return (buf, parity, nz, mz, at_z, z_send, z_recv)

    def stage_start(where, rnd, value):
        buf, parity, size, me = where[:4]
        buf[parity, me] = value
        for k in range(1, size):
            stage_copy(where, rnd, me, k, False).start()

    def stage_wait(where, rnd):
        size, me = where[2:4]
        for k in range(1, size):
            stage_copy(where, rnd, me, k, False).wait_send()
            stage_copy(where, rnd, lax.rem(me + size - k, size), k, True).wait_recv()

    def add_slots(where):
        buf, parity, size = where[:3]
        total = buf[parity, 0]
        for k in range(1, size):
            total = total + buf[parity, k]
        return total

    groups = lengths.shape[1]
    s_at = lax.broadcasted_iota(jnp.int32, (seqs, groups), 0)
    g_at = lax.broadcasted_iota(jnp.int32, (seqs, groups), 1) * views
    there = (s_at >= g_at) & (s_at < g_at + views)
    position = lax.broadcasted_iota(jnp.int32, (seqs, 128), 1)
    local_counts = []
    for m in range(2):
        turn[...] = jnp.zeros_like(turn)
        turn[0:steps, 0:seqs] = masks[m].astype(F32)
        mask = turn[...].T[0:seqs]
        length = jnp.broadcast_to(lengths[m : m + 1, :], (seqs, groups)).astype(F32)
        limit = jnp.sum(jnp.where(there, length, 0.0), axis=1, keepdims=True)
        alive = (position.astype(F32) < limit) & ((mask > 0.0) | (position == 0))
        alive = jnp.where(position < steps, alive.astype(F32), 0.0)
        total = jnp.zeros((seqs, 128), F32)
        for t in range(steps):
            at = m * span + t * seqs
            cells = jnp.broadcast_to(alive[:, t : t + 1], (seqs, 128))
            live[at : at + seqs, :] = cells
            total = total + cells
        local_counts.append(jnp.sum(total, axis=0, keepdims=True))
    n_own = jnp.concatenate(local_counts * 4, axis=0)

    cnt_plane, cnt_line = in_plane(cnt_p, 0), in_line(cnt_z, 0)
    stage_start(cnt_plane, 0, n_own)

    def vec_of(layer, k):
        return vecs[layer, k : k + 1, pl.ds(aligned(section * W, W), W)]

    def matmul_to(out, a, w, first, m):
        r = pl.ds(m * span, span)

        def body(i, _):
            c = pl.ds(aligned(i * HALF, HALF), HALF)
            y = dot(a[r, :], w[:, c], ((1,), (0,)))
            out[r, c] = y if first else out[r, c] + y
            return 0

        lax.fori_loop(0, 2, body, 0)

    def packed(x, y):
        return jnp.concatenate([z[:, k * QUART : (k + 1) * QUART] for z in (x, y) for k in range(4)], axis=0)

    def unpacked(x):
        return jnp.concatenate([x[k : k + 1] for k in range(4)], axis=1)

    def merge_slots(where, counts_of):
        buf, parity, size = where[:3]
        s = [buf[parity, k, 0:4, :] for k in range(size)]
        q = [buf[parity, k, 4:8, :] for k in range(size)]
        n = [wide(counts_of(k), 2) for k in range(size)]
        total, squares, count = sum(s[1:], s[0]), sum(q[1:], q[0]), sum(n[1:], n[0])
        mean = total / count
        for k in range(size):
            d = s[k] / n[k] - mean
            squares = squares + n[k] * d * d
        return jnp.concatenate([total, squares], axis=0)

    def slim_round(which, m):
        return 1 + 2 * which + m, in_plane(slim_p, 2 * m + which % 2), in_line(slim_z, 2 * m + which % 2)

    def forward_stats(layer, m):
        start = jnp.sum(rows[layer, m * span : m * span + seqs, :], axis=0, keepdims=True) * (1.0 / seqs)

        def body(i, carry):
            s, q = carry
            r = pl.ds(aligned(m * span + i * (2 * seqs), 16), 2 * seqs)
            d = rows[layer, r, :] - start
            kept = wide(live[r, :], 8) * d
            return s + fold(kept), q + fold(kept * d)

        zero = jnp.zeros((8, W), F32)
        s, q = lax.fori_loop(0, pairs, body, (zero, zero))
        s, q = jnp.sum(s, axis=0, keepdims=True), jnp.sum(q, axis=0, keepdims=True)
        n = wide(local_counts[m], 8)
        rnd, plane, _ = slim_round(layer, m)
        stage_start(plane, rnd, packed(s + n * start, jnp.maximum(q - s * s / n, 0.0)))

    def forward_middle(layer, m):
        rnd, plane, line = slim_round(layer, m)
        stage_wait(plane, rnd)
        stage_start(line, rnd, merge_slots(plane, lambda k: cnt_p[0, k, m : m + 1, :]))

    def forward_end(layer, m):
        rnd, _, line = slim_round(layer, m)
        stage_wait(line, rnd)
        value = merge_slots(line, lambda k: cnt_z[0, k, m : m + 1, :])
        count = wide(counts[m : m + 1, :], 8)
        mean = unpacked(value[0:4]) / count
        scale = lax.rsqrt(unpacked(value[4:8]) / count + EPS)
        coef[layer, 2 * m : 2 * m + 1, :] = mean
        coef[layer, 2 * m + 1 : 2 * m + 2, :] = scale
        slope = vec_of(layer, 0) * scale
        coef[layer, 4 + 2 * m : 5 + 2 * m, :] = slope
        coef[layer, 5 + 2 * m : 6 + 2 * m, :] = vec_of(layer, 1) - mean * slope

    def forward_scan(layer, m, passes):
        rec = vec_of(layer, 2)
        slope = coef[layer, 4 + 2 * m : 5 + 2 * m, :]
        shift = coef[layer, 5 + 2 * m : 6 + 2 * m, :]

        def body(i, carry):
            h, level = carry
            r = pl.ds(aligned(m * span + i * (2 * seqs), 16), 2 * seqs)
            x = rows[layer, r, :] * slope + shift
            lv = wide(live[r, :], 8)
            alive = lv > 0.0
            both = []
            for k in range(2):
                part = slice(k * seqs, (k + 1) * seqs)
                z = x[part] + rec * h
                soft = jnp.maximum(z, 0.0) + jnp.log(1.0 + jnp.exp(-jnp.abs(z)))
                h = jnp.where(alive[part], soft, h)
                both.append(h)
            two = jnp.concatenate(both, axis=0)
            hid[layer, r, :] = two
            if passes:
                p_own[r, :] = two.astype(BF16)
                level = level + fold(lv * two)
            return h, level

        _, level = lax.fori_loop(0, pairs, body, (jnp.zeros((seqs, W), F32), jnp.zeros((8, W), F32)))
        if not passes:
            return None
        level = jnp.sum(level, axis=0, keepdims=True)
        levels[1:2, :] = level if m == 0 else levels[1:2, :] + level
        here = pl.ds(m * span, span)
        made = across(p_own.at[here, :], p_far.at[here, :], 18 + m)
        made.start()
        return made

    def backward_scan(layer, m, above, between=lambda: None):
        gain, shift, recur = vec_of(layer, 0), vec_of(layer, 1), vec_of(layer, 2)
        for lq in range(4):
            lanes = slice(lq * QUART, (lq + 1) * QUART)
            gq, sq, rec = gain[:, lanes], shift[:, lanes], recur[:, lanes]
            mean = coef[layer, 2 * m : 2 * m + 1, lanes]
            scale = coef[layer, 2 * m + 1 : 2 * m + 2, lanes]

            def body(i, carry):
                down, s1, s2, rsum, sqh, sqa = carry
                i = pairs - 1 - i
                start = m * span + i * (2 * seqs)
                r = pl.ds(aligned(start, 16), 2 * seqs)
                before = pl.ds(aligned(jnp.maximum(start - seqs, 0), 8), seqs)
                normed = (rows[layer, r, lanes] - mean) * scale
                drive = gq * normed + sq
                h2 = hid[layer, r, lanes]
                hb = jnp.where(i > 0, hid[layer, before, lanes], 0.0)
                lv = wide(live[r, :], 2)
                up = above[r, lanes].astype(F32)
                res = f_own[r, lanes].astype(F32)
                aux = res + h2 if layer == 1 else res
                sqh = sqh + fold(lv * (h2 * h2))
                sqa = sqa + fold(lv * (aux * aux))
                grads = [None, None]
                for k in (1, 0):
                    part = slice(k * seqs, (k + 1) * seqs)
                    prior = h2[0:seqs] if k == 1 else hb
                    slope = 0.5 + 0.5 * jnp.tanh(0.5 * (drive[part] + rec * prior))
                    total = up[part] + down
                    gd = lv[part] * slope * total
                    down = (1.0 - lv[part]) * total + rec * gd
                    grads[k] = gd
                    rsum = rsum + fold(gd * prior)
                gd2 = jnp.concatenate(grads, axis=0)
                hid[layer, r, lanes] = gd2
                return down, s1 + fold(gd2), s2 + fold(gd2 * normed), rsum, sqh, sqa

            z8 = jnp.zeros((8, QUART), F32)
            _, s1, s2, rsum, sqh, sqa = lax.fori_loop(
                0, pairs, body, (jnp.zeros((seqs, QUART), F32), z8, z8, z8, z8, z8)
            )
            for k, x in ((m, s1), (2 + m, s2)):
                tot[layer, k : k + 1, lanes] = jnp.sum(x, axis=0, keepdims=True)
            for k, x in ((4, rsum), (5, sqh), (6, sqa)):
                x = jnp.sum(x, axis=0, keepdims=True)
                tot[layer, k : k + 1, lanes] = x if m == 0 else tot[layer, k : k + 1, lanes] + x
            between()

    def backward_stats(layer, m):
        rnd, plane, _ = slim_round(3 - layer, m)
        stage_start(plane, rnd, packed(tot[layer, m : m + 1, :], tot[layer, 2 + m : 3 + m, :]))

    def backward_middle(layer, m):
        rnd, plane, line = slim_round(3 - layer, m)
        stage_wait(plane, rnd)
        stage_start(line, rnd, add_slots(plane))

    def backward_end(layer, m):
        rnd, _, line = slim_round(3 - layer, m)
        stage_wait(line, rnd)
        value = add_slots(line)
        tot[layer, m : m + 1, :] = unpacked(value[0:4])
        tot[layer, 2 + m : 3 + m, :] = unpacked(value[4:8])

    def grad_rows(layer, m, slot):
        gain = vec_of(layer, 0)
        for lh in range(2):
            lanes = slice(lh * HALF, (lh + 1) * HALF)
            mean = coef[layer, 2 * m : 2 * m + 1, lanes]
            scale = coef[layer, 2 * m + 1 : 2 * m + 2, lanes]
            count = wide(counts[m : m + 1, :], 4)
            first = tot[layer, m : m + 1, lanes] / count
            second = tot[layer, 2 + m : 3 + m, lanes] / count * scale
            k = scale * gain[:, lanes]

            def body(i, acc):
                r = pl.ds(aligned(m * span + i * (2 * seqs), 16), 2 * seqs)
                y = hid[layer, r, lanes] - first - (rows[layer, r, lanes] - mean) * second
                y = wide(live[r, :], 4) * (k * y)
                g3[0, r, lanes] = y.astype(BF16)
                return acc + fold(y)

            acc = lax.fori_loop(0, pairs, body, jnp.zeros((8, HALF), F32))
            acc = jnp.sum(acc, axis=0, keepdims=True)
            if m == 0:
                levels[4:5, lanes] = acc
            else:
                top = lax.broadcasted_iota(jnp.int32, (16, HALF), 0) == 0
                minus = jnp.where(top, -(levels[4:5, lanes] + acc), 0.0)
                g3[0, total_rows:sent_rows, lanes] = minus.astype(BF16)
        here = pl.ds(0, span) if m == 0 else pl.ds(span, span + 16)
        made = across(g3.at[0, here, :], g3.at[1, here, :], slot + m)
        made.start()
        return made

    sums_round = {1: (1, 10), 0: (0, 11)}

    def sums_start(layer):
        parity, rnd = sums_round[layer]
        own_sum = -g3[0, total_rows:sent_rows, :].astype(F32)[0:1]
        far_sum = -g3[1, total_rows:sent_rows, :].astype(F32)[0:1]
        value = jnp.concatenate([own_sum, far_sum, tot[layer, 4:7, :], jnp.zeros((3, W), F32)], axis=0)
        stage_start(in_plane(wide_p, parity), rnd, value)

    def sums_middle(layer):
        parity, rnd = sums_round[layer]
        stage_wait(in_plane(wide_p, parity), rnd)
        stage_start(in_line(wide_z, parity), rnd, add_slots(in_plane(wide_p, parity)))

    def sums_end(layer):
        parity, rnd = sums_round[layer]
        stage_wait(in_line(wide_z, parity), rnd)
        vtot[layer] = add_slots(in_line(wide_z, parity))
        tot[layer, 4:7, :] = vtot[layer, 2:5, :]
        tot[layer, 7:8, :] = wide(counts[0:1, :] + counts[1:2, :], 8)
        env["summed"].add(layer)

        @pl.when(section == layer)
        def _():
            pltpu.make_async_copy(tot.at[layer], v.at[section], v_sems.at[0]).start()

        @pl.when(section != layer)
        def _():
            v_across(layer).start()

    def v_across(layer):
        return pltpu.make_async_remote_copy(
            src_ref=tot.at[layer], dst_ref=v.at[section], send_sem=v_sems.at[1], recv_sem=v_sems.at[2],
            device_id=sibling, device_id_type=MESH,
        )

    def transpose(src, begin=0, end=W // 128):
        def body(j, _):
            c = pl.ds(aligned(j * 128, 128), 128)
            src_t[c, 0:total_rows] = src[0:total_rows, c].T
            return 0

        lax.fori_loop(begin, end, body, 0)

    def transpose_level(src, layer):
        top = lax.broadcasted_iota(jnp.int32, (16, W), 0) == 0
        src[total_rows:sent_rows, :] = jnp.where(top, levels[2 + layer : 3 + layer, :], 0.0).astype(BF16)

        def body(j, _):
            c = pl.ds(aligned(j * 128, 128), 128)
            src_t[c, total_rows:] = src[total_rows:, c].T
            level = src[total_rows:sent_rows, c].astype(F32)[0:1]
            column[layer, c, :] = jnp.broadcast_to(level, (128, 128)).T.astype(BF16)
            return 0

        lax.fori_loop(0, W // 128, body, 0)

    def weight_part(block, grads, c):
        lanes = pl.ds(c * HALF, HALF)

        def body(j, _):
            r = pl.ds(aligned(j * HALF, HALF), HALF)
            block[r, lanes] = dot(src_t[r, :], grads[:, lanes], ((1,), (0,))).astype(BF16)
            return 0

        lax.fori_loop(0, W // HALF, body, 0)

    def source_grad(store, w_own, w_far, between):
        for m in range(2):
            r = pl.ds(m * span, span)

            def body(i, _):
                c = pl.ds(aligned(i * HALF, HALF), HALF)
                y = dot(g3[0, r, :], w_own[c, :], ((1,), (1,))) + dot(g3[1, r, :], w_far[c, :], ((1,), (1,)))
                store(r, c, y)
                return 0

            lax.fori_loop(0, 2, body, 0)
            between()

    env = dict(summed=set(), vtot=vtot, column=column, space=space, ar_send=ar_send, ar_recv=ar_recv,
               ar_other=ar_other, o=o, section=section, here={"batch": b})
    xs = [a for a in bits if a["link"] == "x"]
    ys = [a for a in bits if a["link"] == "y"]
    zs = [a for a in bits if a["link"] == "z"]
    orders = (xs + ys + zs, ys + xs + zs)
    blocks = {
        (1, 0): f_far.at[pl.ds(0, W), :],
        (1, 1): p_far.at[pl.ds(0, W), :],
        (0, 0): wc.at[1, 1],
        (0, 1): wr1,
    }
    parts = {}
    for layer in (1, 0):
        for index in range(4):
            part, side = index // 2, index % 2

            def lane_of(sec, part=part, side=side):
                return (sec if part == 0 else 1 - sec) * W + side * HALF

            block = blocks[layer, part].at[:, pl.ds(side * HALF, HALF)]
            parts[layer, index] = Reduction(env, layer, index, block, orders, lane_of)
    order = Order()

    def weight_grads(layer, between):
        for part in range(2):
            if part == 1:
                between()
            for c in range(2):
                weight_part(blocks[layer, part], g3.at[part], c)
                order.work(2.0)
                order.begin(parts[layer, 2 * part + c], 0)
                order.begin(parts[layer, 2 * part + c], 1)

    def arrived(layer, sends):
        for made in sends:
            made.wait()
        sums_start(layer)

    send_f = []
    for m in range(2):
        by_units(frames, f_own, m)
        fetch(grad_out, m).start()
        if m == 0:
            wait_heads(frames, 1)
        patch_heads(f_own, m)
        here = pl.ds(m * span, span)
        made = across(f_own.at[here, :], f_far.at[here, :], (0, 24)[m])
        made.start()
        send_f.append(made)
    start_across_w(1, w_plan(1), slot_of[1])
    stage_wait(cnt_plane, 0)
    stage_start(cnt_line, 0, add_slots(cnt_plane))
    wait_w(0, w_plan(0), slot_of[0], 0)
    matmul_to(rows.at[0], f_own, wc.at[0, 0], True, 0)
    matmul_to(rows.at[0], f_own, wc.at[0, 0], True, 1)
    wait_w(0, w_plan(0), slot_of[0], 1)
    send_f[0].wait()
    matmul_to(rows.at[0], f_far, wc.at[0, 1], False, 0)
    forward_stats(0, 0)
    send_f[1].wait()

    @pl.when(section == 1)
    def _():
        heads_copy(grad_out, 2).start()

    matmul_to(rows.at[0], f_far, wc.at[0, 1], False, 1)
    forward_middle(0, 0)
    forward_stats(0, 1)
    send_vec.wait_send()
    across(vecs.at[other], vecs.at[other], 3).wait_recv()
    stage_wait(cnt_line, 0)
    counts[...] = add_slots(cnt_line)
    forward_end(0, 0)
    sends = [forward_scan(0, 0, True)]
    forward_middle(0, 1)
    by_units(grad_out, g3.at[1], 0)
    wait_heads(grad_out, 2)
    patch_heads(g3.at[1], 0)
    forward_end(0, 1)
    sends.append(forward_scan(0, 1, True))
    wait_w(1, w_plan(1), slot_of[1], 0)
    matmul_to(rows.at[1], p_own, wc.at[1, 0], True, 0)
    wait_w(1, w_plan(1), slot_of[1], 1)
    sends[0].wait()
    matmul_to(rows.at[1], p_far, wc.at[1, 1], False, 0)
    forward_stats(1, 0)
    matmul_to(rows.at[1], p_own, wc.at[1, 0], True, 1)
    forward_middle(1, 0)
    sends[1].wait()
    matmul_to(rows.at[1], p_far, wc.at[1, 1], False, 1)
    forward_stats(1, 1)
    done_w(0, w_plan(0), slot_of[0])

    start_local_w(0, late_plan, slot_of[2])
    start_across_w(0, late_plan, slot_of[2])

    @pl.when(section == 1)
    def _():
        wc[0, 1, width - late_row :, :] = jnp.zeros((W - width + late_row, W), BF16)

    def source_level():
        def body(i, acc):
            r = pl.ds(aligned(i * (2 * seqs), 16), 2 * seqs)
            return acc + fold(wide(live[r, :], 8) * f_own[r, :].astype(F32))

        acc = lax.fori_loop(0, 2 * pairs, body, jnp.zeros((8, W), F32))
        levels[0:1, :] = jnp.sum(acc, axis=0, keepdims=True)

    forward_end(1, 0)
    forward_scan(1, 0, False)
    forward_middle(1, 1)
    by_units(grad_out, g3.at[1], 1)
    patch_heads(g3.at[1], 1)
    source_level()
    forward_end(1, 1)
    level_plane, level_line = in_plane(wide_p, 0), in_line(wide_z, 0)
    stage_start(level_plane, 9, jnp.concatenate([levels[0:2, :], jnp.zeros((6, W), F32)], axis=0))
    forward_scan(1, 1, False)
    backward_scan(1, 0, g3.at[1])
    backward_stats(1, 0)
    stage_wait(level_plane, 9)
    stage_start(level_line, 9, add_slots(level_plane))
    backward_scan(1, 1, g3.at[1])
    backward_stats(1, 1)
    backward_middle(1, 0)
    pl.semaphore_signal(credit.at[0], inc=1, device_id=sibling, device_id_type=MESH)
    transpose(p_own, 0, W // 256)
    backward_middle(1, 1)
    backward_end(1, 0)
    pl.semaphore_wait(credit.at[0], 1)
    sends = [grad_rows(1, 0, 20)]
    transpose(p_own, W // 256)
    stage_wait(level_line, 9)
    levels[2:4, :] = (add_slots(level_line) / wide(counts[0:1, :] + counts[1:2, :], 8))[0:2]
    transpose_level(p_own, 1)
    backward_end(1, 1)
    sends.append(grad_rows(1, 1, 20))
    weight_grads(1, lambda: arrived(1, sends))
    wait_w(1, w_plan(1), slot_of[1], 2)
    done_w(1, w_plan(1), slot_of[1])

    def keep_down(r, c, y):
        p_own[r, c] = y.astype(BF16)

    source_grad(keep_down, wc.at[1, 0], wr1, lambda: order.work(3.0))
    pl.semaphore_signal(credit.at[1], inc=1, device_id=sibling, device_id_type=MESH)
    sums_middle(1)
    backward_scan(0, 0, p_own, lambda: order.work(0.6))
    backward_stats(0, 0)
    backward_scan(0, 1, p_own, lambda: order.work(0.6))
    backward_stats(0, 1)
    backward_middle(0, 0)
    sums_end(1)
    transpose(f_own)
    transpose_level(f_own, 0)
    backward_middle(0, 1)
    order.work(3.0)
    backward_end(0, 0)
    pl.semaphore_wait(credit.at[1], 1)
    sends = [grad_rows(0, 0, 22)]
    backward_end(0, 1)
    sends.append(grad_rows(0, 1, 22))
    order.work(2.0)
    weight_grads(0, lambda: arrived(0, sends))
    wait_w(0, late_plan, slot_of[2], 0)
    wait_w(0, late_plan, slot_of[2], 1)
    done_w(0, late_plan, slot_of[2])

    def keep_source(r, c, y):
        rows[0, r, c] = y

    fetch(grad_out, 0).start()
    fetch(grad_out, 1).start()
    sums_middle(0)
    source_grad(keep_source, wc.at[0, 0], wc.at[0, 1], lambda: order.work(3.0))
    sums_end(0)

    def give(m):
        return pltpu.make_async_copy(staged.at[m], gf.at[m], stage_sem.at[m])

    for m in range(2):
        fetch(grad_out, m).wait()

        def finish_frames(i, _, m=m):
            straight = staged[m, pl.ds(2 * i, 2)].astype(F32).reshape(2 * seqs, half)
            y = rows[0, pl.ds(aligned(m * span + 2 * i * seqs, 8), 2 * seqs), :]
            y = jnp.where(section == 0, y[:, :half], y[:, late_shift : late_shift + half])
            staged[m, pl.ds(2 * i, 2)] = (y + straight).reshape(2, seqs, half).astype(BF16)
            return 0

        lax.fori_loop(0, pairs, finish_frames, 0)
        give(m).start()
        order.work(2.0)
    order.drain()
    for m in range(2):
        give(m).wait()

    for layer in range(2):

        @pl.when(section == layer)
        def _(layer=layer):
            pltpu.make_async_copy(tot.at[layer], v.at[section], v_sems.at[0]).wait()
            pltpu.make_async_remote_copy(
                src_ref=tot.at[layer], dst_ref=v.at[other], send_sem=v_sems.at[1], recv_sem=v_sems.at[2],
                device_id=sibling, device_id_type=MESH,
            ).wait_recv()

        @pl.when(section != layer)
        def _(layer=layer):
            v_across(layer).wait_send()

    own_part, far_part = v[section], v[other]
    first = jnp.where(section == 0, own_part, far_part)
    second = jnp.where(section == 0, far_part, own_part)
    for row, terms in ((0, (2, 3)), (1, (0, 1)), (2, (4,))):
        for lane, x in ((0, first), (W, second)):
            total = x[terms[0] : terms[0] + 1, :]
            for k in terms[1:]:
                total = total + x[k : k + 1, :]
            vectors[row : row + 1, lane : lane + W] = total
    squares = jnp.sum(first[5:7, :] + second[5:7, :], axis=1, keepdims=True)
    root = jnp.sqrt(squares / (first[7:8, 0:1] * width))
    for k in range(2):
        vectors[3 + k : 4 + k, :] = jnp.broadcast_to(root[k : k + 1], (1, 2 * W))
    vectors[5:8, :] = jnp.zeros((3, 2 * W), F32)


def write_results(o, gf, vectors, grad_weight, grad_frames, grad_gains, grad_shifts, grad_recurs, table):
    width = grad_weight.shape[2]
    grad_weight[0] = o[...][:, :width].astype(F32)
    grad_frames[...] = gf[...]

    @pl.when(pl.program_id(0) == 0)
    def _():
        for k, out in enumerate((grad_gains, grad_shifts, grad_recurs)):
            out[...] = vectors[k : k + 1, 0:width]
        table[...] = jnp.concatenate([vectors[3:4, 0:1], vectors[4:5, 0:1]], axis=1)


def results(o, gf, vectors):
    micro, steps, seqs, half = gf.shape
    width = 2 * half
    count = W * 2 // 256
    frames = micro * steps // count
    whole = lambda shape: pl.BlockSpec(shape, lambda i: (0, 0))
    out = pl.pallas_call(
        write_results,
        grid=(count,),
        in_specs=[
            pl.BlockSpec((256, 2 * W), lambda i: (i, 0)),
            pl.BlockSpec((frames, seqs, half), lambda i: (i, 0, 0)),
            whole((8, 2 * W)),
        ],
        out_specs=(
            pl.BlockSpec((1, 256, width), lambda i: (0, i, 0)),
            pl.BlockSpec((frames, seqs, half), lambda i: (i, 0, 0)),
            whole((1, width)),
            whole((1, width)),
            whole((1, width)),
            whole((1, 2)),
        ),
        out_shape=(
            jax.ShapeDtypeStruct((1, width, width), F32),
            jax.ShapeDtypeStruct((micro * steps, seqs, half), BF16),
            jax.ShapeDtypeStruct((1, width), F32),
            jax.ShapeDtypeStruct((1, width), F32),
            jax.ShapeDtypeStruct((1, width), F32),
            jax.ShapeDtypeStruct((1, 2), F32),
        ),
        compiler_params=pltpu.CompilerParams(vmem_limit_bytes=64 * 1024 * 1024),
    )(o.reshape(2 * W, 2 * W), gf.reshape(micro * steps, seqs, half), vectors)
    return out[1].reshape(gf.shape), out[0], *out[2:]


def whole_step(dims, frames, grad_out, weights, gains, shifts, recurs, lengths, masks):
    nz, ny, nx = dims
    micro, steps, seqs, half = frames.shape
    width = 2 * half
    views = seqs // lengths.shape[1]
    rows = micro * steps * seqs
    np_ = ny * nx
    wide_rows = (rows + 16 + 127) // 128 * 128
    depth = (nx * ny * nz - 1).bit_length()
    any_ = pl.BlockSpec(memory_space=pl.ANY)
    held = pl.BlockSpec(memory_space=pltpu.VMEM)
    dma = pltpu.SemaphoreType.DMA
    return pl.pallas_call(
        functools.partial(kernel, dims, steps, seqs, views),
        out_shape=(
            jax.ShapeDtypeStruct((2, W, 2 * W), BF16),
            jax.ShapeDtypeStruct(frames.shape, BF16),
            jax.ShapeDtypeStruct((8, 2 * W), F32),
        ),
        in_specs=[any_] * 3 + [held] * 5,
        out_specs=(any_, any_, held),
        scratch_shapes=[
            pltpu.VMEM((wide_rows, W), BF16),
            pltpu.VMEM((rows, W), BF16),
            pltpu.VMEM((wide_rows, W), BF16),
            pltpu.VMEM((rows, W), BF16),
            pltpu.VMEM((2, wide_rows, W), BF16),
            pltpu.VMEM((2, 2, W, W), BF16),
            pltpu.VMEM((W, W), BF16),
            pltpu.VMEM((W, wide_rows), BF16),
            pltpu.VMEM((rows, 128), F32),
            pltpu.VMEM((128, 128), F32),
            pltpu.VMEM(frames.shape, BF16),
            pltpu.VMEM((micro, steps, seqs, 128), BF16),
            pltpu.VMEM((5, W, (width - W) % 128), BF16),
            pltpu.VMEM((2, 8, W), F32),
            pltpu.VMEM((2, 8, 2 * W), F32),
            pltpu.VMEM((2, rows, W), F32),
            pltpu.VMEM((2, rows, W), F32),
            pltpu.VMEM((2, 8, W), F32),
            pltpu.VMEM((2, 8, W), F32),
            pltpu.VMEM((2, 8, W), F32),
            pltpu.VMEM((8, W), F32),
            pltpu.VMEM((2, W, 128), BF16),
            pltpu.VMEM((8, 128), F32),
            pltpu.VMEM((1, np_, 8, 128), F32),
            pltpu.VMEM((1, nz, 8, 128), F32),
            pltpu.VMEM((4, np_, 8, QUART), F32),
            pltpu.VMEM((4, nz, 8, QUART), F32),
            pltpu.VMEM((2, np_, 8, W), F32),
            pltpu.VMEM((2, nz, 8, W), F32),
            pltpu.VMEM((2, 4, W, HALF), BF16),
            dma((3, 25)),
            dma((3,)),
            dma((2,)),
            pltpu.SemaphoreType.REGULAR((2,)),
            dma((12, max(np_, 2))),
            dma((12, max(np_, 2))),
            dma((12, max(nz, 2))),
            dma((12, max(nz, 2))),
            dma((2, 4, 2, 2 * depth + 2)),
            dma((2, 4, 2, 2 * depth + 2)),
            dma((2, 4, 2, 2)),
        ],
        compiler_params=pltpu.CompilerParams(
            collective_id=0, has_side_effects=True, vmem_limit_bytes=64 * 1024 * 1024
        ),
    )(frames, grad_out, weights, gains, shifts, recurs, lengths, masks)


def shards(dims, frames, grad_out, weights, gains, shifts, recurs, lengths, masks):
    return results(*whole_step(dims, frames, grad_out, weights, gains, shifts, recurs, lengths, masks))


def solution(mesh):
    in_specs = (
        P(None, None, "batch", "section"),
        P(None, None, "batch", "section"),
        P("section", None, None),
        P("section", None),
        P("section", None),
        P("section", None),
        P(None, "batch"),
        P(None, None, "batch"),
    )
    out_specs = (
        P(None, None, "batch", "section"),
        P("section", None, None),
        P("section", None),
        P("section", None),
        P("section", None),
        P("section", None),
    )
    body = functools.partial(shards, grid_of(mesh.shape["batch"]))
    return jax.shard_map(body, mesh=mesh, in_specs=in_specs, out_specs=out_specs, check_vma=False)
```

```python
import functools

import jax
import jax.numpy as jnp
from jax import lax
from jax.experimental import pallas as pl
from jax.experimental.pallas import tpu as pltpu
from jax.sharding import PartitionSpec as P

EPS = 1e-05
W = 1024
HALF = W // 2
QUART = W // 4
PAIRS = 1
PART = W // PAIRS // 2
MESH = pl.DeviceIdType.MESH
F32 = jnp.float32
BF16 = jnp.bfloat16


def grid_of(size):
    if size == 16:
        return (4, 2, 2)
    if size == 128:
        return (8, 4, 4)
    return (size, 1, 1)


def aligned(x, k):
    return pl.multiple_of(x, k)


def wide(x, reps):
    return jnp.concatenate([x] * reps, axis=1)


def fold(x):
    rows = x.shape[0]
    total = x[0:8]
    for k in range(8, rows, 8):
        total = total + x[k : k + 8]
    return total


def dot(a, b, dims):
    return lax.dot_general(a, b, (dims, ((), ())), preferred_element_type=F32)


class Reduction:
    def __init__(self, env, layer, index, block, orders, lane_of):
        self.env, self.layer, self.index, self.block, self.orders = env, layer, index, block, orders
        self.lane_of = lane_of
        self.space = env["space"].at[layer, index]
        self.depth = len(orders[0])
        self.regions = [self.halves(i, order) for i, order in enumerate(orders)]
        self.step = 0
        self.waits = []
        depth = self.depth
        self.steps = [functools.partial(self.scatter, 0)]
        self.steps += [functools.partial(self.scatter, k) for k in range(1, depth)]
        self.steps += [functools.partial(self.gather, k) for k in range(depth - 1, 0, -1)]
        self.steps += [self.give, self.finish]

    def halves(self, i, order):
        row, rows, lane, lanes = 0, W, i * PART, PART
        out = [(row, rows, lane, lanes)]
        for axis in order:
            if rows > 16:
                rows //= 2
                row = row + axis["bit"] * rows
            else:
                lanes //= 2
                lane = lane + axis["bit"] * lanes
            out.append((row, rows, lane, lanes))
        return out

    @property
    def free_to_go(self):
        return self.step != self.depth or self.layer in self.env["summed"]

    @property
    def done(self):
        return self.step >= len(self.steps)

    def advance(self):
        self.sent = []
        self.steps[self.step]()
        self.step += 1
        return self.sent

    def remote(self, i, src, dst, slot, where, recv=None):
        sems = (self.layer, self.index, i, slot)
        return pltpu.make_async_remote_copy(
            src_ref=src, dst_ref=dst, send_sem=self.env["ar_send"].at[sems],
            recv_sem=self.env["ar_recv"].at[sems] if recv is None else recv, device_id=where, device_id_type=MESH,
        )

    def wait(self):
        for made, came in self.waits:
            made.wait_send()
            came.wait_recv()
        self.waits = []

    def came_at(self, i, k):
        row = sum(r[1] for r in self.regions[i][1 : k + 1])
        _, rows, _, lanes = self.regions[i][k + 1]
        return row, rows, i * PART, lanes

    def scatter(self, k):
        if k > 0:
            self.wait()
            self.add(k - 1)
        for i, order in enumerate(self.orders):
            self.scatter_part(i, k, order[k])

    def start_part(self, i):
        self.sent = []
        self.scatter_part(i, 0, self.orders[i][0])
        if i == 1:
            self.step = 1
        return self.sent

    def scatter_part(self, i, k, axis):
        row, rows, lane, lanes = self.regions[i][k]
        _, rows2, _, lanes2 = self.regions[i][k + 1]
        give_row = row + (1 - axis["bit"]) * rows2 if rows2 < rows else row
        give_lane = lane if rows2 < rows else lane + (1 - axis["bit"]) * lanes2
        src = self.block.at[pl.ds(aligned(give_row, 16), rows2), pl.ds(aligned(give_lane, 128), lanes2)]
        at, n, at_lane, n_lanes = self.came_at(i, k)
        dst = self.space.at[pl.ds(at, n), pl.ds(at_lane, n_lanes)]
        made = self.remote(i, src, dst, k, axis["partner"])
        made.start()
        self.waits.append((made, made))
        self.sent.append((axis["link"], rows2 * lanes2 * 2))

    def add(self, k, last=False):
        rows = self.regions[0][k + 1][1]
        size = min(rows, 32)
        out = []
        for i in range(2):
            row, _, lane, lanes = self.regions[i][k + 1]
            at, _, at_lane, _ = self.came_at(i, k)
            lane = aligned(lane, 128)
            extra = None
            if last:
                part = self.index // PAIRS
                first = aligned((self.index % PAIRS) * 2 * PART + lane, 128)
                extra = self.env["vtot"][self.layer, part : part + 1, pl.ds(first, lanes)]
            out.append((row, lane, lanes, at, at_lane, self.local(i, k + 1)[0], extra))

        def body(j, _):
            for row, lane, lanes, at, at_lane, home, extra in out:
                here = pl.ds(aligned(row + j * size, 16), size)
                total = self.block[here, pl.ds(lane, lanes)].astype(F32)
                total = total + self.space[pl.ds(aligned(at + j * size, 16), size), pl.ds(at_lane, lanes)].astype(F32)
                if last:
                    column = self.env["column"][self.layer, here, :].astype(F32)
                    total = total + wide(column, lanes // 128) * extra
                    to = pl.ds(aligned(home + j * size, 16), size)
                    self.space[to, pl.ds(lane, lanes)] = total.astype(BF16)
                else:
                    self.block[here, pl.ds(lane, lanes)] = total.astype(BF16)
            return 0

        lax.fori_loop(0, rows // size, body, 0)

    def local(self, i, k):
        row, rows, lane, lanes = self.regions[i][k]
        return row - self.regions[i][1][0], rows, lane, lanes

    def gather(self, k):
        self.wait()
        if k == self.depth - 1:
            self.add(k, last=True)
        for i, order in enumerate(self.orders):
            axis = order[k]
            row, rows, lane, lanes = self.local(i, k + 1)
            row0, rows0, lane0, lanes0 = self.local(i, k)
            if rows0 > rows:
                far = (row0 + (1 - axis["bit"]) * rows, rows, lane, lanes)
            else:
                far = (row, rows, lane0 + (1 - axis["bit"]) * lanes, lanes)
            refs = [
                self.space.at[pl.ds(aligned(r, 16), n), pl.ds(aligned(c, 128), w)]
                for r, n, c, w in ((row, rows, lane, lanes), far)
            ]
            made = self.remote(i, refs[0], refs[0], self.depth + k, axis["partner"])
            made.start()
            self.waits.append((made, self.remote(i, refs[1], refs[1], self.depth + k, axis["partner"])))
            self.sent.append((axis["link"], rows * lanes * 2))

    def result(self, i, bit, section):
        rows = self.regions[i][1][1]
        lane = aligned(self.lane_of(section) + i * PART, PART)
        return self.env["o"].at[section, pl.ds(aligned(bit * rows, 16), rows), pl.ds(lane, PART)]

    def gathered(self, i):
        return self.space.at[pl.ds(0, self.regions[i][1][1]), pl.ds(i * PART, PART)]

    def deliver(self, i, near, straight):
        axis, section = self.orders[i][0], self.env["section"]
        slot = 2 * self.depth + (0 if near else 1)
        recv = None if straight else self.env["ar_other"].at[self.layer, self.index, i, 0 if near else 1]
        where = dict(self.env["here"] if near else axis["partner"], section=self.layer)
        return self.remote(i, self.gathered(i), self.result(i, axis["bit"], section), slot, where, recv)

    def arrival(self, i, near, straight):
        axis, section = self.orders[i][0], self.env["section"]
        slot = 2 * self.depth + (0 if near else 1)
        recv = None if straight else self.env["ar_other"].at[self.layer, self.index, i, 0 if near else 1]
        bit = axis["bit"] if near else 1 - axis["bit"]
        frm = section if straight else 1 - section
        where = dict(self.env["here"] if near else axis["partner"], section=frm)
        return self.remote(i, self.gathered(i), self.result(i, bit, frm), slot, where, recv)

    def kept(self, i):
        sem = self.env["ar_recv"].at[self.layer, self.index, i, 2 * self.depth]
        return pltpu.make_async_copy(
            self.gathered(i), self.result(i, self.orders[i][0]["bit"], self.env["section"]), sem
        )

    def give(self):
        self.wait()

        @pl.when(self.env["section"] == self.layer)
        def _():
            for i in range(2):
                self.deliver(i, False, True).start()
                self.kept(i).start()

        @pl.when(self.env["section"] != self.layer)
        def _():
            for i in range(2):
                self.deliver(i, False, False).start()
                self.deliver(i, True, False).start()

        for i, order in enumerate(self.orders):
            self.sent.append((order[0]["link"], self.regions[i][1][1] * PART * 2))

    def finish(self):
        @pl.when(self.env["section"] == self.layer)
        def _():
            for i in range(2):
                self.kept(i).wait()
                self.deliver(i, False, True).wait_send()
                self.arrival(i, False, True).wait_recv()
                self.arrival(i, True, False).wait_recv()
                self.arrival(i, False, False).wait_recv()

        @pl.when(self.env["section"] != self.layer)
        def _():
            for i in range(2):
                self.deliver(i, False, False).wait_send()
                self.deliver(i, True, False).wait_send()


class Order:
    RATE, HOP = 70e3, 1.8

    def __init__(self):
        self.now = 0.0
        self.free = {}
        self.going = []

    def sent(self, copies):
        end = self.now
        for link, size in copies:
            self.free[link] = max(self.now, self.free.get(link, 0.0)) + size / self.RATE
            end = max(end, self.free[link])
        return end + self.HOP

    def begin(self, one, i):
        end = self.sent(one.start_part(i))
        if i == 0:
            one.due = end
        else:
            one.due = max(one.due, end)
            self.going.append(one)

    def advance(self, one):
        self.now = max(self.now, one.due) + 0.4
        one.due = self.sent(one.advance())
        if one.done:
            self.going.remove(one)

    def work(self, cost):
        self.now += cost
        while True:
            due = [x for x in self.going if x.due <= self.now and x.free_to_go]
            if not due:
                return
            self.advance(min(due, key=lambda x: x.due))

    def drain(self):
        while self.going:
            self.advance(min(self.going, key=lambda x: x.due))


def kernel(dims, steps, seqs, views, frames, grad_out, weights, gains, shifts, recurs, lengths, masks, o, gf, vectors, f_own, f_far, p_own, p_far, g3, wc, wr1, src_t, live, turn,
           staged, heads, tails, v, vecs, rows, hid, coef, tot, vtot, levels, column, counts, cnt_p, cnt_z, slim_p, slim_z,
           wide_p, wide_z, space, sems, v_sems, stage_sem, credit, pl_send, pl_recv, z_send, z_recv, ar_send, ar_recv,
           ar_other):
    nz, ny, nx = dims
    np_ = ny * nx
    span = steps * seqs
    total_rows = 2 * span
    sent_rows = total_rows + 16
    pairs = steps // 2
    section = lax.axis_index("section")
    other = 1 - section
    b = lax.axis_index("batch")
    mp = lax.rem(b, np_)
    mz = b // np_

    def at_plane(i):
        return {"batch": b - mp + i}

    def at_z(i):
        return {"batch": b + (i - mz) * np_}

    bits = []
    for link, count, stride in (("x", nx, 1), ("y", ny, nx), ("z", nz, np_)):
        while count > 1:
            bit = lax.rem(b // stride, 2)
            bits.append(dict(bit=bit, partner={"batch": b + (1 - 2 * bit) * stride}, link=link))
            count //= 2
            stride *= 2
    sibling = {"section": other}

    def local(src, dst, slot):
        return pltpu.make_async_copy(src, dst, sems.at[0, slot])

    def across(src, dst, slot):
        return pltpu.make_async_remote_copy(
            src_ref=src, dst_ref=dst, send_sem=sems.at[1, slot], recv_sem=sems.at[2, slot],
            device_id=sibling, device_id_type=MESH,
        )

    half = frames.shape[3]
    width = 2 * half
    lead = W - half
    rest = width - W
    full = rest // 128 * 128

    def fetch(source, m):
        return pltpu.make_async_copy(source.at[m], staged.at[m], stage_sem.at[m])

    def by_units(source, target, m):
        fetch(source, m).wait()

        @pl.when(section == 0)
        def _():
            pad = jnp.zeros((2 * seqs, lead), F32)

            def place(i, _):
                x = staged[m, pl.ds(2 * i, 2)].astype(F32).reshape(2 * seqs, half)
                to = pl.ds(aligned(m * span + 2 * i * seqs, 16), 2 * seqs)
                target[to, :] = jnp.concatenate([x, pad], axis=1).astype(BF16)
                return 0

            lax.fori_loop(0, pairs, place, 0)

        @pl.when(section == 1)
        def _():
            pad = jnp.zeros((2 * seqs, 2 * lead), F32)

            def place(i, _):
                x = staged[m, pl.ds(2 * i, 2)].astype(F32).reshape(2 * seqs, half)
                to = pl.ds(aligned(m * span + 2 * i * seqs, 16), 2 * seqs)
                target[to, :] = jnp.concatenate([x[:, lead:], pad], axis=1).astype(BF16)
                return 0

            lax.fori_loop(0, pairs, place, 0)

    def patch_heads(target, m):
        @pl.when(section == 0)
        def _():
            lane = lax.broadcasted_iota(jnp.int32, (2 * seqs, 128), 1)

            def place(i, _):
                to = pl.ds(aligned(m * span + 2 * i * seqs, 16), 2 * seqs)
                head = heads[m, pl.ds(2 * i, 2)].astype(F32).reshape(2 * seqs, 128)
                head = pltpu.roll(head, 128 - lead, 1)
                old = target[to, W - 128 :].astype(F32)
                target[to, W - 128 :] = jnp.where(lane < 128 - lead, old, head).astype(BF16)
                return 0

            lax.fori_loop(0, pairs, place, 0)

    def pieces(row, count, u, block, spot):
        r = pl.ds(row, count)
        to = pl.ds(0, count)
        if u == 0:
            return [(weights.at[0, r, pl.ds(0, W)], block.at[to, :])]
        return [
            (weights.at[0, r, pl.ds(W, full)], block.at[to, pl.ds(0, full)]),
            (weights.at[0, r, pl.ds(W + full, rest - full)], tails.at[spot, to, :]),
        ]

    rows_of = {0: (0, W), 1: (W, rest)}

    def w_plan(layer):
        mine, far = rows_of[layer], rows_of[1 - layer]
        plan = [
            (mine, layer, far, 1 - layer, wc.at[layer, 0], 2 * layer),
            (far, layer, mine, 1 - layer, wc.at[layer, 1], 2 * layer + 1),
        ]
        if layer == 1:
            plan.append((mine, 0, far, 1, wr1, 4))
        return plan

    late_row = (width - half) // 16 * 16
    late_shift = half - late_row
    late_plan = [
        ((0, W), 0, (late_row, width - late_row), 1, wc.at[0, 0], 0),
        ((0, W), 1, (late_row, width - late_row), 0, wc.at[0, 1], 1),
    ]
    slot_of = {0: 4, 1: 8, 2: 14}

    def local_w(plan, base, which):
        r, u, _, _, block, spot = plan[which]
        return [local(a, t, base + 2 * which + i) for i, (a, t) in enumerate(pieces(*r, u, block, spot))]

    def across_w(plan, base, which):
        _, _, r, u, block, spot = plan[which]
        return [across(a, t, base + 2 * which + i) for i, (a, t) in enumerate(pieces(*r, u, block, spot))]

    def start_local_w(layer, plan, base):
        @pl.when(section == layer)
        def _():
            for which in range(len(plan)):
                for made in local_w(plan, base, which):
                    made.start()

    def start_across_w(layer, plan, base):
        @pl.when(section == layer)
        def _():
            for which in range(len(plan)):
                for made in across_w(plan, base, which):
                    made.start()

    def last_units(block, spot):
        def body(i, _):
            r = pl.ds(aligned(i * 128, 128), 128)
            x = tails[spot, r, :].astype(F32)
            x = jnp.concatenate([x, jnp.zeros((128, 128 - x.shape[1]), F32)], axis=1)
            block[r, full:] = x.astype(BF16)
            return 0

        lax.fori_loop(0, W // 128, body, 0)

    def wait_w(layer, plan, base, which):
        _, own_u, _, far_u, block, spot = plan[which]

        @pl.when(section == layer)
        def _():
            for made in local_w(plan, base, which):
                made.wait()
            if own_u == 1:
                last_units(block, spot)

        @pl.when(section != layer)
        def _():
            for made in across_w(plan, base, which):
                made.wait_recv()
            if far_u == 1:
                last_units(block, spot)

    def done_w(layer, plan, base):
        @pl.when(section == layer)
        def _():
            for which in range(len(plan)):
                for made in across_w(plan, base, which):
                    made.wait_send()

    def heads_copy(source, slot):
        return across(source.at[:, :, :, pl.ds(0, 128)], heads, slot)

    def wait_heads(source, slot):
        @pl.when(section == 0)
        def _():
            heads_copy(source, slot).wait_recv()

        @pl.when(section == 1)
        def _():
            heads_copy(source, slot).wait_send()

    fetch(frames, 0).start()
    fetch(frames, 1).start()
    for layer in range(2):
        start_local_w(layer, w_plan(layer), slot_of[layer])

    barrier = pltpu.get_barrier_semaphore()
    greeted = [dict(sibling)]
    greeted += [at_plane(lax.rem(mp + k, np_)) for k in range(1, np_)]
    greeted += [at_z(lax.rem(mz + k, nz)) for k in range(1, nz)]
    greeted += [dict(axis["partner"], section=other) for axis in bits]
    for where in greeted:
        pl.semaphore_signal(barrier, inc=1, device_id=where, device_id_type=MESH)

    for k, (x, fill) in enumerate(((gains, 0.0), (shifts, -1e30), (recurs, 0.0))):
        vecs[section, k : k + 1, 0:width] = x[...]
        vecs[section, k : k + 1, width:] = jnp.full((1, 2 * W - width), fill, F32)
    vecs[section, 3:8, :] = jnp.zeros((5, 2 * W), F32)

    gap = jnp.zeros((W - rest, W), BF16)

    @pl.when(section == 0)
    def _():
        wc[0, 1, rest:, :] = gap
        wc[1, 1, rest:, :] = gap

    @pl.when(section == 1)
    def _():
        wc[0, 0, rest:, :] = gap
        wc[1, 0, rest:, :] = gap
        wr1[rest:, :] = gap

    for spot in (0, 2):
        tails[spot, rest:, :] = jnp.zeros((W - rest, rest - full), BF16)
    for spare in (f_own, p_own, g3.at[0], g3.at[1]):
        spare[sent_rows:, :] = jnp.zeros((spare.shape[0] - sent_rows, W), BF16)

    pl.semaphore_wait(barrier, len(greeted))

    @pl.when(section == 1)
    def _():
        heads_copy(frames, 1).start()

    start_across_w(0, w_plan(0), slot_of[0])
    send_vec = across(vecs.at[section], vecs.at[section], 3)
    send_vec.start()

    def stage_copy(where, rnd, slot, k, back):
        buf, parity, size, me, at, send, recv = where
        there = at(lax.rem(me + (size - k if back else k), size))
        ref = buf.at[parity, slot]
        return pltpu.make_async_remote_copy(
            src_ref=ref, dst_ref=ref, send_sem=send.at[rnd, k], recv_sem=recv.at[rnd, k],
            device_id=there, device_id_type=MESH,
        )

    def in_plane(buf, parity):
        return (buf, parity, np_, mp, at_plane, pl_send, pl_recv)

    def in_line(buf, parity):
        return (buf, parity, nz, mz, at_z, z_send, z_recv)

    def stage_start(where, rnd, value):
        buf, parity, size, me = where[:4]
        buf[parity, me] = value
        for k in range(1, size):
            stage_copy(where, rnd, me, k, False).start()

    def stage_wait(where, rnd):
        size, me = where[2:4]
        for k in range(1, size):
            stage_copy(where, rnd, me, k, False).wait_send()
            stage_copy(where, rnd, lax.rem(me + size - k, size), k, True).wait_recv()

    def add_slots(where):
        buf, parity, size = where[:3]
        total = buf[parity, 0]
        for k in range(1, size):
            total = total + buf[parity, k]
        return total

    groups = lengths.shape[1]
    s_at = lax.broadcasted_iota(jnp.int32, (seqs, groups), 0)
    g_at = lax.broadcasted_iota(jnp.int32, (seqs, groups), 1) * views
    there = (s_at >= g_at) & (s_at < g_at + views)
    position = lax.broadcasted_iota(jnp.int32, (seqs, 128), 1)
    local_counts = []
    for m in range(2):
        turn[...] = jnp.zeros_like(turn)
        turn[0:steps, 0:seqs] = masks[m].astype(F32)
        mask = turn[...].T[0:seqs]
        length = jnp.broadcast_to(lengths[m : m + 1, :], (seqs, groups)).astype(F32)
        limit = jnp.sum(jnp.where(there, length, 0.0), axis=1, keepdims=True)
        alive = (position.astype(F32) < limit) & ((mask > 0.0) | (position == 0))
        alive = jnp.where(position < steps, alive.astype(F32), 0.0)
        total = jnp.zeros((seqs, 128), F32)
        for t in range(steps):
            at = m * span + t * seqs
            cells = jnp.broadcast_to(alive[:, t : t + 1], (seqs, 128))
            live[at : at + seqs, :] = cells
            total = total + cells
        local_counts.append(jnp.sum(total, axis=0, keepdims=True))
    n_own = jnp.concatenate(local_counts * 4, axis=0)

    cnt_plane, cnt_line = in_plane(cnt_p, 0), in_line(cnt_z, 0)
    stage_start(cnt_plane, 0, n_own)

    def vec_of(layer, k):
        return vecs[layer, k : k + 1, pl.ds(aligned(section * W, W), W)]

    def matmul_to(out, a, w, first, m):
        r = pl.ds(m * span, span)

        def body(i, _):
            c = pl.ds(aligned(i * HALF, HALF), HALF)
            y = dot(a[r, :], w[:, c], ((1,), (0,)))
            out[r, c] = y if first else out[r, c] + y
            return 0

        lax.fori_loop(0, 2, body, 0)

    def packed(x, y):
        return jnp.concatenate([z[:, k * QUART : (k + 1) * QUART] for z in (x, y) for k in range(4)], axis=0)

    def unpacked(x):
        return jnp.concatenate([x[k : k + 1] for k in range(4)], axis=1)

    def merge_slots(where, counts_of):
        buf, parity, size = where[:3]
        s = [buf[parity, k, 0:4, :] for k in range(size)]
        q = [buf[parity, k, 4:8, :] for k in range(size)]
        n = [wide(counts_of(k), 2) for k in range(size)]
        total, squares, count = sum(s[1:], s[0]), sum(q[1:], q[0]), sum(n[1:], n[0])
        mean = total / count
        for k in range(size):
            d = s[k] / n[k] - mean
            squares = squares + n[k] * d * d
        return jnp.concatenate([total, squares], axis=0)

    def slim_round(which, m):
        return 1 + 2 * which + m, in_plane(slim_p, 2 * m + which % 2), in_line(slim_z, 2 * m + which % 2)

    def forward_stats(layer, m):
        start = jnp.sum(rows[layer, m * span : m * span + seqs, :], axis=0, keepdims=True) * (1.0 / seqs)

        def body(i, carry):
            s, q = carry
            r = pl.ds(aligned(m * span + i * (2 * seqs), 16), 2 * seqs)
            d = rows[layer, r, :] - start
            kept = wide(live[r, :], 8) * d
            return s + fold(kept), q + fold(kept * d)

        zero = jnp.zeros((8, W), F32)
        s, q = lax.fori_loop(0, pairs, body, (zero, zero))
        s, q = jnp.sum(s, axis=0, keepdims=True), jnp.sum(q, axis=0, keepdims=True)
        n = wide(local_counts[m], 8)
        rnd, plane, _ = slim_round(layer, m)
        stage_start(plane, rnd, packed(s + n * start, jnp.maximum(q - s * s / n, 0.0)))

    def forward_middle(layer, m):
        rnd, plane, line = slim_round(layer, m)
        stage_wait(plane, rnd)
        stage_start(line, rnd, merge_slots(plane, lambda k: cnt_p[0, k, m : m + 1, :]))

    def forward_end(layer, m):
        rnd, _, line = slim_round(layer, m)
        stage_wait(line, rnd)
        value = merge_slots(line, lambda k: cnt_z[0, k, m : m + 1, :])
        count = wide(counts[m : m + 1, :], 8)
        mean = unpacked(value[0:4]) / count
        scale = lax.rsqrt(unpacked(value[4:8]) / count + EPS)
        coef[layer, 2 * m : 2 * m + 1, :] = mean
        coef[layer, 2 * m + 1 : 2 * m + 2, :] = scale
        slope = vec_of(layer, 0) * scale
        coef[layer, 4 + 2 * m : 5 + 2 * m, :] = slope
        coef[layer, 5 + 2 * m : 6 + 2 * m, :] = vec_of(layer, 1) - mean * slope

    def forward_scan(layer, m, passes):
        rec = vec_of(layer, 2)
        slope = coef[layer, 4 + 2 * m : 5 + 2 * m, :]
        shift = coef[layer, 5 + 2 * m : 6 + 2 * m, :]

        def body(i, carry):
            h, level = carry
            r = pl.ds(aligned(m * span + i * (2 * seqs), 16), 2 * seqs)
            x = rows[layer, r, :] * slope + shift
            lv = wide(live[r, :], 8)
            alive = lv > 0.0
            both = []
            for k in range(2):
                part = slice(k * seqs, (k + 1) * seqs)
                z = x[part] + rec * h
                soft = jnp.maximum(z, 0.0) + jnp.log(1.0 + jnp.exp(-jnp.abs(z)))
                h = jnp.where(alive[part], soft, h)
                both.append(h)
            two = jnp.concatenate(both, axis=0)
            hid[layer, r, :] = two
            if passes:
                p_own[r, :] = two.astype(BF16)
                level = level + fold(lv * two)
            return h, level

        _, level = lax.fori_loop(0, pairs, body, (jnp.zeros((seqs, W), F32), jnp.zeros((8, W), F32)))
        if not passes:
            return None
        level = jnp.sum(level, axis=0, keepdims=True)
        levels[1:2, :] = level if m == 0 else levels[1:2, :] + level
        here = pl.ds(m * span, span)
        made = across(p_own.at[here, :], p_far.at[here, :], 18 + m)
        made.start()
        return made

    def backward_scan(layer, m, above, between=lambda: None):
        gain, shift, recur = vec_of(layer, 0), vec_of(layer, 1), vec_of(layer, 2)
        for lq in range(4):
            lanes = slice(lq * QUART, (lq + 1) * QUART)
            gq, sq, rec = gain[:, lanes], shift[:, lanes], recur[:, lanes]
            mean = coef[layer, 2 * m : 2 * m + 1, lanes]
            scale = coef[layer, 2 * m + 1 : 2 * m + 2, lanes]

            def body(i, carry):
                down, s1, s2, rsum, sqh, sqa = carry
                i = pairs - 1 - i
                start = m * span + i * (2 * seqs)
                r = pl.ds(aligned(start, 16), 2 * seqs)
                before = pl.ds(aligned(jnp.maximum(start - seqs, 0), 8), seqs)
                normed = (rows[layer, r, lanes] - mean) * scale
                drive = gq * normed + sq
                h2 = hid[layer, r, lanes]
                hb = jnp.where(i > 0, hid[layer, before, lanes], 0.0)
                lv = wide(live[r, :], 2)
                up = above[r, lanes].astype(F32)
                res = f_own[r, lanes].astype(F32)
                aux = res + h2 if layer == 1 else res
                sqh = sqh + fold(lv * (h2 * h2))
                sqa = sqa + fold(lv * (aux * aux))
                grads = [None, None]
                for k in (1, 0):
                    part = slice(k * seqs, (k + 1) * seqs)
                    prior = h2[0:seqs] if k == 1 else hb
                    slope = 0.5 + 0.5 * jnp.tanh(0.5 * (drive[part] + rec * prior))
                    total = up[part] + down
                    gd = lv[part] * slope * total
                    down = (1.0 - lv[part]) * total + rec * gd
                    grads[k] = gd
                    rsum = rsum + fold(gd * prior)
                gd2 = jnp.concatenate(grads, axis=0)
                hid[layer, r, lanes] = gd2
                return down, s1 + fold(gd2), s2 + fold(gd2 * normed), rsum, sqh, sqa

            z8 = jnp.zeros((8, QUART), F32)
            _, s1, s2, rsum, sqh, sqa = lax.fori_loop(
                0, pairs, body, (jnp.zeros((seqs, QUART), F32), z8, z8, z8, z8, z8)
            )
            for k, x in ((m, s1), (2 + m, s2)):
                tot[layer, k : k + 1, lanes] = jnp.sum(x, axis=0, keepdims=True)
            for k, x in ((4, rsum), (5, sqh), (6, sqa)):
                x = jnp.sum(x, axis=0, keepdims=True)
                tot[layer, k : k + 1, lanes] = x if m == 0 else tot[layer, k : k + 1, lanes] + x
            between()

    def backward_stats(layer, m):
        rnd, plane, _ = slim_round(3 - layer, m)
        stage_start(plane, rnd, packed(tot[layer, m : m + 1, :], tot[layer, 2 + m : 3 + m, :]))

    def backward_middle(layer, m):
        rnd, plane, line = slim_round(3 - layer, m)
        stage_wait(plane, rnd)
        stage_start(line, rnd, add_slots(plane))

    def backward_end(layer, m):
        rnd, _, line = slim_round(3 - layer, m)
        stage_wait(line, rnd)
        value = add_slots(line)
        tot[layer, m : m + 1, :] = unpacked(value[0:4])
        tot[layer, 2 + m : 3 + m, :] = unpacked(value[4:8])

    def grad_rows(layer, m, slot):
        gain = vec_of(layer, 0)
        for lh in range(2):
            lanes = slice(lh * HALF, (lh + 1) * HALF)
            mean = coef[layer, 2 * m : 2 * m + 1, lanes]
            scale = coef[layer, 2 * m + 1 : 2 * m + 2, lanes]
            count = wide(counts[m : m + 1, :], 4)
            first = tot[layer, m : m + 1, lanes] / count
            second = tot[layer, 2 + m : 3 + m, lanes] / count * scale
            k = scale * gain[:, lanes]

            def body(i, acc):
                r = pl.ds(aligned(m * span + i * (2 * seqs), 16), 2 * seqs)
                y = hid[layer, r, lanes] - first - (rows[layer, r, lanes] - mean) * second
                y = wide(live[r, :], 4) * (k * y)
                g3[0, r, lanes] = y.astype(BF16)
                return acc + fold(y)

            acc = lax.fori_loop(0, pairs, body, jnp.zeros((8, HALF), F32))
            acc = jnp.sum(acc, axis=0, keepdims=True)
            if m == 0:
                levels[4:5, lanes] = acc
            else:
                top = lax.broadcasted_iota(jnp.int32, (16, HALF), 0) == 0
                minus = jnp.where(top, -(levels[4:5, lanes] + acc), 0.0)
                g3[0, total_rows:sent_rows, lanes] = minus.astype(BF16)
        here = pl.ds(0, span) if m == 0 else pl.ds(span, span + 16)
        made = across(g3.at[0, here, :], g3.at[1, here, :], slot + m)
        made.start()
        return made

    sums_round = {1: (1, 10), 0: (0, 11)}

    def sums_start(layer):
        parity, rnd = sums_round[layer]
        own_sum = -g3[0, total_rows:sent_rows, :].astype(F32)[0:1]
        far_sum = -g3[1, total_rows:sent_rows, :].astype(F32)[0:1]
        value = jnp.concatenate([own_sum, far_sum, tot[layer, 4:7, :], jnp.zeros((3, W), F32)], axis=0)
        stage_start(in_plane(wide_p, parity), rnd, value)

    def sums_middle(layer):
        parity, rnd = sums_round[layer]
        stage_wait(in_plane(wide_p, parity), rnd)
        stage_start(in_line(wide_z, parity), rnd, add_slots(in_plane(wide_p, parity)))

    def sums_end(layer):
        parity, rnd = sums_round[layer]
        stage_wait(in_line(wide_z, parity), rnd)
        vtot[layer] = add_slots(in_line(wide_z, parity))
        tot[layer, 4:7, :] = vtot[layer, 2:5, :]
        tot[layer, 7:8, :] = wide(counts[0:1, :] + counts[1:2, :], 8)
        env["summed"].add(layer)

        @pl.when(section == layer)
        def _():
            pltpu.make_async_copy(tot.at[layer], v.at[section], v_sems.at[0]).start()

        @pl.when(section != layer)
        def _():
            v_across(layer).start()

    def v_across(layer):
        return pltpu.make_async_remote_copy(
            src_ref=tot.at[layer], dst_ref=v.at[section], send_sem=v_sems.at[1], recv_sem=v_sems.at[2],
            device_id=sibling, device_id_type=MESH,
        )

    def transpose(src, begin=0, end=W // 128):
        def body(j, _):
            c = pl.ds(aligned(j * 128, 128), 128)
            src_t[c, 0:total_rows] = src[0:total_rows, c].T
            return 0

        lax.fori_loop(begin, end, body, 0)

    def transpose_level(src, layer):
        top = lax.broadcasted_iota(jnp.int32, (16, W), 0) == 0
        src[total_rows:sent_rows, :] = jnp.where(top, levels[2 + layer : 3 + layer, :], 0.0).astype(BF16)

        def body(j, _):
            c = pl.ds(aligned(j * 128, 128), 128)
            src_t[c, total_rows:] = src[total_rows:, c].T
            level = src[total_rows:sent_rows, c].astype(F32)[0:1]
            column[layer, c, :] = jnp.broadcast_to(level, (128, 128)).T.astype(BF16)
            return 0

        lax.fori_loop(0, W // 128, body, 0)

    def weight_part(block, grads, c):
        lanes = pl.ds(c * HALF, HALF)

        def body(j, _):
            r = pl.ds(aligned(j * HALF, HALF), HALF)
            block[r, lanes] = dot(src_t[r, :], grads[:, lanes], ((1,), (0,))).astype(BF16)
            return 0

        lax.fori_loop(0, W // HALF, body, 0)

    def source_grad(store, w_own, w_far, between):
        for m in range(2):
            r = pl.ds(m * span, span)

            def body(i, _):
                c = pl.ds(aligned(i * HALF, HALF), HALF)
                y = dot(g3[0, r, :], w_own[c, :], ((1,), (1,))) + dot(g3[1, r, :], w_far[c, :], ((1,), (1,)))
                store(r, c, y)
                return 0

            lax.fori_loop(0, 2, body, 0)
            between()

    env = dict(summed=set(), vtot=vtot, column=column, space=space, ar_send=ar_send, ar_recv=ar_recv,
               ar_other=ar_other, o=o, section=section, here={"batch": b})
    xs = [a for a in bits if a["link"] == "x"]
    ys = [a for a in bits if a["link"] == "y"]
    zs = [a for a in bits if a["link"] == "z"]
    orders = (xs + ys + zs, ys + xs + zs)
    blocks = {
        (1, 0): f_far.at[pl.ds(0, W), :],
        (1, 1): p_far.at[pl.ds(0, W), :],
        (0, 0): wc.at[1, 1],
        (0, 1): wr1,
    }
    parts = {}
    for layer in (1, 0):
        for index in range(2 * PAIRS):
            part, side = index // PAIRS, index % PAIRS

            def lane_of(sec, part=part, side=side):
                return (sec if part == 0 else 1 - sec) * W + side * 2 * PART

            block = blocks[layer, part].at[:, pl.ds(side * 2 * PART, 2 * PART)]
            parts[layer, index] = Reduction(env, layer, index, block, orders, lane_of)
    order = Order()

    def weight_grads(layer, between):
        for part in range(2):
            if part == 1:
                between()
            for c in range(2):
                weight_part(blocks[layer, part], g3.at[part], c)
                order.work(2.0)
                for k in range(c * HALF // PART, (c + 1) * HALF // PART):
                    order.begin(parts[layer, part * PAIRS + k // 2], k % 2)

    def arrived(layer, sends):
        for made in sends:
            made.wait()
        sums_start(layer)

    send_f = []
    for m in range(2):
        by_units(frames, f_own, m)
        fetch(grad_out, m).start()
        if m == 0:
            wait_heads(frames, 1)
        patch_heads(f_own, m)
        here = pl.ds(m * span, span)
        made = across(f_own.at[here, :], f_far.at[here, :], (0, 24)[m])
        made.start()
        send_f.append(made)
    start_across_w(1, w_plan(1), slot_of[1])
    stage_wait(cnt_plane, 0)
    stage_start(cnt_line, 0, add_slots(cnt_plane))
    wait_w(0, w_plan(0), slot_of[0], 0)
    matmul_to(rows.at[0], f_own, wc.at[0, 0], True, 0)
    matmul_to(rows.at[0], f_own, wc.at[0, 0], True, 1)
    wait_w(0, w_plan(0), slot_of[0], 1)
    send_f[0].wait()
    matmul_to(rows.at[0], f_far, wc.at[0, 1], False, 0)
    forward_stats(0, 0)
    send_f[1].wait()

    @pl.when(section == 1)
    def _():
        heads_copy(grad_out, 2).start()

    matmul_to(rows.at[0], f_far, wc.at[0, 1], False, 1)
    forward_middle(0, 0)
    forward_stats(0, 1)
    send_vec.wait_send()
    across(vecs.at[other], vecs.at[other], 3).wait_recv()
    stage_wait(cnt_line, 0)
    counts[...] = add_slots(cnt_line)
    forward_end(0, 0)
    sends = [forward_scan(0, 0, True)]
    forward_middle(0, 1)
    by_units(grad_out, g3.at[1], 0)
    wait_heads(grad_out, 2)
    patch_heads(g3.at[1], 0)
    forward_end(0, 1)
    sends.append(forward_scan(0, 1, True))
    wait_w(1, w_plan(1), slot_of[1], 0)
    matmul_to(rows.at[1], p_own, wc.at[1, 0], True, 0)
    wait_w(1, w_plan(1), slot_of[1], 1)
    sends[0].wait()
    matmul_to(rows.at[1], p_far, wc.at[1, 1], False, 0)
    forward_stats(1, 0)
    matmul_to(rows.at[1], p_own, wc.at[1, 0], True, 1)
    forward_middle(1, 0)
    sends[1].wait()
    matmul_to(rows.at[1], p_far, wc.at[1, 1], False, 1)
    forward_stats(1, 1)
    done_w(0, w_plan(0), slot_of[0])

    start_local_w(0, late_plan, slot_of[2])
    start_across_w(0, late_plan, slot_of[2])

    @pl.when(section == 1)
    def _():
        wc[0, 1, width - late_row :, :] = jnp.zeros((W - width + late_row, W), BF16)

    def source_level():
        def body(i, acc):
            r = pl.ds(aligned(i * (2 * seqs), 16), 2 * seqs)
            return acc + fold(wide(live[r, :], 8) * f_own[r, :].astype(F32))

        acc = lax.fori_loop(0, 2 * pairs, body, jnp.zeros((8, W), F32))
        levels[0:1, :] = jnp.sum(acc, axis=0, keepdims=True)

    forward_end(1, 0)
    forward_scan(1, 0, False)
    forward_middle(1, 1)
    by_units(grad_out, g3.at[1], 1)
    patch_heads(g3.at[1], 1)
    source_level()
    forward_end(1, 1)
    level_plane, level_line = in_plane(wide_p, 0), in_line(wide_z, 0)
    stage_start(level_plane, 9, jnp.concatenate([levels[0:2, :], jnp.zeros((6, W), F32)], axis=0))
    forward_scan(1, 1, False)
    backward_scan(1, 0, g3.at[1])
    backward_stats(1, 0)
    stage_wait(level_plane, 9)
    stage_start(level_line, 9, add_slots(level_plane))
    backward_scan(1, 1, g3.at[1])
    backward_stats(1, 1)
    backward_middle(1, 0)
    pl.semaphore_signal(credit.at[0], inc=1, device_id=sibling, device_id_type=MESH)
    transpose(p_own, 0, W // 256)
    backward_middle(1, 1)
    backward_end(1, 0)
    pl.semaphore_wait(credit.at[0], 1)
    sends = [grad_rows(1, 0, 20)]
    transpose(p_own, W // 256)
    stage_wait(level_line, 9)
    levels[2:4, :] = (add_slots(level_line) / wide(counts[0:1, :] + counts[1:2, :], 8))[0:2]
    transpose_level(p_own, 1)
    backward_end(1, 1)
    sends.append(grad_rows(1, 1, 20))
    weight_grads(1, lambda: arrived(1, sends))
    wait_w(1, w_plan(1), slot_of[1], 2)
    done_w(1, w_plan(1), slot_of[1])

    def keep_down(r, c, y):
        p_own[r, c] = y.astype(BF16)

    source_grad(keep_down, wc.at[1, 0], wr1, lambda: order.work(3.0))
    pl.semaphore_signal(credit.at[1], inc=1, device_id=sibling, device_id_type=MESH)
    sums_middle(1)
    backward_scan(0, 0, p_own, lambda: order.work(0.6))
    backward_stats(0, 0)
    backward_scan(0, 1, p_own, lambda: order.work(0.6))
    backward_stats(0, 1)
    backward_middle(0, 0)
    sums_end(1)
    transpose(f_own)
    transpose_level(f_own, 0)
    backward_middle(0, 1)
    order.work(3.0)
    backward_end(0, 0)
    pl.semaphore_wait(credit.at[1], 1)
    sends = [grad_rows(0, 0, 22)]
    backward_end(0, 1)
    sends.append(grad_rows(0, 1, 22))
    order.work(2.0)
    weight_grads(0, lambda: arrived(0, sends))
    wait_w(0, late_plan, slot_of[2], 0)
    wait_w(0, late_plan, slot_of[2], 1)
    done_w(0, late_plan, slot_of[2])

    def keep_source(r, c, y):
        rows[0, r, c] = y

    fetch(grad_out, 0).start()
    fetch(grad_out, 1).start()
    sums_middle(0)
    source_grad(keep_source, wc.at[0, 0], wc.at[0, 1], lambda: order.work(3.0))
    sums_end(0)

    def give(m):
        return pltpu.make_async_copy(staged.at[m], gf.at[m], stage_sem.at[m])

    for m in range(2):
        fetch(grad_out, m).wait()

        def finish_frames(i, _, m=m):
            straight = staged[m, pl.ds(2 * i, 2)].astype(F32).reshape(2 * seqs, half)
            y = rows[0, pl.ds(aligned(m * span + 2 * i * seqs, 8), 2 * seqs), :]
            y = jnp.where(section == 0, y[:, :half], y[:, late_shift : late_shift + half])
            staged[m, pl.ds(2 * i, 2)] = (y + straight).reshape(2, seqs, half).astype(BF16)
            return 0

        lax.fori_loop(0, pairs, finish_frames, 0)
        give(m).start()
        order.work(2.0)
    order.drain()
    for m in range(2):
        give(m).wait()

    for layer in range(2):

        @pl.when(section == layer)
        def _(layer=layer):
            pltpu.make_async_copy(tot.at[layer], v.at[section], v_sems.at[0]).wait()
            pltpu.make_async_remote_copy(
                src_ref=tot.at[layer], dst_ref=v.at[other], send_sem=v_sems.at[1], recv_sem=v_sems.at[2],
                device_id=sibling, device_id_type=MESH,
            ).wait_recv()

        @pl.when(section != layer)
        def _(layer=layer):
            v_across(layer).wait_send()

    own_part, far_part = v[section], v[other]
    first = jnp.where(section == 0, own_part, far_part)
    second = jnp.where(section == 0, far_part, own_part)
    for row, terms in ((0, (2, 3)), (1, (0, 1)), (2, (4,))):
        for lane, x in ((0, first), (W, second)):
            total = x[terms[0] : terms[0] + 1, :]
            for k in terms[1:]:
                total = total + x[k : k + 1, :]
            vectors[row : row + 1, lane : lane + W] = total
    squares = jnp.sum(first[5:7, :] + second[5:7, :], axis=1, keepdims=True)
    root = jnp.sqrt(squares / (first[7:8, 0:1] * width))
    for k in range(2):
        vectors[3 + k : 4 + k, :] = jnp.broadcast_to(root[k : k + 1], (1, 2 * W))
    vectors[5:8, :] = jnp.zeros((3, 2 * W), F32)


def write_results(o, gf, vectors, grad_weight, grad_frames, grad_gains, grad_shifts, grad_recurs, table):
    width = grad_weight.shape[2]
    grad_weight[0] = o[...][:, :width].astype(F32)
    grad_frames[...] = gf[...]

    @pl.when(pl.program_id(0) == 0)
    def _():
        for k, out in enumerate((grad_gains, grad_shifts, grad_recurs)):
            out[...] = vectors[k : k + 1, 0:width]
        table[...] = jnp.concatenate([vectors[3:4, 0:1], vectors[4:5, 0:1]], axis=1)


def results(o, gf, vectors):
    micro, steps, seqs, half = gf.shape
    width = 2 * half
    count = W * 2 // 256
    frames = micro * steps // count
    whole = lambda shape: pl.BlockSpec(shape, lambda i: (0, 0))
    out = pl.pallas_call(
        write_results,
        grid=(count,),
        in_specs=[
            pl.BlockSpec((256, 2 * W), lambda i: (i, 0)),
            pl.BlockSpec((frames, seqs, half), lambda i: (i, 0, 0)),
            whole((8, 2 * W)),
        ],
        out_specs=(
            pl.BlockSpec((1, 256, width), lambda i: (0, i, 0)),
            pl.BlockSpec((frames, seqs, half), lambda i: (i, 0, 0)),
            whole((1, width)),
            whole((1, width)),
            whole((1, width)),
            whole((1, 2)),
        ),
        out_shape=(
            jax.ShapeDtypeStruct((1, width, width), F32),
            jax.ShapeDtypeStruct((micro * steps, seqs, half), BF16),
            jax.ShapeDtypeStruct((1, width), F32),
            jax.ShapeDtypeStruct((1, width), F32),
            jax.ShapeDtypeStruct((1, width), F32),
            jax.ShapeDtypeStruct((1, 2), F32),
        ),
        compiler_params=pltpu.CompilerParams(vmem_limit_bytes=64 * 1024 * 1024),
    )(o.reshape(2 * W, 2 * W), gf.reshape(micro * steps, seqs, half), vectors)
    return out[1].reshape(gf.shape), out[0], *out[2:]


def whole_step(dims, frames, grad_out, weights, gains, shifts, recurs, lengths, masks):
    nz, ny, nx = dims
    micro, steps, seqs, half = frames.shape
    width = 2 * half
    views = seqs // lengths.shape[1]
    rows = micro * steps * seqs
    np_ = ny * nx
    wide_rows = (rows + 16 + 127) // 128 * 128
    depth = (nx * ny * nz - 1).bit_length()
    any_ = pl.BlockSpec(memory_space=pl.ANY)
    held = pl.BlockSpec(memory_space=pltpu.VMEM)
    dma = pltpu.SemaphoreType.DMA
    return pl.pallas_call(
        functools.partial(kernel, dims, steps, seqs, views),
        out_shape=(
            jax.ShapeDtypeStruct((2, W, 2 * W), BF16),
            jax.ShapeDtypeStruct(frames.shape, BF16),
            jax.ShapeDtypeStruct((8, 2 * W), F32),
        ),
        in_specs=[any_] * 3 + [held] * 5,
        out_specs=(any_, any_, held),
        scratch_shapes=[
            pltpu.VMEM((wide_rows, W), BF16),
            pltpu.VMEM((rows, W), BF16),
            pltpu.VMEM((wide_rows, W), BF16),
            pltpu.VMEM((rows, W), BF16),
            pltpu.VMEM((2, wide_rows, W), BF16),
            pltpu.VMEM((2, 2, W, W), BF16),
            pltpu.VMEM((W, W), BF16),
            pltpu.VMEM((W, wide_rows), BF16),
            pltpu.VMEM((rows, 128), F32),
            pltpu.VMEM((128, 128), F32),
            pltpu.VMEM(frames.shape, BF16),
            pltpu.VMEM((micro, steps, seqs, 128), BF16),
            pltpu.VMEM((5, W, (width - W) % 128), BF16),
            pltpu.VMEM((2, 8, W), F32),
            pltpu.VMEM((2, 8, 2 * W), F32),
            pltpu.VMEM((2, rows, W), F32),
            pltpu.VMEM((2, rows, W), F32),
            pltpu.VMEM((2, 8, W), F32),
            pltpu.VMEM((2, 8, W), F32),
            pltpu.VMEM((2, 8, W), F32),
            pltpu.VMEM((8, W), F32),
            pltpu.VMEM((2, W, 128), BF16),
            pltpu.VMEM((8, 128), F32),
            pltpu.VMEM((1, np_, 8, 128), F32),
            pltpu.VMEM((1, nz, 8, 128), F32),
            pltpu.VMEM((4, np_, 8, QUART), F32),
            pltpu.VMEM((4, nz, 8, QUART), F32),
            pltpu.VMEM((2, np_, 8, W), F32),
            pltpu.VMEM((2, nz, 8, W), F32),
            pltpu.VMEM((2, 2 * PAIRS, W, 2 * PART), BF16),
            dma((3, 25)),
            dma((3,)),
            dma((2,)),
            pltpu.SemaphoreType.REGULAR((2,)),
            dma((12, max(np_, 2))),
            dma((12, max(np_, 2))),
            dma((12, max(nz, 2))),
            dma((12, max(nz, 2))),
            dma((2, 2 * PAIRS, 2, 2 * depth + 2)),
            dma((2, 2 * PAIRS, 2, 2 * depth + 2)),
            dma((2, 2 * PAIRS, 2, 2)),
        ],
        compiler_params=pltpu.CompilerParams(
            collective_id=0, has_side_effects=True, vmem_limit_bytes=64 * 1024 * 1024
        ),
    )(frames, grad_out, weights, gains, shifts, recurs, lengths, masks)


def shards(dims, frames, grad_out, weights, gains, shifts, recurs, lengths, masks):
    return results(*whole_step(dims, frames, grad_out, weights, gains, shifts, recurs, lengths, masks))


def solution(mesh):
    in_specs = (
        P(None, None, "batch", "section"),
        P(None, None, "batch", "section"),
        P("section", None, None),
        P("section", None),
        P("section", None),
        P("section", None),
        P(None, "batch"),
        P(None, None, "batch"),
    )
    out_specs = (
        P(None, None, "batch", "section"),
        P("section", None, None),
        P("section", None),
        P("section", None),
        P("section", None),
        P("section", None),
    )
    body = functools.partial(shards, grid_of(mesh.shape["batch"]))
    return jax.shard_map(body, mesh=mesh, in_specs=in_specs, out_specs=out_specs, check_vma=False)
```

```python
import functools

import jax
import jax.numpy as jnp
from jax import lax
from jax.experimental import pallas as pl
from jax.experimental.pallas import tpu as pltpu
from jax.sharding import PartitionSpec as P

EPS = 1e-05
W = 1024
HALF = W // 2
QUART = W // 4
PAIRS = 2
PART = W // PAIRS // 2
MESH = pl.DeviceIdType.MESH
F32 = jnp.float32
BF16 = jnp.bfloat16


def grid_of(size):
    if size == 16:
        return (4, 2, 2)
    if size == 128:
        return (8, 4, 4)
    return (size, 1, 1)


def aligned(x, k):
    return pl.multiple_of(x, k)


def wide(x, reps):
    return jnp.concatenate([x] * reps, axis=1)


def fold(x):
    rows = x.shape[0]
    total = x[0:8]
    for k in range(8, rows, 8):
        total = total + x[k : k + 8]
    return total


def dot(a, b, dims):
    return lax.dot_general(a, b, (dims, ((), ())), preferred_element_type=F32)


class Reduction:
    def __init__(self, env, layer, index, block, orders, lane_of):
        self.env, self.layer, self.index, self.block, self.orders = env, layer, index, block, orders
        self.lane_of = lane_of
        self.space = env["space"].at[layer, index]
        self.depth = len(orders[0])
        self.regions = [self.shares(i, order) for i, order in enumerate(orders)]
        self.step = 0
        self.waits = []
        self.slot = [0, 0]
        depth = self.depth
        self.steps = [functools.partial(self.scatter, k) for k in range(depth)]
        self.steps += [functools.partial(self.gather, k) for k in range(depth - 1, 0, -1)]
        self.steps += [self.give, self.finish]

    def shares(self, i, order):
        out = [(0, W, i * PART, PART)]
        for axis in order:
            out.append(self.share(out[-1], axis, axis["index"]))
        return out

    def share(self, region, axis, index):
        row, rows, lane, lanes = region
        by_row = min(axis["size"], rows // 16)
        rows, lanes = rows // by_row, lanes // (axis["size"] // by_row)
        if by_row == axis["size"]:
            return row + index * rows, rows, lane, lanes
        return row + lax.rem(index, by_row) * rows, rows, lane + index // by_row * lanes, lanes

    @property
    def free_to_go(self):
        return self.step != self.depth or self.layer in self.env["summed"]

    @property
    def done(self):
        return self.step >= len(self.steps)

    def advance(self):
        self.sent = []
        self.steps[self.step]()
        self.step += 1
        return self.sent

    def remote(self, i, src, dst, slot, where, recv=None):
        sems = (self.layer, self.index, i, slot)
        return pltpu.make_async_remote_copy(
            src_ref=src, dst_ref=dst, send_sem=self.env["ar_send"].at[sems],
            recv_sem=self.env["ar_recv"].at[sems] if recv is None else recv, device_id=where, device_id_type=MESH,
        )

    def wait(self):
        for made, came in self.waits:
            made.wait_send()
            came.wait_recv()
        self.waits = []

    def take(self, i):
        self.slot[i] += 1
        return self.slot[i] - 1

    def came_at(self, i, k, s):
        row = sum((a["size"] - 1) * self.regions[i][n + 1][1] for n, a in enumerate(self.orders[i][:k]))
        _, rows, _, lanes = self.regions[i][k + 1]
        return row + (s - 1) * rows, rows, i * PART, lanes

    def scatter(self, k):
        if k > 0:
            self.wait()
            self.add(k - 1)
        for i in range(2):
            self.scatter_part(i, k)

    def start_part(self, i):
        self.sent = []
        self.scatter_part(i, 0)
        if i == 1:
            self.step = 1
        return self.sent

    def scatter_part(self, i, k):
        axis = self.orders[i][k]
        for s in range(1, axis["size"]):
            other = lax.rem(axis["index"] + s, axis["size"])
            row, rows, lane, lanes = self.share(self.regions[i][k], axis, other)
            src = self.block.at[pl.ds(aligned(row, 16), rows), pl.ds(aligned(lane, 128), lanes)]
            at, n, at_lane, n_lanes = self.came_at(i, k, s)
            dst = self.space.at[pl.ds(at, n), pl.ds(at_lane, n_lanes)]
            made = self.remote(i, src, dst, self.take(i), axis["at"](other))
            made.start()
            self.waits.append((made, made))
            self.sent.append((axis["link"], rows * lanes * 2))

    def add(self, k, last=False):
        rows = self.regions[0][k + 1][1]
        size = min(rows, 32)
        out = []
        for i in range(2):
            row, _, lane, lanes = self.regions[i][k + 1]
            lane = aligned(lane, 128)
            extra = None
            if last:
                part = self.index // PAIRS
                first = aligned((self.index % PAIRS) * 2 * PART + lane, 128)
                extra = self.env["vtot"][self.layer, part : part + 1, pl.ds(first, lanes)]
            came = [self.came_at(i, k, s) for s in range(1, self.orders[i][k]["size"])]
            out.append((row, lane, lanes, came, self.local(i, self.regions[i][k + 1])[0], extra))

        def body(j, _):
            for row, lane, lanes, came, home, extra in out:
                here = pl.ds(aligned(row + j * size, 16), size)
                total = self.block[here, pl.ds(lane, lanes)].astype(F32)
                for at, _, at_lane, _ in came:
                    there = pl.ds(aligned(at + j * size, 16), size)
                    total = total + self.space[there, pl.ds(at_lane, lanes)].astype(F32)
                if last:
                    column = self.env["column"][self.layer, here, :].astype(F32)
                    total = total + wide(column, lanes // 128) * extra
                    to = pl.ds(aligned(home + j * size, 16), size)
                    self.space[to, pl.ds(lane, lanes)] = total.astype(BF16)
                else:
                    self.block[here, pl.ds(lane, lanes)] = total.astype(BF16)
            return 0

        lax.fori_loop(0, rows // size, body, 0)

    def local(self, i, region):
        row, rows, lane, lanes = region
        return row - self.regions[i][1][0], rows, lane, lanes

    def gather(self, k):
        self.wait()
        if k == self.depth - 1:
            self.add(k, last=True)

        def ref(i, region):
            row, rows, lane, lanes = self.local(i, region)
            return self.space.at[pl.ds(aligned(row, 16), rows), pl.ds(aligned(lane, 128), lanes)]

        for i, order in enumerate(self.orders):
            axis = order[k]
            mine = ref(i, self.regions[i][k + 1])
            for s in range(1, axis["size"]):
                to = lax.rem(axis["index"] + s, axis["size"])
                frm = lax.rem(axis["index"] + axis["size"] - s, axis["size"])
                slot = self.take(i)
                made = self.remote(i, mine, mine, slot, axis["at"](to))
                made.start()
                theirs = ref(i, self.share(self.regions[i][k], axis, frm))
                self.waits.append((made, self.remote(i, theirs, theirs, slot, axis["at"](frm))))
                self.sent.append((axis["link"], self.regions[i][k + 1][1] * self.regions[i][k + 1][3] * 2))

    def result(self, i, index, section):
        rows = self.regions[i][1][1]
        lane = aligned(self.lane_of(section) + i * PART, PART)
        return self.env["o"].at[section, pl.ds(aligned(index * rows, 16), rows), pl.ds(lane, PART)]

    def gathered(self, i):
        return self.space.at[pl.ds(0, self.regions[i][1][1]), pl.ds(i * PART, PART)]

    def deliver(self, i, s, straight):
        axis, section = self.orders[i][0], self.env["section"]
        recv = None if straight else self.env["ar_other"].at[self.layer, self.index, i, s]
        where = dict(axis["at"](lax.rem(axis["index"] + s, axis["size"])), section=self.layer)
        target = self.result(i, axis["index"], section)
        return self.remote(i, self.gathered(i), target, self.slot[i] + s, where, recv)

    def arrival(self, i, s, straight):
        axis, section = self.orders[i][0], self.env["section"]
        recv = None if straight else self.env["ar_other"].at[self.layer, self.index, i, s]
        index = lax.rem(axis["index"] + axis["size"] - s, axis["size"])
        frm = section if straight else 1 - section
        where = dict(axis["at"](index), section=frm)
        return self.remote(i, self.gathered(i), self.result(i, index, frm), self.slot[i] + s, where, recv)

    def kept(self, i):
        sem = self.env["ar_recv"].at[self.layer, self.index, i, self.slot[i]]
        target = self.result(i, self.orders[i][0]["index"], self.env["section"])
        return pltpu.make_async_copy(self.gathered(i), target, sem)

    def give(self):
        self.wait()

        @pl.when(self.env["section"] == self.layer)
        def _():
            for i in range(2):
                for s in range(1, self.orders[i][0]["size"]):
                    self.deliver(i, s, True).start()
                self.kept(i).start()

        @pl.when(self.env["section"] != self.layer)
        def _():
            for i in range(2):
                for s in range(self.orders[i][0]["size"] - 1, -1, -1):
                    self.deliver(i, s, False).start()

        for i, order in enumerate(self.orders):
            self.sent.append((order[0]["link"], self.regions[i][1][1] * PART * 2 * (order[0]["size"] - 1)))

    def finish(self):
        @pl.when(self.env["section"] == self.layer)
        def _():
            for i in range(2):
                size = self.orders[i][0]["size"]
                self.kept(i).wait()
                for s in range(1, size):
                    self.deliver(i, s, True).wait_send()
                    self.arrival(i, s, True).wait_recv()
                for s in range(size):
                    self.arrival(i, s, False).wait_recv()

        @pl.when(self.env["section"] != self.layer)
        def _():
            for i in range(2):
                for s in range(self.orders[i][0]["size"]):
                    self.deliver(i, s, False).wait_send()


class Order:
    RATE, HOP = 70e3, 1.8

    def __init__(self):
        self.now = 0.0
        self.free = {}
        self.going = []

    def sent(self, copies):
        end = self.now
        for link, size in copies:
            self.free[link] = max(self.now, self.free.get(link, 0.0)) + size / self.RATE
            end = max(end, self.free[link])
        return end + self.HOP

    def begin(self, one, i):
        end = self.sent(one.start_part(i))
        if i == 0:
            one.due = end
        else:
            one.due = max(one.due, end)
            self.going.append(one)

    def advance(self, one):
        self.now = max(self.now, one.due) + 0.4
        one.due = self.sent(one.advance())
        if one.done:
            self.going.remove(one)

    def work(self, cost):
        self.now += cost
        while True:
            due = [x for x in self.going if x.due <= self.now and x.free_to_go]
            if not due:
                return
            self.advance(min(due, key=lambda x: x.due))

    def drain(self):
        while self.going:
            self.advance(min(self.going, key=lambda x: x.due))


def kernel(dims, steps, seqs, views, frames, grad_out, weights, gains, shifts, recurs, lengths, masks, o, gf, vectors, f_own, f_far, p_own, p_far, g3, wc, wr1, src_t, live, turn,
           staged, heads, tails, v, vecs, rows, hid, coef, tot, vtot, levels, column, counts, cnt_p, cnt_z, slim_p, slim_z,
           wide_p, wide_z, space, sems, v_sems, stage_sem, credit, pl_send, pl_recv, z_send, z_recv, ar_send, ar_recv,
           ar_other):
    nz, ny, nx = dims
    np_ = ny * nx
    span = steps * seqs
    total_rows = 2 * span
    sent_rows = total_rows + 16
    pairs = steps // 2
    section = lax.axis_index("section")
    other = 1 - section
    b = lax.axis_index("batch")
    mp = lax.rem(b, np_)
    mz = b // np_

    def at_plane(i):
        return {"batch": b - mp + i}

    def at_z(i):
        return {"batch": b + (i - mz) * np_}

    def axis_of(link, size, stride):
        index = lax.rem(b // stride, size)
        return dict(link=link, size=size, index=index, at=lambda i: {"batch": b + (i - index) * stride})

    axes = [axis_of("x", nx, 1), axis_of("y", ny, nx), axis_of("z", nz, np_)]
    axes = [a for a in axes if a["size"] > 1]
    orders = (axes, [axes[1], axes[0], *axes[2:]] if len(axes) > 1 else axes)
    sibling = {"section": other}

    def local(src, dst, slot):
        return pltpu.make_async_copy(src, dst, sems.at[0, slot])

    def across(src, dst, slot):
        return pltpu.make_async_remote_copy(
            src_ref=src, dst_ref=dst, send_sem=sems.at[1, slot], recv_sem=sems.at[2, slot],
            device_id=sibling, device_id_type=MESH,
        )

    half = frames.shape[3]
    width = 2 * half
    lead = W - half
    rest = width - W
    full = rest // 128 * 128

    def fetch(source, m):
        return pltpu.make_async_copy(source.at[m], staged.at[m], stage_sem.at[m])

    def by_units(source, target, m):
        fetch(source, m).wait()

        @pl.when(section == 0)
        def _():
            pad = jnp.zeros((2 * seqs, lead), F32)

            def place(i, _):
                x = staged[m, pl.ds(2 * i, 2)].astype(F32).reshape(2 * seqs, half)
                to = pl.ds(aligned(m * span + 2 * i * seqs, 16), 2 * seqs)
                target[to, :] = jnp.concatenate([x, pad], axis=1).astype(BF16)
                return 0

            lax.fori_loop(0, pairs, place, 0)

        @pl.when(section == 1)
        def _():
            pad = jnp.zeros((2 * seqs, 2 * lead), F32)

            def place(i, _):
                x = staged[m, pl.ds(2 * i, 2)].astype(F32).reshape(2 * seqs, half)
                to = pl.ds(aligned(m * span + 2 * i * seqs, 16), 2 * seqs)
                target[to, :] = jnp.concatenate([x[:, lead:], pad], axis=1).astype(BF16)
                return 0

            lax.fori_loop(0, pairs, place, 0)

    def patch_heads(target, m):
        @pl.when(section == 0)
        def _():
            lane = lax.broadcasted_iota(jnp.int32, (2 * seqs, 128), 1)

            def place(i, _):
                to = pl.ds(aligned(m * span + 2 * i * seqs, 16), 2 * seqs)
                head = heads[m, pl.ds(2 * i, 2)].astype(F32).reshape(2 * seqs, 128)
                head = pltpu.roll(head, 128 - lead, 1)
                old = target[to, W - 128 :].astype(F32)
                target[to, W - 128 :] = jnp.where(lane < 128 - lead, old, head).astype(BF16)
                return 0

            lax.fori_loop(0, pairs, place, 0)

    def pieces(row, count, u, block, spot):
        r = pl.ds(row, count)
        to = pl.ds(0, count)
        if u == 0:
            return [(weights.at[0, r, pl.ds(0, W)], block.at[to, :])]
        return [
            (weights.at[0, r, pl.ds(W, full)], block.at[to, pl.ds(0, full)]),
            (weights.at[0, r, pl.ds(W + full, rest - full)], tails.at[spot, to, :]),
        ]

    rows_of = {0: (0, W), 1: (W, rest)}

    def w_plan(layer):
        mine, far = rows_of[layer], rows_of[1 - layer]
        plan = [
            (mine, layer, far, 1 - layer, wc.at[layer, 0], 2 * layer),
            (far, layer, mine, 1 - layer, wc.at[layer, 1], 2 * layer + 1),
        ]
        if layer == 1:
            plan.append((mine, 0, far, 1, wr1, 4))
        return plan

    late_row = (width - half) // 16 * 16
    late_shift = half - late_row
    late_plan = [
        ((0, W), 0, (late_row, width - late_row), 1, wc.at[0, 0], 0),
        ((0, W), 1, (late_row, width - late_row), 0, wc.at[0, 1], 1),
    ]
    slot_of = {0: 4, 1: 8, 2: 14}

    def local_w(plan, base, which):
        r, u, _, _, block, spot = plan[which]
        return [local(a, t, base + 2 * which + i) for i, (a, t) in enumerate(pieces(*r, u, block, spot))]

    def across_w(plan, base, which):
        _, _, r, u, block, spot = plan[which]
        return [across(a, t, base + 2 * which + i) for i, (a, t) in enumerate(pieces(*r, u, block, spot))]

    def start_local_w(layer, plan, base):
        @pl.when(section == layer)
        def _():
            for which in range(len(plan)):
                for made in local_w(plan, base, which):
                    made.start()

    def start_across_w(layer, plan, base):
        @pl.when(section == layer)
        def _():
            for which in range(len(plan)):
                for made in across_w(plan, base, which):
                    made.start()

    def last_units(block, spot):
        def body(i, _):
            r = pl.ds(aligned(i * 128, 128), 128)
            x = tails[spot, r, :].astype(F32)
            x = jnp.concatenate([x, jnp.zeros((128, 128 - x.shape[1]), F32)], axis=1)
            block[r, full:] = x.astype(BF16)
            return 0

        lax.fori_loop(0, W // 128, body, 0)

    def wait_w(layer, plan, base, which):
        _, own_u, _, far_u, block, spot = plan[which]

        @pl.when(section == layer)
        def _():
            for made in local_w(plan, base, which):
                made.wait()
            if own_u == 1:
                last_units(block, spot)

        @pl.when(section != layer)
        def _():
            for made in across_w(plan, base, which):
                made.wait_recv()
            if far_u == 1:
                last_units(block, spot)

    def done_w(layer, plan, base):
        @pl.when(section == layer)
        def _():
            for which in range(len(plan)):
                for made in across_w(plan, base, which):
                    made.wait_send()

    def heads_copy(source, slot):
        return across(source.at[:, :, :, pl.ds(0, 128)], heads, slot)

    def wait_heads(source, slot):
        @pl.when(section == 0)
        def _():
            heads_copy(source, slot).wait_recv()

        @pl.when(section == 1)
        def _():
            heads_copy(source, slot).wait_send()

    fetch(frames, 0).start()
    fetch(frames, 1).start()
    for layer in range(2):
        start_local_w(layer, w_plan(layer), slot_of[layer])

    barrier = pltpu.get_barrier_semaphore()
    greeted = [dict(sibling)]
    greeted += [at_plane(lax.rem(mp + k, np_)) for k in range(1, np_)]
    greeted += [at_z(lax.rem(mz + k, nz)) for k in range(1, nz)]
    for axis in axes[:2]:
        for s in range(1, axis["size"]):
            greeted.append(dict(axis["at"](lax.rem(axis["index"] + s, axis["size"])), section=other))
    for where in greeted:
        pl.semaphore_signal(barrier, inc=1, device_id=where, device_id_type=MESH)

    for k, (x, fill) in enumerate(((gains, 0.0), (shifts, -1e30), (recurs, 0.0))):
        vecs[section, k : k + 1, 0:width] = x[...]
        vecs[section, k : k + 1, width:] = jnp.full((1, 2 * W - width), fill, F32)
    vecs[section, 3:8, :] = jnp.zeros((5, 2 * W), F32)

    gap = jnp.zeros((W - rest, W), BF16)

    @pl.when(section == 0)
    def _():
        wc[0, 1, rest:, :] = gap
        wc[1, 1, rest:, :] = gap

    @pl.when(section == 1)
    def _():
        wc[0, 0, rest:, :] = gap
        wc[1, 0, rest:, :] = gap
        wr1[rest:, :] = gap

    for spot in (0, 2):
        tails[spot, rest:, :] = jnp.zeros((W - rest, rest - full), BF16)
    for spare in (f_own, p_own, g3.at[0], g3.at[1]):
        spare[sent_rows:, :] = jnp.zeros((spare.shape[0] - sent_rows, W), BF16)

    pl.semaphore_wait(barrier, len(greeted))

    @pl.when(section == 1)
    def _():
        heads_copy(frames, 1).start()

    start_across_w(0, w_plan(0), slot_of[0])
    send_vec = across(vecs.at[section], vecs.at[section], 3)
    send_vec.start()

    def stage_copy(where, rnd, slot, k, back):
        buf, parity, size, me, at, send, recv = where
        there = at(lax.rem(me + (size - k if back else k), size))
        ref = buf.at[parity, slot]
        return pltpu.make_async_remote_copy(
            src_ref=ref, dst_ref=ref, send_sem=send.at[rnd, k], recv_sem=recv.at[rnd, k],
            device_id=there, device_id_type=MESH,
        )

    def in_plane(buf, parity):
        return (buf, parity, np_, mp, at_plane, pl_send, pl_recv)

    def in_line(buf, parity):
        return (buf, parity, nz, mz, at_z, z_send, z_recv)

    def stage_start(where, rnd, value):
        buf, parity, size, me = where[:4]
        buf[parity, me] = value
        for k in range(1, size):
            stage_copy(where, rnd, me, k, False).start()

    def stage_wait(where, rnd):
        size, me = where[2:4]
        for k in range(1, size):
            stage_copy(where, rnd, me, k, False).wait_send()
            stage_copy(where, rnd, lax.rem(me + size - k, size), k, True).wait_recv()

    def add_slots(where):
        buf, parity, size = where[:3]
        total = buf[parity, 0]
        for k in range(1, size):
            total = total + buf[parity, k]
        return total

    groups = lengths.shape[1]
    s_at = lax.broadcasted_iota(jnp.int32, (seqs, groups), 0)
    g_at = lax.broadcasted_iota(jnp.int32, (seqs, groups), 1) * views
    there = (s_at >= g_at) & (s_at < g_at + views)
    position = lax.broadcasted_iota(jnp.int32, (seqs, 128), 1)
    local_counts = []
    for m in range(2):
        turn[...] = jnp.zeros_like(turn)
        turn[0:steps, 0:seqs] = masks[m].astype(F32)
        mask = turn[...].T[0:seqs]
        length = jnp.broadcast_to(lengths[m : m + 1, :], (seqs, groups)).astype(F32)
        limit = jnp.sum(jnp.where(there, length, 0.0), axis=1, keepdims=True)
        alive = (position.astype(F32) < limit) & ((mask > 0.0) | (position == 0))
        alive = jnp.where(position < steps, alive.astype(F32), 0.0)
        total = jnp.zeros((seqs, 128), F32)
        for t in range(steps):
            at = m * span + t * seqs
            cells = jnp.broadcast_to(alive[:, t : t + 1], (seqs, 128))
            live[at : at + seqs, :] = cells
            total = total + cells
        local_counts.append(jnp.sum(total, axis=0, keepdims=True))
    n_own = jnp.concatenate(local_counts * 4, axis=0)

    cnt_plane, cnt_line = in_plane(cnt_p, 0), in_line(cnt_z, 0)
    stage_start(cnt_plane, 0, n_own)

    def vec_of(layer, k):
        return vecs[layer, k : k + 1, pl.ds(aligned(section * W, W), W)]

    def matmul_to(out, a, w, first, m):
        r = pl.ds(m * span, span)

        def body(i, _):
            c = pl.ds(aligned(i * HALF, HALF), HALF)
            y = dot(a[r, :], w[:, c], ((1,), (0,)))
            out[r, c] = y if first else out[r, c] + y
            return 0

        lax.fori_loop(0, 2, body, 0)

    def packed(x, y):
        return jnp.concatenate([z[:, k * QUART : (k + 1) * QUART] for z in (x, y) for k in range(4)], axis=0)

    def unpacked(x):
        return jnp.concatenate([x[k : k + 1] for k in range(4)], axis=1)

    def merge_slots(where, counts_of):
        buf, parity, size = where[:3]
        s = [buf[parity, k, 0:4, :] for k in range(size)]
        q = [buf[parity, k, 4:8, :] for k in range(size)]
        n = [wide(counts_of(k), 2) for k in range(size)]
        total, squares, count = sum(s[1:], s[0]), sum(q[1:], q[0]), sum(n[1:], n[0])
        mean = total / count
        for k in range(size):
            d = s[k] / n[k] - mean
            squares = squares + n[k] * d * d
        return jnp.concatenate([total, squares], axis=0)

    def slim_round(which, m):
        return 1 + 2 * which + m, in_plane(slim_p, 2 * m + which % 2), in_line(slim_z, 2 * m + which % 2)

    def forward_stats(layer, m):
        start = jnp.sum(rows[layer, m * span : m * span + seqs, :], axis=0, keepdims=True) * (1.0 / seqs)

        def body(i, carry):
            s, q = carry
            r = pl.ds(aligned(m * span + i * (2 * seqs), 16), 2 * seqs)
            d = rows[layer, r, :] - start
            kept = wide(live[r, :], 8) * d
            return s + fold(kept), q + fold(kept * d)

        zero = jnp.zeros((8, W), F32)
        s, q = lax.fori_loop(0, pairs, body, (zero, zero))
        s, q = jnp.sum(s, axis=0, keepdims=True), jnp.sum(q, axis=0, keepdims=True)
        n = wide(local_counts[m], 8)
        rnd, plane, _ = slim_round(layer, m)
        stage_start(plane, rnd, packed(s + n * start, jnp.maximum(q - s * s / n, 0.0)))

    def forward_middle(layer, m):
        rnd, plane, line = slim_round(layer, m)
        stage_wait(plane, rnd)
        stage_start(line, rnd, merge_slots(plane, lambda k: cnt_p[0, k, m : m + 1, :]))

    def forward_end(layer, m):
        rnd, _, line = slim_round(layer, m)
        stage_wait(line, rnd)
        value = merge_slots(line, lambda k: cnt_z[0, k, m : m + 1, :])
        count = wide(counts[m : m + 1, :], 8)
        mean = unpacked(value[0:4]) / count
        scale = lax.rsqrt(unpacked(value[4:8]) / count + EPS)
        coef[layer, 2 * m : 2 * m + 1, :] = mean
        coef[layer, 2 * m + 1 : 2 * m + 2, :] = scale
        slope = vec_of(layer, 0) * scale
        coef[layer, 4 + 2 * m : 5 + 2 * m, :] = slope
        coef[layer, 5 + 2 * m : 6 + 2 * m, :] = vec_of(layer, 1) - mean * slope

    def forward_scan(layer, m, passes):
        rec = vec_of(layer, 2)
        slope = coef[layer, 4 + 2 * m : 5 + 2 * m, :]
        shift = coef[layer, 5 + 2 * m : 6 + 2 * m, :]

        def body(i, carry):
            h, level = carry
            r = pl.ds(aligned(m * span + i * (2 * seqs), 16), 2 * seqs)
            x = rows[layer, r, :] * slope + shift
            lv = wide(live[r, :], 8)
            alive = lv > 0.0
            both = []
            for k in range(2):
                part = slice(k * seqs, (k + 1) * seqs)
                z = x[part] + rec * h
                soft = jnp.maximum(z, 0.0) + jnp.log(1.0 + jnp.exp(-jnp.abs(z)))
                h = jnp.where(alive[part], soft, h)
                both.append(h)
            two = jnp.concatenate(both, axis=0)
            hid[layer, r, :] = two
            if passes:
                p_own[r, :] = two.astype(BF16)
                level = level + fold(lv * two)
            return h, level

        _, level = lax.fori_loop(0, pairs, body, (jnp.zeros((seqs, W), F32), jnp.zeros((8, W), F32)))
        if not passes:
            return None
        level = jnp.sum(level, axis=0, keepdims=True)
        levels[1:2, :] = level if m == 0 else levels[1:2, :] + level
        here = pl.ds(m * span, span)
        made = across(p_own.at[here, :], p_far.at[here, :], 18 + m)
        made.start()
        return made

    def backward_scan(layer, m, above, between=lambda: None):
        gain, shift, recur = vec_of(layer, 0), vec_of(layer, 1), vec_of(layer, 2)
        for lq in range(4):
            lanes = slice(lq * QUART, (lq + 1) * QUART)
            gq, sq, rec = gain[:, lanes], shift[:, lanes], recur[:, lanes]
            mean = coef[layer, 2 * m : 2 * m + 1, lanes]
            scale = coef[layer, 2 * m + 1 : 2 * m + 2, lanes]

            def body(i, carry):
                down, s1, s2, rsum, sqh, sqa = carry
                i = pairs - 1 - i
                start = m * span + i * (2 * seqs)
                r = pl.ds(aligned(start, 16), 2 * seqs)
                before = pl.ds(aligned(jnp.maximum(start - seqs, 0), 8), seqs)
                normed = (rows[layer, r, lanes] - mean) * scale
                drive = gq * normed + sq
                h2 = hid[layer, r, lanes]
                hb = jnp.where(i > 0, hid[layer, before, lanes], 0.0)
                lv = wide(live[r, :], 2)
                up = above[r, lanes].astype(F32)
                res = f_own[r, lanes].astype(F32)
                aux = res + h2 if layer == 1 else res
                sqh = sqh + fold(lv * (h2 * h2))
                sqa = sqa + fold(lv * (aux * aux))
                grads = [None, None]
                for k in (1, 0):
                    part = slice(k * seqs, (k + 1) * seqs)
                    prior = h2[0:seqs] if k == 1 else hb
                    slope = 0.5 + 0.5 * jnp.tanh(0.5 * (drive[part] + rec * prior))
                    total = up[part] + down
                    gd = lv[part] * slope * total
                    down = (1.0 - lv[part]) * total + rec * gd
                    grads[k] = gd
                    rsum = rsum + fold(gd * prior)
                gd2 = jnp.concatenate(grads, axis=0)
                hid[layer, r, lanes] = gd2
                return down, s1 + fold(gd2), s2 + fold(gd2 * normed), rsum, sqh, sqa

            z8 = jnp.zeros((8, QUART), F32)
            _, s1, s2, rsum, sqh, sqa = lax.fori_loop(
                0, pairs, body, (jnp.zeros((seqs, QUART), F32), z8, z8, z8, z8, z8)
            )
            for k, x in ((m, s1), (2 + m, s2)):
                tot[layer, k : k + 1, lanes] = jnp.sum(x, axis=0, keepdims=True)
            for k, x in ((4, rsum), (5, sqh), (6, sqa)):
                x = jnp.sum(x, axis=0, keepdims=True)
                tot[layer, k : k + 1, lanes] = x if m == 0 else tot[layer, k : k + 1, lanes] + x
            between()

    def backward_stats(layer, m):
        rnd, plane, _ = slim_round(3 - layer, m)
        stage_start(plane, rnd, packed(tot[layer, m : m + 1, :], tot[layer, 2 + m : 3 + m, :]))

    def backward_middle(layer, m):
        rnd, plane, line = slim_round(3 - layer, m)
        stage_wait(plane, rnd)
        stage_start(line, rnd, add_slots(plane))

    def backward_end(layer, m):
        rnd, _, line = slim_round(3 - layer, m)
        stage_wait(line, rnd)
        value = add_slots(line)
        tot[layer, m : m + 1, :] = unpacked(value[0:4])
        tot[layer, 2 + m : 3 + m, :] = unpacked(value[4:8])

    def grad_rows(layer, m, slot):
        gain = vec_of(layer, 0)
        for lh in range(2):
            lanes = slice(lh * HALF, (lh + 1) * HALF)
            mean = coef[layer, 2 * m : 2 * m + 1, lanes]
            scale = coef[layer, 2 * m + 1 : 2 * m + 2, lanes]
            count = wide(counts[m : m + 1, :], 4)
            first = tot[layer, m : m + 1, lanes] / count
            second = tot[layer, 2 + m : 3 + m, lanes] / count * scale
            k = scale * gain[:, lanes]

            def body(i, acc):
                r = pl.ds(aligned(m * span + i * (2 * seqs), 16), 2 * seqs)
                y = hid[layer, r, lanes] - first - (rows[layer, r, lanes] - mean) * second
                y = wide(live[r, :], 4) * (k * y)
                g3[0, r, lanes] = y.astype(BF16)
                return acc + fold(y)

            acc = lax.fori_loop(0, pairs, body, jnp.zeros((8, HALF), F32))
            acc = jnp.sum(acc, axis=0, keepdims=True)
            if m == 0:
                levels[4:5, lanes] = acc
            else:
                top = lax.broadcasted_iota(jnp.int32, (16, HALF), 0) == 0
                minus = jnp.where(top, -(levels[4:5, lanes] + acc), 0.0)
                g3[0, total_rows:sent_rows, lanes] = minus.astype(BF16)
        here = pl.ds(0, span) if m == 0 else pl.ds(span, span + 16)
        made = across(g3.at[0, here, :], g3.at[1, here, :], slot + m)
        made.start()
        return made

    sums_round = {1: (1, 10), 0: (0, 11)}

    def sums_start(layer):
        parity, rnd = sums_round[layer]
        own_sum = -g3[0, total_rows:sent_rows, :].astype(F32)[0:1]
        far_sum = -g3[1, total_rows:sent_rows, :].astype(F32)[0:1]
        value = jnp.concatenate([own_sum, far_sum, tot[layer, 4:7, :], jnp.zeros((3, W), F32)], axis=0)
        stage_start(in_plane(wide_p, parity), rnd, value)

    def sums_middle(layer):
        parity, rnd = sums_round[layer]
        stage_wait(in_plane(wide_p, parity), rnd)
        stage_start(in_line(wide_z, parity), rnd, add_slots(in_plane(wide_p, parity)))

    def sums_end(layer):
        parity, rnd = sums_round[layer]
        stage_wait(in_line(wide_z, parity), rnd)
        vtot[layer] = add_slots(in_line(wide_z, parity))
        tot[layer, 4:7, :] = vtot[layer, 2:5, :]
        tot[layer, 7:8, :] = wide(counts[0:1, :] + counts[1:2, :], 8)
        env["summed"].add(layer)

        @pl.when(section == layer)
        def _():
            pltpu.make_async_copy(tot.at[layer], v.at[section], v_sems.at[0]).start()

        @pl.when(section != layer)
        def _():
            v_across(layer).start()

    def v_across(layer):
        return pltpu.make_async_remote_copy(
            src_ref=tot.at[layer], dst_ref=v.at[section], send_sem=v_sems.at[1], recv_sem=v_sems.at[2],
            device_id=sibling, device_id_type=MESH,
        )

    def transpose(src, begin=0, end=W // 128):
        def body(j, _):
            c = pl.ds(aligned(j * 128, 128), 128)
            src_t[c, 0:total_rows] = src[0:total_rows, c].T
            return 0

        lax.fori_loop(begin, end, body, 0)

    def transpose_level(src, layer):
        top = lax.broadcasted_iota(jnp.int32, (16, W), 0) == 0
        src[total_rows:sent_rows, :] = jnp.where(top, levels[2 + layer : 3 + layer, :], 0.0).astype(BF16)

        def body(j, _):
            c = pl.ds(aligned(j * 128, 128), 128)
            src_t[c, total_rows:] = src[total_rows:, c].T
            level = src[total_rows:sent_rows, c].astype(F32)[0:1]
            column[layer, c, :] = jnp.broadcast_to(level, (128, 128)).T.astype(BF16)
            return 0

        lax.fori_loop(0, W // 128, body, 0)

    def weight_part(block, grads, c):
        lanes = pl.ds(c * HALF, HALF)

        def body(j, _):
            r = pl.ds(aligned(j * HALF, HALF), HALF)
            block[r, lanes] = dot(src_t[r, :], grads[:, lanes], ((1,), (0,))).astype(BF16)
            return 0

        lax.fori_loop(0, W // HALF, body, 0)

    def source_grad(store, w_own, w_far, between):
        for m in range(2):
            r = pl.ds(m * span, span)

            for i in range(2):
                c = pl.ds(i * HALF, HALF)
                y = dot(g3[0, r, :], w_own[c, :], ((1,), (1,))) + dot(g3[1, r, :], w_far[c, :], ((1,), (1,)))
                store(r, c, y)
                between()

    env = dict(summed=set(), vtot=vtot, column=column, space=space, ar_send=ar_send, ar_recv=ar_recv,
               ar_other=ar_other, o=o, section=section, here={"batch": b})
    blocks = {
        (1, 0): f_far.at[pl.ds(0, W), :],
        (1, 1): p_far.at[pl.ds(0, W), :],
        (0, 0): wc.at[1, 1],
        (0, 1): wr1,
    }
    parts = {}
    for layer in (1, 0):
        for index in range(2 * PAIRS):
            part, side = index // PAIRS, index % PAIRS

            def lane_of(sec, part=part, side=side):
                return (sec if part == 0 else 1 - sec) * W + side * 2 * PART

            block = blocks[layer, part].at[:, pl.ds(side * 2 * PART, 2 * PART)]
            parts[layer, index] = Reduction(env, layer, index, block, orders, lane_of)
    order = Order()

    def weight_grads(layer, between):
        for part in range(2):
            if part == 1:
                between()
            for c in range(2):
                weight_part(blocks[layer, part], g3.at[part], c)
                order.work(2.0)
                for k in range(c * HALF // PART, (c + 1) * HALF // PART):
                    order.begin(parts[layer, part * PAIRS + k // 2], k % 2)

    def arrived(layer, sends):
        for made in sends:
            made.wait()
        sums_start(layer)

    send_f = []
    for m in range(2):
        by_units(frames, f_own, m)
        fetch(grad_out, m).start()
        if m == 0:
            wait_heads(frames, 1)
        patch_heads(f_own, m)
        here = pl.ds(m * span, span)
        made = across(f_own.at[here, :], f_far.at[here, :], (0, 24)[m])
        made.start()
        send_f.append(made)
    start_across_w(1, w_plan(1), slot_of[1])
    stage_wait(cnt_plane, 0)
    stage_start(cnt_line, 0, add_slots(cnt_plane))
    wait_w(0, w_plan(0), slot_of[0], 0)
    matmul_to(rows.at[0], f_own, wc.at[0, 0], True, 0)
    matmul_to(rows.at[0], f_own, wc.at[0, 0], True, 1)
    wait_w(0, w_plan(0), slot_of[0], 1)
    send_f[0].wait()
    matmul_to(rows.at[0], f_far, wc.at[0, 1], False, 0)
    forward_stats(0, 0)
    send_f[1].wait()

    @pl.when(section == 1)
    def _():
        heads_copy(grad_out, 2).start()

    matmul_to(rows.at[0], f_far, wc.at[0, 1], False, 1)
    forward_middle(0, 0)
    forward_stats(0, 1)
    send_vec.wait_send()
    across(vecs.at[other], vecs.at[other], 3).wait_recv()
    stage_wait(cnt_line, 0)
    counts[...] = add_slots(cnt_line)
    forward_end(0, 0)
    sends = [forward_scan(0, 0, True)]
    forward_middle(0, 1)
    by_units(grad_out, g3.at[1], 0)
    wait_heads(grad_out, 2)
    patch_heads(g3.at[1], 0)
    forward_end(0, 1)
    sends.append(forward_scan(0, 1, True))
    wait_w(1, w_plan(1), slot_of[1], 0)
    matmul_to(rows.at[1], p_own, wc.at[1, 0], True, 0)
    wait_w(1, w_plan(1), slot_of[1], 1)
    sends[0].wait()
    matmul_to(rows.at[1], p_far, wc.at[1, 1], False, 0)
    forward_stats(1, 0)
    matmul_to(rows.at[1], p_own, wc.at[1, 0], True, 1)
    forward_middle(1, 0)
    sends[1].wait()
    matmul_to(rows.at[1], p_far, wc.at[1, 1], False, 1)
    forward_stats(1, 1)
    done_w(0, w_plan(0), slot_of[0])

    start_local_w(0, late_plan, slot_of[2])
    start_across_w(0, late_plan, slot_of[2])

    @pl.when(section == 1)
    def _():
        wc[0, 1, width - late_row :, :] = jnp.zeros((W - width + late_row, W), BF16)

    def source_level():
        def body(i, acc):
            r = pl.ds(aligned(i * (2 * seqs), 16), 2 * seqs)
            return acc + fold(wide(live[r, :], 8) * f_own[r, :].astype(F32))

        acc = lax.fori_loop(0, 2 * pairs, body, jnp.zeros((8, W), F32))
        levels[0:1, :] = jnp.sum(acc, axis=0, keepdims=True)

    forward_end(1, 0)
    forward_scan(1, 0, False)
    forward_middle(1, 1)
    by_units(grad_out, g3.at[1], 1)
    patch_heads(g3.at[1], 1)
    source_level()
    forward_end(1, 1)
    level_plane, level_line = in_plane(wide_p, 0), in_line(wide_z, 0)
    stage_start(level_plane, 9, jnp.concatenate([levels[0:2, :], jnp.zeros((6, W), F32)], axis=0))
    forward_scan(1, 1, False)
    backward_scan(1, 0, g3.at[1])
    backward_stats(1, 0)
    stage_wait(level_plane, 9)
    stage_start(level_line, 9, add_slots(level_plane))
    backward_scan(1, 1, g3.at[1])
    backward_stats(1, 1)
    backward_middle(1, 0)
    pl.semaphore_signal(credit.at[0], inc=1, device_id=sibling, device_id_type=MESH)
    transpose(p_own, 0, W // 256)
    backward_middle(1, 1)
    backward_end(1, 0)
    pl.semaphore_wait(credit.at[0], 1)
    sends = [grad_rows(1, 0, 20)]
    transpose(p_own, W // 256)
    stage_wait(level_line, 9)
    levels[2:4, :] = (add_slots(level_line) / wide(counts[0:1, :] + counts[1:2, :], 8))[0:2]
    transpose_level(p_own, 1)
    backward_end(1, 1)
    sends.append(grad_rows(1, 1, 20))
    weight_grads(1, lambda: arrived(1, sends))
    wait_w(1, w_plan(1), slot_of[1], 2)
    done_w(1, w_plan(1), slot_of[1])

    def keep_down(r, c, y):
        p_own[r, c] = y.astype(BF16)

    source_grad(keep_down, wc.at[1, 0], wr1, lambda: order.work(2.0))
    pl.semaphore_signal(credit.at[1], inc=1, device_id=sibling, device_id_type=MESH)
    sums_middle(1)
    backward_scan(0, 0, p_own, lambda: order.work(0.6))
    backward_stats(0, 0)
    backward_scan(0, 1, p_own, lambda: order.work(0.6))
    backward_stats(0, 1)
    backward_middle(0, 0)
    sums_end(1)
    transpose(f_own)
    transpose_level(f_own, 0)
    backward_middle(0, 1)
    order.work(3.0)
    backward_end(0, 0)
    pl.semaphore_wait(credit.at[1], 1)
    sends = [grad_rows(0, 0, 22)]
    backward_end(0, 1)
    sends.append(grad_rows(0, 1, 22))
    order.work(2.0)
    weight_grads(0, lambda: arrived(0, sends))
    wait_w(0, late_plan, slot_of[2], 0)
    wait_w(0, late_plan, slot_of[2], 1)
    done_w(0, late_plan, slot_of[2])

    def keep_source(r, c, y):
        rows[0, r, c] = y

    fetch(grad_out, 0).start()
    fetch(grad_out, 1).start()
    sums_middle(0)
    source_grad(keep_source, wc.at[0, 0], wc.at[0, 1], lambda: order.work(2.0))
    sums_end(0)

    def give(m):
        return pltpu.make_async_copy(staged.at[m], gf.at[m], stage_sem.at[m])

    for m in range(2):
        fetch(grad_out, m).wait()

        def finish_frames(i, _, m=m):
            straight = staged[m, pl.ds(2 * i, 2)].astype(F32).reshape(2 * seqs, half)
            y = rows[0, pl.ds(aligned(m * span + 2 * i * seqs, 8), 2 * seqs), :]
            y = jnp.where(section == 0, y[:, :half], y[:, late_shift : late_shift + half])
            staged[m, pl.ds(2 * i, 2)] = (y + straight).reshape(2, seqs, half).astype(BF16)
            return 0

        lax.fori_loop(0, pairs, finish_frames, 0)
        give(m).start()
        order.work(2.0)
    order.drain()
    for m in range(2):
        give(m).wait()

    for layer in range(2):

        @pl.when(section == layer)
        def _(layer=layer):
            pltpu.make_async_copy(tot.at[layer], v.at[section], v_sems.at[0]).wait()
            pltpu.make_async_remote_copy(
                src_ref=tot.at[layer], dst_ref=v.at[other], send_sem=v_sems.at[1], recv_sem=v_sems.at[2],
                device_id=sibling, device_id_type=MESH,
            ).wait_recv()

        @pl.when(section != layer)
        def _(layer=layer):
            v_across(layer).wait_send()

    own_part, far_part = v[section], v[other]
    first = jnp.where(section == 0, own_part, far_part)
    second = jnp.where(section == 0, far_part, own_part)
    for row, terms in ((0, (2, 3)), (1, (0, 1)), (2, (4,))):
        for lane, x in ((0, first), (W, second)):
            total = x[terms[0] : terms[0] + 1, :]
            for k in terms[1:]:
                total = total + x[k : k + 1, :]
            vectors[row : row + 1, lane : lane + W] = total
    squares = jnp.sum(first[5:7, :] + second[5:7, :], axis=1, keepdims=True)
    root = jnp.sqrt(squares / (first[7:8, 0:1] * width))
    for k in range(2):
        vectors[3 + k : 4 + k, :] = jnp.broadcast_to(root[k : k + 1], (1, 2 * W))
    vectors[5:8, :] = jnp.zeros((3, 2 * W), F32)


def write_results(o, gf, vectors, grad_weight, grad_frames, grad_gains, grad_shifts, grad_recurs, table):
    width = grad_weight.shape[2]
    grad_weight[0] = o[...][:, :width].astype(F32)
    grad_frames[...] = gf[...]

    @pl.when(pl.program_id(0) == 0)
    def _():
        for k, out in enumerate((grad_gains, grad_shifts, grad_recurs)):
            out[...] = vectors[k : k + 1, 0:width]
        table[...] = jnp.concatenate([vectors[3:4, 0:1], vectors[4:5, 0:1]], axis=1)


def results(o, gf, vectors):
    micro, steps, seqs, half = gf.shape
    width = 2 * half
    count = W * 2 // 256
    frames = micro * steps // count
    whole = lambda shape: pl.BlockSpec(shape, lambda i: (0, 0))
    out = pl.pallas_call(
        write_results,
        grid=(count,),
        in_specs=[
            pl.BlockSpec((256, 2 * W), lambda i: (i, 0)),
            pl.BlockSpec((frames, seqs, half), lambda i: (i, 0, 0)),
            whole((8, 2 * W)),
        ],
        out_specs=(
            pl.BlockSpec((1, 256, width), lambda i: (0, i, 0)),
            pl.BlockSpec((frames, seqs, half), lambda i: (i, 0, 0)),
            whole((1, width)),
            whole((1, width)),
            whole((1, width)),
            whole((1, 2)),
        ),
        out_shape=(
            jax.ShapeDtypeStruct((1, width, width), F32),
            jax.ShapeDtypeStruct((micro * steps, seqs, half), BF16),
            jax.ShapeDtypeStruct((1, width), F32),
            jax.ShapeDtypeStruct((1, width), F32),
            jax.ShapeDtypeStruct((1, width), F32),
            jax.ShapeDtypeStruct((1, 2), F32),
        ),
        compiler_params=pltpu.CompilerParams(vmem_limit_bytes=64 * 1024 * 1024),
    )(o.reshape(2 * W, 2 * W), gf.reshape(micro * steps, seqs, half), vectors)
    return out[1].reshape(gf.shape), out[0], *out[2:]


def whole_step(dims, frames, grad_out, weights, gains, shifts, recurs, lengths, masks):
    nz, ny, nx = dims
    micro, steps, seqs, half = frames.shape
    width = 2 * half
    views = seqs // lengths.shape[1]
    rows = micro * steps * seqs
    np_ = ny * nx
    wide_rows = (rows + 16 + 127) // 128 * 128
    across_first = max(nx, ny, nz if np_ == 1 else 1)
    copies = 2 * (nx + ny + nz) + across_first
    came_rows = (nx - 1) * (W // nx) + (ny - 1) * (W // np_) + (nz - 1) * max(W // np_ // nz, 16)
    any_ = pl.BlockSpec(memory_space=pl.ANY)
    held = pl.BlockSpec(memory_space=pltpu.VMEM)
    dma = pltpu.SemaphoreType.DMA
    return pl.pallas_call(
        functools.partial(kernel, dims, steps, seqs, views),
        out_shape=(
            jax.ShapeDtypeStruct((2, W, 2 * W), BF16),
            jax.ShapeDtypeStruct(frames.shape, BF16),
            jax.ShapeDtypeStruct((8, 2 * W), F32),
        ),
        in_specs=[any_] * 3 + [held] * 5,
        out_specs=(any_, any_, held),
        scratch_shapes=[
            pltpu.VMEM((wide_rows, W), BF16),
            pltpu.VMEM((rows, W), BF16),
            pltpu.VMEM((wide_rows, W), BF16),
            pltpu.VMEM((rows, W), BF16),
            pltpu.VMEM((2, wide_rows, W), BF16),
            pltpu.VMEM((2, 2, W, W), BF16),
            pltpu.VMEM((W, W), BF16),
            pltpu.VMEM((W, wide_rows), BF16),
            pltpu.VMEM((rows, 128), F32),
            pltpu.VMEM((128, 128), F32),
            pltpu.VMEM(frames.shape, BF16),
            pltpu.VMEM((micro, steps, seqs, 128), BF16),
            pltpu.VMEM((5, W, (width - W) % 128), BF16),
            pltpu.VMEM((2, 8, W), F32),
            pltpu.VMEM((2, 8, 2 * W), F32),
            pltpu.VMEM((2, rows, W), F32),
            pltpu.VMEM((2, rows, W), F32),
            pltpu.VMEM((2, 8, W), F32),
            pltpu.VMEM((2, 8, W), F32),
            pltpu.VMEM((2, 8, W), F32),
            pltpu.VMEM((8, W), F32),
            pltpu.VMEM((2, W, 128), BF16),
            pltpu.VMEM((8, 128), F32),
            pltpu.VMEM((1, np_, 8, 128), F32),
            pltpu.VMEM((1, nz, 8, 128), F32),
            pltpu.VMEM((4, np_, 8, QUART), F32),
            pltpu.VMEM((4, nz, 8, QUART), F32),
            pltpu.VMEM((2, np_, 8, W), F32),
            pltpu.VMEM((2, nz, 8, W), F32),
            pltpu.VMEM((2, 2 * PAIRS, max(came_rows, W), 2 * PART), BF16),
            dma((3, 25)),
            dma((3,)),
            dma((2,)),
            pltpu.SemaphoreType.REGULAR((2,)),
            dma((12, max(np_, 2))),
            dma((12, max(np_, 2))),
            dma((12, max(nz, 2))),
            dma((12, max(nz, 2))),
            dma((2, 2 * PAIRS, 2, copies)),
            dma((2, 2 * PAIRS, 2, copies)),
            dma((2, 2 * PAIRS, 2, across_first)),
        ],
        compiler_params=pltpu.CompilerParams(
            collective_id=0, has_side_effects=True, vmem_limit_bytes=64 * 1024 * 1024
        ),
    )(frames, grad_out, weights, gains, shifts, recurs, lengths, masks)


def shards(dims, frames, grad_out, weights, gains, shifts, recurs, lengths, masks):
    return results(*whole_step(dims, frames, grad_out, weights, gains, shifts, recurs, lengths, masks))


def solution(mesh):
    in_specs = (
        P(None, None, "batch", "section"),
        P(None, None, "batch", "section"),
        P("section", None, None),
        P("section", None),
        P("section", None),
        P("section", None),
        P(None, "batch"),
        P(None, None, "batch"),
    )
    out_specs = (
        P(None, None, "batch", "section"),
        P("section", None, None),
        P("section", None),
        P("section", None),
        P("section", None),
        P("section", None),
    )
    body = functools.partial(shards, grid_of(mesh.shape["batch"]))
    return jax.shard_map(body, mesh=mesh, in_specs=in_specs, out_specs=out_specs, check_vma=False)
```

```python
import functools

import jax
import jax.numpy as jnp
from jax import lax
from jax.experimental import pallas as pl
from jax.experimental.pallas import tpu as pltpu
from jax.sharding import PartitionSpec as P

EPS = 1e-05
W = 1024
HALF = W // 2
QUART = W // 4
PAIRS = 2
PART = W // PAIRS // 2
MESH = pl.DeviceIdType.MESH
F32 = jnp.float32
BF16 = jnp.bfloat16


def grid_of(size):
    if size == 16:
        return (4, 2, 2)
    if size == 128:
        return (8, 4, 4)
    return (size, 1, 1)


def aligned(x, k):
    return pl.multiple_of(x, k)


def wide(x, reps):
    return jnp.concatenate([x] * reps, axis=1)


def fold(x):
    rows = x.shape[0]
    total = x[0:8]
    for k in range(8, rows, 8):
        total = total + x[k : k + 8]
    return total


def dot(a, b, dims):
    return lax.dot_general(a, b, (dims, ((), ())), preferred_element_type=F32)


class Reduction:
    def __init__(self, env, layer, index, block, orders, lane_of):
        self.env, self.layer, self.index, self.block, self.orders = env, layer, index, block, orders
        self.lane_of = lane_of
        self.space = env["space"].at[layer, index]
        self.depth = len(orders[0])
        self.regions = [self.shares(i, order) for i, order in enumerate(orders)]
        self.step = 0
        self.waits = []
        self.slot = [0, 0]
        depth = self.depth
        self.steps = [functools.partial(self.scatter, k) for k in range(depth)]
        self.steps += [functools.partial(self.gather, k) for k in range(depth - 1, 0, -1)]
        self.steps += [self.give, self.finish]

    def shares(self, i, order):
        out = [(0, W, i * PART, PART)]
        for axis in order:
            out.append(self.share(out[-1], axis, axis["index"]))
        return out

    def share(self, region, axis, index):
        row, rows, lane, lanes = region
        by_row = min(axis["size"], rows // 16)
        rows, lanes = rows // by_row, lanes // (axis["size"] // by_row)
        if by_row == axis["size"]:
            return row + index * rows, rows, lane, lanes
        return row + lax.rem(index, by_row) * rows, rows, lane + index // by_row * lanes, lanes

    @property
    def free_to_go(self):
        return self.step != self.depth or self.layer in self.env["summed"]

    @property
    def done(self):
        return self.step >= len(self.steps)

    def advance(self):
        self.sent = []
        self.steps[self.step]()
        self.step += 1
        return self.sent

    def remote(self, i, src, dst, slot, where, recv=None):
        sems = (self.layer, self.index, i, slot)
        return pltpu.make_async_remote_copy(
            src_ref=src, dst_ref=dst, send_sem=self.env["ar_send"].at[sems],
            recv_sem=self.env["ar_recv"].at[sems] if recv is None else recv, device_id=where, device_id_type=MESH,
        )

    def wait(self):
        for made, came in self.waits:
            made.wait_send()
            came.wait_recv()
        self.waits = []

    def take(self, i):
        self.slot[i] += 1
        return self.slot[i] - 1

    def came_at(self, i, k, s):
        row = sum((a["size"] - 1) * self.regions[i][n + 1][1] for n, a in enumerate(self.orders[i][:k]))
        _, rows, _, lanes = self.regions[i][k + 1]
        return row + (s - 1) * rows, rows, i * PART, lanes

    def scatter(self, k):
        if k > 0:
            self.wait()
            self.add(k - 1)
        for i in range(2):
            self.scatter_part(i, k)

    def start_part(self, i):
        self.sent = []
        self.scatter_part(i, 0)
        if i == 1:
            self.step = 1
        return self.sent

    def scatter_part(self, i, k):
        axis = self.orders[i][k]
        for s in range(1, axis["size"]):
            other = lax.rem(axis["index"] + s, axis["size"])
            row, rows, lane, lanes = self.share(self.regions[i][k], axis, other)
            src = self.block.at[pl.ds(aligned(row, 16), rows), pl.ds(aligned(lane, 128), lanes)]
            at, n, at_lane, n_lanes = self.came_at(i, k, s)
            dst = self.space.at[pl.ds(at, n), pl.ds(at_lane, n_lanes)]
            made = self.remote(i, src, dst, self.take(i), axis["at"](other))
            made.start()
            self.waits.append((made, made))
            self.sent.append((axis["link"], rows * lanes * 2))

    def add(self, k, last=False):
        rows = self.regions[0][k + 1][1]
        size = min(rows, 32)
        out = []
        for i in range(2):
            row, _, lane, lanes = self.regions[i][k + 1]
            lane = aligned(lane, 128)
            extra = None
            if last:
                part = self.index // PAIRS
                first = aligned((self.index % PAIRS) * 2 * PART + lane, 128)
                extra = self.env["vtot"][self.layer, part : part + 1, pl.ds(first, lanes)]
            came = [self.came_at(i, k, s) for s in range(1, self.orders[i][k]["size"])]
            out.append((row, lane, lanes, came, self.local(i, self.regions[i][k + 1])[0], extra))

        def body(j, _):
            for row, lane, lanes, came, home, extra in out:
                here = pl.ds(aligned(row + j * size, 16), size)
                total = self.block[here, pl.ds(lane, lanes)].astype(F32)
                for at, _, at_lane, _ in came:
                    there = pl.ds(aligned(at + j * size, 16), size)
                    total = total + self.space[there, pl.ds(at_lane, lanes)].astype(F32)
                if last:
                    column = self.env["column"][self.layer, here, :].astype(F32)
                    total = total + wide(column, lanes // 128) * extra
                    to = pl.ds(aligned(home + j * size, 16), size)
                    self.space[to, pl.ds(lane, lanes)] = total.astype(BF16)
                else:
                    self.block[here, pl.ds(lane, lanes)] = total.astype(BF16)
            return 0

        lax.fori_loop(0, rows // size, body, 0)

    def local(self, i, region):
        row, rows, lane, lanes = region
        return row - self.regions[i][1][0], rows, lane, lanes

    def gather(self, k):
        self.wait()
        if k == self.depth - 1:
            self.add(k, last=True)

        def ref(i, region):
            row, rows, lane, lanes = self.local(i, region)
            return self.space.at[pl.ds(aligned(row, 16), rows), pl.ds(aligned(lane, 128), lanes)]

        for i, order in enumerate(self.orders):
            axis = order[k]
            mine = ref(i, self.regions[i][k + 1])
            for s in range(1, axis["size"]):
                to = lax.rem(axis["index"] + s, axis["size"])
                frm = lax.rem(axis["index"] + axis["size"] - s, axis["size"])
                slot = self.take(i)
                made = self.remote(i, mine, mine, slot, axis["at"](to))
                made.start()
                theirs = ref(i, self.share(self.regions[i][k], axis, frm))
                self.waits.append((made, self.remote(i, theirs, theirs, slot, axis["at"](frm))))
                self.sent.append((axis["link"], self.regions[i][k + 1][1] * self.regions[i][k + 1][3] * 2))

    def result(self, i, index, section):
        rows = self.regions[i][1][1]
        lane = aligned(self.lane_of(section) + i * PART, PART)
        return self.env["o"].at[section, pl.ds(aligned(index * rows, 16), rows), pl.ds(lane, PART)]

    def gathered(self, i):
        return self.space.at[pl.ds(0, self.regions[i][1][1]), pl.ds(i * PART, PART)]

    def deliver(self, i, s, straight):
        axis, section = self.orders[i][0], self.env["section"]
        recv = None if straight else self.env["ar_other"].at[self.layer, self.index, i, s]
        where = dict(axis["at"](lax.rem(axis["index"] + s, axis["size"])), section=self.layer)
        target = self.result(i, axis["index"], section)
        return self.remote(i, self.gathered(i), target, self.slot[i] + s, where, recv)

    def arrival(self, i, s, straight):
        axis, section = self.orders[i][0], self.env["section"]
        recv = None if straight else self.env["ar_other"].at[self.layer, self.index, i, s]
        index = lax.rem(axis["index"] + axis["size"] - s, axis["size"])
        frm = section if straight else 1 - section
        where = dict(axis["at"](index), section=frm)
        return self.remote(i, self.gathered(i), self.result(i, index, frm), self.slot[i] + s, where, recv)

    def kept(self, i):
        sem = self.env["ar_recv"].at[self.layer, self.index, i, self.slot[i]]
        target = self.result(i, self.orders[i][0]["index"], self.env["section"])
        return pltpu.make_async_copy(self.gathered(i), target, sem)

    def give(self):
        self.wait()

        @pl.when(self.env["section"] == self.layer)
        def _():
            for i in range(2):
                for s in range(1, self.orders[i][0]["size"]):
                    self.deliver(i, s, True).start()
                self.kept(i).start()

        @pl.when(self.env["section"] != self.layer)
        def _():
            for i in range(2):
                for s in range(self.orders[i][0]["size"] - 1, -1, -1):
                    self.deliver(i, s, False).start()

        for i, order in enumerate(self.orders):
            self.sent.append((order[0]["link"], self.regions[i][1][1] * PART * 2 * (order[0]["size"] - 1)))

    def finish(self):
        @pl.when(self.env["section"] == self.layer)
        def _():
            for i in range(2):
                size = self.orders[i][0]["size"]
                self.kept(i).wait()
                for s in range(1, size):
                    self.deliver(i, s, True).wait_send()
                    self.arrival(i, s, True).wait_recv()
                for s in range(size):
                    self.arrival(i, s, False).wait_recv()

        @pl.when(self.env["section"] != self.layer)
        def _():
            for i in range(2):
                for s in range(self.orders[i][0]["size"]):
                    self.deliver(i, s, False).wait_send()


class Order:
    RATE, HOP = 55e3, 2.0

    def __init__(self):
        self.now = 0.0
        self.free = {}
        self.going = []

    def sent(self, copies):
        end = self.now
        for link, size in copies:
            self.free[link] = max(self.now, self.free.get(link, 0.0)) + size / self.RATE
            end = max(end, self.free[link])
        return end + self.HOP

    def begin(self, one, i):
        end = self.sent(one.start_part(i))
        if i == 0:
            one.due = end
        else:
            one.due = max(one.due, end)
            self.going.append(one)

    def advance(self, one):
        self.now = max(self.now, one.due) + 0.4
        one.due = self.sent(one.advance())
        if one.done:
            self.going.remove(one)

    def work(self, cost):
        self.now += cost
        while True:
            due = [x for x in self.going if x.due <= self.now and x.free_to_go]
            if not due:
                return
            self.advance(min(due, key=lambda x: x.due))

    def drain(self):
        while self.going:
            self.advance(min(self.going, key=lambda x: x.due))


def kernel(dims, steps, seqs, views, frames, grad_out, weights, gains, shifts, recurs, lengths, masks, o, gf, vectors, f_own, f_far, p_own, p_far, g3, wc, wr1, src_t, live, turn,
           staged, heads, tails, v, vecs, rows, hid, coef, tot, vtot, levels, column, counts, cnt_p, cnt_z, slim_p, slim_z,
           wide_p, wide_z, space, sems, v_sems, stage_sem, credit, pl_send, pl_recv, z_send, z_recv, ar_send, ar_recv,
           ar_other):
    nz, ny, nx = dims
    np_ = ny * nx
    span = steps * seqs
    total_rows = 2 * span
    sent_rows = total_rows + 16
    pairs = steps // 2
    section = lax.axis_index("section")
    other = 1 - section
    b = lax.axis_index("batch")
    mp = lax.rem(b, np_)
    mz = b // np_

    def at_plane(i):
        return {"batch": b - mp + i}

    def at_z(i):
        return {"batch": b + (i - mz) * np_}

    def axis_of(link, size, stride):
        index = lax.rem(b // stride, size)
        return dict(link=link, size=size, index=index, at=lambda i: {"batch": b + (i - index) * stride})

    def halvings(link, size, stride):
        out = []
        while size > 1:
            out.append(axis_of(link, 2, stride))
            size //= 2
            stride *= 2
        return out

    xs, ys, zs = halvings("x", nx, 1), halvings("y", ny, nx), halvings("z", nz, np_)
    orders = (xs + ys + zs, ys + xs + zs)
    sibling = {"section": other}

    def local(src, dst, slot):
        return pltpu.make_async_copy(src, dst, sems.at[0, slot])

    def across(src, dst, slot):
        return pltpu.make_async_remote_copy(
            src_ref=src, dst_ref=dst, send_sem=sems.at[1, slot], recv_sem=sems.at[2, slot],
            device_id=sibling, device_id_type=MESH,
        )

    half = frames.shape[3]
    width = 2 * half
    lead = W - half
    rest = width - W
    full = rest // 128 * 128

    def fetch(source, m):
        return pltpu.make_async_copy(source.at[m], staged.at[m], stage_sem.at[m])

    def by_units(source, target, m):
        fetch(source, m).wait()

        @pl.when(section == 0)
        def _():
            pad = jnp.zeros((2 * seqs, lead), F32)

            def place(i, _):
                x = staged[m, pl.ds(2 * i, 2)].astype(F32).reshape(2 * seqs, half)
                to = pl.ds(aligned(m * span + 2 * i * seqs, 16), 2 * seqs)
                target[to, :] = jnp.concatenate([x, pad], axis=1).astype(BF16)
                return 0

            lax.fori_loop(0, pairs, place, 0)

        @pl.when(section == 1)
        def _():
            pad = jnp.zeros((2 * seqs, 2 * lead), F32)

            def place(i, _):
                x = staged[m, pl.ds(2 * i, 2)].astype(F32).reshape(2 * seqs, half)
                to = pl.ds(aligned(m * span + 2 * i * seqs, 16), 2 * seqs)
                target[to, :] = jnp.concatenate([x[:, lead:], pad], axis=1).astype(BF16)
                return 0

            lax.fori_loop(0, pairs, place, 0)

    def patch_heads(target, m):
        @pl.when(section == 0)
        def _():
            lane = lax.broadcasted_iota(jnp.int32, (2 * seqs, 128), 1)

            def place(i, _):
                to = pl.ds(aligned(m * span + 2 * i * seqs, 16), 2 * seqs)
                head = heads[m, pl.ds(2 * i, 2)].astype(F32).reshape(2 * seqs, 128)
                head = pltpu.roll(head, 128 - lead, 1)
                old = target[to, W - 128 :].astype(F32)
                target[to, W - 128 :] = jnp.where(lane < 128 - lead, old, head).astype(BF16)
                return 0

            lax.fori_loop(0, pairs, place, 0)

    def pieces(row, count, u, block, spot):
        r = pl.ds(row, count)
        to = pl.ds(0, count)
        if u == 0:
            return [(weights.at[0, r, pl.ds(0, W)], block.at[to, :])]
        return [
            (weights.at[0, r, pl.ds(W, full)], block.at[to, pl.ds(0, full)]),
            (weights.at[0, r, pl.ds(W + full, rest - full)], tails.at[spot, to, :]),
        ]

    rows_of = {0: (0, W), 1: (W, rest)}

    def w_plan(layer):
        mine, far = rows_of[layer], rows_of[1 - layer]
        plan = [
            (mine, layer, far, 1 - layer, wc.at[layer, 0], 2 * layer),
            (far, layer, mine, 1 - layer, wc.at[layer, 1], 2 * layer + 1),
        ]
        if layer == 1:
            plan.append((mine, 0, far, 1, wr1, 4))
        return plan

    late_row = (width - half) // 16 * 16
    late_shift = half - late_row
    late_plan = [
        ((0, W), 0, (late_row, width - late_row), 1, wc.at[0, 0], 0),
        ((0, W), 1, (late_row, width - late_row), 0, wc.at[0, 1], 1),
    ]
    slot_of = {0: 4, 1: 8, 2: 14}

    def local_w(plan, base, which):
        r, u, _, _, block, spot = plan[which]
        return [local(a, t, base + 2 * which + i) for i, (a, t) in enumerate(pieces(*r, u, block, spot))]

    def across_w(plan, base, which):
        _, _, r, u, block, spot = plan[which]
        return [across(a, t, base + 2 * which + i) for i, (a, t) in enumerate(pieces(*r, u, block, spot))]

    def start_local_w(layer, plan, base):
        @pl.when(section == layer)
        def _():
            for which in range(len(plan)):
                for made in local_w(plan, base, which):
                    made.start()

    def start_across_w(layer, plan, base):
        @pl.when(section == layer)
        def _():
            for which in range(len(plan)):
                for made in across_w(plan, base, which):
                    made.start()

    def last_units(block, spot):
        def body(i, _):
            r = pl.ds(aligned(i * 128, 128), 128)
            x = tails[spot, r, :].astype(F32)
            x = jnp.concatenate([x, jnp.zeros((128, 128 - x.shape[1]), F32)], axis=1)
            block[r, full:] = x.astype(BF16)
            return 0

        lax.fori_loop(0, W // 128, body, 0)

    def wait_w(layer, plan, base, which):
        _, own_u, _, far_u, block, spot = plan[which]

        @pl.when(section == layer)
        def _():
            for made in local_w(plan, base, which):
                made.wait()
            if own_u == 1:
                last_units(block, spot)

        @pl.when(section != layer)
        def _():
            for made in across_w(plan, base, which):
                made.wait_recv()
            if far_u == 1:
                last_units(block, spot)

    def done_w(layer, plan, base):
        @pl.when(section == layer)
        def _():
            for which in range(len(plan)):
                for made in across_w(plan, base, which):
                    made.wait_send()

    def heads_copy(source, slot):
        return across(source.at[:, :, :, pl.ds(0, 128)], heads, slot)

    def wait_heads(source, slot):
        @pl.when(section == 0)
        def _():
            heads_copy(source, slot).wait_recv()

        @pl.when(section == 1)
        def _():
            heads_copy(source, slot).wait_send()

    fetch(frames, 0).start()
    fetch(frames, 1).start()
    for layer in range(2):
        start_local_w(layer, w_plan(layer), slot_of[layer])

    barrier = pltpu.get_barrier_semaphore()
    greeted = [dict(sibling)]
    greeted += [at_plane(lax.rem(mp + k, np_)) for k in range(1, np_)]
    greeted += [at_z(lax.rem(mz + k, nz)) for k in range(1, nz)]
    for axis in (xs + zs)[:1] + (ys + zs)[:1]:
        for s in range(1, axis["size"]):
            greeted.append(dict(axis["at"](lax.rem(axis["index"] + s, axis["size"])), section=other))
    for where in greeted:
        pl.semaphore_signal(barrier, inc=1, device_id=where, device_id_type=MESH)

    for k, (x, fill) in enumerate(((gains, 0.0), (shifts, -1e30), (recurs, 0.0))):
        vecs[section, k : k + 1, 0:width] = x[...]
        vecs[section, k : k + 1, width:] = jnp.full((1, 2 * W - width), fill, F32)
    vecs[section, 3:8, :] = jnp.zeros((5, 2 * W), F32)

    gap = jnp.zeros((W - rest, W), BF16)

    @pl.when(section == 0)
    def _():
        wc[0, 1, rest:, :] = gap
        wc[1, 1, rest:, :] = gap

    @pl.when(section == 1)
    def _():
        wc[0, 0, rest:, :] = gap
        wc[1, 0, rest:, :] = gap
        wr1[rest:, :] = gap

    for spot in (0, 2):
        tails[spot, rest:, :] = jnp.zeros((W - rest, rest - full), BF16)
    for spare in (f_own, p_own, g3.at[0], g3.at[1]):
        spare[sent_rows:, :] = jnp.zeros((spare.shape[0] - sent_rows, W), BF16)

    pl.semaphore_wait(barrier, len(greeted))

    @pl.when(section == 1)
    def _():
        heads_copy(frames, 1).start()

    start_across_w(0, w_plan(0), slot_of[0])
    send_vec = across(vecs.at[section], vecs.at[section], 3)
    send_vec.start()

    def stage_copy(where, rnd, slot, k, back):
        buf, parity, size, me, at, send, recv = where
        there = at(lax.rem(me + (size - k if back else k), size))
        ref = buf.at[parity, slot]
        return pltpu.make_async_remote_copy(
            src_ref=ref, dst_ref=ref, send_sem=send.at[rnd, k], recv_sem=recv.at[rnd, k],
            device_id=there, device_id_type=MESH,
        )

    def in_plane(buf, parity):
        return (buf, parity, np_, mp, at_plane, pl_send, pl_recv)

    def in_line(buf, parity):
        return (buf, parity, nz, mz, at_z, z_send, z_recv)

    def stage_start(where, rnd, value):
        buf, parity, size, me = where[:4]
        buf[parity, me] = value
        for k in range(1, size):
            stage_copy(where, rnd, me, k, False).start()

    def stage_wait(where, rnd):
        size, me = where[2:4]
        for k in range(1, size):
            stage_copy(where, rnd, me, k, False).wait_send()
            stage_copy(where, rnd, lax.rem(me + size - k, size), k, True).wait_recv()

    def add_slots(where):
        buf, parity, size = where[:3]
        total = buf[parity, 0]
        for k in range(1, size):
            total = total + buf[parity, k]
        return total

    groups = lengths.shape[1]
    s_at = lax.broadcasted_iota(jnp.int32, (seqs, groups), 0)
    g_at = lax.broadcasted_iota(jnp.int32, (seqs, groups), 1) * views
    there = (s_at >= g_at) & (s_at < g_at + views)
    position = lax.broadcasted_iota(jnp.int32, (seqs, 128), 1)
    local_counts = []
    for m in range(2):
        turn[...] = jnp.zeros_like(turn)
        turn[0:steps, 0:seqs] = masks[m].astype(F32)
        mask = turn[...].T[0:seqs]
        length = jnp.broadcast_to(lengths[m : m + 1, :], (seqs, groups)).astype(F32)
        limit = jnp.sum(jnp.where(there, length, 0.0), axis=1, keepdims=True)
        alive = (position.astype(F32) < limit) & ((mask > 0.0) | (position == 0))
        alive = jnp.where(position < steps, alive.astype(F32), 0.0)
        total = jnp.zeros((seqs, 128), F32)
        for t in range(steps):
            at = m * span + t * seqs
            cells = jnp.broadcast_to(alive[:, t : t + 1], (seqs, 128))
            live[at : at + seqs, :] = cells
            total = total + cells
        local_counts.append(jnp.sum(total, axis=0, keepdims=True))
    n_own = jnp.concatenate([local_counts[0]] * 2 + [local_counts[1]] * 2, axis=0)
    n_own = jnp.concatenate([n_own, n_own], axis=0)

    cnt_plane, cnt_line = in_plane(cnt_p, 0), in_line(cnt_z, 0)
    stage_start(cnt_plane, 0, n_own)

    def vec_of(layer, k, lh):
        return vecs[layer, k : k + 1, pl.ds(aligned(section * W + lh * HALF, HALF), HALF)]

    def half_of(lh):
        return slice(lh * HALF, (lh + 1) * HALF)

    def matmul_to(out, a, w, first, lh):
        lanes = half_of(lh)

        def body(m, _):
            r = pl.ds(aligned(m * span, 16), span)
            y = dot(a[r, :], w[:, lanes], ((1,), (0,)))
            out[r, lanes] = y if first else out[r, lanes] + y
            return 0

        lax.fori_loop(0, 2, body, 0)

    def packed(x, y):
        return jnp.concatenate([z[:, k * QUART : (k + 1) * QUART] for z in (*x, *y) for k in range(2)], axis=0)

    def unpacked(x, m):
        return jnp.concatenate([x[2 * m + k : 2 * m + k + 1] for k in range(2)], axis=1)

    def merge_slots(where, counts_of):
        buf, parity, size = where[:3]
        s = [buf[parity, k, 0:4, :] for k in range(size)]
        q = [buf[parity, k, 4:8, :] for k in range(size)]
        n = [wide(counts_of(k), 2) for k in range(size)]
        total, squares, count = sum(s[1:], s[0]), sum(q[1:], q[0]), sum(n[1:], n[0])
        mean = total / count
        for k in range(size):
            d = s[k] / n[k] - mean
            squares = squares + n[k] * d * d
        return jnp.concatenate([total, squares], axis=0)

    def slim_round(which, lh):
        return 1 + 2 * which + lh, in_plane(slim_p, 2 * lh + which % 2), in_line(slim_z, 2 * lh + which % 2)

    def forward_stats(layer, lh):
        lanes = half_of(lh)
        sums, squares = [], []
        for m in range(2):
            start = jnp.sum(rows[layer, m * span : m * span + seqs, lanes], axis=0, keepdims=True) * (1.0 / seqs)

            def body(i, carry):
                s, q = carry
                r = pl.ds(aligned(m * span + i * (2 * seqs), 16), 2 * seqs)
                d = rows[layer, r, lanes] - start
                kept = wide(live[r, :], 4) * d
                return s + fold(kept), q + fold(kept * d)

            zero = jnp.zeros((8, HALF), F32)
            s, q = lax.fori_loop(0, pairs, body, (zero, zero))
            s, q = jnp.sum(s, axis=0, keepdims=True), jnp.sum(q, axis=0, keepdims=True)
            n = wide(local_counts[m], 4)
            sums.append(s + n * start)
            squares.append(jnp.maximum(q - s * s / n, 0.0))
        rnd, plane, _ = slim_round(layer, lh)
        stage_start(plane, rnd, packed(sums, squares))

    def forward_middle(layer, lh):
        rnd, plane, line = slim_round(layer, lh)
        stage_wait(plane, rnd)
        stage_start(line, rnd, merge_slots(plane, lambda k: cnt_p[0, k, 0:4, :]))

    def forward_end(layer, lh):
        rnd, _, line = slim_round(layer, lh)
        lanes = half_of(lh)
        stage_wait(line, rnd)
        value = merge_slots(line, lambda k: cnt_z[0, k, 0:4, :])
        for m in range(2):
            count = wide(counts[2 * m : 2 * m + 1, :], 4)
            mean = unpacked(value[0:4], m) / count
            scale = lax.rsqrt(unpacked(value[4:8], m) / count + EPS)
            coef[layer, 2 * m : 2 * m + 1, lanes] = mean
            coef[layer, 2 * m + 1 : 2 * m + 2, lanes] = scale
            slope = vec_of(layer, 0, lh) * scale
            coef[layer, 4 + 2 * m : 5 + 2 * m, lanes] = slope
            coef[layer, 5 + 2 * m : 6 + 2 * m, lanes] = vec_of(layer, 1, lh) - mean * slope

    def forward_scan(layer, lh, passes):
        lanes = half_of(lh)
        rec = vec_of(layer, 2, lh)
        slope = [coef[layer, 4 + 2 * m : 5 + 2 * m, lanes] for m in range(2)]
        shift = [coef[layer, 5 + 2 * m : 6 + 2 * m, lanes] for m in range(2)]

        def body(i, carry):
            states, level = carry
            out = []
            for m in range(2):
                r = pl.ds(aligned(m * span + i * (2 * seqs), 16), 2 * seqs)
                x = rows[layer, r, lanes] * slope[m] + shift[m]
                lv = wide(live[r, :], 4)
                alive = lv > 0.0
                h = states[m]
                both = []
                for k in range(2):
                    part = slice(k * seqs, (k + 1) * seqs)
                    z = x[part] + rec * h
                    soft = jnp.maximum(z, 0.0) + jnp.log(1.0 + jnp.exp(-jnp.abs(z)))
                    h = jnp.where(alive[part], soft, h)
                    both.append(h)
                two = jnp.concatenate(both, axis=0)
                hid[layer, r, lanes] = two
                if passes:
                    p_own[r, lanes] = two.astype(BF16)
                    level = level + fold(lv * two)
                out.append(h)
            return tuple(out), level

        zero = jnp.zeros((seqs, HALF), F32)
        _, level = lax.fori_loop(0, pairs, body, ((zero, zero), jnp.zeros((8, HALF), F32)))
        if not passes:
            return None
        levels[1:2, lanes] = jnp.sum(level, axis=0, keepdims=True)
        made = across(p_own.at[pl.ds(0, total_rows), lanes], p_far.at[:, lanes], 18 + lh)
        made.start()
        return made

    def backward_scan(layer, lh, above, between=lambda: None):
        for lq in range(2 * lh, 2 * lh + 2):
            lanes = slice(lq * QUART, (lq + 1) * QUART)
            gq, sq, rec = (vec_of(layer, k, lh)[:, (lq % 2) * QUART : (lq % 2 + 1) * QUART] for k in range(3))
            mean = [coef[layer, 2 * m : 2 * m + 1, lanes] for m in range(2)]
            scale = [coef[layer, 2 * m + 1 : 2 * m + 2, lanes] for m in range(2)]

            def body(i, carry):
                down, s1, s2, rsum, sqh, sqa = carry
                down, s1, s2 = list(down), list(s1), list(s2)
                i = pairs - 1 - i
                for m in range(2):
                    start = m * span + i * (2 * seqs)
                    r = pl.ds(aligned(start, 16), 2 * seqs)
                    before = pl.ds(aligned(jnp.maximum(start - seqs, 0), 8), seqs)
                    normed = (rows[layer, r, lanes] - mean[m]) * scale[m]
                    drive = gq * normed + sq
                    h2 = hid[layer, r, lanes]
                    hb = jnp.where(i > 0, hid[layer, before, lanes], 0.0)
                    lv = wide(live[r, :], 2)
                    up = above[r, lanes].astype(F32)
                    res = f_own[r, lanes].astype(F32)
                    aux = res + h2 if layer == 1 else res
                    sqh = sqh + fold(lv * (h2 * h2))
                    sqa = sqa + fold(lv * (aux * aux))
                    grads = [None, None]
                    for k in (1, 0):
                        part = slice(k * seqs, (k + 1) * seqs)
                        prior = h2[0:seqs] if k == 1 else hb
                        slope = 0.5 + 0.5 * jnp.tanh(0.5 * (drive[part] + rec * prior))
                        total = up[part] + down[m]
                        gd = lv[part] * slope * total
                        down[m] = (1.0 - lv[part]) * total + rec * gd
                        grads[k] = gd
                        rsum = rsum + fold(gd * prior)
                    gd2 = jnp.concatenate(grads, axis=0)
                    hid[layer, r, lanes] = gd2
                    s1[m] = s1[m] + fold(gd2)
                    s2[m] = s2[m] + fold(gd2 * normed)
                return tuple(down), tuple(s1), tuple(s2), rsum, sqh, sqa

            zero = jnp.zeros((seqs, QUART), F32)
            z8 = jnp.zeros((8, QUART), F32)
            _, s1, s2, rsum, sqh, sqa = lax.fori_loop(
                0, pairs, body, ((zero, zero), (z8, z8), (z8, z8), z8, z8, z8)
            )
            for k, x in enumerate((s1[0], s1[1], s2[0], s2[1], rsum, sqh, sqa)):
                tot[layer, k : k + 1, lanes] = jnp.sum(x, axis=0, keepdims=True)
            between()

    def backward_stats(layer, lh):
        rnd, plane, _ = slim_round(3 - layer, lh)
        t = tot[layer, 0:4, half_of(lh)]
        stage_start(plane, rnd, packed([t[0:1], t[1:2]], [t[2:3], t[3:4]]))

    def backward_middle(layer, lh):
        rnd, plane, line = slim_round(3 - layer, lh)
        stage_wait(plane, rnd)
        stage_start(line, rnd, add_slots(plane))

    def backward_end(layer, lh):
        rnd, _, line = slim_round(3 - layer, lh)
        stage_wait(line, rnd)
        value = add_slots(line)
        for m in range(2):
            tot[layer, m : m + 1, half_of(lh)] = unpacked(value[0:4], m)
            tot[layer, 2 + m : 3 + m, half_of(lh)] = unpacked(value[4:8], m)

    def grad_rows(layer, lh, slot):
        lanes = half_of(lh)
        acc = jnp.zeros((8, HALF), F32)
        for m in range(2):
            mean = coef[layer, 2 * m : 2 * m + 1, lanes]
            scale = coef[layer, 2 * m + 1 : 2 * m + 2, lanes]
            count = wide(counts[2 * m : 2 * m + 1, :], 4)
            first = tot[layer, m : m + 1, lanes] / count
            second = tot[layer, 2 + m : 3 + m, lanes] / count * scale
            k = coef[layer, 4 + 2 * m : 5 + 2 * m, lanes]

            def body(i, acc):
                r = pl.ds(aligned(m * span + i * (2 * seqs), 16), 2 * seqs)
                y = hid[layer, r, lanes] - first - (rows[layer, r, lanes] - mean) * second
                y = wide(live[r, :], 4) * (k * y)
                g3[0, r, lanes] = y.astype(BF16)
                return acc + fold(y)

            acc = lax.fori_loop(0, pairs, body, acc)
        top = lax.broadcasted_iota(jnp.int32, (16, HALF), 0) == 0
        minus = jnp.where(top, -jnp.sum(acc, axis=0, keepdims=True), 0.0)
        g3[0, total_rows:sent_rows, lanes] = minus.astype(BF16)
        made = across(g3.at[0, pl.ds(0, sent_rows), lanes], g3.at[1, pl.ds(0, sent_rows), lanes], slot + lh)
        made.start()
        return made

    sums_round = {1: (1, 10), 0: (0, 11)}

    def sums_start(layer):
        parity, rnd = sums_round[layer]
        own_sum = -g3[0, total_rows:sent_rows, :].astype(F32)[0:1]
        far_sum = -g3[1, total_rows:sent_rows, :].astype(F32)[0:1]
        value = jnp.concatenate([own_sum, far_sum, tot[layer, 4:7, :], jnp.zeros((3, W), F32)], axis=0)
        stage_start(in_plane(wide_p, parity), rnd, value)

    def sums_middle(layer):
        parity, rnd = sums_round[layer]
        stage_wait(in_plane(wide_p, parity), rnd)
        stage_start(in_line(wide_z, parity), rnd, add_slots(in_plane(wide_p, parity)))

    def sums_end(layer):
        parity, rnd = sums_round[layer]
        stage_wait(in_line(wide_z, parity), rnd)
        vtot[layer] = add_slots(in_line(wide_z, parity))
        tot[layer, 4:7, :] = vtot[layer, 2:5, :]
        tot[layer, 7:8, :] = wide(counts[0:1, :] + counts[2:3, :], 8)
        env["summed"].add(layer)

        @pl.when(section == layer)
        def _():
            pltpu.make_async_copy(tot.at[layer], v.at[section], v_sems.at[0]).start()

        @pl.when(section != layer)
        def _():
            v_across(layer).start()

    def v_across(layer):
        return pltpu.make_async_remote_copy(
            src_ref=tot.at[layer], dst_ref=v.at[section], send_sem=v_sems.at[1], recv_sem=v_sems.at[2],
            device_id=sibling, device_id_type=MESH,
        )

    def transpose(src, begin=0, end=W // 128):
        def body(j, _):
            c = pl.ds(aligned(j * 128, 128), 128)
            src_t[c, 0:total_rows] = src[0:total_rows, c].T
            return 0

        lax.fori_loop(begin, end, body, 0)

    def transpose_level(src, layer):
        top = lax.broadcasted_iota(jnp.int32, (16, W), 0) == 0
        src[total_rows:sent_rows, :] = jnp.where(top, levels[2 + layer : 3 + layer, :], 0.0).astype(BF16)

        def body(j, _):
            c = pl.ds(aligned(j * 128, 128), 128)
            src_t[c, total_rows:] = src[total_rows:, c].T
            level = src[total_rows:sent_rows, c].astype(F32)[0:1]
            column[layer, c, :] = jnp.broadcast_to(level, (128, 128)).T.astype(BF16)
            return 0

        lax.fori_loop(0, W // 128, body, 0)

    def weight_part(block, grads, c):
        lanes = pl.ds(c * HALF, HALF)

        def body(j, _):
            r = pl.ds(aligned(j * HALF, HALF), HALF)
            block[r, lanes] = dot(src_t[r, :], grads[:, lanes], ((1,), (0,))).astype(BF16)
            return 0

        lax.fori_loop(0, W // HALF, body, 0)

    def source_grad(store, w_own, w_far, half_index):
        c = half_of(half_index)

        def body(m, _):
            r = pl.ds(aligned(m * span, 16), span)
            y = dot(g3[0, r, :], w_own[c, :], ((1,), (1,))) + dot(g3[1, r, :], w_far[c, :], ((1,), (1,)))
            store(r, c, y)
            return 0

        lax.fori_loop(0, 2, body, 0)

    env = dict(summed=set(), vtot=vtot, column=column, space=space, ar_send=ar_send, ar_recv=ar_recv,
               ar_other=ar_other, o=o, section=section, here={"batch": b})
    blocks = {
        (1, 0): f_far.at[pl.ds(0, W), :],
        (1, 1): p_far.at[pl.ds(0, W), :],
        (0, 0): wc.at[1, 1],
        (0, 1): wr1,
    }
    parts = {}
    for layer in (1, 0):
        for index in range(2 * PAIRS):
            part, side = index // PAIRS, index % PAIRS

            def lane_of(sec, part=part, side=side):
                return (sec if part == 0 else 1 - sec) * W + side * 2 * PART

            block = blocks[layer, part].at[:, pl.ds(side * 2 * PART, 2 * PART)]
            parts[layer, index] = Reduction(env, layer, index, block, orders, lane_of)
    order = Order()

    def weight_grads(layer, part, c):
        weight_part(blocks[layer, part], g3.at[part], c)
        order.work(2.0)
        for k in range(c * HALF // PART, (c + 1) * HALF // PART):
            order.begin(parts[layer, part * PAIRS + k // 2], k % 2)

    def arrived(layer, sends):
        for made in sends:
            made.wait()
        sums_start(layer)

    send_f = []
    for m in range(2):
        by_units(frames, f_own, m)
        fetch(grad_out, m).start()
        if m == 0:
            wait_heads(frames, 1)
        patch_heads(f_own, m)
        here = pl.ds(m * span, span)
        made = across(f_own.at[here, :], f_far.at[here, :], (0, 24)[m])
        made.start()
        send_f.append(made)
    start_across_w(1, w_plan(1), slot_of[1])
    stage_wait(cnt_plane, 0)
    stage_start(cnt_line, 0, add_slots(cnt_plane))
    wait_w(0, w_plan(0), slot_of[0], 0)
    matmul_to(rows.at[0], f_own, wc.at[0, 0], True, 0)
    matmul_to(rows.at[0], f_own, wc.at[0, 0], True, 1)
    wait_w(0, w_plan(0), slot_of[0], 1)
    for made in send_f:
        made.wait()

    @pl.when(section == 1)
    def _():
        heads_copy(grad_out, 2).start()

    matmul_to(rows.at[0], f_far, wc.at[0, 1], False, 0)
    forward_stats(0, 0)
    matmul_to(rows.at[0], f_far, wc.at[0, 1], False, 1)
    forward_middle(0, 0)
    forward_stats(0, 1)
    send_vec.wait_send()
    across(vecs.at[other], vecs.at[other], 3).wait_recv()
    by_units(grad_out, g3.at[1], 0)
    wait_heads(grad_out, 2)
    patch_heads(g3.at[1], 0)
    stage_wait(cnt_line, 0)
    counts[...] = add_slots(cnt_line)
    forward_end(0, 0)
    forward_middle(0, 1)
    sends = [forward_scan(0, 0, True)]
    forward_end(0, 1)
    sends.append(forward_scan(0, 1, True))
    wait_w(1, w_plan(1), slot_of[1], 0)
    matmul_to(rows.at[1], p_own, wc.at[1, 0], True, 0)
    matmul_to(rows.at[1], p_own, wc.at[1, 0], True, 1)
    wait_w(1, w_plan(1), slot_of[1], 1)
    for made in sends:
        made.wait()
    matmul_to(rows.at[1], p_far, wc.at[1, 1], False, 0)
    forward_stats(1, 0)
    done_w(0, w_plan(0), slot_of[0])

    start_local_w(0, late_plan, slot_of[2])
    start_across_w(0, late_plan, slot_of[2])

    @pl.when(section == 1)
    def _():
        wc[0, 1, width - late_row :, :] = jnp.zeros((W - width + late_row, W), BF16)

    def source_level():
        def body(i, acc):
            r = pl.ds(aligned(i * (2 * seqs), 16), 2 * seqs)
            return acc + fold(wide(live[r, :], 8) * f_own[r, :].astype(F32))

        acc = lax.fori_loop(0, 2 * pairs, body, jnp.zeros((8, W), F32))
        levels[0:1, :] = jnp.sum(acc, axis=0, keepdims=True)

    matmul_to(rows.at[1], p_far, wc.at[1, 1], False, 1)
    forward_middle(1, 0)
    forward_stats(1, 1)
    by_units(grad_out, g3.at[1], 1)
    patch_heads(g3.at[1], 1)
    forward_end(1, 0)
    forward_middle(1, 1)
    forward_scan(1, 0, False)
    backward_scan(1, 0, g3.at[1])
    backward_stats(1, 0)
    forward_end(1, 1)
    source_level()
    level_plane, level_line = in_plane(wide_p, 0), in_line(wide_z, 0)
    stage_start(level_plane, 9, jnp.concatenate([levels[0:2, :], jnp.zeros((6, W), F32)], axis=0))
    forward_scan(1, 1, False)
    backward_middle(1, 0)
    stage_wait(level_plane, 9)
    stage_start(level_line, 9, add_slots(level_plane))
    backward_scan(1, 1, g3.at[1])
    backward_stats(1, 1)
    pl.semaphore_signal(credit.at[0], inc=1, device_id=sibling, device_id_type=MESH)
    backward_end(1, 0)
    pl.semaphore_wait(credit.at[0], 1)
    sends = [grad_rows(1, 0, 20)]
    transpose(p_own, 0, W // 256)
    backward_middle(1, 1)
    transpose(p_own, W // 256)
    stage_wait(level_line, 9)
    levels[2:4, :] = (add_slots(level_line) / wide(counts[0:1, :] + counts[2:3, :], 8))[0:2]
    transpose_level(p_own, 1)
    weight_grads(1, 0, 0)
    backward_end(1, 1)
    sends.append(grad_rows(1, 1, 20))
    weight_grads(1, 0, 1)
    arrived(1, sends)
    weight_grads(1, 1, 0)
    weight_grads(1, 1, 1)
    wait_w(1, w_plan(1), slot_of[1], 2)
    done_w(1, w_plan(1), slot_of[1])

    def keep_down(r, c, y):
        p_own[r, c] = y.astype(BF16)

    source_grad(keep_down, wc.at[1, 0], wr1, 0)
    order.work(2.5)
    sums_middle(1)
    backward_scan(0, 0, p_own, lambda: order.work(1.3))
    backward_stats(0, 0)
    source_grad(keep_down, wc.at[1, 0], wr1, 1)
    pl.semaphore_signal(credit.at[1], inc=1, device_id=sibling, device_id_type=MESH)
    order.work(2.5)
    sums_end(1)
    backward_middle(0, 0)
    backward_scan(0, 1, p_own, lambda: order.work(1.3))
    backward_stats(0, 1)
    backward_end(0, 0)
    pl.semaphore_wait(credit.at[1], 1)
    sends = [grad_rows(0, 0, 22)]
    order.work(1.3)
    transpose(f_own, 0, W // 256)
    backward_middle(0, 1)
    transpose(f_own, W // 256)
    transpose_level(f_own, 0)
    order.work(4.0)
    weight_grads(0, 0, 0)
    backward_end(0, 1)
    sends.append(grad_rows(0, 1, 22))
    order.work(1.3)
    weight_grads(0, 0, 1)
    arrived(0, sends)
    weight_grads(0, 1, 0)
    weight_grads(0, 1, 1)
    wait_w(0, late_plan, slot_of[2], 0)
    wait_w(0, late_plan, slot_of[2], 1)
    done_w(0, late_plan, slot_of[2])

    def keep_source(r, c, y):
        rows[0, r, c] = y

    fetch(grad_out, 0).start()
    fetch(grad_out, 1).start()
    source_grad(keep_source, wc.at[0, 0], wc.at[0, 1], 0)
    order.work(2.5)
    sums_middle(0)
    source_grad(keep_source, wc.at[0, 0], wc.at[0, 1], 1)
    order.work(2.5)
    sums_end(0)

    def give(m):
        return pltpu.make_async_copy(staged.at[m], gf.at[m], stage_sem.at[m])

    for m in range(2):
        fetch(grad_out, m).wait()

        def finish_frames(i, _, m=m):
            straight = staged[m, pl.ds(2 * i, 2)].astype(F32).reshape(2 * seqs, half)
            y = rows[0, pl.ds(aligned(m * span + 2 * i * seqs, 8), 2 * seqs), :]
            y = jnp.where(section == 0, y[:, :half], y[:, late_shift : late_shift + half])
            staged[m, pl.ds(2 * i, 2)] = (y + straight).reshape(2, seqs, half).astype(BF16)
            return 0

        lax.fori_loop(0, pairs, finish_frames, 0)
        give(m).start()
        order.work(2.0)
    order.drain()
    for m in range(2):
        give(m).wait()

    for layer in range(2):

        @pl.when(section == layer)
        def _(layer=layer):
            pltpu.make_async_copy(tot.at[layer], v.at[section], v_sems.at[0]).wait()
            pltpu.make_async_remote_copy(
                src_ref=tot.at[layer], dst_ref=v.at[other], send_sem=v_sems.at[1], recv_sem=v_sems.at[2],
                device_id=sibling, device_id_type=MESH,
            ).wait_recv()

        @pl.when(section != layer)
        def _(layer=layer):
            v_across(layer).wait_send()

    own_part, far_part = v[section], v[other]
    first = jnp.where(section == 0, own_part, far_part)
    second = jnp.where(section == 0, far_part, own_part)
    for row, terms in ((0, (2, 3)), (1, (0, 1)), (2, (4,))):
        for lane, x in ((0, first), (W, second)):
            total = x[terms[0] : terms[0] + 1, :]
            for k in terms[1:]:
                total = total + x[k : k + 1, :]
            vectors[row : row + 1, lane : lane + W] = total
    squares = jnp.sum(first[5:7, :] + second[5:7, :], axis=1, keepdims=True)
    root = jnp.sqrt(squares / (first[7:8, 0:1] * width))
    for k in range(2):
        vectors[3 + k : 4 + k, :] = jnp.broadcast_to(root[k : k + 1], (1, 2 * W))
    vectors[5:8, :] = jnp.zeros((3, 2 * W), F32)


def write_results(o, gf, vectors, grad_weight, grad_frames, grad_gains, grad_shifts, grad_recurs, table):
    width = grad_weight.shape[2]
    grad_weight[0] = o[...][:, :width].astype(F32)
    grad_frames[...] = gf[...]

    @pl.when(pl.program_id(0) == 0)
    def _():
        for k, out in enumerate((grad_gains, grad_shifts, grad_recurs)):
            out[...] = vectors[k : k + 1, 0:width]
        table[...] = jnp.concatenate([vectors[3:4, 0:1], vectors[4:5, 0:1]], axis=1)


def results(o, gf, vectors):
    micro, steps, seqs, half = gf.shape
    width = 2 * half
    count = W * 2 // 256
    frames = micro * steps // count
    whole = lambda shape: pl.BlockSpec(shape, lambda i: (0, 0))
    out = pl.pallas_call(
        write_results,
        grid=(count,),
        in_specs=[
            pl.BlockSpec((256, 2 * W), lambda i: (i, 0)),
            pl.BlockSpec((frames, seqs, half), lambda i: (i, 0, 0)),
            whole((8, 2 * W)),
        ],
        out_specs=(
            pl.BlockSpec((1, 256, width), lambda i: (0, i, 0)),
            pl.BlockSpec((frames, seqs, half), lambda i: (i, 0, 0)),
            whole((1, width)),
            whole((1, width)),
            whole((1, width)),
            whole((1, 2)),
        ),
        out_shape=(
            jax.ShapeDtypeStruct((1, width, width), F32),
            jax.ShapeDtypeStruct((micro * steps, seqs, half), BF16),
            jax.ShapeDtypeStruct((1, width), F32),
            jax.ShapeDtypeStruct((1, width), F32),
            jax.ShapeDtypeStruct((1, width), F32),
            jax.ShapeDtypeStruct((1, 2), F32),
        ),
        compiler_params=pltpu.CompilerParams(vmem_limit_bytes=64 * 1024 * 1024),
    )(o.reshape(2 * W, 2 * W), gf.reshape(micro * steps, seqs, half), vectors)
    return out[1].reshape(gf.shape), out[0], *out[2:]


def whole_step(dims, frames, grad_out, weights, gains, shifts, recurs, lengths, masks):
    nz, ny, nx = dims
    micro, steps, seqs, half = frames.shape
    width = 2 * half
    views = seqs // lengths.shape[1]
    rows = micro * steps * seqs
    np_ = ny * nx
    wide_rows = (rows + 16 + 127) // 128 * 128
    across_first = max(nx, ny, nz if np_ == 1 else 1)
    copies = 2 * (nx + ny + nz) + across_first
    came_rows = (nx - 1) * (W // nx) + (ny - 1) * (W // np_) + (nz - 1) * max(W // np_ // nz, 16)
    any_ = pl.BlockSpec(memory_space=pl.ANY)
    held = pl.BlockSpec(memory_space=pltpu.VMEM)
    dma = pltpu.SemaphoreType.DMA
    return pl.pallas_call(
        functools.partial(kernel, dims, steps, seqs, views),
        out_shape=(
            jax.ShapeDtypeStruct((2, W, 2 * W), BF16),
            jax.ShapeDtypeStruct(frames.shape, BF16),
            jax.ShapeDtypeStruct((8, 2 * W), F32),
        ),
        in_specs=[any_] * 3 + [held] * 5,
        out_specs=(any_, any_, held),
        scratch_shapes=[
            pltpu.VMEM((wide_rows, W), BF16),
            pltpu.VMEM((rows, W), BF16),
            pltpu.VMEM((wide_rows, W), BF16),
            pltpu.VMEM((rows, W), BF16),
            pltpu.VMEM((2, wide_rows, W), BF16),
            pltpu.VMEM((2, 2, W, W), BF16),
            pltpu.VMEM((W, W), BF16),
            pltpu.VMEM((W, wide_rows), BF16),
            pltpu.VMEM((rows, 128), F32),
            pltpu.VMEM((128, 128), F32),
            pltpu.VMEM(frames.shape, BF16),
            pltpu.VMEM((micro, steps, seqs, 128), BF16),
            pltpu.VMEM((5, W, (width - W) % 128), BF16),
            pltpu.VMEM((2, 8, W), F32),
            pltpu.VMEM((2, 8, 2 * W), F32),
            pltpu.VMEM((2, rows, W), F32),
            pltpu.VMEM((2, rows, W), F32),
            pltpu.VMEM((2, 8, W), F32),
            pltpu.VMEM((2, 8, W), F32),
            pltpu.VMEM((2, 8, W), F32),
            pltpu.VMEM((8, W), F32),
            pltpu.VMEM((2, W, 128), BF16),
            pltpu.VMEM((8, 128), F32),
            pltpu.VMEM((1, np_, 8, 128), F32),
            pltpu.VMEM((1, nz, 8, 128), F32),
            pltpu.VMEM((4, np_, 8, QUART), F32),
            pltpu.VMEM((4, nz, 8, QUART), F32),
            pltpu.VMEM((2, np_, 8, W), F32),
            pltpu.VMEM((2, nz, 8, W), F32),
            pltpu.VMEM((2, 2 * PAIRS, max(came_rows, W), 2 * PART), BF16),
            dma((3, 25)),
            dma((3,)),
            dma((2,)),
            pltpu.SemaphoreType.REGULAR((2,)),
            dma((12, max(np_, 2))),
            dma((12, max(np_, 2))),
            dma((12, max(nz, 2))),
            dma((12, max(nz, 2))),
            dma((2, 2 * PAIRS, 2, copies)),
            dma((2, 2 * PAIRS, 2, copies)),
            dma((2, 2 * PAIRS, 2, across_first)),
        ],
        compiler_params=pltpu.CompilerParams(
            collective_id=0, has_side_effects=True, vmem_limit_bytes=64 * 1024 * 1024
        ),
    )(frames, grad_out, weights, gains, shifts, recurs, lengths, masks)


def shards(dims, frames, grad_out, weights, gains, shifts, recurs, lengths, masks):
    return results(*whole_step(dims, frames, grad_out, weights, gains, shifts, recurs, lengths, masks))


def solution(mesh):
    in_specs = (
        P(None, None, "batch", "section"),
        P(None, None, "batch", "section"),
        P("section", None, None),
        P("section", None),
        P("section", None),
        P("section", None),
        P(None, "batch"),
        P(None, None, "batch"),
    )
    out_specs = (
        P(None, None, "batch", "section"),
        P("section", None, None),
        P("section", None),
        P("section", None),
        P("section", None),
        P("section", None),
    )
    body = functools.partial(shards, grid_of(mesh.shape["batch"]))
    return jax.shard_map(body, mesh=mesh, in_specs=in_specs, out_specs=out_specs, check_vma=False)
```

```python
import functools

import jax
import jax.numpy as jnp
from jax import lax
from jax.experimental import pallas as pl
from jax.experimental.pallas import tpu as pltpu
from jax.sharding import PartitionSpec as P

EPS = 1e-05
W = 1024
HALF = W // 2
QUART = W // 4
PAIRS = 2
PART = W // PAIRS // 2
MESH = pl.DeviceIdType.MESH
F32 = jnp.float32
BF16 = jnp.bfloat16


def grid_of(size):
    if size == 16:
        return (4, 2, 2)
    if size == 128:
        return (8, 4, 4)
    return (size, 1, 1)


def aligned(x, k):
    return pl.multiple_of(x, k)


def wide(x, reps):
    return jnp.concatenate([x] * reps, axis=1)


def fold(x):
    rows = x.shape[0]
    total = x[0:8]
    for k in range(8, rows, 8):
        total = total + x[k : k + 8]
    return total


def dot(a, b, dims):
    return lax.dot_general(a, b, (dims, ((), ())), preferred_element_type=F32)


class Reduction:
    def __init__(self, env, layer, index, block, orders, lane_of):
        self.env, self.layer, self.index, self.block, self.orders = env, layer, index, block, orders
        self.lane_of = lane_of
        self.space = env["space"].at[layer, index]
        self.depth = len(orders[0])
        self.regions = [self.shares(i, order) for i, order in enumerate(orders)]
        self.step = 0
        self.waits = []
        self.slot = [0, 0]
        depth = self.depth
        self.steps = [functools.partial(self.scatter, k) for k in range(depth)]
        self.steps += [functools.partial(self.gather, k) for k in range(depth - 1, 0, -1)]
        self.steps += [self.give, self.finish]

    def shares(self, i, order):
        out = [(0, W, i * PART, PART)]
        for axis in order:
            out.append(self.share(out[-1], axis, axis["index"]))
        return out

    def share(self, region, axis, index):
        row, rows, lane, lanes = region
        by_row = min(axis["size"], rows // 16)
        rows, lanes = rows // by_row, lanes // (axis["size"] // by_row)
        if by_row == axis["size"]:
            return row + index * rows, rows, lane, lanes
        return row + lax.rem(index, by_row) * rows, rows, lane + index // by_row * lanes, lanes

    @property
    def free_to_go(self):
        return self.step != self.depth or self.layer in self.env["summed"]

    @property
    def done(self):
        return self.step >= len(self.steps)

    def advance(self):
        self.sent = []
        self.steps[self.step]()
        self.step += 1
        return self.sent

    def remote(self, i, src, dst, slot, where, recv=None):
        sems = (self.layer, self.index, i, slot)
        return pltpu.make_async_remote_copy(
            src_ref=src, dst_ref=dst, send_sem=self.env["ar_send"].at[sems],
            recv_sem=self.env["ar_recv"].at[sems] if recv is None else recv, device_id=where, device_id_type=MESH,
        )

    def wait(self):
        for made, came in self.waits:
            made.wait_send()
            came.wait_recv()
        self.waits = []

    def take(self, i):
        self.slot[i] += 1
        return self.slot[i] - 1

    def came_at(self, i, k, s):
        row = sum((a["size"] - 1) * self.regions[i][n + 1][1] for n, a in enumerate(self.orders[i][:k]))
        _, rows, _, lanes = self.regions[i][k + 1]
        return row + (s - 1) * rows, rows, i * PART, lanes

    def scatter(self, k):
        if k > 0:
            self.wait()
            self.add(k - 1)
        for i in range(2):
            self.scatter_part(i, k)

    def start_part(self, i):
        self.sent = []
        self.scatter_part(i, 0)
        if i == 1:
            self.step = 1
        return self.sent

    def scatter_part(self, i, k):
        axis = self.orders[i][k]
        for s in range(1, axis["size"]):
            other = lax.rem(axis["index"] + s, axis["size"])
            row, rows, lane, lanes = self.share(self.regions[i][k], axis, other)
            src = self.block.at[pl.ds(aligned(row, 16), rows), pl.ds(aligned(lane, 128), lanes)]
            at, n, at_lane, n_lanes = self.came_at(i, k, s)
            dst = self.space.at[pl.ds(at, n), pl.ds(at_lane, n_lanes)]
            made = self.remote(i, src, dst, self.take(i), axis["at"](other))
            made.start()
            self.waits.append((made, made))
            self.sent.append((axis["link"], rows * lanes * 2))

    def add(self, k, last=False):
        rows = self.regions[0][k + 1][1]
        size = min(rows, 32)
        out = []
        for i in range(2):
            row, _, lane, lanes = self.regions[i][k + 1]
            lane = aligned(lane, 128)
            extra = None
            if last:
                part = self.index // PAIRS
                first = aligned((self.index % PAIRS) * 2 * PART + lane, 128)
                extra = self.env["vtot"][self.layer, part, 0:1, pl.ds(first, lanes)]
            came = [self.came_at(i, k, s) for s in range(1, self.orders[i][k]["size"])]
            out.append((row, lane, lanes, came, self.local(i, self.regions[i][k + 1])[0], extra))

        def body(j, _):
            for row, lane, lanes, came, home, extra in out:
                here = pl.ds(aligned(row + j * size, 16), size)
                total = self.block[here, pl.ds(lane, lanes)].astype(F32)
                for at, _, at_lane, _ in came:
                    there = pl.ds(aligned(at + j * size, 16), size)
                    total = total + self.space[there, pl.ds(at_lane, lanes)].astype(F32)
                if last:
                    column = self.env["column"][self.layer, here, :].astype(F32)
                    total = total + wide(column, lanes // 128) * extra
                    to = pl.ds(aligned(home + j * size, 16), size)
                    self.space[to, pl.ds(lane, lanes)] = total.astype(BF16)
                else:
                    self.block[here, pl.ds(lane, lanes)] = total.astype(BF16)
            return 0

        lax.fori_loop(0, rows // size, body, 0)

    def local(self, i, region):
        row, rows, lane, lanes = region
        return row - self.regions[i][1][0], rows, lane, lanes

    def gather(self, k):
        self.wait()
        if k == self.depth - 1:
            self.add(k, last=True)

        def ref(i, region):
            row, rows, lane, lanes = self.local(i, region)
            return self.space.at[pl.ds(aligned(row, 16), rows), pl.ds(aligned(lane, 128), lanes)]

        for i, order in enumerate(self.orders):
            axis = order[k]
            mine = ref(i, self.regions[i][k + 1])
            for s in range(1, axis["size"]):
                to = lax.rem(axis["index"] + s, axis["size"])
                frm = lax.rem(axis["index"] + axis["size"] - s, axis["size"])
                slot = self.take(i)
                made = self.remote(i, mine, mine, slot, axis["at"](to))
                made.start()
                theirs = ref(i, self.share(self.regions[i][k], axis, frm))
                self.waits.append((made, self.remote(i, theirs, theirs, slot, axis["at"](frm))))
                self.sent.append((axis["link"], self.regions[i][k + 1][1] * self.regions[i][k + 1][3] * 2))

    def result(self, i, index, section):
        rows = self.regions[i][1][1]
        lane = aligned(self.lane_of(section) + i * PART, PART)
        return self.env["o"].at[section, pl.ds(aligned(index * rows, 16), rows), pl.ds(lane, PART)]

    def gathered(self, i):
        return self.space.at[pl.ds(0, self.regions[i][1][1]), pl.ds(i * PART, PART)]

    def deliver(self, i, s, straight):
        axis, section = self.orders[i][0], self.env["section"]
        recv = None if straight else self.env["ar_other"].at[self.layer, self.index, i, s]
        where = dict(axis["at"](lax.rem(axis["index"] + s, axis["size"])), section=self.layer)
        target = self.result(i, axis["index"], section)
        return self.remote(i, self.gathered(i), target, self.slot[i] + s, where, recv)

    def arrival(self, i, s, straight):
        axis, section = self.orders[i][0], self.env["section"]
        recv = None if straight else self.env["ar_other"].at[self.layer, self.index, i, s]
        index = lax.rem(axis["index"] + axis["size"] - s, axis["size"])
        frm = section if straight else 1 - section
        where = dict(axis["at"](index), section=frm)
        return self.remote(i, self.gathered(i), self.result(i, index, frm), self.slot[i] + s, where, recv)

    def kept(self, i):
        sem = self.env["ar_recv"].at[self.layer, self.index, i, self.slot[i]]
        target = self.result(i, self.orders[i][0]["index"], self.env["section"])
        return pltpu.make_async_copy(self.gathered(i), target, sem)

    def give(self):
        self.wait()

        @pl.when(self.env["section"] == self.layer)
        def _():
            for i in range(2):
                for s in range(1, self.orders[i][0]["size"]):
                    self.deliver(i, s, True).start()
                self.kept(i).start()

        @pl.when(self.env["section"] != self.layer)
        def _():
            for i in range(2):
                for s in range(self.orders[i][0]["size"] - 1, -1, -1):
                    self.deliver(i, s, False).start()

        for i, order in enumerate(self.orders):
            self.sent.append((order[0]["link"], self.regions[i][1][1] * PART * 2 * (order[0]["size"] - 1)))

    def finish(self):
        @pl.when(self.env["section"] == self.layer)
        def _():
            for i in range(2):
                size = self.orders[i][0]["size"]
                self.kept(i).wait()
                for s in range(1, size):
                    self.deliver(i, s, True).wait_send()
                    self.arrival(i, s, True).wait_recv()
                for s in range(size):
                    self.arrival(i, s, False).wait_recv()

        @pl.when(self.env["section"] != self.layer)
        def _():
            for i in range(2):
                for s in range(self.orders[i][0]["size"]):
                    self.deliver(i, s, False).wait_send()


class Order:
    RATE, HOP, QUEUE = 55e3, 2.0, 2.0

    def __init__(self):
        self.now = 0.0
        self.free = {}
        self.going = []
        self.held = []

    def sent(self, copies):
        end = self.now
        for link, size in copies:
            self.free[link] = max(self.now, self.free.get(link, 0.0)) + size / self.RATE
            end = max(end, self.free[link])
        return end + self.HOP

    def begin(self, one, i):
        self.held.append((one, i))
        self.release()

    def release(self, always=False):
        while self.held and (always or self.busy() < self.QUEUE):
            one, i = self.held.pop(0)
            end = self.sent(one.start_part(i))
            if i == 0:
                one.due = end
            else:
                one.due = max(one.due, end)
                self.going.append(one)

    def busy(self):
        link = self.held[0][0].orders[self.held[0][1]][:1]
        return max([self.free.get(a["link"], 0.0) - self.now for a in link], default=0.0)

    def advance(self, one):
        self.now = max(self.now, one.due) + 0.4
        one.due = self.sent(one.advance())
        if one.done:
            self.going.remove(one)

    def work(self, cost):
        self.now += cost
        while True:
            self.release()
            due = [x for x in self.going if x.due <= self.now and x.free_to_go]
            if not due:
                return
            self.advance(min(due, key=lambda x: x.due))

    def drain(self):
        while self.going or self.held:
            self.release(always=not self.going)
            self.advance(min(self.going, key=lambda x: x.due))


def kernel(dims, steps, seqs, views, frames, grad_out, weights, gains, shifts, recurs, lengths, masks, o, gf, vectors, f_own, f_far, p_own, p_far, g3, wc, wr1, src_t, live, turn,
           staged, heads, tails, v, vecs, rows, hid, coef, tot, vtot, levels, column, counts, cnt_p, cnt_z, slim_p, slim_z,
           wide_p, wide_z, space, sems, v_sems, stage_sem, credit, pl_send, pl_recv, z_send, z_recv, ar_send, ar_recv,
           ar_other):
    nz, ny, nx = dims
    np_ = ny * nx
    span = steps * seqs
    total_rows = 2 * span
    sent_rows = total_rows + 16
    pairs = steps // 2
    section = lax.axis_index("section")
    other = 1 - section
    b = lax.axis_index("batch")
    mp = lax.rem(b, np_)
    mz = b // np_

    def at_plane(i):
        return {"batch": b - mp + i}

    def at_z(i):
        return {"batch": b + (i - mz) * np_}

    def axis_of(link, size, stride):
        index = lax.rem(b // stride, size)
        return dict(link=link, size=size, index=index, at=lambda i: {"batch": b + (i - index) * stride})

    def halvings(link, size, stride):
        out = []
        while size > 1:
            out.append(axis_of(link, 2, stride))
            size //= 2
            stride *= 2
        return out

    xs, ys, zs = halvings("x", nx, 1), halvings("y", ny, nx), halvings("z", nz, np_)
    orders = (xs + ys + zs, ys + xs + zs)
    sibling = {"section": other}

    def local(src, dst, slot):
        return pltpu.make_async_copy(src, dst, sems.at[0, slot])

    def across(src, dst, slot):
        return pltpu.make_async_remote_copy(
            src_ref=src, dst_ref=dst, send_sem=sems.at[1, slot], recv_sem=sems.at[2, slot],
            device_id=sibling, device_id_type=MESH,
        )

    half = frames.shape[3]
    width = 2 * half
    lead = W - half
    rest = width - W
    full = rest // 128 * 128

    def fetch(source, m):
        return pltpu.make_async_copy(source.at[m], staged.at[m], stage_sem.at[m])

    def by_units(source, target, m):
        fetch(source, m).wait()

        @pl.when(section == 0)
        def _():
            pad = jnp.zeros((2 * seqs, lead), F32)

            def place(i, _):
                x = staged[m, pl.ds(2 * i, 2)].astype(F32).reshape(2 * seqs, half)
                to = pl.ds(aligned(m * span + 2 * i * seqs, 16), 2 * seqs)
                target[to, :] = jnp.concatenate([x, pad], axis=1).astype(BF16)
                return 0

            lax.fori_loop(0, pairs, place, 0)

        @pl.when(section == 1)
        def _():
            pad = jnp.zeros((2 * seqs, 2 * lead), F32)

            def place(i, _):
                x = staged[m, pl.ds(2 * i, 2)].astype(F32).reshape(2 * seqs, half)
                to = pl.ds(aligned(m * span + 2 * i * seqs, 16), 2 * seqs)
                target[to, :] = jnp.concatenate([x[:, lead:], pad], axis=1).astype(BF16)
                return 0

            lax.fori_loop(0, pairs, place, 0)

    def patch_heads(target, m):
        @pl.when(section == 0)
        def _():
            lane = lax.broadcasted_iota(jnp.int32, (2 * seqs, 128), 1)

            def place(i, _):
                to = pl.ds(aligned(m * span + 2 * i * seqs, 16), 2 * seqs)
                head = heads[m, pl.ds(2 * i, 2)].astype(F32).reshape(2 * seqs, 128)
                head = pltpu.roll(head, 128 - lead, 1)
                old = target[to, W - 128 :].astype(F32)
                target[to, W - 128 :] = jnp.where(lane < 128 - lead, old, head).astype(BF16)
                return 0

            lax.fori_loop(0, pairs, place, 0)

    def pieces(row, count, u, block, spot):
        r = pl.ds(row, count)
        to = pl.ds(0, count)
        if u == 0:
            return [(weights.at[0, r, pl.ds(0, W)], block.at[to, :])]
        return [
            (weights.at[0, r, pl.ds(W, full)], block.at[to, pl.ds(0, full)]),
            (weights.at[0, r, pl.ds(W + full, rest - full)], tails.at[spot, to, :]),
        ]

    rows_of = {0: (0, W), 1: (W, rest)}

    def w_plan(layer):
        mine, far = rows_of[layer], rows_of[1 - layer]
        plan = [
            (mine, layer, far, 1 - layer, wc.at[layer, 0], 2 * layer),
            (far, layer, mine, 1 - layer, wc.at[layer, 1], 2 * layer + 1),
        ]
        if layer == 1:
            plan.append((mine, 0, far, 1, wr1, 4))
        return plan

    late_row = (width - half) // 16 * 16
    late_shift = half - late_row
    late_plan = [
        ((0, W), 0, (late_row, width - late_row), 1, wc.at[0, 0], 0),
        ((0, W), 1, (late_row, width - late_row), 0, wc.at[0, 1], 1),
    ]
    slot_of = {0: 4, 1: 8, 2: 14}

    def local_w(plan, base, which):
        r, u, _, _, block, spot = plan[which]
        return [local(a, t, base + 2 * which + i) for i, (a, t) in enumerate(pieces(*r, u, block, spot))]

    def across_w(plan, base, which):
        _, _, r, u, block, spot = plan[which]
        return [across(a, t, base + 2 * which + i) for i, (a, t) in enumerate(pieces(*r, u, block, spot))]

    def start_local_w(layer, plan, base):
        @pl.when(section == layer)
        def _():
            for which in range(len(plan)):
                for made in local_w(plan, base, which):
                    made.start()

    def start_across_w(layer, plan, base):
        @pl.when(section == layer)
        def _():
            for which in range(len(plan)):
                for made in across_w(plan, base, which):
                    made.start()

    def last_units(block, spot):
        def body(i, _):
            r = pl.ds(aligned(i * 128, 128), 128)
            x = tails[spot, r, :].astype(F32)
            x = jnp.concatenate([x, jnp.zeros((128, 128 - x.shape[1]), F32)], axis=1)
            block[r, full:] = x.astype(BF16)
            return 0

        lax.fori_loop(0, W // 128, body, 0)

    def wait_w(layer, plan, base, which):
        _, own_u, _, far_u, block, spot = plan[which]

        @pl.when(section == layer)
        def _():
            for made in local_w(plan, base, which):
                made.wait()
            if own_u == 1:
                last_units(block, spot)

        @pl.when(section != layer)
        def _():
            for made in across_w(plan, base, which):
                made.wait_recv()
            if far_u == 1:
                last_units(block, spot)

    def done_w(layer, plan, base):
        @pl.when(section == layer)
        def _():
            for which in range(len(plan)):
                for made in across_w(plan, base, which):
                    made.wait_send()

    def heads_copy(source, slot):
        return across(source.at[:, :, :, pl.ds(0, 128)], heads, slot)

    def wait_heads(source, slot):
        @pl.when(section == 0)
        def _():
            heads_copy(source, slot).wait_recv()

        @pl.when(section == 1)
        def _():
            heads_copy(source, slot).wait_send()

    fetch(frames, 0).start()
    fetch(frames, 1).start()
    for layer in range(2):
        start_local_w(layer, w_plan(layer), slot_of[layer])

    barrier = pltpu.get_barrier_semaphore()
    greeted = [dict(sibling)]
    greeted += [at_plane(lax.rem(mp + k, np_)) for k in range(1, np_)]
    greeted += [at_z(lax.rem(mz + k, nz)) for k in range(1, nz)]
    for axis in (xs + zs)[:1] + (ys + zs)[:1]:
        for s in range(1, axis["size"]):
            greeted.append(dict(axis["at"](lax.rem(axis["index"] + s, axis["size"])), section=other))
    for where in greeted:
        pl.semaphore_signal(barrier, inc=1, device_id=where, device_id_type=MESH)

    for k, (x, fill) in enumerate(((gains, 0.0), (shifts, -1e30), (recurs, 0.0))):
        vecs[section, k : k + 1, 0:width] = x[...]
        vecs[section, k : k + 1, width:] = jnp.full((1, 2 * W - width), fill, F32)
    vecs[section, 3:8, :] = jnp.zeros((5, 2 * W), F32)

    gap = jnp.zeros((W - rest, W), BF16)

    @pl.when(section == 0)
    def _():
        wc[0, 1, rest:, :] = gap
        wc[1, 1, rest:, :] = gap

    @pl.when(section == 1)
    def _():
        wc[0, 0, rest:, :] = gap
        wc[1, 0, rest:, :] = gap
        wr1[rest:, :] = gap

    for spot in (0, 2):
        tails[spot, rest:, :] = jnp.zeros((W - rest, rest - full), BF16)
    for spare in (f_own, p_own, g3.at[0], g3.at[1]):
        spare[sent_rows:, :] = jnp.zeros((spare.shape[0] - sent_rows, W), BF16)

    pl.semaphore_wait(barrier, len(greeted))

    @pl.when(section == 1)
    def _():
        heads_copy(frames, 1).start()

    start_across_w(0, w_plan(0), slot_of[0])
    send_vec = across(vecs.at[section], vecs.at[section], 3)
    send_vec.start()

    def stage_copy(where, rnd, slot, k, back):
        buf, parity, size, me, at, send, recv = where
        there = at(lax.rem(me + (size - k if back else k), size))
        ref = buf.at[parity, slot]
        return pltpu.make_async_remote_copy(
            src_ref=ref, dst_ref=ref, send_sem=send.at[rnd, k], recv_sem=recv.at[rnd, k],
            device_id=there, device_id_type=MESH,
        )

    def in_plane(buf, parity):
        return (buf, parity, np_, mp, at_plane, pl_send, pl_recv)

    def in_line(buf, parity):
        return (buf, parity, nz, mz, at_z, z_send, z_recv)

    def stage_start(where, rnd, value):
        buf, parity, size, me = where[:4]
        buf[parity, me] = value
        for k in range(1, size):
            stage_copy(where, rnd, me, k, False).start()

    def stage_wait(where, rnd):
        size, me = where[2:4]
        for k in range(1, size):
            stage_copy(where, rnd, me, k, False).wait_send()
            stage_copy(where, rnd, lax.rem(me + size - k, size), k, True).wait_recv()

    def add_slots(where):
        buf, parity, size = where[:3]
        total = buf[parity, 0]
        for k in range(1, size):
            total = total + buf[parity, k]
        return total

    groups = lengths.shape[1]
    s_at = lax.broadcasted_iota(jnp.int32, (seqs, groups), 0)
    g_at = lax.broadcasted_iota(jnp.int32, (seqs, groups), 1) * views
    there = (s_at >= g_at) & (s_at < g_at + views)
    position = lax.broadcasted_iota(jnp.int32, (seqs, 128), 1)
    local_counts = []
    for m in range(2):
        turn[...] = jnp.zeros_like(turn)
        turn[0:steps, 0:seqs] = masks[m].astype(F32)
        mask = turn[...].T[0:seqs]
        length = jnp.broadcast_to(lengths[m : m + 1, :], (seqs, groups)).astype(F32)
        limit = jnp.sum(jnp.where(there, length, 0.0), axis=1, keepdims=True)
        alive = (position.astype(F32) < limit) & ((mask > 0.0) | (position == 0))
        alive = jnp.where(position < steps, alive.astype(F32), 0.0)
        total = jnp.zeros((seqs, 128), F32)
        for t in range(steps):
            at = m * span + t * seqs
            cells = jnp.broadcast_to(alive[:, t : t + 1], (seqs, 128))
            live[at : at + seqs, :] = cells
            total = total + cells
        local_counts.append(jnp.sum(total, axis=0, keepdims=True))
    n_own = jnp.concatenate([local_counts[0]] * 2 + [local_counts[1]] * 2, axis=0)
    n_own = jnp.concatenate([n_own, n_own], axis=0)

    cnt_plane, cnt_line = in_plane(cnt_p, 0), in_line(cnt_z, 0)
    stage_start(cnt_plane, 0, n_own)

    def vec_of(layer, k, lh):
        return vecs[layer, k : k + 1, pl.ds(aligned(section * W + lh * HALF, HALF), HALF)]

    def half_of(lh):
        return slice(lh * HALF, (lh + 1) * HALF)

    def matmul_to(out, a, w, first, lh):
        lanes = half_of(lh)

        def body(m, _):
            r = pl.ds(aligned(m * span, 16), span)
            y = dot(a[r, :], w[:, lanes], ((1,), (0,)))
            out[r, lanes] = y if first else out[r, lanes] + y
            return 0

        lax.fori_loop(0, 2, body, 0)

    def packed(x, y):
        return jnp.concatenate([z[:, k * QUART : (k + 1) * QUART] for z in (*x, *y) for k in range(2)], axis=0)

    def unpacked(x, m):
        return jnp.concatenate([x[2 * m + k : 2 * m + k + 1] for k in range(2)], axis=1)

    def merge_slots(where, counts_of):
        buf, parity, size = where[:3]
        s = [buf[parity, k, 0:4, :] for k in range(size)]
        q = [buf[parity, k, 4:8, :] for k in range(size)]
        n = [wide(counts_of(k), 2) for k in range(size)]
        total, squares, count = sum(s[1:], s[0]), sum(q[1:], q[0]), sum(n[1:], n[0])
        mean = total / count
        for k in range(size):
            d = s[k] / n[k] - mean
            squares = squares + n[k] * d * d
        return jnp.concatenate([total, squares], axis=0)

    def slim_round(which, lh):
        return 1 + 2 * which + lh, in_plane(slim_p, 2 * lh + which % 2), in_line(slim_z, 2 * lh + which % 2)

    def forward_stats(layer, lh):
        lanes = half_of(lh)
        sums, squares = [], []
        for m in range(2):
            start = jnp.sum(rows[layer, m * span : m * span + seqs, lanes], axis=0, keepdims=True) * (1.0 / seqs)

            def body(i, carry):
                s, q = carry
                r = pl.ds(aligned(m * span + i * (2 * seqs), 16), 2 * seqs)
                d = rows[layer, r, lanes] - start
                kept = wide(live[r, :], 4) * d
                return s + fold(kept), q + fold(kept * d)

            zero = jnp.zeros((8, HALF), F32)
            s, q = lax.fori_loop(0, pairs, body, (zero, zero))
            s, q = jnp.sum(s, axis=0, keepdims=True), jnp.sum(q, axis=0, keepdims=True)
            n = wide(local_counts[m], 4)
            sums.append(s + n * start)
            squares.append(jnp.maximum(q - s * s / n, 0.0))
        rnd, plane, _ = slim_round(layer, lh)
        stage_start(plane, rnd, packed(sums, squares))

    def forward_middle(layer, lh):
        rnd, plane, line = slim_round(layer, lh)
        stage_wait(plane, rnd)
        stage_start(line, rnd, merge_slots(plane, lambda k: cnt_p[0, k, 0:4, :]))

    def forward_end(layer, lh):
        rnd, _, line = slim_round(layer, lh)
        lanes = half_of(lh)
        stage_wait(line, rnd)
        value = merge_slots(line, lambda k: cnt_z[0, k, 0:4, :])
        for m in range(2):
            count = wide(counts[2 * m : 2 * m + 1, :], 4)
            mean = unpacked(value[0:4], m) / count
            scale = lax.rsqrt(unpacked(value[4:8], m) / count + EPS)
            coef[layer, 2 * m : 2 * m + 1, lanes] = mean
            coef[layer, 2 * m + 1 : 2 * m + 2, lanes] = scale
            slope = vec_of(layer, 0, lh) * scale
            coef[layer, 4 + 2 * m : 5 + 2 * m, lanes] = slope
            coef[layer, 5 + 2 * m : 6 + 2 * m, lanes] = vec_of(layer, 1, lh) - mean * slope

    def forward_scan(layer, lh, passes):
        lanes = half_of(lh)
        rec = vec_of(layer, 2, lh)
        slope = [coef[layer, 4 + 2 * m : 5 + 2 * m, lanes] for m in range(2)]
        shift = [coef[layer, 5 + 2 * m : 6 + 2 * m, lanes] for m in range(2)]

        def body(i, carry):
            states, level = carry
            out = []
            for m in range(2):
                r = pl.ds(aligned(m * span + i * (2 * seqs), 16), 2 * seqs)
                x = rows[layer, r, lanes] * slope[m] + shift[m]
                lv = wide(live[r, :], 4)
                alive = lv > 0.0
                h = states[m]
                both = []
                for k in range(2):
                    part = slice(k * seqs, (k + 1) * seqs)
                    z = x[part] + rec * h
                    soft = jnp.maximum(z, 0.0) + jnp.log(1.0 + jnp.exp(-jnp.abs(z)))
                    h = jnp.where(alive[part], soft, h)
                    both.append(h)
                two = jnp.concatenate(both, axis=0)
                hid[layer, r, lanes] = two
                if passes:
                    p_own[r, lanes] = two.astype(BF16)
                    level = level + fold(lv * two)
                out.append(h)
            return tuple(out), level

        zero = jnp.zeros((seqs, HALF), F32)
        _, level = lax.fori_loop(0, pairs, body, ((zero, zero), jnp.zeros((8, HALF), F32)))
        if not passes:
            return None
        levels[1:2, lanes] = jnp.sum(level, axis=0, keepdims=True)
        made = across(p_own.at[pl.ds(0, total_rows), lanes], p_far.at[:, lanes], 18 + lh)
        made.start()
        return made

    def backward_scan(layer, lh, above, between=lambda: None):
        for lq in range(2 * lh, 2 * lh + 2):
            lanes = slice(lq * QUART, (lq + 1) * QUART)
            gq, sq, rec = (vec_of(layer, k, lh)[:, (lq % 2) * QUART : (lq % 2 + 1) * QUART] for k in range(3))
            mean = [coef[layer, 2 * m : 2 * m + 1, lanes] for m in range(2)]
            scale = [coef[layer, 2 * m + 1 : 2 * m + 2, lanes] for m in range(2)]

            def body(i, carry):
                down, s1, s2, rsum, sqh, sqa = carry
                down, s1, s2 = list(down), list(s1), list(s2)
                i = pairs - 1 - i
                for m in range(2):
                    start = m * span + i * (2 * seqs)
                    r = pl.ds(aligned(start, 16), 2 * seqs)
                    before = pl.ds(aligned(jnp.maximum(start - seqs, 0), 8), seqs)
                    normed = (rows[layer, r, lanes] - mean[m]) * scale[m]
                    drive = gq * normed + sq
                    h2 = hid[layer, r, lanes]
                    hb = jnp.where(i > 0, hid[layer, before, lanes], 0.0)
                    lv = wide(live[r, :], 2)
                    up = above[r, lanes].astype(F32)
                    res = f_own[r, lanes].astype(F32)
                    aux = res + h2 if layer == 1 else res
                    sqh = sqh + fold(lv * (h2 * h2))
                    sqa = sqa + fold(lv * (aux * aux))
                    grads = [None, None]
                    for k in (1, 0):
                        part = slice(k * seqs, (k + 1) * seqs)
                        prior = h2[0:seqs] if k == 1 else hb
                        slope = 0.5 + 0.5 * jnp.tanh(0.5 * (drive[part] + rec * prior))
                        total = up[part] + down[m]
                        gd = lv[part] * slope * total
                        down[m] = (1.0 - lv[part]) * total + rec * gd
                        grads[k] = gd
                        rsum = rsum + fold(gd * prior)
                    gd2 = jnp.concatenate(grads, axis=0)
                    hid[layer, r, lanes] = gd2
                    s1[m] = s1[m] + fold(gd2)
                    s2[m] = s2[m] + fold(gd2 * normed)
                return tuple(down), tuple(s1), tuple(s2), rsum, sqh, sqa

            zero = jnp.zeros((seqs, QUART), F32)
            z8 = jnp.zeros((8, QUART), F32)
            _, s1, s2, rsum, sqh, sqa = lax.fori_loop(
                0, pairs, body, ((zero, zero), (z8, z8), (z8, z8), z8, z8, z8)
            )
            for k, x in enumerate((s1[0], s1[1], s2[0], s2[1], rsum, sqh, sqa)):
                tot[layer, k : k + 1, lanes] = jnp.sum(x, axis=0, keepdims=True)
            between()

    def backward_stats(layer, lh):
        rnd, plane, _ = slim_round(3 - layer, lh)
        t = tot[layer, 0:4, half_of(lh)]
        stage_start(plane, rnd, packed([t[0:1], t[1:2]], [t[2:3], t[3:4]]))

    def backward_middle(layer, lh):
        rnd, plane, line = slim_round(3 - layer, lh)
        stage_wait(plane, rnd)
        stage_start(line, rnd, add_slots(plane))

    def backward_end(layer, lh):
        rnd, _, line = slim_round(3 - layer, lh)
        stage_wait(line, rnd)
        value = add_slots(line)
        for m in range(2):
            tot[layer, m : m + 1, half_of(lh)] = unpacked(value[0:4], m)
            tot[layer, 2 + m : 3 + m, half_of(lh)] = unpacked(value[4:8], m)

    def grad_rows(layer, lh, slot):
        lanes = half_of(lh)
        acc = jnp.zeros((8, HALF), F32)
        for m in range(2):
            mean = coef[layer, 2 * m : 2 * m + 1, lanes]
            scale = coef[layer, 2 * m + 1 : 2 * m + 2, lanes]
            count = wide(counts[2 * m : 2 * m + 1, :], 4)
            first = tot[layer, m : m + 1, lanes] / count
            second = tot[layer, 2 + m : 3 + m, lanes] / count * scale
            k = coef[layer, 4 + 2 * m : 5 + 2 * m, lanes]

            def body(i, acc):
                r = pl.ds(aligned(m * span + i * (2 * seqs), 16), 2 * seqs)
                y = hid[layer, r, lanes] - first - (rows[layer, r, lanes] - mean) * second
                y = wide(live[r, :], 4) * (k * y)
                g3[0, r, lanes] = y.astype(BF16)
                return acc + fold(y)

            acc = lax.fori_loop(0, pairs, body, acc)
        top = lax.broadcasted_iota(jnp.int32, (16, HALF), 0) == 0
        minus = jnp.where(top, -jnp.sum(acc, axis=0, keepdims=True), 0.0)
        g3[0, total_rows:sent_rows, lanes] = minus.astype(BF16)
        made = across(g3.at[0, pl.ds(0, sent_rows), lanes], g3.at[1, pl.ds(0, sent_rows), lanes], slot + lh)
        made.start()
        return made

    sums_round = {1: (1, 10), 0: (0, 11)}

    def sums_start(layer):
        parity, rnd = sums_round[layer]
        own_sum = -g3[0, total_rows:sent_rows, :].astype(F32)[0:1]
        value = jnp.concatenate([own_sum, tot[layer, 4:7, :], jnp.zeros((4, W), F32)], axis=0)
        stage_start(in_plane(wide_p, parity), rnd, value)

    def sums_middle(layer):
        parity, rnd = sums_round[layer]
        stage_wait(in_plane(wide_p, parity), rnd)
        stage_start(in_line(wide_z, parity), rnd, add_slots(in_plane(wide_p, parity)))

    def swap_sums(layer):
        return across(vtot.at[layer, 0], vtot.at[layer, 1], 25 + layer)

    def sums_end(layer):
        parity, rnd = sums_round[layer]
        stage_wait(in_line(wide_z, parity), rnd)
        vtot[layer, 0] = add_slots(in_line(wide_z, parity))
        swap_sums(layer).start()
        tot[layer, 4:7, :] = vtot[layer, 0, 1:4, :]
        tot[layer, 7:8, :] = wide(counts[0:1, :] + counts[2:3, :], 8)

        @pl.when(section == layer)
        def _():
            pltpu.make_async_copy(tot.at[layer], v.at[section], v_sems.at[0]).start()

        @pl.when(section != layer)
        def _():
            v_across(layer).start()

    def sums_there(layer):
        swap_sums(layer).wait()
        env["summed"].add(layer)

    def v_across(layer):
        return pltpu.make_async_remote_copy(
            src_ref=tot.at[layer], dst_ref=v.at[section], send_sem=v_sems.at[1], recv_sem=v_sems.at[2],
            device_id=sibling, device_id_type=MESH,
        )

    def transpose(src, begin=0, end=W // 128):
        def body(j, _):
            c = pl.ds(aligned(j * 128, 128), 128)
            src_t[c, 0:total_rows] = src[0:total_rows, c].T
            return 0

        lax.fori_loop(begin, end, body, 0)

    def transpose_level(src, layer):
        top = lax.broadcasted_iota(jnp.int32, (16, W), 0) == 0
        src[total_rows:sent_rows, :] = jnp.where(top, levels[2 + layer : 3 + layer, :], 0.0).astype(BF16)

        def body(j, _):
            c = pl.ds(aligned(j * 128, 128), 128)
            src_t[c, total_rows:] = src[total_rows:, c].T
            level = src[total_rows:sent_rows, c].astype(F32)[0:1]
            column[layer, c, :] = jnp.broadcast_to(level, (128, 128)).T.astype(BF16)
            return 0

        lax.fori_loop(0, W // 128, body, 0)

    def weight_part(block, grads, c):
        lanes = pl.ds(c * HALF, HALF)

        def body(j, _):
            r = pl.ds(aligned(j * HALF, HALF), HALF)
            block[r, lanes] = dot(src_t[r, :], grads[:, lanes], ((1,), (0,))).astype(BF16)
            return 0

        lax.fori_loop(0, W // HALF, body, 0)

    def source_grad(store, w_own, w_far, half_index):
        c = half_of(half_index)

        def body(m, _):
            r = pl.ds(aligned(m * span, 16), span)
            y = dot(g3[0, r, :], w_own[c, :], ((1,), (1,))) + dot(g3[1, r, :], w_far[c, :], ((1,), (1,)))
            store(r, c, y)
            return 0

        lax.fori_loop(0, 2, body, 0)

    env = dict(summed=set(), vtot=vtot, column=column, space=space, ar_send=ar_send, ar_recv=ar_recv,
               ar_other=ar_other, o=o, section=section, here={"batch": b})
    blocks = {
        (1, 0): f_far.at[pl.ds(0, W), :],
        (1, 1): p_far.at[pl.ds(0, W), :],
        (0, 0): wc.at[1, 1],
        (0, 1): wr1,
    }
    parts = {}
    for layer in (1, 0):
        for index in range(2 * PAIRS):
            part, side = index // PAIRS, index % PAIRS

            def lane_of(sec, part=part, side=side):
                return (sec if part == 0 else 1 - sec) * W + side * 2 * PART

            block = blocks[layer, part].at[:, pl.ds(side * 2 * PART, 2 * PART)]
            parts[layer, index] = Reduction(env, layer, index, block, orders, lane_of)
    order = Order()

    def weight_grads(layer, part, c):
        weight_part(blocks[layer, part], g3.at[part], c)
        order.work(2.0)
        for k in range(c * HALF // PART, (c + 1) * HALF // PART):
            order.begin(parts[layer, part * PAIRS + k // 2], k % 2)

    def arrived(sends):
        for made in sends:
            made.wait()

    send_f = []
    for m in range(2):
        by_units(frames, f_own, m)
        fetch(grad_out, m).start()
        if m == 0:
            wait_heads(frames, 1)
        patch_heads(f_own, m)
        here = pl.ds(m * span, span)
        made = across(f_own.at[here, :], f_far.at[here, :], (0, 24)[m])
        made.start()
        send_f.append(made)
    start_across_w(1, w_plan(1), slot_of[1])
    stage_wait(cnt_plane, 0)
    stage_start(cnt_line, 0, add_slots(cnt_plane))
    wait_w(0, w_plan(0), slot_of[0], 0)
    matmul_to(rows.at[0], f_own, wc.at[0, 0], True, 0)
    matmul_to(rows.at[0], f_own, wc.at[0, 0], True, 1)
    wait_w(0, w_plan(0), slot_of[0], 1)
    for made in send_f:
        made.wait()

    @pl.when(section == 1)
    def _():
        heads_copy(grad_out, 2).start()

    matmul_to(rows.at[0], f_far, wc.at[0, 1], False, 0)
    forward_stats(0, 0)
    matmul_to(rows.at[0], f_far, wc.at[0, 1], False, 1)
    forward_middle(0, 0)
    forward_stats(0, 1)
    send_vec.wait_send()
    across(vecs.at[other], vecs.at[other], 3).wait_recv()
    by_units(grad_out, g3.at[1], 0)
    wait_heads(grad_out, 2)
    patch_heads(g3.at[1], 0)
    stage_wait(cnt_line, 0)
    counts[...] = add_slots(cnt_line)
    forward_end(0, 0)
    forward_middle(0, 1)
    sends = [forward_scan(0, 0, True)]
    forward_end(0, 1)
    sends.append(forward_scan(0, 1, True))
    wait_w(1, w_plan(1), slot_of[1], 0)
    matmul_to(rows.at[1], p_own, wc.at[1, 0], True, 0)
    matmul_to(rows.at[1], p_own, wc.at[1, 0], True, 1)
    wait_w(1, w_plan(1), slot_of[1], 1)
    for made in sends:
        made.wait()
    matmul_to(rows.at[1], p_far, wc.at[1, 1], False, 0)
    forward_stats(1, 0)
    done_w(0, w_plan(0), slot_of[0])

    start_local_w(0, late_plan, slot_of[2])
    start_across_w(0, late_plan, slot_of[2])

    @pl.when(section == 1)
    def _():
        wc[0, 1, width - late_row :, :] = jnp.zeros((W - width + late_row, W), BF16)

    def source_level():
        def body(i, acc):
            r = pl.ds(aligned(i * (2 * seqs), 16), 2 * seqs)
            return acc + fold(wide(live[r, :], 8) * f_own[r, :].astype(F32))

        acc = lax.fori_loop(0, 2 * pairs, body, jnp.zeros((8, W), F32))
        levels[0:1, :] = jnp.sum(acc, axis=0, keepdims=True)

    matmul_to(rows.at[1], p_far, wc.at[1, 1], False, 1)
    forward_middle(1, 0)
    forward_stats(1, 1)
    by_units(grad_out, g3.at[1], 1)
    patch_heads(g3.at[1], 1)
    forward_end(1, 0)
    forward_middle(1, 1)
    forward_scan(1, 0, False)
    backward_scan(1, 0, g3.at[1])
    backward_stats(1, 0)
    forward_end(1, 1)
    source_level()
    level_plane, level_line = in_plane(wide_p, 0), in_line(wide_z, 0)
    stage_start(level_plane, 9, jnp.concatenate([levels[0:2, :], jnp.zeros((6, W), F32)], axis=0))
    forward_scan(1, 1, False)
    backward_middle(1, 0)
    stage_wait(level_plane, 9)
    stage_start(level_line, 9, add_slots(level_plane))
    backward_scan(1, 1, g3.at[1])
    backward_stats(1, 1)
    pl.semaphore_signal(credit.at[0], inc=1, device_id=sibling, device_id_type=MESH)
    backward_end(1, 0)
    pl.semaphore_wait(credit.at[0], 1)
    sends = [grad_rows(1, 0, 20)]
    transpose(p_own, 0, W // 256)
    backward_middle(1, 1)
    transpose(p_own, W // 256)
    stage_wait(level_line, 9)
    levels[2:4, :] = (add_slots(level_line) / wide(counts[0:1, :] + counts[2:3, :], 8))[0:2]
    transpose_level(p_own, 1)
    backward_end(1, 1)
    sends.append(grad_rows(1, 1, 20))
    sums_start(1)
    weight_grads(1, 0, 0)
    sums_middle(1)
    weight_grads(1, 0, 1)
    sums_end(1)
    arrived(sends)
    weight_grads(1, 1, 0)
    weight_grads(1, 1, 1)
    sums_there(1)
    wait_w(1, w_plan(1), slot_of[1], 2)
    done_w(1, w_plan(1), slot_of[1])

    def keep_down(r, c, y):
        p_own[r, c] = y.astype(BF16)

    source_grad(keep_down, wc.at[1, 0], wr1, 0)
    order.work(2.5)
    backward_scan(0, 0, p_own, lambda: order.work(1.3))
    backward_stats(0, 0)
    source_grad(keep_down, wc.at[1, 0], wr1, 1)
    pl.semaphore_signal(credit.at[1], inc=1, device_id=sibling, device_id_type=MESH)
    order.work(2.5)
    backward_middle(0, 0)
    backward_scan(0, 1, p_own, lambda: order.work(1.3))
    backward_stats(0, 1)
    backward_end(0, 0)
    pl.semaphore_wait(credit.at[1], 1)
    sends = [grad_rows(0, 0, 22)]
    order.work(1.3)
    transpose(f_own, 0, W // 256)
    backward_middle(0, 1)
    transpose(f_own, W // 256)
    transpose_level(f_own, 0)
    order.work(4.0)
    weight_grads(0, 0, 0)
    backward_end(0, 1)
    sends.append(grad_rows(0, 1, 22))
    sums_start(0)
    order.work(1.3)
    weight_grads(0, 0, 1)
    arrived(sends)
    weight_grads(0, 1, 0)
    weight_grads(0, 1, 1)
    wait_w(0, late_plan, slot_of[2], 0)
    wait_w(0, late_plan, slot_of[2], 1)
    done_w(0, late_plan, slot_of[2])

    def keep_source(r, c, y):
        rows[0, r, c] = y

    fetch(grad_out, 0).start()
    fetch(grad_out, 1).start()
    source_grad(keep_source, wc.at[0, 0], wc.at[0, 1], 0)
    order.work(2.5)
    sums_middle(0)
    source_grad(keep_source, wc.at[0, 0], wc.at[0, 1], 1)
    order.work(2.5)
    sums_end(0)
    sums_there(0)

    def give(m):
        return pltpu.make_async_copy(staged.at[m], gf.at[m], stage_sem.at[m])

    for m in range(2):
        fetch(grad_out, m).wait()

        def finish_frames(i, _, m=m):
            straight = staged[m, pl.ds(2 * i, 2)].astype(F32).reshape(2 * seqs, half)
            y = rows[0, pl.ds(aligned(m * span + 2 * i * seqs, 8), 2 * seqs), :]
            y = jnp.where(section == 0, y[:, :half], y[:, late_shift : late_shift + half])
            staged[m, pl.ds(2 * i, 2)] = (y + straight).reshape(2, seqs, half).astype(BF16)
            return 0

        lax.fori_loop(0, pairs, finish_frames, 0)
        give(m).start()
        order.work(2.0)
    order.drain()
    for m in range(2):
        give(m).wait()

    for layer in range(2):

        @pl.when(section == layer)
        def _(layer=layer):
            pltpu.make_async_copy(tot.at[layer], v.at[section], v_sems.at[0]).wait()
            pltpu.make_async_remote_copy(
                src_ref=tot.at[layer], dst_ref=v.at[other], send_sem=v_sems.at[1], recv_sem=v_sems.at[2],
                device_id=sibling, device_id_type=MESH,
            ).wait_recv()

        @pl.when(section != layer)
        def _(layer=layer):
            v_across(layer).wait_send()

    own_part, far_part = v[section], v[other]
    first = jnp.where(section == 0, own_part, far_part)
    second = jnp.where(section == 0, far_part, own_part)
    for row, terms in ((0, (2, 3)), (1, (0, 1)), (2, (4,))):
        for lane, x in ((0, first), (W, second)):
            total = x[terms[0] : terms[0] + 1, :]
            for k in terms[1:]:
                total = total + x[k : k + 1, :]
            vectors[row : row + 1, lane : lane + W] = total
    squares = jnp.sum(first[5:7, :] + second[5:7, :], axis=1, keepdims=True)
    root = jnp.sqrt(squares / (first[7:8, 0:1] * width))
    for k in range(2):
        vectors[3 + k : 4 + k, :] = jnp.broadcast_to(root[k : k + 1], (1, 2 * W))
    vectors[5:8, :] = jnp.zeros((3, 2 * W), F32)


def write_results(o, gf, vectors, grad_weight, grad_frames, grad_gains, grad_shifts, grad_recurs, table):
    width = grad_weight.shape[2]
    grad_weight[0] = o[...][:, :width].astype(F32)
    grad_frames[...] = gf[...]

    @pl.when(pl.program_id(0) == 0)
    def _():
        for k, out in enumerate((grad_gains, grad_shifts, grad_recurs)):
            out[...] = vectors[k : k + 1, 0:width]
        table[...] = jnp.concatenate([vectors[3:4, 0:1], vectors[4:5, 0:1]], axis=1)


def results(o, gf, vectors):
    micro, steps, seqs, half = gf.shape
    width = 2 * half
    count = W * 2 // 256
    frames = micro * steps // count
    whole = lambda shape: pl.BlockSpec(shape, lambda i: (0, 0))
    out = pl.pallas_call(
        write_results,
        grid=(count,),
        in_specs=[
            pl.BlockSpec((256, 2 * W), lambda i: (i, 0)),
            pl.BlockSpec((frames, seqs, half), lambda i: (i, 0, 0)),
            whole((8, 2 * W)),
        ],
        out_specs=(
            pl.BlockSpec((1, 256, width), lambda i: (0, i, 0)),
            pl.BlockSpec((frames, seqs, half), lambda i: (i, 0, 0)),
            whole((1, width)),
            whole((1, width)),
            whole((1, width)),
            whole((1, 2)),
        ),
        out_shape=(
            jax.ShapeDtypeStruct((1, width, width), F32),
            jax.ShapeDtypeStruct((micro * steps, seqs, half), BF16),
            jax.ShapeDtypeStruct((1, width), F32),
            jax.ShapeDtypeStruct((1, width), F32),
            jax.ShapeDtypeStruct((1, width), F32),
            jax.ShapeDtypeStruct((1, 2), F32),
        ),
        compiler_params=pltpu.CompilerParams(vmem_limit_bytes=64 * 1024 * 1024),
    )(o.reshape(2 * W, 2 * W), gf.reshape(micro * steps, seqs, half), vectors)
    return out[1].reshape(gf.shape), out[0], *out[2:]


def whole_step(dims, frames, grad_out, weights, gains, shifts, recurs, lengths, masks):
    nz, ny, nx = dims
    micro, steps, seqs, half = frames.shape
    width = 2 * half
    views = seqs // lengths.shape[1]
    rows = micro * steps * seqs
    np_ = ny * nx
    wide_rows = (rows + 16 + 127) // 128 * 128
    across_first = max(nx, ny, nz if np_ == 1 else 1)
    copies = 2 * (nx + ny + nz) + across_first
    came_rows = (nx - 1) * (W // nx) + (ny - 1) * (W // np_) + (nz - 1) * max(W // np_ // nz, 16)
    any_ = pl.BlockSpec(memory_space=pl.ANY)
    held = pl.BlockSpec(memory_space=pltpu.VMEM)
    dma = pltpu.SemaphoreType.DMA
    return pl.pallas_call(
        functools.partial(kernel, dims, steps, seqs, views),
        out_shape=(
            jax.ShapeDtypeStruct((2, W, 2 * W), BF16),
            jax.ShapeDtypeStruct(frames.shape, BF16),
            jax.ShapeDtypeStruct((8, 2 * W), F32),
        ),
        in_specs=[any_] * 3 + [held] * 5,
        out_specs=(any_, any_, held),
        scratch_shapes=[
            pltpu.VMEM((wide_rows, W), BF16),
            pltpu.VMEM((rows, W), BF16),
            pltpu.VMEM((wide_rows, W), BF16),
            pltpu.VMEM((rows, W), BF16),
            pltpu.VMEM((2, wide_rows, W), BF16),
            pltpu.VMEM((2, 2, W, W), BF16),
            pltpu.VMEM((W, W), BF16),
            pltpu.VMEM((W, wide_rows), BF16),
            pltpu.VMEM((rows, 128), F32),
            pltpu.VMEM((128, 128), F32),
            pltpu.VMEM(frames.shape, BF16),
            pltpu.VMEM((micro, steps, seqs, 128), BF16),
            pltpu.VMEM((5, W, (width - W) % 128), BF16),
            pltpu.VMEM((2, 8, W), F32),
            pltpu.VMEM((2, 8, 2 * W), F32),
            pltpu.VMEM((2, rows, W), F32),
            pltpu.VMEM((2, rows, W), F32),
            pltpu.VMEM((2, 8, W), F32),
            pltpu.VMEM((2, 8, W), F32),
            pltpu.VMEM((2, 2, 8, W), F32),
            pltpu.VMEM((8, W), F32),
            pltpu.VMEM((2, W, 128), BF16),
            pltpu.VMEM((8, 128), F32),
            pltpu.VMEM((1, np_, 8, 128), F32),
            pltpu.VMEM((1, nz, 8, 128), F32),
            pltpu.VMEM((4, np_, 8, QUART), F32),
            pltpu.VMEM((4, nz, 8, QUART), F32),
            pltpu.VMEM((2, np_, 8, W), F32),
            pltpu.VMEM((2, nz, 8, W), F32),
            pltpu.VMEM((2, 2 * PAIRS, max(came_rows, W), 2 * PART), BF16),
            dma((3, 27)),
            dma((3,)),
            dma((2,)),
            pltpu.SemaphoreType.REGULAR((2,)),
            dma((12, max(np_, 2))),
            dma((12, max(np_, 2))),
            dma((12, max(nz, 2))),
            dma((12, max(nz, 2))),
            dma((2, 2 * PAIRS, 2, copies)),
            dma((2, 2 * PAIRS, 2, copies)),
            dma((2, 2 * PAIRS, 2, across_first)),
        ],
        compiler_params=pltpu.CompilerParams(
            collective_id=0, has_side_effects=True, vmem_limit_bytes=64 * 1024 * 1024
        ),
    )(frames, grad_out, weights, gains, shifts, recurs, lengths, masks)


def shards(dims, frames, grad_out, weights, gains, shifts, recurs, lengths, masks):
    return results(*whole_step(dims, frames, grad_out, weights, gains, shifts, recurs, lengths, masks))


def solution(mesh):
    in_specs = (
        P(None, None, "batch", "section"),
        P(None, None, "batch", "section"),
        P("section", None, None),
        P("section", None),
        P("section", None),
        P("section", None),
        P(None, "batch"),
        P(None, None, "batch"),
    )
    out_specs = (
        P(None, None, "batch", "section"),
        P("section", None, None),
        P("section", None),
        P("section", None),
        P("section", None),
        P("section", None),
    )
    body = functools.partial(shards, grid_of(mesh.shape["batch"]))
    return jax.shard_map(body, mesh=mesh, in_specs=in_specs, out_specs=out_specs, check_vma=False)
```

```python
import functools

import jax
import jax.numpy as jnp
from jax import lax
from jax.experimental import pallas as pl
from jax.experimental.pallas import tpu as pltpu
from jax.sharding import PartitionSpec as P

EPS = 1e-05
W = 1024
HALF = W // 2
QUART = W // 4
PAIRS = 2
PART = W // PAIRS // 2
MESH = pl.DeviceIdType.MESH
F32 = jnp.float32
BF16 = jnp.bfloat16


def grid_of(size):
    if size == 16:
        return (4, 2, 2)
    if size == 128:
        return (8, 4, 4)
    return (size, 1, 1)


def aligned(x, k):
    return pl.multiple_of(x, k)


def wide(x, reps):
    return jnp.concatenate([x] * reps, axis=1)


def fold(x):
    rows = x.shape[0]
    total = x[0:8]
    for k in range(8, rows, 8):
        total = total + x[k : k + 8]
    return total


def repeat(count, body, init, times):
    while count % times:
        times -= 1

    def several(i, carry):
        for j in range(times):
            carry = body(i * times + j, carry)
        return carry

    return lax.fori_loop(0, count // times, several, init)


def dot(a, b, dims):
    return lax.dot_general(a, b, (dims, ((), ())), preferred_element_type=F32)


class Reduction:
    def __init__(self, env, layer, index, block, orders, lane_of):
        self.env, self.layer, self.index, self.block, self.orders = env, layer, index, block, orders
        self.lane_of = lane_of
        self.space = env["space"].at[layer, index]
        self.depth = len(orders[0])
        self.regions = [self.shares(i, order) for i, order in enumerate(orders)]
        self.step = 0
        self.waits = []
        self.slot = [0, 0]
        depth = self.depth
        self.steps = [functools.partial(self.scatter, k) for k in range(depth)]
        self.steps += [functools.partial(self.gather, k) for k in range(depth - 1, 0, -1)]
        self.steps += [self.give, self.finish]

    def shares(self, i, order):
        out = [(0, W, i * PART, PART)]
        for axis in order:
            out.append(self.share(out[-1], axis, axis["index"]))
        return out

    def share(self, region, axis, index):
        row, rows, lane, lanes = region
        by_row = min(axis["size"], rows // 16)
        rows, lanes = rows // by_row, lanes // (axis["size"] // by_row)
        if by_row == axis["size"]:
            return row + index * rows, rows, lane, lanes
        return row + lax.rem(index, by_row) * rows, rows, lane + index // by_row * lanes, lanes

    @property
    def free_to_go(self):
        return self.step != self.depth or self.layer in self.env["summed"]

    @property
    def done(self):
        return self.step >= len(self.steps)

    def advance(self):
        self.sent = []
        self.steps[self.step]()
        self.step += 1
        return self.sent

    def remote(self, i, src, dst, slot, where, recv=None):
        sems = (self.layer, self.index, i, slot)
        return pltpu.make_async_remote_copy(
            src_ref=src, dst_ref=dst, send_sem=self.env["ar_send"].at[sems],
            recv_sem=self.env["ar_recv"].at[sems] if recv is None else recv, device_id=where, device_id_type=MESH,
        )

    def wait(self):
        for made, came in self.waits:
            made.wait_send()
            came.wait_recv()
        self.waits = []

    def take(self, i):
        self.slot[i] += 1
        return self.slot[i] - 1

    def came_at(self, i, k, s):
        row = sum((a["size"] - 1) * self.regions[i][n + 1][1] for n, a in enumerate(self.orders[i][:k]))
        _, rows, _, lanes = self.regions[i][k + 1]
        return row + (s - 1) * rows, rows, i * PART, lanes

    def scatter(self, k):
        if k > 0:
            self.wait()
            self.add(k - 1)
        for i in range(2):
            self.scatter_part(i, k)

    def start_part(self, i):
        self.sent = []
        self.scatter_part(i, 0)
        if i == 1:
            self.step = 1
        return self.sent

    def scatter_part(self, i, k):
        axis = self.orders[i][k]
        for s in range(1, axis["size"]):
            other = lax.rem(axis["index"] + s, axis["size"])
            row, rows, lane, lanes = self.share(self.regions[i][k], axis, other)
            src = self.block.at[pl.ds(aligned(row, 16), rows), pl.ds(aligned(lane, 128), lanes)]
            at, n, at_lane, n_lanes = self.came_at(i, k, s)
            dst = self.space.at[pl.ds(at, n), pl.ds(at_lane, n_lanes)]
            made = self.remote(i, src, dst, self.take(i), axis["at"](other))
            made.start()
            self.waits.append((made, made))
            self.sent.append((axis["link"], rows * lanes * 2))

    def add(self, k, last=False):
        rows = self.regions[0][k + 1][1]
        size = min(rows, 128)
        out = []
        for i in range(2):
            row, _, lane, lanes = self.regions[i][k + 1]
            lane = aligned(lane, 128)
            extra = None
            if last:
                part = self.index // PAIRS
                first = aligned((self.index % PAIRS) * 2 * PART + lane, 128)
                extra = self.env["vtot"][self.layer, part, 0:1, pl.ds(first, lanes)]
            came = [self.came_at(i, k, s) for s in range(1, self.orders[i][k]["size"])]
            out.append((row, lane, lanes, came, self.local(i, self.regions[i][k + 1])[0], extra))

        def body(j, _):
            for row, lane, lanes, came, home, extra in out:
                here = pl.ds(aligned(row + j * size, 16), size)
                total = self.block[here, pl.ds(lane, lanes)].astype(F32)
                for at, _, at_lane, _ in came:
                    there = pl.ds(aligned(at + j * size, 16), size)
                    total = total + self.space[there, pl.ds(at_lane, lanes)].astype(F32)
                if last:
                    column = self.env["column"][self.layer, here, :].astype(F32)
                    total = total + wide(column, lanes // 128) * extra
                    to = pl.ds(aligned(home + j * size, 16), size)
                    self.space[to, pl.ds(lane, lanes)] = total.astype(BF16)
                else:
                    self.block[here, pl.ds(lane, lanes)] = total.astype(BF16)
            return 0

        lax.fori_loop(0, rows // size, body, 0)

    def local(self, i, region):
        row, rows, lane, lanes = region
        return row - self.regions[i][1][0], rows, lane, lanes

    def gather(self, k):
        self.wait()
        if k == self.depth - 1:
            self.add(k, last=True)

        def ref(i, region):
            row, rows, lane, lanes = self.local(i, region)
            return self.space.at[pl.ds(aligned(row, 16), rows), pl.ds(aligned(lane, 128), lanes)]

        for i, order in enumerate(self.orders):
            axis = order[k]
            mine = ref(i, self.regions[i][k + 1])
            for s in range(1, axis["size"]):
                to = lax.rem(axis["index"] + s, axis["size"])
                frm = lax.rem(axis["index"] + axis["size"] - s, axis["size"])
                slot = self.take(i)
                made = self.remote(i, mine, mine, slot, axis["at"](to))
                made.start()
                theirs = ref(i, self.share(self.regions[i][k], axis, frm))
                self.waits.append((made, self.remote(i, theirs, theirs, slot, axis["at"](frm))))
                self.sent.append((axis["link"], self.regions[i][k + 1][1] * self.regions[i][k + 1][3] * 2))

    def result(self, i, index, section):
        rows = self.regions[i][1][1]
        lane = aligned(self.lane_of(section) + i * PART, PART)
        return self.env["o"].at[section, pl.ds(aligned(index * rows, 16), rows), pl.ds(lane, PART)]

    def gathered(self, i):
        return self.space.at[pl.ds(0, self.regions[i][1][1]), pl.ds(i * PART, PART)]

    def deliver(self, i, s, straight):
        axis, section = self.orders[i][0], self.env["section"]
        recv = None if straight else self.env["ar_other"].at[self.layer, self.index, i, s]
        where = dict(axis["at"](lax.rem(axis["index"] + s, axis["size"])), section=self.layer)
        target = self.result(i, axis["index"], section)
        return self.remote(i, self.gathered(i), target, self.slot[i] + s, where, recv)

    def arrival(self, i, s, straight):
        axis, section = self.orders[i][0], self.env["section"]
        recv = None if straight else self.env["ar_other"].at[self.layer, self.index, i, s]
        index = lax.rem(axis["index"] + axis["size"] - s, axis["size"])
        frm = section if straight else 1 - section
        where = dict(axis["at"](index), section=frm)
        return self.remote(i, self.gathered(i), self.result(i, index, frm), self.slot[i] + s, where, recv)

    def kept(self, i):
        sem = self.env["ar_recv"].at[self.layer, self.index, i, self.slot[i]]
        target = self.result(i, self.orders[i][0]["index"], self.env["section"])
        return pltpu.make_async_copy(self.gathered(i), target, sem)

    def give(self):
        self.wait()

        @pl.when(self.env["section"] == self.layer)
        def _():
            for i in range(2):
                for s in range(1, self.orders[i][0]["size"]):
                    self.deliver(i, s, True).start()
                self.kept(i).start()

        @pl.when(self.env["section"] != self.layer)
        def _():
            for i in range(2):
                for s in range(self.orders[i][0]["size"] - 1, -1, -1):
                    self.deliver(i, s, False).start()

        for i, order in enumerate(self.orders):
            self.sent.append((order[0]["link"], self.regions[i][1][1] * PART * 2 * (order[0]["size"] - 1)))

    def finish(self):
        @pl.when(self.env["section"] == self.layer)
        def _():
            for i in range(2):
                size = self.orders[i][0]["size"]
                self.kept(i).wait()
                for s in range(1, size):
                    self.deliver(i, s, True).wait_send()
                    self.arrival(i, s, True).wait_recv()
                for s in range(size):
                    self.arrival(i, s, False).wait_recv()

        @pl.when(self.env["section"] != self.layer)
        def _():
            for i in range(2):
                for s in range(self.orders[i][0]["size"]):
                    self.deliver(i, s, False).wait_send()


class Order:
    RATE, HOP, QUEUE = 90e3, 1.5, 1e9

    def __init__(self):
        self.now = 0.0
        self.free = {}
        self.going = []
        self.held = []

    def sent(self, copies):
        end = self.now
        for link, size in copies:
            self.free[link] = max(self.now, self.free.get(link, 0.0)) + size / self.RATE
            end = max(end, self.free[link])
        return end + self.HOP

    def begin(self, one, i):
        self.held.append((one, i))
        self.release()

    def release(self, always=False):
        while self.held and (always or self.busy() < self.QUEUE):
            one, i = self.held.pop(0)
            end = self.sent(one.start_part(i))
            if i == 0:
                one.due = end
            else:
                one.due = max(one.due, end)
                self.going.append(one)

    def busy(self):
        link = self.held[0][0].orders[self.held[0][1]][:1]
        return max([self.free.get(a["link"], 0.0) - self.now for a in link], default=0.0)

    def advance(self, one):
        self.now = max(self.now, one.due) + 0.4
        one.due = self.sent(one.advance())
        if one.done:
            self.going.remove(one)

    def work(self, cost):
        self.now += cost
        while True:
            self.release()
            due = [x for x in self.going if x.due <= self.now and x.free_to_go]
            if not due:
                return
            self.advance(min(due, key=lambda x: x.due))

    def drain(self):
        while self.going or self.held:
            self.release(always=not self.going)
            self.advance(min(self.going, key=lambda x: x.due))


def kernel(dims, steps, seqs, views, frames, grad_out, weights, gains, shifts, recurs, lengths, masks, o, gf, vectors, f_own, f_far, p_own, p_far, g3, wc, wr1, src_t, live, turn,
           staged, heads, tails, v, vecs, rows, hid, coef, tot, vtot, levels, column, counts, cnt_p, cnt_z, slim_p, slim_z,
           wide_p, wide_z, space, sems, v_sems, stage_sem, credit, pl_send, pl_recv, z_send, z_recv, ar_send, ar_recv,
           ar_other):
    nz, ny, nx = dims
    np_ = ny * nx
    span = steps * seqs
    total_rows = 2 * span
    sent_rows = total_rows + 16
    pairs = steps // 2
    section = lax.axis_index("section")
    other = 1 - section
    b = lax.axis_index("batch")
    mp = lax.rem(b, np_)
    mz = b // np_

    def at_plane(i):
        return {"batch": b - mp + i}

    def at_z(i):
        return {"batch": b + (i - mz) * np_}

    def axis_of(link, size, stride):
        index = lax.rem(b // stride, size)
        return dict(link=link, size=size, index=index, at=lambda i: {"batch": b + (i - index) * stride})

    def halvings(link, size, stride):
        out = []
        while size > 1:
            out.append(axis_of(link, 2, stride))
            size //= 2
            stride *= 2
        return out

    xs, ys, zs = halvings("x", nx, 1), halvings("y", ny, nx), halvings("z", nz, np_)
    orders = (xs + ys + zs, ys + xs + zs)
    sibling = {"section": other}

    def local(src, dst, slot):
        return pltpu.make_async_copy(src, dst, sems.at[0, slot])

    def across(src, dst, slot):
        return pltpu.make_async_remote_copy(
            src_ref=src, dst_ref=dst, send_sem=sems.at[1, slot], recv_sem=sems.at[2, slot],
            device_id=sibling, device_id_type=MESH,
        )

    half = frames.shape[3]
    width = 2 * half
    lead = W - half
    rest = width - W
    full = rest // 128 * 128

    def fetch(source, m):
        return pltpu.make_async_copy(source.at[m], staged.at[m], stage_sem.at[m])

    def by_units(source, target, m):
        fetch(source, m).wait()

        @pl.when(section == 0)
        def _():
            pad = jnp.zeros((2 * seqs, lead), F32)

            def place(i, _):
                x = staged[m, pl.ds(2 * i, 2)].astype(F32).reshape(2 * seqs, half)
                to = pl.ds(aligned(m * span + 2 * i * seqs, 16), 2 * seqs)
                target[to, :] = jnp.concatenate([x, pad], axis=1).astype(BF16)
                return 0

            repeat(pairs, place, 0, 3)

        @pl.when(section == 1)
        def _():
            pad = jnp.zeros((2 * seqs, 2 * lead), F32)

            def place(i, _):
                x = staged[m, pl.ds(2 * i, 2)].astype(F32).reshape(2 * seqs, half)
                to = pl.ds(aligned(m * span + 2 * i * seqs, 16), 2 * seqs)
                target[to, :] = jnp.concatenate([x[:, lead:], pad], axis=1).astype(BF16)
                return 0

            repeat(pairs, place, 0, 3)

    def patch_heads(target, m):
        @pl.when(section == 0)
        def _():
            lane = lax.broadcasted_iota(jnp.int32, (2 * seqs, 128), 1)

            def place(i, _):
                to = pl.ds(aligned(m * span + 2 * i * seqs, 16), 2 * seqs)
                head = heads[m, pl.ds(2 * i, 2)].astype(F32).reshape(2 * seqs, 128)
                head = pltpu.roll(head, 128 - lead, 1)
                old = target[to, W - 128 :].astype(F32)
                target[to, W - 128 :] = jnp.where(lane < 128 - lead, old, head).astype(BF16)
                return 0

            repeat(pairs, place, 0, 3)

    def pieces(row, count, u, block, spot):
        r = pl.ds(row, count)
        to = pl.ds(0, count)
        if u == 0:
            return [(weights.at[0, r, pl.ds(0, W)], block.at[to, :])]
        return [
            (weights.at[0, r, pl.ds(W, full)], block.at[to, pl.ds(0, full)]),
            (weights.at[0, r, pl.ds(W + full, rest - full)], tails.at[spot, to, :]),
        ]

    rows_of = {0: (0, W), 1: (W, rest)}

    def w_plan(layer):
        mine, far = rows_of[layer], rows_of[1 - layer]
        plan = [
            (mine, layer, far, 1 - layer, wc.at[layer, 0], 2 * layer),
            (far, layer, mine, 1 - layer, wc.at[layer, 1], 2 * layer + 1),
        ]
        if layer == 1:
            plan.append((mine, 0, far, 1, wr1, 4))
        return plan

    late_row = (width - half) // 16 * 16
    late_shift = half - late_row
    late_plan = [
        ((0, W), 0, (late_row, width - late_row), 1, wc.at[0, 0], 0),
        ((0, W), 1, (late_row, width - late_row), 0, wc.at[0, 1], 1),
    ]
    slot_of = {0: 4, 1: 8, 2: 14}

    def local_w(plan, base, which):
        r, u, _, _, block, spot = plan[which]
        return [local(a, t, base + 2 * which + i) for i, (a, t) in enumerate(pieces(*r, u, block, spot))]

    def across_w(plan, base, which):
        _, _, r, u, block, spot = plan[which]
        return [across(a, t, base + 2 * which + i) for i, (a, t) in enumerate(pieces(*r, u, block, spot))]

    def start_local_w(layer, plan, base):
        @pl.when(section == layer)
        def _():
            for which in range(len(plan)):
                for made in local_w(plan, base, which):
                    made.start()

    def start_across_w(layer, plan, base):
        @pl.when(section == layer)
        def _():
            for which in range(len(plan)):
                for made in across_w(plan, base, which):
                    made.start()

    def last_units(block, spot):
        def body(i, _):
            r = pl.ds(aligned(i * 128, 128), 128)
            x = tails[spot, r, :].astype(F32)
            x = jnp.concatenate([x, jnp.zeros((128, 128 - x.shape[1]), F32)], axis=1)
            block[r, full:] = x.astype(BF16)
            return 0

        lax.fori_loop(0, W // 128, body, 0)

    def wait_w(layer, plan, base, which):
        _, own_u, _, far_u, block, spot = plan[which]

        @pl.when(section == layer)
        def _():
            for made in local_w(plan, base, which):
                made.wait()
            if own_u == 1:
                last_units(block, spot)

        @pl.when(section != layer)
        def _():
            for made in across_w(plan, base, which):
                made.wait_recv()
            if far_u == 1:
                last_units(block, spot)

    def done_w(layer, plan, base):
        @pl.when(section == layer)
        def _():
            for which in range(len(plan)):
                for made in across_w(plan, base, which):
                    made.wait_send()

    def heads_copy(source, slot):
        return across(source.at[:, :, :, pl.ds(0, 128)], heads, slot)

    def wait_heads(source, slot):
        @pl.when(section == 0)
        def _():
            heads_copy(source, slot).wait_recv()

        @pl.when(section == 1)
        def _():
            heads_copy(source, slot).wait_send()

    fetch(frames, 0).start()
    fetch(frames, 1).start()
    for layer in range(2):
        start_local_w(layer, w_plan(layer), slot_of[layer])

    barrier = pltpu.get_barrier_semaphore()
    greeted = [dict(sibling)]
    greeted += [at_plane(lax.rem(mp + k, np_)) for k in range(1, np_)]
    greeted += [at_z(lax.rem(mz + k, nz)) for k in range(1, nz)]
    for axis in (xs + zs)[:1] + (ys + zs)[:1]:
        for s in range(1, axis["size"]):
            greeted.append(dict(axis["at"](lax.rem(axis["index"] + s, axis["size"])), section=other))
    for where in greeted:
        pl.semaphore_signal(barrier, inc=1, device_id=where, device_id_type=MESH)

    for k, (x, fill) in enumerate(((gains, 0.0), (shifts, -1e30), (recurs, 0.0))):
        vecs[section, k : k + 1, 0:width] = x[...]
        vecs[section, k : k + 1, width:] = jnp.full((1, 2 * W - width), fill, F32)
    vecs[section, 3:8, :] = jnp.zeros((5, 2 * W), F32)

    gap = jnp.zeros((W - rest, W), BF16)

    @pl.when(section == 0)
    def _():
        wc[0, 1, rest:, :] = gap
        wc[1, 1, rest:, :] = gap

    @pl.when(section == 1)
    def _():
        wc[0, 0, rest:, :] = gap
        wc[1, 0, rest:, :] = gap
        wr1[rest:, :] = gap

    for spot in (0, 2):
        tails[spot, rest:, :] = jnp.zeros((W - rest, rest - full), BF16)
    for spare in (f_own, p_own, g3.at[0], g3.at[1]):
        spare[sent_rows:, :] = jnp.zeros((spare.shape[0] - sent_rows, W), BF16)

    pl.semaphore_wait(barrier, len(greeted))

    @pl.when(section == 1)
    def _():
        heads_copy(frames, 1).start()

    start_across_w(0, w_plan(0), slot_of[0])
    send_vec = across(vecs.at[section], vecs.at[section], 3)
    send_vec.start()

    def stage_copy(where, rnd, slot, k, back):
        buf, parity, size, me, at, send, recv = where
        there = at(lax.rem(me + (size - k if back else k), size))
        ref = buf.at[parity, slot]
        return pltpu.make_async_remote_copy(
            src_ref=ref, dst_ref=ref, send_sem=send.at[rnd, k], recv_sem=recv.at[rnd, k],
            device_id=there, device_id_type=MESH,
        )

    def in_plane(buf, parity):
        return (buf, parity, np_, mp, at_plane, pl_send, pl_recv)

    def in_line(buf, parity):
        return (buf, parity, nz, mz, at_z, z_send, z_recv)

    def stage_start(where, rnd, value):
        buf, parity, size, me = where[:4]
        buf[parity, me] = value
        for k in range(1, size):
            stage_copy(where, rnd, me, k, False).start()

    def stage_wait(where, rnd):
        size, me = where[2:4]
        for k in range(1, size):
            stage_copy(where, rnd, me, k, False).wait_send()
            stage_copy(where, rnd, lax.rem(me + size - k, size), k, True).wait_recv()

    def add_slots(where):
        buf, parity, size = where[:3]
        total = buf[parity, 0]
        for k in range(1, size):
            total = total + buf[parity, k]
        return total

    groups = lengths.shape[1]
    s_at = lax.broadcasted_iota(jnp.int32, (seqs, groups), 0)
    g_at = lax.broadcasted_iota(jnp.int32, (seqs, groups), 1) * views
    there = (s_at >= g_at) & (s_at < g_at + views)
    position = lax.broadcasted_iota(jnp.int32, (seqs, 128), 1)
    local_counts = []
    for m in range(2):
        turn[...] = jnp.zeros_like(turn)
        turn[0:steps, 0:seqs] = masks[m].astype(F32)
        mask = turn[...].T[0:seqs]
        length = jnp.broadcast_to(lengths[m : m + 1, :], (seqs, groups)).astype(F32)
        limit = jnp.sum(jnp.where(there, length, 0.0), axis=1, keepdims=True)
        alive = (position.astype(F32) < limit) & ((mask > 0.0) | (position == 0))
        alive = jnp.where(position < steps, alive.astype(F32), 0.0)
        total = jnp.zeros((seqs, 128), F32)
        for t in range(steps):
            at = m * span + t * seqs
            cells = jnp.broadcast_to(alive[:, t : t + 1], (seqs, 128))
            live[at : at + seqs, :] = cells
            total = total + cells
        local_counts.append(jnp.sum(total, axis=0, keepdims=True))
    n_own = jnp.concatenate([local_counts[0]] * 2 + [local_counts[1]] * 2, axis=0)
    n_own = jnp.concatenate([n_own, n_own], axis=0)

    cnt_plane, cnt_line = in_plane(cnt_p, 0), in_line(cnt_z, 0)
    stage_start(cnt_plane, 0, n_own)

    def vec_of(layer, k, lh):
        return vecs[layer, k : k + 1, pl.ds(aligned(section * W + lh * HALF, HALF), HALF)]

    def half_of(lh):
        return slice(lh * HALF, (lh + 1) * HALF)

    def matmul_to(out, a, w, first, lh):
        lanes = half_of(lh)

        def body(m, _):
            r = pl.ds(aligned(m * span, 16), span)
            y = dot(a[r, :], w[:, lanes], ((1,), (0,)))
            out[r, lanes] = y if first else out[r, lanes] + y
            return 0

        lax.fori_loop(0, 2, body, 0)

    def packed(x, y):
        return jnp.concatenate([z[:, k * QUART : (k + 1) * QUART] for z in (*x, *y) for k in range(2)], axis=0)

    def unpacked(x, m):
        return jnp.concatenate([x[2 * m + k : 2 * m + k + 1] for k in range(2)], axis=1)

    def merge_slots(where, counts_of):
        buf, parity, size = where[:3]
        s = [buf[parity, k, 0:4, :] for k in range(size)]
        q = [buf[parity, k, 4:8, :] for k in range(size)]
        n = [wide(counts_of(k), 2) for k in range(size)]
        total, squares, count = sum(s[1:], s[0]), sum(q[1:], q[0]), sum(n[1:], n[0])
        mean = total / count
        for k in range(size):
            d = s[k] / n[k] - mean
            squares = squares + n[k] * d * d
        return jnp.concatenate([total, squares], axis=0)

    def slim_round(which, lh):
        return 1 + 2 * which + lh, in_plane(slim_p, 2 * lh + which % 2), in_line(slim_z, 2 * lh + which % 2)

    def forward_stats(layer, lh):
        lanes = half_of(lh)
        sums, squares = [], []
        for m in range(2):
            start = jnp.sum(rows[layer, m * span : m * span + seqs, lanes], axis=0, keepdims=True) * (1.0 / seqs)

            def body(i, carry):
                s, q = carry
                r = pl.ds(aligned(m * span + i * (2 * seqs), 16), 2 * seqs)
                d = rows[layer, r, lanes] - start
                kept = wide(live[r, :], 4) * d
                return s + fold(kept), q + fold(kept * d)

            zero = jnp.zeros((8, HALF), F32)
            s, q = repeat(pairs, body, (zero, zero), 4)
            s, q = jnp.sum(s, axis=0, keepdims=True), jnp.sum(q, axis=0, keepdims=True)
            n = wide(local_counts[m], 4)
            sums.append(s + n * start)
            squares.append(jnp.maximum(q - s * s / n, 0.0))
        rnd, plane, _ = slim_round(layer, lh)
        stage_start(plane, rnd, packed(sums, squares))

    def forward_middle(layer, lh):
        rnd, plane, line = slim_round(layer, lh)
        stage_wait(plane, rnd)
        stage_start(line, rnd, merge_slots(plane, lambda k: cnt_p[0, k, 0:4, :]))

    def forward_end(layer, lh):
        rnd, _, line = slim_round(layer, lh)
        lanes = half_of(lh)
        stage_wait(line, rnd)
        value = merge_slots(line, lambda k: cnt_z[0, k, 0:4, :])
        for m in range(2):
            count = wide(counts[2 * m : 2 * m + 1, :], 4)
            mean = unpacked(value[0:4], m) / count
            scale = lax.rsqrt(unpacked(value[4:8], m) / count + EPS)
            coef[layer, 2 * m : 2 * m + 1, lanes] = mean
            coef[layer, 2 * m + 1 : 2 * m + 2, lanes] = scale
            slope = vec_of(layer, 0, lh) * scale
            coef[layer, 4 + 2 * m : 5 + 2 * m, lanes] = slope
            coef[layer, 5 + 2 * m : 6 + 2 * m, lanes] = vec_of(layer, 1, lh) - mean * slope

    def forward_scan(layer, lh, passes):
        lanes = half_of(lh)
        rec = vec_of(layer, 2, lh)
        slope = [coef[layer, 4 + 2 * m : 5 + 2 * m, lanes] for m in range(2)]
        shift = [coef[layer, 5 + 2 * m : 6 + 2 * m, lanes] for m in range(2)]

        def body(i, carry):
            states, level = carry
            out = []
            for m in range(2):
                r = pl.ds(aligned(m * span + i * (2 * seqs), 16), 2 * seqs)
                x = rows[layer, r, lanes] * slope[m] + shift[m]
                lv = wide(live[r, :], 4)
                alive = lv > 0.0
                h = states[m]
                both = []
                for k in range(2):
                    part = slice(k * seqs, (k + 1) * seqs)
                    z = x[part] + rec * h
                    soft = jnp.maximum(z, 0.0) + jnp.log(1.0 + jnp.exp(-jnp.abs(z)))
                    h = jnp.where(alive[part], soft, h)
                    both.append(h)
                two = jnp.concatenate(both, axis=0)
                hid[layer, r, lanes] = two
                if passes:
                    p_own[r, lanes] = two.astype(BF16)
                    level = level + fold(lv * two)
                out.append(h)
            return tuple(out), level

        zero = jnp.zeros((seqs, HALF), F32)
        _, level = repeat(pairs, body, ((zero, zero), jnp.zeros((8, HALF), F32)), 2)
        if not passes:
            return None
        levels[1:2, lanes] = jnp.sum(level, axis=0, keepdims=True)
        made = across(p_own.at[pl.ds(0, total_rows), lanes], p_far.at[:, lanes], 18 + lh)
        made.start()
        return made

    def backward_scan(layer, lh, above, between=lambda: None):
        for lq in range(2 * lh, 2 * lh + 2):
            lanes = slice(lq * QUART, (lq + 1) * QUART)
            gq, sq, rec = (vec_of(layer, k, lh)[:, (lq % 2) * QUART : (lq % 2 + 1) * QUART] for k in range(3))
            mean = [coef[layer, 2 * m : 2 * m + 1, lanes] for m in range(2)]
            scale = [coef[layer, 2 * m + 1 : 2 * m + 2, lanes] for m in range(2)]

            def body(i, carry):
                down, s1, s2, rsum, sqh, sqa = carry
                down, s1, s2 = list(down), list(s1), list(s2)
                i = pairs - 1 - i
                for m in range(2):
                    start = m * span + i * (2 * seqs)
                    r = pl.ds(aligned(start, 16), 2 * seqs)
                    before = pl.ds(aligned(jnp.maximum(start - seqs, 0), 8), seqs)
                    normed = (rows[layer, r, lanes] - mean[m]) * scale[m]
                    drive = gq * normed + sq
                    h2 = hid[layer, r, lanes]
                    hb = jnp.where(i > 0, hid[layer, before, lanes], 0.0)
                    lv = wide(live[r, :], 2)
                    up = above[r, lanes].astype(F32)
                    res = f_own[r, lanes].astype(F32)
                    aux = res + h2 if layer == 1 else res
                    sqh = sqh + fold(lv * (h2 * h2))
                    sqa = sqa + fold(lv * (aux * aux))
                    grads = [None, None]
                    for k in (1, 0):
                        part = slice(k * seqs, (k + 1) * seqs)
                        prior = h2[0:seqs] if k == 1 else hb
                        slope = 0.5 + 0.5 * jnp.tanh(0.5 * (drive[part] + rec * prior))
                        total = up[part] + down[m]
                        gd = lv[part] * slope * total
                        down[m] = (1.0 - lv[part]) * total + rec * gd
                        grads[k] = gd
                        rsum = rsum + fold(gd * prior)
                    gd2 = jnp.concatenate(grads, axis=0)
                    hid[layer, r, lanes] = gd2
                    s1[m] = s1[m] + fold(gd2)
                    s2[m] = s2[m] + fold(gd2 * normed)
                return tuple(down), tuple(s1), tuple(s2), rsum, sqh, sqa

            zero = jnp.zeros((seqs, QUART), F32)
            z8 = jnp.zeros((8, QUART), F32)
            _, s1, s2, rsum, sqh, sqa = repeat(
                pairs, body, ((zero, zero), (z8, z8), (z8, z8), z8, z8, z8), 2
            )
            for k, x in enumerate((s1[0], s1[1], s2[0], s2[1], rsum, sqh, sqa)):
                tot[layer, k : k + 1, lanes] = jnp.sum(x, axis=0, keepdims=True)
            between()

    def backward_stats(layer, lh):
        rnd, plane, _ = slim_round(3 - layer, lh)
        t = tot[layer, 0:4, half_of(lh)]
        stage_start(plane, rnd, packed([t[0:1], t[1:2]], [t[2:3], t[3:4]]))

    def backward_middle(layer, lh):
        rnd, plane, line = slim_round(3 - layer, lh)
        stage_wait(plane, rnd)
        stage_start(line, rnd, add_slots(plane))

    def backward_end(layer, lh):
        rnd, _, line = slim_round(3 - layer, lh)
        stage_wait(line, rnd)
        value = add_slots(line)
        for m in range(2):
            tot[layer, m : m + 1, half_of(lh)] = unpacked(value[0:4], m)
            tot[layer, 2 + m : 3 + m, half_of(lh)] = unpacked(value[4:8], m)

    def grad_rows(layer, lh, slot):
        lanes = half_of(lh)
        acc = jnp.zeros((8, HALF), F32)
        for m in range(2):
            mean = coef[layer, 2 * m : 2 * m + 1, lanes]
            scale = coef[layer, 2 * m + 1 : 2 * m + 2, lanes]
            count = wide(counts[2 * m : 2 * m + 1, :], 4)
            first = tot[layer, m : m + 1, lanes] / count
            second = tot[layer, 2 + m : 3 + m, lanes] / count * scale
            k = coef[layer, 4 + 2 * m : 5 + 2 * m, lanes]

            def body(i, acc):
                r = pl.ds(aligned(m * span + i * (2 * seqs), 16), 2 * seqs)
                y = hid[layer, r, lanes] - first - (rows[layer, r, lanes] - mean) * second
                y = wide(live[r, :], 4) * (k * y)
                g3[0, r, lanes] = y.astype(BF16)
                return acc + fold(y)

            acc = repeat(pairs, body, acc, 4)
        top = lax.broadcasted_iota(jnp.int32, (16, HALF), 0) == 0
        minus = jnp.where(top, -jnp.sum(acc, axis=0, keepdims=True), 0.0)
        g3[0, total_rows:sent_rows, lanes] = minus.astype(BF16)
        made = across(g3.at[0, pl.ds(0, sent_rows), lanes], g3.at[1, pl.ds(0, sent_rows), lanes], slot + lh)
        made.start()
        return made

    sums_round = {1: (1, 10), 0: (0, 11)}

    def sums_start(layer):
        parity, rnd = sums_round[layer]
        own_sum = -g3[0, total_rows:sent_rows, :].astype(F32)[0:1]
        value = jnp.concatenate([own_sum, tot[layer, 4:7, :], jnp.zeros((4, W), F32)], axis=0)
        stage_start(in_plane(wide_p, parity), rnd, value)

    def sums_middle(layer):
        parity, rnd = sums_round[layer]
        stage_wait(in_plane(wide_p, parity), rnd)
        stage_start(in_line(wide_z, parity), rnd, add_slots(in_plane(wide_p, parity)))

    def swap_sums(layer):
        return across(vtot.at[layer, 0], vtot.at[layer, 1], 25 + layer)

    def sums_end(layer):
        parity, rnd = sums_round[layer]
        stage_wait(in_line(wide_z, parity), rnd)
        vtot[layer, 0] = add_slots(in_line(wide_z, parity))
        swap_sums(layer).start()
        tot[layer, 4:7, :] = vtot[layer, 0, 1:4, :]
        tot[layer, 7:8, :] = wide(counts[0:1, :] + counts[2:3, :], 8)

        @pl.when(section == layer)
        def _():
            pltpu.make_async_copy(tot.at[layer], v.at[section], v_sems.at[0]).start()

        @pl.when(section != layer)
        def _():
            v_across(layer).start()

    def sums_there(layer):
        swap_sums(layer).wait()
        env["summed"].add(layer)

    def v_across(layer):
        return pltpu.make_async_remote_copy(
            src_ref=tot.at[layer], dst_ref=v.at[section], send_sem=v_sems.at[1], recv_sem=v_sems.at[2],
            device_id=sibling, device_id_type=MESH,
        )

    def transpose(src, begin=0, end=W // 128):
        def body(j, _):
            c = pl.ds(aligned(j * 128, 128), 128)
            src_t[c, 0:total_rows] = src[0:total_rows, c].T
            return 0

        lax.fori_loop(begin, end, body, 0)

    def transpose_level(src, layer):
        top = lax.broadcasted_iota(jnp.int32, (16, W), 0) == 0
        src[total_rows:sent_rows, :] = jnp.where(top, levels[2 + layer : 3 + layer, :], 0.0).astype(BF16)

        def body(j, _):
            c = pl.ds(aligned(j * 128, 128), 128)
            src_t[c, total_rows:] = src[total_rows:, c].T
            level = src[total_rows:sent_rows, c].astype(F32)[0:1]
            column[layer, c, :] = jnp.broadcast_to(level, (128, 128)).T.astype(BF16)
            return 0

        lax.fori_loop(0, W // 128, body, 0)

    def weight_part(block, grads, c):
        lanes = pl.ds(c * HALF, HALF)

        def body(j, _):
            r = pl.ds(aligned(j * HALF, HALF), HALF)
            block[r, lanes] = dot(src_t[r, :], grads[:, lanes], ((1,), (0,))).astype(BF16)
            return 0

        lax.fori_loop(0, W // HALF, body, 0)

    def source_grad(store, w_own, w_far, half_index):
        c = half_of(half_index)

        def body(m, _):
            r = pl.ds(aligned(m * span, 16), span)
            y = dot(g3[0, r, :], w_own[c, :], ((1,), (1,))) + dot(g3[1, r, :], w_far[c, :], ((1,), (1,)))
            store(r, c, y)
            return 0

        lax.fori_loop(0, 2, body, 0)

    env = dict(summed=set(), vtot=vtot, column=column, space=space, ar_send=ar_send, ar_recv=ar_recv,
               ar_other=ar_other, o=o, section=section, here={"batch": b})
    blocks = {
        (1, 0): f_far.at[pl.ds(0, W), :],
        (1, 1): p_far.at[pl.ds(0, W), :],
        (0, 0): wc.at[1, 1],
        (0, 1): wr1,
    }
    parts = {}
    for layer in (1, 0):
        for index in range(2 * PAIRS):
            part, side = index // PAIRS, index % PAIRS

            def lane_of(sec, part=part, side=side):
                return (sec if part == 0 else 1 - sec) * W + side * 2 * PART

            block = blocks[layer, part].at[:, pl.ds(side * 2 * PART, 2 * PART)]
            parts[layer, index] = Reduction(env, layer, index, block, orders, lane_of)
    order = Order()

    def weight_grads(layer, part, c):
        weight_part(blocks[layer, part], g3.at[part], c)
        order.work(2.0)
        for k in range(c * HALF // PART, (c + 1) * HALF // PART):
            order.begin(parts[layer, part * PAIRS + k // 2], k % 2)

    def arrived(sends):
        for made in sends:
            made.wait()

    send_f = []
    for m in range(2):
        by_units(frames, f_own, m)
        fetch(grad_out, m).start()
        if m == 0:
            wait_heads(frames, 1)
        patch_heads(f_own, m)
        here = pl.ds(m * span, span)
        made = across(f_own.at[here, :], f_far.at[here, :], (0, 24)[m])
        made.start()
        send_f.append(made)
    start_across_w(1, w_plan(1), slot_of[1])
    stage_wait(cnt_plane, 0)
    stage_start(cnt_line, 0, add_slots(cnt_plane))
    wait_w(0, w_plan(0), slot_of[0], 0)
    matmul_to(rows.at[0], f_own, wc.at[0, 0], True, 0)
    matmul_to(rows.at[0], f_own, wc.at[0, 0], True, 1)
    wait_w(0, w_plan(0), slot_of[0], 1)
    for made in send_f:
        made.wait()

    @pl.when(section == 1)
    def _():
        heads_copy(grad_out, 2).start()

    matmul_to(rows.at[0], f_far, wc.at[0, 1], False, 0)
    forward_stats(0, 0)
    matmul_to(rows.at[0], f_far, wc.at[0, 1], False, 1)
    forward_middle(0, 0)
    forward_stats(0, 1)
    send_vec.wait_send()
    across(vecs.at[other], vecs.at[other], 3).wait_recv()
    by_units(grad_out, g3.at[1], 0)
    wait_heads(grad_out, 2)
    patch_heads(g3.at[1], 0)
    stage_wait(cnt_line, 0)
    counts[...] = add_slots(cnt_line)
    forward_end(0, 0)
    forward_middle(0, 1)
    sends = [forward_scan(0, 0, True)]
    forward_end(0, 1)
    sends.append(forward_scan(0, 1, True))
    wait_w(1, w_plan(1), slot_of[1], 0)
    matmul_to(rows.at[1], p_own, wc.at[1, 0], True, 0)
    matmul_to(rows.at[1], p_own, wc.at[1, 0], True, 1)
    wait_w(1, w_plan(1), slot_of[1], 1)
    for made in sends:
        made.wait()
    matmul_to(rows.at[1], p_far, wc.at[1, 1], False, 0)
    forward_stats(1, 0)
    done_w(0, w_plan(0), slot_of[0])

    start_local_w(0, late_plan, slot_of[2])
    start_across_w(0, late_plan, slot_of[2])

    @pl.when(section == 1)
    def _():
        wc[0, 1, width - late_row :, :] = jnp.zeros((W - width + late_row, W), BF16)

    def source_level():
        def body(i, acc):
            r = pl.ds(aligned(i * (2 * seqs), 16), 2 * seqs)
            return acc + fold(wide(live[r, :], 8) * f_own[r, :].astype(F32))

        acc = repeat(2 * pairs, body, jnp.zeros((8, W), F32), 3)
        levels[0:1, :] = jnp.sum(acc, axis=0, keepdims=True)

    matmul_to(rows.at[1], p_far, wc.at[1, 1], False, 1)
    forward_middle(1, 0)
    forward_stats(1, 1)
    by_units(grad_out, g3.at[1], 1)
    patch_heads(g3.at[1], 1)
    forward_end(1, 0)
    forward_middle(1, 1)
    forward_scan(1, 0, False)
    backward_scan(1, 0, g3.at[1])
    backward_stats(1, 0)
    forward_end(1, 1)
    source_level()
    level_plane, level_line = in_plane(wide_p, 0), in_line(wide_z, 0)
    stage_start(level_plane, 9, jnp.concatenate([levels[0:2, :], jnp.zeros((6, W), F32)], axis=0))
    forward_scan(1, 1, False)
    backward_middle(1, 0)
    stage_wait(level_plane, 9)
    stage_start(level_line, 9, add_slots(level_plane))
    backward_scan(1, 1, g3.at[1])
    backward_stats(1, 1)
    pl.semaphore_signal(credit.at[0], inc=1, device_id=sibling, device_id_type=MESH)
    backward_end(1, 0)
    pl.semaphore_wait(credit.at[0], 1)
    sends = [grad_rows(1, 0, 20)]
    transpose(p_own, 0, W // 256)
    backward_middle(1, 1)
    transpose(p_own, W // 256)
    stage_wait(level_line, 9)
    levels[2:4, :] = (add_slots(level_line) / wide(counts[0:1, :] + counts[2:3, :], 8))[0:2]
    transpose_level(p_own, 1)
    backward_end(1, 1)
    sends.append(grad_rows(1, 1, 20))
    sums_start(1)
    weight_grads(1, 0, 0)
    sums_middle(1)
    weight_grads(1, 0, 1)
    sums_end(1)
    arrived(sends)
    weight_grads(1, 1, 0)
    weight_grads(1, 1, 1)
    sums_there(1)
    wait_w(1, w_plan(1), slot_of[1], 2)
    done_w(1, w_plan(1), slot_of[1])

    def keep_down(r, c, y):
        p_own[r, c] = y.astype(BF16)

    source_grad(keep_down, wc.at[1, 0], wr1, 0)
    order.work(2.5)
    backward_scan(0, 0, p_own, lambda: order.work(1.3))
    backward_stats(0, 0)
    source_grad(keep_down, wc.at[1, 0], wr1, 1)
    pl.semaphore_signal(credit.at[1], inc=1, device_id=sibling, device_id_type=MESH)
    order.work(2.5)
    backward_middle(0, 0)
    backward_scan(0, 1, p_own, lambda: order.work(1.3))
    backward_stats(0, 1)
    backward_end(0, 0)
    pl.semaphore_wait(credit.at[1], 1)
    sends = [grad_rows(0, 0, 22)]
    order.work(1.3)
    transpose(f_own, 0, W // 256)
    backward_middle(0, 1)
    transpose(f_own, W // 256)
    transpose_level(f_own, 0)
    order.work(4.0)
    weight_grads(0, 0, 0)
    backward_end(0, 1)
    sends.append(grad_rows(0, 1, 22))
    sums_start(0)
    order.work(1.3)
    weight_grads(0, 0, 1)
    arrived(sends)
    weight_grads(0, 1, 0)
    weight_grads(0, 1, 1)
    wait_w(0, late_plan, slot_of[2], 0)
    wait_w(0, late_plan, slot_of[2], 1)
    done_w(0, late_plan, slot_of[2])

    def keep_source(r, c, y):
        rows[0, r, c] = y

    fetch(grad_out, 0).start()
    fetch(grad_out, 1).start()
    source_grad(keep_source, wc.at[0, 0], wc.at[0, 1], 0)
    order.work(2.5)
    sums_middle(0)
    source_grad(keep_source, wc.at[0, 0], wc.at[0, 1], 1)
    order.work(2.5)
    sums_end(0)
    sums_there(0)

    def give(m):
        return pltpu.make_async_copy(staged.at[m], gf.at[m], stage_sem.at[m])

    for m in range(2):
        fetch(grad_out, m).wait()

        def finish_frames(i, _, m=m):
            straight = staged[m, pl.ds(2 * i, 2)].astype(F32).reshape(2 * seqs, half)
            y = rows[0, pl.ds(aligned(m * span + 2 * i * seqs, 8), 2 * seqs), :]
            y = jnp.where(section == 0, y[:, :half], y[:, late_shift : late_shift + half])
            staged[m, pl.ds(2 * i, 2)] = (y + straight).reshape(2, seqs, half).astype(BF16)
            return 0

        repeat(pairs, finish_frames, 0, 3)
        give(m).start()
        order.work(2.0)
    order.drain()
    for m in range(2):
        give(m).wait()

    for layer in range(2):

        @pl.when(section == layer)
        def _(layer=layer):
            pltpu.make_async_copy(tot.at[layer], v.at[section], v_sems.at[0]).wait()
            pltpu.make_async_remote_copy(
                src_ref=tot.at[layer], dst_ref=v.at[other], send_sem=v_sems.at[1], recv_sem=v_sems.at[2],
                device_id=sibling, device_id_type=MESH,
            ).wait_recv()

        @pl.when(section != layer)
        def _(layer=layer):
            v_across(layer).wait_send()

    own_part, far_part = v[section], v[other]
    first = jnp.where(section == 0, own_part, far_part)
    second = jnp.where(section == 0, far_part, own_part)
    for row, terms in ((0, (2, 3)), (1, (0, 1)), (2, (4,))):
        for lane, x in ((0, first), (W, second)):
            total = x[terms[0] : terms[0] + 1, :]
            for k in terms[1:]:
                total = total + x[k : k + 1, :]
            vectors[row : row + 1, lane : lane + W] = total
    squares = jnp.sum(first[5:7, :] + second[5:7, :], axis=1, keepdims=True)
    root = jnp.sqrt(squares / (first[7:8, 0:1] * width))
    for k in range(2):
        vectors[3 + k : 4 + k, :] = jnp.broadcast_to(root[k : k + 1], (1, 2 * W))
    vectors[5:8, :] = jnp.zeros((3, 2 * W), F32)


def write_results(o, gf, vectors, grad_weight, grad_frames, grad_gains, grad_shifts, grad_recurs, table):
    width = grad_weight.shape[2]
    grad_weight[0] = o[...][:, :width].astype(F32)
    grad_frames[...] = gf[...]

    @pl.when(pl.program_id(0) == 0)
    def _():
        for k, out in enumerate((grad_gains, grad_shifts, grad_recurs)):
            out[...] = vectors[k : k + 1, 0:width]
        table[...] = jnp.concatenate([vectors[3:4, 0:1], vectors[4:5, 0:1]], axis=1)


def results(o, gf, vectors):
    micro, steps, seqs, half = gf.shape
    width = 2 * half
    count = W * 2 // 256
    frames = micro * steps // count
    whole = lambda shape: pl.BlockSpec(shape, lambda i: (0, 0))
    out = pl.pallas_call(
        write_results,
        grid=(count,),
        in_specs=[
            pl.BlockSpec((256, 2 * W), lambda i: (i, 0)),
            pl.BlockSpec((frames, seqs, half), lambda i: (i, 0, 0)),
            whole((8, 2 * W)),
        ],
        out_specs=(
            pl.BlockSpec((1, 256, width), lambda i: (0, i, 0)),
            pl.BlockSpec((frames, seqs, half), lambda i: (i, 0, 0)),
            whole((1, width)),
            whole((1, width)),
            whole((1, width)),
            whole((1, 2)),
        ),
        out_shape=(
            jax.ShapeDtypeStruct((1, width, width), F32),
            jax.ShapeDtypeStruct((micro * steps, seqs, half), BF16),
            jax.ShapeDtypeStruct((1, width), F32),
            jax.ShapeDtypeStruct((1, width), F32),
            jax.ShapeDtypeStruct((1, width), F32),
            jax.ShapeDtypeStruct((1, 2), F32),
        ),
        compiler_params=pltpu.CompilerParams(vmem_limit_bytes=64 * 1024 * 1024),
    )(o.reshape(2 * W, 2 * W), gf.reshape(micro * steps, seqs, half), vectors)
    return out[1].reshape(gf.shape), out[0], *out[2:]


def whole_step(dims, frames, grad_out, weights, gains, shifts, recurs, lengths, masks):
    nz, ny, nx = dims
    micro, steps, seqs, half = frames.shape
    width = 2 * half
    views = seqs // lengths.shape[1]
    rows = micro * steps * seqs
    np_ = ny * nx
    wide_rows = (rows + 16 + 127) // 128 * 128
    across_first = max(nx, ny, nz if np_ == 1 else 1)
    copies = 2 * (nx + ny + nz) + across_first
    came_rows = (nx - 1) * (W // nx) + (ny - 1) * (W // np_) + (nz - 1) * max(W // np_ // nz, 16)
    any_ = pl.BlockSpec(memory_space=pl.ANY)
    held = pl.BlockSpec(memory_space=pltpu.VMEM)
    dma = pltpu.SemaphoreType.DMA
    return pl.pallas_call(
        functools.partial(kernel, dims, steps, seqs, views),
        out_shape=(
            jax.ShapeDtypeStruct((2, W, 2 * W), BF16),
            jax.ShapeDtypeStruct(frames.shape, BF16),
            jax.ShapeDtypeStruct((8, 2 * W), F32),
        ),
        in_specs=[any_] * 3 + [held] * 5,
        out_specs=(any_, any_, held),
        scratch_shapes=[
            pltpu.VMEM((wide_rows, W), BF16),
            pltpu.VMEM((rows, W), BF16),
            pltpu.VMEM((wide_rows, W), BF16),
            pltpu.VMEM((rows, W), BF16),
            pltpu.VMEM((2, wide_rows, W), BF16),
            pltpu.VMEM((2, 2, W, W), BF16),
            pltpu.VMEM((W, W), BF16),
            pltpu.VMEM((W, wide_rows), BF16),
            pltpu.VMEM((rows, 128), F32),
            pltpu.VMEM((128, 128), F32),
            pltpu.VMEM(frames.shape, BF16),
            pltpu.VMEM((micro, steps, seqs, 128), BF16),
            pltpu.VMEM((5, W, (width - W) % 128), BF16),
            pltpu.VMEM((2, 8, W), F32),
            pltpu.VMEM((2, 8, 2 * W), F32),
            pltpu.VMEM((2, rows, W), F32),
            pltpu.VMEM((2, rows, W), F32),
            pltpu.VMEM((2, 8, W), F32),
            pltpu.VMEM((2, 8, W), F32),
            pltpu.VMEM((2, 2, 8, W), F32),
            pltpu.VMEM((8, W), F32),
            pltpu.VMEM((2, W, 128), BF16),
            pltpu.VMEM((8, 128), F32),
            pltpu.VMEM((1, np_, 8, 128), F32),
            pltpu.VMEM((1, nz, 8, 128), F32),
            pltpu.VMEM((4, np_, 8, QUART), F32),
            pltpu.VMEM((4, nz, 8, QUART), F32),
            pltpu.VMEM((2, np_, 8, W), F32),
            pltpu.VMEM((2, nz, 8, W), F32),
            pltpu.VMEM((2, 2 * PAIRS, max(came_rows, W), 2 * PART), BF16),
            dma((3, 27)),
            dma((3,)),
            dma((2,)),
            pltpu.SemaphoreType.REGULAR((2,)),
            dma((12, max(np_, 2))),
            dma((12, max(np_, 2))),
            dma((12, max(nz, 2))),
            dma((12, max(nz, 2))),
            dma((2, 2 * PAIRS, 2, copies)),
            dma((2, 2 * PAIRS, 2, copies)),
            dma((2, 2 * PAIRS, 2, across_first)),
        ],
        compiler_params=pltpu.CompilerParams(
            collective_id=0, has_side_effects=True, vmem_limit_bytes=64 * 1024 * 1024
        ),
    )(frames, grad_out, weights, gains, shifts, recurs, lengths, masks)


def shards(dims, frames, grad_out, weights, gains, shifts, recurs, lengths, masks):
    return results(*whole_step(dims, frames, grad_out, weights, gains, shifts, recurs, lengths, masks))


def solution(mesh):
    in_specs = (
        P(None, None, "batch", "section"),
        P(None, None, "batch", "section"),
        P("section", None, None),
        P("section", None),
        P("section", None),
        P("section", None),
        P(None, "batch"),
        P(None, None, "batch"),
    )
    out_specs = (
        P(None, None, "batch", "section"),
        P("section", None, None),
        P("section", None),
        P("section", None),
        P("section", None),
        P("section", None),
    )
    body = functools.partial(shards, grid_of(mesh.shape["batch"]))
    return jax.shard_map(body, mesh=mesh, in_specs=in_specs, out_specs=out_specs, check_vma=False)
```

```python
import functools

import jax
import jax.numpy as jnp
from jax import lax
from jax.experimental import pallas as pl
from jax.experimental.pallas import tpu as pltpu
from jax.sharding import PartitionSpec as P

EPS = 1e-05
W = 1024
HALF = W // 2
QUART = W // 4
PAIRS = 2
PART = W // PAIRS // 2
MESH = pl.DeviceIdType.MESH
F32 = jnp.float32
BF16 = jnp.bfloat16


def grid_of(size):
    if size == 16:
        return (4, 2, 2)
    if size == 128:
        return (8, 4, 4)
    return (size, 1, 1)


def aligned(x, k):
    return pl.multiple_of(x, k)


def wide(x, reps):
    return jnp.concatenate([x] * reps, axis=1)


def fold(x):
    rows = x.shape[0]
    total = x[0:8]
    for k in range(8, rows, 8):
        total = total + x[k : k + 8]
    return total


def dot(a, b, dims):
    return lax.dot_general(a, b, (dims, ((), ())), preferred_element_type=F32)


def only(condition, run):
    if condition is None:
        run()
    else:
        pl.when(condition)(lambda: (run(), None)[1])


class Reduction:
    def __init__(self, env, layer, index, block, orders, lane_of):
        self.env, self.layer, self.index, self.block, self.orders = env, layer, index, block, orders
        self.lane_of = lane_of
        self.space = env["space"].at[layer, index]
        self.depth = len(orders[0])
        self.regions = [self.shares(i, order) for i, order in enumerate(orders)]
        self.step = 0
        self.waits = []
        self.slot = [0, 0]
        depth = self.depth
        self.steps = [functools.partial(self.scatter, k) for k in range(depth)]
        self.steps += [functools.partial(self.gather, k) for k in range(depth - 1, 0, -1)]
        self.steps += [self.give, self.finish]

    def shares(self, i, order):
        out = [(0, W, i * PART, PART)]
        for axis in order:
            out.append(self.share(out[-1], axis, axis["index"]))
        return out

    def share(self, region, axis, index):
        if axis["fold"]:
            return region
        row, rows, lane, lanes = region
        by_row = min(axis["size"], rows // 16)
        rows, lanes = rows // by_row, lanes // (axis["size"] // by_row)
        if by_row == axis["size"]:
            return row + index * rows, rows, lane, lanes
        return row + lax.rem(index, by_row) * rows, rows, lane + index // by_row * lanes, lanes

    @property
    def free_to_go(self):
        return self.step != self.depth or self.layer in self.env["summed"]

    @property
    def done(self):
        return self.step >= len(self.steps)

    def advance(self):
        self.sent = []
        self.steps[self.step]()
        self.step += 1
        return self.sent

    def remote(self, i, src, dst, slot, where, recv=None):
        sems = (self.layer, self.index, i, slot)
        return pltpu.make_async_remote_copy(
            src_ref=src, dst_ref=dst, send_sem=self.env["ar_send"].at[sems],
            recv_sem=self.env["ar_recv"].at[sems] if recv is None else recv, device_id=where, device_id_type=MESH,
        )

    def wait(self):
        for made, came, sends, receives in self.waits:
            only(sends, made.wait_send)
            only(receives, came.wait_recv)
        self.waits = []

    def take(self, i):
        self.slot[i] += 1
        return self.slot[i] - 1

    def came_at(self, i, k, s):
        row = sum((a["size"] - 1) * self.regions[i][n + 1][1] for n, a in enumerate(self.orders[i][:k]))
        _, rows, _, lanes = self.regions[i][k + 1]
        return row + (s - 1) * rows, rows, i * PART, lanes

    def scatter(self, k):
        if k > 0:
            self.wait()
            self.add(k - 1)
        for i in range(2):
            self.scatter_part(i, k)

    def start_part(self, i):
        self.sent = []
        self.scatter_part(i, 0)
        if i == 1:
            self.step = 1
        return self.sent

    def scatter_part(self, i, k):
        axis = self.orders[i][k]
        for s in range(1, axis["size"]):
            other = lax.rem(axis["index"] + s, axis["size"])
            row, rows, lane, lanes = self.share(self.regions[i][k], axis, other)
            src = self.block.at[pl.ds(aligned(row, 16), rows), pl.ds(aligned(lane, 128), lanes)]
            at, n, at_lane, n_lanes = self.came_at(i, k, s)
            dst = self.space.at[pl.ds(at, n), pl.ds(at_lane, n_lanes)]
            made = self.remote(i, src, dst, self.take(i), axis["at"](other))
            only(axis["sends"], made.start)
            self.waits.append((made, made, axis["sends"], axis["receives"]))
            self.sent.append((axis["link"], rows * lanes * 2))

    def add(self, k, last=False):
        rows = self.regions[0][k + 1][1]
        size = min(rows, 32)
        out = []
        for i in range(2):
            row, _, lane, lanes = self.regions[i][k + 1]
            lane = aligned(lane, 128)
            extra = None
            if last:
                part = self.index // PAIRS
                first = aligned((self.index % PAIRS) * 2 * PART + lane, 128)
                extra = self.env["vtot"][self.layer, part : part + 1, pl.ds(first, lanes)]
            came = [self.came_at(i, k, s) for s in range(1, self.orders[i][k]["size"])]
            out.append((row, lane, lanes, came, self.local(i, self.regions[i][k + 1])[0], extra))

        def body(j, _):
            for row, lane, lanes, came, home, extra in out:
                here = pl.ds(aligned(row + j * size, 16), size)
                total = self.block[here, pl.ds(lane, lanes)].astype(F32)
                for at, _, at_lane, _ in came:
                    there = pl.ds(aligned(at + j * size, 16), size)
                    total = total + self.space[there, pl.ds(at_lane, lanes)].astype(F32)
                if last:
                    column = self.env["column"][self.layer, here, :].astype(F32)
                    total = total + wide(column, lanes // 128) * extra
                    to = pl.ds(aligned(home + j * size, 16), size)
                    self.space[to, pl.ds(lane, lanes)] = total.astype(BF16)
                else:
                    self.block[here, pl.ds(lane, lanes)] = total.astype(BF16)
            return 0

        only(self.orders[0][k]["receives"], lambda: lax.fori_loop(0, rows // size, body, 0))

    def local(self, i, region):
        row, rows, lane, lanes = region
        return row - self.regions[i][1][0], rows, lane, lanes

    def gather(self, k):
        self.wait()
        if k == self.depth - 1:
            self.add(k, last=True)

        def ref(i, region):
            row, rows, lane, lanes = self.local(i, region)
            return self.space.at[pl.ds(aligned(row, 16), rows), pl.ds(aligned(lane, 128), lanes)]

        for i, order in enumerate(self.orders):
            axis = order[k]
            mine = ref(i, self.regions[i][k + 1])
            for s in range(1, axis["size"]):
                to = lax.rem(axis["index"] + s, axis["size"])
                frm = lax.rem(axis["index"] + axis["size"] - s, axis["size"])
                slot = self.take(i)
                made = self.remote(i, mine, mine, slot, axis["at"](to))
                only(axis["receives"], made.start)
                theirs = ref(i, self.share(self.regions[i][k], axis, frm))
                came = self.remote(i, theirs, theirs, slot, axis["at"](frm))
                self.waits.append((made, came, axis["receives"], axis["sends"]))
                self.sent.append((axis["link"], self.regions[i][k + 1][1] * self.regions[i][k + 1][3] * 2))

    def result(self, i, index, section):
        rows = self.regions[i][1][1]
        lane = aligned(self.lane_of(section) + i * PART, PART)
        return self.env["o"].at[section, pl.ds(aligned(index * rows, 16), rows), pl.ds(lane, PART)]

    def gathered(self, i):
        return self.space.at[pl.ds(0, self.regions[i][1][1]), pl.ds(i * PART, PART)]

    def deliver(self, i, s, straight):
        axis, section = self.orders[i][0], self.env["section"]
        recv = None if straight else self.env["ar_other"].at[self.layer, self.index, i, s]
        where = dict(axis["at"](lax.rem(axis["index"] + s, axis["size"])), section=self.layer)
        target = self.result(i, axis["index"], section)
        return self.remote(i, self.gathered(i), target, self.slot[i] + s, where, recv)

    def arrival(self, i, s, straight):
        axis, section = self.orders[i][0], self.env["section"]
        recv = None if straight else self.env["ar_other"].at[self.layer, self.index, i, s]
        index = lax.rem(axis["index"] + axis["size"] - s, axis["size"])
        frm = section if straight else 1 - section
        where = dict(axis["at"](index), section=frm)
        return self.remote(i, self.gathered(i), self.result(i, index, frm), self.slot[i] + s, where, recv)

    def kept(self, i):
        sem = self.env["ar_recv"].at[self.layer, self.index, i, self.slot[i]]
        target = self.result(i, self.orders[i][0]["index"], self.env["section"])
        return pltpu.make_async_copy(self.gathered(i), target, sem)

    def give(self):
        self.wait()

        @pl.when(self.env["section"] == self.layer)
        def _():
            for i in range(2):
                for s in range(1, self.orders[i][0]["size"]):
                    self.deliver(i, s, True).start()
                self.kept(i).start()

        @pl.when(self.env["section"] != self.layer)
        def _():
            for i in range(2):
                for s in range(self.orders[i][0]["size"] - 1, -1, -1):
                    self.deliver(i, s, False).start()

        for i, order in enumerate(self.orders):
            self.sent.append((order[0]["link"], self.regions[i][1][1] * PART * 2 * (order[0]["size"] - 1)))

    def finish(self):
        @pl.when(self.env["section"] == self.layer)
        def _():
            for i in range(2):
                size = self.orders[i][0]["size"]
                self.kept(i).wait()
                for s in range(1, size):
                    self.deliver(i, s, True).wait_send()
                    self.arrival(i, s, True).wait_recv()
                for s in range(size):
                    self.arrival(i, s, False).wait_recv()

        @pl.when(self.env["section"] != self.layer)
        def _():
            for i in range(2):
                for s in range(self.orders[i][0]["size"]):
                    self.deliver(i, s, False).wait_send()


class Order:
    RATE, HOP = 70e3, 1.8

    def __init__(self):
        self.now = 0.0
        self.free = {}
        self.going = []

    def sent(self, copies):
        end = self.now
        for link, size in copies:
            self.free[link] = max(self.now, self.free.get(link, 0.0)) + size / self.RATE
            end = max(end, self.free[link])
        return end + self.HOP

    def begin(self, one, i):
        end = self.sent(one.start_part(i))
        if i == 0:
            one.due = end
        else:
            one.due = max(one.due, end)
            self.going.append(one)

    def advance(self, one):
        self.now = max(self.now, one.due) + 0.4
        one.due = self.sent(one.advance())
        if one.done:
            self.going.remove(one)

    def work(self, cost):
        self.now += cost
        while True:
            due = [x for x in self.going if x.due <= self.now and x.free_to_go]
            if not due:
                return
            self.advance(min(due, key=lambda x: x.due))

    def drain(self):
        while self.going:
            self.advance(min(self.going, key=lambda x: x.due))


def kernel(dims, steps, seqs, views, frames, grad_out, weights, gains, shifts, recurs, lengths, masks, o, gf, vectors, f_own, f_far, p_own, p_far, g3, wc, wr1, src_t, live, turn,
           staged, heads, tails, v, vecs, rows, hid, coef, tot, vtot, levels, column, counts, cnt_p, cnt_z, slim_p, slim_z,
           wide_p, wide_z, space, sems, v_sems, stage_sem, credit, pl_send, pl_recv, z_send, z_recv, ar_send, ar_recv,
           ar_other):
    nz, ny, nx = dims
    np_ = ny * nx
    span = steps * seqs
    total_rows = 2 * span
    sent_rows = total_rows + 16
    pairs = steps // 2
    section = lax.axis_index("section")
    other = 1 - section
    b = lax.axis_index("batch")
    mp = lax.rem(b, np_)
    mz = b // np_

    def at_plane(i):
        return {"batch": b - mp + i}

    def at_z(i):
        return {"batch": b + (i - mz) * np_}

    def axis_of(link, index, stride, fold=False, sends=None, receives=None):
        at = lambda i: {"batch": b + (i - index) * stride}
        return dict(link=link, size=2, index=index, at=at, fold=fold, sends=sends, receives=receives)

    def halvings(link, size, stride):
        out = []
        while size > 1:
            out.append(axis_of(link, lax.rem(b // stride, 2), stride))
            size //= 2
            stride *= 2
        return out

    xs, ys, zs = halvings("x", nx, 1), halvings("y", ny, nx), halvings("z", nz, np_)
    if nz == 4:
        inner = (mz == 1) | (mz == 2)
        outer = (mz == 0) | (mz == 3)
        zs = [
            axis_of("z", lax.rem(mz, 2), np_, True, outer, inner),
            axis_of("z", mz // 2, np_, False, inner, inner),
        ]
    orders = (xs + ys + zs, ys + xs + zs)
    sibling = {"section": other}

    def local(src, dst, slot):
        return pltpu.make_async_copy(src, dst, sems.at[0, slot])

    def across(src, dst, slot):
        return pltpu.make_async_remote_copy(
            src_ref=src, dst_ref=dst, send_sem=sems.at[1, slot], recv_sem=sems.at[2, slot],
            device_id=sibling, device_id_type=MESH,
        )

    half = frames.shape[3]
    width = 2 * half
    lead = W - half
    rest = width - W
    full = rest // 128 * 128

    def fetch(source, m):
        return pltpu.make_async_copy(source.at[m], staged.at[m], stage_sem.at[m])

    def by_units(source, target, m):
        fetch(source, m).wait()

        @pl.when(section == 0)
        def _():
            pad = jnp.zeros((2 * seqs, lead), F32)

            def place(i, _):
                x = staged[m, pl.ds(2 * i, 2)].astype(F32).reshape(2 * seqs, half)
                to = pl.ds(aligned(m * span + 2 * i * seqs, 16), 2 * seqs)
                target[to, :] = jnp.concatenate([x, pad], axis=1).astype(BF16)
                return 0

            lax.fori_loop(0, pairs, place, 0)

        @pl.when(section == 1)
        def _():
            pad = jnp.zeros((2 * seqs, 2 * lead), F32)

            def place(i, _):
                x = staged[m, pl.ds(2 * i, 2)].astype(F32).reshape(2 * seqs, half)
                to = pl.ds(aligned(m * span + 2 * i * seqs, 16), 2 * seqs)
                target[to, :] = jnp.concatenate([x[:, lead:], pad], axis=1).astype(BF16)
                return 0

            lax.fori_loop(0, pairs, place, 0)

    def patch_heads(target, m):
        @pl.when(section == 0)
        def _():
            lane = lax.broadcasted_iota(jnp.int32, (2 * seqs, 128), 1)

            def place(i, _):
                to = pl.ds(aligned(m * span + 2 * i * seqs, 16), 2 * seqs)
                head = heads[m, pl.ds(2 * i, 2)].astype(F32).reshape(2 * seqs, 128)
                head = pltpu.roll(head, 128 - lead, 1)
                old = target[to, W - 128 :].astype(F32)
                target[to, W - 128 :] = jnp.where(lane < 128 - lead, old, head).astype(BF16)
                return 0

            lax.fori_loop(0, pairs, place, 0)

    def pieces(row, count, u, block, spot):
        r = pl.ds(row, count)
        to = pl.ds(0, count)
        if u == 0:
            return [(weights.at[0, r, pl.ds(0, W)], block.at[to, :])]
        return [
            (weights.at[0, r, pl.ds(W, full)], block.at[to, pl.ds(0, full)]),
            (weights.at[0, r, pl.ds(W + full, rest - full)], tails.at[spot, to, :]),
        ]

    rows_of = {0: (0, W), 1: (W, rest)}

    def w_plan(layer):
        mine, far = rows_of[layer], rows_of[1 - layer]
        plan = [
            (mine, layer, far, 1 - layer, wc.at[layer, 0], 2 * layer),
            (far, layer, mine, 1 - layer, wc.at[layer, 1], 2 * layer + 1),
        ]
        if layer == 1:
            plan.append((mine, 0, far, 1, wr1, 4))
        return plan

    late_row = (width - half) // 16 * 16
    late_shift = half - late_row
    late_plan = [
        ((0, W), 0, (late_row, width - late_row), 1, wc.at[0, 0], 0),
        ((0, W), 1, (late_row, width - late_row), 0, wc.at[0, 1], 1),
    ]
    slot_of = {0: 4, 1: 8, 2: 14}

    def local_w(plan, base, which):
        r, u, _, _, block, spot = plan[which]
        return [local(a, t, base + 2 * which + i) for i, (a, t) in enumerate(pieces(*r, u, block, spot))]

    def across_w(plan, base, which):
        _, _, r, u, block, spot = plan[which]
        return [across(a, t, base + 2 * which + i) for i, (a, t) in enumerate(pieces(*r, u, block, spot))]

    def start_local_w(layer, plan, base):
        @pl.when(section == layer)
        def _():
            for which in range(len(plan)):
                for made in local_w(plan, base, which):
                    made.start()

    def start_across_w(layer, plan, base):
        @pl.when(section == layer)
        def _():
            for which in range(len(plan)):
                for made in across_w(plan, base, which):
                    made.start()

    def last_units(block, spot):
        def body(i, _):
            r = pl.ds(aligned(i * 128, 128), 128)
            x = tails[spot, r, :].astype(F32)
            x = jnp.concatenate([x, jnp.zeros((128, 128 - x.shape[1]), F32)], axis=1)
            block[r, full:] = x.astype(BF16)
            return 0

        lax.fori_loop(0, W // 128, body, 0)

    def wait_w(layer, plan, base, which):
        _, own_u, _, far_u, block, spot = plan[which]

        @pl.when(section == layer)
        def _():
            for made in local_w(plan, base, which):
                made.wait()
            if own_u == 1:
                last_units(block, spot)

        @pl.when(section != layer)
        def _():
            for made in across_w(plan, base, which):
                made.wait_recv()
            if far_u == 1:
                last_units(block, spot)

    def done_w(layer, plan, base):
        @pl.when(section == layer)
        def _():
            for which in range(len(plan)):
                for made in across_w(plan, base, which):
                    made.wait_send()

    def heads_copy(source, slot):
        return across(source.at[:, :, :, pl.ds(0, 128)], heads, slot)

    def wait_heads(source, slot):
        @pl.when(section == 0)
        def _():
            heads_copy(source, slot).wait_recv()

        @pl.when(section == 1)
        def _():
            heads_copy(source, slot).wait_send()

    fetch(frames, 0).start()
    fetch(frames, 1).start()
    for layer in range(2):
        start_local_w(layer, w_plan(layer), slot_of[layer])

    barrier = pltpu.get_barrier_semaphore()
    greeted = [dict(sibling)]
    greeted += [at_plane(lax.rem(mp + k, np_)) for k in range(1, np_)]
    greeted += [at_z(lax.rem(mz + k, nz)) for k in range(1, nz)]
    for axis in (xs + zs)[:1] + (ys + zs)[:1]:
        greeted.append(dict(axis["at"](1 - axis["index"]), section=other))
    for where in greeted:
        pl.semaphore_signal(barrier, inc=1, device_id=where, device_id_type=MESH)

    for k, (x, fill) in enumerate(((gains, 0.0), (shifts, -1e30), (recurs, 0.0))):
        vecs[section, k : k + 1, 0:width] = x[...]
        vecs[section, k : k + 1, width:] = jnp.full((1, 2 * W - width), fill, F32)
    vecs[section, 3:8, :] = jnp.zeros((5, 2 * W), F32)

    gap = jnp.zeros((W - rest, W), BF16)

    @pl.when(section == 0)
    def _():
        wc[0, 1, rest:, :] = gap
        wc[1, 1, rest:, :] = gap

    @pl.when(section == 1)
    def _():
        wc[0, 0, rest:, :] = gap
        wc[1, 0, rest:, :] = gap
        wr1[rest:, :] = gap

    for spot in (0, 2):
        tails[spot, rest:, :] = jnp.zeros((W - rest, rest - full), BF16)
    for spare in (f_own, p_own, g3.at[0], g3.at[1]):
        spare[sent_rows:, :] = jnp.zeros((spare.shape[0] - sent_rows, W), BF16)

    pl.semaphore_wait(barrier, len(greeted))

    @pl.when(section == 1)
    def _():
        heads_copy(frames, 1).start()

    start_across_w(0, w_plan(0), slot_of[0])
    send_vec = across(vecs.at[section], vecs.at[section], 3)
    send_vec.start()

    def stage_copy(where, rnd, slot, k, back):
        buf, parity, size, me, at, send, recv = where
        there = at(lax.rem(me + (size - k if back else k), size))
        ref = buf.at[parity, slot]
        return pltpu.make_async_remote_copy(
            src_ref=ref, dst_ref=ref, send_sem=send.at[rnd, k], recv_sem=recv.at[rnd, k],
            device_id=there, device_id_type=MESH,
        )

    def in_plane(buf, parity):
        return (buf, parity, np_, mp, at_plane, pl_send, pl_recv)

    def in_line(buf, parity):
        return (buf, parity, nz, mz, at_z, z_send, z_recv)

    def stage_start(where, rnd, value):
        buf, parity, size, me = where[:4]
        buf[parity, me] = value
        for k in range(1, size):
            stage_copy(where, rnd, me, k, False).start()

    def stage_wait(where, rnd):
        size, me = where[2:4]
        for k in range(1, size):
            stage_copy(where, rnd, me, k, False).wait_send()
            stage_copy(where, rnd, lax.rem(me + size - k, size), k, True).wait_recv()

    def add_slots(where):
        buf, parity, size = where[:3]
        total = buf[parity, 0]
        for k in range(1, size):
            total = total + buf[parity, k]
        return total

    groups = lengths.shape[1]
    s_at = lax.broadcasted_iota(jnp.int32, (seqs, groups), 0)
    g_at = lax.broadcasted_iota(jnp.int32, (seqs, groups), 1) * views
    there = (s_at >= g_at) & (s_at < g_at + views)
    position = lax.broadcasted_iota(jnp.int32, (seqs, 128), 1)
    local_counts = []
    for m in range(2):
        turn[...] = jnp.zeros_like(turn)
        turn[0:steps, 0:seqs] = masks[m].astype(F32)
        mask = turn[...].T[0:seqs]
        length = jnp.broadcast_to(lengths[m : m + 1, :], (seqs, groups)).astype(F32)
        limit = jnp.sum(jnp.where(there, length, 0.0), axis=1, keepdims=True)
        alive = (position.astype(F32) < limit) & ((mask > 0.0) | (position == 0))
        alive = jnp.where(position < steps, alive.astype(F32), 0.0)
        total = jnp.zeros((seqs, 128), F32)
        for t in range(steps):
            at = m * span + t * seqs
            cells = jnp.broadcast_to(alive[:, t : t + 1], (seqs, 128))
            live[at : at + seqs, :] = cells
            total = total + cells
        local_counts.append(jnp.sum(total, axis=0, keepdims=True))
    n_own = jnp.concatenate(local_counts * 4, axis=0)

    cnt_plane, cnt_line = in_plane(cnt_p, 0), in_line(cnt_z, 0)
    stage_start(cnt_plane, 0, n_own)

    def vec_of(layer, k):
        return vecs[layer, k : k + 1, pl.ds(aligned(section * W, W), W)]

    def matmul_to(out, a, w, first, m):
        r = pl.ds(m * span, span)

        def body(i, _):
            c = pl.ds(aligned(i * HALF, HALF), HALF)
            y = dot(a[r, :], w[:, c], ((1,), (0,)))
            out[r, c] = y if first else out[r, c] + y
            return 0

        lax.fori_loop(0, 2, body, 0)

    def packed(x, y):
        return jnp.concatenate([z[:, k * QUART : (k + 1) * QUART] for z in (x, y) for k in range(4)], axis=0)

    def unpacked(x):
        return jnp.concatenate([x[k : k + 1] for k in range(4)], axis=1)

    def merge_slots(where, counts_of):
        buf, parity, size = where[:3]
        s = [buf[parity, k, 0:4, :] for k in range(size)]
        q = [buf[parity, k, 4:8, :] for k in range(size)]
        n = [wide(counts_of(k), 2) for k in range(size)]
        total, squares, count = sum(s[1:], s[0]), sum(q[1:], q[0]), sum(n[1:], n[0])
        mean = total / count
        for k in range(size):
            d = s[k] / n[k] - mean
            squares = squares + n[k] * d * d
        return jnp.concatenate([total, squares], axis=0)

    def slim_round(which, m):
        return 1 + 2 * which + m, in_plane(slim_p, 2 * m + which % 2), in_line(slim_z, 2 * m + which % 2)

    def forward_stats(layer, m):
        start = jnp.sum(rows[layer, m * span : m * span + seqs, :], axis=0, keepdims=True) * (1.0 / seqs)

        def body(i, carry):
            s, q = carry
            r = pl.ds(aligned(m * span + i * (2 * seqs), 16), 2 * seqs)
            d = rows[layer, r, :] - start
            kept = wide(live[r, :], 8) * d
            return s + fold(kept), q + fold(kept * d)

        zero = jnp.zeros((8, W), F32)
        s, q = lax.fori_loop(0, pairs, body, (zero, zero))
        s, q = jnp.sum(s, axis=0, keepdims=True), jnp.sum(q, axis=0, keepdims=True)
        n = wide(local_counts[m], 8)
        rnd, plane, _ = slim_round(layer, m)
        stage_start(plane, rnd, packed(s + n * start, jnp.maximum(q - s * s / n, 0.0)))

    def forward_middle(layer, m):
        rnd, plane, line = slim_round(layer, m)
        stage_wait(plane, rnd)
        stage_start(line, rnd, merge_slots(plane, lambda k: cnt_p[0, k, m : m + 1, :]))

    def forward_end(layer, m):
        rnd, _, line = slim_round(layer, m)
        stage_wait(line, rnd)
        value = merge_slots(line, lambda k: cnt_z[0, k, m : m + 1, :])
        count = wide(counts[m : m + 1, :], 8)
        mean = unpacked(value[0:4]) / count
        scale = lax.rsqrt(unpacked(value[4:8]) / count + EPS)
        coef[layer, 2 * m : 2 * m + 1, :] = mean
        coef[layer, 2 * m + 1 : 2 * m + 2, :] = scale
        slope = vec_of(layer, 0) * scale
        coef[layer, 4 + 2 * m : 5 + 2 * m, :] = slope
        coef[layer, 5 + 2 * m : 6 + 2 * m, :] = vec_of(layer, 1) - mean * slope

    def forward_scan(layer, m, passes):
        rec = vec_of(layer, 2)
        slope = coef[layer, 4 + 2 * m : 5 + 2 * m, :]
        shift = coef[layer, 5 + 2 * m : 6 + 2 * m, :]

        def body(i, carry):
            h, level = carry
            r = pl.ds(aligned(m * span + i * (2 * seqs), 16), 2 * seqs)
            x = rows[layer, r, :] * slope + shift
            lv = wide(live[r, :], 8)
            alive = lv > 0.0
            both = []
            for k in range(2):
                part = slice(k * seqs, (k + 1) * seqs)
                z = x[part] + rec * h
                soft = jnp.maximum(z, 0.0) + jnp.log(1.0 + jnp.exp(-jnp.abs(z)))
                h = jnp.where(alive[part], soft, h)
                both.append(h)
            two = jnp.concatenate(both, axis=0)
            hid[layer, r, :] = two
            if passes:
                p_own[r, :] = two.astype(BF16)
                level = level + fold(lv * two)
            return h, level

        _, level = lax.fori_loop(0, pairs, body, (jnp.zeros((seqs, W), F32), jnp.zeros((8, W), F32)))
        if not passes:
            return None
        level = jnp.sum(level, axis=0, keepdims=True)
        levels[1:2, :] = level if m == 0 else levels[1:2, :] + level
        here = pl.ds(m * span, span)
        made = across(p_own.at[here, :], p_far.at[here, :], 18 + m)
        made.start()
        return made

    def backward_scan(layer, m, above, between=lambda: None):
        gain, shift, recur = vec_of(layer, 0), vec_of(layer, 1), vec_of(layer, 2)
        for lq in range(4):
            lanes = slice(lq * QUART, (lq + 1) * QUART)
            gq, sq, rec = gain[:, lanes], shift[:, lanes], recur[:, lanes]
            mean = coef[layer, 2 * m : 2 * m + 1, lanes]
            scale = coef[layer, 2 * m + 1 : 2 * m + 2, lanes]

            def body(i, carry):
                down, s1, s2, rsum, sqh, sqa = carry
                i = pairs - 1 - i
                start = m * span + i * (2 * seqs)
                r = pl.ds(aligned(start, 16), 2 * seqs)
                before = pl.ds(aligned(jnp.maximum(start - seqs, 0), 8), seqs)
                normed = (rows[layer, r, lanes] - mean) * scale
                drive = gq * normed + sq
                h2 = hid[layer, r, lanes]
                hb = jnp.where(i > 0, hid[layer, before, lanes], 0.0)
                lv = wide(live[r, :], 2)
                up = above[r, lanes].astype(F32)
                res = f_own[r, lanes].astype(F32)
                aux = res + h2 if layer == 1 else res
                sqh = sqh + fold(lv * (h2 * h2))
                sqa = sqa + fold(lv * (aux * aux))
                grads = [None, None]
                for k in (1, 0):
                    part = slice(k * seqs, (k + 1) * seqs)
                    prior = h2[0:seqs] if k == 1 else hb
                    slope = 0.5 + 0.5 * jnp.tanh(0.5 * (drive[part] + rec * prior))
                    total = up[part] + down
                    gd = lv[part] * slope * total
                    down = (1.0 - lv[part]) * total + rec * gd
                    grads[k] = gd
                    rsum = rsum + fold(gd * prior)
                gd2 = jnp.concatenate(grads, axis=0)
                hid[layer, r, lanes] = gd2
                return down, s1 + fold(gd2), s2 + fold(gd2 * normed), rsum, sqh, sqa

            z8 = jnp.zeros((8, QUART), F32)
            _, s1, s2, rsum, sqh, sqa = lax.fori_loop(
                0, pairs, body, (jnp.zeros((seqs, QUART), F32), z8, z8, z8, z8, z8)
            )
            for k, x in ((m, s1), (2 + m, s2)):
                tot[layer, k : k + 1, lanes] = jnp.sum(x, axis=0, keepdims=True)
            for k, x in ((4, rsum), (5, sqh), (6, sqa)):
                x = jnp.sum(x, axis=0, keepdims=True)
                tot[layer, k : k + 1, lanes] = x if m == 0 else tot[layer, k : k + 1, lanes] + x
            between()

    def backward_stats(layer, m):
        rnd, plane, _ = slim_round(3 - layer, m)
        stage_start(plane, rnd, packed(tot[layer, m : m + 1, :], tot[layer, 2 + m : 3 + m, :]))

    def backward_middle(layer, m):
        rnd, plane, line = slim_round(3 - layer, m)
        stage_wait(plane, rnd)
        stage_start(line, rnd, add_slots(plane))

    def backward_end(layer, m):
        rnd, _, line = slim_round(3 - layer, m)
        stage_wait(line, rnd)
        value = add_slots(line)
        tot[layer, m : m + 1, :] = unpacked(value[0:4])
        tot[layer, 2 + m : 3 + m, :] = unpacked(value[4:8])

    def grad_rows(layer, m, slot):
        gain = vec_of(layer, 0)
        for lh in range(2):
            lanes = slice(lh * HALF, (lh + 1) * HALF)
            mean = coef[layer, 2 * m : 2 * m + 1, lanes]
            scale = coef[layer, 2 * m + 1 : 2 * m + 2, lanes]
            count = wide(counts[m : m + 1, :], 4)
            first = tot[layer, m : m + 1, lanes] / count
            second = tot[layer, 2 + m : 3 + m, lanes] / count * scale
            k = scale * gain[:, lanes]

            def body(i, acc):
                r = pl.ds(aligned(m * span + i * (2 * seqs), 16), 2 * seqs)
                y = hid[layer, r, lanes] - first - (rows[layer, r, lanes] - mean) * second
                y = wide(live[r, :], 4) * (k * y)
                g3[0, r, lanes] = y.astype(BF16)
                return acc + fold(y)

            acc = lax.fori_loop(0, pairs, body, jnp.zeros((8, HALF), F32))
            acc = jnp.sum(acc, axis=0, keepdims=True)
            if m == 0:
                levels[4:5, lanes] = acc
            else:
                top = lax.broadcasted_iota(jnp.int32, (16, HALF), 0) == 0
                minus = jnp.where(top, -(levels[4:5, lanes] + acc), 0.0)
                g3[0, total_rows:sent_rows, lanes] = minus.astype(BF16)
        here = pl.ds(0, span) if m == 0 else pl.ds(span, span + 16)
        made = across(g3.at[0, here, :], g3.at[1, here, :], slot + m)
        made.start()
        return made

    sums_round = {1: (1, 10), 0: (0, 11)}

    def sums_start(layer):
        parity, rnd = sums_round[layer]
        own_sum = -g3[0, total_rows:sent_rows, :].astype(F32)[0:1]
        far_sum = -g3[1, total_rows:sent_rows, :].astype(F32)[0:1]
        value = jnp.concatenate([own_sum, far_sum, tot[layer, 4:7, :], jnp.zeros((3, W), F32)], axis=0)
        stage_start(in_plane(wide_p, parity), rnd, value)

    def sums_middle(layer):
        parity, rnd = sums_round[layer]
        stage_wait(in_plane(wide_p, parity), rnd)
        stage_start(in_line(wide_z, parity), rnd, add_slots(in_plane(wide_p, parity)))

    def sums_end(layer):
        parity, rnd = sums_round[layer]
        stage_wait(in_line(wide_z, parity), rnd)
        vtot[layer] = add_slots(in_line(wide_z, parity))
        tot[layer, 4:7, :] = vtot[layer, 2:5, :]
        tot[layer, 7:8, :] = wide(counts[0:1, :] + counts[1:2, :], 8)
        env["summed"].add(layer)

        @pl.when(section == layer)
        def _():
            pltpu.make_async_copy(tot.at[layer], v.at[section], v_sems.at[0]).start()

        @pl.when(section != layer)
        def _():
            v_across(layer).start()

    def v_across(layer):
        return pltpu.make_async_remote_copy(
            src_ref=tot.at[layer], dst_ref=v.at[section], send_sem=v_sems.at[1], recv_sem=v_sems.at[2],
            device_id=sibling, device_id_type=MESH,
        )

    def transpose(src, begin=0, end=W // 128):
        def body(j, _):
            c = pl.ds(aligned(j * 128, 128), 128)
            src_t[c, 0:total_rows] = src[0:total_rows, c].T
            return 0

        lax.fori_loop(begin, end, body, 0)

    def transpose_level(src, layer):
        top = lax.broadcasted_iota(jnp.int32, (16, W), 0) == 0
        src[total_rows:sent_rows, :] = jnp.where(top, levels[2 + layer : 3 + layer, :], 0.0).astype(BF16)

        def body(j, _):
            c = pl.ds(aligned(j * 128, 128), 128)
            src_t[c, total_rows:] = src[total_rows:, c].T
            level = src[total_rows:sent_rows, c].astype(F32)[0:1]
            column[layer, c, :] = jnp.broadcast_to(level, (128, 128)).T.astype(BF16)
            return 0

        lax.fori_loop(0, W // 128, body, 0)

    def weight_part(block, grads, c):
        lanes = pl.ds(c * HALF, HALF)

        def body(j, _):
            r = pl.ds(aligned(j * HALF, HALF), HALF)
            block[r, lanes] = dot(src_t[r, :], grads[:, lanes], ((1,), (0,))).astype(BF16)
            return 0

        lax.fori_loop(0, W // HALF, body, 0)

    def source_grad(store, w_own, w_far, between):
        for m in range(2):
            r = pl.ds(m * span, span)

            def body(i, _):
                c = pl.ds(aligned(i * HALF, HALF), HALF)
                y = dot(g3[0, r, :], w_own[c, :], ((1,), (1,))) + dot(g3[1, r, :], w_far[c, :], ((1,), (1,)))
                store(r, c, y)
                return 0

            lax.fori_loop(0, 2, body, 0)
            between()

    env = dict(summed=set(), vtot=vtot, column=column, space=space, ar_send=ar_send, ar_recv=ar_recv,
               ar_other=ar_other, o=o, section=section, here={"batch": b})
    blocks = {
        (1, 0): f_far.at[pl.ds(0, W), :],
        (1, 1): p_far.at[pl.ds(0, W), :],
        (0, 0): wc.at[1, 1],
        (0, 1): wr1,
    }
    parts = {}
    for layer in (1, 0):
        for index in range(2 * PAIRS):
            part, side = index // PAIRS, index % PAIRS

            def lane_of(sec, part=part, side=side):
                return (sec if part == 0 else 1 - sec) * W + side * 2 * PART

            block = blocks[layer, part].at[:, pl.ds(side * 2 * PART, 2 * PART)]
            parts[layer, index] = Reduction(env, layer, index, block, orders, lane_of)
    order = Order()

    def weight_grads(layer, between):
        for part in range(2):
            if part == 1:
                between()
            for c in range(2):
                weight_part(blocks[layer, part], g3.at[part], c)
                order.work(2.0)
                for k in range(c * HALF // PART, (c + 1) * HALF // PART):
                    order.begin(parts[layer, part * PAIRS + k // 2], k % 2)

    def arrived(layer, sends):
        for made in sends:
            made.wait()
        sums_start(layer)

    send_f = []
    for m in range(2):
        by_units(frames, f_own, m)
        fetch(grad_out, m).start()
        if m == 0:
            wait_heads(frames, 1)
        patch_heads(f_own, m)
        here = pl.ds(m * span, span)
        made = across(f_own.at[here, :], f_far.at[here, :], (0, 24)[m])
        made.start()
        send_f.append(made)
    start_across_w(1, w_plan(1), slot_of[1])
    stage_wait(cnt_plane, 0)
    stage_start(cnt_line, 0, add_slots(cnt_plane))
    wait_w(0, w_plan(0), slot_of[0], 0)
    matmul_to(rows.at[0], f_own, wc.at[0, 0], True, 0)
    matmul_to(rows.at[0], f_own, wc.at[0, 0], True, 1)
    wait_w(0, w_plan(0), slot_of[0], 1)
    send_f[0].wait()
    matmul_to(rows.at[0], f_far, wc.at[0, 1], False, 0)
    forward_stats(0, 0)
    send_f[1].wait()

    @pl.when(section == 1)
    def _():
        heads_copy(grad_out, 2).start()

    matmul_to(rows.at[0], f_far, wc.at[0, 1], False, 1)
    forward_middle(0, 0)
    forward_stats(0, 1)
    send_vec.wait_send()
    across(vecs.at[other], vecs.at[other], 3).wait_recv()
    stage_wait(cnt_line, 0)
    counts[...] = add_slots(cnt_line)
    forward_end(0, 0)
    sends = [forward_scan(0, 0, True)]
    forward_middle(0, 1)
    by_units(grad_out, g3.at[1], 0)
    wait_heads(grad_out, 2)
    patch_heads(g3.at[1], 0)
    forward_end(0, 1)
    sends.append(forward_scan(0, 1, True))
    wait_w(1, w_plan(1), slot_of[1], 0)
    matmul_to(rows.at[1], p_own, wc.at[1, 0], True, 0)
    wait_w(1, w_plan(1), slot_of[1], 1)
    sends[0].wait()
    matmul_to(rows.at[1], p_far, wc.at[1, 1], False, 0)
    forward_stats(1, 0)
    matmul_to(rows.at[1], p_own, wc.at[1, 0], True, 1)
    forward_middle(1, 0)
    sends[1].wait()
    matmul_to(rows.at[1], p_far, wc.at[1, 1], False, 1)
    forward_stats(1, 1)
    done_w(0, w_plan(0), slot_of[0])

    start_local_w(0, late_plan, slot_of[2])
    start_across_w(0, late_plan, slot_of[2])

    @pl.when(section == 1)
    def _():
        wc[0, 1, width - late_row :, :] = jnp.zeros((W - width + late_row, W), BF16)

    def source_level():
        def body(i, acc):
            r = pl.ds(aligned(i * (2 * seqs), 16), 2 * seqs)
            return acc + fold(wide(live[r, :], 8) * f_own[r, :].astype(F32))

        acc = lax.fori_loop(0, 2 * pairs, body, jnp.zeros((8, W), F32))
        levels[0:1, :] = jnp.sum(acc, axis=0, keepdims=True)

    forward_end(1, 0)
    forward_scan(1, 0, False)
    forward_middle(1, 1)
    by_units(grad_out, g3.at[1], 1)
    patch_heads(g3.at[1], 1)
    source_level()
    forward_end(1, 1)
    level_plane, level_line = in_plane(wide_p, 0), in_line(wide_z, 0)
    stage_start(level_plane, 9, jnp.concatenate([levels[0:2, :], jnp.zeros((6, W), F32)], axis=0))
    forward_scan(1, 1, False)
    backward_scan(1, 0, g3.at[1])
    backward_stats(1, 0)
    stage_wait(level_plane, 9)
    stage_start(level_line, 9, add_slots(level_plane))
    backward_scan(1, 1, g3.at[1])
    backward_stats(1, 1)
    backward_middle(1, 0)
    pl.semaphore_signal(credit.at[0], inc=1, device_id=sibling, device_id_type=MESH)
    transpose(p_own, 0, W // 256)
    backward_middle(1, 1)
    backward_end(1, 0)
    pl.semaphore_wait(credit.at[0], 1)
    sends = [grad_rows(1, 0, 20)]
    transpose(p_own, W // 256)
    stage_wait(level_line, 9)
    levels[2:4, :] = (add_slots(level_line) / wide(counts[0:1, :] + counts[1:2, :], 8))[0:2]
    transpose_level(p_own, 1)
    backward_end(1, 1)
    sends.append(grad_rows(1, 1, 20))
    weight_grads(1, lambda: arrived(1, sends))
    wait_w(1, w_plan(1), slot_of[1], 2)
    done_w(1, w_plan(1), slot_of[1])

    def keep_down(r, c, y):
        p_own[r, c] = y.astype(BF16)

    source_grad(keep_down, wc.at[1, 0], wr1, lambda: order.work(3.0))
    pl.semaphore_signal(credit.at[1], inc=1, device_id=sibling, device_id_type=MESH)
    sums_middle(1)
    backward_scan(0, 0, p_own, lambda: order.work(0.6))
    backward_stats(0, 0)
    backward_scan(0, 1, p_own, lambda: order.work(0.6))
    backward_stats(0, 1)
    backward_middle(0, 0)
    sums_end(1)
    transpose(f_own)
    transpose_level(f_own, 0)
    backward_middle(0, 1)
    order.work(3.0)
    backward_end(0, 0)
    pl.semaphore_wait(credit.at[1], 1)
    sends = [grad_rows(0, 0, 22)]
    backward_end(0, 1)
    sends.append(grad_rows(0, 1, 22))
    order.work(2.0)
    weight_grads(0, lambda: arrived(0, sends))
    wait_w(0, late_plan, slot_of[2], 0)
    wait_w(0, late_plan, slot_of[2], 1)
    done_w(0, late_plan, slot_of[2])

    def keep_source(r, c, y):
        rows[0, r, c] = y

    fetch(grad_out, 0).start()
    fetch(grad_out, 1).start()
    sums_middle(0)
    source_grad(keep_source, wc.at[0, 0], wc.at[0, 1], lambda: order.work(3.0))
    sums_end(0)

    def give(m):
        return pltpu.make_async_copy(staged.at[m], gf.at[m], stage_sem.at[m])

    for m in range(2):
        fetch(grad_out, m).wait()

        def finish_frames(i, _, m=m):
            straight = staged[m, pl.ds(2 * i, 2)].astype(F32).reshape(2 * seqs, half)
            y = rows[0, pl.ds(aligned(m * span + 2 * i * seqs, 8), 2 * seqs), :]
            y = jnp.where(section == 0, y[:, :half], y[:, late_shift : late_shift + half])
            staged[m, pl.ds(2 * i, 2)] = (y + straight).reshape(2, seqs, half).astype(BF16)
            return 0

        lax.fori_loop(0, pairs, finish_frames, 0)
        give(m).start()
        order.work(2.0)
    order.drain()
    for m in range(2):
        give(m).wait()

    for layer in range(2):

        @pl.when(section == layer)
        def _(layer=layer):
            pltpu.make_async_copy(tot.at[layer], v.at[section], v_sems.at[0]).wait()
            pltpu.make_async_remote_copy(
                src_ref=tot.at[layer], dst_ref=v.at[other], send_sem=v_sems.at[1], recv_sem=v_sems.at[2],
                device_id=sibling, device_id_type=MESH,
            ).wait_recv()

        @pl.when(section != layer)
        def _(layer=layer):
            v_across(layer).wait_send()

    own_part, far_part = v[section], v[other]
    first = jnp.where(section == 0, own_part, far_part)
    second = jnp.where(section == 0, far_part, own_part)
    for row, terms in ((0, (2, 3)), (1, (0, 1)), (2, (4,))):
        for lane, x in ((0, first), (W, second)):
            total = x[terms[0] : terms[0] + 1, :]
            for k in terms[1:]:
                total = total + x[k : k + 1, :]
            vectors[row : row + 1, lane : lane + W] = total
    squares = jnp.sum(first[5:7, :] + second[5:7, :], axis=1, keepdims=True)
    root = jnp.sqrt(squares / (first[7:8, 0:1] * width))
    for k in range(2):
        vectors[3 + k : 4 + k, :] = jnp.broadcast_to(root[k : k + 1], (1, 2 * W))
    vectors[5:8, :] = jnp.zeros((3, 2 * W), F32)


def write_results(o, gf, vectors, grad_weight, grad_frames, grad_gains, grad_shifts, grad_recurs, table):
    width = grad_weight.shape[2]
    grad_weight[0] = o[...][:, :width].astype(F32)
    grad_frames[...] = gf[...]

    @pl.when(pl.program_id(0) == 0)
    def _():
        for k, out in enumerate((grad_gains, grad_shifts, grad_recurs)):
            out[...] = vectors[k : k + 1, 0:width]
        table[...] = jnp.concatenate([vectors[3:4, 0:1], vectors[4:5, 0:1]], axis=1)


def results(o, gf, vectors):
    micro, steps, seqs, half = gf.shape
    width = 2 * half
    count = W * 2 // 256
    frames = micro * steps // count
    whole = lambda shape: pl.BlockSpec(shape, lambda i: (0, 0))
    out = pl.pallas_call(
        write_results,
        grid=(count,),
        in_specs=[
            pl.BlockSpec((256, 2 * W), lambda i: (i, 0)),
            pl.BlockSpec((frames, seqs, half), lambda i: (i, 0, 0)),
            whole((8, 2 * W)),
        ],
        out_specs=(
            pl.BlockSpec((1, 256, width), lambda i: (0, i, 0)),
            pl.BlockSpec((frames, seqs, half), lambda i: (i, 0, 0)),
            whole((1, width)),
            whole((1, width)),
            whole((1, width)),
            whole((1, 2)),
        ),
        out_shape=(
            jax.ShapeDtypeStruct((1, width, width), F32),
            jax.ShapeDtypeStruct((micro * steps, seqs, half), BF16),
            jax.ShapeDtypeStruct((1, width), F32),
            jax.ShapeDtypeStruct((1, width), F32),
            jax.ShapeDtypeStruct((1, width), F32),
            jax.ShapeDtypeStruct((1, 2), F32),
        ),
        compiler_params=pltpu.CompilerParams(vmem_limit_bytes=64 * 1024 * 1024),
    )(o.reshape(2 * W, 2 * W), gf.reshape(micro * steps, seqs, half), vectors)
    return out[1].reshape(gf.shape), out[0], *out[2:]


def whole_step(dims, frames, grad_out, weights, gains, shifts, recurs, lengths, masks):
    nz, ny, nx = dims
    micro, steps, seqs, half = frames.shape
    width = 2 * half
    views = seqs // lengths.shape[1]
    rows = micro * steps * seqs
    np_ = ny * nx
    wide_rows = (rows + 16 + 127) // 128 * 128
    depth = (nx * ny * nz - 1).bit_length()
    space_rows = W * 9 // 8 if nz == 4 else W
    any_ = pl.BlockSpec(memory_space=pl.ANY)
    held = pl.BlockSpec(memory_space=pltpu.VMEM)
    dma = pltpu.SemaphoreType.DMA
    return pl.pallas_call(
        functools.partial(kernel, dims, steps, seqs, views),
        out_shape=(
            jax.ShapeDtypeStruct((2, W, 2 * W), BF16),
            jax.ShapeDtypeStruct(frames.shape, BF16),
            jax.ShapeDtypeStruct((8, 2 * W), F32),
        ),
        in_specs=[any_] * 3 + [held] * 5,
        out_specs=(any_, any_, held),
        scratch_shapes=[
            pltpu.VMEM((wide_rows, W), BF16),
            pltpu.VMEM((rows, W), BF16),
            pltpu.VMEM((wide_rows, W), BF16),
            pltpu.VMEM((rows, W), BF16),
            pltpu.VMEM((2, wide_rows, W), BF16),
            pltpu.VMEM((2, 2, W, W), BF16),
            pltpu.VMEM((W, W), BF16),
            pltpu.VMEM((W, wide_rows), BF16),
            pltpu.VMEM((rows, 128), F32),
            pltpu.VMEM((128, 128), F32),
            pltpu.VMEM(frames.shape, BF16),
            pltpu.VMEM((micro, steps, seqs, 128), BF16),
            pltpu.VMEM((5, W, (width - W) % 128), BF16),
            pltpu.VMEM((2, 8, W), F32),
            pltpu.VMEM((2, 8, 2 * W), F32),
            pltpu.VMEM((2, rows, W), F32),
            pltpu.VMEM((2, rows, W), F32),
            pltpu.VMEM((2, 8, W), F32),
            pltpu.VMEM((2, 8, W), F32),
            pltpu.VMEM((2, 8, W), F32),
            pltpu.VMEM((8, W), F32),
            pltpu.VMEM((2, W, 128), BF16),
            pltpu.VMEM((8, 128), F32),
            pltpu.VMEM((1, np_, 8, 128), F32),
            pltpu.VMEM((1, nz, 8, 128), F32),
            pltpu.VMEM((4, np_, 8, QUART), F32),
            pltpu.VMEM((4, nz, 8, QUART), F32),
            pltpu.VMEM((2, np_, 8, W), F32),
            pltpu.VMEM((2, nz, 8, W), F32),
            pltpu.VMEM((2, 2 * PAIRS, space_rows, 2 * PART), BF16),
            dma((3, 25)),
            dma((3,)),
            dma((2,)),
            pltpu.SemaphoreType.REGULAR((2,)),
            dma((12, max(np_, 2))),
            dma((12, max(np_, 2))),
            dma((12, max(nz, 2))),
            dma((12, max(nz, 2))),
            dma((2, 2 * PAIRS, 2, 2 * depth + 2)),
            dma((2, 2 * PAIRS, 2, 2 * depth + 2)),
            dma((2, 2 * PAIRS, 2, 2)),
        ],
        compiler_params=pltpu.CompilerParams(
            collective_id=0, has_side_effects=True, vmem_limit_bytes=64 * 1024 * 1024
        ),
    )(frames, grad_out, weights, gains, shifts, recurs, lengths, masks)


def shards(dims, frames, grad_out, weights, gains, shifts, recurs, lengths, masks):
    return results(*whole_step(dims, frames, grad_out, weights, gains, shifts, recurs, lengths, masks))


def solution(mesh):
    in_specs = (
        P(None, None, "batch", "section"),
        P(None, None, "batch", "section"),
        P("section", None, None),
        P("section", None),
        P("section", None),
        P("section", None),
        P(None, "batch"),
        P(None, None, "batch"),
    )
    out_specs = (
        P(None, None, "batch", "section"),
        P("section", None, None),
        P("section", None),
        P("section", None),
        P("section", None),
        P("section", None),
    )
    body = functools.partial(shards, grid_of(mesh.shape["batch"]))
    return jax.shard_map(body, mesh=mesh, in_specs=in_specs, out_specs=out_specs, check_vma=False)
```

```python
import functools

import jax
import jax.numpy as jnp
from jax import lax
from jax.experimental import pallas as pl
from jax.experimental.pallas import tpu as pltpu
from jax.sharding import PartitionSpec as P

EPS = 1e-05
W = 1024
HALF = W // 2
QUART = W // 4
PAIRS = 2
PART = W // PAIRS // 2
MESH = pl.DeviceIdType.MESH
F32 = jnp.float32
BF16 = jnp.bfloat16


def grid_of(size):
    if size == 16:
        return (4, 2, 2)
    if size == 128:
        return (8, 4, 4)
    return (size, 1, 1)


def aligned(x, k):
    return pl.multiple_of(x, k)


def wide(x, reps):
    return jnp.concatenate([x] * reps, axis=1)


def fold(x):
    rows = x.shape[0]
    total = x[0:8]
    for k in range(8, rows, 8):
        total = total + x[k : k + 8]
    return total


def repeat(count, body, init, times):
    while count % times:
        times -= 1

    def several(i, carry):
        for j in range(times):
            carry = body(i * times + j, carry)
        return carry

    return lax.fori_loop(0, count // times, several, init)


def dot(a, b, dims):
    return lax.dot_general(a, b, (dims, ((), ())), preferred_element_type=F32)


class Reduction:
    def __init__(self, env, layer, index, block, orders, lane_of):
        self.env, self.layer, self.index, self.block, self.orders = env, layer, index, block, orders
        self.lane_of = lane_of
        self.space = env["space"].at[layer, index]
        self.depth = len(orders[0])
        self.regions = [self.shares(i, order) for i, order in enumerate(orders)]
        self.step = 0
        self.waits = []
        self.slot = [0, 0]
        depth = self.depth
        self.steps = [functools.partial(self.scatter, k) for k in range(depth)]
        self.steps += [functools.partial(self.gather, k) for k in range(depth - 1, 0, -1)]
        self.steps += [self.give, self.finish]

    def shares(self, i, order):
        out = [(0, W, i * PART, PART)]
        for axis in order:
            out.append(self.share(out[-1], axis, axis["index"]))
        return out

    def share(self, region, axis, index):
        row, rows, lane, lanes = region
        by_row = min(axis["size"], rows // 16)
        rows, lanes = rows // by_row, lanes // (axis["size"] // by_row)
        if by_row == axis["size"]:
            return row + index * rows, rows, lane, lanes
        return row + lax.rem(index, by_row) * rows, rows, lane + index // by_row * lanes, lanes

    @property
    def free_to_go(self):
        return self.step != self.depth or self.layer in self.env["summed"]

    @property
    def done(self):
        return self.step >= len(self.steps)

    def advance(self):
        self.sent = []
        self.steps[self.step]()
        self.step += 1
        return self.sent

    def remote(self, i, src, dst, slot, where, recv=None):
        sems = (self.layer, self.index, i, slot)
        return pltpu.make_async_remote_copy(
            src_ref=src, dst_ref=dst, send_sem=self.env["ar_send"].at[sems],
            recv_sem=self.env["ar_recv"].at[sems] if recv is None else recv, device_id=where, device_id_type=MESH,
        )

    def wait(self):
        for made, came in self.waits:
            made.wait_send()
            came.wait_recv()
        self.waits = []

    def take(self, i):
        self.slot[i] += 1
        return self.slot[i] - 1

    def came_at(self, i, k, s):
        row = sum((a["size"] - 1) * self.regions[i][n + 1][1] for n, a in enumerate(self.orders[i][:k]))
        _, rows, _, lanes = self.regions[i][k + 1]
        return row + (s - 1) * rows, rows, i * PART, lanes

    def scatter(self, k):
        if k > 0:
            self.wait()
            self.add(k - 1)
        for i in range(2):
            self.scatter_part(i, k)

    def start_part(self, i):
        self.sent = []
        self.scatter_part(i, 0)
        if i == 1:
            self.step = 1
        return self.sent

    def scatter_part(self, i, k):
        axis = self.orders[i][k]
        for s in range(1, axis["size"]):
            other = lax.rem(axis["index"] + s, axis["size"])
            row, rows, lane, lanes = self.share(self.regions[i][k], axis, other)
            src = self.block.at[pl.ds(aligned(row, 16), rows), pl.ds(aligned(lane, 128), lanes)]
            at, n, at_lane, n_lanes = self.came_at(i, k, s)
            dst = self.space.at[pl.ds(at, n), pl.ds(at_lane, n_lanes)]
            made = self.remote(i, src, dst, self.take(i), axis["at"](other))
            made.start()
            self.waits.append((made, made))
            self.sent.append((axis["link"], rows * lanes * 2))

    def add(self, k, last=False):
        rows = self.regions[0][k + 1][1]
        size = min(rows, 128)
        out = []
        for i in range(2):
            row, _, lane, lanes = self.regions[i][k + 1]
            lane = aligned(lane, 128)
            extra = None
            if last:
                part = self.index // PAIRS
                first = aligned((self.index % PAIRS) * 2 * PART + lane, 128)
                extra = self.env["vtot"][self.layer, part, 0:1, pl.ds(first, lanes)]
            came = [self.came_at(i, k, s) for s in range(1, self.orders[i][k]["size"])]
            out.append((row, lane, lanes, came, self.local(i, self.regions[i][k + 1])[0], extra))

        def body(j, _):
            for row, lane, lanes, came, home, extra in out:
                here = pl.ds(aligned(row + j * size, 16), size)
                total = self.block[here, pl.ds(lane, lanes)].astype(F32)
                for at, _, at_lane, _ in came:
                    there = pl.ds(aligned(at + j * size, 16), size)
                    total = total + self.space[there, pl.ds(at_lane, lanes)].astype(F32)
                if last:
                    column = self.env["column"][self.layer, here, :].astype(F32)
                    total = total + wide(column, lanes // 128) * extra
                    to = pl.ds(aligned(home + j * size, 16), size)
                    self.space[to, pl.ds(lane, lanes)] = total.astype(BF16)
                else:
                    self.block[here, pl.ds(lane, lanes)] = total.astype(BF16)
            return 0

        lax.fori_loop(0, rows // size, body, 0)

    def local(self, i, region):
        row, rows, lane, lanes = region
        return row - self.regions[i][1][0], rows, lane, lanes

    def gather(self, k):
        self.wait()
        if k == self.depth - 1:
            self.add(k, last=True)

        def ref(i, region):
            row, rows, lane, lanes = self.local(i, region)
            return self.space.at[pl.ds(aligned(row, 16), rows), pl.ds(aligned(lane, 128), lanes)]

        for i, order in enumerate(self.orders):
            axis = order[k]
            mine = ref(i, self.regions[i][k + 1])
            for s in range(1, axis["size"]):
                to = lax.rem(axis["index"] + s, axis["size"])
                frm = lax.rem(axis["index"] + axis["size"] - s, axis["size"])
                slot = self.take(i)
                made = self.remote(i, mine, mine, slot, axis["at"](to))
                made.start()
                theirs = ref(i, self.share(self.regions[i][k], axis, frm))
                self.waits.append((made, self.remote(i, theirs, theirs, slot, axis["at"](frm))))
                self.sent.append((axis["link"], self.regions[i][k + 1][1] * self.regions[i][k + 1][3] * 2))

    def result(self, i, index, section):
        rows = self.regions[i][1][1]
        lane = aligned(self.lane_of(section) + i * PART, PART)
        return self.env["o"].at[section, pl.ds(aligned(index * rows, 16), rows), pl.ds(lane, PART)]

    def gathered(self, i):
        return self.space.at[pl.ds(0, self.regions[i][1][1]), pl.ds(i * PART, PART)]

    def deliver(self, i, s, straight):
        axis, section = self.orders[i][0], self.env["section"]
        recv = None if straight else self.env["ar_other"].at[self.layer, self.index, i, s]
        where = dict(axis["at"](lax.rem(axis["index"] + s, axis["size"])), section=self.layer)
        target = self.result(i, axis["index"], section)
        return self.remote(i, self.gathered(i), target, self.slot[i] + s, where, recv)

    def arrival(self, i, s, straight):
        axis, section = self.orders[i][0], self.env["section"]
        recv = None if straight else self.env["ar_other"].at[self.layer, self.index, i, s]
        index = lax.rem(axis["index"] + axis["size"] - s, axis["size"])
        frm = section if straight else 1 - section
        where = dict(axis["at"](index), section=frm)
        return self.remote(i, self.gathered(i), self.result(i, index, frm), self.slot[i] + s, where, recv)

    def kept(self, i):
        sem = self.env["ar_recv"].at[self.layer, self.index, i, self.slot[i]]
        target = self.result(i, self.orders[i][0]["index"], self.env["section"])
        return pltpu.make_async_copy(self.gathered(i), target, sem)

    def give(self):
        self.wait()

        @pl.when(self.env["section"] == self.layer)
        def _():
            for i in range(2):
                for s in range(1, self.orders[i][0]["size"]):
                    self.deliver(i, s, True).start()
                self.kept(i).start()

        @pl.when(self.env["section"] != self.layer)
        def _():
            for i in range(2):
                for s in range(self.orders[i][0]["size"] - 1, -1, -1):
                    self.deliver(i, s, False).start()

        for i, order in enumerate(self.orders):
            self.sent.append((order[0]["link"], self.regions[i][1][1] * PART * 2 * (order[0]["size"] - 1)))

    def finish(self):
        @pl.when(self.env["section"] == self.layer)
        def _():
            for i in range(2):
                size = self.orders[i][0]["size"]
                self.kept(i).wait()
                for s in range(1, size):
                    self.deliver(i, s, True).wait_send()
                    self.arrival(i, s, True).wait_recv()
                for s in range(size):
                    self.arrival(i, s, False).wait_recv()

        @pl.when(self.env["section"] != self.layer)
        def _():
            for i in range(2):
                for s in range(self.orders[i][0]["size"]):
                    self.deliver(i, s, False).wait_send()


class Order:
    RATE, HOP, QUEUE = 52e3, 2.2, 1e9

    def __init__(self):
        self.now = 0.0
        self.free = {}
        self.going = []
        self.held = []

    def sent(self, copies):
        end = self.now
        for link, size in copies:
            self.free[link] = max(self.now, self.free.get(link, 0.0)) + size / self.RATE
            end = max(end, self.free[link])
        return end + self.HOP

    def begin(self, one, i):
        self.held.append((one, i))
        self.release()

    def release(self, always=False):
        while self.held and (always or self.busy() < self.QUEUE):
            one, i = self.held.pop(0)
            end = self.sent(one.start_part(i))
            if i == 0:
                one.due = end
            else:
                one.due = max(one.due, end)
                self.going.append(one)

    def busy(self):
        link = self.held[0][0].orders[self.held[0][1]][:1]
        return max([self.free.get(a["link"], 0.0) - self.now for a in link], default=0.0)

    def advance(self, one):
        self.now = max(self.now, one.due) + 0.4
        one.due = self.sent(one.advance())
        if one.done:
            self.going.remove(one)

    def work(self, cost):
        self.now += cost
        while True:
            self.release()
            due = [x for x in self.going if x.due <= self.now and x.free_to_go]
            if not due:
                return
            self.advance(min(due, key=lambda x: x.due))

    def drain(self):
        while self.going or self.held:
            self.release(always=not self.going)
            self.advance(min(self.going, key=lambda x: x.due))


def kernel(dims, steps, seqs, views, frames, grad_out, weights, gains, shifts, recurs, lengths, masks, o, gf, vectors, f_own, f_far, p_own, p_far, g3, wc, wr1, src_t, live, turn,
           staged, heads, tails, v, vecs, rows, hid, coef, tot, vtot, levels, column, counts, cnt_p, cnt_z, slim_p, slim_z,
           wide_p, wide_z, space, sems, v_sems, stage_sem, credit, pl_send, pl_recv, z_send, z_recv, ar_send, ar_recv,
           ar_other):
    nz, ny, nx = dims
    np_ = ny * nx
    span = steps * seqs
    total_rows = 2 * span
    sent_rows = total_rows + 16
    pairs = steps // 2
    section = lax.axis_index("section")
    other = 1 - section
    b = lax.axis_index("batch")
    mp = lax.rem(b, np_)
    mz = b // np_

    def at_plane(i):
        return {"batch": b - mp + i}

    def at_z(i):
        return {"batch": b + (i - mz) * np_}

    def axis_of(link, size, stride):
        index = lax.rem(b // stride, size)
        return dict(link=link, size=size, index=index, at=lambda i: {"batch": b + (i - index) * stride})

    def halvings(link, size, stride):
        out = []
        while size > 1:
            out.append(axis_of(link, 2, stride))
            size //= 2
            stride *= 2
        return out

    xs, ys, zs = halvings("x", nx, 1), halvings("y", ny, nx), halvings("z", nz, np_)
    orders = (xs + ys + zs, ys + xs + zs)
    sibling = {"section": other}

    def local(src, dst, slot):
        return pltpu.make_async_copy(src, dst, sems.at[0, slot])

    def across(src, dst, slot):
        return pltpu.make_async_remote_copy(
            src_ref=src, dst_ref=dst, send_sem=sems.at[1, slot], recv_sem=sems.at[2, slot],
            device_id=sibling, device_id_type=MESH,
        )

    half = frames.shape[3]
    width = 2 * half
    lead = W - half
    rest = width - W
    full = rest // 128 * 128

    def fetch(source, m):
        return pltpu.make_async_copy(source.at[m], staged.at[m], stage_sem.at[m])

    def by_units(source, target, m):
        fetch(source, m).wait()

        @pl.when(section == 0)
        def _():
            pad = jnp.zeros((2 * seqs, lead), F32)

            def place(i, _):
                x = staged[m, pl.ds(2 * i, 2)].astype(F32).reshape(2 * seqs, half)
                to = pl.ds(aligned(m * span + 2 * i * seqs, 16), 2 * seqs)
                target[to, :] = jnp.concatenate([x, pad], axis=1).astype(BF16)
                return 0

            repeat(pairs, place, 0, 3)

        @pl.when(section == 1)
        def _():
            pad = jnp.zeros((2 * seqs, 2 * lead), F32)

            def place(i, _):
                x = staged[m, pl.ds(2 * i, 2)].astype(F32).reshape(2 * seqs, half)
                to = pl.ds(aligned(m * span + 2 * i * seqs, 16), 2 * seqs)
                target[to, :] = jnp.concatenate([x[:, lead:], pad], axis=1).astype(BF16)
                return 0

            repeat(pairs, place, 0, 3)

    def patch_heads(target, m):
        @pl.when(section == 0)
        def _():
            lane = lax.broadcasted_iota(jnp.int32, (2 * seqs, 128), 1)

            def place(i, _):
                to = pl.ds(aligned(m * span + 2 * i * seqs, 16), 2 * seqs)
                head = heads[m, pl.ds(2 * i, 2)].astype(F32).reshape(2 * seqs, 128)
                head = pltpu.roll(head, 128 - lead, 1)
                old = target[to, W - 128 :].astype(F32)
                target[to, W - 128 :] = jnp.where(lane < 128 - lead, old, head).astype(BF16)
                return 0

            repeat(pairs, place, 0, 3)

    def pieces(row, count, u, block, spot):
        r = pl.ds(row, count)
        to = pl.ds(0, count)
        if u == 0:
            return [(weights.at[0, r, pl.ds(0, W)], block.at[to, :])]
        return [
            (weights.at[0, r, pl.ds(W, full)], block.at[to, pl.ds(0, full)]),
            (weights.at[0, r, pl.ds(W + full, rest - full)], tails.at[spot, to, :]),
        ]

    rows_of = {0: (0, W), 1: (W, rest)}

    def w_plan(layer):
        mine, far = rows_of[layer], rows_of[1 - layer]
        plan = [
            (mine, layer, far, 1 - layer, wc.at[layer, 0], 2 * layer),
            (far, layer, mine, 1 - layer, wc.at[layer, 1], 2 * layer + 1),
        ]
        if layer == 1:
            plan.append((mine, 0, far, 1, wr1, 4))
        return plan

    late_row = (width - half) // 16 * 16
    late_shift = half - late_row
    late_plan = [
        ((0, W), 0, (late_row, width - late_row), 1, wc.at[0, 0], 0),
        ((0, W), 1, (late_row, width - late_row), 0, wc.at[0, 1], 1),
    ]
    slot_of = {0: 4, 1: 8, 2: 14}

    def local_w(plan, base, which):
        r, u, _, _, block, spot = plan[which]
        return [local(a, t, base + 2 * which + i) for i, (a, t) in enumerate(pieces(*r, u, block, spot))]

    def across_w(plan, base, which):
        _, _, r, u, block, spot = plan[which]
        return [across(a, t, base + 2 * which + i) for i, (a, t) in enumerate(pieces(*r, u, block, spot))]

    def start_local_w(layer, plan, base):
        @pl.when(section == layer)
        def _():
            for which in range(len(plan)):
                for made in local_w(plan, base, which):
                    made.start()

    def start_across_w(layer, plan, base):
        @pl.when(section == layer)
        def _():
            for which in range(len(plan)):
                for made in across_w(plan, base, which):
                    made.start()

    def last_units(block, spot):
        def body(i, _):
            r = pl.ds(aligned(i * 128, 128), 128)
            x = tails[spot, r, :].astype(F32)
            x = jnp.concatenate([x, jnp.zeros((128, 128 - x.shape[1]), F32)], axis=1)
            block[r, full:] = x.astype(BF16)
            return 0

        lax.fori_loop(0, W // 128, body, 0)

    def wait_w(layer, plan, base, which):
        _, own_u, _, far_u, block, spot = plan[which]

        @pl.when(section == layer)
        def _():
            for made in local_w(plan, base, which):
                made.wait()
            if own_u == 1:
                last_units(block, spot)

        @pl.when(section != layer)
        def _():
            for made in across_w(plan, base, which):
                made.wait_recv()
            if far_u == 1:
                last_units(block, spot)

    def done_w(layer, plan, base):
        @pl.when(section == layer)
        def _():
            for which in range(len(plan)):
                for made in across_w(plan, base, which):
                    made.wait_send()

    def heads_copy(source, slot):
        return across(source.at[:, :, :, pl.ds(0, 128)], heads, slot)

    def wait_heads(source, slot):
        @pl.when(section == 0)
        def _():
            heads_copy(source, slot).wait_recv()

        @pl.when(section == 1)
        def _():
            heads_copy(source, slot).wait_send()

    fetch(frames, 0).start()
    fetch(frames, 1).start()
    for layer in range(2):
        start_local_w(layer, w_plan(layer), slot_of[layer])

    barrier = pltpu.get_barrier_semaphore()
    greeted = [dict(sibling)]
    greeted += [at_plane(lax.rem(mp + k, np_)) for k in range(1, np_)]
    greeted += [at_z(lax.rem(mz + k, nz)) for k in range(1, nz)]
    for axis in (xs + zs)[:1] + (ys + zs)[:1]:
        for s in range(1, axis["size"]):
            greeted.append(dict(axis["at"](lax.rem(axis["index"] + s, axis["size"])), section=other))
    for where in greeted:
        pl.semaphore_signal(barrier, inc=1, device_id=where, device_id_type=MESH)

    for k, (x, fill) in enumerate(((gains, 0.0), (shifts, -1e30), (recurs, 0.0))):
        vecs[section, k : k + 1, 0:width] = x[...]
        vecs[section, k : k + 1, width:] = jnp.full((1, 2 * W - width), fill, F32)
    vecs[section, 3:8, :] = jnp.zeros((5, 2 * W), F32)

    gap = jnp.zeros((W - rest, W), BF16)

    @pl.when(section == 0)
    def _():
        wc[0, 1, rest:, :] = gap
        wc[1, 1, rest:, :] = gap

    @pl.when(section == 1)
    def _():
        wc[0, 0, rest:, :] = gap
        wc[1, 0, rest:, :] = gap
        wr1[rest:, :] = gap

    for spot in (0, 2):
        tails[spot, rest:, :] = jnp.zeros((W - rest, rest - full), BF16)
    for spare in (f_own, p_own, g3.at[0], g3.at[1]):
        spare[sent_rows:, :] = jnp.zeros((spare.shape[0] - sent_rows, W), BF16)

    pl.semaphore_wait(barrier, len(greeted))

    @pl.when(section == 1)
    def _():
        heads_copy(frames, 1).start()

    start_across_w(0, w_plan(0), slot_of[0])
    send_vec = across(vecs.at[section], vecs.at[section], 3)
    send_vec.start()

    def stage_copy(where, rnd, slot, k, back):
        buf, parity, size, me, at, send, recv = where
        there = at(lax.rem(me + (size - k if back else k), size))
        ref = buf.at[parity, slot]
        return pltpu.make_async_remote_copy(
            src_ref=ref, dst_ref=ref, send_sem=send.at[rnd, k], recv_sem=recv.at[rnd, k],
            device_id=there, device_id_type=MESH,
        )

    def in_plane(buf, parity):
        return (buf, parity, np_, mp, at_plane, pl_send, pl_recv)

    def in_line(buf, parity):
        return (buf, parity, nz, mz, at_z, z_send, z_recv)

    def stage_start(where, rnd, value):
        buf, parity, size, me = where[:4]
        buf[parity, me] = value
        for k in range(1, size):
            stage_copy(where, rnd, me, k, False).start()

    def stage_wait(where, rnd):
        size, me = where[2:4]
        for k in range(1, size):
            stage_copy(where, rnd, me, k, False).wait_send()
            stage_copy(where, rnd, lax.rem(me + size - k, size), k, True).wait_recv()

    def add_slots(where):
        buf, parity, size = where[:3]
        total = buf[parity, 0]
        for k in range(1, size):
            total = total + buf[parity, k]
        return total

    groups = lengths.shape[1]
    s_at = lax.broadcasted_iota(jnp.int32, (seqs, groups), 0)
    g_at = lax.broadcasted_iota(jnp.int32, (seqs, groups), 1) * views
    there = (s_at >= g_at) & (s_at < g_at + views)
    position = lax.broadcasted_iota(jnp.int32, (seqs, 128), 1)
    local_counts = []
    for m in range(2):
        turn[...] = jnp.zeros_like(turn)
        turn[0:steps, 0:seqs] = masks[m].astype(F32)
        mask = turn[...].T[0:seqs]
        length = jnp.broadcast_to(lengths[m : m + 1, :], (seqs, groups)).astype(F32)
        limit = jnp.sum(jnp.where(there, length, 0.0), axis=1, keepdims=True)
        alive = (position.astype(F32) < limit) & ((mask > 0.0) | (position == 0))
        alive = jnp.where(position < steps, alive.astype(F32), 0.0)
        total = jnp.zeros((seqs, 128), F32)
        for t in range(steps):
            at = m * span + t * seqs
            cells = jnp.broadcast_to(alive[:, t : t + 1], (seqs, 128))
            live[at : at + seqs, :] = cells
            total = total + cells
        local_counts.append(jnp.sum(total, axis=0, keepdims=True))
    n_own = jnp.concatenate([local_counts[0]] * 2 + [local_counts[1]] * 2, axis=0)
    n_own = jnp.concatenate([n_own, n_own], axis=0)

    cnt_plane, cnt_line = in_plane(cnt_p, 0), in_line(cnt_z, 0)
    stage_start(cnt_plane, 0, n_own)

    def vec_of(layer, k, lh):
        return vecs[layer, k : k + 1, pl.ds(aligned(section * W + lh * HALF, HALF), HALF)]

    def half_of(lh):
        return slice(lh * HALF, (lh + 1) * HALF)

    def matmul_to(out, a, w, first, lh):
        lanes = half_of(lh)

        def body(m, _):
            r = pl.ds(aligned(m * span, 16), span)
            y = dot(a[r, :], w[:, lanes], ((1,), (0,)))
            out[r, lanes] = y if first else out[r, lanes] + y
            return 0

        lax.fori_loop(0, 2, body, 0)

    def packed(x, y):
        return jnp.concatenate([z[:, k * QUART : (k + 1) * QUART] for z in (*x, *y) for k in range(2)], axis=0)

    def unpacked(x, m):
        return jnp.concatenate([x[2 * m + k : 2 * m + k + 1] for k in range(2)], axis=1)

    def merge_slots(where, counts_of):
        buf, parity, size = where[:3]
        s = [buf[parity, k, 0:4, :] for k in range(size)]
        q = [buf[parity, k, 4:8, :] for k in range(size)]
        n = [wide(counts_of(k), 2) for k in range(size)]
        total, squares, count = sum(s[1:], s[0]), sum(q[1:], q[0]), sum(n[1:], n[0])
        mean = total / count
        for k in range(size):
            d = s[k] / n[k] - mean
            squares = squares + n[k] * d * d
        return jnp.concatenate([total, squares], axis=0)

    def slim_round(which, lh):
        return 1 + 2 * which + lh, in_plane(slim_p, 2 * lh + which % 2), in_line(slim_z, 2 * lh + which % 2)

    def forward_stats(layer, lh):
        lanes = half_of(lh)
        sums, squares = [], []
        for m in range(2):
            start = jnp.sum(rows[layer, m * span : m * span + seqs, lanes], axis=0, keepdims=True) * (1.0 / seqs)

            def body(i, carry):
                s, q = carry
                r = pl.ds(aligned(m * span + i * (2 * seqs), 16), 2 * seqs)
                d = rows[layer, r, lanes] - start
                kept = wide(live[r, :], 4) * d
                return s + fold(kept), q + fold(kept * d)

            zero = jnp.zeros((8, HALF), F32)
            s, q = repeat(pairs, body, (zero, zero), 4)
            s, q = jnp.sum(s, axis=0, keepdims=True), jnp.sum(q, axis=0, keepdims=True)
            n = wide(local_counts[m], 4)
            sums.append(s + n * start)
            squares.append(jnp.maximum(q - s * s / n, 0.0))
        rnd, plane, _ = slim_round(layer, lh)
        stage_start(plane, rnd, packed(sums, squares))

    def forward_middle(layer, lh):
        rnd, plane, line = slim_round(layer, lh)
        stage_wait(plane, rnd)
        stage_start(line, rnd, merge_slots(plane, lambda k: cnt_p[0, k, 0:4, :]))

    def forward_end(layer, lh):
        rnd, _, line = slim_round(layer, lh)
        lanes = half_of(lh)
        stage_wait(line, rnd)
        value = merge_slots(line, lambda k: cnt_z[0, k, 0:4, :])
        for m in range(2):
            count = wide(counts[2 * m : 2 * m + 1, :], 4)
            mean = unpacked(value[0:4], m) / count
            scale = lax.rsqrt(unpacked(value[4:8], m) / count + EPS)
            coef[layer, 2 * m : 2 * m + 1, lanes] = mean
            coef[layer, 2 * m + 1 : 2 * m + 2, lanes] = scale
            slope = vec_of(layer, 0, lh) * scale
            coef[layer, 4 + 2 * m : 5 + 2 * m, lanes] = slope
            coef[layer, 5 + 2 * m : 6 + 2 * m, lanes] = vec_of(layer, 1, lh) - mean * slope

    def forward_scan(layer, lh, passes):
        lanes = half_of(lh)
        rec = vec_of(layer, 2, lh)
        slope = [coef[layer, 4 + 2 * m : 5 + 2 * m, lanes] for m in range(2)]
        shift = [coef[layer, 5 + 2 * m : 6 + 2 * m, lanes] for m in range(2)]

        def body(i, carry):
            states, level = carry
            out = []
            for m in range(2):
                r = pl.ds(aligned(m * span + i * (2 * seqs), 16), 2 * seqs)
                x = rows[layer, r, lanes] * slope[m] + shift[m]
                lv = wide(live[r, :], 4)
                alive = lv > 0.0
                h = states[m]
                both = []
                for k in range(2):
                    part = slice(k * seqs, (k + 1) * seqs)
                    z = x[part] + rec * h
                    soft = jnp.maximum(z, 0.0) + jnp.log(1.0 + jnp.exp(-jnp.abs(z)))
                    h = jnp.where(alive[part], soft, h)
                    both.append(h)
                two = jnp.concatenate(both, axis=0)
                hid[layer, r, lanes] = two
                if passes:
                    p_own[r, lanes] = two.astype(BF16)
                    level = level + fold(lv * two)
                out.append(h)
            return tuple(out), level

        zero = jnp.zeros((seqs, HALF), F32)
        _, level = repeat(pairs, body, ((zero, zero), jnp.zeros((8, HALF), F32)), 2)
        if not passes:
            return None
        levels[1:2, lanes] = jnp.sum(level, axis=0, keepdims=True)
        made = across(p_own.at[pl.ds(0, total_rows), lanes], p_far.at[:, lanes], 18 + lh)
        made.start()
        return made

    def backward_scan(layer, lh, above, between=lambda: None):
        for lq in range(2 * lh, 2 * lh + 2):
            lanes = slice(lq * QUART, (lq + 1) * QUART)
            gq, sq, rec = (vec_of(layer, k, lh)[:, (lq % 2) * QUART : (lq % 2 + 1) * QUART] for k in range(3))
            mean = [coef[layer, 2 * m : 2 * m + 1, lanes] for m in range(2)]
            scale = [coef[layer, 2 * m + 1 : 2 * m + 2, lanes] for m in range(2)]

            def body(i, carry):
                down, s1, s2, rsum, sqh, sqa = carry
                down, s1, s2 = list(down), list(s1), list(s2)
                i = pairs - 1 - i
                for m in range(2):
                    start = m * span + i * (2 * seqs)
                    r = pl.ds(aligned(start, 16), 2 * seqs)
                    before = pl.ds(aligned(jnp.maximum(start - seqs, 0), 8), seqs)
                    normed = (rows[layer, r, lanes] - mean[m]) * scale[m]
                    drive = gq * normed + sq
                    h2 = hid[layer, r, lanes]
                    hb = jnp.where(i > 0, hid[layer, before, lanes], 0.0)
                    lv = wide(live[r, :], 2)
                    up = above[r, lanes].astype(F32)
                    res = f_own[r, lanes].astype(F32)
                    aux = res + h2 if layer == 1 else res
                    sqh = sqh + fold(lv * (h2 * h2))
                    sqa = sqa + fold(lv * (aux * aux))
                    grads = [None, None]
                    for k in (1, 0):
                        part = slice(k * seqs, (k + 1) * seqs)
                        prior = h2[0:seqs] if k == 1 else hb
                        slope = 0.5 + 0.5 * jnp.tanh(0.5 * (drive[part] + rec * prior))
                        total = up[part] + down[m]
                        gd = lv[part] * slope * total
                        down[m] = (1.0 - lv[part]) * total + rec * gd
                        grads[k] = gd
                        rsum = rsum + fold(gd * prior)
                    gd2 = jnp.concatenate(grads, axis=0)
                    hid[layer, r, lanes] = gd2
                    s1[m] = s1[m] + fold(gd2)
                    s2[m] = s2[m] + fold(gd2 * normed)
                return tuple(down), tuple(s1), tuple(s2), rsum, sqh, sqa

            zero = jnp.zeros((seqs, QUART), F32)
            z8 = jnp.zeros((8, QUART), F32)
            _, s1, s2, rsum, sqh, sqa = repeat(
                pairs, body, ((zero, zero), (z8, z8), (z8, z8), z8, z8, z8), 2
            )
            for k, x in enumerate((s1[0], s1[1], s2[0], s2[1], rsum, sqh, sqa)):
                tot[layer, k : k + 1, lanes] = jnp.sum(x, axis=0, keepdims=True)
            between()

    def backward_stats(layer, lh):
        rnd, plane, _ = slim_round(3 - layer, lh)
        t = tot[layer, 0:4, half_of(lh)]
        stage_start(plane, rnd, packed([t[0:1], t[1:2]], [t[2:3], t[3:4]]))

    def backward_middle(layer, lh):
        rnd, plane, line = slim_round(3 - layer, lh)
        stage_wait(plane, rnd)
        stage_start(line, rnd, add_slots(plane))

    def backward_end(layer, lh):
        rnd, _, line = slim_round(3 - layer, lh)
        stage_wait(line, rnd)
        value = add_slots(line)
        for m in range(2):
            tot[layer, m : m + 1, half_of(lh)] = unpacked(value[0:4], m)
            tot[layer, 2 + m : 3 + m, half_of(lh)] = unpacked(value[4:8], m)

    def grad_rows(layer, lh, slot):
        lanes = half_of(lh)
        acc = jnp.zeros((8, HALF), F32)
        for m in range(2):
            mean = coef[layer, 2 * m : 2 * m + 1, lanes]
            scale = coef[layer, 2 * m + 1 : 2 * m + 2, lanes]
            count = wide(counts[2 * m : 2 * m + 1, :], 4)
            first = tot[layer, m : m + 1, lanes] / count
            second = tot[layer, 2 + m : 3 + m, lanes] / count * scale
            k = coef[layer, 4 + 2 * m : 5 + 2 * m, lanes]

            def body(i, acc):
                r = pl.ds(aligned(m * span + i * (2 * seqs), 16), 2 * seqs)
                y = hid[layer, r, lanes] - first - (rows[layer, r, lanes] - mean) * second
                y = wide(live[r, :], 4) * (k * y)
                g3[0, r, lanes] = y.astype(BF16)
                return acc + fold(y)

            acc = repeat(pairs, body, acc, 4)
        top = lax.broadcasted_iota(jnp.int32, (16, HALF), 0) == 0
        minus = jnp.where(top, -jnp.sum(acc, axis=0, keepdims=True), 0.0)
        g3[0, total_rows:sent_rows, lanes] = minus.astype(BF16)
        made = across(g3.at[0, pl.ds(0, sent_rows), lanes], g3.at[1, pl.ds(0, sent_rows), lanes], slot + lh)
        made.start()
        return made

    sums_round = {1: (1, 10), 0: (0, 11)}

    def sums_start(layer):
        parity, rnd = sums_round[layer]
        own_sum = -g3[0, total_rows:sent_rows, :].astype(F32)[0:1]
        value = jnp.concatenate([own_sum, tot[layer, 4:7, :], jnp.zeros((4, W), F32)], axis=0)
        stage_start(in_plane(wide_p, parity), rnd, value)

    def sums_middle(layer):
        parity, rnd = sums_round[layer]
        stage_wait(in_plane(wide_p, parity), rnd)
        stage_start(in_line(wide_z, parity), rnd, add_slots(in_plane(wide_p, parity)))

    def swap_sums(layer):
        return across(vtot.at[layer, 0], vtot.at[layer, 1], 25 + layer)

    def sums_end(layer):
        parity, rnd = sums_round[layer]
        stage_wait(in_line(wide_z, parity), rnd)
        vtot[layer, 0] = add_slots(in_line(wide_z, parity))
        swap_sums(layer).start()
        tot[layer, 4:7, :] = vtot[layer, 0, 1:4, :]
        tot[layer, 7:8, :] = wide(counts[0:1, :] + counts[2:3, :], 8)

        @pl.when(section == layer)
        def _():
            pltpu.make_async_copy(tot.at[layer], v.at[section], v_sems.at[0]).start()

        @pl.when(section != layer)
        def _():
            v_across(layer).start()

    def sums_there(layer):
        swap_sums(layer).wait()
        env["summed"].add(layer)

    def v_across(layer):
        return pltpu.make_async_remote_copy(
            src_ref=tot.at[layer], dst_ref=v.at[section], send_sem=v_sems.at[1], recv_sem=v_sems.at[2],
            device_id=sibling, device_id_type=MESH,
        )

    def transpose(src, begin=0, end=W // 128):
        def body(j, _):
            c = pl.ds(aligned(j * 128, 128), 128)
            src_t[c, 0:total_rows] = src[0:total_rows, c].T
            return 0

        lax.fori_loop(begin, end, body, 0)

    def transpose_level(src, layer):
        top = lax.broadcasted_iota(jnp.int32, (16, W), 0) == 0
        src[total_rows:sent_rows, :] = jnp.where(top, levels[2 + layer : 3 + layer, :], 0.0).astype(BF16)

        def body(j, _):
            c = pl.ds(aligned(j * 128, 128), 128)
            src_t[c, total_rows:] = src[total_rows:, c].T
            level = src[total_rows:sent_rows, c].astype(F32)[0:1]
            column[layer, c, :] = jnp.broadcast_to(level, (128, 128)).T.astype(BF16)
            return 0

        lax.fori_loop(0, W // 128, body, 0)

    def weight_part(block, grads, c):
        lanes = pl.ds(c * HALF, HALF)

        def body(j, _):
            r = pl.ds(aligned(j * HALF, HALF), HALF)
            block[r, lanes] = dot(src_t[r, :], grads[:, lanes], ((1,), (0,))).astype(BF16)
            return 0

        lax.fori_loop(0, W // HALF, body, 0)

    def source_grad(store, w_own, w_far, half_index):
        c = half_of(half_index)

        def body(m, _):
            r = pl.ds(aligned(m * span, 16), span)
            y = dot(g3[0, r, :], w_own[c, :], ((1,), (1,))) + dot(g3[1, r, :], w_far[c, :], ((1,), (1,)))
            store(r, c, y)
            return 0

        lax.fori_loop(0, 2, body, 0)

    env = dict(summed=set(), vtot=vtot, column=column, space=space, ar_send=ar_send, ar_recv=ar_recv,
               ar_other=ar_other, o=o, section=section, here={"batch": b})
    blocks = {
        (1, 0): f_far.at[pl.ds(0, W), :],
        (1, 1): p_far.at[pl.ds(0, W), :],
        (0, 0): wc.at[1, 1],
        (0, 1): wr1,
    }
    parts = {}
    for layer in (1, 0):
        for index in range(2 * PAIRS):
            part, side = index // PAIRS, index % PAIRS

            def lane_of(sec, part=part, side=side):
                return (sec if part == 0 else 1 - sec) * W + side * 2 * PART

            block = blocks[layer, part].at[:, pl.ds(side * 2 * PART, 2 * PART)]
            parts[layer, index] = Reduction(env, layer, index, block, orders, lane_of)
    order = Order()

    def weight_grads(layer, part, c):
        weight_part(blocks[layer, part], g3.at[part], c)
        order.work(2.8)
        for k in range(c * HALF // PART, (c + 1) * HALF // PART):
            order.begin(parts[layer, part * PAIRS + k // 2], k % 2)

    def arrived(sends):
        for made in sends:
            made.wait()

    send_f = []
    for m in range(2):
        by_units(frames, f_own, m)
        fetch(grad_out, m).start()
        if m == 0:
            wait_heads(frames, 1)
        patch_heads(f_own, m)
        here = pl.ds(m * span, span)
        made = across(f_own.at[here, :], f_far.at[here, :], (0, 24)[m])
        made.start()
        send_f.append(made)
    start_across_w(1, w_plan(1), slot_of[1])
    stage_wait(cnt_plane, 0)
    stage_start(cnt_line, 0, add_slots(cnt_plane))
    wait_w(0, w_plan(0), slot_of[0], 0)
    matmul_to(rows.at[0], f_own, wc.at[0, 0], True, 0)
    matmul_to(rows.at[0], f_own, wc.at[0, 0], True, 1)
    wait_w(0, w_plan(0), slot_of[0], 1)
    for made in send_f:
        made.wait()

    @pl.when(section == 1)
    def _():
        heads_copy(grad_out, 2).start()

    matmul_to(rows.at[0], f_far, wc.at[0, 1], False, 0)
    forward_stats(0, 0)
    matmul_to(rows.at[0], f_far, wc.at[0, 1], False, 1)
    forward_middle(0, 0)
    forward_stats(0, 1)
    send_vec.wait_send()
    across(vecs.at[other], vecs.at[other], 3).wait_recv()
    by_units(grad_out, g3.at[1], 0)
    wait_heads(grad_out, 2)
    patch_heads(g3.at[1], 0)
    stage_wait(cnt_line, 0)
    counts[...] = add_slots(cnt_line)
    forward_end(0, 0)
    forward_middle(0, 1)
    sends = [forward_scan(0, 0, True)]
    forward_end(0, 1)
    sends.append(forward_scan(0, 1, True))
    wait_w(1, w_plan(1), slot_of[1], 0)
    matmul_to(rows.at[1], p_own, wc.at[1, 0], True, 0)
    matmul_to(rows.at[1], p_own, wc.at[1, 0], True, 1)
    wait_w(1, w_plan(1), slot_of[1], 1)
    for made in sends:
        made.wait()
    matmul_to(rows.at[1], p_far, wc.at[1, 1], False, 0)
    forward_stats(1, 0)
    done_w(0, w_plan(0), slot_of[0])

    start_local_w(0, late_plan, slot_of[2])
    start_across_w(0, late_plan, slot_of[2])

    @pl.when(section == 1)
    def _():
        wc[0, 1, width - late_row :, :] = jnp.zeros((W - width + late_row, W), BF16)

    def source_level():
        def body(i, acc):
            r = pl.ds(aligned(i * (2 * seqs), 16), 2 * seqs)
            return acc + fold(wide(live[r, :], 8) * f_own[r, :].astype(F32))

        acc = repeat(2 * pairs, body, jnp.zeros((8, W), F32), 3)
        levels[0:1, :] = jnp.sum(acc, axis=0, keepdims=True)

    matmul_to(rows.at[1], p_far, wc.at[1, 1], False, 1)
    forward_middle(1, 0)
    forward_stats(1, 1)
    by_units(grad_out, g3.at[1], 1)
    patch_heads(g3.at[1], 1)
    forward_end(1, 0)
    forward_middle(1, 1)
    forward_scan(1, 0, False)
    backward_scan(1, 0, g3.at[1])
    backward_stats(1, 0)
    forward_end(1, 1)
    source_level()
    level_plane, level_line = in_plane(wide_p, 0), in_line(wide_z, 0)
    stage_start(level_plane, 9, jnp.concatenate([levels[0:2, :], jnp.zeros((6, W), F32)], axis=0))
    forward_scan(1, 1, False)
    backward_middle(1, 0)
    stage_wait(level_plane, 9)
    stage_start(level_line, 9, add_slots(level_plane))
    backward_scan(1, 1, g3.at[1])
    backward_stats(1, 1)
    pl.semaphore_signal(credit.at[0], inc=1, device_id=sibling, device_id_type=MESH)
    backward_end(1, 0)
    pl.semaphore_wait(credit.at[0], 1)
    sends = [grad_rows(1, 0, 20)]
    transpose(p_own, 0, W // 256)
    backward_middle(1, 1)
    transpose(p_own, W // 256)
    stage_wait(level_line, 9)
    levels[2:4, :] = (add_slots(level_line) / wide(counts[0:1, :] + counts[2:3, :], 8))[0:2]
    transpose_level(p_own, 1)
    backward_end(1, 1)
    sends.append(grad_rows(1, 1, 20))
    sums_start(1)
    weight_grads(1, 0, 0)
    sums_middle(1)
    weight_grads(1, 0, 1)
    sums_end(1)
    arrived(sends)
    weight_grads(1, 1, 0)
    weight_grads(1, 1, 1)
    sums_there(1)
    wait_w(1, w_plan(1), slot_of[1], 2)
    done_w(1, w_plan(1), slot_of[1])

    def keep_down(r, c, y):
        p_own[r, c] = y.astype(BF16)

    source_grad(keep_down, wc.at[1, 0], wr1, 0)
    order.work(4.0)
    backward_scan(0, 0, p_own, lambda: order.work(1.8))
    backward_stats(0, 0)
    source_grad(keep_down, wc.at[1, 0], wr1, 1)
    pl.semaphore_signal(credit.at[1], inc=1, device_id=sibling, device_id_type=MESH)
    order.work(4.0)
    backward_middle(0, 0)
    order.work(1.0)
    backward_scan(0, 1, p_own, lambda: order.work(1.8))
    backward_stats(0, 1)
    backward_end(0, 0)
    pl.semaphore_wait(credit.at[1], 1)
    sends = [grad_rows(0, 0, 22)]
    order.work(1.8)
    transpose(f_own, 0, W // 256)
    backward_middle(0, 1)
    transpose(f_own, W // 256)
    transpose_level(f_own, 0)
    order.work(6.0)
    weight_grads(0, 0, 0)
    backward_end(0, 1)
    order.work(1.0)
    sends.append(grad_rows(0, 1, 22))
    sums_start(0)
    order.work(1.8)
    weight_grads(0, 0, 1)
    arrived(sends)
    weight_grads(0, 1, 0)
    weight_grads(0, 1, 1)
    wait_w(0, late_plan, slot_of[2], 0)
    wait_w(0, late_plan, slot_of[2], 1)
    done_w(0, late_plan, slot_of[2])

    def keep_source(r, c, y):
        rows[0, r, c] = y

    fetch(grad_out, 0).start()
    fetch(grad_out, 1).start()
    source_grad(keep_source, wc.at[0, 0], wc.at[0, 1], 0)
    order.work(4.0)
    sums_middle(0)
    source_grad(keep_source, wc.at[0, 0], wc.at[0, 1], 1)
    order.work(4.0)
    sums_end(0)
    sums_there(0)

    def give(m):
        return pltpu.make_async_copy(staged.at[m], gf.at[m], stage_sem.at[m])

    for m in range(2):
        fetch(grad_out, m).wait()

        def finish_frames(i, _, m=m):
            straight = staged[m, pl.ds(2 * i, 2)].astype(F32).reshape(2 * seqs, half)
            y = rows[0, pl.ds(aligned(m * span + 2 * i * seqs, 8), 2 * seqs), :]
            y = jnp.where(section == 0, y[:, :half], y[:, late_shift : late_shift + half])
            staged[m, pl.ds(2 * i, 2)] = (y + straight).reshape(2, seqs, half).astype(BF16)
            return 0

        repeat(pairs, finish_frames, 0, 3)
        give(m).start()
        order.work(3.0)
    order.drain()
    for m in range(2):
        give(m).wait()

    for layer in range(2):

        @pl.when(section == layer)
        def _(layer=layer):
            pltpu.make_async_copy(tot.at[layer], v.at[section], v_sems.at[0]).wait()
            pltpu.make_async_remote_copy(
                src_ref=tot.at[layer], dst_ref=v.at[other], send_sem=v_sems.at[1], recv_sem=v_sems.at[2],
                device_id=sibling, device_id_type=MESH,
            ).wait_recv()

        @pl.when(section != layer)
        def _(layer=layer):
            v_across(layer).wait_send()

    own_part, far_part = v[section], v[other]
    first = jnp.where(section == 0, own_part, far_part)
    second = jnp.where(section == 0, far_part, own_part)
    for row, terms in ((0, (2, 3)), (1, (0, 1)), (2, (4,))):
        for lane, x in ((0, first), (W, second)):
            total = x[terms[0] : terms[0] + 1, :]
            for k in terms[1:]:
                total = total + x[k : k + 1, :]
            vectors[row : row + 1, lane : lane + W] = total
    squares = jnp.sum(first[5:7, :] + second[5:7, :], axis=1, keepdims=True)
    root = jnp.sqrt(squares / (first[7:8, 0:1] * width))
    for k in range(2):
        vectors[3 + k : 4 + k, :] = jnp.broadcast_to(root[k : k + 1], (1, 2 * W))
    vectors[5:8, :] = jnp.zeros((3, 2 * W), F32)


def write_results(o, gf, vectors, grad_weight, grad_frames, grad_gains, grad_shifts, grad_recurs, table):
    width = grad_weight.shape[2]
    grad_weight[0] = o[...][:, :width].astype(F32)
    grad_frames[...] = gf[...]

    @pl.when(pl.program_id(0) == 0)
    def _():
        for k, out in enumerate((grad_gains, grad_shifts, grad_recurs)):
            out[...] = vectors[k : k + 1, 0:width]
        table[...] = jnp.concatenate([vectors[3:4, 0:1], vectors[4:5, 0:1]], axis=1)


def results(o, gf, vectors):
    micro, steps, seqs, half = gf.shape
    width = 2 * half
    count = W * 2 // 256
    frames = micro * steps // count
    whole = lambda shape: pl.BlockSpec(shape, lambda i: (0, 0))
    out = pl.pallas_call(
        write_results,
        grid=(count,),
        in_specs=[
            pl.BlockSpec((256, 2 * W), lambda i: (i, 0)),
            pl.BlockSpec((frames, seqs, half), lambda i: (i, 0, 0)),
            whole((8, 2 * W)),
        ],
        out_specs=(
            pl.BlockSpec((1, 256, width), lambda i: (0, i, 0)),
            pl.BlockSpec((frames, seqs, half), lambda i: (i, 0, 0)),
            whole((1, width)),
            whole((1, width)),
            whole((1, width)),
            whole((1, 2)),
        ),
        out_shape=(
            jax.ShapeDtypeStruct((1, width, width), F32),
            jax.ShapeDtypeStruct((micro * steps, seqs, half), BF16),
            jax.ShapeDtypeStruct((1, width), F32),
            jax.ShapeDtypeStruct((1, width), F32),
            jax.ShapeDtypeStruct((1, width), F32),
            jax.ShapeDtypeStruct((1, 2), F32),
        ),
        compiler_params=pltpu.CompilerParams(vmem_limit_bytes=64 * 1024 * 1024),
    )(o.reshape(2 * W, 2 * W), gf.reshape(micro * steps, seqs, half), vectors)
    return out[1].reshape(gf.shape), out[0], *out[2:]


def whole_step(dims, frames, grad_out, weights, gains, shifts, recurs, lengths, masks):
    nz, ny, nx = dims
    micro, steps, seqs, half = frames.shape
    width = 2 * half
    views = seqs // lengths.shape[1]
    rows = micro * steps * seqs
    np_ = ny * nx
    wide_rows = (rows + 16 + 127) // 128 * 128
    across_first = max(nx, ny, nz if np_ == 1 else 1)
    copies = 2 * (nx + ny + nz) + across_first
    came_rows = (nx - 1) * (W // nx) + (ny - 1) * (W // np_) + (nz - 1) * max(W // np_ // nz, 16)
    any_ = pl.BlockSpec(memory_space=pl.ANY)
    held = pl.BlockSpec(memory_space=pltpu.VMEM)
    dma = pltpu.SemaphoreType.DMA
    return pl.pallas_call(
        functools.partial(kernel, dims, steps, seqs, views),
        out_shape=(
            jax.ShapeDtypeStruct((2, W, 2 * W), BF16),
            jax.ShapeDtypeStruct(frames.shape, BF16),
            jax.ShapeDtypeStruct((8, 2 * W), F32),
        ),
        in_specs=[any_] * 3 + [held] * 5,
        out_specs=(any_, any_, held),
        scratch_shapes=[
            pltpu.VMEM((wide_rows, W), BF16),
            pltpu.VMEM((rows, W), BF16),
            pltpu.VMEM((wide_rows, W), BF16),
            pltpu.VMEM((rows, W), BF16),
            pltpu.VMEM((2, wide_rows, W), BF16),
            pltpu.VMEM((2, 2, W, W), BF16),
            pltpu.VMEM((W, W), BF16),
            pltpu.VMEM((W, wide_rows), BF16),
            pltpu.VMEM((rows, 128), F32),
            pltpu.VMEM((128, 128), F32),
            pltpu.VMEM(frames.shape, BF16),
            pltpu.VMEM((micro, steps, seqs, 128), BF16),
            pltpu.VMEM((5, W, (width - W) % 128), BF16),
            pltpu.VMEM((2, 8, W), F32),
            pltpu.VMEM((2, 8, 2 * W), F32),
            pltpu.VMEM((2, rows, W), F32),
            pltpu.VMEM((2, rows, W), F32),
            pltpu.VMEM((2, 8, W), F32),
            pltpu.VMEM((2, 8, W), F32),
            pltpu.VMEM((2, 2, 8, W), F32),
            pltpu.VMEM((8, W), F32),
            pltpu.VMEM((2, W, 128), BF16),
            pltpu.VMEM((8, 128), F32),
            pltpu.VMEM((1, np_, 8, 128), F32),
            pltpu.VMEM((1, nz, 8, 128), F32),
            pltpu.VMEM((4, np_, 8, QUART), F32),
            pltpu.VMEM((4, nz, 8, QUART), F32),
            pltpu.VMEM((2, np_, 8, W), F32),
            pltpu.VMEM((2, nz, 8, W), F32),
            pltpu.VMEM((2, 2 * PAIRS, max(came_rows, W), 2 * PART), BF16),
            dma((3, 27)),
            dma((3,)),
            dma((2,)),
            pltpu.SemaphoreType.REGULAR((2,)),
            dma((12, max(np_, 2))),
            dma((12, max(np_, 2))),
            dma((12, max(nz, 2))),
            dma((12, max(nz, 2))),
            dma((2, 2 * PAIRS, 2, copies)),
            dma((2, 2 * PAIRS, 2, copies)),
            dma((2, 2 * PAIRS, 2, across_first)),
        ],
        compiler_params=pltpu.CompilerParams(
            collective_id=0, has_side_effects=True, vmem_limit_bytes=64 * 1024 * 1024
        ),
    )(frames, grad_out, weights, gains, shifts, recurs, lengths, masks)


def shards(dims, frames, grad_out, weights, gains, shifts, recurs, lengths, masks):
    return results(*whole_step(dims, frames, grad_out, weights, gains, shifts, recurs, lengths, masks))


def solution(mesh):
    in_specs = (
        P(None, None, "batch", "section"),
        P(None, None, "batch", "section"),
        P("section", None, None),
        P("section", None),
        P("section", None),
        P("section", None),
        P(None, "batch"),
        P(None, None, "batch"),
    )
    out_specs = (
        P(None, None, "batch", "section"),
        P("section", None, None),
        P("section", None),
        P("section", None),
        P("section", None),
        P("section", None),
    )
    body = functools.partial(shards, grid_of(mesh.shape["batch"]))
    return jax.shard_map(body, mesh=mesh, in_specs=in_specs, out_specs=out_specs, check_vma=False)
```

```python
import functools

import jax
import jax.numpy as jnp
from jax import lax
from jax.experimental import pallas as pl
from jax.experimental.pallas import tpu as pltpu
from jax.sharding import PartitionSpec as P

EPS = 1e-05
W = 1024
HALF = W // 2
QUART = W // 4
PAIRS = 2
PART = W // PAIRS // 2
MESH = pl.DeviceIdType.MESH
F32 = jnp.float32
BF16 = jnp.bfloat16


def grid_of(size):
    if size == 16:
        return (4, 2, 2)
    if size == 128:
        return (8, 4, 4)
    return (size, 1, 1)


def aligned(x, k):
    return pl.multiple_of(x, k)


def wide(x, reps):
    return jnp.concatenate([x] * reps, axis=1)


def fold(x):
    rows = x.shape[0]
    total = x[0:8]
    for k in range(8, rows, 8):
        total = total + x[k : k + 8]
    return total


def repeat(count, body, init, times):
    while count % times:
        times -= 1

    def several(i, carry):
        for j in range(times):
            carry = body(i * times + j, carry)
        return carry

    return lax.fori_loop(0, count // times, several, init)


def dot(a, b, dims):
    return lax.dot_general(a, b, (dims, ((), ())), preferred_element_type=F32)


class Reduction:
    def __init__(self, env, layer, index, block, orders, lane_of):
        self.env, self.layer, self.index, self.block, self.orders = env, layer, index, block, orders
        self.lane_of = lane_of
        self.space = env["space"].at[layer, index]
        self.depth = len(orders[0])
        self.regions = [self.shares(i, order) for i, order in enumerate(orders)]
        self.step = 0
        self.waits = []
        self.slot = [0, 0]
        depth = self.depth
        self.steps = [functools.partial(self.scatter, k) for k in range(depth)]
        self.steps += [functools.partial(self.gather, k) for k in range(depth - 1, 0, -1)]
        self.steps += [self.give, self.finish]

    def shares(self, i, order):
        out = [(0, W, i * PART, PART)]
        for axis in order:
            out.append(self.share(out[-1], axis, axis["index"]))
        return out

    def share(self, region, axis, index):
        row, rows, lane, lanes = region
        by_row = min(axis["size"], rows // 16)
        rows, lanes = rows // by_row, lanes // (axis["size"] // by_row)
        if by_row == axis["size"]:
            return row + index * rows, rows, lane, lanes
        return row + lax.rem(index, by_row) * rows, rows, lane + index // by_row * lanes, lanes

    @property
    def free_to_go(self):
        return self.step != self.depth or self.layer in self.env["summed"]

    @property
    def done(self):
        return self.step >= len(self.steps)

    def advance(self):
        self.sent = []
        self.steps[self.step]()
        self.step += 1
        return self.sent

    def remote(self, i, src, dst, slot, where, recv=None):
        sems = (self.layer, self.index, i, slot)
        return pltpu.make_async_remote_copy(
            src_ref=src, dst_ref=dst, send_sem=self.env["ar_send"].at[sems],
            recv_sem=self.env["ar_recv"].at[sems] if recv is None else recv, device_id=where, device_id_type=MESH,
        )

    def wait(self):
        for made, came in self.waits:
            made.wait_send()
            came.wait_recv()
        self.waits = []

    def take(self, i):
        self.slot[i] += 1
        return self.slot[i] - 1

    def came_at(self, i, k, s):
        row = sum((a["size"] - 1) * self.regions[i][n + 1][1] for n, a in enumerate(self.orders[i][:k]))
        _, rows, _, lanes = self.regions[i][k + 1]
        return row + (s - 1) * rows, rows, i * PART, lanes

    def scatter(self, k):
        if k > 0:
            self.wait()
            self.add(k - 1)
        for i in range(2):
            self.scatter_part(i, k)

    def start_part(self, i):
        self.sent = []
        self.scatter_part(i, 0)
        if i == 1:
            self.step = 1
        return self.sent

    def scatter_part(self, i, k):
        axis = self.orders[i][k]
        for s in range(1, axis["size"]):
            other = lax.rem(axis["index"] + s, axis["size"])
            row, rows, lane, lanes = self.share(self.regions[i][k], axis, other)
            src = self.block.at[pl.ds(aligned(row, 16), rows), pl.ds(aligned(lane, 128), lanes)]
            at, n, at_lane, n_lanes = self.came_at(i, k, s)
            dst = self.space.at[pl.ds(at, n), pl.ds(at_lane, n_lanes)]
            made = self.remote(i, src, dst, self.take(i), axis["at"](other))
            made.start()
            self.waits.append((made, made))
            self.sent.append((axis["link"], rows * lanes * 2))

    def add(self, k, last=False):
        rows = self.regions[0][k + 1][1]
        size = min(rows, 128)
        out = []
        for i in range(2):
            row, _, lane, lanes = self.regions[i][k + 1]
            lane = aligned(lane, 128)
            extra = None
            if last:
                part = self.index // PAIRS
                first = aligned((self.index % PAIRS) * 2 * PART + lane, 128)
                extra = self.env["vtot"][self.layer, part, 0:1, pl.ds(first, lanes)]
            came = [self.came_at(i, k, s) for s in range(1, self.orders[i][k]["size"])]
            out.append((row, lane, lanes, came, self.local(i, self.regions[i][k + 1])[0], extra))

        def body(j, _):
            for row, lane, lanes, came, home, extra in out:
                here = pl.ds(aligned(row + j * size, 16), size)
                total = self.block[here, pl.ds(lane, lanes)].astype(F32)
                for at, _, at_lane, _ in came:
                    there = pl.ds(aligned(at + j * size, 16), size)
                    total = total + self.space[there, pl.ds(at_lane, lanes)].astype(F32)
                if last:
                    column = self.env["column"][self.layer, here, :].astype(F32)
                    total = total + wide(column, lanes // 128) * extra
                    to = pl.ds(aligned(home + j * size, 16), size)
                    self.space[to, pl.ds(lane, lanes)] = total.astype(BF16)
                else:
                    self.block[here, pl.ds(lane, lanes)] = total.astype(BF16)
            return 0

        lax.fori_loop(0, rows // size, body, 0)

    def local(self, i, region):
        row, rows, lane, lanes = region
        return row - self.regions[i][1][0], rows, lane, lanes

    def gather(self, k):
        self.wait()
        if k == self.depth - 1:
            self.add(k, last=True)

        def ref(i, region):
            row, rows, lane, lanes = self.local(i, region)
            return self.space.at[pl.ds(aligned(row, 16), rows), pl.ds(aligned(lane, 128), lanes)]

        for i, order in enumerate(self.orders):
            axis = order[k]
            mine = ref(i, self.regions[i][k + 1])
            for s in range(1, axis["size"]):
                to = lax.rem(axis["index"] + s, axis["size"])
                frm = lax.rem(axis["index"] + axis["size"] - s, axis["size"])
                slot = self.take(i)
                made = self.remote(i, mine, mine, slot, axis["at"](to))
                made.start()
                theirs = ref(i, self.share(self.regions[i][k], axis, frm))
                self.waits.append((made, self.remote(i, theirs, theirs, slot, axis["at"](frm))))
                self.sent.append((axis["link"], self.regions[i][k + 1][1] * self.regions[i][k + 1][3] * 2))

    def result(self, i, index, section):
        rows = self.regions[i][1][1]
        lane = aligned(self.lane_of(section) + i * PART, PART)
        return self.env["o"].at[section, pl.ds(aligned(index * rows, 16), rows), pl.ds(lane, PART)]

    def gathered(self, i):
        return self.space.at[pl.ds(0, self.regions[i][1][1]), pl.ds(i * PART, PART)]

    def deliver(self, i, s, straight):
        axis, section = self.orders[i][0], self.env["section"]
        recv = None if straight else self.env["ar_other"].at[self.layer, self.index, i, s]
        where = dict(axis["at"](lax.rem(axis["index"] + s, axis["size"])), section=self.layer)
        target = self.result(i, axis["index"], section)
        return self.remote(i, self.gathered(i), target, self.slot[i] + s, where, recv)

    def arrival(self, i, s, straight):
        axis, section = self.orders[i][0], self.env["section"]
        recv = None if straight else self.env["ar_other"].at[self.layer, self.index, i, s]
        index = lax.rem(axis["index"] + axis["size"] - s, axis["size"])
        frm = section if straight else 1 - section
        where = dict(axis["at"](index), section=frm)
        return self.remote(i, self.gathered(i), self.result(i, index, frm), self.slot[i] + s, where, recv)

    def kept(self, i):
        sem = self.env["ar_recv"].at[self.layer, self.index, i, self.slot[i]]
        target = self.result(i, self.orders[i][0]["index"], self.env["section"])
        return pltpu.make_async_copy(self.gathered(i), target, sem)

    def give(self):
        self.wait()

        @pl.when(self.env["section"] == self.layer)
        def _():
            for i in range(2):
                for s in range(1, self.orders[i][0]["size"]):
                    self.deliver(i, s, True).start()
                self.kept(i).start()

        @pl.when(self.env["section"] != self.layer)
        def _():
            for i in range(2):
                for s in range(self.orders[i][0]["size"] - 1, -1, -1):
                    self.deliver(i, s, False).start()

        for i, order in enumerate(self.orders):
            self.sent.append((order[0]["link"], self.regions[i][1][1] * PART * 2 * (order[0]["size"] - 1)))

    def finish(self):
        @pl.when(self.env["section"] == self.layer)
        def _():
            for i in range(2):
                size = self.orders[i][0]["size"]
                self.kept(i).wait()
                for s in range(1, size):
                    self.deliver(i, s, True).wait_send()
                    self.arrival(i, s, True).wait_recv()
                for s in range(size):
                    self.arrival(i, s, False).wait_recv()

        @pl.when(self.env["section"] != self.layer)
        def _():
            for i in range(2):
                for s in range(self.orders[i][0]["size"]):
                    self.deliver(i, s, False).wait_send()


class Order:
    RATE, HOP, QUEUE = 52e3, 2.2, 1e9

    def __init__(self):
        self.now = 0.0
        self.free = {}
        self.going = []
        self.held = []

    def sent(self, copies):
        end = self.now
        for link, size in copies:
            self.free[link] = max(self.now, self.free.get(link, 0.0)) + size / self.RATE
            end = max(end, self.free[link])
        return end + self.HOP

    def begin(self, one, i):
        self.held.append((one, i))
        self.release()

    def release(self, always=False):
        while self.held and (always or self.busy() < self.QUEUE):
            one, i = self.held.pop(0)
            end = self.sent(one.start_part(i))
            if i == 0:
                one.due = end
            else:
                one.due = max(one.due, end)
                self.going.append(one)

    def busy(self):
        link = self.held[0][0].orders[self.held[0][1]][:1]
        return max([self.free.get(a["link"], 0.0) - self.now for a in link], default=0.0)

    def advance(self, one):
        self.now = max(self.now, one.due) + 0.4
        one.due = self.sent(one.advance())
        if one.done:
            self.going.remove(one)

    def work(self, cost):
        self.now += cost
        while True:
            self.release()
            due = [x for x in self.going if x.due <= self.now and x.free_to_go]
            if not due:
                return
            self.advance(min(due, key=lambda x: x.due))

    def drain(self):
        while self.going or self.held:
            self.release(always=not self.going)
            self.advance(min(self.going, key=lambda x: x.due))


def kernel(dims, steps, seqs, views, frames, grad_out, weights, gains, shifts, recurs, lengths, masks, o, gf, vectors, f_own, f_far, p_own, p_far, g3, wc, wr1, src_t, live, turn,
           staged, heads, tails, v, vecs, rows, hid, coef, tot, vtot, levels, column, counts, cnt_p, cnt_z, slim_p, slim_z,
           wide_p, wide_z, space, sems, v_sems, stage_sem, credit, pl_send, pl_recv, z_send, z_recv, ar_send, ar_recv,
           ar_other):
    nz, ny, nx = dims
    np_ = ny * nx
    span = steps * seqs
    total_rows = 2 * span
    sent_rows = total_rows + 16
    pairs = steps // 2
    section = lax.axis_index("section")
    other = 1 - section
    b = lax.axis_index("batch")
    mp = lax.rem(b, np_)
    mz = b // np_

    def at_plane(i):
        return {"batch": b - mp + i}

    def at_z(i):
        return {"batch": b + (i - mz) * np_}

    def axis_of(link, size, stride):
        index = lax.rem(b // stride, size)
        return dict(link=link, size=size, index=index, at=lambda i: {"batch": b + (i - index) * stride})

    def halvings(link, size, stride):
        out = []
        while size > 1:
            out.append(axis_of(link, 2, stride))
            size //= 2
            stride *= 2
        return out

    xs, ys, zs = halvings("x", nx, 1), halvings("y", ny, nx), halvings("z", nz, np_)
    orders = (xs + ys + zs, ys + xs + zs)
    sibling = {"section": other}

    def local(src, dst, slot):
        return pltpu.make_async_copy(src, dst, sems.at[0, slot])

    def across(src, dst, slot):
        return pltpu.make_async_remote_copy(
            src_ref=src, dst_ref=dst, send_sem=sems.at[1, slot], recv_sem=sems.at[2, slot],
            device_id=sibling, device_id_type=MESH,
        )

    half = frames.shape[3]
    width = 2 * half
    lead = W - half
    rest = width - W
    full = rest // 128 * 128

    def fetch(source, m):
        return pltpu.make_async_copy(source.at[m], staged.at[m], stage_sem.at[m])

    def by_units(source, target, m):
        fetch(source, m).wait()

        @pl.when(section == 0)
        def _():
            pad = jnp.zeros((2 * seqs, lead), F32)

            def place(i, _):
                x = staged[m, pl.ds(2 * i, 2)].astype(F32).reshape(2 * seqs, half)
                to = pl.ds(aligned(m * span + 2 * i * seqs, 16), 2 * seqs)
                target[to, :] = jnp.concatenate([x, pad], axis=1).astype(BF16)
                return 0

            repeat(pairs, place, 0, 3)

        @pl.when(section == 1)
        def _():
            pad = jnp.zeros((2 * seqs, 2 * lead), F32)

            def place(i, _):
                x = staged[m, pl.ds(2 * i, 2)].astype(F32).reshape(2 * seqs, half)
                to = pl.ds(aligned(m * span + 2 * i * seqs, 16), 2 * seqs)
                target[to, :] = jnp.concatenate([x[:, lead:], pad], axis=1).astype(BF16)
                return 0

            repeat(pairs, place, 0, 3)

    def patch_heads(target, m):
        @pl.when(section == 0)
        def _():
            lane = lax.broadcasted_iota(jnp.int32, (2 * seqs, 128), 1)

            def place(i, _):
                to = pl.ds(aligned(m * span + 2 * i * seqs, 16), 2 * seqs)
                head = heads[m, pl.ds(2 * i, 2)].astype(F32).reshape(2 * seqs, 128)
                head = pltpu.roll(head, 128 - lead, 1)
                old = target[to, W - 128 :].astype(F32)
                target[to, W - 128 :] = jnp.where(lane < 128 - lead, old, head).astype(BF16)
                return 0

            repeat(pairs, place, 0, 3)

    def pieces(row, count, u, block, spot):
        r = pl.ds(row, count)
        to = pl.ds(0, count)
        if u == 0:
            return [(weights.at[0, r, pl.ds(0, W)], block.at[to, :])]
        return [
            (weights.at[0, r, pl.ds(W, full)], block.at[to, pl.ds(0, full)]),
            (weights.at[0, r, pl.ds(W + full, rest - full)], tails.at[spot, to, :]),
        ]

    rows_of = {0: (0, W), 1: (W, rest)}

    def w_plan(layer):
        mine, far = rows_of[layer], rows_of[1 - layer]
        plan = [
            (mine, layer, far, 1 - layer, wc.at[layer, 0], 2 * layer),
            (far, layer, mine, 1 - layer, wc.at[layer, 1], 2 * layer + 1),
        ]
        if layer == 1:
            plan.append((mine, 0, far, 1, wr1, 4))
        return plan

    late_row = (width - half) // 16 * 16
    late_shift = half - late_row
    late_plan = [
        ((0, W), 0, (late_row, width - late_row), 1, wc.at[0, 0], 0),
        ((0, W), 1, (late_row, width - late_row), 0, wc.at[0, 1], 1),
    ]
    slot_of = {0: 4, 1: 8, 2: 14}

    def local_w(plan, base, which):
        r, u, _, _, block, spot = plan[which]
        return [local(a, t, base + 2 * which + i) for i, (a, t) in enumerate(pieces(*r, u, block, spot))]

    def across_w(plan, base, which):
        _, _, r, u, block, spot = plan[which]
        return [across(a, t, base + 2 * which + i) for i, (a, t) in enumerate(pieces(*r, u, block, spot))]

    def start_local_w(layer, plan, base):
        @pl.when(section == layer)
        def _():
            for which in range(len(plan)):
                for made in local_w(plan, base, which):
                    made.start()

    def start_across_w(layer, plan, base):
        @pl.when(section == layer)
        def _():
            for which in range(len(plan)):
                for made in across_w(plan, base, which):
                    made.start()

    def last_units(block, spot):
        def body(i, _):
            r = pl.ds(aligned(i * 128, 128), 128)
            x = tails[spot, r, :].astype(F32)
            x = jnp.concatenate([x, jnp.zeros((128, 128 - x.shape[1]), F32)], axis=1)
            block[r, full:] = x.astype(BF16)
            return 0

        lax.fori_loop(0, W // 128, body, 0)

    def wait_w(layer, plan, base, which):
        _, own_u, _, far_u, block, spot = plan[which]

        @pl.when(section == layer)
        def _():
            for made in local_w(plan, base, which):
                made.wait()
            if own_u == 1:
                last_units(block, spot)

        @pl.when(section != layer)
        def _():
            for made in across_w(plan, base, which):
                made.wait_recv()
            if far_u == 1:
                last_units(block, spot)

    def done_w(layer, plan, base):
        @pl.when(section == layer)
        def _():
            for which in range(len(plan)):
                for made in across_w(plan, base, which):
                    made.wait_send()

    def heads_copy(source, slot):
        return across(source.at[:, :, :, pl.ds(0, 128)], heads, slot)

    def wait_heads(source, slot):
        @pl.when(section == 0)
        def _():
            heads_copy(source, slot).wait_recv()

        @pl.when(section == 1)
        def _():
            heads_copy(source, slot).wait_send()

    fetch(frames, 0).start()
    fetch(frames, 1).start()
    for layer in range(2):
        start_local_w(layer, w_plan(layer), slot_of[layer])

    barrier = pltpu.get_barrier_semaphore()
    greeted = [dict(sibling)]
    greeted += [at_plane(lax.rem(mp + k, np_)) for k in range(1, np_)]
    greeted += [at_z(lax.rem(mz + k, nz)) for k in range(1, nz)]
    for axis in (xs + zs)[:1] + (ys + zs)[:1]:
        for s in range(1, axis["size"]):
            greeted.append(dict(axis["at"](lax.rem(axis["index"] + s, axis["size"])), section=other))
    for where in greeted:
        pl.semaphore_signal(barrier, inc=1, device_id=where, device_id_type=MESH)

    for k, (x, fill) in enumerate(((gains, 0.0), (shifts, -1e30), (recurs, 0.0))):
        vecs[section, k : k + 1, 0:width] = x[...]
        vecs[section, k : k + 1, width:] = jnp.full((1, 2 * W - width), fill, F32)
    vecs[section, 3:8, :] = jnp.zeros((5, 2 * W), F32)

    gap = jnp.zeros((W - rest, W), BF16)

    @pl.when(section == 0)
    def _():
        wc[0, 1, rest:, :] = gap
        wc[1, 1, rest:, :] = gap

    @pl.when(section == 1)
    def _():
        wc[0, 0, rest:, :] = gap
        wc[1, 0, rest:, :] = gap
        wr1[rest:, :] = gap

    for spot in (0, 2):
        tails[spot, rest:, :] = jnp.zeros((W - rest, rest - full), BF16)
    for spare in (f_own, p_own, g3.at[0], g3.at[1]):
        spare[sent_rows:, :] = jnp.zeros((spare.shape[0] - sent_rows, W), BF16)

    pl.semaphore_wait(barrier, len(greeted))

    @pl.when(section == 1)
    def _():
        heads_copy(frames, 1).start()

    start_across_w(0, w_plan(0), slot_of[0])
    send_vec = across(vecs.at[section], vecs.at[section], 3)
    send_vec.start()

    def stage_copy(where, rnd, slot, k, back):
        buf, parity, size, me, at, send, recv = where
        there = at(lax.rem(me + (size - k if back else k), size))
        ref = buf.at[parity, slot]
        return pltpu.make_async_remote_copy(
            src_ref=ref, dst_ref=ref, send_sem=send.at[rnd, k], recv_sem=recv.at[rnd, k],
            device_id=there, device_id_type=MESH,
        )

    def in_plane(buf, parity):
        return (buf, parity, np_, mp, at_plane, pl_send, pl_recv)

    def in_line(buf, parity):
        return (buf, parity, nz, mz, at_z, z_send, z_recv)

    def stage_start(where, rnd, value):
        buf, parity, size, me = where[:4]
        buf[parity, me] = value
        for k in range(1, size):
            stage_copy(where, rnd, me, k, False).start()

    def stage_wait(where, rnd):
        size, me = where[2:4]
        for k in range(1, size):
            stage_copy(where, rnd, me, k, False).wait_send()
            stage_copy(where, rnd, lax.rem(me + size - k, size), k, True).wait_recv()

    def add_slots(where):
        buf, parity, size = where[:3]
        total = buf[parity, 0]
        for k in range(1, size):
            total = total + buf[parity, k]
        return total

    groups = lengths.shape[1]
    s_at = lax.broadcasted_iota(jnp.int32, (seqs, groups), 0)
    g_at = lax.broadcasted_iota(jnp.int32, (seqs, groups), 1) * views
    there = (s_at >= g_at) & (s_at < g_at + views)
    position = lax.broadcasted_iota(jnp.int32, (seqs, 128), 1)
    local_counts = []
    for m in range(2):
        turn[...] = jnp.zeros_like(turn)
        turn[0:steps, 0:seqs] = masks[m].astype(F32)
        mask = turn[...].T[0:seqs]
        length = jnp.broadcast_to(lengths[m : m + 1, :], (seqs, groups)).astype(F32)
        limit = jnp.sum(jnp.where(there, length, 0.0), axis=1, keepdims=True)
        alive = (position.astype(F32) < limit) & ((mask > 0.0) | (position == 0))
        alive = jnp.where(position < steps, alive.astype(F32), 0.0)
        total = jnp.zeros((seqs, 128), F32)
        for t in range(steps):
            at = m * span + t * seqs
            cells = jnp.broadcast_to(alive[:, t : t + 1], (seqs, 128))
            live[at : at + seqs, :] = cells
            total = total + cells
        local_counts.append(jnp.sum(total, axis=0, keepdims=True))
    n_own = jnp.concatenate([local_counts[0]] * 2 + [local_counts[1]] * 2, axis=0)
    n_own = jnp.concatenate([n_own, n_own], axis=0)

    cnt_plane, cnt_line = in_plane(cnt_p, 0), in_line(cnt_z, 0)
    stage_start(cnt_plane, 0, n_own)

    def vec_of(layer, k, lh):
        return vecs[layer, k : k + 1, pl.ds(aligned(section * W + lh * HALF, HALF), HALF)]

    def half_of(lh):
        return slice(lh * HALF, (lh + 1) * HALF)

    def matmul_to(out, a, w, first, lh):
        lanes = half_of(lh)

        def body(m, _):
            r = pl.ds(aligned(m * span, 16), span)
            y = dot(a[r, :], w[:, lanes], ((1,), (0,)))
            out[r, lanes] = y if first else out[r, lanes] + y
            return 0

        lax.fori_loop(0, 2, body, 0)

    def packed(x, y):
        return jnp.concatenate([z[:, k * QUART : (k + 1) * QUART] for z in (*x, *y) for k in range(2)], axis=0)

    def unpacked(x, m):
        return jnp.concatenate([x[2 * m + k : 2 * m + k + 1] for k in range(2)], axis=1)

    def merge_slots(where, counts_of):
        buf, parity, size = where[:3]
        s = [buf[parity, k, 0:4, :] for k in range(size)]
        q = [buf[parity, k, 4:8, :] for k in range(size)]
        n = [wide(counts_of(k), 2) for k in range(size)]
        total, squares, count = sum(s[1:], s[0]), sum(q[1:], q[0]), sum(n[1:], n[0])
        mean = total / count
        for k in range(size):
            d = s[k] / n[k] - mean
            squares = squares + n[k] * d * d
        return jnp.concatenate([total, squares], axis=0)

    def slim_round(which, lh):
        return 1 + 2 * which + lh, in_plane(slim_p, 2 * lh + which % 2), in_line(slim_z, 2 * lh + which % 2)

    def forward_stats(layer, lh):
        lanes = half_of(lh)
        sums, squares = [], []
        for m in range(2):
            start = jnp.sum(rows[layer, m * span : m * span + seqs, lanes], axis=0, keepdims=True) * (1.0 / seqs)

            def body(i, carry):
                s, q = carry
                r = pl.ds(aligned(m * span + i * (2 * seqs), 16), 2 * seqs)
                d = rows[layer, r, lanes] - start
                kept = wide(live[r, :], 4) * d
                return s + fold(kept), q + fold(kept * d)

            zero = jnp.zeros((8, HALF), F32)
            s, q = repeat(pairs, body, (zero, zero), 4)
            s, q = jnp.sum(s, axis=0, keepdims=True), jnp.sum(q, axis=0, keepdims=True)
            n = wide(local_counts[m], 4)
            sums.append(s + n * start)
            squares.append(jnp.maximum(q - s * s / n, 0.0))
        rnd, plane, _ = slim_round(layer, lh)
        stage_start(plane, rnd, packed(sums, squares))

    def forward_middle(layer, lh):
        rnd, plane, line = slim_round(layer, lh)
        stage_wait(plane, rnd)
        stage_start(line, rnd, merge_slots(plane, lambda k: cnt_p[0, k, 0:4, :]))

    def forward_end(layer, lh):
        rnd, _, line = slim_round(layer, lh)
        lanes = half_of(lh)
        stage_wait(line, rnd)
        value = merge_slots(line, lambda k: cnt_z[0, k, 0:4, :])
        for m in range(2):
            count = wide(counts[2 * m : 2 * m + 1, :], 4)
            mean = unpacked(value[0:4], m) / count
            scale = lax.rsqrt(unpacked(value[4:8], m) / count + EPS)
            coef[layer, 2 * m : 2 * m + 1, lanes] = mean
            coef[layer, 2 * m + 1 : 2 * m + 2, lanes] = scale
            slope = vec_of(layer, 0, lh) * scale
            coef[layer, 4 + 2 * m : 5 + 2 * m, lanes] = slope
            coef[layer, 5 + 2 * m : 6 + 2 * m, lanes] = vec_of(layer, 1, lh) - mean * slope

    def forward_scan(layer, lh, passes):
        lanes = half_of(lh)
        rec = vec_of(layer, 2, lh)
        slope = [coef[layer, 4 + 2 * m : 5 + 2 * m, lanes] for m in range(2)]
        shift = [coef[layer, 5 + 2 * m : 6 + 2 * m, lanes] for m in range(2)]

        def body(i, carry):
            states, level = carry
            out = []
            for m in range(2):
                r = pl.ds(aligned(m * span + i * (2 * seqs), 16), 2 * seqs)
                x = rows[layer, r, lanes] * slope[m] + shift[m]
                lv = wide(live[r, :], 4)
                alive = lv > 0.0
                h = states[m]
                both = []
                for k in range(2):
                    part = slice(k * seqs, (k + 1) * seqs)
                    z = x[part] + rec * h
                    soft = jnp.maximum(z, 0.0) + jnp.log(1.0 + jnp.exp(-jnp.abs(z)))
                    h = jnp.where(alive[part], soft, h)
                    both.append(h)
                two = jnp.concatenate(both, axis=0)
                hid[layer, r, lanes] = two
                if passes:
                    p_own[r, lanes] = two.astype(BF16)
                    level = level + fold(lv * two)
                out.append(h)
            return tuple(out), level

        zero = jnp.zeros((seqs, HALF), F32)
        _, level = repeat(pairs, body, ((zero, zero), jnp.zeros((8, HALF), F32)), 2)
        if not passes:
            return None
        levels[1:2, lanes] = jnp.sum(level, axis=0, keepdims=True)
        made = across(p_own.at[pl.ds(0, total_rows), lanes], p_far.at[:, lanes], 18 + lh)
        made.start()
        return made

    def backward_scan(layer, lh, above, between=lambda: None):
        for lq in range(2 * lh, 2 * lh + 2):
            lanes = slice(lq * QUART, (lq + 1) * QUART)
            gq, sq, rec = (vec_of(layer, k, lh)[:, (lq % 2) * QUART : (lq % 2 + 1) * QUART] for k in range(3))
            mean = [coef[layer, 2 * m : 2 * m + 1, lanes] for m in range(2)]
            scale = [coef[layer, 2 * m + 1 : 2 * m + 2, lanes] for m in range(2)]

            def body(i, carry):
                down, s1, s2, rsum, sqh, sqa = carry
                down, s1, s2 = list(down), list(s1), list(s2)
                i = pairs - 1 - i
                for m in range(2):
                    start = m * span + i * (2 * seqs)
                    r = pl.ds(aligned(start, 16), 2 * seqs)
                    before = pl.ds(aligned(jnp.maximum(start - seqs, 0), 8), seqs)
                    normed = (rows[layer, r, lanes] - mean[m]) * scale[m]
                    drive = gq * normed + sq
                    h2 = hid[layer, r, lanes]
                    hb = jnp.where(i > 0, hid[layer, before, lanes], 0.0)
                    lv = wide(live[r, :], 2)
                    up = above[r, lanes].astype(F32)
                    res = f_own[r, lanes].astype(F32)
                    aux = res + h2 if layer == 1 else res
                    sqh = sqh + fold(lv * (h2 * h2))
                    sqa = sqa + fold(lv * (aux * aux))
                    grads = [None, None]
                    for k in (1, 0):
                        part = slice(k * seqs, (k + 1) * seqs)
                        prior = h2[0:seqs] if k == 1 else hb
                        slope = 0.5 + 0.5 * jnp.tanh(0.5 * (drive[part] + rec * prior))
                        total = up[part] + down[m]
                        gd = lv[part] * slope * total
                        down[m] = (1.0 - lv[part]) * total + rec * gd
                        grads[k] = gd
                        rsum = rsum + fold(gd * prior)
                    gd2 = jnp.concatenate(grads, axis=0)
                    hid[layer, r, lanes] = gd2
                    s1[m] = s1[m] + fold(gd2)
                    s2[m] = s2[m] + fold(gd2 * normed)
                return tuple(down), tuple(s1), tuple(s2), rsum, sqh, sqa

            zero = jnp.zeros((seqs, QUART), F32)
            z8 = jnp.zeros((8, QUART), F32)
            _, s1, s2, rsum, sqh, sqa = repeat(
                pairs, body, ((zero, zero), (z8, z8), (z8, z8), z8, z8, z8), 2
            )
            for k, x in enumerate((s1[0], s1[1], s2[0], s2[1], rsum, sqh, sqa)):
                tot[layer, k : k + 1, lanes] = jnp.sum(x, axis=0, keepdims=True)
            between()

    def backward_stats(layer, lh):
        rnd, plane, _ = slim_round(3 - layer, lh)
        t = tot[layer, 0:4, half_of(lh)]
        stage_start(plane, rnd, packed([t[0:1], t[1:2]], [t[2:3], t[3:4]]))

    def backward_middle(layer, lh):
        rnd, plane, line = slim_round(3 - layer, lh)
        stage_wait(plane, rnd)
        stage_start(line, rnd, add_slots(plane))

    def backward_end(layer, lh):
        rnd, _, line = slim_round(3 - layer, lh)
        stage_wait(line, rnd)
        value = add_slots(line)
        for m in range(2):
            tot[layer, m : m + 1, half_of(lh)] = unpacked(value[0:4], m)
            tot[layer, 2 + m : 3 + m, half_of(lh)] = unpacked(value[4:8], m)

    def grad_rows(layer, lh, slot):
        lanes = half_of(lh)
        acc = jnp.zeros((8, HALF), F32)
        for m in range(2):
            mean = coef[layer, 2 * m : 2 * m + 1, lanes]
            scale = coef[layer, 2 * m + 1 : 2 * m + 2, lanes]
            count = wide(counts[2 * m : 2 * m + 1, :], 4)
            first = tot[layer, m : m + 1, lanes] / count
            second = tot[layer, 2 + m : 3 + m, lanes] / count * scale
            k = coef[layer, 4 + 2 * m : 5 + 2 * m, lanes]

            def body(i, acc):
                r = pl.ds(aligned(m * span + i * (2 * seqs), 16), 2 * seqs)
                y = hid[layer, r, lanes] - first - (rows[layer, r, lanes] - mean) * second
                y = wide(live[r, :], 4) * (k * y)
                g3[0, r, lanes] = y.astype(BF16)
                return acc + fold(y)

            acc = repeat(pairs, body, acc, 4)
        top = lax.broadcasted_iota(jnp.int32, (16, HALF), 0) == 0
        minus = jnp.where(top, -jnp.sum(acc, axis=0, keepdims=True), 0.0)
        g3[0, total_rows:sent_rows, lanes] = minus.astype(BF16)
        made = across(g3.at[0, pl.ds(0, sent_rows), lanes], g3.at[1, pl.ds(0, sent_rows), lanes], slot + lh)
        made.start()
        return made

    sums_round = {1: (1, 10), 0: (0, 11)}

    def sums_start(layer):
        parity, rnd = sums_round[layer]
        own_sum = -g3[0, total_rows:sent_rows, :].astype(F32)[0:1]
        value = jnp.concatenate([own_sum, tot[layer, 4:7, :], jnp.zeros((4, W), F32)], axis=0)
        stage_start(in_plane(wide_p, parity), rnd, value)

    def sums_middle(layer):
        parity, rnd = sums_round[layer]
        stage_wait(in_plane(wide_p, parity), rnd)
        stage_start(in_line(wide_z, parity), rnd, add_slots(in_plane(wide_p, parity)))

    def swap_sums(layer):
        return across(vtot.at[layer, 0], vtot.at[layer, 1], 25 + layer)

    def sums_end(layer):
        parity, rnd = sums_round[layer]
        stage_wait(in_line(wide_z, parity), rnd)
        vtot[layer, 0] = add_slots(in_line(wide_z, parity))
        swap_sums(layer).start()
        tot[layer, 4:7, :] = vtot[layer, 0, 1:4, :]
        tot[layer, 7:8, :] = wide(counts[0:1, :] + counts[2:3, :], 8)

        @pl.when(section == layer)
        def _():
            pltpu.make_async_copy(tot.at[layer], v.at[section], v_sems.at[0]).start()

        @pl.when(section != layer)
        def _():
            v_across(layer).start()

    def sums_there(layer):
        swap_sums(layer).wait()
        env["summed"].add(layer)

    def v_across(layer):
        return pltpu.make_async_remote_copy(
            src_ref=tot.at[layer], dst_ref=v.at[section], send_sem=v_sems.at[1], recv_sem=v_sems.at[2],
            device_id=sibling, device_id_type=MESH,
        )

    def transpose(src, begin=0, end=W // 128):
        def body(j, _):
            c = pl.ds(aligned(j * 128, 128), 128)
            src_t[c, 0:total_rows] = src[0:total_rows, c].T
            return 0

        lax.fori_loop(begin, end, body, 0)

    def transpose_level(src, layer):
        top = lax.broadcasted_iota(jnp.int32, (16, W), 0) == 0
        src[total_rows:sent_rows, :] = jnp.where(top, levels[2 + layer : 3 + layer, :], 0.0).astype(BF16)

        def body(j, _):
            c = pl.ds(aligned(j * 128, 128), 128)
            src_t[c, total_rows:] = src[total_rows:, c].T
            level = src[total_rows:sent_rows, c].astype(F32)[0:1]
            column[layer, c, :] = jnp.broadcast_to(level, (128, 128)).T.astype(BF16)
            return 0

        lax.fori_loop(0, W // 128, body, 0)

    def weight_part(block, grads, c):
        lanes = pl.ds(c * HALF, HALF)

        def body(j, _):
            r = pl.ds(aligned(j * HALF, HALF), HALF)
            block[r, lanes] = dot(src_t[r, :], grads[:, lanes], ((1,), (0,))).astype(BF16)
            return 0

        lax.fori_loop(0, W // HALF, body, 0)

    def source_grad(store, w_own, w_far, half_index):
        c = half_of(half_index)

        def body(m, _):
            r = pl.ds(aligned(m * span, 16), span)
            y = dot(g3[0, r, :], w_own[c, :], ((1,), (1,))) + dot(g3[1, r, :], w_far[c, :], ((1,), (1,)))
            store(r, c, y)
            return 0

        lax.fori_loop(0, 2, body, 0)

    env = dict(summed=set(), vtot=vtot, column=column, space=space, ar_send=ar_send, ar_recv=ar_recv,
               ar_other=ar_other, o=o, section=section, here={"batch": b})
    blocks = {
        (1, 0): f_far.at[pl.ds(0, W), :],
        (1, 1): p_far.at[pl.ds(0, W), :],
        (0, 0): wc.at[1, 1],
        (0, 1): wr1,
    }
    parts = {}
    for layer in (1, 0):
        for index in range(2 * PAIRS):
            part, side = index // PAIRS, index % PAIRS

            def lane_of(sec, part=part, side=side):
                return (sec if part == 0 else 1 - sec) * W + side * 2 * PART

            block = blocks[layer, part].at[:, pl.ds(side * 2 * PART, 2 * PART)]
            parts[layer, index] = Reduction(env, layer, index, block, orders, lane_of)
    order = Order()

    def weight_grads(layer, part, c):
        weight_part(blocks[layer, part], g3.at[part], c)
        order.work(2.8)
        for k in range(c * HALF // PART, (c + 1) * HALF // PART):
            order.begin(parts[layer, part * PAIRS + k // 2], k % 2)

    def arrived(sends):
        for made in sends:
            made.wait()

    send_f = []
    for m in range(2):
        by_units(frames, f_own, m)
        fetch(grad_out, m).start()
        if m == 0:
            wait_heads(frames, 1)
        patch_heads(f_own, m)
        here = pl.ds(m * span, span)
        made = across(f_own.at[here, :], f_far.at[here, :], (0, 24)[m])
        made.start()
        send_f.append(made)
    start_across_w(1, w_plan(1), slot_of[1])
    stage_wait(cnt_plane, 0)
    stage_start(cnt_line, 0, add_slots(cnt_plane))
    wait_w(0, w_plan(0), slot_of[0], 0)
    matmul_to(rows.at[0], f_own, wc.at[0, 0], True, 0)
    matmul_to(rows.at[0], f_own, wc.at[0, 0], True, 1)
    wait_w(0, w_plan(0), slot_of[0], 1)
    for made in send_f:
        made.wait()

    @pl.when(section == 1)
    def _():
        heads_copy(grad_out, 2).start()

    matmul_to(rows.at[0], f_far, wc.at[0, 1], False, 0)
    forward_stats(0, 0)
    matmul_to(rows.at[0], f_far, wc.at[0, 1], False, 1)
    forward_middle(0, 0)
    forward_stats(0, 1)
    send_vec.wait_send()
    across(vecs.at[other], vecs.at[other], 3).wait_recv()
    by_units(grad_out, g3.at[1], 0)
    wait_heads(grad_out, 2)
    patch_heads(g3.at[1], 0)
    stage_wait(cnt_line, 0)
    counts[...] = add_slots(cnt_line)
    forward_end(0, 0)
    forward_middle(0, 1)
    sends = [forward_scan(0, 0, True)]
    forward_end(0, 1)
    sends.append(forward_scan(0, 1, True))
    wait_w(1, w_plan(1), slot_of[1], 0)
    matmul_to(rows.at[1], p_own, wc.at[1, 0], True, 0)
    matmul_to(rows.at[1], p_own, wc.at[1, 0], True, 1)
    wait_w(1, w_plan(1), slot_of[1], 1)
    for made in sends:
        made.wait()
    matmul_to(rows.at[1], p_far, wc.at[1, 1], False, 0)
    forward_stats(1, 0)
    done_w(0, w_plan(0), slot_of[0])

    start_local_w(0, late_plan, slot_of[2])
    start_across_w(0, late_plan, slot_of[2])

    @pl.when(section == 1)
    def _():
        wc[0, 1, width - late_row :, :] = jnp.zeros((W - width + late_row, W), BF16)

    def source_level():
        def body(i, acc):
            r = pl.ds(aligned(i * (2 * seqs), 16), 2 * seqs)
            return acc + fold(wide(live[r, :], 8) * f_own[r, :].astype(F32))

        acc = repeat(2 * pairs, body, jnp.zeros((8, W), F32), 3)
        levels[0:1, :] = jnp.sum(acc, axis=0, keepdims=True)

    matmul_to(rows.at[1], p_far, wc.at[1, 1], False, 1)
    forward_middle(1, 0)
    forward_stats(1, 1)
    by_units(grad_out, g3.at[1], 1)
    patch_heads(g3.at[1], 1)
    forward_end(1, 0)
    forward_middle(1, 1)
    forward_scan(1, 0, False)
    backward_scan(1, 0, g3.at[1])
    backward_stats(1, 0)
    forward_end(1, 1)
    source_level()
    level_plane, level_line = in_plane(wide_p, 0), in_line(wide_z, 0)
    stage_start(level_plane, 9, jnp.concatenate([levels[0:2, :], jnp.zeros((6, W), F32)], axis=0))
    forward_scan(1, 1, False)
    backward_middle(1, 0)
    stage_wait(level_plane, 9)
    stage_start(level_line, 9, add_slots(level_plane))
    backward_scan(1, 1, g3.at[1])
    backward_stats(1, 1)
    pl.semaphore_signal(credit.at[0], inc=1, device_id=sibling, device_id_type=MESH)
    backward_end(1, 0)
    pl.semaphore_wait(credit.at[0], 1)
    sends = [grad_rows(1, 0, 20)]
    transpose(p_own, 0, W // 256)
    backward_middle(1, 1)
    transpose(p_own, W // 256)
    stage_wait(level_line, 9)
    levels[2:4, :] = (add_slots(level_line) / wide(counts[0:1, :] + counts[2:3, :], 8))[0:2]
    transpose_level(p_own, 1)
    backward_end(1, 1)
    sends.append(grad_rows(1, 1, 20))
    sums_start(1)
    weight_grads(1, 0, 0)
    sums_middle(1)
    weight_grads(1, 0, 1)
    sums_end(1)
    arrived(sends)
    weight_grads(1, 1, 0)
    weight_grads(1, 1, 1)
    sums_there(1)
    wait_w(1, w_plan(1), slot_of[1], 2)
    done_w(1, w_plan(1), slot_of[1])

    def keep_down(r, c, y):
        p_own[r, c] = y.astype(BF16)

    source_grad(keep_down, wc.at[1, 0], wr1, 0)
    order.work(4.0)
    source_grad(keep_down, wc.at[1, 0], wr1, 1)
    pl.semaphore_signal(credit.at[1], inc=1, device_id=sibling, device_id_type=MESH)
    order.work(4.0)
    backward_scan(0, 0, p_own, lambda: order.work(1.8))
    backward_stats(0, 0)
    backward_scan(0, 1, p_own, lambda: order.work(1.8))
    backward_stats(0, 1)
    transpose(f_own, 0, W // 256)
    backward_middle(0, 0)
    backward_middle(0, 1)
    transpose(f_own, W // 256)
    transpose_level(f_own, 0)
    order.work(7.0)
    backward_end(0, 0)
    pl.semaphore_wait(credit.at[1], 1)
    sends = [grad_rows(0, 0, 22)]
    backward_end(0, 1)
    sends.append(grad_rows(0, 1, 22))
    sums_start(0)
    order.work(3.6)
    weight_grads(0, 0, 0)
    weight_grads(0, 0, 1)
    arrived(sends)
    weight_grads(0, 1, 0)
    weight_grads(0, 1, 1)
    wait_w(0, late_plan, slot_of[2], 0)
    wait_w(0, late_plan, slot_of[2], 1)
    done_w(0, late_plan, slot_of[2])

    def keep_source(r, c, y):
        rows[0, r, c] = y

    fetch(grad_out, 0).start()
    fetch(grad_out, 1).start()
    source_grad(keep_source, wc.at[0, 0], wc.at[0, 1], 0)
    order.work(4.0)
    sums_middle(0)
    source_grad(keep_source, wc.at[0, 0], wc.at[0, 1], 1)
    order.work(4.0)
    sums_end(0)
    sums_there(0)

    def give(m):
        return pltpu.make_async_copy(staged.at[m], gf.at[m], stage_sem.at[m])

    for m in range(2):
        fetch(grad_out, m).wait()

        def finish_frames(i, _, m=m):
            straight = staged[m, pl.ds(2 * i, 2)].astype(F32).reshape(2 * seqs, half)
            y = rows[0, pl.ds(aligned(m * span + 2 * i * seqs, 8), 2 * seqs), :]
            y = jnp.where(section == 0, y[:, :half], y[:, late_shift : late_shift + half])
            staged[m, pl.ds(2 * i, 2)] = (y + straight).reshape(2, seqs, half).astype(BF16)
            return 0

        repeat(pairs, finish_frames, 0, 3)
        give(m).start()
        order.work(3.0)
    order.drain()
    for m in range(2):
        give(m).wait()

    for layer in range(2):

        @pl.when(section == layer)
        def _(layer=layer):
            pltpu.make_async_copy(tot.at[layer], v.at[section], v_sems.at[0]).wait()
            pltpu.make_async_remote_copy(
                src_ref=tot.at[layer], dst_ref=v.at[other], send_sem=v_sems.at[1], recv_sem=v_sems.at[2],
                device_id=sibling, device_id_type=MESH,
            ).wait_recv()

        @pl.when(section != layer)
        def _(layer=layer):
            v_across(layer).wait_send()

    own_part, far_part = v[section], v[other]
    first = jnp.where(section == 0, own_part, far_part)
    second = jnp.where(section == 0, far_part, own_part)
    for row, terms in ((0, (2, 3)), (1, (0, 1)), (2, (4,))):
        for lane, x in ((0, first), (W, second)):
            total = x[terms[0] : terms[0] + 1, :]
            for k in terms[1:]:
                total = total + x[k : k + 1, :]
            vectors[row : row + 1, lane : lane + W] = total
    squares = jnp.sum(first[5:7, :] + second[5:7, :], axis=1, keepdims=True)
    root = jnp.sqrt(squares / (first[7:8, 0:1] * width))
    for k in range(2):
        vectors[3 + k : 4 + k, :] = jnp.broadcast_to(root[k : k + 1], (1, 2 * W))
    vectors[5:8, :] = jnp.zeros((3, 2 * W), F32)


def write_results(o, gf, vectors, grad_weight, grad_frames, grad_gains, grad_shifts, grad_recurs, table):
    width = grad_weight.shape[2]
    grad_weight[0] = o[...][:, :width].astype(F32)
    grad_frames[...] = gf[...]

    @pl.when(pl.program_id(0) == 0)
    def _():
        for k, out in enumerate((grad_gains, grad_shifts, grad_recurs)):
            out[...] = vectors[k : k + 1, 0:width]
        table[...] = jnp.concatenate([vectors[3:4, 0:1], vectors[4:5, 0:1]], axis=1)


def results(o, gf, vectors):
    micro, steps, seqs, half = gf.shape
    width = 2 * half
    count = W * 2 // 256
    frames = micro * steps // count
    whole = lambda shape: pl.BlockSpec(shape, lambda i: (0, 0))
    out = pl.pallas_call(
        write_results,
        grid=(count,),
        in_specs=[
            pl.BlockSpec((256, 2 * W), lambda i: (i, 0)),
            pl.BlockSpec((frames, seqs, half), lambda i: (i, 0, 0)),
            whole((8, 2 * W)),
        ],
        out_specs=(
            pl.BlockSpec((1, 256, width), lambda i: (0, i, 0)),
            pl.BlockSpec((frames, seqs, half), lambda i: (i, 0, 0)),
            whole((1, width)),
            whole((1, width)),
            whole((1, width)),
            whole((1, 2)),
        ),
        out_shape=(
            jax.ShapeDtypeStruct((1, width, width), F32),
            jax.ShapeDtypeStruct((micro * steps, seqs, half), BF16),
            jax.ShapeDtypeStruct((1, width), F32),
            jax.ShapeDtypeStruct((1, width), F32),
            jax.ShapeDtypeStruct((1, width), F32),
            jax.ShapeDtypeStruct((1, 2), F32),
        ),
        compiler_params=pltpu.CompilerParams(vmem_limit_bytes=64 * 1024 * 1024),
    )(o.reshape(2 * W, 2 * W), gf.reshape(micro * steps, seqs, half), vectors)
    return out[1].reshape(gf.shape), out[0], *out[2:]


def whole_step(dims, frames, grad_out, weights, gains, shifts, recurs, lengths, masks):
    nz, ny, nx = dims
    micro, steps, seqs, half = frames.shape
    width = 2 * half
    views = seqs // lengths.shape[1]
    rows = micro * steps * seqs
    np_ = ny * nx
    wide_rows = (rows + 16 + 127) // 128 * 128
    across_first = max(nx, ny, nz if np_ == 1 else 1)
    copies = 2 * (nx + ny + nz) + across_first
    came_rows = (nx - 1) * (W // nx) + (ny - 1) * (W // np_) + (nz - 1) * max(W // np_ // nz, 16)
    any_ = pl.BlockSpec(memory_space=pl.ANY)
    held = pl.BlockSpec(memory_space=pltpu.VMEM)
    dma = pltpu.SemaphoreType.DMA
    return pl.pallas_call(
        functools.partial(kernel, dims, steps, seqs, views),
        out_shape=(
            jax.ShapeDtypeStruct((2, W, 2 * W), BF16),
            jax.ShapeDtypeStruct(frames.shape, BF16),
            jax.ShapeDtypeStruct((8, 2 * W), F32),
        ),
        in_specs=[any_] * 3 + [held] * 5,
        out_specs=(any_, any_, held),
        scratch_shapes=[
            pltpu.VMEM((wide_rows, W), BF16),
            pltpu.VMEM((rows, W), BF16),
            pltpu.VMEM((wide_rows, W), BF16),
            pltpu.VMEM((rows, W), BF16),
            pltpu.VMEM((2, wide_rows, W), BF16),
            pltpu.VMEM((2, 2, W, W), BF16),
            pltpu.VMEM((W, W), BF16),
            pltpu.VMEM((W, wide_rows), BF16),
            pltpu.VMEM((rows, 128), F32),
            pltpu.VMEM((128, 128), F32),
            pltpu.VMEM(frames.shape, BF16),
            pltpu.VMEM((micro, steps, seqs, 128), BF16),
            pltpu.VMEM((5, W, (width - W) % 128), BF16),
            pltpu.VMEM((2, 8, W), F32),
            pltpu.VMEM((2, 8, 2 * W), F32),
            pltpu.VMEM((2, rows, W), F32),
            pltpu.VMEM((2, rows, W), F32),
            pltpu.VMEM((2, 8, W), F32),
            pltpu.VMEM((2, 8, W), F32),
            pltpu.VMEM((2, 2, 8, W), F32),
            pltpu.VMEM((8, W), F32),
            pltpu.VMEM((2, W, 128), BF16),
            pltpu.VMEM((8, 128), F32),
            pltpu.VMEM((1, np_, 8, 128), F32),
            pltpu.VMEM((1, nz, 8, 128), F32),
            pltpu.VMEM((4, np_, 8, QUART), F32),
            pltpu.VMEM((4, nz, 8, QUART), F32),
            pltpu.VMEM((2, np_, 8, W), F32),
            pltpu.VMEM((2, nz, 8, W), F32),
            pltpu.VMEM((2, 2 * PAIRS, max(came_rows, W), 2 * PART), BF16),
            dma((3, 27)),
            dma((3,)),
            dma((2,)),
            pltpu.SemaphoreType.REGULAR((2,)),
            dma((12, max(np_, 2))),
            dma((12, max(np_, 2))),
            dma((12, max(nz, 2))),
            dma((12, max(nz, 2))),
            dma((2, 2 * PAIRS, 2, copies)),
            dma((2, 2 * PAIRS, 2, copies)),
            dma((2, 2 * PAIRS, 2, across_first)),
        ],
        compiler_params=pltpu.CompilerParams(
            collective_id=0, has_side_effects=True, vmem_limit_bytes=64 * 1024 * 1024
        ),
    )(frames, grad_out, weights, gains, shifts, recurs, lengths, masks)


def shards(dims, frames, grad_out, weights, gains, shifts, recurs, lengths, masks):
    return results(*whole_step(dims, frames, grad_out, weights, gains, shifts, recurs, lengths, masks))


def solution(mesh):
    in_specs = (
        P(None, None, "batch", "section"),
        P(None, None, "batch", "section"),
        P("section", None, None),
        P("section", None),
        P("section", None),
        P("section", None),
        P(None, "batch"),
        P(None, None, "batch"),
    )
    out_specs = (
        P(None, None, "batch", "section"),
        P("section", None, None),
        P("section", None),
        P("section", None),
        P("section", None),
        P("section", None),
    )
    body = functools.partial(shards, grid_of(mesh.shape["batch"]))
    return jax.shard_map(body, mesh=mesh, in_specs=in_specs, out_specs=out_specs, check_vma=False)
```

```python
import functools

import jax
import jax.numpy as jnp
from jax import lax
from jax.experimental import pallas as pl
from jax.experimental.pallas import tpu as pltpu
from jax.sharding import PartitionSpec as P

EPS = 1e-05
W = 1024
HALF = W // 2
QUART = W // 4
MESH = pl.DeviceIdType.MESH
F32 = jnp.float32
BF16 = jnp.bfloat16


def grid_of(size):
    if size == 16:
        return (4, 2, 2)
    if size == 128:
        return (8, 4, 4)
    return (size, 1, 1)


def aligned(x, k):
    return pl.multiple_of(x, k)


def wide(x, reps):
    return jnp.concatenate([x] * reps, axis=1)


def fold(x):
    rows = x.shape[0]
    total = x[0:8]
    for k in range(8, rows, 8):
        total = total + x[k : k + 8]
    return total


def dot(a, b, dims):
    return lax.dot_general(a, b, (dims, ((), ())), preferred_element_type=F32)


class Reduction:
    def __init__(self, env, layer, index, block, orders, lane_of):
        self.env, self.layer, self.index, self.block, self.orders = env, layer, index, block, orders
        self.lane_of = lane_of
        self.space = env["space"].at[layer, index]
        self.depth = len(orders[0])
        self.regions = [self.halves(i, order) for i, order in enumerate(orders)]
        self.step = 0
        self.waits = []
        depth = self.depth
        self.steps = [functools.partial(self.scatter, 0)]
        self.steps += [functools.partial(self.scatter, k) for k in range(1, depth)]
        self.steps += [functools.partial(self.gather, k) for k in range(depth - 1, 0, -1)]
        self.steps += [self.give, self.finish]

    def halves(self, i, order):
        row, rows, lane, lanes = 0, W, i * QUART, QUART
        out = [(row, rows, lane, lanes)]
        for axis in order:
            if rows > 16:
                rows //= 2
                row = row + axis["bit"] * rows
            else:
                lanes //= 2
                lane = lane + axis["bit"] * lanes
            out.append((row, rows, lane, lanes))
        return out

    @property
    def free_to_go(self):
        return self.step != self.depth or self.layer in self.env["summed"]

    @property
    def done(self):
        return self.step >= len(self.steps)

    def advance(self):
        self.sent = []
        self.steps[self.step]()
        self.step += 1
        return self.sent

    def remote(self, i, src, dst, slot, where, recv=None):
        sems = (self.layer, self.index, i, slot)
        return pltpu.make_async_remote_copy(
            src_ref=src, dst_ref=dst, send_sem=self.env["ar_send"].at[sems],
            recv_sem=self.env["ar_recv"].at[sems] if recv is None else recv, device_id=where, device_id_type=MESH,
        )

    def wait(self):
        for made, came in self.waits:
            made.wait_send()
            came.wait_recv()
        self.waits = []

    def came_at(self, i, k):
        row = sum(r[1] for r in self.regions[i][1 : k + 1])
        _, rows, _, lanes = self.regions[i][k + 1]
        return row, rows, i * QUART, lanes

    def scatter(self, k):
        if k > 0:
            self.wait()
            self.add(k - 1)
        for i, order in enumerate(self.orders):
            self.scatter_part(i, k, order[k])

    def start_part(self, i):
        self.sent = []
        self.scatter_part(i, 0, self.orders[i][0])
        if i == 1:
            self.step = 1
        return self.sent

    def scatter_part(self, i, k, axis):
        row, rows, lane, lanes = self.regions[i][k]
        _, rows2, _, lanes2 = self.regions[i][k + 1]
        give_row = row + (1 - axis["bit"]) * rows2 if rows2 < rows else row
        give_lane = lane if rows2 < rows else lane + (1 - axis["bit"]) * lanes2
        src = self.block.at[pl.ds(aligned(give_row, 16), rows2), pl.ds(aligned(give_lane, 128), lanes2)]
        at, n, at_lane, n_lanes = self.came_at(i, k)
        dst = self.space.at[pl.ds(at, n), pl.ds(at_lane, n_lanes)]
        made = self.remote(i, src, dst, k, axis["partner"])
        made.start()
        self.waits.append((made, made))
        self.sent.append((axis["link"], rows2 * lanes2 * 2))

    def add(self, k, last=False):
        rows = self.regions[0][k + 1][1]
        size = min(rows, 32)
        out = []
        for i in range(2):
            row, _, lane, lanes = self.regions[i][k + 1]
            at, _, at_lane, _ = self.came_at(i, k)
            lane = aligned(lane, 128)
            extra = None
            if last:
                part = self.index // 2
                first = aligned((self.index % 2) * HALF + lane, 128)
                extra = self.env["vtot"][self.layer, part : part + 1, pl.ds(first, lanes)]
            out.append((row, lane, lanes, at, at_lane, self.local(i, k + 1)[0], extra))

        def body(j, _):
            for row, lane, lanes, at, at_lane, home, extra in out:
                here = pl.ds(aligned(row + j * size, 16), size)
                total = self.block[here, pl.ds(lane, lanes)].astype(F32)
                total = total + self.space[pl.ds(aligned(at + j * size, 16), size), pl.ds(at_lane, lanes)].astype(F32)
                if last:
                    column = self.env["column"][self.layer, here, :].astype(F32)
                    total = total + wide(column, lanes // 128) * extra
                    to = pl.ds(aligned(home + j * size, 16), size)
                    self.space[to, pl.ds(lane, lanes)] = total.astype(BF16)
                else:
                    self.block[here, pl.ds(lane, lanes)] = total.astype(BF16)
            return 0

        lax.fori_loop(0, rows // size, body, 0)

    def local(self, i, k):
        row, rows, lane, lanes = self.regions[i][k]
        return row - self.regions[i][1][0], rows, lane, lanes

    def gather(self, k):
        self.wait()
        if k == self.depth - 1:
            self.add(k, last=True)
        for i, order in enumerate(self.orders):
            axis = order[k]
            row, rows, lane, lanes = self.local(i, k + 1)
            row0, rows0, lane0, lanes0 = self.local(i, k)
            if rows0 > rows:
                far = (row0 + (1 - axis["bit"]) * rows, rows, lane, lanes)
            else:
                far = (row, rows, lane0 + (1 - axis["bit"]) * lanes, lanes)
            refs = [
                self.space.at[pl.ds(aligned(r, 16), n), pl.ds(aligned(c, 128), w)]
                for r, n, c, w in ((row, rows, lane, lanes), far)
            ]
            made = self.remote(i, refs[0], refs[0], self.depth + k, axis["partner"])
            made.start()
            self.waits.append((made, self.remote(i, refs[1], refs[1], self.depth + k, axis["partner"])))
            self.sent.append((axis["link"], rows * lanes * 2))

    def result(self, i, bit, section):
        rows = self.regions[i][1][1]
        lane = aligned(self.lane_of(section) + i * QUART, QUART)
        return self.env["o"].at[section, pl.ds(aligned(bit * rows, 16), rows), pl.ds(lane, QUART)]

    def gathered(self, i):
        return self.space.at[pl.ds(0, self.regions[i][1][1]), pl.ds(i * QUART, QUART)]

    def deliver(self, i, near, straight):
        axis, section = self.orders[i][0], self.env["section"]
        slot = 2 * self.depth + (0 if near else 1)
        recv = None if straight else self.env["ar_other"].at[self.layer, self.index, i, 0 if near else 1]
        where = dict(self.env["here"] if near else axis["partner"], section=self.layer)
        return self.remote(i, self.gathered(i), self.result(i, axis["bit"], section), slot, where, recv)

    def arrival(self, i, near, straight):
        axis, section = self.orders[i][0], self.env["section"]
        slot = 2 * self.depth + (0 if near else 1)
        recv = None if straight else self.env["ar_other"].at[self.layer, self.index, i, 0 if near else 1]
        bit = axis["bit"] if near else 1 - axis["bit"]
        frm = section if straight else 1 - section
        where = dict(self.env["here"] if near else axis["partner"], section=frm)
        return self.remote(i, self.gathered(i), self.result(i, bit, frm), slot, where, recv)

    def kept(self, i):
        sem = self.env["ar_recv"].at[self.layer, self.index, i, 2 * self.depth]
        return pltpu.make_async_copy(
            self.gathered(i), self.result(i, self.orders[i][0]["bit"], self.env["section"]), sem
        )

    def give(self):
        self.wait()

        @pl.when(self.env["section"] == self.layer)
        def _():
            for i in range(2):
                self.deliver(i, False, True).start()
                self.kept(i).start()

        @pl.when(self.env["section"] != self.layer)
        def _():
            for i in range(2):
                self.deliver(i, False, False).start()
                self.deliver(i, True, False).start()

        for i, order in enumerate(self.orders):
            self.sent.append((order[0]["link"], self.regions[i][1][1] * QUART * 2))

    def finish(self):
        @pl.when(self.env["section"] == self.layer)
        def _():
            for i in range(2):
                self.kept(i).wait()
                self.deliver(i, False, True).wait_send()
                self.arrival(i, False, True).wait_recv()
                self.arrival(i, True, False).wait_recv()
                self.arrival(i, False, False).wait_recv()

        @pl.when(self.env["section"] != self.layer)
        def _():
            for i in range(2):
                self.deliver(i, False, False).wait_send()
                self.deliver(i, True, False).wait_send()


class Order:
    RATE, HOP = 52e3, 2.2

    def __init__(self):
        self.now = 0.0
        self.free = {}
        self.going = []

    def sent(self, copies):
        end = self.now
        for link, size in copies:
            self.free[link] = max(self.now, self.free.get(link, 0.0)) + size / self.RATE
            end = max(end, self.free[link])
        return end + self.HOP

    def begin(self, one, i):
        end = self.sent(one.start_part(i))
        if i == 0:
            one.due = end
        else:
            one.due = max(one.due, end)
            self.going.append(one)

    def advance(self, one):
        self.now = max(self.now, one.due) + 0.4
        one.due = self.sent(one.advance())
        if one.done:
            self.going.remove(one)

    def work(self, cost):
        self.now += cost
        while True:
            due = [x for x in self.going if x.due <= self.now and x.free_to_go]
            if not due:
                return
            self.advance(min(due, key=lambda x: x.due))

    def drain(self):
        while self.going:
            self.advance(min(self.going, key=lambda x: x.due))


def kernel(dims, steps, seqs, views, frames, grad_out, weights, gains, shifts, recurs, lengths, masks, o, gf, vectors, f_own, f_far, p_own, p_far, g3, wc, wr1, src_t, live, turn,
           staged, heads, tails, v, vecs, rows, hid, coef, tot, vtot, levels, column, counts, cnt_p, cnt_z, slim_p, slim_z,
           wide_p, wide_z, space, sems, v_sems, stage_sem, credit, pl_send, pl_recv, z_send, z_recv, ar_send, ar_recv,
           ar_other):
    nz, ny, nx = dims
    np_ = ny * nx
    span = steps * seqs
    total_rows = 2 * span
    sent_rows = total_rows + 16
    pairs = steps // 2
    section = lax.axis_index("section")
    other = 1 - section
    b = lax.axis_index("batch")
    mp = lax.rem(b, np_)
    mz = b // np_

    def at_plane(i):
        return {"batch": b - mp + i}

    def at_z(i):
        return {"batch": b + (i - mz) * np_}

    bits = []
    for link, count, stride in (("x", nx, 1), ("y", ny, nx), ("z", nz, np_)):
        while count > 1:
            bit = lax.rem(b // stride, 2)
            bits.append(dict(bit=bit, partner={"batch": b + (1 - 2 * bit) * stride}, link=link))
            count //= 2
            stride *= 2
    sibling = {"section": other}

    def local(src, dst, slot):
        return pltpu.make_async_copy(src, dst, sems.at[0, slot])

    def across(src, dst, slot):
        return pltpu.make_async_remote_copy(
            src_ref=src, dst_ref=dst, send_sem=sems.at[1, slot], recv_sem=sems.at[2, slot],
            device_id=sibling, device_id_type=MESH,
        )

    half = frames.shape[3]
    width = 2 * half
    lead = W - half
    rest = width - W
    full = rest // 128 * 128

    def fetch(source, m):
        return pltpu.make_async_copy(source.at[m], staged.at[m], stage_sem.at[m])

    def by_units(source, target, m):
        fetch(source, m).wait()

        @pl.when(section == 0)
        def _():
            pad = jnp.zeros((2 * seqs, lead), F32)

            def place(i, _):
                x = staged[m, pl.ds(2 * i, 2)].astype(F32).reshape(2 * seqs, half)
                to = pl.ds(aligned(m * span + 2 * i * seqs, 16), 2 * seqs)
                target[to, :] = jnp.concatenate([x, pad], axis=1).astype(BF16)
                return 0

            lax.fori_loop(0, pairs, place, 0)

        @pl.when(section == 1)
        def _():
            pad = jnp.zeros((2 * seqs, 2 * lead), F32)

            def place(i, _):
                x = staged[m, pl.ds(2 * i, 2)].astype(F32).reshape(2 * seqs, half)
                to = pl.ds(aligned(m * span + 2 * i * seqs, 16), 2 * seqs)
                target[to, :] = jnp.concatenate([x[:, lead:], pad], axis=1).astype(BF16)
                return 0

            lax.fori_loop(0, pairs, place, 0)

    def patch_heads(target, m):
        @pl.when(section == 0)
        def _():
            lane = lax.broadcasted_iota(jnp.int32, (2 * seqs, 128), 1)

            def place(i, _):
                to = pl.ds(aligned(m * span + 2 * i * seqs, 16), 2 * seqs)
                head = heads[m, pl.ds(2 * i, 2)].astype(F32).reshape(2 * seqs, 128)
                head = pltpu.roll(head, 128 - lead, 1)
                old = target[to, W - 128 :].astype(F32)
                target[to, W - 128 :] = jnp.where(lane < 128 - lead, old, head).astype(BF16)
                return 0

            lax.fori_loop(0, pairs, place, 0)

    def pieces(row, count, u, block, spot):
        r = pl.ds(row, count)
        to = pl.ds(0, count)
        if u == 0:
            return [(weights.at[0, r, pl.ds(0, W)], block.at[to, :])]
        return [
            (weights.at[0, r, pl.ds(W, full)], block.at[to, pl.ds(0, full)]),
            (weights.at[0, r, pl.ds(W + full, rest - full)], tails.at[spot, to, :]),
        ]

    rows_of = {0: (0, W), 1: (W, rest)}

    def w_plan(layer):
        mine, far = rows_of[layer], rows_of[1 - layer]
        plan = [
            (mine, layer, far, 1 - layer, wc.at[layer, 0], 2 * layer),
            (far, layer, mine, 1 - layer, wc.at[layer, 1], 2 * layer + 1),
        ]
        if layer == 1:
            plan.append((mine, 0, far, 1, wr1, 4))
        return plan

    late_row = (width - half) // 16 * 16
    late_shift = half - late_row
    late_plan = [
        ((0, W), 0, (late_row, width - late_row), 1, wc.at[0, 0], 0),
        ((0, W), 1, (late_row, width - late_row), 0, wc.at[0, 1], 1),
    ]
    slot_of = {0: 4, 1: 8, 2: 14}

    def local_w(plan, base, which):
        r, u, _, _, block, spot = plan[which]
        return [local(a, t, base + 2 * which + i) for i, (a, t) in enumerate(pieces(*r, u, block, spot))]

    def across_w(plan, base, which):
        _, _, r, u, block, spot = plan[which]
        return [across(a, t, base + 2 * which + i) for i, (a, t) in enumerate(pieces(*r, u, block, spot))]

    def start_local_w(layer, plan, base):
        @pl.when(section == layer)
        def _():
            for which in range(len(plan)):
                for made in local_w(plan, base, which):
                    made.start()

    def start_across_w(layer, plan, base):
        @pl.when(section == layer)
        def _():
            for which in range(len(plan)):
                for made in across_w(plan, base, which):
                    made.start()

    def last_units(block, spot):
        def body(i, _):
            r = pl.ds(aligned(i * 128, 128), 128)
            x = tails[spot, r, :].astype(F32)
            x = jnp.concatenate([x, jnp.zeros((128, 128 - x.shape[1]), F32)], axis=1)
            block[r, full:] = x.astype(BF16)
            return 0

        lax.fori_loop(0, W // 128, body, 0)

    def wait_w(layer, plan, base, which):
        _, own_u, _, far_u, block, spot = plan[which]

        @pl.when(section == layer)
        def _():
            for made in local_w(plan, base, which):
                made.wait()
            if own_u == 1:
                last_units(block, spot)

        @pl.when(section != layer)
        def _():
            for made in across_w(plan, base, which):
                made.wait_recv()
            if far_u == 1:
                last_units(block, spot)

    def done_w(layer, plan, base):
        @pl.when(section == layer)
        def _():
            for which in range(len(plan)):
                for made in across_w(plan, base, which):
                    made.wait_send()

    def heads_copy(source, slot):
        return across(source.at[:, :, :, pl.ds(0, 128)], heads, slot)

    def wait_heads(source, slot):
        @pl.when(section == 0)
        def _():
            heads_copy(source, slot).wait_recv()

        @pl.when(section == 1)
        def _():
            heads_copy(source, slot).wait_send()

    fetch(frames, 0).start()
    fetch(frames, 1).start()
    for layer in range(2):
        start_local_w(layer, w_plan(layer), slot_of[layer])

    barrier = pltpu.get_barrier_semaphore()
    greeted = [dict(sibling)]
    greeted += [at_plane(lax.rem(mp + k, np_)) for k in range(1, np_)]
    greeted += [at_z(lax.rem(mz + k, nz)) for k in range(1, nz)]
    greeted += [dict(axis["partner"], section=other) for axis in bits]
    for where in greeted:
        pl.semaphore_signal(barrier, inc=1, device_id=where, device_id_type=MESH)

    for k, (x, fill) in enumerate(((gains, 0.0), (shifts, -1e30), (recurs, 0.0))):
        vecs[section, k : k + 1, 0:width] = x[...]
        vecs[section, k : k + 1, width:] = jnp.full((1, 2 * W - width), fill, F32)
    vecs[section, 3:8, :] = jnp.zeros((5, 2 * W), F32)

    gap = jnp.zeros((W - rest, W), BF16)

    @pl.when(section == 0)
    def _():
        wc[0, 1, rest:, :] = gap
        wc[1, 1, rest:, :] = gap

    @pl.when(section == 1)
    def _():
        wc[0, 0, rest:, :] = gap
        wc[1, 0, rest:, :] = gap
        wr1[rest:, :] = gap

    for spot in (0, 2):
        tails[spot, rest:, :] = jnp.zeros((W - rest, rest - full), BF16)
    for spare in (f_own, p_own, g3.at[0], g3.at[1]):
        spare[sent_rows:, :] = jnp.zeros((spare.shape[0] - sent_rows, W), BF16)

    pl.semaphore_wait(barrier, len(greeted))

    @pl.when(section == 1)
    def _():
        heads_copy(frames, 1).start()

    start_across_w(0, w_plan(0), slot_of[0])
    send_vec = across(vecs.at[section], vecs.at[section], 3)
    send_vec.start()

    def stage_copy(where, rnd, slot, k, back):
        buf, parity, size, me, at, send, recv = where
        there = at(lax.rem(me + (size - k if back else k), size))
        ref = buf.at[parity, slot]
        return pltpu.make_async_remote_copy(
            src_ref=ref, dst_ref=ref, send_sem=send.at[rnd, k], recv_sem=recv.at[rnd, k],
            device_id=there, device_id_type=MESH,
        )

    def in_plane(buf, parity):
        return (buf, parity, np_, mp, at_plane, pl_send, pl_recv)

    def in_line(buf, parity):
        return (buf, parity, nz, mz, at_z, z_send, z_recv)

    def stage_start(where, rnd, value):
        buf, parity, size, me = where[:4]
        buf[parity, me] = value
        for k in range(1, size):
            stage_copy(where, rnd, me, k, False).start()

    def stage_wait(where, rnd):
        size, me = where[2:4]
        for k in range(1, size):
            stage_copy(where, rnd, me, k, False).wait_send()
            stage_copy(where, rnd, lax.rem(me + size - k, size), k, True).wait_recv()

    def add_slots(where):
        buf, parity, size = where[:3]
        total = buf[parity, 0]
        for k in range(1, size):
            total = total + buf[parity, k]
        return total

    groups = lengths.shape[1]
    s_at = lax.broadcasted_iota(jnp.int32, (seqs, groups), 0)
    g_at = lax.broadcasted_iota(jnp.int32, (seqs, groups), 1) * views
    there = (s_at >= g_at) & (s_at < g_at + views)
    position = lax.broadcasted_iota(jnp.int32, (seqs, 128), 1)
    local_counts = []
    for m in range(2):
        turn[...] = jnp.zeros_like(turn)
        turn[0:steps, 0:seqs] = masks[m].astype(F32)
        mask = turn[...].T[0:seqs]
        length = jnp.broadcast_to(lengths[m : m + 1, :], (seqs, groups)).astype(F32)
        limit = jnp.sum(jnp.where(there, length, 0.0), axis=1, keepdims=True)
        alive = (position.astype(F32) < limit) & ((mask > 0.0) | (position == 0))
        alive = jnp.where(position < steps, alive.astype(F32), 0.0)
        total = jnp.zeros((seqs, 128), F32)
        for t in range(steps):
            at = m * span + t * seqs
            cells = jnp.broadcast_to(alive[:, t : t + 1], (seqs, 128))
            live[at : at + seqs, :] = cells
            total = total + cells
        local_counts.append(jnp.sum(total, axis=0, keepdims=True))
    n_own = jnp.concatenate(local_counts * 4, axis=0)

    cnt_plane, cnt_line = in_plane(cnt_p, 0), in_line(cnt_z, 0)
    stage_start(cnt_plane, 0, n_own)

    def vec_of(layer, k):
        return vecs[layer, k : k + 1, pl.ds(aligned(section * W, W), W)]

    def matmul_to(out, a, w, first, m):
        r = pl.ds(m * span, span)

        def body(i, _):
            c = pl.ds(aligned(i * HALF, HALF), HALF)
            y = dot(a[r, :], w[:, c], ((1,), (0,)))
            out[r, c] = y if first else out[r, c] + y
            return 0

        lax.fori_loop(0, 2, body, 0)

    def packed(x, y):
        return jnp.concatenate([z[:, k * QUART : (k + 1) * QUART] for z in (x, y) for k in range(4)], axis=0)

    def unpacked(x):
        return jnp.concatenate([x[k : k + 1] for k in range(4)], axis=1)

    def merge_slots(where, counts_of):
        buf, parity, size = where[:3]
        s = [buf[parity, k, 0:4, :] for k in range(size)]
        q = [buf[parity, k, 4:8, :] for k in range(size)]
        n = [wide(counts_of(k), 2) for k in range(size)]
        total, squares, count = sum(s[1:], s[0]), sum(q[1:], q[0]), sum(n[1:], n[0])
        mean = total / count
        for k in range(size):
            d = s[k] / n[k] - mean
            squares = squares + n[k] * d * d
        return jnp.concatenate([total, squares], axis=0)

    def slim_round(which, m):
        return 1 + 2 * which + m, in_plane(slim_p, 2 * m + which % 2), in_line(slim_z, 2 * m + which % 2)

    def forward_stats(layer, m):
        start = jnp.sum(rows[layer, m * span : m * span + seqs, :], axis=0, keepdims=True) * (1.0 / seqs)

        def body(i, carry):
            s, q = carry
            r = pl.ds(aligned(m * span + i * (2 * seqs), 16), 2 * seqs)
            d = rows[layer, r, :] - start
            kept = wide(live[r, :], 8) * d
            return s + fold(kept), q + fold(kept * d)

        zero = jnp.zeros((8, W), F32)
        s, q = lax.fori_loop(0, pairs, body, (zero, zero))
        s, q = jnp.sum(s, axis=0, keepdims=True), jnp.sum(q, axis=0, keepdims=True)
        n = wide(local_counts[m], 8)
        rnd, plane, _ = slim_round(layer, m)
        stage_start(plane, rnd, packed(s + n * start, jnp.maximum(q - s * s / n, 0.0)))

    def forward_middle(layer, m):
        rnd, plane, line = slim_round(layer, m)
        stage_wait(plane, rnd)
        stage_start(line, rnd, merge_slots(plane, lambda k: cnt_p[0, k, m : m + 1, :]))

    def forward_end(layer, m):
        rnd, _, line = slim_round(layer, m)
        stage_wait(line, rnd)
        value = merge_slots(line, lambda k: cnt_z[0, k, m : m + 1, :])
        count = wide(counts[m : m + 1, :], 8)
        mean = unpacked(value[0:4]) / count
        scale = lax.rsqrt(unpacked(value[4:8]) / count + EPS)
        coef[layer, 2 * m : 2 * m + 1, :] = mean
        coef[layer, 2 * m + 1 : 2 * m + 2, :] = scale
        slope = vec_of(layer, 0) * scale
        coef[layer, 4 + 2 * m : 5 + 2 * m, :] = slope
        coef[layer, 5 + 2 * m : 6 + 2 * m, :] = vec_of(layer, 1) - mean * slope

    def forward_scan(layer, m, passes):
        rec = vec_of(layer, 2)
        slope = coef[layer, 4 + 2 * m : 5 + 2 * m, :]
        shift = coef[layer, 5 + 2 * m : 6 + 2 * m, :]

        def body(i, carry):
            h, level = carry
            r = pl.ds(aligned(m * span + i * (2 * seqs), 16), 2 * seqs)
            x = rows[layer, r, :] * slope + shift
            lv = wide(live[r, :], 8)
            alive = lv > 0.0
            both = []
            for k in range(2):
                part = slice(k * seqs, (k + 1) * seqs)
                z = x[part] + rec * h
                soft = jnp.maximum(z, 0.0) + jnp.log(1.0 + jnp.exp(-jnp.abs(z)))
                h = jnp.where(alive[part], soft, h)
                both.append(h)
            two = jnp.concatenate(both, axis=0)
            hid[layer, r, :] = two
            if passes:
                p_own[r, :] = two.astype(BF16)
                level = level + fold(lv * two)
            return h, level

        _, level = lax.fori_loop(0, pairs, body, (jnp.zeros((seqs, W), F32), jnp.zeros((8, W), F32)))
        if not passes:
            return None
        level = jnp.sum(level, axis=0, keepdims=True)
        levels[1:2, :] = level if m == 0 else levels[1:2, :] + level
        here = pl.ds(m * span, span)
        made = across(p_own.at[here, :], p_far.at[here, :], 18 + m)
        made.start()
        return made

    def backward_scan(layer, m, above, between=lambda: None):
        gain, shift, recur = vec_of(layer, 0), vec_of(layer, 1), vec_of(layer, 2)
        for lq in range(4):
            lanes = slice(lq * QUART, (lq + 1) * QUART)
            gq, sq, rec = gain[:, lanes], shift[:, lanes], recur[:, lanes]
            mean = coef[layer, 2 * m : 2 * m + 1, lanes]
            scale = coef[layer, 2 * m + 1 : 2 * m + 2, lanes]

            def body(i, carry):
                down, s1, s2, rsum, sqh, sqa = carry
                i = pairs - 1 - i
                start = m * span + i * (2 * seqs)
                r = pl.ds(aligned(start, 16), 2 * seqs)
                before = pl.ds(aligned(jnp.maximum(start - seqs, 0), 8), seqs)
                normed = (rows[layer, r, lanes] - mean) * scale
                drive = gq * normed + sq
                h2 = hid[layer, r, lanes]
                hb = jnp.where(i > 0, hid[layer, before, lanes], 0.0)
                lv = wide(live[r, :], 2)
                up = above[r, lanes].astype(F32)
                res = f_own[r, lanes].astype(F32)
                aux = res + h2 if layer == 1 else res
                sqh = sqh + fold(lv * (h2 * h2))
                sqa = sqa + fold(lv * (aux * aux))
                grads = [None, None]
                for k in (1, 0):
                    part = slice(k * seqs, (k + 1) * seqs)
                    prior = h2[0:seqs] if k == 1 else hb
                    slope = 0.5 + 0.5 * jnp.tanh(0.5 * (drive[part] + rec * prior))
                    total = up[part] + down
                    gd = lv[part] * slope * total
                    down = (1.0 - lv[part]) * total + rec * gd
                    grads[k] = gd
                    rsum = rsum + fold(gd * prior)
                gd2 = jnp.concatenate(grads, axis=0)
                hid[layer, r, lanes] = gd2
                return down, s1 + fold(gd2), s2 + fold(gd2 * normed), rsum, sqh, sqa

            z8 = jnp.zeros((8, QUART), F32)
            _, s1, s2, rsum, sqh, sqa = lax.fori_loop(
                0, pairs, body, (jnp.zeros((seqs, QUART), F32), z8, z8, z8, z8, z8)
            )
            for k, x in ((m, s1), (2 + m, s2)):
                tot[layer, k : k + 1, lanes] = jnp.sum(x, axis=0, keepdims=True)
            for k, x in ((4, rsum), (5, sqh), (6, sqa)):
                x = jnp.sum(x, axis=0, keepdims=True)
                tot[layer, k : k + 1, lanes] = x if m == 0 else tot[layer, k : k + 1, lanes] + x
            between()

    def backward_stats(layer, m):
        rnd, plane, _ = slim_round(3 - layer, m)
        stage_start(plane, rnd, packed(tot[layer, m : m + 1, :], tot[layer, 2 + m : 3 + m, :]))

    def backward_middle(layer, m):
        rnd, plane, line = slim_round(3 - layer, m)
        stage_wait(plane, rnd)
        stage_start(line, rnd, add_slots(plane))

    def backward_end(layer, m):
        rnd, _, line = slim_round(3 - layer, m)
        stage_wait(line, rnd)
        value = add_slots(line)
        tot[layer, m : m + 1, :] = unpacked(value[0:4])
        tot[layer, 2 + m : 3 + m, :] = unpacked(value[4:8])

    def grad_rows(layer, m, slot):
        gain = vec_of(layer, 0)
        for lh in range(2):
            lanes = slice(lh * HALF, (lh + 1) * HALF)
            mean = coef[layer, 2 * m : 2 * m + 1, lanes]
            scale = coef[layer, 2 * m + 1 : 2 * m + 2, lanes]
            count = wide(counts[m : m + 1, :], 4)
            first = tot[layer, m : m + 1, lanes] / count
            second = tot[layer, 2 + m : 3 + m, lanes] / count * scale
            k = scale * gain[:, lanes]

            def body(i, acc):
                r = pl.ds(aligned(m * span + i * (2 * seqs), 16), 2 * seqs)
                y = hid[layer, r, lanes] - first - (rows[layer, r, lanes] - mean) * second
                y = wide(live[r, :], 4) * (k * y)
                g3[0, r, lanes] = y.astype(BF16)
                return acc + fold(y)

            acc = lax.fori_loop(0, pairs, body, jnp.zeros((8, HALF), F32))
            acc = jnp.sum(acc, axis=0, keepdims=True)
            if m == 0:
                levels[4:5, lanes] = acc
            else:
                top = lax.broadcasted_iota(jnp.int32, (16, HALF), 0) == 0
                minus = jnp.where(top, -(levels[4:5, lanes] + acc), 0.0)
                g3[0, total_rows:sent_rows, lanes] = minus.astype(BF16)
        here = pl.ds(0, span) if m == 0 else pl.ds(span, span + 16)
        made = across(g3.at[0, here, :], g3.at[1, here, :], slot + m)
        made.start()
        return made

    sums_round = {1: (1, 10), 0: (0, 11)}

    def sums_start(layer):
        parity, rnd = sums_round[layer]
        own_sum = -g3[0, total_rows:sent_rows, :].astype(F32)[0:1]
        far_sum = -g3[1, total_rows:sent_rows, :].astype(F32)[0:1]
        value = jnp.concatenate([own_sum, far_sum, tot[layer, 4:7, :], jnp.zeros((3, W), F32)], axis=0)
        stage_start(in_plane(wide_p, parity), rnd, value)

    def sums_middle(layer):
        parity, rnd = sums_round[layer]
        stage_wait(in_plane(wide_p, parity), rnd)
        stage_start(in_line(wide_z, parity), rnd, add_slots(in_plane(wide_p, parity)))

    def sums_end(layer):
        parity, rnd = sums_round[layer]
        stage_wait(in_line(wide_z, parity), rnd)
        vtot[layer] = add_slots(in_line(wide_z, parity))
        tot[layer, 4:7, :] = vtot[layer, 2:5, :]
        tot[layer, 7:8, :] = wide(counts[0:1, :] + counts[1:2, :], 8)
        env["summed"].add(layer)

        @pl.when(section == layer)
        def _():
            pltpu.make_async_copy(tot.at[layer], v.at[section], v_sems.at[0]).start()

        @pl.when(section != layer)
        def _():
            v_across(layer).start()

    def v_across(layer):
        return pltpu.make_async_remote_copy(
            src_ref=tot.at[layer], dst_ref=v.at[section], send_sem=v_sems.at[1], recv_sem=v_sems.at[2],
            device_id=sibling, device_id_type=MESH,
        )

    def transpose(src, begin=0, end=W // 128):
        def body(j, _):
            c = pl.ds(aligned(j * 128, 128), 128)
            src_t[c, 0:total_rows] = src[0:total_rows, c].T
            return 0

        lax.fori_loop(begin, end, body, 0)

    def transpose_level(src, layer):
        top = lax.broadcasted_iota(jnp.int32, (16, W), 0) == 0
        src[total_rows:sent_rows, :] = jnp.where(top, levels[2 + layer : 3 + layer, :], 0.0).astype(BF16)

        def body(j, _):
            c = pl.ds(aligned(j * 128, 128), 128)
            src_t[c, total_rows:] = src[total_rows:, c].T
            level = src[total_rows:sent_rows, c].astype(F32)[0:1]
            column[layer, c, :] = jnp.broadcast_to(level, (128, 128)).T.astype(BF16)
            return 0

        lax.fori_loop(0, W // 128, body, 0)

    def weight_part(block, grads, c):
        lanes = pl.ds(c * HALF, HALF)

        def body(j, _):
            r = pl.ds(aligned(j * HALF, HALF), HALF)
            block[r, lanes] = dot(src_t[r, :], grads[:, lanes], ((1,), (0,))).astype(BF16)
            return 0

        lax.fori_loop(0, W // HALF, body, 0)

    def source_grad(store, w_own, w_far, between):
        for m in range(2):
            r = pl.ds(m * span, span)

            def body(i, _):
                c = pl.ds(aligned(i * HALF, HALF), HALF)
                y = dot(g3[0, r, :], w_own[c, :], ((1,), (1,))) + dot(g3[1, r, :], w_far[c, :], ((1,), (1,)))
                store(r, c, y)
                return 0

            lax.fori_loop(0, 2, body, 0)
            between()

    env = dict(summed=set(), vtot=vtot, column=column, space=space, ar_send=ar_send, ar_recv=ar_recv,
               ar_other=ar_other, o=o, section=section, here={"batch": b})
    xs = [a for a in bits if a["link"] == "x"]
    ys = [a for a in bits if a["link"] == "y"]
    zs = [a for a in bits if a["link"] == "z"]
    orders = (xs + ys + zs, ys + xs + zs)
    blocks = {
        (1, 0): f_far.at[pl.ds(0, W), :],
        (1, 1): p_far.at[pl.ds(0, W), :],
        (0, 0): wc.at[1, 1],
        (0, 1): wr1,
    }
    parts = {}
    for layer in (1, 0):
        for index in range(4):
            part, side = index // 2, index % 2

            def lane_of(sec, part=part, side=side):
                return (sec if part == 0 else 1 - sec) * W + side * HALF

            block = blocks[layer, part].at[:, pl.ds(side * HALF, HALF)]
            parts[layer, index] = Reduction(env, layer, index, block, orders, lane_of)
    order = Order()

    def weight_grads(layer, between):
        for part in range(2):
            if part == 1:
                between()
            for c in range(2):
                weight_part(blocks[layer, part], g3.at[part], c)
                order.work(2.8)
                order.begin(parts[layer, 2 * part + c], 0)
                order.begin(parts[layer, 2 * part + c], 1)

    def arrived(layer, sends):
        for made in sends:
            made.wait()
        sums_start(layer)

    send_f = []
    for m in range(2):
        by_units(frames, f_own, m)
        fetch(grad_out, m).start()
        if m == 0:
            wait_heads(frames, 1)
        patch_heads(f_own, m)
        here = pl.ds(m * span, span)
        made = across(f_own.at[here, :], f_far.at[here, :], (0, 24)[m])
        made.start()
        send_f.append(made)
    start_across_w(1, w_plan(1), slot_of[1])
    stage_wait(cnt_plane, 0)
    stage_start(cnt_line, 0, add_slots(cnt_plane))
    wait_w(0, w_plan(0), slot_of[0], 0)
    matmul_to(rows.at[0], f_own, wc.at[0, 0], True, 0)
    matmul_to(rows.at[0], f_own, wc.at[0, 0], True, 1)
    wait_w(0, w_plan(0), slot_of[0], 1)
    send_f[0].wait()
    matmul_to(rows.at[0], f_far, wc.at[0, 1], False, 0)
    forward_stats(0, 0)
    send_f[1].wait()

    @pl.when(section == 1)
    def _():
        heads_copy(grad_out, 2).start()

    matmul_to(rows.at[0], f_far, wc.at[0, 1], False, 1)
    forward_middle(0, 0)
    forward_stats(0, 1)
    send_vec.wait_send()
    across(vecs.at[other], vecs.at[other], 3).wait_recv()
    stage_wait(cnt_line, 0)
    counts[...] = add_slots(cnt_line)
    forward_end(0, 0)
    sends = [forward_scan(0, 0, True)]
    forward_middle(0, 1)
    by_units(grad_out, g3.at[1], 0)
    wait_heads(grad_out, 2)
    patch_heads(g3.at[1], 0)
    forward_end(0, 1)
    sends.append(forward_scan(0, 1, True))
    wait_w(1, w_plan(1), slot_of[1], 0)
    matmul_to(rows.at[1], p_own, wc.at[1, 0], True, 0)
    wait_w(1, w_plan(1), slot_of[1], 1)
    sends[0].wait()
    matmul_to(rows.at[1], p_far, wc.at[1, 1], False, 0)
    forward_stats(1, 0)
    matmul_to(rows.at[1], p_own, wc.at[1, 0], True, 1)
    forward_middle(1, 0)
    sends[1].wait()
    matmul_to(rows.at[1], p_far, wc.at[1, 1], False, 1)
    forward_stats(1, 1)
    done_w(0, w_plan(0), slot_of[0])

    start_local_w(0, late_plan, slot_of[2])
    start_across_w(0, late_plan, slot_of[2])

    @pl.when(section == 1)
    def _():
        wc[0, 1, width - late_row :, :] = jnp.zeros((W - width + late_row, W), BF16)

    def source_level():
        def body(i, acc):
            r = pl.ds(aligned(i * (2 * seqs), 16), 2 * seqs)
            return acc + fold(wide(live[r, :], 8) * f_own[r, :].astype(F32))

        acc = lax.fori_loop(0, 2 * pairs, body, jnp.zeros((8, W), F32))
        levels[0:1, :] = jnp.sum(acc, axis=0, keepdims=True)

    forward_end(1, 0)
    forward_scan(1, 0, False)
    forward_middle(1, 1)
    by_units(grad_out, g3.at[1], 1)
    patch_heads(g3.at[1], 1)
    source_level()
    forward_end(1, 1)
    level_plane, level_line = in_plane(wide_p, 0), in_line(wide_z, 0)
    stage_start(level_plane, 9, jnp.concatenate([levels[0:2, :], jnp.zeros((6, W), F32)], axis=0))
    forward_scan(1, 1, False)
    backward_scan(1, 0, g3.at[1])
    backward_stats(1, 0)
    stage_wait(level_plane, 9)
    stage_start(level_line, 9, add_slots(level_plane))
    backward_scan(1, 1, g3.at[1])
    backward_stats(1, 1)
    backward_middle(1, 0)
    pl.semaphore_signal(credit.at[0], inc=1, device_id=sibling, device_id_type=MESH)
    transpose(p_own, 0, W // 256)
    backward_middle(1, 1)
    backward_end(1, 0)
    pl.semaphore_wait(credit.at[0], 1)
    sends = [grad_rows(1, 0, 20)]
    transpose(p_own, W // 256)
    stage_wait(level_line, 9)
    levels[2:4, :] = (add_slots(level_line) / wide(counts[0:1, :] + counts[1:2, :], 8))[0:2]
    transpose_level(p_own, 1)
    backward_end(1, 1)
    sends.append(grad_rows(1, 1, 20))
    weight_grads(1, lambda: arrived(1, sends))
    wait_w(1, w_plan(1), slot_of[1], 2)
    done_w(1, w_plan(1), slot_of[1])

    def keep_down(r, c, y):
        p_own[r, c] = y.astype(BF16)

    source_grad(keep_down, wc.at[1, 0], wr1, lambda: order.work(4.0))
    pl.semaphore_signal(credit.at[1], inc=1, device_id=sibling, device_id_type=MESH)
    sums_middle(1)
    backward_scan(0, 0, p_own, lambda: order.work(1.0))
    backward_stats(0, 0)
    backward_scan(0, 1, p_own, lambda: order.work(1.0))
    backward_stats(0, 1)
    backward_middle(0, 0)
    sums_end(1)
    transpose(f_own)
    transpose_level(f_own, 0)
    backward_middle(0, 1)
    order.work(8.0)
    backward_end(0, 0)
    pl.semaphore_wait(credit.at[1], 1)
    sends = [grad_rows(0, 0, 22)]
    backward_end(0, 1)
    sends.append(grad_rows(0, 1, 22))
    order.work(4.0)
    weight_grads(0, lambda: arrived(0, sends))
    wait_w(0, late_plan, slot_of[2], 0)
    wait_w(0, late_plan, slot_of[2], 1)
    done_w(0, late_plan, slot_of[2])

    def keep_source(r, c, y):
        rows[0, r, c] = y

    fetch(grad_out, 0).start()
    fetch(grad_out, 1).start()
    sums_middle(0)
    source_grad(keep_source, wc.at[0, 0], wc.at[0, 1], lambda: order.work(4.0))
    sums_end(0)

    def give(m):
        return pltpu.make_async_copy(staged.at[m], gf.at[m], stage_sem.at[m])

    for m in range(2):
        fetch(grad_out, m).wait()

        def finish_frames(i, _, m=m):
            straight = staged[m, pl.ds(2 * i, 2)].astype(F32).reshape(2 * seqs, half)
            y = rows[0, pl.ds(aligned(m * span + 2 * i * seqs, 8), 2 * seqs), :]
            y = jnp.where(section == 0, y[:, :half], y[:, late_shift : late_shift + half])
            staged[m, pl.ds(2 * i, 2)] = (y + straight).reshape(2, seqs, half).astype(BF16)
            return 0

        lax.fori_loop(0, pairs, finish_frames, 0)
        give(m).start()
        order.work(3.0)
    order.drain()
    for m in range(2):
        give(m).wait()

    for layer in range(2):

        @pl.when(section == layer)
        def _(layer=layer):
            pltpu.make_async_copy(tot.at[layer], v.at[section], v_sems.at[0]).wait()
            pltpu.make_async_remote_copy(
                src_ref=tot.at[layer], dst_ref=v.at[other], send_sem=v_sems.at[1], recv_sem=v_sems.at[2],
                device_id=sibling, device_id_type=MESH,
            ).wait_recv()

        @pl.when(section != layer)
        def _(layer=layer):
            v_across(layer).wait_send()

    own_part, far_part = v[section], v[other]
    first = jnp.where(section == 0, own_part, far_part)
    second = jnp.where(section == 0, far_part, own_part)
    for row, terms in ((0, (2, 3)), (1, (0, 1)), (2, (4,))):
        for lane, x in ((0, first), (W, second)):
            total = x[terms[0] : terms[0] + 1, :]
            for k in terms[1:]:
                total = total + x[k : k + 1, :]
            vectors[row : row + 1, lane : lane + W] = total
    squares = jnp.sum(first[5:7, :] + second[5:7, :], axis=1, keepdims=True)
    root = jnp.sqrt(squares / (first[7:8, 0:1] * width))
    for k in range(2):
        vectors[3 + k : 4 + k, :] = jnp.broadcast_to(root[k : k + 1], (1, 2 * W))
    vectors[5:8, :] = jnp.zeros((3, 2 * W), F32)


def write_results(o, gf, vectors, grad_weight, grad_frames, grad_gains, grad_shifts, grad_recurs, table):
    width = grad_weight.shape[2]
    grad_weight[0] = o[...][:, :width].astype(F32)
    grad_frames[...] = gf[...]

    @pl.when(pl.program_id(0) == 0)
    def _():
        for k, out in enumerate((grad_gains, grad_shifts, grad_recurs)):
            out[...] = vectors[k : k + 1, 0:width]
        table[...] = jnp.concatenate([vectors[3:4, 0:1], vectors[4:5, 0:1]], axis=1)


def results(o, gf, vectors):
    micro, steps, seqs, half = gf.shape
    width = 2 * half
    count = W * 2 // 256
    frames = micro * steps // count
    whole = lambda shape: pl.BlockSpec(shape, lambda i: (0, 0))
    out = pl.pallas_call(
        write_results,
        grid=(count,),
        in_specs=[
            pl.BlockSpec((256, 2 * W), lambda i: (i, 0)),
            pl.BlockSpec((frames, seqs, half), lambda i: (i, 0, 0)),
            whole((8, 2 * W)),
        ],
        out_specs=(
            pl.BlockSpec((1, 256, width), lambda i: (0, i, 0)),
            pl.BlockSpec((frames, seqs, half), lambda i: (i, 0, 0)),
            whole((1, width)),
            whole((1, width)),
            whole((1, width)),
            whole((1, 2)),
        ),
        out_shape=(
            jax.ShapeDtypeStruct((1, width, width), F32),
            jax.ShapeDtypeStruct((micro * steps, seqs, half), BF16),
            jax.ShapeDtypeStruct((1, width), F32),
            jax.ShapeDtypeStruct((1, width), F32),
            jax.ShapeDtypeStruct((1, width), F32),
            jax.ShapeDtypeStruct((1, 2), F32),
        ),
        compiler_params=pltpu.CompilerParams(vmem_limit_bytes=64 * 1024 * 1024),
    )(o.reshape(2 * W, 2 * W), gf.reshape(micro * steps, seqs, half), vectors)
    return out[1].reshape(gf.shape), out[0], *out[2:]


def whole_step(dims, frames, grad_out, weights, gains, shifts, recurs, lengths, masks):
    nz, ny, nx = dims
    micro, steps, seqs, half = frames.shape
    width = 2 * half
    views = seqs // lengths.shape[1]
    rows = micro * steps * seqs
    np_ = ny * nx
    wide_rows = (rows + 16 + 127) // 128 * 128
    depth = (nx * ny * nz - 1).bit_length()
    any_ = pl.BlockSpec(memory_space=pl.ANY)
    held = pl.BlockSpec(memory_space=pltpu.VMEM)
    dma = pltpu.SemaphoreType.DMA
    return pl.pallas_call(
        functools.partial(kernel, dims, steps, seqs, views),
        out_shape=(
            jax.ShapeDtypeStruct((2, W, 2 * W), BF16),
            jax.ShapeDtypeStruct(frames.shape, BF16),
            jax.ShapeDtypeStruct((8, 2 * W), F32),
        ),
        in_specs=[any_] * 3 + [held] * 5,
        out_specs=(any_, any_, held),
        scratch_shapes=[
            pltpu.VMEM((wide_rows, W), BF16),
            pltpu.VMEM((rows, W), BF16),
            pltpu.VMEM((wide_rows, W), BF16),
            pltpu.VMEM((rows, W), BF16),
            pltpu.VMEM((2, wide_rows, W), BF16),
            pltpu.VMEM((2, 2, W, W), BF16),
            pltpu.VMEM((W, W), BF16),
            pltpu.VMEM((W, wide_rows), BF16),
            pltpu.VMEM((rows, 128), F32),
            pltpu.VMEM((128, 128), F32),
            pltpu.VMEM(frames.shape, BF16),
            pltpu.VMEM((micro, steps, seqs, 128), BF16),
            pltpu.VMEM((5, W, (width - W) % 128), BF16),
            pltpu.VMEM((2, 8, W), F32),
            pltpu.VMEM((2, 8, 2 * W), F32),
            pltpu.VMEM((2, rows, W), F32),
            pltpu.VMEM((2, rows, W), F32),
            pltpu.VMEM((2, 8, W), F32),
            pltpu.VMEM((2, 8, W), F32),
            pltpu.VMEM((2, 8, W), F32),
            pltpu.VMEM((8, W), F32),
            pltpu.VMEM((2, W, 128), BF16),
            pltpu.VMEM((8, 128), F32),
            pltpu.VMEM((1, np_, 8, 128), F32),
            pltpu.VMEM((1, nz, 8, 128), F32),
            pltpu.VMEM((4, np_, 8, QUART), F32),
            pltpu.VMEM((4, nz, 8, QUART), F32),
            pltpu.VMEM((2, np_, 8, W), F32),
            pltpu.VMEM((2, nz, 8, W), F32),
            pltpu.VMEM((2, 4, W, HALF), BF16),
            dma((3, 25)),
            dma((3,)),
            dma((2,)),
            pltpu.SemaphoreType.REGULAR((2,)),
            dma((12, max(np_, 2))),
            dma((12, max(np_, 2))),
            dma((12, max(nz, 2))),
            dma((12, max(nz, 2))),
            dma((2, 4, 2, 2 * depth + 2)),
            dma((2, 4, 2, 2 * depth + 2)),
            dma((2, 4, 2, 2)),
        ],
        compiler_params=pltpu.CompilerParams(
            collective_id=0, has_side_effects=True, vmem_limit_bytes=64 * 1024 * 1024
        ),
    )(frames, grad_out, weights, gains, shifts, recurs, lengths, masks)


def shards(dims, frames, grad_out, weights, gains, shifts, recurs, lengths, masks):
    return results(*whole_step(dims, frames, grad_out, weights, gains, shifts, recurs, lengths, masks))


def solution(mesh):
    in_specs = (
        P(None, None, "batch", "section"),
        P(None, None, "batch", "section"),
        P("section", None, None),
        P("section", None),
        P("section", None),
        P("section", None),
        P(None, "batch"),
        P(None, None, "batch"),
    )
    out_specs = (
        P(None, None, "batch", "section"),
        P("section", None, None),
        P("section", None),
        P("section", None),
        P("section", None),
        P("section", None),
    )
    body = functools.partial(shards, grid_of(mesh.shape["batch"]))
    return jax.shard_map(body, mesh=mesh, in_specs=in_specs, out_specs=out_specs, check_vma=False)
```

```python
import functools

import jax
import jax.numpy as jnp
from jax import lax
from jax.experimental import pallas as pl
from jax.experimental.pallas import tpu as pltpu
from jax.sharding import PartitionSpec as P

EPS = 1e-05
W = 1024
HALF = W // 2
QUART = W // 4
PAIRS = 1
PART = W // PAIRS // 2
MESH = pl.DeviceIdType.MESH
F32 = jnp.float32
BF16 = jnp.bfloat16


def grid_of(size):
    if size == 16:
        return (4, 2, 2)
    if size == 128:
        return (8, 4, 4)
    return (size, 1, 1)


def aligned(x, k):
    return pl.multiple_of(x, k)


def wide(x, reps):
    return jnp.concatenate([x] * reps, axis=1)


def fold(x):
    rows = x.shape[0]
    total = x[0:8]
    for k in range(8, rows, 8):
        total = total + x[k : k + 8]
    return total


def repeat(count, body, init, times):
    while count % times:
        times -= 1

    def several(i, carry):
        for j in range(times):
            carry = body(i * times + j, carry)
        return carry

    return lax.fori_loop(0, count // times, several, init)


def dot(a, b, dims):
    return lax.dot_general(a, b, (dims, ((), ())), preferred_element_type=F32)


class Reduction:
    def __init__(self, env, layer, index, block, orders, lane_of):
        self.env, self.layer, self.index, self.block, self.orders = env, layer, index, block, orders
        self.lane_of = lane_of
        self.space = env["space"].at[layer, index]
        self.depth = len(orders[0])
        self.regions = [self.halves(i, order) for i, order in enumerate(orders)]
        self.step = 0
        self.waits = []
        depth = self.depth
        self.steps = [functools.partial(self.scatter, 0)]
        self.steps += [functools.partial(self.scatter, k) for k in range(1, depth)]
        self.steps += [functools.partial(self.gather, k) for k in range(depth - 1, 0, -1)]
        self.steps += [self.give, self.finish]

    def halves(self, i, order):
        row, rows, lane, lanes = 0, W, i * PART, PART
        out = [(row, rows, lane, lanes)]
        for axis in order:
            if rows > 16:
                rows //= 2
                row = row + axis["bit"] * rows
            else:
                lanes //= 2
                lane = lane + axis["bit"] * lanes
            out.append((row, rows, lane, lanes))
        return out

    @property
    def free_to_go(self):
        return self.step != self.depth or self.layer in self.env["summed"]

    @property
    def done(self):
        return self.step >= len(self.steps)

    def advance(self):
        self.sent = []
        self.steps[self.step]()
        self.step += 1
        return self.sent

    def remote(self, i, src, dst, slot, where, recv=None):
        sems = (self.layer, self.index, i, slot)
        return pltpu.make_async_remote_copy(
            src_ref=src, dst_ref=dst, send_sem=self.env["ar_send"].at[sems],
            recv_sem=self.env["ar_recv"].at[sems] if recv is None else recv, device_id=where, device_id_type=MESH,
        )

    def wait(self):
        for made, came in self.waits:
            made.wait_send()
            came.wait_recv()
        self.waits = []

    def came_at(self, i, k):
        row = sum(r[1] for r in self.regions[i][1 : k + 1])
        _, rows, _, lanes = self.regions[i][k + 1]
        return row, rows, i * PART, lanes

    def scatter(self, k):
        if k > 0:
            self.wait()
            self.add(k - 1)
        for i, order in enumerate(self.orders):
            self.scatter_part(i, k, order[k])

    def start_part(self, i):
        self.sent = []
        self.scatter_part(i, 0, self.orders[i][0])
        if i == 1:
            self.step = 1
        return self.sent

    def scatter_part(self, i, k, axis):
        row, rows, lane, lanes = self.regions[i][k]
        _, rows2, _, lanes2 = self.regions[i][k + 1]
        give_row = row + (1 - axis["bit"]) * rows2 if rows2 < rows else row
        give_lane = lane if rows2 < rows else lane + (1 - axis["bit"]) * lanes2
        src = self.block.at[pl.ds(aligned(give_row, 16), rows2), pl.ds(aligned(give_lane, 128), lanes2)]
        at, n, at_lane, n_lanes = self.came_at(i, k)
        dst = self.space.at[pl.ds(at, n), pl.ds(at_lane, n_lanes)]
        made = self.remote(i, src, dst, k, axis["partner"])
        made.start()
        self.waits.append((made, made))
        self.sent.append((axis["link"], rows2 * lanes2 * 2))

    def add(self, k, last=False):
        rows = self.regions[0][k + 1][1]
        size = min(rows, 64)
        out = []
        for i in range(2):
            row, _, lane, lanes = self.regions[i][k + 1]
            at, _, at_lane, _ = self.came_at(i, k)
            lane = aligned(lane, 128)
            extra = None
            if last:
                part = self.index // PAIRS
                first = aligned((self.index % PAIRS) * 2 * PART + lane, 128)
                extra = self.env["vtot"][self.layer, part : part + 1, pl.ds(first, lanes)]
            out.append((row, lane, lanes, at, at_lane, self.local(i, k + 1)[0], extra))

        def body(j, _):
            for row, lane, lanes, at, at_lane, home, extra in out:
                here = pl.ds(aligned(row + j * size, 16), size)
                total = self.block[here, pl.ds(lane, lanes)].astype(F32)
                total = total + self.space[pl.ds(aligned(at + j * size, 16), size), pl.ds(at_lane, lanes)].astype(F32)
                if last:
                    column = self.env["column"][self.layer, here, :].astype(F32)
                    total = total + wide(column, lanes // 128) * extra
                    to = pl.ds(aligned(home + j * size, 16), size)
                    self.space[to, pl.ds(lane, lanes)] = total.astype(BF16)
                else:
                    self.block[here, pl.ds(lane, lanes)] = total.astype(BF16)
            return 0

        lax.fori_loop(0, rows // size, body, 0)

    def local(self, i, k):
        row, rows, lane, lanes = self.regions[i][k]
        return row - self.regions[i][1][0], rows, lane, lanes

    def gather(self, k):
        self.wait()
        if k == self.depth - 1:
            self.add(k, last=True)
        for i, order in enumerate(self.orders):
            axis = order[k]
            row, rows, lane, lanes = self.local(i, k + 1)
            row0, rows0, lane0, lanes0 = self.local(i, k)
            if rows0 > rows:
                far = (row0 + (1 - axis["bit"]) * rows, rows, lane, lanes)
            else:
                far = (row, rows, lane0 + (1 - axis["bit"]) * lanes, lanes)
            refs = [
                self.space.at[pl.ds(aligned(r, 16), n), pl.ds(aligned(c, 128), w)]
                for r, n, c, w in ((row, rows, lane, lanes), far)
            ]
            made = self.remote(i, refs[0], refs[0], self.depth + k, axis["partner"])
            made.start()
            self.waits.append((made, self.remote(i, refs[1], refs[1], self.depth + k, axis["partner"])))
            self.sent.append((axis["link"], rows * lanes * 2))

    def result(self, i, bit, section):
        rows = self.regions[i][1][1]
        lane = aligned(self.lane_of(section) + i * PART, PART)
        return self.env["o"].at[section, pl.ds(aligned(bit * rows, 16), rows), pl.ds(lane, PART)]

    def gathered(self, i):
        return self.space.at[pl.ds(0, self.regions[i][1][1]), pl.ds(i * PART, PART)]

    def deliver(self, i, near, straight):
        axis, section = self.orders[i][0], self.env["section"]
        slot = 2 * self.depth + (0 if near else 1)
        recv = None if straight else self.env["ar_other"].at[self.layer, self.index, i, 0 if near else 1]
        where = dict(self.env["here"] if near else axis["partner"], section=self.layer)
        return self.remote(i, self.gathered(i), self.result(i, axis["bit"], section), slot, where, recv)

    def arrival(self, i, near, straight):
        axis, section = self.orders[i][0], self.env["section"]
        slot = 2 * self.depth + (0 if near else 1)
        recv = None if straight else self.env["ar_other"].at[self.layer, self.index, i, 0 if near else 1]
        bit = axis["bit"] if near else 1 - axis["bit"]
        frm = section if straight else 1 - section
        where = dict(self.env["here"] if near else axis["partner"], section=frm)
        return self.remote(i, self.gathered(i), self.result(i, bit, frm), slot, where, recv)

    def kept(self, i):
        sem = self.env["ar_recv"].at[self.layer, self.index, i, 2 * self.depth]
        return pltpu.make_async_copy(
            self.gathered(i), self.result(i, self.orders[i][0]["bit"], self.env["section"]), sem
        )

    def give(self):
        self.wait()

        @pl.when(self.env["section"] == self.layer)
        def _():
            for i in range(2):
                self.deliver(i, False, True).start()
                self.kept(i).start()

        @pl.when(self.env["section"] != self.layer)
        def _():
            for i in range(2):
                self.deliver(i, False, False).start()
                self.deliver(i, True, False).start()

        for i, order in enumerate(self.orders):
            self.sent.append((order[0]["link"], self.regions[i][1][1] * PART * 2))

    def finish(self):
        @pl.when(self.env["section"] == self.layer)
        def _():
            for i in range(2):
                self.kept(i).wait()
                self.deliver(i, False, True).wait_send()
                self.arrival(i, False, True).wait_recv()
                self.arrival(i, True, False).wait_recv()
                self.arrival(i, False, False).wait_recv()

        @pl.when(self.env["section"] != self.layer)
        def _():
            for i in range(2):
                self.deliver(i, False, False).wait_send()
                self.deliver(i, True, False).wait_send()


class Order:
    RATE, HOP = 70e3, 1.8

    def __init__(self):
        self.now = 0.0
        self.free = {}
        self.going = []

    def sent(self, copies):
        end = self.now
        for link, size in copies:
            self.free[link] = max(self.now, self.free.get(link, 0.0)) + size / self.RATE
            end = max(end, self.free[link])
        return end + self.HOP

    def begin(self, one, i):
        end = self.sent(one.start_part(i))
        if i == 0:
            one.due = end
        else:
            one.due = max(one.due, end)
            self.going.append(one)

    def advance(self, one):
        self.now = max(self.now, one.due) + 0.4
        one.due = self.sent(one.advance())
        if one.done:
            self.going.remove(one)

    def work(self, cost):
        self.now += cost
        while True:
            due = [x for x in self.going if x.due <= self.now and x.free_to_go]
            if not due:
                return
            self.advance(min(due, key=lambda x: x.due))

    def drain(self):
        while self.going:
            self.advance(min(self.going, key=lambda x: x.due))


def kernel(dims, steps, seqs, views, frames, grad_out, weights, gains, shifts, recurs, lengths, masks, o, gf, vectors, f_own, f_far, p_own, p_far, g3, wc, wr1, src_t, live, turn,
           staged, heads, tails, v, vecs, rows, hid, coef, tot, vtot, levels, column, counts, cnt_p, cnt_z, slim_p, slim_z,
           wide_p, wide_z, space, sems, v_sems, stage_sem, credit, pl_send, pl_recv, z_send, z_recv, ar_send, ar_recv,
           ar_other):
    nz, ny, nx = dims
    np_ = ny * nx
    span = steps * seqs
    total_rows = 2 * span
    sent_rows = total_rows + 16
    pairs = steps // 2
    section = lax.axis_index("section")
    other = 1 - section
    b = lax.axis_index("batch")
    mp = lax.rem(b, np_)
    mz = b // np_

    def at_plane(i):
        return {"batch": b - mp + i}

    def at_z(i):
        return {"batch": b + (i - mz) * np_}

    bits = []
    for link, count, stride in (("x", nx, 1), ("y", ny, nx), ("z", nz, np_)):
        while count > 1:
            bit = lax.rem(b // stride, 2)
            bits.append(dict(bit=bit, partner={"batch": b + (1 - 2 * bit) * stride}, link=link))
            count //= 2
            stride *= 2
    sibling = {"section": other}

    def local(src, dst, slot):
        return pltpu.make_async_copy(src, dst, sems.at[0, slot])

    def across(src, dst, slot):
        return pltpu.make_async_remote_copy(
            src_ref=src, dst_ref=dst, send_sem=sems.at[1, slot], recv_sem=sems.at[2, slot],
            device_id=sibling, device_id_type=MESH,
        )

    half = frames.shape[3]
    width = 2 * half
    lead = W - half
    rest = width - W
    full = rest // 128 * 128

    def fetch(source, m):
        return pltpu.make_async_copy(source.at[m], staged.at[m], stage_sem.at[m])

    def by_units(source, target, m):
        fetch(source, m).wait()

        @pl.when(section == 0)
        def _():
            pad = jnp.zeros((2 * seqs, lead), F32)

            def place(i, _):
                x = staged[m, pl.ds(2 * i, 2)].astype(F32).reshape(2 * seqs, half)
                to = pl.ds(aligned(m * span + 2 * i * seqs, 16), 2 * seqs)
                target[to, :] = jnp.concatenate([x, pad], axis=1).astype(BF16)
                return 0

            repeat(pairs, place, 0, 3)

        @pl.when(section == 1)
        def _():
            pad = jnp.zeros((2 * seqs, 2 * lead), F32)

            def place(i, _):
                x = staged[m, pl.ds(2 * i, 2)].astype(F32).reshape(2 * seqs, half)
                to = pl.ds(aligned(m * span + 2 * i * seqs, 16), 2 * seqs)
                target[to, :] = jnp.concatenate([x[:, lead:], pad], axis=1).astype(BF16)
                return 0

            repeat(pairs, place, 0, 3)

    def patch_heads(target, m):
        @pl.when(section == 0)
        def _():
            lane = lax.broadcasted_iota(jnp.int32, (2 * seqs, 128), 1)

            def place(i, _):
                to = pl.ds(aligned(m * span + 2 * i * seqs, 16), 2 * seqs)
                head = heads[m, pl.ds(2 * i, 2)].astype(F32).reshape(2 * seqs, 128)
                head = pltpu.roll(head, 128 - lead, 1)
                old = target[to, W - 128 :].astype(F32)
                target[to, W - 128 :] = jnp.where(lane < 128 - lead, old, head).astype(BF16)
                return 0

            repeat(pairs, place, 0, 3)

    def pieces(row, count, u, block, spot):
        r = pl.ds(row, count)
        to = pl.ds(0, count)
        if u == 0:
            return [(weights.at[0, r, pl.ds(0, W)], block.at[to, :])]
        return [
            (weights.at[0, r, pl.ds(W, full)], block.at[to, pl.ds(0, full)]),
            (weights.at[0, r, pl.ds(W + full, rest - full)], tails.at[spot, to, :]),
        ]

    rows_of = {0: (0, W), 1: (W, rest)}

    def w_plan(layer):
        mine, far = rows_of[layer], rows_of[1 - layer]
        plan = [
            (mine, layer, far, 1 - layer, wc.at[layer, 0], 2 * layer),
            (far, layer, mine, 1 - layer, wc.at[layer, 1], 2 * layer + 1),
        ]
        if layer == 1:
            plan.append((mine, 0, far, 1, wr1, 4))
        return plan

    late_row = (width - half) // 16 * 16
    late_shift = half - late_row
    late_plan = [
        ((0, W), 0, (late_row, width - late_row), 1, wc.at[0, 0], 0),
        ((0, W), 1, (late_row, width - late_row), 0, wc.at[0, 1], 1),
    ]
    slot_of = {0: 4, 1: 8, 2: 14}

    def local_w(plan, base, which):
        r, u, _, _, block, spot = plan[which]
        return [local(a, t, base + 2 * which + i) for i, (a, t) in enumerate(pieces(*r, u, block, spot))]

    def across_w(plan, base, which):
        _, _, r, u, block, spot = plan[which]
        return [across(a, t, base + 2 * which + i) for i, (a, t) in enumerate(pieces(*r, u, block, spot))]

    def start_local_w(layer, plan, base):
        @pl.when(section == layer)
        def _():
            for which in range(len(plan)):
                for made in local_w(plan, base, which):
                    made.start()

    def start_across_w(layer, plan, base):
        @pl.when(section == layer)
        def _():
            for which in range(len(plan)):
                for made in across_w(plan, base, which):
                    made.start()

    def last_units(block, spot):
        def body(i, _):
            r = pl.ds(aligned(i * 128, 128), 128)
            x = tails[spot, r, :].astype(F32)
            x = jnp.concatenate([x, jnp.zeros((128, 128 - x.shape[1]), F32)], axis=1)
            block[r, full:] = x.astype(BF16)
            return 0

        lax.fori_loop(0, W // 128, body, 0)

    def wait_w(layer, plan, base, which):
        _, own_u, _, far_u, block, spot = plan[which]

        @pl.when(section == layer)
        def _():
            for made in local_w(plan, base, which):
                made.wait()
            if own_u == 1:
                last_units(block, spot)

        @pl.when(section != layer)
        def _():
            for made in across_w(plan, base, which):
                made.wait_recv()
            if far_u == 1:
                last_units(block, spot)

    def done_w(layer, plan, base):
        @pl.when(section == layer)
        def _():
            for which in range(len(plan)):
                for made in across_w(plan, base, which):
                    made.wait_send()

    def heads_copy(source, slot):
        return across(source.at[:, :, :, pl.ds(0, 128)], heads, slot)

    def wait_heads(source, slot):
        @pl.when(section == 0)
        def _():
            heads_copy(source, slot).wait_recv()

        @pl.when(section == 1)
        def _():
            heads_copy(source, slot).wait_send()

    fetch(frames, 0).start()
    fetch(frames, 1).start()
    for layer in range(2):
        start_local_w(layer, w_plan(layer), slot_of[layer])

    barrier = pltpu.get_barrier_semaphore()
    greeted = [dict(sibling)]
    greeted += [at_plane(lax.rem(mp + k, np_)) for k in range(1, np_)]
    greeted += [at_z(lax.rem(mz + k, nz)) for k in range(1, nz)]
    greeted += [dict(axis["partner"], section=other) for axis in bits]
    for where in greeted:
        pl.semaphore_signal(barrier, inc=1, device_id=where, device_id_type=MESH)

    for k, (x, fill) in enumerate(((gains, 0.0), (shifts, -1e30), (recurs, 0.0))):
        vecs[section, k : k + 1, 0:width] = x[...]
        vecs[section, k : k + 1, width:] = jnp.full((1, 2 * W - width), fill, F32)
    vecs[section, 3:8, :] = jnp.zeros((5, 2 * W), F32)

    gap = jnp.zeros((W - rest, W), BF16)

    @pl.when(section == 0)
    def _():
        wc[0, 1, rest:, :] = gap
        wc[1, 1, rest:, :] = gap

    @pl.when(section == 1)
    def _():
        wc[0, 0, rest:, :] = gap
        wc[1, 0, rest:, :] = gap
        wr1[rest:, :] = gap

    for spot in (0, 2):
        tails[spot, rest:, :] = jnp.zeros((W - rest, rest - full), BF16)
    for spare in (f_own, p_own, g3.at[0], g3.at[1]):
        spare[sent_rows:, :] = jnp.zeros((spare.shape[0] - sent_rows, W), BF16)

    pl.semaphore_wait(barrier, len(greeted))

    @pl.when(section == 1)
    def _():
        heads_copy(frames, 1).start()

    start_across_w(0, w_plan(0), slot_of[0])
    send_vec = across(vecs.at[section], vecs.at[section], 3)
    send_vec.start()

    def stage_copy(where, rnd, slot, k, back):
        buf, parity, size, me, at, send, recv = where
        there = at(lax.rem(me + (size - k if back else k), size))
        ref = buf.at[parity, slot]
        return pltpu.make_async_remote_copy(
            src_ref=ref, dst_ref=ref, send_sem=send.at[rnd, k], recv_sem=recv.at[rnd, k],
            device_id=there, device_id_type=MESH,
        )

    def in_plane(buf, parity):
        return (buf, parity, np_, mp, at_plane, pl_send, pl_recv)

    def in_line(buf, parity):
        return (buf, parity, nz, mz, at_z, z_send, z_recv)

    def stage_start(where, rnd, value):
        buf, parity, size, me = where[:4]
        buf[parity, me] = value
        for k in range(1, size):
            stage_copy(where, rnd, me, k, False).start()

    def stage_wait(where, rnd):
        size, me = where[2:4]
        for k in range(1, size):
            stage_copy(where, rnd, me, k, False).wait_send()
            stage_copy(where, rnd, lax.rem(me + size - k, size), k, True).wait_recv()

    def add_slots(where):
        buf, parity, size = where[:3]
        total = buf[parity, 0]
        for k in range(1, size):
            total = total + buf[parity, k]
        return total

    groups = lengths.shape[1]
    s_at = lax.broadcasted_iota(jnp.int32, (seqs, groups), 0)
    g_at = lax.broadcasted_iota(jnp.int32, (seqs, groups), 1) * views
    there = (s_at >= g_at) & (s_at < g_at + views)
    position = lax.broadcasted_iota(jnp.int32, (seqs, 128), 1)
    local_counts = []
    for m in range(2):
        turn[...] = jnp.zeros_like(turn)
        turn[0:steps, 0:seqs] = masks[m].astype(F32)
        mask = turn[...].T[0:seqs]
        length = jnp.broadcast_to(lengths[m : m + 1, :], (seqs, groups)).astype(F32)
        limit = jnp.sum(jnp.where(there, length, 0.0), axis=1, keepdims=True)
        alive = (position.astype(F32) < limit) & ((mask > 0.0) | (position == 0))
        alive = jnp.where(position < steps, alive.astype(F32), 0.0)
        total = jnp.zeros((seqs, 128), F32)
        for t in range(steps):
            at = m * span + t * seqs
            cells = jnp.broadcast_to(alive[:, t : t + 1], (seqs, 128))
            live[at : at + seqs, :] = cells
            total = total + cells
        local_counts.append(jnp.sum(total, axis=0, keepdims=True))
    n_own = jnp.concatenate(local_counts * 4, axis=0)

    cnt_plane, cnt_line = in_plane(cnt_p, 0), in_line(cnt_z, 0)
    stage_start(cnt_plane, 0, n_own)

    def vec_of(layer, k):
        return vecs[layer, k : k + 1, pl.ds(aligned(section * W, W), W)]

    def matmul_to(out, a, w, first, m):
        r = pl.ds(m * span, span)

        def body(i, _):
            c = pl.ds(aligned(i * HALF, HALF), HALF)
            y = dot(a[r, :], w[:, c], ((1,), (0,)))
            out[r, c] = y if first else out[r, c] + y
            return 0

        lax.fori_loop(0, 2, body, 0)

    def packed(x, y):
        return jnp.concatenate([z[:, k * QUART : (k + 1) * QUART] for z in (x, y) for k in range(4)], axis=0)

    def unpacked(x):
        return jnp.concatenate([x[k : k + 1] for k in range(4)], axis=1)

    def merge_slots(where, counts_of):
        buf, parity, size = where[:3]
        s = [buf[parity, k, 0:4, :] for k in range(size)]
        q = [buf[parity, k, 4:8, :] for k in range(size)]
        n = [wide(counts_of(k), 2) for k in range(size)]
        total, squares, count = sum(s[1:], s[0]), sum(q[1:], q[0]), sum(n[1:], n[0])
        mean = total / count
        for k in range(size):
            d = s[k] / n[k] - mean
            squares = squares + n[k] * d * d
        return jnp.concatenate([total, squares], axis=0)

    def slim_round(which, m):
        return 1 + 2 * which + m, in_plane(slim_p, 2 * m + which % 2), in_line(slim_z, 2 * m + which % 2)

    def forward_stats(layer, m):
        start = jnp.sum(rows[layer, m * span : m * span + seqs, :], axis=0, keepdims=True) * (1.0 / seqs)

        def body(i, carry):
            s, q = carry
            r = pl.ds(aligned(m * span + i * (2 * seqs), 16), 2 * seqs)
            d = rows[layer, r, :] - start
            kept = wide(live[r, :], 8) * d
            return s + fold(kept), q + fold(kept * d)

        zero = jnp.zeros((8, W), F32)
        s, q = repeat(pairs, body, (zero, zero), 3)
        s, q = jnp.sum(s, axis=0, keepdims=True), jnp.sum(q, axis=0, keepdims=True)
        n = wide(local_counts[m], 8)
        rnd, plane, _ = slim_round(layer, m)
        stage_start(plane, rnd, packed(s + n * start, jnp.maximum(q - s * s / n, 0.0)))

    def forward_middle(layer, m):
        rnd, plane, line = slim_round(layer, m)
        stage_wait(plane, rnd)
        stage_start(line, rnd, merge_slots(plane, lambda k: cnt_p[0, k, m : m + 1, :]))

    def forward_end(layer, m):
        rnd, _, line = slim_round(layer, m)
        stage_wait(line, rnd)
        value = merge_slots(line, lambda k: cnt_z[0, k, m : m + 1, :])
        count = wide(counts[m : m + 1, :], 8)
        mean = unpacked(value[0:4]) / count
        scale = lax.rsqrt(unpacked(value[4:8]) / count + EPS)
        coef[layer, 2 * m : 2 * m + 1, :] = mean
        coef[layer, 2 * m + 1 : 2 * m + 2, :] = scale
        slope = vec_of(layer, 0) * scale
        coef[layer, 4 + 2 * m : 5 + 2 * m, :] = slope
        coef[layer, 5 + 2 * m : 6 + 2 * m, :] = vec_of(layer, 1) - mean * slope

    def forward_scan(layer, m, passes):
        rec = vec_of(layer, 2)
        slope = coef[layer, 4 + 2 * m : 5 + 2 * m, :]
        shift = coef[layer, 5 + 2 * m : 6 + 2 * m, :]

        def body(i, carry):
            h, level = carry
            r = pl.ds(aligned(m * span + i * (2 * seqs), 16), 2 * seqs)
            x = rows[layer, r, :] * slope + shift
            lv = wide(live[r, :], 8)
            alive = lv > 0.0
            both = []
            for k in range(2):
                part = slice(k * seqs, (k + 1) * seqs)
                z = x[part] + rec * h
                soft = jnp.maximum(z, 0.0) + jnp.log(1.0 + jnp.exp(-jnp.abs(z)))
                h = jnp.where(alive[part], soft, h)
                both.append(h)
            two = jnp.concatenate(both, axis=0)
            hid[layer, r, :] = two
            if passes:
                p_own[r, :] = two.astype(BF16)
                level = level + fold(lv * two)
            return h, level

        _, level = lax.fori_loop(0, pairs, body, (jnp.zeros((seqs, W), F32), jnp.zeros((8, W), F32)))
        if not passes:
            return None
        level = jnp.sum(level, axis=0, keepdims=True)
        levels[1:2, :] = level if m == 0 else levels[1:2, :] + level
        here = pl.ds(m * span, span)
        made = across(p_own.at[here, :], p_far.at[here, :], 18 + m)
        made.start()
        return made

    def backward_scan(layer, m, above, between=lambda: None):
        gain, shift, recur = vec_of(layer, 0), vec_of(layer, 1), vec_of(layer, 2)
        for lq in range(4):
            lanes = slice(lq * QUART, (lq + 1) * QUART)
            gq, sq, rec = gain[:, lanes], shift[:, lanes], recur[:, lanes]
            mean = coef[layer, 2 * m : 2 * m + 1, lanes]
            scale = coef[layer, 2 * m + 1 : 2 * m + 2, lanes]

            def body(i, carry):
                down, s1, s2, rsum, sqh, sqa = carry
                i = pairs - 1 - i
                start = m * span + i * (2 * seqs)
                r = pl.ds(aligned(start, 16), 2 * seqs)
                before = pl.ds(aligned(jnp.maximum(start - seqs, 0), 8), seqs)
                normed = (rows[layer, r, lanes] - mean) * scale
                drive = gq * normed + sq
                h2 = hid[layer, r, lanes]
                hb = jnp.where(i > 0, hid[layer, before, lanes], 0.0)
                lv = wide(live[r, :], 2)
                up = above[r, lanes].astype(F32)
                res = f_own[r, lanes].astype(F32)
                aux = res + h2 if layer == 1 else res
                sqh = sqh + fold(lv * (h2 * h2))
                sqa = sqa + fold(lv * (aux * aux))
                grads = [None, None]
                for k in (1, 0):
                    part = slice(k * seqs, (k + 1) * seqs)
                    prior = h2[0:seqs] if k == 1 else hb
                    slope = 0.5 + 0.5 * jnp.tanh(0.5 * (drive[part] + rec * prior))
                    total = up[part] + down
                    gd = lv[part] * slope * total
                    down = (1.0 - lv[part]) * total + rec * gd
                    grads[k] = gd
                    rsum = rsum + fold(gd * prior)
                gd2 = jnp.concatenate(grads, axis=0)
                hid[layer, r, lanes] = gd2
                return down, s1 + fold(gd2), s2 + fold(gd2 * normed), rsum, sqh, sqa

            z8 = jnp.zeros((8, QUART), F32)
            _, s1, s2, rsum, sqh, sqa = lax.fori_loop(
                0, pairs, body, (jnp.zeros((seqs, QUART), F32), z8, z8, z8, z8, z8)
            )
            for k, x in ((m, s1), (2 + m, s2)):
                tot[layer, k : k + 1, lanes] = jnp.sum(x, axis=0, keepdims=True)
            for k, x in ((4, rsum), (5, sqh), (6, sqa)):
                x = jnp.sum(x, axis=0, keepdims=True)
                tot[layer, k : k + 1, lanes] = x if m == 0 else tot[layer, k : k + 1, lanes] + x
            between()

    def backward_stats(layer, m):
        rnd, plane, _ = slim_round(3 - layer, m)
        stage_start(plane, rnd, packed(tot[layer, m : m + 1, :], tot[layer, 2 + m : 3 + m, :]))

    def backward_middle(layer, m):
        rnd, plane, line = slim_round(3 - layer, m)
        stage_wait(plane, rnd)
        stage_start(line, rnd, add_slots(plane))

    def backward_end(layer, m):
        rnd, _, line = slim_round(3 - layer, m)
        stage_wait(line, rnd)
        value = add_slots(line)
        tot[layer, m : m + 1, :] = unpacked(value[0:4])
        tot[layer, 2 + m : 3 + m, :] = unpacked(value[4:8])

    def grad_rows(layer, m, slot):
        gain = vec_of(layer, 0)
        for lh in range(2):
            lanes = slice(lh * HALF, (lh + 1) * HALF)
            mean = coef[layer, 2 * m : 2 * m + 1, lanes]
            scale = coef[layer, 2 * m + 1 : 2 * m + 2, lanes]
            count = wide(counts[m : m + 1, :], 4)
            first = tot[layer, m : m + 1, lanes] / count
            second = tot[layer, 2 + m : 3 + m, lanes] / count * scale
            k = scale * gain[:, lanes]

            def body(i, acc):
                r = pl.ds(aligned(m * span + i * (2 * seqs), 16), 2 * seqs)
                y = hid[layer, r, lanes] - first - (rows[layer, r, lanes] - mean) * second
                y = wide(live[r, :], 4) * (k * y)
                g3[0, r, lanes] = y.astype(BF16)
                return acc + fold(y)

            acc = repeat(pairs, body, jnp.zeros((8, HALF), F32), 3)
            acc = jnp.sum(acc, axis=0, keepdims=True)
            if m == 0:
                levels[4:5, lanes] = acc
            else:
                top = lax.broadcasted_iota(jnp.int32, (16, HALF), 0) == 0
                minus = jnp.where(top, -(levels[4:5, lanes] + acc), 0.0)
                g3[0, total_rows:sent_rows, lanes] = minus.astype(BF16)
        here = pl.ds(0, span) if m == 0 else pl.ds(span, span + 16)
        made = across(g3.at[0, here, :], g3.at[1, here, :], slot + m)
        made.start()
        return made

    sums_round = {1: (1, 10), 0: (0, 11)}

    def sums_start(layer):
        parity, rnd = sums_round[layer]
        own_sum = -g3[0, total_rows:sent_rows, :].astype(F32)[0:1]
        far_sum = -g3[1, total_rows:sent_rows, :].astype(F32)[0:1]
        value = jnp.concatenate([own_sum, far_sum, tot[layer, 4:7, :], jnp.zeros((3, W), F32)], axis=0)
        stage_start(in_plane(wide_p, parity), rnd, value)

    def sums_middle(layer):
        parity, rnd = sums_round[layer]
        stage_wait(in_plane(wide_p, parity), rnd)
        stage_start(in_line(wide_z, parity), rnd, add_slots(in_plane(wide_p, parity)))

    def sums_end(layer):
        parity, rnd = sums_round[layer]
        stage_wait(in_line(wide_z, parity), rnd)
        vtot[layer] = add_slots(in_line(wide_z, parity))
        tot[layer, 4:7, :] = vtot[layer, 2:5, :]
        tot[layer, 7:8, :] = wide(counts[0:1, :] + counts[1:2, :], 8)
        env["summed"].add(layer)

        @pl.when(section == layer)
        def _():
            pltpu.make_async_copy(tot.at[layer], v.at[section], v_sems.at[0]).start()

        @pl.when(section != layer)
        def _():
            v_across(layer).start()

    def v_across(layer):
        return pltpu.make_async_remote_copy(
            src_ref=tot.at[layer], dst_ref=v.at[section], send_sem=v_sems.at[1], recv_sem=v_sems.at[2],
            device_id=sibling, device_id_type=MESH,
        )

    def transpose(src, begin=0, end=W // 128):
        def body(j, _):
            c = pl.ds(aligned(j * 128, 128), 128)
            src_t[c, 0:total_rows] = src[0:total_rows, c].T
            return 0

        lax.fori_loop(begin, end, body, 0)

    def transpose_level(src, layer):
        top = lax.broadcasted_iota(jnp.int32, (16, W), 0) == 0
        src[total_rows:sent_rows, :] = jnp.where(top, levels[2 + layer : 3 + layer, :], 0.0).astype(BF16)

        def body(j, _):
            c = pl.ds(aligned(j * 128, 128), 128)
            src_t[c, total_rows:] = src[total_rows:, c].T
            level = src[total_rows:sent_rows, c].astype(F32)[0:1]
            column[layer, c, :] = jnp.broadcast_to(level, (128, 128)).T.astype(BF16)
            return 0

        lax.fori_loop(0, W // 128, body, 0)

    def weight_part(block, grads, c):
        lanes = pl.ds(c * HALF, HALF)

        def body(j, _):
            r = pl.ds(aligned(j * HALF, HALF), HALF)
            block[r, lanes] = dot(src_t[r, :], grads[:, lanes], ((1,), (0,))).astype(BF16)
            return 0

        lax.fori_loop(0, W // HALF, body, 0)

    def source_grad(store, w_own, w_far, between):
        for m in range(2):
            r = pl.ds(m * span, span)

            def body(i, _):
                c = pl.ds(aligned(i * HALF, HALF), HALF)
                y = dot(g3[0, r, :], w_own[c, :], ((1,), (1,))) + dot(g3[1, r, :], w_far[c, :], ((1,), (1,)))
                store(r, c, y)
                return 0

            lax.fori_loop(0, 2, body, 0)
            between()

    env = dict(summed=set(), vtot=vtot, column=column, space=space, ar_send=ar_send, ar_recv=ar_recv,
               ar_other=ar_other, o=o, section=section, here={"batch": b})
    xs = [a for a in bits if a["link"] == "x"]
    ys = [a for a in bits if a["link"] == "y"]
    zs = [a for a in bits if a["link"] == "z"]
    orders = (xs + ys + zs, ys + xs + zs)
    blocks = {
        (1, 0): f_far.at[pl.ds(0, W), :],
        (1, 1): p_far.at[pl.ds(0, W), :],
        (0, 0): wc.at[1, 1],
        (0, 1): wr1,
    }
    parts = {}
    for layer in (1, 0):
        for index in range(2 * PAIRS):
            part, side = index // PAIRS, index % PAIRS

            def lane_of(sec, part=part, side=side):
                return (sec if part == 0 else 1 - sec) * W + side * 2 * PART

            block = blocks[layer, part].at[:, pl.ds(side * 2 * PART, 2 * PART)]
            parts[layer, index] = Reduction(env, layer, index, block, orders, lane_of)
    order = Order()

    def weight_grads(layer, between):
        for part in range(2):
            if part == 1:
                between()
            for c in range(2):
                weight_part(blocks[layer, part], g3.at[part], c)
                order.work(2.0)
                for k in range(c * HALF // PART, (c + 1) * HALF // PART):
                    order.begin(parts[layer, part * PAIRS + k // 2], k % 2)

    def arrived(layer, sends):
        for made in sends:
            made.wait()
        sums_start(layer)

    send_f = []
    for m in range(2):
        by_units(frames, f_own, m)
        fetch(grad_out, m).start()
        if m == 0:
            wait_heads(frames, 1)
        patch_heads(f_own, m)
        here = pl.ds(m * span, span)
        made = across(f_own.at[here, :], f_far.at[here, :], (0, 24)[m])
        made.start()
        send_f.append(made)
    start_across_w(1, w_plan(1), slot_of[1])
    stage_wait(cnt_plane, 0)
    stage_start(cnt_line, 0, add_slots(cnt_plane))
    wait_w(0, w_plan(0), slot_of[0], 0)
    matmul_to(rows.at[0], f_own, wc.at[0, 0], True, 0)
    matmul_to(rows.at[0], f_own, wc.at[0, 0], True, 1)
    wait_w(0, w_plan(0), slot_of[0], 1)
    send_f[0].wait()
    matmul_to(rows.at[0], f_far, wc.at[0, 1], False, 0)
    forward_stats(0, 0)
    send_f[1].wait()

    @pl.when(section == 1)
    def _():
        heads_copy(grad_out, 2).start()

    matmul_to(rows.at[0], f_far, wc.at[0, 1], False, 1)
    forward_middle(0, 0)
    forward_stats(0, 1)
    send_vec.wait_send()
    across(vecs.at[other], vecs.at[other], 3).wait_recv()
    stage_wait(cnt_line, 0)
    counts[...] = add_slots(cnt_line)
    forward_end(0, 0)
    sends = [forward_scan(0, 0, True)]
    forward_middle(0, 1)
    by_units(grad_out, g3.at[1], 0)
    wait_heads(grad_out, 2)
    patch_heads(g3.at[1], 0)
    forward_end(0, 1)
    sends.append(forward_scan(0, 1, True))
    wait_w(1, w_plan(1), slot_of[1], 0)
    matmul_to(rows.at[1], p_own, wc.at[1, 0], True, 0)
    wait_w(1, w_plan(1), slot_of[1], 1)
    sends[0].wait()
    matmul_to(rows.at[1], p_far, wc.at[1, 1], False, 0)
    forward_stats(1, 0)
    matmul_to(rows.at[1], p_own, wc.at[1, 0], True, 1)
    forward_middle(1, 0)
    sends[1].wait()
    matmul_to(rows.at[1], p_far, wc.at[1, 1], False, 1)
    forward_stats(1, 1)
    done_w(0, w_plan(0), slot_of[0])

    start_local_w(0, late_plan, slot_of[2])
    start_across_w(0, late_plan, slot_of[2])

    @pl.when(section == 1)
    def _():
        wc[0, 1, width - late_row :, :] = jnp.zeros((W - width + late_row, W), BF16)

    def source_level():
        def body(i, acc):
            r = pl.ds(aligned(i * (2 * seqs), 16), 2 * seqs)
            return acc + fold(wide(live[r, :], 8) * f_own[r, :].astype(F32))

        acc = repeat(2 * pairs, body, jnp.zeros((8, W), F32), 3)
        levels[0:1, :] = jnp.sum(acc, axis=0, keepdims=True)

    forward_end(1, 0)
    forward_scan(1, 0, False)
    forward_middle(1, 1)
    by_units(grad_out, g3.at[1], 1)
    patch_heads(g3.at[1], 1)
    source_level()
    forward_end(1, 1)
    level_plane, level_line = in_plane(wide_p, 0), in_line(wide_z, 0)
    stage_start(level_plane, 9, jnp.concatenate([levels[0:2, :], jnp.zeros((6, W), F32)], axis=0))
    forward_scan(1, 1, False)
    backward_scan(1, 0, g3.at[1])
    backward_stats(1, 0)
    stage_wait(level_plane, 9)
    stage_start(level_line, 9, add_slots(level_plane))
    backward_scan(1, 1, g3.at[1])
    backward_stats(1, 1)
    backward_middle(1, 0)
    pl.semaphore_signal(credit.at[0], inc=1, device_id=sibling, device_id_type=MESH)
    transpose(p_own, 0, W // 256)
    backward_middle(1, 1)
    backward_end(1, 0)
    pl.semaphore_wait(credit.at[0], 1)
    sends = [grad_rows(1, 0, 20)]
    transpose(p_own, W // 256)
    stage_wait(level_line, 9)
    levels[2:4, :] = (add_slots(level_line) / wide(counts[0:1, :] + counts[1:2, :], 8))[0:2]
    transpose_level(p_own, 1)
    backward_end(1, 1)
    sends.append(grad_rows(1, 1, 20))
    weight_grads(1, lambda: arrived(1, sends))
    wait_w(1, w_plan(1), slot_of[1], 2)
    done_w(1, w_plan(1), slot_of[1])

    def keep_down(r, c, y):
        p_own[r, c] = y.astype(BF16)

    source_grad(keep_down, wc.at[1, 0], wr1, lambda: order.work(3.0))
    pl.semaphore_signal(credit.at[1], inc=1, device_id=sibling, device_id_type=MESH)
    sums_middle(1)
    backward_scan(0, 0, p_own, lambda: order.work(0.6))
    backward_stats(0, 0)
    backward_scan(0, 1, p_own, lambda: order.work(0.6))
    backward_stats(0, 1)
    backward_middle(0, 0)
    sums_end(1)
    transpose(f_own)
    transpose_level(f_own, 0)
    backward_middle(0, 1)
    order.work(3.0)
    backward_end(0, 0)
    pl.semaphore_wait(credit.at[1], 1)
    sends = [grad_rows(0, 0, 22)]
    backward_end(0, 1)
    sends.append(grad_rows(0, 1, 22))
    order.work(2.0)
    weight_grads(0, lambda: arrived(0, sends))
    wait_w(0, late_plan, slot_of[2], 0)
    wait_w(0, late_plan, slot_of[2], 1)
    done_w(0, late_plan, slot_of[2])

    def keep_source(r, c, y):
        rows[0, r, c] = y

    fetch(grad_out, 0).start()
    fetch(grad_out, 1).start()
    sums_middle(0)
    source_grad(keep_source, wc.at[0, 0], wc.at[0, 1], lambda: order.work(3.0))
    sums_end(0)

    def give(m):
        return pltpu.make_async_copy(staged.at[m], gf.at[m], stage_sem.at[m])

    for m in range(2):
        fetch(grad_out, m).wait()

        def finish_frames(i, _, m=m):
            straight = staged[m, pl.ds(2 * i, 2)].astype(F32).reshape(2 * seqs, half)
            y = rows[0, pl.ds(aligned(m * span + 2 * i * seqs, 8), 2 * seqs), :]
            y = jnp.where(section == 0, y[:, :half], y[:, late_shift : late_shift + half])
            staged[m, pl.ds(2 * i, 2)] = (y + straight).reshape(2, seqs, half).astype(BF16)
            return 0

        repeat(pairs, finish_frames, 0, 3)
        give(m).start()
        order.work(2.0)
    order.drain()
    for m in range(2):
        give(m).wait()

    for layer in range(2):

        @pl.when(section == layer)
        def _(layer=layer):
            pltpu.make_async_copy(tot.at[layer], v.at[section], v_sems.at[0]).wait()
            pltpu.make_async_remote_copy(
                src_ref=tot.at[layer], dst_ref=v.at[other], send_sem=v_sems.at[1], recv_sem=v_sems.at[2],
                device_id=sibling, device_id_type=MESH,
            ).wait_recv()

        @pl.when(section != layer)
        def _(layer=layer):
            v_across(layer).wait_send()

    own_part, far_part = v[section], v[other]
    first = jnp.where(section == 0, own_part, far_part)
    second = jnp.where(section == 0, far_part, own_part)
    for row, terms in ((0, (2, 3)), (1, (0, 1)), (2, (4,))):
        for lane, x in ((0, first), (W, second)):
            total = x[terms[0] : terms[0] + 1, :]
            for k in terms[1:]:
                total = total + x[k : k + 1, :]
            vectors[row : row + 1, lane : lane + W] = total
    squares = jnp.sum(first[5:7, :] + second[5:7, :], axis=1, keepdims=True)
    root = jnp.sqrt(squares / (first[7:8, 0:1] * width))
    for k in range(2):
        vectors[3 + k : 4 + k, :] = jnp.broadcast_to(root[k : k + 1], (1, 2 * W))
    vectors[5:8, :] = jnp.zeros((3, 2 * W), F32)


def write_results(o, gf, vectors, grad_weight, grad_frames, grad_gains, grad_shifts, grad_recurs, table):
    width = grad_weight.shape[2]
    grad_weight[0] = o[...][:, :width].astype(F32)
    grad_frames[...] = gf[...]

    @pl.when(pl.program_id(0) == 0)
    def _():
        for k, out in enumerate((grad_gains, grad_shifts, grad_recurs)):
            out[...] = vectors[k : k + 1, 0:width]
        table[...] = jnp.concatenate([vectors[3:4, 0:1], vectors[4:5, 0:1]], axis=1)


def results(o, gf, vectors):
    micro, steps, seqs, half = gf.shape
    width = 2 * half
    count = W * 2 // 256
    frames = micro * steps // count
    whole = lambda shape: pl.BlockSpec(shape, lambda i: (0, 0))
    out = pl.pallas_call(
        write_results,
        grid=(count,),
        in_specs=[
            pl.BlockSpec((256, 2 * W), lambda i: (i, 0)),
            pl.BlockSpec((frames, seqs, half), lambda i: (i, 0, 0)),
            whole((8, 2 * W)),
        ],
        out_specs=(
            pl.BlockSpec((1, 256, width), lambda i: (0, i, 0)),
            pl.BlockSpec((frames, seqs, half), lambda i: (i, 0, 0)),
            whole((1, width)),
            whole((1, width)),
            whole((1, width)),
            whole((1, 2)),
        ),
        out_shape=(
            jax.ShapeDtypeStruct((1, width, width), F32),
            jax.ShapeDtypeStruct((micro * steps, seqs, half), BF16),
            jax.ShapeDtypeStruct((1, width), F32),
            jax.ShapeDtypeStruct((1, width), F32),
            jax.ShapeDtypeStruct((1, width), F32),
            jax.ShapeDtypeStruct((1, 2), F32),
        ),
        compiler_params=pltpu.CompilerParams(vmem_limit_bytes=64 * 1024 * 1024),
    )(o.reshape(2 * W, 2 * W), gf.reshape(micro * steps, seqs, half), vectors)
    return out[1].reshape(gf.shape), out[0], *out[2:]


def whole_step(dims, frames, grad_out, weights, gains, shifts, recurs, lengths, masks):
    nz, ny, nx = dims
    micro, steps, seqs, half = frames.shape
    width = 2 * half
    views = seqs // lengths.shape[1]
    rows = micro * steps * seqs
    np_ = ny * nx
    wide_rows = (rows + 16 + 127) // 128 * 128
    depth = (nx * ny * nz - 1).bit_length()
    any_ = pl.BlockSpec(memory_space=pl.ANY)
    held = pl.BlockSpec(memory_space=pltpu.VMEM)
    dma = pltpu.SemaphoreType.DMA
    return pl.pallas_call(
        functools.partial(kernel, dims, steps, seqs, views),
        out_shape=(
            jax.ShapeDtypeStruct((2, W, 2 * W), BF16),
            jax.ShapeDtypeStruct(frames.shape, BF16),
            jax.ShapeDtypeStruct((8, 2 * W), F32),
        ),
        in_specs=[any_] * 3 + [held] * 5,
        out_specs=(any_, any_, held),
        scratch_shapes=[
            pltpu.VMEM((wide_rows, W), BF16),
            pltpu.VMEM((rows, W), BF16),
            pltpu.VMEM((wide_rows, W), BF16),
            pltpu.VMEM((rows, W), BF16),
            pltpu.VMEM((2, wide_rows, W), BF16),
            pltpu.VMEM((2, 2, W, W), BF16),
            pltpu.VMEM((W, W), BF16),
            pltpu.VMEM((W, wide_rows), BF16),
            pltpu.VMEM((rows, 128), F32),
            pltpu.VMEM((128, 128), F32),
            pltpu.VMEM(frames.shape, BF16),
            pltpu.VMEM((micro, steps, seqs, 128), BF16),
            pltpu.VMEM((5, W, (width - W) % 128), BF16),
            pltpu.VMEM((2, 8, W), F32),
            pltpu.VMEM((2, 8, 2 * W), F32),
            pltpu.VMEM((2, rows, W), F32),
            pltpu.VMEM((2, rows, W), F32),
            pltpu.VMEM((2, 8, W), F32),
            pltpu.VMEM((2, 8, W), F32),
            pltpu.VMEM((2, 8, W), F32),
            pltpu.VMEM((8, W), F32),
            pltpu.VMEM((2, W, 128), BF16),
            pltpu.VMEM((8, 128), F32),
            pltpu.VMEM((1, np_, 8, 128), F32),
            pltpu.VMEM((1, nz, 8, 128), F32),
            pltpu.VMEM((4, np_, 8, QUART), F32),
            pltpu.VMEM((4, nz, 8, QUART), F32),
            pltpu.VMEM((2, np_, 8, W), F32),
            pltpu.VMEM((2, nz, 8, W), F32),
            pltpu.VMEM((2, 2 * PAIRS, W, 2 * PART), BF16),
            dma((3, 25)),
            dma((3,)),
            dma((2,)),
            pltpu.SemaphoreType.REGULAR((2,)),
            dma((12, max(np_, 2))),
            dma((12, max(np_, 2))),
            dma((12, max(nz, 2))),
            dma((12, max(nz, 2))),
            dma((2, 2 * PAIRS, 2, 2 * depth + 2)),
            dma((2, 2 * PAIRS, 2, 2 * depth + 2)),
            dma((2, 2 * PAIRS, 2, 2)),
        ],
        compiler_params=pltpu.CompilerParams(
            collective_id=0, has_side_effects=True, vmem_limit_bytes=64 * 1024 * 1024
        ),
    )(frames, grad_out, weights, gains, shifts, recurs, lengths, masks)


def shards(dims, frames, grad_out, weights, gains, shifts, recurs, lengths, masks):
    return results(*whole_step(dims, frames, grad_out, weights, gains, shifts, recurs, lengths, masks))


def solution(mesh):
    in_specs = (
        P(None, None, "batch", "section"),
        P(None, None, "batch", "section"),
        P("section", None, None),
        P("section", None),
        P("section", None),
        P("section", None),
        P(None, "batch"),
        P(None, None, "batch"),
    )
    out_specs = (
        P(None, None, "batch", "section"),
        P("section", None, None),
        P("section", None),
        P("section", None),
        P("section", None),
        P("section", None),
    )
    body = functools.partial(shards, grid_of(mesh.shape["batch"]))
    return jax.shard_map(body, mesh=mesh, in_specs=in_specs, out_specs=out_specs, check_vma=False)
```

```python
import functools

import jax
import jax.numpy as jnp
from jax import lax
from jax.experimental import pallas as pl
from jax.experimental.pallas import tpu as pltpu
from jax.sharding import PartitionSpec as P

EPS = 1e-05
W = 1024
HALF = W // 2
QUART = W // 4
PAIRS = 1
PART = W // PAIRS // 2
MESH = pl.DeviceIdType.MESH
F32 = jnp.float32
BF16 = jnp.bfloat16


def grid_of(size):
    if size == 16:
        return (4, 2, 2)
    if size == 128:
        return (8, 4, 4)
    return (size, 1, 1)


def aligned(x, k):
    return pl.multiple_of(x, k)


def wide(x, reps):
    return jnp.concatenate([x] * reps, axis=1)


def fold(x):
    rows = x.shape[0]
    total = x[0:8]
    for k in range(8, rows, 8):
        total = total + x[k : k + 8]
    return total


def repeat(count, body, init, times):
    while count % times:
        times -= 1

    def several(i, carry):
        for j in range(times):
            carry = body(i * times + j, carry)
        return carry

    return lax.fori_loop(0, count // times, several, init)


def dot(a, b, dims):
    return lax.dot_general(a, b, (dims, ((), ())), preferred_element_type=F32)


class Reduction:
    def __init__(self, env, layer, index, block, orders, lane_of):
        self.env, self.layer, self.index, self.block, self.orders = env, layer, index, block, orders
        self.lane_of = lane_of
        self.space = env["space"].at[layer, index]
        self.depth = len(orders[0])
        self.regions = [self.halves(i, order) for i, order in enumerate(orders)]
        self.step = 0
        self.waits = []
        depth = self.depth
        self.steps = [functools.partial(self.scatter, 0)]
        self.steps += [functools.partial(self.scatter, k) for k in range(1, depth)]
        self.steps += [functools.partial(self.gather, k) for k in range(depth - 1, 0, -1)]
        self.steps += [self.give, self.finish]

    def halves(self, i, order):
        row, rows, lane, lanes = 0, W, i * PART, PART
        out = [(row, rows, lane, lanes)]
        for axis in order:
            if rows > 16:
                rows //= 2
                row = row + axis["bit"] * rows
            else:
                lanes //= 2
                lane = lane + axis["bit"] * lanes
            out.append((row, rows, lane, lanes))
        return out

    @property
    def free_to_go(self):
        return self.step != self.depth or self.layer in self.env["summed"]

    @property
    def done(self):
        return self.step >= len(self.steps)

    def advance(self):
        self.sent = []
        self.steps[self.step]()
        self.step += 1
        return self.sent

    def remote(self, i, src, dst, slot, where, recv=None):
        sems = (self.layer, self.index, i, slot)
        return pltpu.make_async_remote_copy(
            src_ref=src, dst_ref=dst, send_sem=self.env["ar_send"].at[sems],
            recv_sem=self.env["ar_recv"].at[sems] if recv is None else recv, device_id=where, device_id_type=MESH,
        )

    def wait(self):
        for made, came in self.waits:
            made.wait_send()
            came.wait_recv()
        self.waits = []

    def came_at(self, i, k):
        row = sum(r[1] for r in self.regions[i][1 : k + 1])
        _, rows, _, lanes = self.regions[i][k + 1]
        return row, rows, i * PART, lanes

    def scatter(self, k):
        if k > 0:
            self.wait()
            self.add(k - 1)
        for i, order in enumerate(self.orders):
            self.scatter_part(i, k, order[k])

    def start_part(self, i):
        self.sent = []
        self.scatter_part(i, 0, self.orders[i][0])
        if i == 1:
            self.step = 1
        return self.sent

    def scatter_part(self, i, k, axis):
        row, rows, lane, lanes = self.regions[i][k]
        _, rows2, _, lanes2 = self.regions[i][k + 1]
        give_row = row + (1 - axis["bit"]) * rows2 if rows2 < rows else row
        give_lane = lane if rows2 < rows else lane + (1 - axis["bit"]) * lanes2
        src = self.block.at[pl.ds(aligned(give_row, 16), rows2), pl.ds(aligned(give_lane, 128), lanes2)]
        at, n, at_lane, n_lanes = self.came_at(i, k)
        dst = self.space.at[pl.ds(at, n), pl.ds(at_lane, n_lanes)]
        made = self.remote(i, src, dst, k, axis["partner"])
        made.start()
        self.waits.append((made, made))
        self.sent.append((axis["link"], rows2 * lanes2 * 2))

    def add(self, k, last=False):
        rows = self.regions[0][k + 1][1]
        size = min(rows, 64)
        out = []
        for i in range(2):
            row, _, lane, lanes = self.regions[i][k + 1]
            at, _, at_lane, _ = self.came_at(i, k)
            lane = aligned(lane, 128)
            extra = None
            if last:
                part = self.index // PAIRS
                first = aligned((self.index % PAIRS) * 2 * PART + lane, 128)
                extra = self.env["vtot"][self.layer, part : part + 1, pl.ds(first, lanes)]
            out.append((row, lane, lanes, at, at_lane, self.local(i, k + 1)[0], extra))

        def body(j, _):
            for row, lane, lanes, at, at_lane, home, extra in out:
                here = pl.ds(aligned(row + j * size, 16), size)
                total = self.block[here, pl.ds(lane, lanes)].astype(F32)
                total = total + self.space[pl.ds(aligned(at + j * size, 16), size), pl.ds(at_lane, lanes)].astype(F32)
                if last:
                    column = self.env["column"][self.layer, here, :].astype(F32)
                    total = total + wide(column, lanes // 128) * extra
                    to = pl.ds(aligned(home + j * size, 16), size)
                    self.space[to, pl.ds(lane, lanes)] = total.astype(BF16)
                else:
                    self.block[here, pl.ds(lane, lanes)] = total.astype(BF16)
            return 0

        lax.fori_loop(0, rows // size, body, 0)

    def local(self, i, k):
        row, rows, lane, lanes = self.regions[i][k]
        return row - self.regions[i][1][0], rows, lane, lanes

    def gather(self, k):
        self.wait()
        if k == self.depth - 1:
            self.add(k, last=True)
        for i, order in enumerate(self.orders):
            axis = order[k]
            row, rows, lane, lanes = self.local(i, k + 1)
            row0, rows0, lane0, lanes0 = self.local(i, k)
            if rows0 > rows:
                far = (row0 + (1 - axis["bit"]) * rows, rows, lane, lanes)
            else:
                far = (row, rows, lane0 + (1 - axis["bit"]) * lanes, lanes)
            refs = [
                self.space.at[pl.ds(aligned(r, 16), n), pl.ds(aligned(c, 128), w)]
                for r, n, c, w in ((row, rows, lane, lanes), far)
            ]
            made = self.remote(i, refs[0], refs[0], self.depth + k, axis["partner"])
            made.start()
            self.waits.append((made, self.remote(i, refs[1], refs[1], self.depth + k, axis["partner"])))
            self.sent.append((axis["link"], rows * lanes * 2))

    def result(self, i, bit, section):
        rows = self.regions[i][1][1]
        lane = aligned(self.lane_of(section) + i * PART, PART)
        return self.env["o"].at[section, pl.ds(aligned(bit * rows, 16), rows), pl.ds(lane, PART)]

    def gathered(self, i):
        return self.space.at[pl.ds(0, self.regions[i][1][1]), pl.ds(i * PART, PART)]

    def deliver(self, i, near, straight):
        axis, section = self.orders[i][0], self.env["section"]
        slot = 2 * self.depth + (0 if near else 1)
        recv = None if straight else self.env["ar_other"].at[self.layer, self.index, i, 0 if near else 1]
        where = dict(self.env["here"] if near else axis["partner"], section=self.layer)
        return self.remote(i, self.gathered(i), self.result(i, axis["bit"], section), slot, where, recv)

    def arrival(self, i, near, straight):
        axis, section = self.orders[i][0], self.env["section"]
        slot = 2 * self.depth + (0 if near else 1)
        recv = None if straight else self.env["ar_other"].at[self.layer, self.index, i, 0 if near else 1]
        bit = axis["bit"] if near else 1 - axis["bit"]
        frm = section if straight else 1 - section
        where = dict(self.env["here"] if near else axis["partner"], section=frm)
        return self.remote(i, self.gathered(i), self.result(i, bit, frm), slot, where, recv)

    def kept(self, i):
        sem = self.env["ar_recv"].at[self.layer, self.index, i, 2 * self.depth]
        return pltpu.make_async_copy(
            self.gathered(i), self.result(i, self.orders[i][0]["bit"], self.env["section"]), sem
        )

    def give(self):
        self.wait()

        @pl.when(self.env["section"] == self.layer)
        def _():
            for i in range(2):
                self.deliver(i, False, True).start()
                self.kept(i).start()

        @pl.when(self.env["section"] != self.layer)
        def _():
            for i in range(2):
                self.deliver(i, False, False).start()
                self.deliver(i, True, False).start()

        for i, order in enumerate(self.orders):
            self.sent.append((order[0]["link"], self.regions[i][1][1] * PART * 2))

    def finish(self):
        @pl.when(self.env["section"] == self.layer)
        def _():
            for i in range(2):
                self.kept(i).wait()
                self.deliver(i, False, True).wait_send()
                self.arrival(i, False, True).wait_recv()
                self.arrival(i, True, False).wait_recv()
                self.arrival(i, False, False).wait_recv()

        @pl.when(self.env["section"] != self.layer)
        def _():
            for i in range(2):
                self.deliver(i, False, False).wait_send()
                self.deliver(i, True, False).wait_send()


class Order:
    RATE, HOP = 70e3, 1.8

    def __init__(self):
        self.now = 0.0
        self.free = {}
        self.going = []

    def sent(self, copies):
        end = self.now
        for link, size in copies:
            self.free[link] = max(self.now, self.free.get(link, 0.0)) + size / self.RATE
            end = max(end, self.free[link])
        return end + self.HOP

    def begin(self, one, i):
        end = self.sent(one.start_part(i))
        if i == 0:
            one.due = end
        else:
            one.due = max(one.due, end)
            self.going.append(one)

    def advance(self, one):
        self.now = max(self.now, one.due) + 0.4
        one.due = self.sent(one.advance())
        if one.done:
            self.going.remove(one)

    def work(self, cost):
        self.now += cost
        while True:
            due = [x for x in self.going if x.due <= self.now and x.free_to_go]
            if not due:
                return
            self.advance(min(due, key=lambda x: x.due))

    def drain(self):
        while self.going:
            self.advance(min(self.going, key=lambda x: x.due))


def kernel(dims, steps, seqs, views, frames, grad_out, weights, gains, shifts, recurs, lengths, masks, o, gf, vectors, f_own, f_far, p_own, p_far, g3, wc, wr1, src_t, live, turn,
           staged, heads, tails, v, vecs, rows, hid, coef, tot, vtot, levels, column, counts, cnt_p, cnt_z, slim_p, slim_z,
           wide_p, wide_z, space, sems, v_sems, stage_sem, credit, pl_send, pl_recv, z_send, z_recv, ar_send, ar_recv,
           ar_other):
    nz, ny, nx = dims
    np_ = ny * nx
    span = steps * seqs
    total_rows = 2 * span
    sent_rows = total_rows + 16
    pairs = steps // 2
    section = lax.axis_index("section")
    other = 1 - section
    b = lax.axis_index("batch")
    mp = lax.rem(b, np_)
    mz = b // np_

    def at_plane(i):
        return {"batch": b - mp + i}

    def at_z(i):
        return {"batch": b + (i - mz) * np_}

    bits = []
    for link, count, stride in (("x", nx, 1), ("y", ny, nx), ("z", nz, np_)):
        while count > 1:
            bit = lax.rem(b // stride, 2)
            bits.append(dict(bit=bit, partner={"batch": b + (1 - 2 * bit) * stride}, link=link))
            count //= 2
            stride *= 2
    sibling = {"section": other}

    def local(src, dst, slot):
        return pltpu.make_async_copy(src, dst, sems.at[0, slot])

    def across(src, dst, slot):
        return pltpu.make_async_remote_copy(
            src_ref=src, dst_ref=dst, send_sem=sems.at[1, slot], recv_sem=sems.at[2, slot],
            device_id=sibling, device_id_type=MESH,
        )

    half = frames.shape[3]
    width = 2 * half
    lead = W - half
    rest = width - W
    full = rest // 128 * 128

    def fetch(source, m):
        return pltpu.make_async_copy(source.at[m], staged.at[m], stage_sem.at[m])

    def by_units(source, target, m):
        fetch(source, m).wait()

        @pl.when(section == 0)
        def _():
            pad = jnp.zeros((2 * seqs, lead), F32)

            def place(i, _):
                x = staged[m, pl.ds(2 * i, 2)].astype(F32).reshape(2 * seqs, half)
                to = pl.ds(aligned(m * span + 2 * i * seqs, 16), 2 * seqs)
                target[to, :] = jnp.concatenate([x, pad], axis=1).astype(BF16)
                return 0

            repeat(pairs, place, 0, 3)

        @pl.when(section == 1)
        def _():
            pad = jnp.zeros((2 * seqs, 2 * lead), F32)

            def place(i, _):
                x = staged[m, pl.ds(2 * i, 2)].astype(F32).reshape(2 * seqs, half)
                to = pl.ds(aligned(m * span + 2 * i * seqs, 16), 2 * seqs)
                target[to, :] = jnp.concatenate([x[:, lead:], pad], axis=1).astype(BF16)
                return 0

            repeat(pairs, place, 0, 3)

    def patch_heads(target, m):
        @pl.when(section == 0)
        def _():
            lane = lax.broadcasted_iota(jnp.int32, (2 * seqs, 128), 1)

            def place(i, _):
                to = pl.ds(aligned(m * span + 2 * i * seqs, 16), 2 * seqs)
                head = heads[m, pl.ds(2 * i, 2)].astype(F32).reshape(2 * seqs, 128)
                head = pltpu.roll(head, 128 - lead, 1)
                old = target[to, W - 128 :].astype(F32)
                target[to, W - 128 :] = jnp.where(lane < 128 - lead, old, head).astype(BF16)
                return 0

            repeat(pairs, place, 0, 3)

    def pieces(row, count, u, block, spot):
        r = pl.ds(row, count)
        to = pl.ds(0, count)
        if u == 0:
            return [(weights.at[0, r, pl.ds(0, W)], block.at[to, :])]
        return [
            (weights.at[0, r, pl.ds(W, full)], block.at[to, pl.ds(0, full)]),
            (weights.at[0, r, pl.ds(W + full, rest - full)], tails.at[spot, to, :]),
        ]

    rows_of = {0: (0, W), 1: (W, rest)}

    def w_plan(layer):
        mine, far = rows_of[layer], rows_of[1 - layer]
        plan = [
            (mine, layer, far, 1 - layer, wc.at[layer, 0], 2 * layer),
            (far, layer, mine, 1 - layer, wc.at[layer, 1], 2 * layer + 1),
        ]
        if layer == 1:
            plan.append((mine, 0, far, 1, wr1, 4))
        return plan

    late_row = (width - half) // 16 * 16
    late_shift = half - late_row
    late_plan = [
        ((0, W), 0, (late_row, width - late_row), 1, wc.at[0, 0], 0),
        ((0, W), 1, (late_row, width - late_row), 0, wc.at[0, 1], 1),
    ]
    slot_of = {0: 4, 1: 8, 2: 14}

    def local_w(plan, base, which):
        r, u, _, _, block, spot = plan[which]
        return [local(a, t, base + 2 * which + i) for i, (a, t) in enumerate(pieces(*r, u, block, spot))]

    def across_w(plan, base, which):
        _, _, r, u, block, spot = plan[which]
        return [across(a, t, base + 2 * which + i) for i, (a, t) in enumerate(pieces(*r, u, block, spot))]

    def start_local_w(layer, plan, base):
        @pl.when(section == layer)
        def _():
            for which in range(len(plan)):
                for made in local_w(plan, base, which):
                    made.start()

    def start_across_w(layer, plan, base):
        @pl.when(section == layer)
        def _():
            for which in range(len(plan)):
                for made in across_w(plan, base, which):
                    made.start()

    def last_units(block, spot):
        def body(i, _):
            r = pl.ds(aligned(i * 128, 128), 128)
            x = tails[spot, r, :].astype(F32)
            x = jnp.concatenate([x, jnp.zeros((128, 128 - x.shape[1]), F32)], axis=1)
            block[r, full:] = x.astype(BF16)
            return 0

        lax.fori_loop(0, W // 128, body, 0)

    def wait_w(layer, plan, base, which):
        _, own_u, _, far_u, block, spot = plan[which]

        @pl.when(section == layer)
        def _():
            for made in local_w(plan, base, which):
                made.wait()
            if own_u == 1:
                last_units(block, spot)

        @pl.when(section != layer)
        def _():
            for made in across_w(plan, base, which):
                made.wait_recv()
            if far_u == 1:
                last_units(block, spot)

    def done_w(layer, plan, base):
        @pl.when(section == layer)
        def _():
            for which in range(len(plan)):
                for made in across_w(plan, base, which):
                    made.wait_send()

    def heads_copy(source, slot):
        return across(source.at[:, :, :, pl.ds(0, 128)], heads, slot)

    def wait_heads(source, slot):
        @pl.when(section == 0)
        def _():
            heads_copy(source, slot).wait_recv()

        @pl.when(section == 1)
        def _():
            heads_copy(source, slot).wait_send()

    fetch(frames, 0).start()
    fetch(frames, 1).start()
    for layer in range(2):
        start_local_w(layer, w_plan(layer), slot_of[layer])

    barrier = pltpu.get_barrier_semaphore()
    greeted = [dict(sibling)]
    greeted += [at_plane(lax.rem(mp + k, np_)) for k in range(1, np_)]
    greeted += [at_z(lax.rem(mz + k, nz)) for k in range(1, nz)]
    greeted += [dict(axis["partner"], section=other) for axis in bits]
    for where in greeted:
        pl.semaphore_signal(barrier, inc=1, device_id=where, device_id_type=MESH)

    for k, (x, fill) in enumerate(((gains, 0.0), (shifts, -1e30), (recurs, 0.0))):
        vecs[section, k : k + 1, 0:width] = x[...]
        vecs[section, k : k + 1, width:] = jnp.full((1, 2 * W - width), fill, F32)
    vecs[section, 3:8, :] = jnp.zeros((5, 2 * W), F32)

    gap = jnp.zeros((W - rest, W), BF16)

    @pl.when(section == 0)
    def _():
        wc[0, 1, rest:, :] = gap
        wc[1, 1, rest:, :] = gap

    @pl.when(section == 1)
    def _():
        wc[0, 0, rest:, :] = gap
        wc[1, 0, rest:, :] = gap
        wr1[rest:, :] = gap

    for spot in (0, 2):
        tails[spot, rest:, :] = jnp.zeros((W - rest, rest - full), BF16)
    for spare in (f_own, p_own, g3.at[0], g3.at[1]):
        spare[sent_rows:, :] = jnp.zeros((spare.shape[0] - sent_rows, W), BF16)

    pl.semaphore_wait(barrier, len(greeted))

    @pl.when(section == 1)
    def _():
        heads_copy(frames, 1).start()

    start_across_w(0, w_plan(0), slot_of[0])
    send_vec = across(vecs.at[section], vecs.at[section], 3)
    send_vec.start()

    def stage_copy(where, rnd, slot, k, back):
        buf, parity, size, me, at, send, recv = where
        there = at(lax.rem(me + (size - k if back else k), size))
        ref = buf.at[parity, slot]
        return pltpu.make_async_remote_copy(
            src_ref=ref, dst_ref=ref, send_sem=send.at[rnd, k], recv_sem=recv.at[rnd, k],
            device_id=there, device_id_type=MESH,
        )

    def in_plane(buf, parity):
        return (buf, parity, np_, mp, at_plane, pl_send, pl_recv)

    def in_line(buf, parity):
        return (buf, parity, nz, mz, at_z, z_send, z_recv)

    def stage_start(where, rnd, value):
        buf, parity, size, me = where[:4]
        buf[parity, me] = value
        for k in range(1, size):
            stage_copy(where, rnd, me, k, False).start()

    def stage_wait(where, rnd):
        size, me = where[2:4]
        for k in range(1, size):
            stage_copy(where, rnd, me, k, False).wait_send()
            stage_copy(where, rnd, lax.rem(me + size - k, size), k, True).wait_recv()

    def add_slots(where):
        buf, parity, size = where[:3]
        total = buf[parity, 0]
        for k in range(1, size):
            total = total + buf[parity, k]
        return total

    groups = lengths.shape[1]
    s_at = lax.broadcasted_iota(jnp.int32, (seqs, groups), 0)
    g_at = lax.broadcasted_iota(jnp.int32, (seqs, groups), 1) * views
    there = (s_at >= g_at) & (s_at < g_at + views)
    position = lax.broadcasted_iota(jnp.int32, (seqs, 128), 1)
    local_counts = []
    for m in range(2):
        turn[...] = jnp.zeros_like(turn)
        turn[0:steps, 0:seqs] = masks[m].astype(F32)
        mask = turn[...].T[0:seqs]
        length = jnp.broadcast_to(lengths[m : m + 1, :], (seqs, groups)).astype(F32)
        limit = jnp.sum(jnp.where(there, length, 0.0), axis=1, keepdims=True)
        alive = (position.astype(F32) < limit) & ((mask > 0.0) | (position == 0))
        alive = jnp.where(position < steps, alive.astype(F32), 0.0)
        total = jnp.zeros((seqs, 128), F32)
        for t in range(steps):
            at = m * span + t * seqs
            cells = jnp.broadcast_to(alive[:, t : t + 1], (seqs, 128))
            live[at : at + seqs, :] = cells
            total = total + cells
        local_counts.append(jnp.sum(total, axis=0, keepdims=True))
    n_own = jnp.concatenate(local_counts * 4, axis=0)

    cnt_plane, cnt_line = in_plane(cnt_p, 0), in_line(cnt_z, 0)
    stage_start(cnt_plane, 0, n_own)

    def vec_of(layer, k):
        return vecs[layer, k : k + 1, pl.ds(aligned(section * W, W), W)]

    def matmul_to(out, a, w, first, m):
        r = pl.ds(m * span, span)

        def body(i, _):
            c = pl.ds(aligned(i * HALF, HALF), HALF)
            y = dot(a[r, :], w[:, c], ((1,), (0,)))
            out[r, c] = y if first else out[r, c] + y
            return 0

        lax.fori_loop(0, 2, body, 0)

    def packed(x, y):
        return jnp.concatenate([z[:, k * QUART : (k + 1) * QUART] for z in (x, y) for k in range(4)], axis=0)

    def unpacked(x):
        return jnp.concatenate([x[k : k + 1] for k in range(4)], axis=1)

    def merge_slots(where, counts_of):
        buf, parity, size = where[:3]
        s = [buf[parity, k, 0:4, :] for k in range(size)]
        q = [buf[parity, k, 4:8, :] for k in range(size)]
        n = [wide(counts_of(k), 2) for k in range(size)]
        total, squares, count = sum(s[1:], s[0]), sum(q[1:], q[0]), sum(n[1:], n[0])
        mean = total / count
        for k in range(size):
            d = s[k] / n[k] - mean
            squares = squares + n[k] * d * d
        return jnp.concatenate([total, squares], axis=0)

    def slim_round(which, m):
        return 1 + 2 * which + m, in_plane(slim_p, 2 * m + which % 2), in_line(slim_z, 2 * m + which % 2)

    def forward_stats(layer, m):
        start = jnp.sum(rows[layer, m * span : m * span + seqs, :], axis=0, keepdims=True) * (1.0 / seqs)

        def body(i, carry):
            s, q = carry
            r = pl.ds(aligned(m * span + i * (2 * seqs), 16), 2 * seqs)
            d = rows[layer, r, :] - start
            kept = wide(live[r, :], 8) * d
            return s + fold(kept), q + fold(kept * d)

        zero = jnp.zeros((8, W), F32)
        s, q = repeat(pairs, body, (zero, zero), 3)
        s, q = jnp.sum(s, axis=0, keepdims=True), jnp.sum(q, axis=0, keepdims=True)
        n = wide(local_counts[m], 8)
        rnd, plane, _ = slim_round(layer, m)
        stage_start(plane, rnd, packed(s + n * start, jnp.maximum(q - s * s / n, 0.0)))

    def forward_middle(layer, m):
        rnd, plane, line = slim_round(layer, m)
        stage_wait(plane, rnd)
        stage_start(line, rnd, merge_slots(plane, lambda k: cnt_p[0, k, m : m + 1, :]))

    def forward_end(layer, m):
        rnd, _, line = slim_round(layer, m)
        stage_wait(line, rnd)
        value = merge_slots(line, lambda k: cnt_z[0, k, m : m + 1, :])
        count = wide(counts[m : m + 1, :], 8)
        mean = unpacked(value[0:4]) / count
        scale = lax.rsqrt(unpacked(value[4:8]) / count + EPS)
        coef[layer, 2 * m : 2 * m + 1, :] = mean
        coef[layer, 2 * m + 1 : 2 * m + 2, :] = scale
        slope = vec_of(layer, 0) * scale
        coef[layer, 4 + 2 * m : 5 + 2 * m, :] = slope
        coef[layer, 5 + 2 * m : 6 + 2 * m, :] = vec_of(layer, 1) - mean * slope

    def forward_scan(layer, m, passes):
        rec = vec_of(layer, 2)
        slope = coef[layer, 4 + 2 * m : 5 + 2 * m, :]
        shift = coef[layer, 5 + 2 * m : 6 + 2 * m, :]

        def body(i, carry):
            h, level = carry
            r = pl.ds(aligned(m * span + i * (2 * seqs), 16), 2 * seqs)
            x = rows[layer, r, :] * slope + shift
            lv = wide(live[r, :], 8)
            alive = lv > 0.0
            both = []
            for k in range(2):
                part = slice(k * seqs, (k + 1) * seqs)
                z = x[part] + rec * h
                soft = jnp.maximum(z, 0.0) + jnp.log(1.0 + jnp.exp(-jnp.abs(z)))
                h = jnp.where(alive[part], soft, h)
                both.append(h)
            two = jnp.concatenate(both, axis=0)
            hid[layer, r, :] = two
            if passes:
                p_own[r, :] = two.astype(BF16)
                level = level + fold(lv * two)
            return h, level

        _, level = lax.fori_loop(0, pairs, body, (jnp.zeros((seqs, W), F32), jnp.zeros((8, W), F32)))
        if not passes:
            return None
        level = jnp.sum(level, axis=0, keepdims=True)
        levels[1:2, :] = level if m == 0 else levels[1:2, :] + level
        here = pl.ds(m * span, span)
        made = across(p_own.at[here, :], p_far.at[here, :], 18 + m)
        made.start()
        return made

    def backward_scan(layer, m, above, between=lambda: None):
        gain, shift, recur = vec_of(layer, 0), vec_of(layer, 1), vec_of(layer, 2)
        for lq in range(4):
            lanes = slice(lq * QUART, (lq + 1) * QUART)
            gq, sq, rec = gain[:, lanes], shift[:, lanes], recur[:, lanes]
            mean = coef[layer, 2 * m : 2 * m + 1, lanes]
            scale = coef[layer, 2 * m + 1 : 2 * m + 2, lanes]

            def body(i, carry):
                down, s1, s2, rsum, sqh, sqa = carry
                i = pairs - 1 - i
                start = m * span + i * (2 * seqs)
                r = pl.ds(aligned(start, 16), 2 * seqs)
                before = pl.ds(aligned(jnp.maximum(start - seqs, 0), 8), seqs)
                normed = (rows[layer, r, lanes] - mean) * scale
                drive = gq * normed + sq
                h2 = hid[layer, r, lanes]
                hb = jnp.where(i > 0, hid[layer, before, lanes], 0.0)
                lv = wide(live[r, :], 2)
                up = above[r, lanes].astype(F32)
                res = f_own[r, lanes].astype(F32)
                aux = res + h2 if layer == 1 else res
                sqh = sqh + fold(lv * (h2 * h2))
                sqa = sqa + fold(lv * (aux * aux))
                grads = [None, None]
                for k in (1, 0):
                    part = slice(k * seqs, (k + 1) * seqs)
                    prior = h2[0:seqs] if k == 1 else hb
                    slope = 0.5 + 0.5 * jnp.tanh(0.5 * (drive[part] + rec * prior))
                    total = up[part] + down
                    gd = lv[part] * slope * total
                    down = (1.0 - lv[part]) * total + rec * gd
                    grads[k] = gd
                    rsum = rsum + fold(gd * prior)
                gd2 = jnp.concatenate(grads, axis=0)
                hid[layer, r, lanes] = gd2
                return down, s1 + fold(gd2), s2 + fold(gd2 * normed), rsum, sqh, sqa

            z8 = jnp.zeros((8, QUART), F32)
            _, s1, s2, rsum, sqh, sqa = lax.fori_loop(
                0, pairs, body, (jnp.zeros((seqs, QUART), F32), z8, z8, z8, z8, z8)
            )
            for k, x in ((m, s1), (2 + m, s2)):
                tot[layer, k : k + 1, lanes] = jnp.sum(x, axis=0, keepdims=True)
            for k, x in ((4, rsum), (5, sqh), (6, sqa)):
                x = jnp.sum(x, axis=0, keepdims=True)
                tot[layer, k : k + 1, lanes] = x if m == 0 else tot[layer, k : k + 1, lanes] + x
            between()

    def backward_stats(layer, m):
        rnd, plane, _ = slim_round(3 - layer, m)
        stage_start(plane, rnd, packed(tot[layer, m : m + 1, :], tot[layer, 2 + m : 3 + m, :]))

    def backward_middle(layer, m):
        rnd, plane, line = slim_round(3 - layer, m)
        stage_wait(plane, rnd)
        stage_start(line, rnd, add_slots(plane))

    def backward_end(layer, m):
        rnd, _, line = slim_round(3 - layer, m)
        stage_wait(line, rnd)
        value = add_slots(line)
        tot[layer, m : m + 1, :] = unpacked(value[0:4])
        tot[layer, 2 + m : 3 + m, :] = unpacked(value[4:8])

    def grad_rows(layer, m, slot):
        gain = vec_of(layer, 0)
        for lh in range(2):
            lanes = slice(lh * HALF, (lh + 1) * HALF)
            mean = coef[layer, 2 * m : 2 * m + 1, lanes]
            scale = coef[layer, 2 * m + 1 : 2 * m + 2, lanes]
            count = wide(counts[m : m + 1, :], 4)
            first = tot[layer, m : m + 1, lanes] / count
            second = tot[layer, 2 + m : 3 + m, lanes] / count * scale
            k = scale * gain[:, lanes]

            def body(i, acc):
                r = pl.ds(aligned(m * span + i * (2 * seqs), 16), 2 * seqs)
                y = hid[layer, r, lanes] - first - (rows[layer, r, lanes] - mean) * second
                y = wide(live[r, :], 4) * (k * y)
                g3[0, r, lanes] = y.astype(BF16)
                return acc + fold(y)

            acc = repeat(pairs, body, jnp.zeros((8, HALF), F32), 3)
            acc = jnp.sum(acc, axis=0, keepdims=True)
            if m == 0:
                levels[4:5, lanes] = acc
            else:
                top = lax.broadcasted_iota(jnp.int32, (16, HALF), 0) == 0
                minus = jnp.where(top, -(levels[4:5, lanes] + acc), 0.0)
                g3[0, total_rows:sent_rows, lanes] = minus.astype(BF16)
        here = pl.ds(0, span) if m == 0 else pl.ds(span, span + 16)
        made = across(g3.at[0, here, :], g3.at[1, here, :], slot + m)
        made.start()
        return made

    sums_round = {1: (1, 10), 0: (0, 11)}

    def sums_start(layer):
        parity, rnd = sums_round[layer]
        own_sum = -g3[0, total_rows:sent_rows, :].astype(F32)[0:1]
        far_sum = -g3[1, total_rows:sent_rows, :].astype(F32)[0:1]
        value = jnp.concatenate([own_sum, far_sum, tot[layer, 4:7, :], jnp.zeros((3, W), F32)], axis=0)
        stage_start(in_plane(wide_p, parity), rnd, value)

    def sums_middle(layer):
        parity, rnd = sums_round[layer]
        stage_wait(in_plane(wide_p, parity), rnd)
        stage_start(in_line(wide_z, parity), rnd, add_slots(in_plane(wide_p, parity)))

    def sums_end(layer):
        parity, rnd = sums_round[layer]
        stage_wait(in_line(wide_z, parity), rnd)
        vtot[layer] = add_slots(in_line(wide_z, parity))
        tot[layer, 4:7, :] = vtot[layer, 2:5, :]
        tot[layer, 7:8, :] = wide(counts[0:1, :] + counts[1:2, :], 8)
        env["summed"].add(layer)

        @pl.when(section == layer)
        def _():
            pltpu.make_async_copy(tot.at[layer], v.at[section], v_sems.at[0]).start()

        @pl.when(section != layer)
        def _():
            v_across(layer).start()

    def v_across(layer):
        return pltpu.make_async_remote_copy(
            src_ref=tot.at[layer], dst_ref=v.at[section], send_sem=v_sems.at[1], recv_sem=v_sems.at[2],
            device_id=sibling, device_id_type=MESH,
        )

    def transpose(src, begin=0, end=W // 128):
        def body(j, _):
            c = pl.ds(aligned(j * 128, 128), 128)
            src_t[c, 0:total_rows] = src[0:total_rows, c].T
            return 0

        lax.fori_loop(begin, end, body, 0)

    def transpose_level(src, layer):
        top = lax.broadcasted_iota(jnp.int32, (16, W), 0) == 0
        src[total_rows:sent_rows, :] = jnp.where(top, levels[2 + layer : 3 + layer, :], 0.0).astype(BF16)

        def body(j, _):
            c = pl.ds(aligned(j * 128, 128), 128)
            src_t[c, total_rows:] = src[total_rows:, c].T
            level = src[total_rows:sent_rows, c].astype(F32)[0:1]
            column[layer, c, :] = jnp.broadcast_to(level, (128, 128)).T.astype(BF16)
            return 0

        lax.fori_loop(0, W // 128, body, 0)

    def weight_part(block, grads, c):
        lanes = pl.ds(c * HALF, HALF)

        def body(j, _):
            r = pl.ds(aligned(j * HALF, HALF), HALF)
            block[r, lanes] = dot(src_t[r, :], grads[:, lanes], ((1,), (0,))).astype(BF16)
            return 0

        lax.fori_loop(0, W // HALF, body, 0)

    def source_grad(store, w_own, w_far, between):
        for m in range(2):
            r = pl.ds(m * span, span)

            def body(i, _):
                c = pl.ds(aligned(i * HALF, HALF), HALF)
                y = dot(g3[0, r, :], w_own[c, :], ((1,), (1,))) + dot(g3[1, r, :], w_far[c, :], ((1,), (1,)))
                store(r, c, y)
                return 0

            lax.fori_loop(0, 2, body, 0)
            between()

    env = dict(summed=set(), vtot=vtot, column=column, space=space, ar_send=ar_send, ar_recv=ar_recv,
               ar_other=ar_other, o=o, section=section, here={"batch": b})
    xs = [a for a in bits if a["link"] == "x"]
    ys = [a for a in bits if a["link"] == "y"]
    zs = [a for a in bits if a["link"] == "z"]
    orders = (xs + ys + zs, ys + xs + zs)
    blocks = {
        (1, 0): f_far.at[pl.ds(0, W), :],
        (1, 1): p_far.at[pl.ds(0, W), :],
        (0, 0): wc.at[1, 1],
        (0, 1): wr1,
    }
    parts = {}
    for layer in (1, 0):
        for index in range(2 * PAIRS):
            part, side = index // PAIRS, index % PAIRS

            def lane_of(sec, part=part, side=side):
                return (sec if part == 0 else 1 - sec) * W + side * 2 * PART

            block = blocks[layer, part].at[:, pl.ds(side * 2 * PART, 2 * PART)]
            parts[layer, index] = Reduction(env, layer, index, block, orders, lane_of)
    order = Order()

    def weight_grads(layer, between):
        for part in range(2):
            if part == 1:
                between()
            for c in range(2):
                weight_part(blocks[layer, part], g3.at[part], c)
                order.work(2.0)
                for k in range(c * HALF // PART, (c + 1) * HALF // PART):
                    order.begin(parts[layer, part * PAIRS + k // 2], k % 2)

    def arrived(layer, sends):
        for made in sends:
            made.wait()
        sums_start(layer)

    send_f = []
    for m in range(2):
        by_units(frames, f_own, m)
        fetch(grad_out, m).start()
        if m == 0:
            wait_heads(frames, 1)
        patch_heads(f_own, m)
        here = pl.ds(m * span, span)
        made = across(f_own.at[here, :], f_far.at[here, :], (0, 24)[m])
        made.start()
        send_f.append(made)
    start_across_w(1, w_plan(1), slot_of[1])
    stage_wait(cnt_plane, 0)
    stage_start(cnt_line, 0, add_slots(cnt_plane))
    wait_w(0, w_plan(0), slot_of[0], 0)
    matmul_to(rows.at[0], f_own, wc.at[0, 0], True, 0)
    matmul_to(rows.at[0], f_own, wc.at[0, 0], True, 1)
    wait_w(0, w_plan(0), slot_of[0], 1)
    send_f[0].wait()
    matmul_to(rows.at[0], f_far, wc.at[0, 1], False, 0)
    forward_stats(0, 0)
    send_f[1].wait()

    @pl.when(section == 1)
    def _():
        heads_copy(grad_out, 2).start()

    matmul_to(rows.at[0], f_far, wc.at[0, 1], False, 1)
    forward_middle(0, 0)
    forward_stats(0, 1)
    send_vec.wait_send()
    across(vecs.at[other], vecs.at[other], 3).wait_recv()
    stage_wait(cnt_line, 0)
    counts[...] = add_slots(cnt_line)
    forward_end(0, 0)
    sends = [forward_scan(0, 0, True)]
    forward_middle(0, 1)
    by_units(grad_out, g3.at[1], 0)
    wait_heads(grad_out, 2)
    patch_heads(g3.at[1], 0)
    forward_end(0, 1)
    sends.append(forward_scan(0, 1, True))
    wait_w(1, w_plan(1), slot_of[1], 0)
    matmul_to(rows.at[1], p_own, wc.at[1, 0], True, 0)
    wait_w(1, w_plan(1), slot_of[1], 1)
    sends[0].wait()
    matmul_to(rows.at[1], p_far, wc.at[1, 1], False, 0)
    forward_stats(1, 0)
    matmul_to(rows.at[1], p_own, wc.at[1, 0], True, 1)
    forward_middle(1, 0)
    sends[1].wait()
    matmul_to(rows.at[1], p_far, wc.at[1, 1], False, 1)
    forward_stats(1, 1)
    done_w(0, w_plan(0), slot_of[0])

    start_local_w(0, late_plan, slot_of[2])
    start_across_w(0, late_plan, slot_of[2])

    @pl.when(section == 1)
    def _():
        wc[0, 1, width - late_row :, :] = jnp.zeros((W - width + late_row, W), BF16)

    def source_level():
        def body(i, acc):
            r = pl.ds(aligned(i * (2 * seqs), 16), 2 * seqs)
            return acc + fold(wide(live[r, :], 8) * f_own[r, :].astype(F32))

        acc = repeat(2 * pairs, body, jnp.zeros((8, W), F32), 3)
        levels[0:1, :] = jnp.sum(acc, axis=0, keepdims=True)

    forward_end(1, 0)
    forward_scan(1, 0, False)
    forward_middle(1, 1)
    by_units(grad_out, g3.at[1], 1)
    patch_heads(g3.at[1], 1)
    source_level()
    forward_end(1, 1)
    level_plane, level_line = in_plane(wide_p, 0), in_line(wide_z, 0)
    stage_start(level_plane, 9, jnp.concatenate([levels[0:2, :], jnp.zeros((6, W), F32)], axis=0))
    forward_scan(1, 1, False)
    backward_scan(1, 0, g3.at[1])
    backward_stats(1, 0)
    stage_wait(level_plane, 9)
    stage_start(level_line, 9, add_slots(level_plane))
    backward_scan(1, 1, g3.at[1])
    backward_stats(1, 1)
    backward_middle(1, 0)
    pl.semaphore_signal(credit.at[0], inc=1, device_id=sibling, device_id_type=MESH)
    transpose(p_own, 0, W // 256)
    backward_middle(1, 1)
    backward_end(1, 0)
    pl.semaphore_wait(credit.at[0], 1)
    sends = [grad_rows(1, 0, 20)]
    transpose(p_own, W // 256)
    stage_wait(level_line, 9)
    levels[2:4, :] = (add_slots(level_line) / wide(counts[0:1, :] + counts[1:2, :], 8))[0:2]
    transpose_level(p_own, 1)
    backward_end(1, 1)
    sends.append(grad_rows(1, 1, 20))
    weight_grads(1, lambda: arrived(1, sends))
    wait_w(1, w_plan(1), slot_of[1], 2)
    done_w(1, w_plan(1), slot_of[1])

    def keep_down(r, c, y):
        p_own[r, c] = y.astype(BF16)

    source_grad(keep_down, wc.at[1, 0], wr1, lambda: order.work(3.0))
    pl.semaphore_signal(credit.at[1], inc=1, device_id=sibling, device_id_type=MESH)
    backward_scan(0, 0, p_own, lambda: order.work(0.6))
    backward_stats(0, 0)
    backward_scan(0, 1, p_own, lambda: order.work(0.6))
    backward_stats(0, 1)
    backward_middle(0, 0)
    sums_middle(1)
    transpose(f_own)
    transpose_level(f_own, 0)
    backward_middle(0, 1)
    order.work(3.0)
    backward_end(0, 0)
    pl.semaphore_wait(credit.at[1], 1)
    sends = [grad_rows(0, 0, 22)]
    backward_end(0, 1)
    sends.append(grad_rows(0, 1, 22))
    sums_end(1)
    order.work(2.0)
    weight_grads(0, lambda: arrived(0, sends))
    wait_w(0, late_plan, slot_of[2], 0)
    wait_w(0, late_plan, slot_of[2], 1)
    done_w(0, late_plan, slot_of[2])

    def keep_source(r, c, y):
        rows[0, r, c] = y

    fetch(grad_out, 0).start()
    fetch(grad_out, 1).start()
    source_grad(keep_source, wc.at[0, 0], wc.at[0, 1], lambda: order.work(3.0))
    sums_middle(0)

    def give(m):
        return pltpu.make_async_copy(staged.at[m], gf.at[m], stage_sem.at[m])

    for m in range(2):
        fetch(grad_out, m).wait()

        def finish_frames(i, _, m=m):
            straight = staged[m, pl.ds(2 * i, 2)].astype(F32).reshape(2 * seqs, half)
            y = rows[0, pl.ds(aligned(m * span + 2 * i * seqs, 8), 2 * seqs), :]
            y = jnp.where(section == 0, y[:, :half], y[:, late_shift : late_shift + half])
            staged[m, pl.ds(2 * i, 2)] = (y + straight).reshape(2, seqs, half).astype(BF16)
            return 0

        repeat(pairs, finish_frames, 0, 3)
        give(m).start()
        order.work(2.0)
    sums_end(0)
    order.drain()
    for m in range(2):
        give(m).wait()

    for layer in range(2):

        @pl.when(section == layer)
        def _(layer=layer):
            pltpu.make_async_copy(tot.at[layer], v.at[section], v_sems.at[0]).wait()
            pltpu.make_async_remote_copy(
                src_ref=tot.at[layer], dst_ref=v.at[other], send_sem=v_sems.at[1], recv_sem=v_sems.at[2],
                device_id=sibling, device_id_type=MESH,
            ).wait_recv()

        @pl.when(section != layer)
        def _(layer=layer):
            v_across(layer).wait_send()

    own_part, far_part = v[section], v[other]
    first = jnp.where(section == 0, own_part, far_part)
    second = jnp.where(section == 0, far_part, own_part)
    for row, terms in ((0, (2, 3)), (1, (0, 1)), (2, (4,))):
        for lane, x in ((0, first), (W, second)):
            total = x[terms[0] : terms[0] + 1, :]
            for k in terms[1:]:
                total = total + x[k : k + 1, :]
            vectors[row : row + 1, lane : lane + W] = total
    squares = jnp.sum(first[5:7, :] + second[5:7, :], axis=1, keepdims=True)
    root = jnp.sqrt(squares / (first[7:8, 0:1] * width))
    for k in range(2):
        vectors[3 + k : 4 + k, :] = jnp.broadcast_to(root[k : k + 1], (1, 2 * W))
    vectors[5:8, :] = jnp.zeros((3, 2 * W), F32)


def write_results(o, gf, vectors, grad_weight, grad_frames, grad_gains, grad_shifts, grad_recurs, table):
    width = grad_weight.shape[2]
    grad_weight[0] = o[...][:, :width].astype(F32)
    grad_frames[...] = gf[...]

    @pl.when(pl.program_id(0) == 0)
    def _():
        for k, out in enumerate((grad_gains, grad_shifts, grad_recurs)):
            out[...] = vectors[k : k + 1, 0:width]
        table[...] = jnp.concatenate([vectors[3:4, 0:1], vectors[4:5, 0:1]], axis=1)


def results(o, gf, vectors):
    micro, steps, seqs, half = gf.shape
    width = 2 * half
    count = W * 2 // 256
    frames = micro * steps // count
    whole = lambda shape: pl.BlockSpec(shape, lambda i: (0, 0))
    out = pl.pallas_call(
        write_results,
        grid=(count,),
        in_specs=[
            pl.BlockSpec((256, 2 * W), lambda i: (i, 0)),
            pl.BlockSpec((frames, seqs, half), lambda i: (i, 0, 0)),
            whole((8, 2 * W)),
        ],
        out_specs=(
            pl.BlockSpec((1, 256, width), lambda i: (0, i, 0)),
            pl.BlockSpec((frames, seqs, half), lambda i: (i, 0, 0)),
            whole((1, width)),
            whole((1, width)),
            whole((1, width)),
            whole((1, 2)),
        ),
        out_shape=(
            jax.ShapeDtypeStruct((1, width, width), F32),
            jax.ShapeDtypeStruct((micro * steps, seqs, half), BF16),
            jax.ShapeDtypeStruct((1, width), F32),
            jax.ShapeDtypeStruct((1, width), F32),
            jax.ShapeDtypeStruct((1, width), F32),
            jax.ShapeDtypeStruct((1, 2), F32),
        ),
        compiler_params=pltpu.CompilerParams(vmem_limit_bytes=64 * 1024 * 1024),
    )(o.reshape(2 * W, 2 * W), gf.reshape(micro * steps, seqs, half), vectors)
    return out[1].reshape(gf.shape), out[0], *out[2:]


def whole_step(dims, frames, grad_out, weights, gains, shifts, recurs, lengths, masks):
    nz, ny, nx = dims
    micro, steps, seqs, half = frames.shape
    width = 2 * half
    views = seqs // lengths.shape[1]
    rows = micro * steps * seqs
    np_ = ny * nx
    wide_rows = (rows + 16 + 127) // 128 * 128
    depth = (nx * ny * nz - 1).bit_length()
    any_ = pl.BlockSpec(memory_space=pl.ANY)
    held = pl.BlockSpec(memory_space=pltpu.VMEM)
    dma = pltpu.SemaphoreType.DMA
    return pl.pallas_call(
        functools.partial(kernel, dims, steps, seqs, views),
        out_shape=(
            jax.ShapeDtypeStruct((2, W, 2 * W), BF16),
            jax.ShapeDtypeStruct(frames.shape, BF16),
            jax.ShapeDtypeStruct((8, 2 * W), F32),
        ),
        in_specs=[any_] * 3 + [held] * 5,
        out_specs=(any_, any_, held),
        scratch_shapes=[
            pltpu.VMEM((wide_rows, W), BF16),
            pltpu.VMEM((rows, W), BF16),
            pltpu.VMEM((wide_rows, W), BF16),
            pltpu.VMEM((rows, W), BF16),
            pltpu.VMEM((2, wide_rows, W), BF16),
            pltpu.VMEM((2, 2, W, W), BF16),
            pltpu.VMEM((W, W), BF16),
            pltpu.VMEM((W, wide_rows), BF16),
            pltpu.VMEM((rows, 128), F32),
            pltpu.VMEM((128, 128), F32),
            pltpu.VMEM(frames.shape, BF16),
            pltpu.VMEM((micro, steps, seqs, 128), BF16),
            pltpu.VMEM((5, W, (width - W) % 128), BF16),
            pltpu.VMEM((2, 8, W), F32),
            pltpu.VMEM((2, 8, 2 * W), F32),
            pltpu.VMEM((2, rows, W), F32),
            pltpu.VMEM((2, rows, W), F32),
            pltpu.VMEM((2, 8, W), F32),
            pltpu.VMEM((2, 8, W), F32),
            pltpu.VMEM((2, 8, W), F32),
            pltpu.VMEM((8, W), F32),
            pltpu.VMEM((2, W, 128), BF16),
            pltpu.VMEM((8, 128), F32),
            pltpu.VMEM((1, np_, 8, 128), F32),
            pltpu.VMEM((1, nz, 8, 128), F32),
            pltpu.VMEM((4, np_, 8, QUART), F32),
            pltpu.VMEM((4, nz, 8, QUART), F32),
            pltpu.VMEM((2, np_, 8, W), F32),
            pltpu.VMEM((2, nz, 8, W), F32),
            pltpu.VMEM((2, 2 * PAIRS, W, 2 * PART), BF16),
            dma((3, 25)),
            dma((3,)),
            dma((2,)),
            pltpu.SemaphoreType.REGULAR((2,)),
            dma((12, max(np_, 2))),
            dma((12, max(np_, 2))),
            dma((12, max(nz, 2))),
            dma((12, max(nz, 2))),
            dma((2, 2 * PAIRS, 2, 2 * depth + 2)),
            dma((2, 2 * PAIRS, 2, 2 * depth + 2)),
            dma((2, 2 * PAIRS, 2, 2)),
        ],
        compiler_params=pltpu.CompilerParams(
            collective_id=0, has_side_effects=True, vmem_limit_bytes=64 * 1024 * 1024
        ),
    )(frames, grad_out, weights, gains, shifts, recurs, lengths, masks)


def shards(dims, frames, grad_out, weights, gains, shifts, recurs, lengths, masks):
    return results(*whole_step(dims, frames, grad_out, weights, gains, shifts, recurs, lengths, masks))


def solution(mesh):
    in_specs = (
        P(None, None, "batch", "section"),
        P(None, None, "batch", "section"),
        P("section", None, None),
        P("section", None),
        P("section", None),
        P("section", None),
        P(None, "batch"),
        P(None, None, "batch"),
    )
    out_specs = (
        P(None, None, "batch", "section"),
        P("section", None, None),
        P("section", None),
        P("section", None),
        P("section", None),
        P("section", None),
    )
    body = functools.partial(shards, grid_of(mesh.shape["batch"]))
    return jax.shard_map(body, mesh=mesh, in_specs=in_specs, out_specs=out_specs, check_vma=False)
```

```python
import functools

import jax
import jax.numpy as jnp
from jax import lax
from jax.experimental import pallas as pl
from jax.experimental.pallas import tpu as pltpu
from jax.sharding import PartitionSpec as P

EPS = 1e-05
W = 1024
HALF = W // 2
QUART = W // 4
PAIRS = 1
PART = W // PAIRS // 2
MESH = pl.DeviceIdType.MESH
F32 = jnp.float32
BF16 = jnp.bfloat16


def grid_of(size):
    if size == 16:
        return (4, 2, 2)
    if size == 128:
        return (8, 4, 4)
    return (size, 1, 1)


def aligned(x, k):
    return pl.multiple_of(x, k)


def wide(x, reps):
    return jnp.concatenate([x] * reps, axis=1)


def fold(x):
    rows = x.shape[0]
    total = x[0:8]
    for k in range(8, rows, 8):
        total = total + x[k : k + 8]
    return total


def repeat(count, body, init, times):
    while count % times:
        times -= 1

    def several(i, carry):
        for j in range(times):
            carry = body(i * times + j, carry)
        return carry

    return lax.fori_loop(0, count // times, several, init)


def dot(a, b, dims):
    return lax.dot_general(a, b, (dims, ((), ())), preferred_element_type=F32)


class Reduction:
    def __init__(self, env, layer, index, block, orders, lane_of):
        self.env, self.layer, self.index, self.block, self.orders = env, layer, index, block, orders
        self.lane_of = lane_of
        self.space = env["space"].at[layer, index]
        self.depth = len(orders[0])
        self.regions = [self.halves(i, order) for i, order in enumerate(orders)]
        self.step = 0
        self.waits = []
        depth = self.depth
        self.steps = [functools.partial(self.scatter, 0)]
        self.steps += [functools.partial(self.scatter, k) for k in range(1, depth)]
        self.steps += [functools.partial(self.gather, k) for k in range(depth - 1, 0, -1)]
        self.steps += [self.give, self.finish]

    def halves(self, i, order):
        row, rows, lane, lanes = 0, W, i * PART, PART
        out = [(row, rows, lane, lanes)]
        for axis in order:
            if rows > 16:
                rows //= 2
                row = row + axis["bit"] * rows
            else:
                lanes //= 2
                lane = lane + axis["bit"] * lanes
            out.append((row, rows, lane, lanes))
        return out

    @property
    def free_to_go(self):
        return self.step != self.depth or self.layer in self.env["summed"]

    @property
    def done(self):
        return self.step >= len(self.steps)

    def advance(self):
        self.sent = []
        self.steps[self.step]()
        self.step += 1
        return self.sent

    def remote(self, i, src, dst, slot, where, recv=None):
        sems = (self.layer, self.index, i, slot)
        return pltpu.make_async_remote_copy(
            src_ref=src, dst_ref=dst, send_sem=self.env["ar_send"].at[sems],
            recv_sem=self.env["ar_recv"].at[sems] if recv is None else recv, device_id=where, device_id_type=MESH,
        )

    def wait(self):
        for made, came in self.waits:
            made.wait_send()
            came.wait_recv()
        self.waits = []

    def came_at(self, i, k):
        row = sum(r[1] for r in self.regions[i][1 : k + 1])
        _, rows, _, lanes = self.regions[i][k + 1]
        return row, rows, i * PART, lanes

    def scatter(self, k):
        if k > 0:
            self.wait()
            self.add(k - 1)
        for i, order in enumerate(self.orders):
            self.scatter_part(i, k, order[k])

    def start_part(self, i):
        self.sent = []
        self.scatter_part(i, 0, self.orders[i][0])
        if i == 1:
            self.step = 1
        return self.sent

    def scatter_part(self, i, k, axis):
        row, rows, lane, lanes = self.regions[i][k]
        _, rows2, _, lanes2 = self.regions[i][k + 1]
        give_row = row + (1 - axis["bit"]) * rows2 if rows2 < rows else row
        give_lane = lane if rows2 < rows else lane + (1 - axis["bit"]) * lanes2
        src = self.block.at[pl.ds(aligned(give_row, 16), rows2), pl.ds(aligned(give_lane, 128), lanes2)]
        at, n, at_lane, n_lanes = self.came_at(i, k)
        dst = self.space.at[pl.ds(at, n), pl.ds(at_lane, n_lanes)]
        made = self.remote(i, src, dst, k, axis["partner"])
        made.start()
        self.waits.append((made, made))
        self.sent.append((axis["link"], rows2 * lanes2 * 2))

    def add(self, k, last=False):
        rows = self.regions[0][k + 1][1]
        size = min(rows, 64)
        out = []
        for i in range(2):
            row, _, lane, lanes = self.regions[i][k + 1]
            at, _, at_lane, _ = self.came_at(i, k)
            lane = aligned(lane, 128)
            extra = None
            if last:
                part = self.index // PAIRS
                first = aligned((self.index % PAIRS) * 2 * PART + lane, 128)
                extra = self.env["vtot"][self.layer, part : part + 1, pl.ds(first, lanes)]
            out.append((row, lane, lanes, at, at_lane, self.local(i, k + 1)[0], extra))

        def body(j, _):
            for row, lane, lanes, at, at_lane, home, extra in out:
                here = pl.ds(aligned(row + j * size, 16), size)
                total = self.block[here, pl.ds(lane, lanes)].astype(F32)
                total = total + self.space[pl.ds(aligned(at + j * size, 16), size), pl.ds(at_lane, lanes)].astype(F32)
                if last:
                    column = self.env["column"][self.layer, here, :].astype(F32)
                    total = total + wide(column, lanes // 128) * extra
                    to = pl.ds(aligned(home + j * size, 16), size)
                    self.space[to, pl.ds(lane, lanes)] = total.astype(BF16)
                else:
                    self.block[here, pl.ds(lane, lanes)] = total.astype(BF16)
            return 0

        lax.fori_loop(0, rows // size, body, 0)

    def local(self, i, k):
        row, rows, lane, lanes = self.regions[i][k]
        return row - self.regions[i][1][0], rows, lane, lanes

    def gather(self, k):
        self.wait()
        if k == self.depth - 1:
            self.add(k, last=True)
        for i, order in enumerate(self.orders):
            axis = order[k]
            row, rows, lane, lanes = self.local(i, k + 1)
            row0, rows0, lane0, lanes0 = self.local(i, k)
            if rows0 > rows:
                far = (row0 + (1 - axis["bit"]) * rows, rows, lane, lanes)
            else:
                far = (row, rows, lane0 + (1 - axis["bit"]) * lanes, lanes)
            refs = [
                self.space.at[pl.ds(aligned(r, 16), n), pl.ds(aligned(c, 128), w)]
                for r, n, c, w in ((row, rows, lane, lanes), far)
            ]
            made = self.remote(i, refs[0], refs[0], self.depth + k, axis["partner"])
            made.start()
            self.waits.append((made, self.remote(i, refs[1], refs[1], self.depth + k, axis["partner"])))
            self.sent.append((axis["link"], rows * lanes * 2))

    def result(self, i, bit, section):
        rows = self.regions[i][1][1]
        lane = aligned(self.lane_of(section) + i * PART, PART)
        return self.env["o"].at[section, pl.ds(aligned(bit * rows, 16), rows), pl.ds(lane, PART)]

    def gathered(self, i):
        return self.space.at[pl.ds(0, self.regions[i][1][1]), pl.ds(i * PART, PART)]

    def deliver(self, i, near, straight):
        axis, section = self.orders[i][0], self.env["section"]
        slot = 2 * self.depth + (0 if near else 1)
        recv = None if straight else self.env["ar_other"].at[self.layer, self.index, i, 0 if near else 1]
        where = dict(self.env["here"] if near else axis["partner"], section=self.layer)
        return self.remote(i, self.gathered(i), self.result(i, axis["bit"], section), slot, where, recv)

    def arrival(self, i, near, straight):
        axis, section = self.orders[i][0], self.env["section"]
        slot = 2 * self.depth + (0 if near else 1)
        recv = None if straight else self.env["ar_other"].at[self.layer, self.index, i, 0 if near else 1]
        bit = axis["bit"] if near else 1 - axis["bit"]
        frm = section if straight else 1 - section
        where = dict(self.env["here"] if near else axis["partner"], section=frm)
        return self.remote(i, self.gathered(i), self.result(i, bit, frm), slot, where, recv)

    def kept(self, i):
        sem = self.env["ar_recv"].at[self.layer, self.index, i, 2 * self.depth]
        return pltpu.make_async_copy(
            self.gathered(i), self.result(i, self.orders[i][0]["bit"], self.env["section"]), sem
        )

    def give(self):
        self.wait()

        @pl.when(self.env["section"] == self.layer)
        def _():
            for i in range(2):
                self.deliver(i, False, True).start()
                self.kept(i).start()

        @pl.when(self.env["section"] != self.layer)
        def _():
            for i in range(2):
                self.deliver(i, False, False).start()
                self.deliver(i, True, False).start()

        for i, order in enumerate(self.orders):
            self.sent.append((order[0]["link"], self.regions[i][1][1] * PART * 2))

    def finish(self):
        @pl.when(self.env["section"] == self.layer)
        def _():
            for i in range(2):
                self.kept(i).wait()
                self.deliver(i, False, True).wait_send()
                self.arrival(i, False, True).wait_recv()
                self.arrival(i, True, False).wait_recv()
                self.arrival(i, False, False).wait_recv()

        @pl.when(self.env["section"] != self.layer)
        def _():
            for i in range(2):
                self.deliver(i, False, False).wait_send()
                self.deliver(i, True, False).wait_send()


class Order:
    RATE, HOP = 70e3, 1.8

    def __init__(self):
        self.now = 0.0
        self.free = {}
        self.going = []

    def sent(self, copies):
        end = self.now
        for link, size in copies:
            self.free[link] = max(self.now, self.free.get(link, 0.0)) + size / self.RATE
            end = max(end, self.free[link])
        return end + self.HOP

    def begin(self, one, i):
        end = self.sent(one.start_part(i))
        if i == 0:
            one.due = end
        else:
            one.due = max(one.due, end)
            self.going.append(one)

    def advance(self, one):
        self.now = max(self.now, one.due) + 0.4
        one.due = self.sent(one.advance())
        if one.done:
            self.going.remove(one)

    def work(self, cost):
        self.now += cost
        while True:
            due = [x for x in self.going if x.due <= self.now and x.free_to_go]
            if not due:
                return
            self.advance(min(due, key=lambda x: x.due))

    def drain(self):
        while self.going:
            self.advance(min(self.going, key=lambda x: x.due))


def kernel(dims, steps, seqs, views, frames, grad_out, weights, gains, shifts, recurs, lengths, masks, o, gf, vectors, f_own, f_far, p_own, p_far, g3, wc, wr1, src_t, live, turn,
           staged, heads, tails, v, vecs, rows, hid, coef, tot, vtot, levels, column, counts, cnt_p, cnt_z, slim_p, slim_z,
           wide_p, wide_z, space, sems, v_sems, stage_sem, credit, pl_send, pl_recv, z_send, z_recv, ar_send, ar_recv,
           ar_other):
    nz, ny, nx = dims
    np_ = ny * nx
    span = steps * seqs
    total_rows = 2 * span
    sent_rows = total_rows + 16
    pairs = steps // 2
    section = lax.axis_index("section")
    other = 1 - section
    b = lax.axis_index("batch")
    mp = lax.rem(b, np_)
    mz = b // np_

    def at_plane(i):
        return {"batch": b - mp + i}

    def at_z(i):
        return {"batch": b + (i - mz) * np_}

    bits = []
    for link, count, stride in (("x", nx, 1), ("y", ny, nx), ("z", nz, np_)):
        while count > 1:
            bit = lax.rem(b // stride, 2)
            bits.append(dict(bit=bit, partner={"batch": b + (1 - 2 * bit) * stride}, link=link))
            count //= 2
            stride *= 2
    sibling = {"section": other}

    def local(src, dst, slot):
        return pltpu.make_async_copy(src, dst, sems.at[0, slot])

    def across(src, dst, slot):
        return pltpu.make_async_remote_copy(
            src_ref=src, dst_ref=dst, send_sem=sems.at[1, slot], recv_sem=sems.at[2, slot],
            device_id=sibling, device_id_type=MESH,
        )

    half = frames.shape[3]
    width = 2 * half
    lead = W - half
    rest = width - W
    full = rest // 128 * 128

    def fetch(source, m):
        return pltpu.make_async_copy(source.at[m], staged.at[m], stage_sem.at[m])

    def by_units(source, target, m):
        fetch(source, m).wait()

        @pl.when(section == 0)
        def _():
            pad = jnp.zeros((2 * seqs, lead), F32)

            def place(i, _):
                x = staged[m, pl.ds(2 * i, 2)].astype(F32).reshape(2 * seqs, half)
                to = pl.ds(aligned(m * span + 2 * i * seqs, 16), 2 * seqs)
                target[to, :] = jnp.concatenate([x, pad], axis=1).astype(BF16)
                return 0

            repeat(pairs, place, 0, 3)

        @pl.when(section == 1)
        def _():
            pad = jnp.zeros((2 * seqs, 2 * lead), F32)

            def place(i, _):
                x = staged[m, pl.ds(2 * i, 2)].astype(F32).reshape(2 * seqs, half)
                to = pl.ds(aligned(m * span + 2 * i * seqs, 16), 2 * seqs)
                target[to, :] = jnp.concatenate([x[:, lead:], pad], axis=1).astype(BF16)
                return 0

            repeat(pairs, place, 0, 3)

    def patch_heads(target, m):
        @pl.when(section == 0)
        def _():
            lane = lax.broadcasted_iota(jnp.int32, (2 * seqs, 128), 1)

            def place(i, _):
                to = pl.ds(aligned(m * span + 2 * i * seqs, 16), 2 * seqs)
                head = heads[m, pl.ds(2 * i, 2)].astype(F32).reshape(2 * seqs, 128)
                head = pltpu.roll(head, 128 - lead, 1)
                old = target[to, W - 128 :].astype(F32)
                target[to, W - 128 :] = jnp.where(lane < 128 - lead, old, head).astype(BF16)
                return 0

            repeat(pairs, place, 0, 3)

    def pieces(row, count, u, block, spot):
        r = pl.ds(row, count)
        to = pl.ds(0, count)
        if u == 0:
            return [(weights.at[0, r, pl.ds(0, W)], block.at[to, :])]
        return [
            (weights.at[0, r, pl.ds(W, full)], block.at[to, pl.ds(0, full)]),
            (weights.at[0, r, pl.ds(W + full, rest - full)], tails.at[spot, to, :]),
        ]

    rows_of = {0: (0, W), 1: (W, rest)}

    def w_plan(layer):
        mine, far = rows_of[layer], rows_of[1 - layer]
        plan = [
            (mine, layer, far, 1 - layer, wc.at[layer, 0], 2 * layer),
            (far, layer, mine, 1 - layer, wc.at[layer, 1], 2 * layer + 1),
        ]
        if layer == 1:
            plan.append((mine, 0, far, 1, wr1, 4))
        return plan

    late_row = (width - half) // 16 * 16
    late_shift = half - late_row
    late_plan = [
        ((0, W), 0, (late_row, width - late_row), 1, wc.at[0, 0], 0),
        ((0, W), 1, (late_row, width - late_row), 0, wc.at[0, 1], 1),
    ]
    slot_of = {0: 4, 1: 8, 2: 14}

    def local_w(plan, base, which):
        r, u, _, _, block, spot = plan[which]
        return [local(a, t, base + 2 * which + i) for i, (a, t) in enumerate(pieces(*r, u, block, spot))]

    def across_w(plan, base, which):
        _, _, r, u, block, spot = plan[which]
        return [across(a, t, base + 2 * which + i) for i, (a, t) in enumerate(pieces(*r, u, block, spot))]

    def start_local_w(layer, plan, base):
        @pl.when(section == layer)
        def _():
            for which in range(len(plan)):
                for made in local_w(plan, base, which):
                    made.start()

    def start_across_w(layer, plan, base):
        @pl.when(section == layer)
        def _():
            for which in range(len(plan)):
                for made in across_w(plan, base, which):
                    made.start()

    def last_units(block, spot):
        def body(i, _):
            r = pl.ds(aligned(i * 128, 128), 128)
            x = tails[spot, r, :].astype(F32)
            x = jnp.concatenate([x, jnp.zeros((128, 128 - x.shape[1]), F32)], axis=1)
            block[r, full:] = x.astype(BF16)
            return 0

        lax.fori_loop(0, W // 128, body, 0)

    def wait_w(layer, plan, base, which):
        _, own_u, _, far_u, block, spot = plan[which]

        @pl.when(section == layer)
        def _():
            for made in local_w(plan, base, which):
                made.wait()
            if own_u == 1:
                last_units(block, spot)

        @pl.when(section != layer)
        def _():
            for made in across_w(plan, base, which):
                made.wait_recv()
            if far_u == 1:
                last_units(block, spot)

    def done_w(layer, plan, base):
        @pl.when(section == layer)
        def _():
            for which in range(len(plan)):
                for made in across_w(plan, base, which):
                    made.wait_send()

    def heads_copy(source, slot):
        return across(source.at[:, :, :, pl.ds(0, 128)], heads, slot)

    def wait_heads(source, slot):
        @pl.when(section == 0)
        def _():
            heads_copy(source, slot).wait_recv()

        @pl.when(section == 1)
        def _():
            heads_copy(source, slot).wait_send()

    fetch(frames, 0).start()
    fetch(frames, 1).start()
    for layer in range(2):
        start_local_w(layer, w_plan(layer), slot_of[layer])

    barrier = pltpu.get_barrier_semaphore()
    greeted = [dict(sibling)]
    greeted += [at_plane(lax.rem(mp + k, np_)) for k in range(1, np_)]
    greeted += [at_z(lax.rem(mz + k, nz)) for k in range(1, nz)]
    greeted += [dict(axis["partner"], section=other) for axis in bits]
    for where in greeted:
        pl.semaphore_signal(barrier, inc=1, device_id=where, device_id_type=MESH)

    for k, (x, fill) in enumerate(((gains, 0.0), (shifts, -1e30), (recurs, 0.0))):
        vecs[section, k : k + 1, 0:width] = x[...]
        vecs[section, k : k + 1, width:] = jnp.full((1, 2 * W - width), fill, F32)
    vecs[section, 3:8, :] = jnp.zeros((5, 2 * W), F32)

    gap = jnp.zeros((W - rest, W), BF16)

    @pl.when(section == 0)
    def _():
        wc[0, 1, rest:, :] = gap
        wc[1, 1, rest:, :] = gap

    @pl.when(section == 1)
    def _():
        wc[0, 0, rest:, :] = gap
        wc[1, 0, rest:, :] = gap
        wr1[rest:, :] = gap

    for spot in (0, 2):
        tails[spot, rest:, :] = jnp.zeros((W - rest, rest - full), BF16)
    for spare in (f_own, p_own, g3.at[0], g3.at[1]):
        spare[sent_rows:, :] = jnp.zeros((spare.shape[0] - sent_rows, W), BF16)

    pl.semaphore_wait(barrier, len(greeted))

    @pl.when(section == 1)
    def _():
        heads_copy(frames, 1).start()

    start_across_w(0, w_plan(0), slot_of[0])
    send_vec = across(vecs.at[section], vecs.at[section], 3)
    send_vec.start()

    def stage_copy(where, rnd, slot, k, back):
        buf, parity, size, me, at, send, recv = where
        there = at(lax.rem(me + (size - k if back else k), size))
        ref = buf.at[parity, slot]
        return pltpu.make_async_remote_copy(
            src_ref=ref, dst_ref=ref, send_sem=send.at[rnd, k], recv_sem=recv.at[rnd, k],
            device_id=there, device_id_type=MESH,
        )

    def in_plane(buf, parity):
        return (buf, parity, np_, mp, at_plane, pl_send, pl_recv)

    def in_line(buf, parity):
        return (buf, parity, nz, mz, at_z, z_send, z_recv)

    def stage_start(where, rnd, value):
        buf, parity, size, me = where[:4]
        buf[parity, me] = value
        for k in range(1, size):
            stage_copy(where, rnd, me, k, False).start()

    def stage_wait(where, rnd):
        size, me = where[2:4]
        for k in range(1, size):
            stage_copy(where, rnd, me, k, False).wait_send()
            stage_copy(where, rnd, lax.rem(me + size - k, size), k, True).wait_recv()

    def add_slots(where):
        buf, parity, size = where[:3]
        total = buf[parity, 0]
        for k in range(1, size):
            total = total + buf[parity, k]
        return total

    groups = lengths.shape[1]
    s_at = lax.broadcasted_iota(jnp.int32, (seqs, groups), 0)
    g_at = lax.broadcasted_iota(jnp.int32, (seqs, groups), 1) * views
    there = (s_at >= g_at) & (s_at < g_at + views)
    position = lax.broadcasted_iota(jnp.int32, (seqs, 128), 1)
    local_counts = []
    for m in range(2):
        turn[...] = jnp.zeros_like(turn)
        turn[0:steps, 0:seqs] = masks[m].astype(F32)
        mask = turn[...].T[0:seqs]
        length = jnp.broadcast_to(lengths[m : m + 1, :], (seqs, groups)).astype(F32)
        limit = jnp.sum(jnp.where(there, length, 0.0), axis=1, keepdims=True)
        alive = (position.astype(F32) < limit) & ((mask > 0.0) | (position == 0))
        alive = jnp.where(position < steps, alive.astype(F32), 0.0)
        total = jnp.zeros((seqs, 128), F32)
        for t in range(steps):
            at = m * span + t * seqs
            cells = jnp.broadcast_to(alive[:, t : t + 1], (seqs, 128))
            live[at : at + seqs, :] = cells
            total = total + cells
        local_counts.append(jnp.sum(total, axis=0, keepdims=True))
    n_own = jnp.concatenate(local_counts * 4, axis=0)

    cnt_plane, cnt_line = in_plane(cnt_p, 0), in_line(cnt_z, 0)
    stage_start(cnt_plane, 0, n_own)

    def vec_of(layer, k):
        return vecs[layer, k : k + 1, pl.ds(aligned(section * W, W), W)]

    def matmul_to(out, a, w, first, m):
        r = pl.ds(m * span, span)

        def body(i, _):
            c = pl.ds(aligned(i * HALF, HALF), HALF)
            y = dot(a[r, :], w[:, c], ((1,), (0,)))
            out[r, c] = y if first else out[r, c] + y
            return 0

        lax.fori_loop(0, 2, body, 0)

    def packed(x, y):
        return jnp.concatenate([z[:, k * QUART : (k + 1) * QUART] for z in (x, y) for k in range(4)], axis=0)

    def unpacked(x):
        return jnp.concatenate([x[k : k + 1] for k in range(4)], axis=1)

    def merge_slots(where, counts_of):
        buf, parity, size = where[:3]
        s = [buf[parity, k, 0:4, :] for k in range(size)]
        q = [buf[parity, k, 4:8, :] for k in range(size)]
        n = [wide(counts_of(k), 2) for k in range(size)]
        total, squares, count = sum(s[1:], s[0]), sum(q[1:], q[0]), sum(n[1:], n[0])
        mean = total / count
        for k in range(size):
            d = s[k] / n[k] - mean
            squares = squares + n[k] * d * d
        return jnp.concatenate([total, squares], axis=0)

    def slim_round(which, m):
        return 1 + 2 * which + m, in_plane(slim_p, 2 * m + which % 2), in_line(slim_z, 2 * m + which % 2)

    def forward_stats(layer, m):
        start = jnp.sum(rows[layer, m * span : m * span + seqs, :], axis=0, keepdims=True) * (1.0 / seqs)

        def body(i, carry):
            s, q = carry
            r = pl.ds(aligned(m * span + i * (2 * seqs), 16), 2 * seqs)
            d = rows[layer, r, :] - start
            kept = wide(live[r, :], 8) * d
            return s + fold(kept), q + fold(kept * d)

        zero = jnp.zeros((8, W), F32)
        s, q = repeat(pairs, body, (zero, zero), 3)
        s, q = jnp.sum(s, axis=0, keepdims=True), jnp.sum(q, axis=0, keepdims=True)
        n = wide(local_counts[m], 8)
        rnd, plane, _ = slim_round(layer, m)
        stage_start(plane, rnd, packed(s + n * start, jnp.maximum(q - s * s / n, 0.0)))

    def forward_middle(layer, m):
        rnd, plane, line = slim_round(layer, m)
        stage_wait(plane, rnd)
        stage_start(line, rnd, merge_slots(plane, lambda k: cnt_p[0, k, m : m + 1, :]))

    def forward_end(layer, m):
        rnd, _, line = slim_round(layer, m)
        stage_wait(line, rnd)
        value = merge_slots(line, lambda k: cnt_z[0, k, m : m + 1, :])
        count = wide(counts[m : m + 1, :], 8)
        mean = unpacked(value[0:4]) / count
        scale = lax.rsqrt(unpacked(value[4:8]) / count + EPS)
        coef[layer, 2 * m : 2 * m + 1, :] = mean
        coef[layer, 2 * m + 1 : 2 * m + 2, :] = scale
        slope = vec_of(layer, 0) * scale
        coef[layer, 4 + 2 * m : 5 + 2 * m, :] = slope
        coef[layer, 5 + 2 * m : 6 + 2 * m, :] = vec_of(layer, 1) - mean * slope

    def forward_scan(layer, m, passes):
        rec = vec_of(layer, 2)
        slope = coef[layer, 4 + 2 * m : 5 + 2 * m, :]
        shift = coef[layer, 5 + 2 * m : 6 + 2 * m, :]

        def body(i, carry):
            h, level = carry
            r = pl.ds(aligned(m * span + i * (2 * seqs), 16), 2 * seqs)
            x = rows[layer, r, :] * slope + shift
            lv = wide(live[r, :], 8)
            alive = lv > 0.0
            both = []
            for k in range(2):
                part = slice(k * seqs, (k + 1) * seqs)
                z = x[part] + rec * h
                soft = jnp.maximum(z, 0.0) + jnp.log(1.0 + jnp.exp(-jnp.abs(z)))
                h = jnp.where(alive[part], soft, h)
                both.append(h)
            two = jnp.concatenate(both, axis=0)
            hid[layer, r, :] = two
            if passes:
                p_own[r, :] = two.astype(BF16)
                level = level + fold(lv * two)
            return h, level

        _, level = lax.fori_loop(0, pairs, body, (jnp.zeros((seqs, W), F32), jnp.zeros((8, W), F32)))
        if not passes:
            return None
        level = jnp.sum(level, axis=0, keepdims=True)
        levels[1:2, :] = level if m == 0 else levels[1:2, :] + level
        here = pl.ds(m * span, span)
        made = across(p_own.at[here, :], p_far.at[here, :], 18 + m)
        made.start()
        return made

    def backward_scan(layer, m, above, between=lambda: None):
        gain, shift, recur = vec_of(layer, 0), vec_of(layer, 1), vec_of(layer, 2)
        for lq in range(4):
            lanes = slice(lq * QUART, (lq + 1) * QUART)
            gq, sq, rec = gain[:, lanes], shift[:, lanes], recur[:, lanes]
            mean = coef[layer, 2 * m : 2 * m + 1, lanes]
            scale = coef[layer, 2 * m + 1 : 2 * m + 2, lanes]

            def body(i, carry):
                down, s1, s2, rsum, sqh, sqa = carry
                i = pairs - 1 - i
                start = m * span + i * (2 * seqs)
                r = pl.ds(aligned(start, 16), 2 * seqs)
                before = pl.ds(aligned(jnp.maximum(start - seqs, 0), 8), seqs)
                normed = (rows[layer, r, lanes] - mean) * scale
                drive = gq * normed + sq
                h2 = hid[layer, r, lanes]
                hb = jnp.where(i > 0, hid[layer, before, lanes], 0.0)
                lv = wide(live[r, :], 2)
                up = above[r, lanes].astype(F32)
                res = f_own[r, lanes].astype(F32)
                aux = res + h2 if layer == 1 else res
                sqh = sqh + fold(lv * (h2 * h2))
                sqa = sqa + fold(lv * (aux * aux))
                grads = [None, None]
                for k in (1, 0):
                    part = slice(k * seqs, (k + 1) * seqs)
                    prior = h2[0:seqs] if k == 1 else hb
                    slope = 0.5 + 0.5 * jnp.tanh(0.5 * (drive[part] + rec * prior))
                    total = up[part] + down
                    gd = lv[part] * slope * total
                    down = (1.0 - lv[part]) * total + rec * gd
                    grads[k] = gd
                    rsum = rsum + fold(gd * prior)
                gd2 = jnp.concatenate(grads, axis=0)
                hid[layer, r, lanes] = gd2
                return down, s1 + fold(gd2), s2 + fold(gd2 * normed), rsum, sqh, sqa

            z8 = jnp.zeros((8, QUART), F32)
            _, s1, s2, rsum, sqh, sqa = lax.fori_loop(
                0, pairs, body, (jnp.zeros((seqs, QUART), F32), z8, z8, z8, z8, z8)
            )
            for k, x in ((m, s1), (2 + m, s2)):
                tot[layer, k : k + 1, lanes] = jnp.sum(x, axis=0, keepdims=True)
            for k, x in ((4, rsum), (5, sqh), (6, sqa)):
                x = jnp.sum(x, axis=0, keepdims=True)
                tot[layer, k : k + 1, lanes] = x if m == 0 else tot[layer, k : k + 1, lanes] + x
            between()

    def backward_stats(layer, m):
        rnd, plane, _ = slim_round(3 - layer, m)
        stage_start(plane, rnd, packed(tot[layer, m : m + 1, :], tot[layer, 2 + m : 3 + m, :]))

    def backward_middle(layer, m):
        rnd, plane, line = slim_round(3 - layer, m)
        stage_wait(plane, rnd)
        stage_start(line, rnd, add_slots(plane))

    def backward_end(layer, m):
        rnd, _, line = slim_round(3 - layer, m)
        stage_wait(line, rnd)
        value = add_slots(line)
        tot[layer, m : m + 1, :] = unpacked(value[0:4])
        tot[layer, 2 + m : 3 + m, :] = unpacked(value[4:8])

    def grad_rows(layer, m, slot):
        gain = vec_of(layer, 0)
        for lh in range(2):
            lanes = slice(lh * HALF, (lh + 1) * HALF)
            mean = coef[layer, 2 * m : 2 * m + 1, lanes]
            scale = coef[layer, 2 * m + 1 : 2 * m + 2, lanes]
            count = wide(counts[m : m + 1, :], 4)
            first = tot[layer, m : m + 1, lanes] / count
            second = tot[layer, 2 + m : 3 + m, lanes] / count * scale
            k = scale * gain[:, lanes]

            def body(i, acc):
                r = pl.ds(aligned(m * span + i * (2 * seqs), 16), 2 * seqs)
                y = hid[layer, r, lanes] - first - (rows[layer, r, lanes] - mean) * second
                y = wide(live[r, :], 4) * (k * y)
                g3[0, r, lanes] = y.astype(BF16)
                return acc + fold(y)

            acc = repeat(pairs, body, jnp.zeros((8, HALF), F32), 3)
            acc = jnp.sum(acc, axis=0, keepdims=True)
            if m == 0:
                levels[4:5, lanes] = acc
            else:
                top = lax.broadcasted_iota(jnp.int32, (16, HALF), 0) == 0
                minus = jnp.where(top, -(levels[4:5, lanes] + acc), 0.0)
                g3[0, total_rows:sent_rows, lanes] = minus.astype(BF16)
        here = pl.ds(0, span) if m == 0 else pl.ds(span, span + 16)
        made = across(g3.at[0, here, :], g3.at[1, here, :], slot + m)
        made.start()
        return made

    sums_round = {1: (1, 10), 0: (0, 11)}

    def sums_start(layer):
        parity, rnd = sums_round[layer]
        own_sum = -g3[0, total_rows:sent_rows, :].astype(F32)[0:1]
        far_sum = -g3[1, total_rows:sent_rows, :].astype(F32)[0:1]
        value = jnp.concatenate([own_sum, far_sum, tot[layer, 4:7, :], jnp.zeros((3, W), F32)], axis=0)
        stage_start(in_plane(wide_p, parity), rnd, value)

    def sums_middle(layer):
        parity, rnd = sums_round[layer]
        stage_wait(in_plane(wide_p, parity), rnd)
        stage_start(in_line(wide_z, parity), rnd, add_slots(in_plane(wide_p, parity)))

    def sums_end(layer):
        parity, rnd = sums_round[layer]
        stage_wait(in_line(wide_z, parity), rnd)
        vtot[layer] = add_slots(in_line(wide_z, parity))
        tot[layer, 4:7, :] = vtot[layer, 2:5, :]
        tot[layer, 7:8, :] = wide(counts[0:1, :] + counts[1:2, :], 8)
        env["summed"].add(layer)

        @pl.when(section == layer)
        def _():
            pltpu.make_async_copy(tot.at[layer], v.at[section], v_sems.at[0]).start()

        @pl.when(section != layer)
        def _():
            v_across(layer).start()

    def v_across(layer):
        return pltpu.make_async_remote_copy(
            src_ref=tot.at[layer], dst_ref=v.at[section], send_sem=v_sems.at[1], recv_sem=v_sems.at[2],
            device_id=sibling, device_id_type=MESH,
        )

    def transpose(src, begin=0, end=W // 128):
        def body(j, _):
            c = pl.ds(aligned(j * 128, 128), 128)
            src_t[c, 0:total_rows] = src[0:total_rows, c].T
            return 0

        lax.fori_loop(begin, end, body, 0)

    def transpose_level(src, layer):
        top = lax.broadcasted_iota(jnp.int32, (16, W), 0) == 0
        src[total_rows:sent_rows, :] = jnp.where(top, levels[2 + layer : 3 + layer, :], 0.0).astype(BF16)

        def body(j, _):
            c = pl.ds(aligned(j * 128, 128), 128)
            src_t[c, total_rows:] = src[total_rows:, c].T
            level = src[total_rows:sent_rows, c].astype(F32)[0:1]
            column[layer, c, :] = jnp.broadcast_to(level, (128, 128)).T.astype(BF16)
            return 0

        lax.fori_loop(0, W // 128, body, 0)

    def weight_part(block, grads, c):
        lanes = pl.ds(c * HALF, HALF)

        def body(j, _):
            r = pl.ds(aligned(j * HALF, HALF), HALF)
            block[r, lanes] = dot(src_t[r, :], grads[:, lanes], ((1,), (0,))).astype(BF16)
            return 0

        lax.fori_loop(0, W // HALF, body, 0)

    def source_grad(store, w_own, w_far, between):
        for m in range(2):
            r = pl.ds(m * span, span)

            def body(i, _):
                c = pl.ds(aligned(i * HALF, HALF), HALF)
                y = dot(g3[0, r, :], w_own[c, :], ((1,), (1,))) + dot(g3[1, r, :], w_far[c, :], ((1,), (1,)))
                store(r, c, y)
                return 0

            lax.fori_loop(0, 2, body, 0)
            between()

    env = dict(summed=set(), vtot=vtot, column=column, space=space, ar_send=ar_send, ar_recv=ar_recv,
               ar_other=ar_other, o=o, section=section, here={"batch": b})
    xs = [a for a in bits if a["link"] == "x"]
    ys = [a for a in bits if a["link"] == "y"]
    zs = [a for a in bits if a["link"] == "z"]
    orders = (xs + ys + zs, ys + xs + zs)
    blocks = {
        (1, 0): f_far.at[pl.ds(0, W), :],
        (1, 1): p_far.at[pl.ds(0, W), :],
        (0, 0): wc.at[1, 1],
        (0, 1): wr1,
    }
    parts = {}
    for layer in (1, 0):
        for index in range(2 * PAIRS):
            part, side = index // PAIRS, index % PAIRS

            def lane_of(sec, part=part, side=side):
                return (sec if part == 0 else 1 - sec) * W + side * 2 * PART

            block = blocks[layer, part].at[:, pl.ds(side * 2 * PART, 2 * PART)]
            parts[layer, index] = Reduction(env, layer, index, block, orders, lane_of)
    order = Order()

    def weight_grads(layer, between):
        for part in range(2):
            if part == 1:
                between()
            for c in range(2):
                weight_part(blocks[layer, part], g3.at[part], c)
                order.work(2.0)
                for k in range(c * HALF // PART, (c + 1) * HALF // PART):
                    order.begin(parts[layer, part * PAIRS + k // 2], k % 2)

    def arrived(layer, sends):
        for made in sends:
            made.wait()
        sums_start(layer)

    send_f = []
    for m in range(2):
        by_units(frames, f_own, m)
        fetch(grad_out, m).start()
        if m == 0:
            wait_heads(frames, 1)
        patch_heads(f_own, m)
        here = pl.ds(m * span, span)
        made = across(f_own.at[here, :], f_far.at[here, :], (0, 24)[m])
        made.start()
        send_f.append(made)
    start_across_w(1, w_plan(1), slot_of[1])
    stage_wait(cnt_plane, 0)
    stage_start(cnt_line, 0, add_slots(cnt_plane))
    wait_w(0, w_plan(0), slot_of[0], 0)
    matmul_to(rows.at[0], f_own, wc.at[0, 0], True, 0)
    matmul_to(rows.at[0], f_own, wc.at[0, 0], True, 1)
    wait_w(0, w_plan(0), slot_of[0], 1)
    send_f[0].wait()
    matmul_to(rows.at[0], f_far, wc.at[0, 1], False, 0)
    forward_stats(0, 0)
    send_f[1].wait()

    @pl.when(section == 1)
    def _():
        heads_copy(grad_out, 2).start()

    matmul_to(rows.at[0], f_far, wc.at[0, 1], False, 1)
    forward_middle(0, 0)
    forward_stats(0, 1)
    send_vec.wait_send()
    across(vecs.at[other], vecs.at[other], 3).wait_recv()
    stage_wait(cnt_line, 0)
    counts[...] = add_slots(cnt_line)
    forward_end(0, 0)
    sends = [forward_scan(0, 0, True)]
    forward_middle(0, 1)
    by_units(grad_out, g3.at[1], 0)
    wait_heads(grad_out, 2)
    patch_heads(g3.at[1], 0)
    forward_end(0, 1)
    sends.append(forward_scan(0, 1, True))
    wait_w(1, w_plan(1), slot_of[1], 0)
    matmul_to(rows.at[1], p_own, wc.at[1, 0], True, 0)
    wait_w(1, w_plan(1), slot_of[1], 1)
    sends[0].wait()
    matmul_to(rows.at[1], p_far, wc.at[1, 1], False, 0)
    forward_stats(1, 0)
    matmul_to(rows.at[1], p_own, wc.at[1, 0], True, 1)
    forward_middle(1, 0)
    sends[1].wait()
    matmul_to(rows.at[1], p_far, wc.at[1, 1], False, 1)
    forward_stats(1, 1)
    done_w(0, w_plan(0), slot_of[0])

    start_local_w(0, late_plan, slot_of[2])
    start_across_w(0, late_plan, slot_of[2])

    @pl.when(section == 1)
    def _():
        wc[0, 1, width - late_row :, :] = jnp.zeros((W - width + late_row, W), BF16)

    def source_level():
        def body(i, acc):
            r = pl.ds(aligned(i * (2 * seqs), 16), 2 * seqs)
            return acc + fold(wide(live[r, :], 8) * f_own[r, :].astype(F32))

        acc = repeat(2 * pairs, body, jnp.zeros((8, W), F32), 3)
        levels[0:1, :] = jnp.sum(acc, axis=0, keepdims=True)

    forward_end(1, 0)
    forward_scan(1, 0, False)
    forward_middle(1, 1)
    by_units(grad_out, g3.at[1], 1)
    patch_heads(g3.at[1], 1)
    source_level()
    forward_end(1, 1)
    level_plane, level_line = in_plane(wide_p, 0), in_line(wide_z, 0)
    stage_start(level_plane, 9, jnp.concatenate([levels[0:2, :], jnp.zeros((6, W), F32)], axis=0))
    forward_scan(1, 1, False)
    backward_scan(1, 0, g3.at[1])
    backward_stats(1, 0)
    stage_wait(level_plane, 9)
    stage_start(level_line, 9, add_slots(level_plane))
    backward_scan(1, 1, g3.at[1])
    backward_stats(1, 1)
    backward_middle(1, 0)
    pl.semaphore_signal(credit.at[0], inc=1, device_id=sibling, device_id_type=MESH)
    transpose(p_own, 0, W // 256)
    backward_middle(1, 1)
    backward_end(1, 0)
    pl.semaphore_wait(credit.at[0], 1)
    sends = [grad_rows(1, 0, 20)]
    transpose(p_own, W // 256)
    stage_wait(level_line, 9)
    levels[2:4, :] = (add_slots(level_line) / wide(counts[0:1, :] + counts[1:2, :], 8))[0:2]
    transpose_level(p_own, 1)
    backward_end(1, 1)
    sends.append(grad_rows(1, 1, 20))
    weight_grads(1, lambda: arrived(1, sends))
    wait_w(1, w_plan(1), slot_of[1], 2)
    done_w(1, w_plan(1), slot_of[1])

    def keep_down(r, c, y):
        p_own[r, c] = y.astype(BF16)

    def first_half(layer, state):
        order.work(3.0)
        if not state:
            sums_middle(layer)
            state.append(layer)

    source_grad(keep_down, wc.at[1, 0], wr1, functools.partial(first_half, 1, []))
    pl.semaphore_signal(credit.at[1], inc=1, device_id=sibling, device_id_type=MESH)
    backward_scan(0, 0, p_own, lambda: order.work(0.6))
    backward_stats(0, 0)
    sums_end(1)
    backward_scan(0, 1, p_own, lambda: order.work(0.6))
    backward_stats(0, 1)
    backward_middle(0, 0)
    transpose(f_own)
    transpose_level(f_own, 0)
    backward_middle(0, 1)
    order.work(3.0)
    backward_end(0, 0)
    pl.semaphore_wait(credit.at[1], 1)
    sends = [grad_rows(0, 0, 22)]
    backward_end(0, 1)
    sends.append(grad_rows(0, 1, 22))
    order.work(2.0)
    weight_grads(0, lambda: arrived(0, sends))
    wait_w(0, late_plan, slot_of[2], 0)
    wait_w(0, late_plan, slot_of[2], 1)
    done_w(0, late_plan, slot_of[2])

    def keep_source(r, c, y):
        rows[0, r, c] = y

    fetch(grad_out, 0).start()
    fetch(grad_out, 1).start()
    sums_middle(0)
    source_grad(keep_source, wc.at[0, 0], wc.at[0, 1], lambda: order.work(3.0))
    sums_end(0)

    def give(m):
        return pltpu.make_async_copy(staged.at[m], gf.at[m], stage_sem.at[m])

    for m in range(2):
        fetch(grad_out, m).wait()

        def finish_frames(i, _, m=m):
            straight = staged[m, pl.ds(2 * i, 2)].astype(F32).reshape(2 * seqs, half)
            y = rows[0, pl.ds(aligned(m * span + 2 * i * seqs, 8), 2 * seqs), :]
            y = jnp.where(section == 0, y[:, :half], y[:, late_shift : late_shift + half])
            staged[m, pl.ds(2 * i, 2)] = (y + straight).reshape(2, seqs, half).astype(BF16)
            return 0

        repeat(pairs, finish_frames, 0, 3)
        give(m).start()
        order.work(2.0)
    order.drain()
    for m in range(2):
        give(m).wait()

    for layer in range(2):

        @pl.when(section == layer)
        def _(layer=layer):
            pltpu.make_async_copy(tot.at[layer], v.at[section], v_sems.at[0]).wait()
            pltpu.make_async_remote_copy(
                src_ref=tot.at[layer], dst_ref=v.at[other], send_sem=v_sems.at[1], recv_sem=v_sems.at[2],
                device_id=sibling, device_id_type=MESH,
            ).wait_recv()

        @pl.when(section != layer)
        def _(layer=layer):
            v_across(layer).wait_send()

    own_part, far_part = v[section], v[other]
    first = jnp.where(section == 0, own_part, far_part)
    second = jnp.where(section == 0, far_part, own_part)
    for row, terms in ((0, (2, 3)), (1, (0, 1)), (2, (4,))):
        for lane, x in ((0, first), (W, second)):
            total = x[terms[0] : terms[0] + 1, :]
            for k in terms[1:]:
                total = total + x[k : k + 1, :]
            vectors[row : row + 1, lane : lane + W] = total
    squares = jnp.sum(first[5:7, :] + second[5:7, :], axis=1, keepdims=True)
    root = jnp.sqrt(squares / (first[7:8, 0:1] * width))
    for k in range(2):
        vectors[3 + k : 4 + k, :] = jnp.broadcast_to(root[k : k + 1], (1, 2 * W))
    vectors[5:8, :] = jnp.zeros((3, 2 * W), F32)


def write_results(o, gf, vectors, grad_weight, grad_frames, grad_gains, grad_shifts, grad_recurs, table):
    width = grad_weight.shape[2]
    grad_weight[0] = o[...][:, :width].astype(F32)
    grad_frames[...] = gf[...]

    @pl.when(pl.program_id(0) == 0)
    def _():
        for k, out in enumerate((grad_gains, grad_shifts, grad_recurs)):
            out[...] = vectors[k : k + 1, 0:width]
        table[...] = jnp.concatenate([vectors[3:4, 0:1], vectors[4:5, 0:1]], axis=1)


def results(o, gf, vectors):
    micro, steps, seqs, half = gf.shape
    width = 2 * half
    count = W * 2 // 256
    frames = micro * steps // count
    whole = lambda shape: pl.BlockSpec(shape, lambda i: (0, 0))
    out = pl.pallas_call(
        write_results,
        grid=(count,),
        in_specs=[
            pl.BlockSpec((256, 2 * W), lambda i: (i, 0)),
            pl.BlockSpec((frames, seqs, half), lambda i: (i, 0, 0)),
            whole((8, 2 * W)),
        ],
        out_specs=(
            pl.BlockSpec((1, 256, width), lambda i: (0, i, 0)),
            pl.BlockSpec((frames, seqs, half), lambda i: (i, 0, 0)),
            whole((1, width)),
            whole((1, width)),
            whole((1, width)),
            whole((1, 2)),
        ),
        out_shape=(
            jax.ShapeDtypeStruct((1, width, width), F32),
            jax.ShapeDtypeStruct((micro * steps, seqs, half), BF16),
            jax.ShapeDtypeStruct((1, width), F32),
            jax.ShapeDtypeStruct((1, width), F32),
            jax.ShapeDtypeStruct((1, width), F32),
            jax.ShapeDtypeStruct((1, 2), F32),
        ),
        compiler_params=pltpu.CompilerParams(vmem_limit_bytes=64 * 1024 * 1024),
    )(o.reshape(2 * W, 2 * W), gf.reshape(micro * steps, seqs, half), vectors)
    return out[1].reshape(gf.shape), out[0], *out[2:]


def whole_step(dims, frames, grad_out, weights, gains, shifts, recurs, lengths, masks):
    nz, ny, nx = dims
    micro, steps, seqs, half = frames.shape
    width = 2 * half
    views = seqs // lengths.shape[1]
    rows = micro * steps * seqs
    np_ = ny * nx
    wide_rows = (rows + 16 + 127) // 128 * 128
    depth = (nx * ny * nz - 1).bit_length()
    any_ = pl.BlockSpec(memory_space=pl.ANY)
    held = pl.BlockSpec(memory_space=pltpu.VMEM)
    dma = pltpu.SemaphoreType.DMA
    return pl.pallas_call(
        functools.partial(kernel, dims, steps, seqs, views),
        out_shape=(
            jax.ShapeDtypeStruct((2, W, 2 * W), BF16),
            jax.ShapeDtypeStruct(frames.shape, BF16),
            jax.ShapeDtypeStruct((8, 2 * W), F32),
        ),
        in_specs=[any_] * 3 + [held] * 5,
        out_specs=(any_, any_, held),
        scratch_shapes=[
            pltpu.VMEM((wide_rows, W), BF16),
            pltpu.VMEM((rows, W), BF16),
            pltpu.VMEM((wide_rows, W), BF16),
            pltpu.VMEM((rows, W), BF16),
            pltpu.VMEM((2, wide_rows, W), BF16),
            pltpu.VMEM((2, 2, W, W), BF16),
            pltpu.VMEM((W, W), BF16),
            pltpu.VMEM((W, wide_rows), BF16),
            pltpu.VMEM((rows, 128), F32),
            pltpu.VMEM((128, 128), F32),
            pltpu.VMEM(frames.shape, BF16),
            pltpu.VMEM((micro, steps, seqs, 128), BF16),
            pltpu.VMEM((5, W, (width - W) % 128), BF16),
            pltpu.VMEM((2, 8, W), F32),
            pltpu.VMEM((2, 8, 2 * W), F32),
            pltpu.VMEM((2, rows, W), F32),
            pltpu.VMEM((2, rows, W), F32),
            pltpu.VMEM((2, 8, W), F32),
            pltpu.VMEM((2, 8, W), F32),
            pltpu.VMEM((2, 8, W), F32),
            pltpu.VMEM((8, W), F32),
            pltpu.VMEM((2, W, 128), BF16),
            pltpu.VMEM((8, 128), F32),
            pltpu.VMEM((1, np_, 8, 128), F32),
            pltpu.VMEM((1, nz, 8, 128), F32),
            pltpu.VMEM((4, np_, 8, QUART), F32),
            pltpu.VMEM((4, nz, 8, QUART), F32),
            pltpu.VMEM((2, np_, 8, W), F32),
            pltpu.VMEM((2, nz, 8, W), F32),
            pltpu.VMEM((2, 2 * PAIRS, W, 2 * PART), BF16),
            dma((3, 25)),
            dma((3,)),
            dma((2,)),
            pltpu.SemaphoreType.REGULAR((2,)),
            dma((12, max(np_, 2))),
            dma((12, max(np_, 2))),
            dma((12, max(nz, 2))),
            dma((12, max(nz, 2))),
            dma((2, 2 * PAIRS, 2, 2 * depth + 2)),
            dma((2, 2 * PAIRS, 2, 2 * depth + 2)),
            dma((2, 2 * PAIRS, 2, 2)),
        ],
        compiler_params=pltpu.CompilerParams(
            collective_id=0, has_side_effects=True, vmem_limit_bytes=64 * 1024 * 1024
        ),
    )(frames, grad_out, weights, gains, shifts, recurs, lengths, masks)


def shards(dims, frames, grad_out, weights, gains, shifts, recurs, lengths, masks):
    return results(*whole_step(dims, frames, grad_out, weights, gains, shifts, recurs, lengths, masks))


def solution(mesh):
    in_specs = (
        P(None, None, "batch", "section"),
        P(None, None, "batch", "section"),
        P("section", None, None),
        P("section", None),
        P("section", None),
        P("section", None),
        P(None, "batch"),
        P(None, None, "batch"),
    )
    out_specs = (
        P(None, None, "batch", "section"),
        P("section", None, None),
        P("section", None),
        P("section", None),
        P("section", None),
        P("section", None),
    )
    body = functools.partial(shards, grid_of(mesh.shape["batch"]))
    return jax.shard_map(body, mesh=mesh, in_specs=in_specs, out_specs=out_specs, check_vma=False)
```

```python
import functools

import jax
import jax.numpy as jnp
from jax import lax
from jax.experimental import pallas as pl
from jax.experimental.pallas import tpu as pltpu
from jax.sharding import PartitionSpec as P

EPS = 1e-05
W = 1024
HALF = W // 2
QUART = W // 4
PAIRS = 1
PART = W // PAIRS // 2
MESH = pl.DeviceIdType.MESH
F32 = jnp.float32
BF16 = jnp.bfloat16


def grid_of(size):
    if size == 16:
        return (4, 2, 2)
    if size == 128:
        return (8, 4, 4)
    return (size, 1, 1)


def aligned(x, k):
    return pl.multiple_of(x, k)


def wide(x, reps):
    return jnp.concatenate([x] * reps, axis=1)


def fold(x):
    rows = x.shape[0]
    total = x[0:8]
    for k in range(8, rows, 8):
        total = total + x[k : k + 8]
    return total


def repeat(count, body, init, times):
    while count % times:
        times -= 1

    def several(i, carry):
        for j in range(times):
            carry = body(i * times + j, carry)
        return carry

    return lax.fori_loop(0, count // times, several, init)


def dot(a, b, dims):
    return lax.dot_general(a, b, (dims, ((), ())), preferred_element_type=F32)


class Reduction:
    def __init__(self, env, layer, index, block, orders, lane_of):
        self.env, self.layer, self.index, self.block, self.orders = env, layer, index, block, orders
        self.lane_of = lane_of
        self.space = env["space"].at[layer, index]
        self.depth = len(orders[0])
        self.regions = [self.halves(i, order) for i, order in enumerate(orders)]
        self.step = 0
        self.waits = []
        depth = self.depth
        self.steps = [functools.partial(self.scatter, 0)]
        self.steps += [functools.partial(self.scatter, k) for k in range(1, depth)]
        self.steps += [functools.partial(self.gather, k) for k in range(depth - 1, 0, -1)]
        self.steps += [self.give, self.finish]

    def halves(self, i, order):
        row, rows, lane, lanes = 0, W, i * PART, PART
        out = [(row, rows, lane, lanes)]
        for axis in order:
            if rows > 16:
                rows //= 2
                row = row + axis["bit"] * rows
            else:
                lanes //= 2
                lane = lane + axis["bit"] * lanes
            out.append((row, rows, lane, lanes))
        return out

    @property
    def free_to_go(self):
        return self.step != self.depth or self.layer in self.env["summed"]

    @property
    def done(self):
        return self.step >= len(self.steps)

    def advance(self):
        self.sent = []
        self.steps[self.step]()
        self.step += 1
        return self.sent

    def remote(self, i, src, dst, slot, where, recv=None):
        sems = (self.layer, self.index, i, slot)
        return pltpu.make_async_remote_copy(
            src_ref=src, dst_ref=dst, send_sem=self.env["ar_send"].at[sems],
            recv_sem=self.env["ar_recv"].at[sems] if recv is None else recv, device_id=where, device_id_type=MESH,
        )

    def wait(self):
        for made, came in self.waits:
            made.wait_send()
            came.wait_recv()
        self.waits = []

    def came_at(self, i, k):
        row = sum(r[1] for r in self.regions[i][1 : k + 1])
        _, rows, _, lanes = self.regions[i][k + 1]
        return row, rows, i * PART, lanes

    def scatter(self, k):
        if k > 0:
            self.wait()
            self.add(k - 1)
        for i, order in enumerate(self.orders):
            self.scatter_part(i, k, order[k])

    def start_part(self, i):
        self.sent = []
        self.scatter_part(i, 0, self.orders[i][0])
        if i == 1:
            self.step = 1
        return self.sent

    def scatter_part(self, i, k, axis):
        row, rows, lane, lanes = self.regions[i][k]
        _, rows2, _, lanes2 = self.regions[i][k + 1]
        give_row = row + (1 - axis["bit"]) * rows2 if rows2 < rows else row
        give_lane = lane if rows2 < rows else lane + (1 - axis["bit"]) * lanes2
        src = self.block.at[pl.ds(aligned(give_row, 16), rows2), pl.ds(aligned(give_lane, 128), lanes2)]
        at, n, at_lane, n_lanes = self.came_at(i, k)
        dst = self.space.at[pl.ds(at, n), pl.ds(at_lane, n_lanes)]
        made = self.remote(i, src, dst, k, axis["partner"])
        made.start()
        self.waits.append((made, made))
        self.sent.append((axis["link"], rows2 * lanes2 * 2))

    def add(self, k, last=False):
        rows = self.regions[0][k + 1][1]
        size = min(rows, 64)
        out = []
        for i in range(2):
            row, _, lane, lanes = self.regions[i][k + 1]
            at, _, at_lane, _ = self.came_at(i, k)
            lane = aligned(lane, 128)
            extra = None
            if last:
                part = self.index // PAIRS
                first = aligned((self.index % PAIRS) * 2 * PART + lane, 128)
                extra = self.env["vtot"][self.layer, part : part + 1, pl.ds(first, lanes)]
            out.append((row, lane, lanes, at, at_lane, self.local(i, k + 1)[0], extra))

        def body(j, _):
            for row, lane, lanes, at, at_lane, home, extra in out:
                here = pl.ds(aligned(row + j * size, 16), size)
                total = self.block[here, pl.ds(lane, lanes)].astype(F32)
                total = total + self.space[pl.ds(aligned(at + j * size, 16), size), pl.ds(at_lane, lanes)].astype(F32)
                if last:
                    column = self.env["column"][self.layer, here, :].astype(F32)
                    total = total + wide(column, lanes // 128) * extra
                    to = pl.ds(aligned(home + j * size, 16), size)
                    self.space[to, pl.ds(lane, lanes)] = total.astype(BF16)
                else:
                    self.block[here, pl.ds(lane, lanes)] = total.astype(BF16)
            return 0

        lax.fori_loop(0, rows // size, body, 0)

    def local(self, i, k):
        row, rows, lane, lanes = self.regions[i][k]
        return row - self.regions[i][1][0], rows, lane, lanes

    def gather(self, k):
        self.wait()
        if k == self.depth - 1:
            self.add(k, last=True)
        for i, order in enumerate(self.orders):
            axis = order[k]
            row, rows, lane, lanes = self.local(i, k + 1)
            row0, rows0, lane0, lanes0 = self.local(i, k)
            if rows0 > rows:
                far = (row0 + (1 - axis["bit"]) * rows, rows, lane, lanes)
            else:
                far = (row, rows, lane0 + (1 - axis["bit"]) * lanes, lanes)
            refs = [
                self.space.at[pl.ds(aligned(r, 16), n), pl.ds(aligned(c, 128), w)]
                for r, n, c, w in ((row, rows, lane, lanes), far)
            ]
            made = self.remote(i, refs[0], refs[0], self.depth + k, axis["partner"])
            made.start()
            self.waits.append((made, self.remote(i, refs[1], refs[1], self.depth + k, axis["partner"])))
            self.sent.append((axis["link"], rows * lanes * 2))

    def result(self, i, bit, section):
        rows = self.regions[i][1][1]
        lane = aligned(self.lane_of(section) + i * PART, PART)
        return self.env["o"].at[section, pl.ds(aligned(bit * rows, 16), rows), pl.ds(lane, PART)]

    def gathered(self, i):
        return self.space.at[pl.ds(0, self.regions[i][1][1]), pl.ds(i * PART, PART)]

    def deliver(self, i, near, straight):
        axis, section = self.orders[i][0], self.env["section"]
        slot = 2 * self.depth + (0 if near else 1)
        recv = None if straight else self.env["ar_other"].at[self.layer, self.index, i, 0 if near else 1]
        where = dict(self.env["here"] if near else axis["partner"], section=self.layer)
        return self.remote(i, self.gathered(i), self.result(i, axis["bit"], section), slot, where, recv)

    def arrival(self, i, near, straight):
        axis, section = self.orders[i][0], self.env["section"]
        slot = 2 * self.depth + (0 if near else 1)
        recv = None if straight else self.env["ar_other"].at[self.layer, self.index, i, 0 if near else 1]
        bit = axis["bit"] if near else 1 - axis["bit"]
        frm = section if straight else 1 - section
        where = dict(self.env["here"] if near else axis["partner"], section=frm)
        return self.remote(i, self.gathered(i), self.result(i, bit, frm), slot, where, recv)

    def kept(self, i):
        sem = self.env["ar_recv"].at[self.layer, self.index, i, 2 * self.depth]
        return pltpu.make_async_copy(
            self.gathered(i), self.result(i, self.orders[i][0]["bit"], self.env["section"]), sem
        )

    def give(self):
        self.wait()

        @pl.when(self.env["section"] == self.layer)
        def _():
            for i in range(2):
                self.deliver(i, False, True).start()
                self.kept(i).start()

        @pl.when(self.env["section"] != self.layer)
        def _():
            for i in range(2):
                self.deliver(i, False, False).start()
                self.deliver(i, True, False).start()

        for i, order in enumerate(self.orders):
            self.sent.append((order[0]["link"], self.regions[i][1][1] * PART * 2))

    def finish(self):
        @pl.when(self.env["section"] == self.layer)
        def _():
            for i in range(2):
                self.kept(i).wait()
                self.deliver(i, False, True).wait_send()
                self.arrival(i, False, True).wait_recv()
                self.arrival(i, True, False).wait_recv()
                self.arrival(i, False, False).wait_recv()

        @pl.when(self.env["section"] != self.layer)
        def _():
            for i in range(2):
                self.deliver(i, False, False).wait_send()
                self.deliver(i, True, False).wait_send()


class Order:
    RATE, HOP = 70e3, 1.8

    def __init__(self):
        self.now = 0.0
        self.free = {}
        self.going = []

    def sent(self, copies):
        end = self.now
        for link, size in copies:
            self.free[link] = max(self.now, self.free.get(link, 0.0)) + size / self.RATE
            end = max(end, self.free[link])
        return end + self.HOP

    def begin(self, one, i):
        end = self.sent(one.start_part(i))
        if i == 0:
            one.due = end
        else:
            one.due = max(one.due, end)
            self.going.append(one)

    def advance(self, one):
        self.now = max(self.now, one.due) + 0.4
        one.due = self.sent(one.advance())
        if one.done:
            self.going.remove(one)

    def work(self, cost):
        self.now += cost
        while True:
            due = [x for x in self.going if x.due <= self.now and x.free_to_go]
            if not due:
                return
            self.advance(min(due, key=lambda x: x.due))

    def drain(self):
        while self.going:
            self.advance(min(self.going, key=lambda x: x.due))


def kernel(dims, steps, seqs, views, frames, grad_out, weights, gains, shifts, recurs, lengths, masks, o, gf, vectors, f_own, f_far, p_own, p_far, g3, wc, wr1, src_t, live, turn,
           staged, heads, tails, v, vecs, rows, hid, coef, tot, vtot, levels, column, counts, cnt_p, cnt_z, slim_p, slim_z,
           wide_p, wide_z, space, sems, v_sems, stage_sem, credit, pl_send, pl_recv, z_send, z_recv, ar_send, ar_recv,
           ar_other):
    nz, ny, nx = dims
    np_ = ny * nx
    span = steps * seqs
    total_rows = 2 * span
    sent_rows = total_rows + 16
    pairs = steps // 2
    section = lax.axis_index("section")
    other = 1 - section
    b = lax.axis_index("batch")
    mp = lax.rem(b, np_)
    mz = b // np_

    def at_plane(i):
        return {"batch": b - mp + i}

    def at_z(i):
        return {"batch": b + (i - mz) * np_}

    bits = []
    for link, count, stride in (("x", nx, 1), ("y", ny, nx), ("z", nz, np_)):
        while count > 1:
            bit = lax.rem(b // stride, 2)
            bits.append(dict(bit=bit, partner={"batch": b + (1 - 2 * bit) * stride}, link=link))
            count //= 2
            stride *= 2
    sibling = {"section": other}

    def local(src, dst, slot):
        return pltpu.make_async_copy(src, dst, sems.at[0, slot])

    def across(src, dst, slot):
        return pltpu.make_async_remote_copy(
            src_ref=src, dst_ref=dst, send_sem=sems.at[1, slot], recv_sem=sems.at[2, slot],
            device_id=sibling, device_id_type=MESH,
        )

    half = frames.shape[3]
    width = 2 * half
    lead = W - half
    rest = width - W
    full = rest // 128 * 128

    def fetch(source, m):
        return pltpu.make_async_copy(source.at[m], staged.at[m], stage_sem.at[m])

    def by_units(source, target, m):
        fetch(source, m).wait()

        @pl.when(section == 0)
        def _():
            pad = jnp.zeros((2 * seqs, lead), F32)

            def place(i, _):
                x = staged[m, pl.ds(2 * i, 2)].astype(F32).reshape(2 * seqs, half)
                to = pl.ds(aligned(m * span + 2 * i * seqs, 16), 2 * seqs)
                target[to, :] = jnp.concatenate([x, pad], axis=1).astype(BF16)
                return 0

            repeat(pairs, place, 0, 3)

        @pl.when(section == 1)
        def _():
            pad = jnp.zeros((2 * seqs, 2 * lead), F32)

            def place(i, _):
                x = staged[m, pl.ds(2 * i, 2)].astype(F32).reshape(2 * seqs, half)
                to = pl.ds(aligned(m * span + 2 * i * seqs, 16), 2 * seqs)
                target[to, :] = jnp.concatenate([x[:, lead:], pad], axis=1).astype(BF16)
                return 0

            repeat(pairs, place, 0, 3)

    def patch_heads(target, m):
        @pl.when(section == 0)
        def _():
            lane = lax.broadcasted_iota(jnp.int32, (2 * seqs, 128), 1)

            def place(i, _):
                to = pl.ds(aligned(m * span + 2 * i * seqs, 16), 2 * seqs)
                head = heads[m, pl.ds(2 * i, 2)].astype(F32).reshape(2 * seqs, 128)
                head = pltpu.roll(head, 128 - lead, 1)
                old = target[to, W - 128 :].astype(F32)
                target[to, W - 128 :] = jnp.where(lane < 128 - lead, old, head).astype(BF16)
                return 0

            repeat(pairs, place, 0, 3)

    def pieces(row, count, u, block, spot):
        r = pl.ds(row, count)
        to = pl.ds(0, count)
        if u == 0:
            return [(weights.at[0, r, pl.ds(0, W)], block.at[to, :])]
        return [
            (weights.at[0, r, pl.ds(W, full)], block.at[to, pl.ds(0, full)]),
            (weights.at[0, r, pl.ds(W + full, rest - full)], tails.at[spot, to, :]),
        ]

    rows_of = {0: (0, W), 1: (W, rest)}

    def w_plan(layer):
        mine, far = rows_of[layer], rows_of[1 - layer]
        plan = [
            (mine, layer, far, 1 - layer, wc.at[layer, 0], 2 * layer),
            (far, layer, mine, 1 - layer, wc.at[layer, 1], 2 * layer + 1),
        ]
        if layer == 1:
            plan.append((mine, 0, far, 1, wr1, 4))
        return plan

    late_row = (width - half) // 16 * 16
    late_shift = half - late_row
    late_plan = [
        ((0, W), 0, (late_row, width - late_row), 1, wc.at[0, 0], 0),
        ((0, W), 1, (late_row, width - late_row), 0, wc.at[0, 1], 1),
    ]
    slot_of = {0: 4, 1: 8, 2: 14}

    def local_w(plan, base, which):
        r, u, _, _, block, spot = plan[which]
        return [local(a, t, base + 2 * which + i) for i, (a, t) in enumerate(pieces(*r, u, block, spot))]

    def across_w(plan, base, which):
        _, _, r, u, block, spot = plan[which]
        return [across(a, t, base + 2 * which + i) for i, (a, t) in enumerate(pieces(*r, u, block, spot))]

    def start_local_w(layer, plan, base):
        @pl.when(section == layer)
        def _():
            for which in range(len(plan)):
                for made in local_w(plan, base, which):
                    made.start()

    def start_across_w(layer, plan, base):
        @pl.when(section == layer)
        def _():
            for which in range(len(plan)):
                for made in across_w(plan, base, which):
                    made.start()

    def last_units(block, spot):
        def body(i, _):
            r = pl.ds(aligned(i * 128, 128), 128)
            x = tails[spot, r, :].astype(F32)
            x = jnp.concatenate([x, jnp.zeros((128, 128 - x.shape[1]), F32)], axis=1)
            block[r, full:] = x.astype(BF16)
            return 0

        lax.fori_loop(0, W // 128, body, 0)

    def wait_w(layer, plan, base, which):
        _, own_u, _, far_u, block, spot = plan[which]

        @pl.when(section == layer)
        def _():
            for made in local_w(plan, base, which):
                made.wait()
            if own_u == 1:
                last_units(block, spot)

        @pl.when(section != layer)
        def _():
            for made in across_w(plan, base, which):
                made.wait_recv()
            if far_u == 1:
                last_units(block, spot)

    def done_w(layer, plan, base):
        @pl.when(section == layer)
        def _():
            for which in range(len(plan)):
                for made in across_w(plan, base, which):
                    made.wait_send()

    def heads_copy(source, slot):
        return across(source.at[:, :, :, pl.ds(0, 128)], heads, slot)

    def wait_heads(source, slot):
        @pl.when(section == 0)
        def _():
            heads_copy(source, slot).wait_recv()

        @pl.when(section == 1)
        def _():
            heads_copy(source, slot).wait_send()

    fetch(frames, 0).start()
    fetch(frames, 1).start()
    for layer in range(2):
        start_local_w(layer, w_plan(layer), slot_of[layer])

    barrier = pltpu.get_barrier_semaphore()
    greeted = [dict(sibling)]
    greeted += [at_plane(lax.rem(mp + k, np_)) for k in range(1, np_)]
    greeted += [at_z(lax.rem(mz + k, nz)) for k in range(1, nz)]
    greeted += [dict(axis["partner"], section=other) for axis in bits]
    for where in greeted:
        pl.semaphore_signal(barrier, inc=1, device_id=where, device_id_type=MESH)

    for k, (x, fill) in enumerate(((gains, 0.0), (shifts, -1e30), (recurs, 0.0))):
        vecs[section, k : k + 1, 0:width] = x[...]
        vecs[section, k : k + 1, width:] = jnp.full((1, 2 * W - width), fill, F32)
    vecs[section, 3:8, :] = jnp.zeros((5, 2 * W), F32)

    gap = jnp.zeros((W - rest, W), BF16)

    @pl.when(section == 0)
    def _():
        wc[0, 1, rest:, :] = gap
        wc[1, 1, rest:, :] = gap

    @pl.when(section == 1)
    def _():
        wc[0, 0, rest:, :] = gap
        wc[1, 0, rest:, :] = gap
        wr1[rest:, :] = gap

    for spot in (0, 2):
        tails[spot, rest:, :] = jnp.zeros((W - rest, rest - full), BF16)
    for spare in (f_own, p_own, g3.at[0], g3.at[1]):
        spare[sent_rows:, :] = jnp.zeros((spare.shape[0] - sent_rows, W), BF16)

    pl.semaphore_wait(barrier, len(greeted))

    @pl.when(section == 1)
    def _():
        heads_copy(frames, 1).start()

    start_across_w(0, w_plan(0), slot_of[0])
    send_vec = across(vecs.at[section], vecs.at[section], 3)
    send_vec.start()

    def stage_copy(where, rnd, slot, k, back):
        buf, parity, size, me, at, send, recv = where
        there = at(lax.rem(me + (size - k if back else k), size))
        ref = buf.at[parity, slot]
        return pltpu.make_async_remote_copy(
            src_ref=ref, dst_ref=ref, send_sem=send.at[rnd, k], recv_sem=recv.at[rnd, k],
            device_id=there, device_id_type=MESH,
        )

    def in_plane(buf, parity):
        return (buf, parity, np_, mp, at_plane, pl_send, pl_recv)

    def in_line(buf, parity):
        return (buf, parity, nz, mz, at_z, z_send, z_recv)

    def stage_start(where, rnd, value):
        buf, parity, size, me = where[:4]
        buf[parity, me] = value
        for k in range(1, size):
            stage_copy(where, rnd, me, k, False).start()

    def stage_wait(where, rnd):
        size, me = where[2:4]
        for k in range(1, size):
            stage_copy(where, rnd, me, k, False).wait_send()
            stage_copy(where, rnd, lax.rem(me + size - k, size), k, True).wait_recv()

    def add_slots(where):
        buf, parity, size = where[:3]
        total = buf[parity, 0]
        for k in range(1, size):
            total = total + buf[parity, k]
        return total

    groups = lengths.shape[1]
    s_at = lax.broadcasted_iota(jnp.int32, (seqs, groups), 0)
    g_at = lax.broadcasted_iota(jnp.int32, (seqs, groups), 1) * views
    there = (s_at >= g_at) & (s_at < g_at + views)
    position = lax.broadcasted_iota(jnp.int32, (seqs, 128), 1)
    local_counts = []
    for m in range(2):
        turn[...] = jnp.zeros_like(turn)
        turn[0:steps, 0:seqs] = masks[m].astype(F32)
        mask = turn[...].T[0:seqs]
        length = jnp.broadcast_to(lengths[m : m + 1, :], (seqs, groups)).astype(F32)
        limit = jnp.sum(jnp.where(there, length, 0.0), axis=1, keepdims=True)
        alive = (position.astype(F32) < limit) & ((mask > 0.0) | (position == 0))
        alive = jnp.where(position < steps, alive.astype(F32), 0.0)
        total = jnp.zeros((seqs, 128), F32)
        for t in range(steps):
            at = m * span + t * seqs
            cells = jnp.broadcast_to(alive[:, t : t + 1], (seqs, 128))
            live[at : at + seqs, :] = cells
            total = total + cells
        local_counts.append(jnp.sum(total, axis=0, keepdims=True))
    n_own = jnp.concatenate(local_counts * 4, axis=0)

    cnt_plane, cnt_line = in_plane(cnt_p, 0), in_line(cnt_z, 0)
    stage_start(cnt_plane, 0, n_own)

    def vec_of(layer, k):
        return vecs[layer, k : k + 1, pl.ds(aligned(section * W, W), W)]

    def matmul_to(out, a, w, first, m):
        r = pl.ds(m * span, span)

        def body(i, _):
            c = pl.ds(aligned(i * HALF, HALF), HALF)
            y = dot(a[r, :], w[:, c], ((1,), (0,)))
            out[r, c] = y if first else out[r, c] + y
            return 0

        lax.fori_loop(0, 2, body, 0)

    def packed(x, y):
        return jnp.concatenate([z[:, k * QUART : (k + 1) * QUART] for z in (x, y) for k in range(4)], axis=0)

    def unpacked(x):
        return jnp.concatenate([x[k : k + 1] for k in range(4)], axis=1)

    def merge_slots(where, counts_of):
        buf, parity, size = where[:3]
        s = [buf[parity, k, 0:4, :] for k in range(size)]
        q = [buf[parity, k, 4:8, :] for k in range(size)]
        n = [wide(counts_of(k), 2) for k in range(size)]
        total, squares, count = sum(s[1:], s[0]), sum(q[1:], q[0]), sum(n[1:], n[0])
        mean = total / count
        for k in range(size):
            d = s[k] / n[k] - mean
            squares = squares + n[k] * d * d
        return jnp.concatenate([total, squares], axis=0)

    def slim_round(which, m):
        return 1 + 2 * which + m, in_plane(slim_p, 2 * m + which % 2), in_line(slim_z, 2 * m + which % 2)

    def forward_stats(layer, m):
        start = jnp.sum(rows[layer, m * span : m * span + seqs, :], axis=0, keepdims=True) * (1.0 / seqs)

        def body(i, carry):
            s, q = carry
            r = pl.ds(aligned(m * span + i * (2 * seqs), 16), 2 * seqs)
            d = rows[layer, r, :] - start
            kept = wide(live[r, :], 8) * d
            return s + fold(kept), q + fold(kept * d)

        zero = jnp.zeros((8, W), F32)
        s, q = repeat(pairs, body, (zero, zero), 3)
        s, q = jnp.sum(s, axis=0, keepdims=True), jnp.sum(q, axis=0, keepdims=True)
        n = wide(local_counts[m], 8)
        rnd, plane, _ = slim_round(layer, m)
        stage_start(plane, rnd, packed(s + n * start, jnp.maximum(q - s * s / n, 0.0)))

    def forward_middle(layer, m):
        rnd, plane, line = slim_round(layer, m)
        stage_wait(plane, rnd)
        stage_start(line, rnd, merge_slots(plane, lambda k: cnt_p[0, k, m : m + 1, :]))

    def forward_end(layer, m):
        rnd, _, line = slim_round(layer, m)
        stage_wait(line, rnd)
        value = merge_slots(line, lambda k: cnt_z[0, k, m : m + 1, :])
        count = wide(counts[m : m + 1, :], 8)
        mean = unpacked(value[0:4]) / count
        scale = lax.rsqrt(unpacked(value[4:8]) / count + EPS)
        coef[layer, 2 * m : 2 * m + 1, :] = mean
        coef[layer, 2 * m + 1 : 2 * m + 2, :] = scale
        slope = vec_of(layer, 0) * scale
        coef[layer, 4 + 2 * m : 5 + 2 * m, :] = slope
        coef[layer, 5 + 2 * m : 6 + 2 * m, :] = vec_of(layer, 1) - mean * slope

    def forward_scan(layer, m, passes):
        rec = vec_of(layer, 2)
        slope = coef[layer, 4 + 2 * m : 5 + 2 * m, :]
        shift = coef[layer, 5 + 2 * m : 6 + 2 * m, :]

        def body(i, carry):
            h, level = carry
            r = pl.ds(aligned(m * span + i * (2 * seqs), 16), 2 * seqs)
            x = rows[layer, r, :] * slope + shift
            lv = wide(live[r, :], 8)
            alive = lv > 0.0
            both = []
            for k in range(2):
                part = slice(k * seqs, (k + 1) * seqs)
                z = x[part] + rec * h
                soft = jnp.maximum(z, 0.0) + jnp.log(1.0 + jnp.exp(-jnp.abs(z)))
                h = jnp.where(alive[part], soft, h)
                both.append(h)
            two = jnp.concatenate(both, axis=0)
            hid[layer, r, :] = two
            if passes:
                p_own[r, :] = two.astype(BF16)
                level = level + fold(lv * two)
            return h, level

        _, level = lax.fori_loop(0, pairs, body, (jnp.zeros((seqs, W), F32), jnp.zeros((8, W), F32)))
        if not passes:
            return None
        level = jnp.sum(level, axis=0, keepdims=True)
        levels[1:2, :] = level if m == 0 else levels[1:2, :] + level
        here = pl.ds(m * span, span)
        made = across(p_own.at[here, :], p_far.at[here, :], 18 + m)
        made.start()
        return made

    def backward_scan(layer, m, above, between=lambda: None):
        gain, shift, recur = vec_of(layer, 0), vec_of(layer, 1), vec_of(layer, 2)
        for lq in range(4):
            lanes = slice(lq * QUART, (lq + 1) * QUART)
            gq, sq, rec = gain[:, lanes], shift[:, lanes], recur[:, lanes]
            mean = coef[layer, 2 * m : 2 * m + 1, lanes]
            scale = coef[layer, 2 * m + 1 : 2 * m + 2, lanes]

            def body(i, carry):
                down, s1, s2, rsum, sqh, sqa = carry
                i = pairs - 1 - i
                start = m * span + i * (2 * seqs)
                r = pl.ds(aligned(start, 16), 2 * seqs)
                before = pl.ds(aligned(jnp.maximum(start - seqs, 0), 8), seqs)
                normed = (rows[layer, r, lanes] - mean) * scale
                drive = gq * normed + sq
                h2 = hid[layer, r, lanes]
                hb = jnp.where(i > 0, hid[layer, before, lanes], 0.0)
                lv = wide(live[r, :], 2)
                up = above[r, lanes].astype(F32)
                res = f_own[r, lanes].astype(F32)
                aux = res + h2 if layer == 1 else res
                sqh = sqh + fold(lv * (h2 * h2))
                sqa = sqa + fold(lv * (aux * aux))
                grads = [None, None]
                for k in (1, 0):
                    part = slice(k * seqs, (k + 1) * seqs)
                    prior = h2[0:seqs] if k == 1 else hb
                    slope = 0.5 + 0.5 * jnp.tanh(0.5 * (drive[part] + rec * prior))
                    total = up[part] + down
                    gd = lv[part] * slope * total
                    down = (1.0 - lv[part]) * total + rec * gd
                    grads[k] = gd
                    rsum = rsum + fold(gd * prior)
                gd2 = jnp.concatenate(grads, axis=0)
                hid[layer, r, lanes] = gd2
                return down, s1 + fold(gd2), s2 + fold(gd2 * normed), rsum, sqh, sqa

            z8 = jnp.zeros((8, QUART), F32)
            _, s1, s2, rsum, sqh, sqa = lax.fori_loop(
                0, pairs, body, (jnp.zeros((seqs, QUART), F32), z8, z8, z8, z8, z8)
            )
            for k, x in ((m, s1), (2 + m, s2)):
                tot[layer, k : k + 1, lanes] = jnp.sum(x, axis=0, keepdims=True)
            for k, x in ((4, rsum), (5, sqh), (6, sqa)):
                x = jnp.sum(x, axis=0, keepdims=True)
                tot[layer, k : k + 1, lanes] = x if m == 0 else tot[layer, k : k + 1, lanes] + x
            between()

    def backward_stats(layer, m):
        rnd, plane, _ = slim_round(3 - layer, m)
        stage_start(plane, rnd, packed(tot[layer, m : m + 1, :], tot[layer, 2 + m : 3 + m, :]))

    def backward_middle(layer, m):
        rnd, plane, line = slim_round(3 - layer, m)
        stage_wait(plane, rnd)
        stage_start(line, rnd, add_slots(plane))

    def backward_end(layer, m):
        rnd, _, line = slim_round(3 - layer, m)
        stage_wait(line, rnd)
        value = add_slots(line)
        tot[layer, m : m + 1, :] = unpacked(value[0:4])
        tot[layer, 2 + m : 3 + m, :] = unpacked(value[4:8])

    def grad_rows(layer, m, slot):
        gain = vec_of(layer, 0)
        for lh in range(2):
            lanes = slice(lh * HALF, (lh + 1) * HALF)
            mean = coef[layer, 2 * m : 2 * m + 1, lanes]
            scale = coef[layer, 2 * m + 1 : 2 * m + 2, lanes]
            count = wide(counts[m : m + 1, :], 4)
            first = tot[layer, m : m + 1, lanes] / count
            second = tot[layer, 2 + m : 3 + m, lanes] / count * scale
            k = scale * gain[:, lanes]

            def body(i, acc):
                r = pl.ds(aligned(m * span + i * (2 * seqs), 16), 2 * seqs)
                y = hid[layer, r, lanes] - first - (rows[layer, r, lanes] - mean) * second
                y = wide(live[r, :], 4) * (k * y)
                g3[0, r, lanes] = y.astype(BF16)
                return acc + fold(y)

            acc = repeat(pairs, body, jnp.zeros((8, HALF), F32), 3)
            acc = jnp.sum(acc, axis=0, keepdims=True)
            if m == 0:
                levels[4:5, lanes] = acc
            else:
                top = lax.broadcasted_iota(jnp.int32, (16, HALF), 0) == 0
                minus = jnp.where(top, -(levels[4:5, lanes] + acc), 0.0)
                g3[0, total_rows:sent_rows, lanes] = minus.astype(BF16)
        here = pl.ds(0, span) if m == 0 else pl.ds(span, span + 16)
        made = across(g3.at[0, here, :], g3.at[1, here, :], slot + m)
        made.start()
        return made

    sums_round = {1: (1, 10), 0: (0, 11)}

    def sums_start(layer):
        parity, rnd = sums_round[layer]
        own_sum = -g3[0, total_rows:sent_rows, :].astype(F32)[0:1]
        far_sum = -g3[1, total_rows:sent_rows, :].astype(F32)[0:1]
        value = jnp.concatenate([own_sum, far_sum, tot[layer, 4:7, :], jnp.zeros((3, W), F32)], axis=0)
        stage_start(in_plane(wide_p, parity), rnd, value)

    def sums_middle(layer):
        parity, rnd = sums_round[layer]
        stage_wait(in_plane(wide_p, parity), rnd)
        stage_start(in_line(wide_z, parity), rnd, add_slots(in_plane(wide_p, parity)))

    def sums_end(layer):
        parity, rnd = sums_round[layer]
        stage_wait(in_line(wide_z, parity), rnd)
        vtot[layer] = add_slots(in_line(wide_z, parity))
        tot[layer, 4:7, :] = vtot[layer, 2:5, :]
        tot[layer, 7:8, :] = wide(counts[0:1, :] + counts[1:2, :], 8)
        env["summed"].add(layer)

        @pl.when(section == layer)
        def _():
            pltpu.make_async_copy(tot.at[layer], v.at[section], v_sems.at[0]).start()

        @pl.when(section != layer)
        def _():
            v_across(layer).start()

    def v_across(layer):
        return pltpu.make_async_remote_copy(
            src_ref=tot.at[layer], dst_ref=v.at[section], send_sem=v_sems.at[1], recv_sem=v_sems.at[2],
            device_id=sibling, device_id_type=MESH,
        )

    def transpose(src, begin=0, end=W // 128):
        def body(j, _):
            c = pl.ds(aligned(j * 128, 128), 128)
            src_t[c, 0:total_rows] = src[0:total_rows, c].T
            return 0

        lax.fori_loop(begin, end, body, 0)

    def transpose_level(src, layer):
        top = lax.broadcasted_iota(jnp.int32, (16, W), 0) == 0
        src[total_rows:sent_rows, :] = jnp.where(top, levels[2 + layer : 3 + layer, :], 0.0).astype(BF16)

        def body(j, _):
            c = pl.ds(aligned(j * 128, 128), 128)
            src_t[c, total_rows:] = src[total_rows:, c].T
            level = src[total_rows:sent_rows, c].astype(F32)[0:1]
            column[layer, c, :] = jnp.broadcast_to(level, (128, 128)).T.astype(BF16)
            return 0

        lax.fori_loop(0, W // 128, body, 0)

    def weight_part(block, grads, c):
        lanes = pl.ds(c * HALF, HALF)

        def body(j, _):
            r = pl.ds(aligned(j * HALF, HALF), HALF)
            block[r, lanes] = dot(src_t[r, :], grads[:, lanes], ((1,), (0,))).astype(BF16)
            return 0

        lax.fori_loop(0, W // HALF, body, 0)

    def source_grad(store, w_own, w_far, between):
        for m in range(2):
            r = pl.ds(m * span, span)

            def body(i, _):
                c = pl.ds(aligned(i * HALF, HALF), HALF)
                y = dot(g3[0, r, :], w_own[c, :], ((1,), (1,))) + dot(g3[1, r, :], w_far[c, :], ((1,), (1,)))
                store(r, c, y)
                return 0

            lax.fori_loop(0, 2, body, 0)
            between()

    env = dict(summed=set(), vtot=vtot, column=column, space=space, ar_send=ar_send, ar_recv=ar_recv,
               ar_other=ar_other, o=o, section=section, here={"batch": b})
    xs = [a for a in bits if a["link"] == "x"]
    ys = [a for a in bits if a["link"] == "y"]
    zs = [a for a in bits if a["link"] == "z"]
    orders = (xs + ys + zs, ys + xs + zs)
    blocks = {
        (1, 0): f_far.at[pl.ds(0, W), :],
        (1, 1): p_far.at[pl.ds(0, W), :],
        (0, 0): wc.at[1, 1],
        (0, 1): wr1,
    }
    parts = {}
    for layer in (1, 0):
        for index in range(2 * PAIRS):
            part, side = index // PAIRS, index % PAIRS

            def lane_of(sec, part=part, side=side):
                return (sec if part == 0 else 1 - sec) * W + side * 2 * PART

            block = blocks[layer, part].at[:, pl.ds(side * 2 * PART, 2 * PART)]
            parts[layer, index] = Reduction(env, layer, index, block, orders, lane_of)
    order = Order()

    def weight_grads(layer, between):
        for part in range(2):
            if part == 1:
                between()
            for c in range(2):
                weight_part(blocks[layer, part], g3.at[part], c)
                order.work(2.8)
                for k in range(c * HALF // PART, (c + 1) * HALF // PART):
                    order.begin(parts[layer, part * PAIRS + k // 2], k % 2)

    def arrived(layer, sends):
        for made in sends:
            made.wait()
        sums_start(layer)

    send_f = []
    for m in range(2):
        by_units(frames, f_own, m)
        fetch(grad_out, m).start()
        if m == 0:
            wait_heads(frames, 1)
        patch_heads(f_own, m)
        here = pl.ds(m * span, span)
        made = across(f_own.at[here, :], f_far.at[here, :], (0, 24)[m])
        made.start()
        send_f.append(made)
    start_across_w(1, w_plan(1), slot_of[1])
    stage_wait(cnt_plane, 0)
    stage_start(cnt_line, 0, add_slots(cnt_plane))
    wait_w(0, w_plan(0), slot_of[0], 0)
    matmul_to(rows.at[0], f_own, wc.at[0, 0], True, 0)
    matmul_to(rows.at[0], f_own, wc.at[0, 0], True, 1)
    wait_w(0, w_plan(0), slot_of[0], 1)
    send_f[0].wait()
    matmul_to(rows.at[0], f_far, wc.at[0, 1], False, 0)
    forward_stats(0, 0)
    send_f[1].wait()

    @pl.when(section == 1)
    def _():
        heads_copy(grad_out, 2).start()

    matmul_to(rows.at[0], f_far, wc.at[0, 1], False, 1)
    forward_middle(0, 0)
    forward_stats(0, 1)
    send_vec.wait_send()
    across(vecs.at[other], vecs.at[other], 3).wait_recv()
    stage_wait(cnt_line, 0)
    counts[...] = add_slots(cnt_line)
    forward_end(0, 0)
    sends = [forward_scan(0, 0, True)]
    forward_middle(0, 1)
    by_units(grad_out, g3.at[1], 0)
    wait_heads(grad_out, 2)
    patch_heads(g3.at[1], 0)
    forward_end(0, 1)
    sends.append(forward_scan(0, 1, True))
    wait_w(1, w_plan(1), slot_of[1], 0)
    matmul_to(rows.at[1], p_own, wc.at[1, 0], True, 0)
    wait_w(1, w_plan(1), slot_of[1], 1)
    sends[0].wait()
    matmul_to(rows.at[1], p_far, wc.at[1, 1], False, 0)
    forward_stats(1, 0)
    matmul_to(rows.at[1], p_own, wc.at[1, 0], True, 1)
    forward_middle(1, 0)
    sends[1].wait()
    matmul_to(rows.at[1], p_far, wc.at[1, 1], False, 1)
    forward_stats(1, 1)
    done_w(0, w_plan(0), slot_of[0])

    start_local_w(0, late_plan, slot_of[2])
    start_across_w(0, late_plan, slot_of[2])

    @pl.when(section == 1)
    def _():
        wc[0, 1, width - late_row :, :] = jnp.zeros((W - width + late_row, W), BF16)

    def source_level():
        def body(i, acc):
            r = pl.ds(aligned(i * (2 * seqs), 16), 2 * seqs)
            return acc + fold(wide(live[r, :], 8) * f_own[r, :].astype(F32))

        acc = repeat(2 * pairs, body, jnp.zeros((8, W), F32), 3)
        levels[0:1, :] = jnp.sum(acc, axis=0, keepdims=True)

    forward_end(1, 0)
    forward_scan(1, 0, False)
    forward_middle(1, 1)
    by_units(grad_out, g3.at[1], 1)
    patch_heads(g3.at[1], 1)
    source_level()
    forward_end(1, 1)
    level_plane, level_line = in_plane(wide_p, 0), in_line(wide_z, 0)
    stage_start(level_plane, 9, jnp.concatenate([levels[0:2, :], jnp.zeros((6, W), F32)], axis=0))
    forward_scan(1, 1, False)
    backward_scan(1, 0, g3.at[1])
    backward_stats(1, 0)
    stage_wait(level_plane, 9)
    stage_start(level_line, 9, add_slots(level_plane))
    backward_scan(1, 1, g3.at[1])
    backward_stats(1, 1)
    backward_middle(1, 0)
    pl.semaphore_signal(credit.at[0], inc=1, device_id=sibling, device_id_type=MESH)
    transpose(p_own, 0, W // 256)
    backward_middle(1, 1)
    backward_end(1, 0)
    pl.semaphore_wait(credit.at[0], 1)
    sends = [grad_rows(1, 0, 20)]
    transpose(p_own, W // 256)
    stage_wait(level_line, 9)
    levels[2:4, :] = (add_slots(level_line) / wide(counts[0:1, :] + counts[1:2, :], 8))[0:2]
    transpose_level(p_own, 1)
    backward_end(1, 1)
    sends.append(grad_rows(1, 1, 20))
    weight_grads(1, lambda: arrived(1, sends))
    wait_w(1, w_plan(1), slot_of[1], 2)
    done_w(1, w_plan(1), slot_of[1])

    def keep_down(r, c, y):
        p_own[r, c] = y.astype(BF16)

    source_grad(keep_down, wc.at[1, 0], wr1, lambda: order.work(4.0))
    pl.semaphore_signal(credit.at[1], inc=1, device_id=sibling, device_id_type=MESH)
    sums_middle(1)
    backward_scan(0, 0, p_own, lambda: order.work(1.0))
    backward_stats(0, 0)
    backward_scan(0, 1, p_own, lambda: order.work(1.0))
    backward_stats(0, 1)
    backward_middle(0, 0)
    sums_end(1)
    transpose(f_own)
    transpose_level(f_own, 0)
    backward_middle(0, 1)
    order.work(7.0)
    backward_end(0, 0)
    pl.semaphore_wait(credit.at[1], 1)
    sends = [grad_rows(0, 0, 22)]
    backward_end(0, 1)
    sends.append(grad_rows(0, 1, 22))
    order.work(3.6)
    weight_grads(0, lambda: arrived(0, sends))
    wait_w(0, late_plan, slot_of[2], 0)
    wait_w(0, late_plan, slot_of[2], 1)
    done_w(0, late_plan, slot_of[2])

    def keep_source(r, c, y):
        rows[0, r, c] = y

    fetch(grad_out, 0).start()
    fetch(grad_out, 1).start()
    sums_middle(0)
    source_grad(keep_source, wc.at[0, 0], wc.at[0, 1], lambda: order.work(4.0))
    sums_end(0)

    def give(m):
        return pltpu.make_async_copy(staged.at[m], gf.at[m], stage_sem.at[m])

    for m in range(2):
        fetch(grad_out, m).wait()

        def finish_frames(i, _, m=m):
            straight = staged[m, pl.ds(2 * i, 2)].astype(F32).reshape(2 * seqs, half)
            y = rows[0, pl.ds(aligned(m * span + 2 * i * seqs, 8), 2 * seqs), :]
            y = jnp.where(section == 0, y[:, :half], y[:, late_shift : late_shift + half])
            staged[m, pl.ds(2 * i, 2)] = (y + straight).reshape(2, seqs, half).astype(BF16)
            return 0

        repeat(pairs, finish_frames, 0, 3)
        give(m).start()
        order.work(2.0)
    order.drain()
    for m in range(2):
        give(m).wait()

    for layer in range(2):

        @pl.when(section == layer)
        def _(layer=layer):
            pltpu.make_async_copy(tot.at[layer], v.at[section], v_sems.at[0]).wait()
            pltpu.make_async_remote_copy(
                src_ref=tot.at[layer], dst_ref=v.at[other], send_sem=v_sems.at[1], recv_sem=v_sems.at[2],
                device_id=sibling, device_id_type=MESH,
            ).wait_recv()

        @pl.when(section != layer)
        def _(layer=layer):
            v_across(layer).wait_send()

    own_part, far_part = v[section], v[other]
    first = jnp.where(section == 0, own_part, far_part)
    second = jnp.where(section == 0, far_part, own_part)
    for row, terms in ((0, (2, 3)), (1, (0, 1)), (2, (4,))):
        for lane, x in ((0, first), (W, second)):
            total = x[terms[0] : terms[0] + 1, :]
            for k in terms[1:]:
                total = total + x[k : k + 1, :]
            vectors[row : row + 1, lane : lane + W] = total
    squares = jnp.sum(first[5:7, :] + second[5:7, :], axis=1, keepdims=True)
    root = jnp.sqrt(squares / (first[7:8, 0:1] * width))
    for k in range(2):
        vectors[3 + k : 4 + k, :] = jnp.broadcast_to(root[k : k + 1], (1, 2 * W))
    vectors[5:8, :] = jnp.zeros((3, 2 * W), F32)


def write_results(o, gf, vectors, grad_weight, grad_frames, grad_gains, grad_shifts, grad_recurs, table):
    width = grad_weight.shape[2]
    grad_weight[0] = o[...][:, :width].astype(F32)
    grad_frames[...] = gf[...]

    @pl.when(pl.program_id(0) == 0)
    def _():
        for k, out in enumerate((grad_gains, grad_shifts, grad_recurs)):
            out[...] = vectors[k : k + 1, 0:width]
        table[...] = jnp.concatenate([vectors[3:4, 0:1], vectors[4:5, 0:1]], axis=1)


def results(o, gf, vectors):
    micro, steps, seqs, half = gf.shape
    width = 2 * half
    count = W * 2 // 256
    frames = micro * steps // count
    whole = lambda shape: pl.BlockSpec(shape, lambda i: (0, 0))
    out = pl.pallas_call(
        write_results,
        grid=(count,),
        in_specs=[
            pl.BlockSpec((256, 2 * W), lambda i: (i, 0)),
            pl.BlockSpec((frames, seqs, half), lambda i: (i, 0, 0)),
            whole((8, 2 * W)),
        ],
        out_specs=(
            pl.BlockSpec((1, 256, width), lambda i: (0, i, 0)),
            pl.BlockSpec((frames, seqs, half), lambda i: (i, 0, 0)),
            whole((1, width)),
            whole((1, width)),
            whole((1, width)),
            whole((1, 2)),
        ),
        out_shape=(
            jax.ShapeDtypeStruct((1, width, width), F32),
            jax.ShapeDtypeStruct((micro * steps, seqs, half), BF16),
            jax.ShapeDtypeStruct((1, width), F32),
            jax.ShapeDtypeStruct((1, width), F32),
            jax.ShapeDtypeStruct((1, width), F32),
            jax.ShapeDtypeStruct((1, 2), F32),
        ),
        compiler_params=pltpu.CompilerParams(vmem_limit_bytes=64 * 1024 * 1024),
    )(o.reshape(2 * W, 2 * W), gf.reshape(micro * steps, seqs, half), vectors)
    return out[1].reshape(gf.shape), out[0], *out[2:]


def whole_step(dims, frames, grad_out, weights, gains, shifts, recurs, lengths, masks):
    nz, ny, nx = dims
    micro, steps, seqs, half = frames.shape
    width = 2 * half
    views = seqs // lengths.shape[1]
    rows = micro * steps * seqs
    np_ = ny * nx
    wide_rows = (rows + 16 + 127) // 128 * 128
    depth = (nx * ny * nz - 1).bit_length()
    any_ = pl.BlockSpec(memory_space=pl.ANY)
    held = pl.BlockSpec(memory_space=pltpu.VMEM)
    dma = pltpu.SemaphoreType.DMA
    return pl.pallas_call(
        functools.partial(kernel, dims, steps, seqs, views),
        out_shape=(
            jax.ShapeDtypeStruct((2, W, 2 * W), BF16),
            jax.ShapeDtypeStruct(frames.shape, BF16),
            jax.ShapeDtypeStruct((8, 2 * W), F32),
        ),
        in_specs=[any_] * 3 + [held] * 5,
        out_specs=(any_, any_, held),
        scratch_shapes=[
            pltpu.VMEM((wide_rows, W), BF16),
            pltpu.VMEM((rows, W), BF16),
            pltpu.VMEM((wide_rows, W), BF16),
            pltpu.VMEM((rows, W), BF16),
            pltpu.VMEM((2, wide_rows, W), BF16),
            pltpu.VMEM((2, 2, W, W), BF16),
            pltpu.VMEM((W, W), BF16),
            pltpu.VMEM((W, wide_rows), BF16),
            pltpu.VMEM((rows, 128), F32),
            pltpu.VMEM((128, 128), F32),
            pltpu.VMEM(frames.shape, BF16),
            pltpu.VMEM((micro, steps, seqs, 128), BF16),
            pltpu.VMEM((5, W, (width - W) % 128), BF16),
            pltpu.VMEM((2, 8, W), F32),
            pltpu.VMEM((2, 8, 2 * W), F32),
            pltpu.VMEM((2, rows, W), F32),
            pltpu.VMEM((2, rows, W), F32),
            pltpu.VMEM((2, 8, W), F32),
            pltpu.VMEM((2, 8, W), F32),
            pltpu.VMEM((2, 8, W), F32),
            pltpu.VMEM((8, W), F32),
            pltpu.VMEM((2, W, 128), BF16),
            pltpu.VMEM((8, 128), F32),
            pltpu.VMEM((1, np_, 8, 128), F32),
            pltpu.VMEM((1, nz, 8, 128), F32),
            pltpu.VMEM((4, np_, 8, QUART), F32),
            pltpu.VMEM((4, nz, 8, QUART), F32),
            pltpu.VMEM((2, np_, 8, W), F32),
            pltpu.VMEM((2, nz, 8, W), F32),
            pltpu.VMEM((2, 2 * PAIRS, W, 2 * PART), BF16),
            dma((3, 25)),
            dma((3,)),
            dma((2,)),
            pltpu.SemaphoreType.REGULAR((2,)),
            dma((12, max(np_, 2))),
            dma((12, max(np_, 2))),
            dma((12, max(nz, 2))),
            dma((12, max(nz, 2))),
            dma((2, 2 * PAIRS, 2, 2 * depth + 2)),
            dma((2, 2 * PAIRS, 2, 2 * depth + 2)),
            dma((2, 2 * PAIRS, 2, 2)),
        ],
        compiler_params=pltpu.CompilerParams(
            collective_id=0, has_side_effects=True, vmem_limit_bytes=64 * 1024 * 1024
        ),
    )(frames, grad_out, weights, gains, shifts, recurs, lengths, masks)


def shards(dims, frames, grad_out, weights, gains, shifts, recurs, lengths, masks):
    return results(*whole_step(dims, frames, grad_out, weights, gains, shifts, recurs, lengths, masks))


def solution(mesh):
    in_specs = (
        P(None, None, "batch", "section"),
        P(None, None, "batch", "section"),
        P("section", None, None),
        P("section", None),
        P("section", None),
        P("section", None),
        P(None, "batch"),
        P(None, None, "batch"),
    )
    out_specs = (
        P(None, None, "batch", "section"),
        P("section", None, None),
        P("section", None),
        P("section", None),
        P("section", None),
        P("section", None),
    )
    body = functools.partial(shards, grid_of(mesh.shape["batch"]))
    return jax.shard_map(body, mesh=mesh, in_specs=in_specs, out_specs=out_specs, check_vma=False)
```

```python
import functools

import jax
import jax.numpy as jnp
from jax import lax
from jax.experimental import pallas as pl
from jax.experimental.pallas import tpu as pltpu
from jax.sharding import PartitionSpec as P

EPS = 1e-05
W = 1024
HALF = W // 2
QUART = W // 4
PAIRS = 1
PART = W // PAIRS // 2
MESH = pl.DeviceIdType.MESH
F32 = jnp.float32
BF16 = jnp.bfloat16


def grid_of(size):
    if size == 16:
        return (4, 2, 2)
    if size == 128:
        return (8, 4, 4)
    return (size, 1, 1)


def aligned(x, k):
    return pl.multiple_of(x, k)


def wide(x, reps):
    return jnp.concatenate([x] * reps, axis=1)


def fold(x):
    rows = x.shape[0]
    total = x[0:8]
    for k in range(8, rows, 8):
        total = total + x[k : k + 8]
    return total


def repeat(count, body, init, times):
    while count % times:
        times -= 1

    def several(i, carry):
        for j in range(times):
            carry = body(i * times + j, carry)
        return carry

    return lax.fori_loop(0, count // times, several, init)


def dot(a, b, dims):
    return lax.dot_general(a, b, (dims, ((), ())), preferred_element_type=F32)


class Reduction:
    def __init__(self, env, layer, index, block, orders, lane_of):
        self.env, self.layer, self.index, self.block, self.orders = env, layer, index, block, orders
        self.lane_of = lane_of
        self.space = env["space"].at[layer, index]
        self.depth = len(orders[0])
        self.regions = [self.halves(i, order) for i, order in enumerate(orders)]
        self.step = 0
        self.waits = []
        depth = self.depth
        self.steps = [functools.partial(self.scatter, 0)]
        self.steps += [functools.partial(self.scatter, k) for k in range(1, depth)]
        self.steps += [functools.partial(self.gather, k) for k in range(depth - 1, 0, -1)]
        self.steps += [self.give, self.finish]

    def halves(self, i, order):
        row, rows, lane, lanes = 0, W, i * PART, PART
        out = [(row, rows, lane, lanes)]
        for axis in order:
            if rows > 16:
                rows //= 2
                row = row + axis["bit"] * rows
            else:
                lanes //= 2
                lane = lane + axis["bit"] * lanes
            out.append((row, rows, lane, lanes))
        return out

    @property
    def free_to_go(self):
        return self.step != self.depth or self.layer in self.env["summed"]

    @property
    def done(self):
        return self.step >= len(self.steps)

    def advance(self):
        self.sent = []
        self.steps[self.step]()
        self.step += 1
        return self.sent

    def remote(self, i, src, dst, slot, where, recv=None):
        sems = (self.layer, self.index, i, slot)
        return pltpu.make_async_remote_copy(
            src_ref=src, dst_ref=dst, send_sem=self.env["ar_send"].at[sems],
            recv_sem=self.env["ar_recv"].at[sems] if recv is None else recv, device_id=where, device_id_type=MESH,
        )

    def wait(self):
        for made, came in self.waits:
            made.wait_send()
            came.wait_recv()
        self.waits = []

    def came_at(self, i, k):
        row = sum(r[1] for r in self.regions[i][1 : k + 1])
        _, rows, _, lanes = self.regions[i][k + 1]
        return row, rows, i * PART, lanes

    def scatter(self, k):
        if k > 0:
            self.wait()
            self.add(k - 1)
        for i, order in enumerate(self.orders):
            self.scatter_part(i, k, order[k])

    def start_part(self, i):
        self.sent = []
        self.scatter_part(i, 0, self.orders[i][0])
        if i == 1:
            self.step = 1
        return self.sent

    def scatter_part(self, i, k, axis):
        row, rows, lane, lanes = self.regions[i][k]
        _, rows2, _, lanes2 = self.regions[i][k + 1]
        give_row = row + (1 - axis["bit"]) * rows2 if rows2 < rows else row
        give_lane = lane if rows2 < rows else lane + (1 - axis["bit"]) * lanes2
        src = self.block.at[pl.ds(aligned(give_row, 16), rows2), pl.ds(aligned(give_lane, 128), lanes2)]
        at, n, at_lane, n_lanes = self.came_at(i, k)
        dst = self.space.at[pl.ds(at, n), pl.ds(at_lane, n_lanes)]
        made = self.remote(i, src, dst, k, axis["partner"])
        made.start()
        self.waits.append((made, made))
        self.sent.append((axis["link"], rows2 * lanes2 * 2))

    def add(self, k, last=False):
        rows = self.regions[0][k + 1][1]
        size = min(rows, 64)
        out = []
        for i in range(2):
            row, _, lane, lanes = self.regions[i][k + 1]
            at, _, at_lane, _ = self.came_at(i, k)
            lane = aligned(lane, 128)
            extra = None
            if last:
                part = self.index // PAIRS
                first = aligned((self.index % PAIRS) * 2 * PART + lane, 128)
                extra = self.env["vtot"][self.layer, part : part + 1, pl.ds(first, lanes)]
            out.append((row, lane, lanes, at, at_lane, self.local(i, k + 1)[0], extra))

        def body(j, _):
            for row, lane, lanes, at, at_lane, home, extra in out:
                here = pl.ds(aligned(row + j * size, 16), size)
                total = self.block[here, pl.ds(lane, lanes)].astype(F32)
                total = total + self.space[pl.ds(aligned(at + j * size, 16), size), pl.ds(at_lane, lanes)].astype(F32)
                if last:
                    column = self.env["column"][self.layer, here, :].astype(F32)
                    total = total + wide(column, lanes // 128) * extra
                    to = pl.ds(aligned(home + j * size, 16), size)
                    self.space[to, pl.ds(lane, lanes)] = total.astype(BF16)
                else:
                    self.block[here, pl.ds(lane, lanes)] = total.astype(BF16)
            return 0

        lax.fori_loop(0, rows // size, body, 0)

    def local(self, i, k):
        row, rows, lane, lanes = self.regions[i][k]
        return row - self.regions[i][1][0], rows, lane, lanes

    def gather(self, k):
        self.wait()
        if k == self.depth - 1:
            self.add(k, last=True)
        for i, order in enumerate(self.orders):
            axis = order[k]
            row, rows, lane, lanes = self.local(i, k + 1)
            row0, rows0, lane0, lanes0 = self.local(i, k)
            if rows0 > rows:
                far = (row0 + (1 - axis["bit"]) * rows, rows, lane, lanes)
            else:
                far = (row, rows, lane0 + (1 - axis["bit"]) * lanes, lanes)
            refs = [
                self.space.at[pl.ds(aligned(r, 16), n), pl.ds(aligned(c, 128), w)]
                for r, n, c, w in ((row, rows, lane, lanes), far)
            ]
            made = self.remote(i, refs[0], refs[0], self.depth + k, axis["partner"])
            made.start()
            self.waits.append((made, self.remote(i, refs[1], refs[1], self.depth + k, axis["partner"])))
            self.sent.append((axis["link"], rows * lanes * 2))

    def result(self, i, bit, section):
        rows = self.regions[i][1][1]
        lane = aligned(self.lane_of(section) + i * PART, PART)
        return self.env["o"].at[section, pl.ds(aligned(bit * rows, 16), rows), pl.ds(lane, PART)]

    def gathered(self, i):
        return self.space.at[pl.ds(0, self.regions[i][1][1]), pl.ds(i * PART, PART)]

    def deliver(self, i, near, straight):
        axis, section = self.orders[i][0], self.env["section"]
        slot = 2 * self.depth + (0 if near else 1)
        recv = None if straight else self.env["ar_other"].at[self.layer, self.index, i, 0 if near else 1]
        where = dict(self.env["here"] if near else axis["partner"], section=self.layer)
        return self.remote(i, self.gathered(i), self.result(i, axis["bit"], section), slot, where, recv)

    def arrival(self, i, near, straight):
        axis, section = self.orders[i][0], self.env["section"]
        slot = 2 * self.depth + (0 if near else 1)
        recv = None if straight else self.env["ar_other"].at[self.layer, self.index, i, 0 if near else 1]
        bit = axis["bit"] if near else 1 - axis["bit"]
        frm = section if straight else 1 - section
        where = dict(self.env["here"] if near else axis["partner"], section=frm)
        return self.remote(i, self.gathered(i), self.result(i, bit, frm), slot, where, recv)

    def kept(self, i):
        sem = self.env["ar_recv"].at[self.layer, self.index, i, 2 * self.depth]
        return pltpu.make_async_copy(
            self.gathered(i), self.result(i, self.orders[i][0]["bit"], self.env["section"]), sem
        )

    def give(self):
        self.wait()

        @pl.when(self.env["section"] == self.layer)
        def _():
            for i in range(2):
                self.deliver(i, False, True).start()
                self.kept(i).start()

        @pl.when(self.env["section"] != self.layer)
        def _():
            for i in range(2):
                self.deliver(i, False, False).start()
                self.deliver(i, True, False).start()

        for i, order in enumerate(self.orders):
            self.sent.append((order[0]["link"], self.regions[i][1][1] * PART * 2))

    def finish(self):
        @pl.when(self.env["section"] == self.layer)
        def _():
            for i in range(2):
                self.kept(i).wait()
                self.deliver(i, False, True).wait_send()
                self.arrival(i, False, True).wait_recv()
                self.arrival(i, True, False).wait_recv()
                self.arrival(i, False, False).wait_recv()

        @pl.when(self.env["section"] != self.layer)
        def _():
            for i in range(2):
                self.deliver(i, False, False).wait_send()
                self.deliver(i, True, False).wait_send()


class Order:
    RATE, HOP = 58e3, 2.0

    def __init__(self):
        self.now = 0.0
        self.free = {}
        self.going = []

    def sent(self, copies):
        end = self.now
        for link, size in copies:
            self.free[link] = max(self.now, self.free.get(link, 0.0)) + size / self.RATE
            end = max(end, self.free[link])
        return end + self.HOP

    def begin(self, one, i):
        end = self.sent(one.start_part(i))
        if i == 0:
            one.due = end
        else:
            one.due = max(one.due, end)
            self.going.append(one)

    def advance(self, one):
        self.now = max(self.now, one.due) + 0.4
        one.due = self.sent(one.advance())
        if one.done:
            self.going.remove(one)

    def work(self, cost):
        self.now += cost
        while True:
            due = [x for x in self.going if x.due <= self.now and x.free_to_go]
            if not due:
                return
            self.advance(min(due, key=lambda x: x.due))

    def drain(self):
        while self.going:
            self.advance(min(self.going, key=lambda x: x.due))


def kernel(dims, steps, seqs, views, frames, grad_out, weights, gains, shifts, recurs, lengths, masks, o, gf, vectors, f_own, f_far, p_own, p_far, g3, wc, wr1, src_t, live, turn,
           staged, heads, tails, v, vecs, rows, hid, coef, tot, vtot, levels, column, counts, cnt_p, cnt_z, slim_p, slim_z,
           wide_p, wide_z, space, sems, v_sems, stage_sem, credit, pl_send, pl_recv, z_send, z_recv, ar_send, ar_recv,
           ar_other):
    nz, ny, nx = dims
    np_ = ny * nx
    span = steps * seqs
    total_rows = 2 * span
    sent_rows = total_rows + 16
    pairs = steps // 2
    section = lax.axis_index("section")
    other = 1 - section
    b = lax.axis_index("batch")
    mp = lax.rem(b, np_)
    mz = b // np_

    def at_plane(i):
        return {"batch": b - mp + i}

    def at_z(i):
        return {"batch": b + (i - mz) * np_}

    bits = []
    for link, count, stride in (("x", nx, 1), ("y", ny, nx), ("z", nz, np_)):
        while count > 1:
            bit = lax.rem(b // stride, 2)
            bits.append(dict(bit=bit, partner={"batch": b + (1 - 2 * bit) * stride}, link=link))
            count //= 2
            stride *= 2
    sibling = {"section": other}

    def local(src, dst, slot):
        return pltpu.make_async_copy(src, dst, sems.at[0, slot])

    def across(src, dst, slot):
        return pltpu.make_async_remote_copy(
            src_ref=src, dst_ref=dst, send_sem=sems.at[1, slot], recv_sem=sems.at[2, slot],
            device_id=sibling, device_id_type=MESH,
        )

    half = frames.shape[3]
    width = 2 * half
    lead = W - half
    rest = width - W
    full = rest // 128 * 128

    def fetch(source, m):
        return pltpu.make_async_copy(source.at[m], staged.at[m], stage_sem.at[m])

    def by_units(source, target, m):
        fetch(source, m).wait()

        @pl.when(section == 0)
        def _():
            pad = jnp.zeros((2 * seqs, lead), F32)

            def place(i, _):
                x = staged[m, pl.ds(2 * i, 2)].astype(F32).reshape(2 * seqs, half)
                to = pl.ds(aligned(m * span + 2 * i * seqs, 16), 2 * seqs)
                target[to, :] = jnp.concatenate([x, pad], axis=1).astype(BF16)
                return 0

            repeat(pairs, place, 0, 3)

        @pl.when(section == 1)
        def _():
            pad = jnp.zeros((2 * seqs, 2 * lead), F32)

            def place(i, _):
                x = staged[m, pl.ds(2 * i, 2)].astype(F32).reshape(2 * seqs, half)
                to = pl.ds(aligned(m * span + 2 * i * seqs, 16), 2 * seqs)
                target[to, :] = jnp.concatenate([x[:, lead:], pad], axis=1).astype(BF16)
                return 0

            repeat(pairs, place, 0, 3)

    def patch_heads(target, m):
        @pl.when(section == 0)
        def _():
            lane = lax.broadcasted_iota(jnp.int32, (2 * seqs, 128), 1)

            def place(i, _):
                to = pl.ds(aligned(m * span + 2 * i * seqs, 16), 2 * seqs)
                head = heads[m, pl.ds(2 * i, 2)].astype(F32).reshape(2 * seqs, 128)
                head = pltpu.roll(head, 128 - lead, 1)
                old = target[to, W - 128 :].astype(F32)
                target[to, W - 128 :] = jnp.where(lane < 128 - lead, old, head).astype(BF16)
                return 0

            repeat(pairs, place, 0, 3)

    def pieces(row, count, u, block, spot):
        r = pl.ds(row, count)
        to = pl.ds(0, count)
        if u == 0:
            return [(weights.at[0, r, pl.ds(0, W)], block.at[to, :])]
        return [
            (weights.at[0, r, pl.ds(W, full)], block.at[to, pl.ds(0, full)]),
            (weights.at[0, r, pl.ds(W + full, rest - full)], tails.at[spot, to, :]),
        ]

    rows_of = {0: (0, W), 1: (W, rest)}

    def w_plan(layer):
        mine, far = rows_of[layer], rows_of[1 - layer]
        plan = [
            (mine, layer, far, 1 - layer, wc.at[layer, 0], 2 * layer),
            (far, layer, mine, 1 - layer, wc.at[layer, 1], 2 * layer + 1),
        ]
        if layer == 1:
            plan.append((mine, 0, far, 1, wr1, 4))
        return plan

    late_row = (width - half) // 16 * 16
    late_shift = half - late_row
    late_plan = [
        ((0, W), 0, (late_row, width - late_row), 1, wc.at[0, 0], 0),
        ((0, W), 1, (late_row, width - late_row), 0, wc.at[0, 1], 1),
    ]
    slot_of = {0: 4, 1: 8, 2: 14}

    def local_w(plan, base, which):
        r, u, _, _, block, spot = plan[which]
        return [local(a, t, base + 2 * which + i) for i, (a, t) in enumerate(pieces(*r, u, block, spot))]

    def across_w(plan, base, which):
        _, _, r, u, block, spot = plan[which]
        return [across(a, t, base + 2 * which + i) for i, (a, t) in enumerate(pieces(*r, u, block, spot))]

    def start_local_w(layer, plan, base):
        @pl.when(section == layer)
        def _():
            for which in range(len(plan)):
                for made in local_w(plan, base, which):
                    made.start()

    def start_across_w(layer, plan, base):
        @pl.when(section == layer)
        def _():
            for which in range(len(plan)):
                for made in across_w(plan, base, which):
                    made.start()

    def last_units(block, spot):
        def body(i, _):
            r = pl.ds(aligned(i * 128, 128), 128)
            x = tails[spot, r, :].astype(F32)
            x = jnp.concatenate([x, jnp.zeros((128, 128 - x.shape[1]), F32)], axis=1)
            block[r, full:] = x.astype(BF16)
            return 0

        lax.fori_loop(0, W // 128, body, 0)

    def wait_w(layer, plan, base, which):
        _, own_u, _, far_u, block, spot = plan[which]

        @pl.when(section == layer)
        def _():
            for made in local_w(plan, base, which):
                made.wait()
            if own_u == 1:
                last_units(block, spot)

        @pl.when(section != layer)
        def _():
            for made in across_w(plan, base, which):
                made.wait_recv()
            if far_u == 1:
                last_units(block, spot)

    def done_w(layer, plan, base):
        @pl.when(section == layer)
        def _():
            for which in range(len(plan)):
                for made in across_w(plan, base, which):
                    made.wait_send()

    def heads_copy(source, slot):
        return across(source.at[:, :, :, pl.ds(0, 128)], heads, slot)

    def wait_heads(source, slot):
        @pl.when(section == 0)
        def _():
            heads_copy(source, slot).wait_recv()

        @pl.when(section == 1)
        def _():
            heads_copy(source, slot).wait_send()

    fetch(frames, 0).start()
    fetch(frames, 1).start()
    for layer in range(2):
        start_local_w(layer, w_plan(layer), slot_of[layer])

    barrier = pltpu.get_barrier_semaphore()
    greeted = [dict(sibling)]
    greeted += [at_plane(lax.rem(mp + k, np_)) for k in range(1, np_)]
    greeted += [at_z(lax.rem(mz + k, nz)) for k in range(1, nz)]
    greeted += [dict(axis["partner"], section=other) for axis in bits]
    for where in greeted:
        pl.semaphore_signal(barrier, inc=1, device_id=where, device_id_type=MESH)

    for k, (x, fill) in enumerate(((gains, 0.0), (shifts, -1e30), (recurs, 0.0))):
        vecs[section, k : k + 1, 0:width] = x[...]
        vecs[section, k : k + 1, width:] = jnp.full((1, 2 * W - width), fill, F32)
    vecs[section, 3:8, :] = jnp.zeros((5, 2 * W), F32)

    gap = jnp.zeros((W - rest, W), BF16)

    @pl.when(section == 0)
    def _():
        wc[0, 1, rest:, :] = gap
        wc[1, 1, rest:, :] = gap

    @pl.when(section == 1)
    def _():
        wc[0, 0, rest:, :] = gap
        wc[1, 0, rest:, :] = gap
        wr1[rest:, :] = gap

    for spot in (0, 2):
        tails[spot, rest:, :] = jnp.zeros((W - rest, rest - full), BF16)
    for spare in (f_own, p_own, g3.at[0], g3.at[1]):
        spare[sent_rows:, :] = jnp.zeros((spare.shape[0] - sent_rows, W), BF16)

    pl.semaphore_wait(barrier, len(greeted))

    @pl.when(section == 1)
    def _():
        heads_copy(frames, 1).start()

    start_across_w(0, w_plan(0), slot_of[0])
    send_vec = across(vecs.at[section], vecs.at[section], 3)
    send_vec.start()

    def stage_copy(where, rnd, slot, k, back):
        buf, parity, size, me, at, send, recv = where
        there = at(lax.rem(me + (size - k if back else k), size))
        ref = buf.at[parity, slot]
        return pltpu.make_async_remote_copy(
            src_ref=ref, dst_ref=ref, send_sem=send.at[rnd, k], recv_sem=recv.at[rnd, k],
            device_id=there, device_id_type=MESH,
        )

    def in_plane(buf, parity):
        return (buf, parity, np_, mp, at_plane, pl_send, pl_recv)

    def in_line(buf, parity):
        return (buf, parity, nz, mz, at_z, z_send, z_recv)

    def stage_start(where, rnd, value):
        buf, parity, size, me = where[:4]
        buf[parity, me] = value
        for k in range(1, size):
            stage_copy(where, rnd, me, k, False).start()

    def stage_wait(where, rnd):
        size, me = where[2:4]
        for k in range(1, size):
            stage_copy(where, rnd, me, k, False).wait_send()
            stage_copy(where, rnd, lax.rem(me + size - k, size), k, True).wait_recv()

    def add_slots(where):
        buf, parity, size = where[:3]
        total = buf[parity, 0]
        for k in range(1, size):
            total = total + buf[parity, k]
        return total

    groups = lengths.shape[1]
    s_at = lax.broadcasted_iota(jnp.int32, (seqs, groups), 0)
    g_at = lax.broadcasted_iota(jnp.int32, (seqs, groups), 1) * views
    there = (s_at >= g_at) & (s_at < g_at + views)
    position = lax.broadcasted_iota(jnp.int32, (seqs, 128), 1)
    local_counts = []
    for m in range(2):
        turn[...] = jnp.zeros_like(turn)
        turn[0:steps, 0:seqs] = masks[m].astype(F32)
        mask = turn[...].T[0:seqs]
        length = jnp.broadcast_to(lengths[m : m + 1, :], (seqs, groups)).astype(F32)
        limit = jnp.sum(jnp.where(there, length, 0.0), axis=1, keepdims=True)
        alive = (position.astype(F32) < limit) & ((mask > 0.0) | (position == 0))
        alive = jnp.where(position < steps, alive.astype(F32), 0.0)
        total = jnp.zeros((seqs, 128), F32)
        for t in range(steps):
            at = m * span + t * seqs
            cells = jnp.broadcast_to(alive[:, t : t + 1], (seqs, 128))
            live[at : at + seqs, :] = cells
            total = total + cells
        local_counts.append(jnp.sum(total, axis=0, keepdims=True))
    n_own = jnp.concatenate(local_counts * 4, axis=0)

    cnt_plane, cnt_line = in_plane(cnt_p, 0), in_line(cnt_z, 0)
    stage_start(cnt_plane, 0, n_own)

    def vec_of(layer, k):
        return vecs[layer, k : k + 1, pl.ds(aligned(section * W, W), W)]

    def matmul_to(out, a, w, first, m):
        r = pl.ds(m * span, span)

        def body(i, _):
            c = pl.ds(aligned(i * HALF, HALF), HALF)
            y = dot(a[r, :], w[:, c], ((1,), (0,)))
            out[r, c] = y if first else out[r, c] + y
            return 0

        lax.fori_loop(0, 2, body, 0)

    def packed(x, y):
        return jnp.concatenate([z[:, k * QUART : (k + 1) * QUART] for z in (x, y) for k in range(4)], axis=0)

    def unpacked(x):
        return jnp.concatenate([x[k : k + 1] for k in range(4)], axis=1)

    def merge_slots(where, counts_of):
        buf, parity, size = where[:3]
        s = [buf[parity, k, 0:4, :] for k in range(size)]
        q = [buf[parity, k, 4:8, :] for k in range(size)]
        n = [wide(counts_of(k), 2) for k in range(size)]
        total, squares, count = sum(s[1:], s[0]), sum(q[1:], q[0]), sum(n[1:], n[0])
        mean = total / count
        for k in range(size):
            d = s[k] / n[k] - mean
            squares = squares + n[k] * d * d
        return jnp.concatenate([total, squares], axis=0)

    def slim_round(which, m):
        return 1 + 2 * which + m, in_plane(slim_p, 2 * m + which % 2), in_line(slim_z, 2 * m + which % 2)

    def forward_stats(layer, m):
        start = jnp.sum(rows[layer, m * span : m * span + seqs, :], axis=0, keepdims=True) * (1.0 / seqs)

        def body(i, carry):
            s, q = carry
            r = pl.ds(aligned(m * span + i * (2 * seqs), 16), 2 * seqs)
            d = rows[layer, r, :] - start
            kept = wide(live[r, :], 8) * d
            return s + fold(kept), q + fold(kept * d)

        zero = jnp.zeros((8, W), F32)
        s, q = repeat(pairs, body, (zero, zero), 3)
        s, q = jnp.sum(s, axis=0, keepdims=True), jnp.sum(q, axis=0, keepdims=True)
        n = wide(local_counts[m], 8)
        rnd, plane, _ = slim_round(layer, m)
        stage_start(plane, rnd, packed(s + n * start, jnp.maximum(q - s * s / n, 0.0)))

    def forward_middle(layer, m):
        rnd, plane, line = slim_round(layer, m)
        stage_wait(plane, rnd)
        stage_start(line, rnd, merge_slots(plane, lambda k: cnt_p[0, k, m : m + 1, :]))

    def forward_end(layer, m):
        rnd, _, line = slim_round(layer, m)
        stage_wait(line, rnd)
        value = merge_slots(line, lambda k: cnt_z[0, k, m : m + 1, :])
        count = wide(counts[m : m + 1, :], 8)
        mean = unpacked(value[0:4]) / count
        scale = lax.rsqrt(unpacked(value[4:8]) / count + EPS)
        coef[layer, 2 * m : 2 * m + 1, :] = mean
        coef[layer, 2 * m + 1 : 2 * m + 2, :] = scale
        slope = vec_of(layer, 0) * scale
        coef[layer, 4 + 2 * m : 5 + 2 * m, :] = slope
        coef[layer, 5 + 2 * m : 6 + 2 * m, :] = vec_of(layer, 1) - mean * slope

    def forward_scan(layer, m, passes):
        rec = vec_of(layer, 2)
        slope = coef[layer, 4 + 2 * m : 5 + 2 * m, :]
        shift = coef[layer, 5 + 2 * m : 6 + 2 * m, :]

        def body(i, carry):
            h, level = carry
            r = pl.ds(aligned(m * span + i * (2 * seqs), 16), 2 * seqs)
            x = rows[layer, r, :] * slope + shift
            lv = wide(live[r, :], 8)
            alive = lv > 0.0
            both = []
            for k in range(2):
                part = slice(k * seqs, (k + 1) * seqs)
                z = x[part] + rec * h
                soft = jnp.maximum(z, 0.0) + jnp.log(1.0 + jnp.exp(-jnp.abs(z)))
                h = jnp.where(alive[part], soft, h)
                both.append(h)
            two = jnp.concatenate(both, axis=0)
            hid[layer, r, :] = two
            if passes:
                p_own[r, :] = two.astype(BF16)
                level = level + fold(lv * two)
            return h, level

        _, level = lax.fori_loop(0, pairs, body, (jnp.zeros((seqs, W), F32), jnp.zeros((8, W), F32)))
        if not passes:
            return None
        level = jnp.sum(level, axis=0, keepdims=True)
        levels[1:2, :] = level if m == 0 else levels[1:2, :] + level
        here = pl.ds(m * span, span)
        made = across(p_own.at[here, :], p_far.at[here, :], 18 + m)
        made.start()
        return made

    def backward_scan(layer, m, above, between=lambda: None):
        gain, shift, recur = vec_of(layer, 0), vec_of(layer, 1), vec_of(layer, 2)
        for lq in range(4):
            lanes = slice(lq * QUART, (lq + 1) * QUART)
            gq, sq, rec = gain[:, lanes], shift[:, lanes], recur[:, lanes]
            mean = coef[layer, 2 * m : 2 * m + 1, lanes]
            scale = coef[layer, 2 * m + 1 : 2 * m + 2, lanes]

            def body(i, carry):
                down, s1, s2, rsum, sqh, sqa = carry
                i = pairs - 1 - i
                start = m * span + i * (2 * seqs)
                r = pl.ds(aligned(start, 16), 2 * seqs)
                before = pl.ds(aligned(jnp.maximum(start - seqs, 0), 8), seqs)
                normed = (rows[layer, r, lanes] - mean) * scale
                drive = gq * normed + sq
                h2 = hid[layer, r, lanes]
                hb = jnp.where(i > 0, hid[layer, before, lanes], 0.0)
                lv = wide(live[r, :], 2)
                up = above[r, lanes].astype(F32)
                res = f_own[r, lanes].astype(F32)
                aux = res + h2 if layer == 1 else res
                sqh = sqh + fold(lv * (h2 * h2))
                sqa = sqa + fold(lv * (aux * aux))
                grads = [None, None]
                for k in (1, 0):
                    part = slice(k * seqs, (k + 1) * seqs)
                    prior = h2[0:seqs] if k == 1 else hb
                    slope = 0.5 + 0.5 * jnp.tanh(0.5 * (drive[part] + rec * prior))
                    total = up[part] + down
                    gd = lv[part] * slope * total
                    down = (1.0 - lv[part]) * total + rec * gd
                    grads[k] = gd
                    rsum = rsum + fold(gd * prior)
                gd2 = jnp.concatenate(grads, axis=0)
                hid[layer, r, lanes] = gd2
                return down, s1 + fold(gd2), s2 + fold(gd2 * normed), rsum, sqh, sqa

            z8 = jnp.zeros((8, QUART), F32)
            _, s1, s2, rsum, sqh, sqa = lax.fori_loop(
                0, pairs, body, (jnp.zeros((seqs, QUART), F32), z8, z8, z8, z8, z8)
            )
            for k, x in ((m, s1), (2 + m, s2)):
                tot[layer, k : k + 1, lanes] = jnp.sum(x, axis=0, keepdims=True)
            for k, x in ((4, rsum), (5, sqh), (6, sqa)):
                x = jnp.sum(x, axis=0, keepdims=True)
                tot[layer, k : k + 1, lanes] = x if m == 0 else tot[layer, k : k + 1, lanes] + x
            between()

    def backward_stats(layer, m):
        rnd, plane, _ = slim_round(3 - layer, m)
        stage_start(plane, rnd, packed(tot[layer, m : m + 1, :], tot[layer, 2 + m : 3 + m, :]))

    def backward_middle(layer, m):
        rnd, plane, line = slim_round(3 - layer, m)
        stage_wait(plane, rnd)
        stage_start(line, rnd, add_slots(plane))

    def backward_end(layer, m):
        rnd, _, line = slim_round(3 - layer, m)
        stage_wait(line, rnd)
        value = add_slots(line)
        tot[layer, m : m + 1, :] = unpacked(value[0:4])
        tot[layer, 2 + m : 3 + m, :] = unpacked(value[4:8])

    def grad_rows(layer, m, slot):
        gain = vec_of(layer, 0)
        for lh in range(2):
            lanes = slice(lh * HALF, (lh + 1) * HALF)
            mean = coef[layer, 2 * m : 2 * m + 1, lanes]
            scale = coef[layer, 2 * m + 1 : 2 * m + 2, lanes]
            count = wide(counts[m : m + 1, :], 4)
            first = tot[layer, m : m + 1, lanes] / count
            second = tot[layer, 2 + m : 3 + m, lanes] / count * scale
            k = scale * gain[:, lanes]

            def body(i, acc):
                r = pl.ds(aligned(m * span + i * (2 * seqs), 16), 2 * seqs)
                y = hid[layer, r, lanes] - first - (rows[layer, r, lanes] - mean) * second
                y = wide(live[r, :], 4) * (k * y)
                g3[0, r, lanes] = y.astype(BF16)
                return acc + fold(y)

            acc = repeat(pairs, body, jnp.zeros((8, HALF), F32), 3)
            acc = jnp.sum(acc, axis=0, keepdims=True)
            if m == 0:
                levels[4:5, lanes] = acc
            else:
                top = lax.broadcasted_iota(jnp.int32, (16, HALF), 0) == 0
                minus = jnp.where(top, -(levels[4:5, lanes] + acc), 0.0)
                g3[0, total_rows:sent_rows, lanes] = minus.astype(BF16)
        here = pl.ds(0, span) if m == 0 else pl.ds(span, span + 16)
        made = across(g3.at[0, here, :], g3.at[1, here, :], slot + m)
        made.start()
        return made

    sums_round = {1: (1, 10), 0: (0, 11)}

    def sums_start(layer):
        parity, rnd = sums_round[layer]
        own_sum = -g3[0, total_rows:sent_rows, :].astype(F32)[0:1]
        far_sum = -g3[1, total_rows:sent_rows, :].astype(F32)[0:1]
        value = jnp.concatenate([own_sum, far_sum, tot[layer, 4:7, :], jnp.zeros((3, W), F32)], axis=0)
        stage_start(in_plane(wide_p, parity), rnd, value)

    def sums_middle(layer):
        parity, rnd = sums_round[layer]
        stage_wait(in_plane(wide_p, parity), rnd)
        stage_start(in_line(wide_z, parity), rnd, add_slots(in_plane(wide_p, parity)))

    def sums_end(layer):
        parity, rnd = sums_round[layer]
        stage_wait(in_line(wide_z, parity), rnd)
        vtot[layer] = add_slots(in_line(wide_z, parity))
        tot[layer, 4:7, :] = vtot[layer, 2:5, :]
        tot[layer, 7:8, :] = wide(counts[0:1, :] + counts[1:2, :], 8)
        env["summed"].add(layer)

        @pl.when(section == layer)
        def _():
            pltpu.make_async_copy(tot.at[layer], v.at[section], v_sems.at[0]).start()

        @pl.when(section != layer)
        def _():
            v_across(layer).start()

    def v_across(layer):
        return pltpu.make_async_remote_copy(
            src_ref=tot.at[layer], dst_ref=v.at[section], send_sem=v_sems.at[1], recv_sem=v_sems.at[2],
            device_id=sibling, device_id_type=MESH,
        )

    def transpose(src, begin=0, end=W // 128):
        def body(j, _):
            c = pl.ds(aligned(j * 128, 128), 128)
            src_t[c, 0:total_rows] = src[0:total_rows, c].T
            return 0

        lax.fori_loop(begin, end, body, 0)

    def transpose_level(src, layer):
        top = lax.broadcasted_iota(jnp.int32, (16, W), 0) == 0
        src[total_rows:sent_rows, :] = jnp.where(top, levels[2 + layer : 3 + layer, :], 0.0).astype(BF16)

        def body(j, _):
            c = pl.ds(aligned(j * 128, 128), 128)
            src_t[c, total_rows:] = src[total_rows:, c].T
            level = src[total_rows:sent_rows, c].astype(F32)[0:1]
            column[layer, c, :] = jnp.broadcast_to(level, (128, 128)).T.astype(BF16)
            return 0

        lax.fori_loop(0, W // 128, body, 0)

    def weight_part(block, grads, c):
        lanes = pl.ds(c * HALF, HALF)

        def body(j, _):
            r = pl.ds(aligned(j * HALF, HALF), HALF)
            block[r, lanes] = dot(src_t[r, :], grads[:, lanes], ((1,), (0,))).astype(BF16)
            return 0

        lax.fori_loop(0, W // HALF, body, 0)

    def source_grad(store, w_own, w_far, between):
        for m in range(2):
            r = pl.ds(m * span, span)

            def body(i, _):
                c = pl.ds(aligned(i * HALF, HALF), HALF)
                y = dot(g3[0, r, :], w_own[c, :], ((1,), (1,))) + dot(g3[1, r, :], w_far[c, :], ((1,), (1,)))
                store(r, c, y)
                return 0

            lax.fori_loop(0, 2, body, 0)
            between()

    env = dict(summed=set(), vtot=vtot, column=column, space=space, ar_send=ar_send, ar_recv=ar_recv,
               ar_other=ar_other, o=o, section=section, here={"batch": b})
    xs = [a for a in bits if a["link"] == "x"]
    ys = [a for a in bits if a["link"] == "y"]
    zs = [a for a in bits if a["link"] == "z"]
    orders = (xs + ys + zs, ys + xs + zs)
    blocks = {
        (1, 0): f_far.at[pl.ds(0, W), :],
        (1, 1): p_far.at[pl.ds(0, W), :],
        (0, 0): wc.at[1, 1],
        (0, 1): wr1,
    }
    parts = {}
    for layer in (1, 0):
        for index in range(2 * PAIRS):
            part, side = index // PAIRS, index % PAIRS

            def lane_of(sec, part=part, side=side):
                return (sec if part == 0 else 1 - sec) * W + side * 2 * PART

            block = blocks[layer, part].at[:, pl.ds(side * 2 * PART, 2 * PART)]
            parts[layer, index] = Reduction(env, layer, index, block, orders, lane_of)
    order = Order()

    def weight_grads(layer, between):
        for part in range(2):
            if part == 1:
                between()
            for c in range(2):
                weight_part(blocks[layer, part], g3.at[part], c)
                order.work(2.0)
                for k in range(c * HALF // PART, (c + 1) * HALF // PART):
                    order.begin(parts[layer, part * PAIRS + k // 2], k % 2)

    def arrived(layer, sends):
        for made in sends:
            made.wait()
        sums_start(layer)

    send_f = []
    for m in range(2):
        by_units(frames, f_own, m)
        fetch(grad_out, m).start()
        if m == 0:
            wait_heads(frames, 1)
        patch_heads(f_own, m)
        here = pl.ds(m * span, span)
        made = across(f_own.at[here, :], f_far.at[here, :], (0, 24)[m])
        made.start()
        send_f.append(made)
    start_across_w(1, w_plan(1), slot_of[1])
    stage_wait(cnt_plane, 0)
    stage_start(cnt_line, 0, add_slots(cnt_plane))
    wait_w(0, w_plan(0), slot_of[0], 0)
    matmul_to(rows.at[0], f_own, wc.at[0, 0], True, 0)
    matmul_to(rows.at[0], f_own, wc.at[0, 0], True, 1)
    wait_w(0, w_plan(0), slot_of[0], 1)
    send_f[0].wait()
    matmul_to(rows.at[0], f_far, wc.at[0, 1], False, 0)
    forward_stats(0, 0)
    send_f[1].wait()

    @pl.when(section == 1)
    def _():
        heads_copy(grad_out, 2).start()

    matmul_to(rows.at[0], f_far, wc.at[0, 1], False, 1)
    forward_middle(0, 0)
    forward_stats(0, 1)
    send_vec.wait_send()
    across(vecs.at[other], vecs.at[other], 3).wait_recv()
    stage_wait(cnt_line, 0)
    counts[...] = add_slots(cnt_line)
    forward_end(0, 0)
    sends = [forward_scan(0, 0, True)]
    forward_middle(0, 1)
    by_units(grad_out, g3.at[1], 0)
    wait_heads(grad_out, 2)
    patch_heads(g3.at[1], 0)
    forward_end(0, 1)
    sends.append(forward_scan(0, 1, True))
    wait_w(1, w_plan(1), slot_of[1], 0)
    matmul_to(rows.at[1], p_own, wc.at[1, 0], True, 0)
    wait_w(1, w_plan(1), slot_of[1], 1)
    sends[0].wait()
    matmul_to(rows.at[1], p_far, wc.at[1, 1], False, 0)
    forward_stats(1, 0)
    matmul_to(rows.at[1], p_own, wc.at[1, 0], True, 1)
    forward_middle(1, 0)
    sends[1].wait()
    matmul_to(rows.at[1], p_far, wc.at[1, 1], False, 1)
    forward_stats(1, 1)
    done_w(0, w_plan(0), slot_of[0])

    start_local_w(0, late_plan, slot_of[2])
    start_across_w(0, late_plan, slot_of[2])

    @pl.when(section == 1)
    def _():
        wc[0, 1, width - late_row :, :] = jnp.zeros((W - width + late_row, W), BF16)

    def source_level():
        def body(i, acc):
            r = pl.ds(aligned(i * (2 * seqs), 16), 2 * seqs)
            return acc + fold(wide(live[r, :], 8) * f_own[r, :].astype(F32))

        acc = repeat(2 * pairs, body, jnp.zeros((8, W), F32), 3)
        levels[0:1, :] = jnp.sum(acc, axis=0, keepdims=True)

    forward_end(1, 0)
    forward_scan(1, 0, False)
    forward_middle(1, 1)
    by_units(grad_out, g3.at[1], 1)
    patch_heads(g3.at[1], 1)
    source_level()
    forward_end(1, 1)
    level_plane, level_line = in_plane(wide_p, 0), in_line(wide_z, 0)
    stage_start(level_plane, 9, jnp.concatenate([levels[0:2, :], jnp.zeros((6, W), F32)], axis=0))
    forward_scan(1, 1, False)
    backward_scan(1, 0, g3.at[1])
    backward_stats(1, 0)
    stage_wait(level_plane, 9)
    stage_start(level_line, 9, add_slots(level_plane))
    backward_scan(1, 1, g3.at[1])
    backward_stats(1, 1)
    backward_middle(1, 0)
    pl.semaphore_signal(credit.at[0], inc=1, device_id=sibling, device_id_type=MESH)
    transpose(p_own, 0, W // 256)
    backward_middle(1, 1)
    backward_end(1, 0)
    pl.semaphore_wait(credit.at[0], 1)
    sends = [grad_rows(1, 0, 20)]
    transpose(p_own, W // 256)
    stage_wait(level_line, 9)
    levels[2:4, :] = (add_slots(level_line) / wide(counts[0:1, :] + counts[1:2, :], 8))[0:2]
    transpose_level(p_own, 1)
    backward_end(1, 1)
    sends.append(grad_rows(1, 1, 20))
    weight_grads(1, lambda: arrived(1, sends))
    wait_w(1, w_plan(1), slot_of[1], 2)
    done_w(1, w_plan(1), slot_of[1])

    def keep_down(r, c, y):
        p_own[r, c] = y.astype(BF16)

    source_grad(keep_down, wc.at[1, 0], wr1, lambda: order.work(3.0))
    pl.semaphore_signal(credit.at[1], inc=1, device_id=sibling, device_id_type=MESH)
    sums_middle(1)
    backward_scan(0, 0, p_own, lambda: order.work(0.6))
    backward_stats(0, 0)
    backward_scan(0, 1, p_own, lambda: order.work(0.6))
    backward_stats(0, 1)
    backward_middle(0, 0)
    sums_end(1)
    transpose(f_own)
    transpose_level(f_own, 0)
    backward_middle(0, 1)
    order.work(3.0)
    backward_end(0, 0)
    pl.semaphore_wait(credit.at[1], 1)
    sends = [grad_rows(0, 0, 22)]
    backward_end(0, 1)
    sends.append(grad_rows(0, 1, 22))
    order.work(2.0)
    weight_grads(0, lambda: arrived(0, sends))
    wait_w(0, late_plan, slot_of[2], 0)
    wait_w(0, late_plan, slot_of[2], 1)
    done_w(0, late_plan, slot_of[2])

    def keep_source(r, c, y):
        rows[0, r, c] = y

    fetch(grad_out, 0).start()
    fetch(grad_out, 1).start()
    sums_middle(0)
    source_grad(keep_source, wc.at[0, 0], wc.at[0, 1], lambda: order.work(3.0))
    sums_end(0)

    def give(m):
        return pltpu.make_async_copy(staged.at[m], gf.at[m], stage_sem.at[m])

    for m in range(2):
        fetch(grad_out, m).wait()

        def finish_frames(i, _, m=m):
            straight = staged[m, pl.ds(2 * i, 2)].astype(F32).reshape(2 * seqs, half)
            y = rows[0, pl.ds(aligned(m * span + 2 * i * seqs, 8), 2 * seqs), :]
            y = jnp.where(section == 0, y[:, :half], y[:, late_shift : late_shift + half])
            staged[m, pl.ds(2 * i, 2)] = (y + straight).reshape(2, seqs, half).astype(BF16)
            return 0

        repeat(pairs, finish_frames, 0, 3)
        give(m).start()
        order.work(2.0)
    order.drain()
    for m in range(2):
        give(m).wait()

    for layer in range(2):

        @pl.when(section == layer)
        def _(layer=layer):
            pltpu.make_async_copy(tot.at[layer], v.at[section], v_sems.at[0]).wait()
            pltpu.make_async_remote_copy(
                src_ref=tot.at[layer], dst_ref=v.at[other], send_sem=v_sems.at[1], recv_sem=v_sems.at[2],
                device_id=sibling, device_id_type=MESH,
            ).wait_recv()

        @pl.when(section != layer)
        def _(layer=layer):
            v_across(layer).wait_send()

    own_part, far_part = v[section], v[other]
    first = jnp.where(section == 0, own_part, far_part)
    second = jnp.where(section == 0, far_part, own_part)
    for row, terms in ((0, (2, 3)), (1, (0, 1)), (2, (4,))):
        for lane, x in ((0, first), (W, second)):
            total = x[terms[0] : terms[0] + 1, :]
            for k in terms[1:]:
                total = total + x[k : k + 1, :]
            vectors[row : row + 1, lane : lane + W] = total
    squares = jnp.sum(first[5:7, :] + second[5:7, :], axis=1, keepdims=True)
    root = jnp.sqrt(squares / (first[7:8, 0:1] * width))
    for k in range(2):
        vectors[3 + k : 4 + k, :] = jnp.broadcast_to(root[k : k + 1], (1, 2 * W))
    vectors[5:8, :] = jnp.zeros((3, 2 * W), F32)


def write_results(o, gf, vectors, grad_weight, grad_frames, grad_gains, grad_shifts, grad_recurs, table):
    width = grad_weight.shape[2]
    grad_weight[0] = o[...][:, :width].astype(F32)
    grad_frames[...] = gf[...]

    @pl.when(pl.program_id(0) == 0)
    def _():
        for k, out in enumerate((grad_gains, grad_shifts, grad_recurs)):
            out[...] = vectors[k : k + 1, 0:width]
        table[...] = jnp.concatenate([vectors[3:4, 0:1], vectors[4:5, 0:1]], axis=1)


def results(o, gf, vectors):
    micro, steps, seqs, half = gf.shape
    width = 2 * half
    count = W * 2 // 256
    frames = micro * steps // count
    whole = lambda shape: pl.BlockSpec(shape, lambda i: (0, 0))
    out = pl.pallas_call(
        write_results,
        grid=(count,),
        in_specs=[
            pl.BlockSpec((256, 2 * W), lambda i: (i, 0)),
            pl.BlockSpec((frames, seqs, half), lambda i: (i, 0, 0)),
            whole((8, 2 * W)),
        ],
        out_specs=(
            pl.BlockSpec((1, 256, width), lambda i: (0, i, 0)),
            pl.BlockSpec((frames, seqs, half), lambda i: (i, 0, 0)),
            whole((1, width)),
            whole((1, width)),
            whole((1, width)),
            whole((1, 2)),
        ),
        out_shape=(
            jax.ShapeDtypeStruct((1, width, width), F32),
            jax.ShapeDtypeStruct((micro * steps, seqs, half), BF16),
            jax.ShapeDtypeStruct((1, width), F32),
            jax.ShapeDtypeStruct((1, width), F32),
            jax.ShapeDtypeStruct((1, width), F32),
            jax.ShapeDtypeStruct((1, 2), F32),
        ),
        compiler_params=pltpu.CompilerParams(vmem_limit_bytes=64 * 1024 * 1024),
    )(o.reshape(2 * W, 2 * W), gf.reshape(micro * steps, seqs, half), vectors)
    return out[1].reshape(gf.shape), out[0], *out[2:]


def whole_step(dims, frames, grad_out, weights, gains, shifts, recurs, lengths, masks):
    nz, ny, nx = dims
    micro, steps, seqs, half = frames.shape
    width = 2 * half
    views = seqs // lengths.shape[1]
    rows = micro * steps * seqs
    np_ = ny * nx
    wide_rows = (rows + 16 + 127) // 128 * 128
    depth = (nx * ny * nz - 1).bit_length()
    any_ = pl.BlockSpec(memory_space=pl.ANY)
    held = pl.BlockSpec(memory_space=pltpu.VMEM)
    dma = pltpu.SemaphoreType.DMA
    return pl.pallas_call(
        functools.partial(kernel, dims, steps, seqs, views),
        out_shape=(
            jax.ShapeDtypeStruct((2, W, 2 * W), BF16),
            jax.ShapeDtypeStruct(frames.shape, BF16),
            jax.ShapeDtypeStruct((8, 2 * W), F32),
        ),
        in_specs=[any_] * 3 + [held] * 5,
        out_specs=(any_, any_, held),
        scratch_shapes=[
            pltpu.VMEM((wide_rows, W), BF16),
            pltpu.VMEM((rows, W), BF16),
            pltpu.VMEM((wide_rows, W), BF16),
            pltpu.VMEM((rows, W), BF16),
            pltpu.VMEM((2, wide_rows, W), BF16),
            pltpu.VMEM((2, 2, W, W), BF16),
            pltpu.VMEM((W, W), BF16),
            pltpu.VMEM((W, wide_rows), BF16),
            pltpu.VMEM((rows, 128), F32),
            pltpu.VMEM((128, 128), F32),
            pltpu.VMEM(frames.shape, BF16),
            pltpu.VMEM((micro, steps, seqs, 128), BF16),
            pltpu.VMEM((5, W, (width - W) % 128), BF16),
            pltpu.VMEM((2, 8, W), F32),
            pltpu.VMEM((2, 8, 2 * W), F32),
            pltpu.VMEM((2, rows, W), F32),
            pltpu.VMEM((2, rows, W), F32),
            pltpu.VMEM((2, 8, W), F32),
            pltpu.VMEM((2, 8, W), F32),
            pltpu.VMEM((2, 8, W), F32),
            pltpu.VMEM((8, W), F32),
            pltpu.VMEM((2, W, 128), BF16),
            pltpu.VMEM((8, 128), F32),
            pltpu.VMEM((1, np_, 8, 128), F32),
            pltpu.VMEM((1, nz, 8, 128), F32),
            pltpu.VMEM((4, np_, 8, QUART), F32),
            pltpu.VMEM((4, nz, 8, QUART), F32),
            pltpu.VMEM((2, np_, 8, W), F32),
            pltpu.VMEM((2, nz, 8, W), F32),
            pltpu.VMEM((2, 2 * PAIRS, W, 2 * PART), BF16),
            dma((3, 25)),
            dma((3,)),
            dma((2,)),
            pltpu.SemaphoreType.REGULAR((2,)),
            dma((12, max(np_, 2))),
            dma((12, max(np_, 2))),
            dma((12, max(nz, 2))),
            dma((12, max(nz, 2))),
            dma((2, 2 * PAIRS, 2, 2 * depth + 2)),
            dma((2, 2 * PAIRS, 2, 2 * depth + 2)),
            dma((2, 2 * PAIRS, 2, 2)),
        ],
        compiler_params=pltpu.CompilerParams(
            collective_id=0, has_side_effects=True, vmem_limit_bytes=64 * 1024 * 1024
        ),
    )(frames, grad_out, weights, gains, shifts, recurs, lengths, masks)


def shards(dims, frames, grad_out, weights, gains, shifts, recurs, lengths, masks):
    return results(*whole_step(dims, frames, grad_out, weights, gains, shifts, recurs, lengths, masks))


def solution(mesh):
    in_specs = (
        P(None, None, "batch", "section"),
        P(None, None, "batch", "section"),
        P("section", None, None),
        P("section", None),
        P("section", None),
        P("section", None),
        P(None, "batch"),
        P(None, None, "batch"),
    )
    out_specs = (
        P(None, None, "batch", "section"),
        P("section", None, None),
        P("section", None),
        P("section", None),
        P("section", None),
        P("section", None),
    )
    body = functools.partial(shards, grid_of(mesh.shape["batch"]))
    return jax.shard_map(body, mesh=mesh, in_specs=in_specs, out_specs=out_specs, check_vma=False)
```
